32 devices in a mesh: crop: 16 (over z, y, x), res: 2 (over core).
Axes of the slice: x: 2, y: 2, z: 4, core: 2. Of those that a mesh axis runs over, the one named last changes fastest.
Arguments:
- tokens: bfloat16 [16, 1344, 768], P('crop', 'res'), may hold values from -6 to 6
- cotangent: bfloat16 [16, 1344, 768], P('crop', 'res'), may hold values from -6 to 6
- time_levels: float32 [16], P('crop'), may hold values from 0 to 1
- cath_ids: int32 [16], P('crop'), may hold values from 0 to 1471
- residue_numbers: int32 [16, 1344], P('crop'), may hold values from 0 to 7320, as said below
- chain_mask: int32 [16, 1344], P('crop'), may hold values from 0 to 1, as said below
- time_weight: bfloat16 [256, 256], replicated, may hold values from -0.375 to 0.375
- label_table: bfloat16 [1472, 256], replicated, may hold values from -6 to 6
- modulation_weight: bfloat16 [256, 4608], replicated, may hold values from -0.375 to 0.375
- projection_weight: bfloat16 [768, 2304], replicated, may hold values from -0.21875 to 0.21875
- gate_weight: bfloat16 [768, 768], replicated, may hold values from -0.21875 to 0.21875
- output_weight: bfloat16 [768, 768], replicated, may hold values from -6 to 6
- relative_table: bfloat16 [66, 256], replicated, may hold values from -6 to 6
- pair_gain: bfloat16 [256], replicated, may hold values from 0.099609375 to 1.8984375
- pair_weight: bfloat16 [256, 12], replicated, may hold values from -0.375 to 0.375
- feed_gate: bfloat16 [768, 3072], replicated, may hold values from -0.21875 to 0.21875
- feed_up: bfloat16 [768, 3072], replicated, may hold values from -0.21875 to 0.21875
- feed_down: bfloat16 [3072, 768], replicated, may hold values from -0.109375 to 0.109375
Outputs:
- layer_out: bfloat16 [16, 1344, 768], P('crop', 'res')
- tokens_grad: bfloat16 [16, 1344, 768], P('crop', 'res')
- time_weight_grad: float32 [256, 256], replicated
- label_table_grad: float32 [1472, 256], replicated
- modulation_weight_grad: float32 [256, 4608], replicated
- projection_weight_grad: float32 [768, 2304], P('crop', 'res')
- gate_weight_grad: float32 [768, 768], P('crop', 'res')
- output_weight_grad: float32 [768, 768], P('crop', 'res')
- relative_table_grad: float32 [66, 256], replicated
- pair_gain_grad: float32 [256], replicated
- pair_weight_grad: float32 [256, 12], replicated
- feed_gate_grad: float32 [768, 3072], P('crop', 'res')
- feed_up_grad: float32 [768, 3072], P('crop', 'res')
- feed_down_grad: float32 [3072, 768], P('crop', 'res')
The draws below stay inside these ranges and needn't reach their ends.
Inputs may be any that keep to these rules, and one draw needn't show every extreme that they name: `residue_numbers`: in each crop the first residue has number 0, numbers rise by 1 or more from each residue to the next, and the last residue has number 5 * 1344 + 600. `chain_mask`: the first residue of every crop is marked; every crop holds two to four chains.
All inputs are finite; a program needn't handle non-finite values.
Results may differ from the reference program's by a relative error of at most 0.02.
Values may be sent and summed in bfloat16 or wider, within the bound.
No kernel may reach another device: no remote copies, remote signals or barrier semaphores. Data moves between devices by JAX's collectives and lax.ppermute only.
A program may use at most 320 MiB of HBM per device.

```python
import math
import jax
import jax.numpy as jnp
from jax import lax

D = 768
HEADS = 12
HEAD_DIM = 64
FF = 3072
PAIR = 256
COND = 256
TFREQ = 256
NCATH = 1472
NBIN = 66
CROP_LEN = 1344
CROPS = 16


def chain_layout(key):
    crop_keys = jax.random.split(key, CROPS)

    def one_crop(crop_key):
        break_key, step_key, skip_key, jump_key = jax.random.split(crop_key, 4)
        positions = jnp.arange(CROP_LEN, dtype=jnp.int32)
        breaks = jax.random.randint(break_key, (3,), 1, CROP_LEN, dtype=jnp.int32)
        starts = ((positions == 0) | jnp.any(positions[:, None] == breaks[None, :], axis=1)).astype(jnp.int32)
        skipping = (jax.random.randint(step_key, (CROP_LEN,), 0, 6, dtype=jnp.int32) == 0).astype(jnp.int32)
        skipped = skipping * jax.random.randint(skip_key, (CROP_LEN,), 1, 4, dtype=jnp.int32)
        chain_jumps = starts * jax.random.randint(jump_key, (CROP_LEN,), 20, 200, dtype=jnp.int32)
        strides = 1 + skipped + chain_jumps
        numbers = jnp.cumsum(strides, dtype=jnp.int32) - strides[0]
        numbers = jnp.where(positions == CROP_LEN - 1, 5 * CROP_LEN + 600, numbers).astype(jnp.int32)
        return (starts, numbers)
    return jax.vmap(one_crop)(crop_keys)


def draw_chain_mask(key, part):
    return chain_layout(key)[0]


def draw_residue_numbers(key, part):
    return chain_layout(key)[1]


def plant(result, rng, smallest, largest):
    longest = result.shape.index(max(result.shape))
    spots = []
    for shift in (0, 1):
        where = [jax.random.randint(jax.random.fold_in(rng, axis), (), 0, length) for axis, length in enumerate(result.shape)]
        where[longest] = (where[longest] + shift) % result.shape[longest]
        spots.append(tuple(where))
    return result.at[spots[0]].set(smallest).at[spots[1]].set(largest)


def levels(rng, shape, pieces, low, largest):
    def one(position, parts):
        draws = jax.random.uniform(jax.random.fold_in(jax.random.fold_in(rng, 6), position), (parts,), jnp.float32, low / len(pieces), largest / len(pieces))
        return jnp.repeat(jnp.exp(draws), shape[position] // parts).reshape((-1,) + (1,) * (len(shape) - position - 1))

    loudness = one(*pieces[0])
    for cut in pieces[1:]:
        loudness = loudness * one(*cut)
    return loudness


def noise(key, shape, width, reach, cuts=(), kind=jnp.bfloat16):
    array = width * jax.random.normal(key, shape, jnp.float32)
    if cuts:
        array = array * levels(key, shape, cuts, -0.22, 0.18)
    return jnp.clip(array, -reach, reach).astype(kind)


def setup_inputs(seed: int = 0) -> dict:
    key_list = jax.random.split(jax.random.key(seed), 19)
    return {
        "tokens": noise(key_list[0], (CROPS, CROP_LEN, D), 1.0, 6.0, ((0, 16), (1, 2))),
        "cotangent": noise(key_list[1], (CROPS, CROP_LEN, D), 1.0, 6.0, ((0, 16), (1, 2))),
        "time_levels": jnp.clip(1.0 * jax.random.uniform(key_list[2], (CROPS,), jnp.float32) ** levels(key_list[2], (CROPS,), ((0, 16),), -0.2, 0.2), 0.0, 1.0),
        "cath_ids": plant(jax.random.randint(key_list[3], (CROPS,), 0, NCATH), jax.random.fold_in(key_list[3], 1), 0, NCATH - 1).astype(jnp.int32),
        "residue_numbers": draw_residue_numbers(jax.random.fold_in(key_list[18], 71), 0),
        "chain_mask": draw_chain_mask(jax.random.fold_in(key_list[18], 71), 0),
        "time_weight": noise(key_list[6], (TFREQ, COND), TFREQ ** -0.5, 0.375),
        "label_table": noise(key_list[7], (NCATH, COND), 1.0, 6.0),
        "modulation_weight": noise(key_list[8], (COND, 6 * D), COND ** -0.5, 0.375),
        "projection_weight": noise(key_list[9], (D, 3 * D), D ** -0.5, 0.21875),
        "gate_weight": noise(key_list[10], (D, D), D ** -0.5, 0.21875),
        "output_weight": noise(key_list[11], (D, D), (max(1, D // 512)) ** -0.5, 6.0),
        "relative_table": noise(key_list[12], (NBIN, PAIR), 1.0, 6.0),
        "pair_gain": jnp.clip(1.0 + 0.18 * jax.random.normal(key_list[13], (PAIR,), jnp.float32), 0.099609375, 1.8984375).astype(jnp.bfloat16),
        "pair_weight": noise(key_list[14], (PAIR, HEADS), PAIR ** -0.5, 0.375),
        "feed_gate": noise(key_list[15], (D, FF), D ** -0.5, 0.21875),
        "feed_up": noise(key_list[16], (D, FF), D ** -0.5, 0.21875),
        "feed_down": noise(key_list[17], (FF, D), FF ** -0.5, 0.109375),
    }


@jax.custom_vjp
def low(v):
    return lax.optimization_barrier(v.astype(jnp.bfloat16)).astype(jnp.float32)

@jax.custom_vjp
def low_back(v):
    return v

def low_keep(v):
    return (low(v), None)

def low_pass(kept, grad):
    return (grad,)

def back_keep(v):
    return (v, None)

def back_low(kept, grad):
    return (low(grad),)
low.defvjp(low_keep, low_pass)
low_back.defvjp(back_keep, back_low)

def highest(former, latter):
    return jnp.dot(former, latter, precision=lax.Precision.HIGHEST)

def layer_norm(inputs):
    mean_value = lax.optimization_barrier(jnp.mean(inputs, axis=-1, keepdims=True))
    centred = inputs - mean_value
    spread = lax.optimization_barrier(jnp.mean(centred * centred, axis=-1, keepdims=True))
    return centred * lax.rsqrt(spread + 1e-06)

def time_features(time_levels):
    half_width = TFREQ // 2
    frequency = jnp.exp(-math.log(10000.0) * jnp.arange(half_width, dtype=jnp.float32) / half_width)
    angles = 1000.0 * time_levels[:, None] * frequency[None, :]
    return jnp.concatenate([jnp.sin(angles), jnp.cos(angles)], axis=-1)

def pair_bins(crop_numbers, crop_mask):
    chain_ids = jnp.cumsum(crop_mask, dtype=jnp.int32)
    reach_limit = (NBIN - 2) // 2
    offset = jnp.clip(crop_numbers[None, :] - crop_numbers[:, None], -reach_limit, reach_limit) + reach_limit
    return jnp.where(chain_ids[:, None] == chain_ids[None, :], offset, NBIN - 1).astype(jnp.int32)

def add_arrays(former, latter):
    return former + latter

def crop_forward(weight_list, token_rows, crop_features, crop_label, crop_bins):
    time_weight, label_table, modulation_weight, projection_weight, gate_weight, output_weight, relative_table, pair_gain, pair_weight, feed_gate, feed_up, feed_down = weight_list
    condition = highest(low(crop_features), time_weight) + label_table[crop_label]
    modulation = highest(low(jax.nn.silu(condition)), modulation_weight).reshape(6, D)
    normed_a = low(layer_norm(token_rows) * (1.0 + modulation[1]) + modulation[0])
    projected = low_back(low(highest(normed_a, projection_weight)))
    queries = projected[:, :D].reshape(CROP_LEN, HEADS, HEAD_DIM)
    key_rows = projected[:, D:2 * D].reshape(CROP_LEN, HEADS, HEAD_DIM)
    value_rows = projected[:, 2 * D:].reshape(CROP_LEN, HEADS, HEAD_DIM)
    gate_pre = low_back(highest(normed_a, gate_weight))
    pair_norm = low(layer_norm(relative_table) * pair_gain)
    bias_table = highest(pair_norm, pair_weight)
    pair_bias = jnp.take(bias_table.T, crop_bins, axis=1)
    raw_scores = jnp.einsum('qhd,khd->hqk', queries, key_rows, precision=lax.Precision.HIGHEST) * HEAD_DIM ** (-0.5)
    scores = low_back(raw_scores) + pair_bias
    probability = low(jax.nn.softmax(scores, axis=-1))
    attended = jnp.einsum('hqk,khd->qhd', probability, value_rows, precision=lax.Precision.HIGHEST)
    attended = low_back(attended.reshape(CROP_LEN, D))
    gated_out = low(attended * jax.nn.sigmoid(gate_pre))
    branch = low_back(highest(gated_out, output_weight))
    middle = token_rows + jax.nn.sigmoid(modulation[2]) * branch
    normed_f = low(layer_norm(middle) * (1.0 + modulation[4]) + modulation[3])
    ff_gate_pre = low_back(highest(normed_f, feed_gate))
    ff_up_pre = low_back(highest(normed_f, feed_up))
    hidden = low(jax.nn.silu(ff_gate_pre) * ff_up_pre)
    ff_out = low_back(highest(hidden, feed_down))
    return middle + jax.nn.sigmoid(modulation[5]) * ff_out

def reference(tokens, cotangent, time_levels, cath_ids, residue_numbers, chain_mask, time_weight, label_table, modulation_weight, projection_weight, gate_weight, output_weight, relative_table, pair_gain, pair_weight, feed_gate, feed_up, feed_down):
    weights = tuple((matrix.astype(jnp.float32) for matrix in (time_weight, label_table, modulation_weight, projection_weight, gate_weight, output_weight, relative_table, pair_gain, pair_weight, feed_gate, feed_up, feed_down)))
    features = time_features(time_levels)

    def crop_step(totals, crop_inputs):
        crop_tokens, crop_cotangent, crop_features, crop_label, crop_numbers, crop_mask = crop_inputs
        crop_bins = pair_bins(crop_numbers, crop_mask)

        def forward(weight_list, token_rows):
            return crop_forward(weight_list, token_rows, crop_features, crop_label, crop_bins)
        outputs, backward = jax.vjp(forward, weights, crop_tokens.astype(jnp.float32))
        weight_grads, token_grads = backward(crop_cotangent.astype(jnp.float32))
        totals = jax.tree.map(add_arrays, totals, weight_grads)
        return (totals, (outputs.astype(jnp.bfloat16), token_grads.astype(jnp.bfloat16)))
    zero_grads = jax.tree.map(jnp.zeros_like, weights)
    totals, (layer_out, tokens_grad) = lax.scan(crop_step, zero_grads, (tokens, cotangent, features, cath_ids, residue_numbers, chain_mask))
    return (layer_out, tokens_grad, totals[0], totals[1], totals[2], totals[3], totals[4], totals[5], totals[6], totals[7], totals[8], totals[9], totals[10], totals[11])
```

```python
import functools
import math

import jax
import jax.numpy as jnp
from jax import lax
from jax.experimental import pallas as pl
from jax.experimental.pallas import tpu as pltpu
from jax.sharding import PartitionSpec as P

LANES = 128
NEAR = 31
VMEM_BYTES = 56 * 1024 * 1024
LOG2E = 1.4426950408889634
NONE, RIGHT, LEFT, APART = 0, 1, 2, 3


def layer_norm(inputs):
    mean_value = jnp.mean(inputs, axis=-1, keepdims=True)
    centred = inputs - mean_value
    spread = jnp.mean(centred * centred, axis=-1, keepdims=True)
    return centred * lax.rsqrt(spread + 1e-06)


def modulate(inputs, shift_row, scale_row):
    return layer_norm(inputs) * (1.0 + scale_row) + shift_row


def normalize_rows(table_rows, gain_row):
    return layer_norm(table_rows) * gain_row


def time_features(time_levels, feature_width):
    half_width = feature_width // 2
    frequency = jnp.exp(-math.log(10000.0) * jnp.arange(half_width, dtype=jnp.float32) / half_width)
    angles = 1000.0 * time_levels[:, None] * frequency[None, :]
    return jnp.concatenate([jnp.sin(angles), jnp.cos(angles)], axis=-1)


def across_rows(former, latter):
    return lax.dot_general(
        former, latter, (((0,), (0,)), ((), ())), preferred_element_type=jnp.float32
    )


def against_columns(former, latter):
    return lax.dot_general(
        former, latter, (((1,), (1,)), ((), ())), preferred_element_type=jnp.float32
    )


def split_parts(values):
    upper = lax.reduce_precision(values, 8, 7)
    return (upper.astype(jnp.bfloat16), (values - upper).astype(jnp.bfloat16))


def split_left(narrow, values, former_dim, latter_dim):
    upper, rest = split_parts(values)
    numbers = (((former_dim,), (latter_dim,)), ((), ()))
    return lax.dot_general(
        narrow, upper, numbers, preferred_element_type=jnp.float32
    ) + lax.dot_general(narrow, rest, numbers, preferred_element_type=jnp.float32)


def split_right(values, narrow, former_dim, latter_dim):
    upper, rest = split_parts(values)
    numbers = (((former_dim,), (latter_dim,)), ((), ()))
    return lax.dot_general(
        upper, narrow, numbers, preferred_element_type=jnp.float32
    ) + lax.dot_general(rest, narrow, numbers, preferred_element_type=jnp.float32)


def sigmoid_slope(inputs):
    gate_value = jax.nn.sigmoid(inputs)
    return gate_value * (1.0 - gate_value)


def silu_slope(inputs):
    gate_value = jax.nn.sigmoid(inputs)
    return gate_value * (1.0 + inputs * (1.0 - gate_value))


class Layout:
    def __init__(self, rows, length):
        self.rows = rows
        self.length = length
        self.query_tiles = -(-rows // LANES)
        self.key_tiles = -(-length // LANES)
        self.padded = self.query_tiles * LANES
        self.wide = self.key_tiles * LANES
        self.last = self.key_tiles - 1
        self.groups = (self.query_tiles + 4) * 4
        assert 2 * self.groups + 3 <= LANES
        assert rows - 1 + NEAR < self.padded and length - NEAR >= self.last * LANES
        assert rows % 8 == 0 and self.last > self.query_tiles
        self.block_rows = rows if rows % 16 == 0 else self.padded
        self.pieces = [rows, length - rows] if rows % 16 == 0 else [length]

    def tile_start(self, tile):
        return self.last * LANES if tile < 0 else tile * LANES


def pad_to(values, axis, size, fill):
    widths = [(0, 0)] * values.ndim
    widths[axis] = (0, size - values.shape[axis])
    return jnp.pad(values, widths, constant_values=fill)


def tables_kernel(layout, bin_count, start_ref, pairs_ref, *out_refs):
    members_ref, kinds_ref, forward_ref, backward_ref, places_ref, codes = out_refs
    rows, length, queries, groups = layout.rows, layout.length, layout.query_tiles, layout.groups
    wrap = length - start_ref[0]
    reach = (bin_count - 2) // 2
    zero_bin = LANES - 1
    shape = (LANES, LANES)
    lane = lax.broadcasted_iota(jnp.int32, shape, 1)
    row = lax.broadcasted_iota(jnp.int32, shape, 0)
    last_start = layout.last * LANES

    tiles = pairs_ref.shape[1]
    marks = pairs_ref[1].astype(jnp.float32)
    place = lax.broadcasted_iota(jnp.int32, marks.shape, 0) * LANES + lax.broadcasted_iota(
        jnp.int32, marks.shape, 1
    )
    before = jnp.sum(jnp.where(place < wrap, marks, 0.0), keepdims=True)
    every = jnp.sum(marks, keepdims=True)
    triangle = jnp.where(row <= lane, 1.0, 0.0).astype(jnp.bfloat16)
    running = jnp.dot(marks.astype(jnp.bfloat16), triangle, preferred_element_type=jnp.float32)
    numbers, chains = [], []
    carry = jnp.zeros((1, 1), jnp.float32)
    for tile in range(layout.key_tiles):
        count = running[tile : tile + 1] + carry
        carry = carry + running[tile : tile + 1, LANES - 1 :]
        count = count + jnp.where(place[tile : tile + 1] < wrap, every - before, -before)
        chains.append(jnp.broadcast_to(count.astype(jnp.int32), shape))
        numbers.append(jnp.broadcast_to(pairs_ref[0, tile : tile + 1], shape))
    number_rows = [value.T for value in numbers]
    chain_rows = [value.T for value in chains]

    def bins_of(key_number, key_chain, query_number, query_chain):
        offset = jnp.clip(key_number - query_number, -reach, reach) + reach
        return jnp.where(key_chain == query_chain, offset, bin_count - 1)

    def touches(query, tile):
        begin = -LANES if tile < 0 else tile * LANES
        return (begin <= query + NEAR) & (query - NEAR <= begin + LANES - 1)

    for tile in range(layout.key_tiles):
        size = min(LANES, length - tile * LANES)
        key = tile * LANES + row
        if tile == layout.last:
            other = jnp.full(shape, queries + 3, jnp.int32)
        elif tile == queries - 1:
            other = jnp.full(shape, queries, jnp.int32)
        else:
            other = jnp.where(key < wrap, queries + 1, queries + 2)
        group = jnp.where(key < rows, tile, other)
        slot = group * 4 + chain_rows[tile] - 1
        hit = (lane == slot) | (lane == slot + groups)
        tail = (lane >= 2 * groups) & (lane < 2 * groups + 3)
        values = jnp.where(hit, 1.0, jnp.where(tail, -1.0, 0.0)).astype(jnp.bfloat16)
        members_ref[tile * LANES : tile * LANES + size] = values[:size]

    local = jnp.where(lane >= groups, lane - groups, lane)
    lane_group = local >> 2
    lane_chain = (local & 3) + 1
    lane_begin = jnp.where(
        lane_group < queries,
        lane_group * LANES,
        jnp.where(lane_group == queries, (queries - 1) * LANES, -LANES),
    )
    has_band = (lane_group <= queries) | (lane_group == queries + 3)
    other_right = jnp.where(
        lane_group == queries,
        rows,
        jnp.where(
            lane_group == queries + 3,
            last_start,
            jnp.where(lane_group == queries + 1, 0, 2 * length),
        ),
    )
    right_limit = jnp.where(lane_group > queries, jnp.where(lane_group == queries + 3, wrap, length), wrap)
    for tile in range(queries):
        size = min(LANES, layout.block_rows - tile * LANES)
        query = tile * LANES + row
        near = (lane_begin <= query + NEAR) & (query - NEAR <= lane_begin + LANES - 1) & has_band
        right = jnp.where(lane_group < queries, lane_group - tile, right_limit - other_right) > 0
        same = chain_rows[tile] == lane_chain
        kinds = jnp.where(same, jnp.where(near, NONE, jnp.where(right, RIGHT, LEFT)), APART)
        kinds = jnp.where((lane < 2 * groups) & (query < rows), kinds, NONE)
        kinds_ref[tile * LANES : tile * LANES + size] = kinds[:size]
        for step in range(3):
            near_tile = tile + step - 1
            index = layout.last if near_tile < 0 else near_tile
            if near_tile < queries:
                inside = touches(query, near_tile) & (query < rows)
                inside &= lane < length - index * LANES
                found = bins_of(
                    numbers[index], chains[index], number_rows[tile], chain_rows[tile]
                )
                found = jnp.where(inside, found, zero_bin)
            else:
                found = jnp.full(shape, zero_bin, jnp.int32)
            forward_ref[
                tile * LANES : (tile + 1) * LANES, step * LANES : (step + 1) * LANES
            ] = found

    codes[...] = jnp.full(codes.shape, -1, jnp.int32)
    for tile in range(queries):
        size = min(LANES, rows - tile * LANES)
        code = number_rows[tile] * 8 + chain_rows[tile]
        codes[(tile + 1) * LANES : (tile + 1) * LANES + size] = code[:size]

    for index, tile in enumerate(list(range(queries)) + [-1]):
        source = layout.last if tile < 0 else tile
        key_row = (row - (length - last_start)) if tile < 0 else tile * LANES + row
        present = row < length - source * LANES
        for step in range(3):
            near_tile = tile + step - 1
            if 0 <= near_tile < queries:
                near_query = near_tile * LANES + lane
                inside = touches(near_query, tile) & (near_query < rows) & present
                found = bins_of(
                    number_rows[source], chain_rows[source], numbers[near_tile], chains[near_tile]
                )
                found = jnp.where(inside, found, zero_bin)
            else:
                found = jnp.full(shape, zero_bin, jnp.int32)
            backward_ref[
                index * LANES : (index + 1) * LANES, step * LANES : (step + 1) * LANES
            ] = found
        target = (number_rows[source] + reach - lane) * 8 + chain_rows[source]
        target = jnp.where(present & (lane > 0) & (lane < 2 * reach), target, -9)
        offset = (LANES - (length - last_start)) if tile < 0 else (tile + 1) * LANES
        far = 4 * LANES
        shift = jnp.full(shape, far, jnp.int32)
        for distance in range(-NEAR, NEAR + 1):
            other = codes[offset - distance : offset - distance + LANES]
            shift = jnp.where(other == target, distance, shift)
        if tile < 0:
            base = jnp.zeros(shape, jnp.int32)
        else:
            base = jnp.where(row < LANES // 2, tile - 1, tile) * LANES
        places_ref[index * LANES : (index + 1) * LANES] = jnp.where(
            shift == far, far - 1, key_row - shift - base
        )


def attention_tables(layout, numbers, marks, query_start, bin_count):
    crops = numbers.shape[0]
    pairs = jnp.stack([numbers, marks], axis=1)
    pairs = pad_to(pairs, 2, layout.wide, 0).reshape(crops, 2, layout.key_tiles, LANES)
    spots = (layout.query_tiles + 1) * LANES
    shapes = [
        ((layout.length, LANES), jnp.bfloat16),
        ((layout.block_rows, LANES), jnp.int32),
        ((layout.padded, 3 * LANES), jnp.int32),
        ((spots, 3 * LANES), jnp.int32),
        ((spots, LANES), jnp.int32),
    ]
    return pl.pallas_call(
        functools.partial(tables_kernel, layout, bin_count),
        grid=(crops,),
        in_specs=[
            pl.BlockSpec(memory_space=pltpu.SMEM),
            pl.BlockSpec((None, 2, layout.key_tiles, LANES), lambda crop: (crop, 0, 0, 0)),
        ],
        out_specs=tuple(pl.BlockSpec((None, *shape), lambda crop: (crop, 0, 0)) for shape, _ in shapes),
        out_shape=tuple(jax.ShapeDtypeStruct((crops, *shape), kind) for shape, kind in shapes),
        scratch_shapes=[pltpu.VMEM((layout.padded + 2 * LANES, LANES), jnp.int32)],
        compiler_params=pltpu.CompilerParams(vmem_limit_bytes=VMEM_BYTES),
        cost_estimate=pl.CostEstimate(
            flops=40000000 * crops, bytes_accessed=4000000 * crops, transcendentals=0
        ),
        name="pair_tables",
    )(jnp.reshape(query_start, (1,)).astype(jnp.int32), pairs)


def head_tables(layout, bias_rows, scale):
    bin_count, heads = bias_rows.shape
    table = (bias_rows - bias_rows[bin_count - 1 :]).T / scale
    lane = jnp.arange(LANES, dtype=jnp.int32)
    groups = layout.groups

    def columns(values):
        upper = lax.reduce_precision(values, 8, 7)
        rest = values - upper
        return jnp.where(
            lane < groups, upper[:, None], jnp.where(lane < 2 * groups, rest[:, None], 0.0)
        )

    lookup = pad_to(table, 1, LANES, 0.0)
    stacked = jnp.stack([lookup, columns(table[:, bin_count - 2]), columns(table[:, 0])], 1)
    stacked = pad_to(stacked, 1, 8, 0.0)
    return stacked.reshape(heads // 2, 16, LANES)


NT = (((1,), (1,)), ((), ()))
TN = (((0,), (0,)), ((), ()))


def wide_dot(former, latter, numbers=(((1,), (0,)), ((), ()))):
    return lax.dot_general(former, latter, numbers, preferred_element_type=jnp.float32)


def look_up(table_row, bins):
    table = jnp.broadcast_to(table_row, bins.shape)
    return jnp.take_along_axis(table, bins, axis=1, mode="promise_in_bounds")


def half_of(values, lane, side):
    return jnp.where((lane >= 64) == (side == 1), values, jnp.zeros_like(values))


def row_blocks(total, size):
    return [(start, min(start + size, total)) for start in range(0, total, size)]


def group_columns(kinds, tables, side):
    right = tables[8 * side + 1 : 8 * side + 2]
    left = tables[8 * side + 2 : 8 * side + 3]
    return jnp.where(kinds == RIGHT, right, jnp.where(kinds == LEFT, left, 0.0))


def forward_kernel(layout, scale, *refs):
    count = len(layout.pieces)
    query_ref = refs[0]
    key_refs = refs[1 : 1 + count]
    value_refs = refs[1 + count : 1 + 2 * count]
    members_ref, kinds_ref, bins_ref, tables_ref, out_ref, log_ref = refs[1 + 2 * count : -1]
    scores = refs[-1]
    pair = pl.program_id(1)
    rows, length = layout.block_rows, layout.length
    factor = scale * LOG2E
    lane = lax.broadcasted_iota(jnp.int32, (1, LANES), 1)
    query = query_ref[...]
    keys = jnp.concatenate([ref[...] for ref in key_refs], axis=0)
    values = jnp.concatenate([ref[...] for ref in value_refs], axis=0)
    members = members_ref[...]
    kinds = kinds_ref[...]
    tables = tables_ref[...]
    ones = jnp.ones((length, LANES), jnp.bfloat16)

    @pl.when(pair == 0)
    def _():
        log_ref[...] = jnp.zeros_like(log_ref)

    for side in range(2):
        key_columns = jnp.concatenate([half_of(keys, lane, side), members], axis=1)
        value_columns = jnp.concatenate([half_of(values, lane, side), ones], axis=1)
        extra = group_columns(kinds, tables, side).astype(jnp.bfloat16)
        query_columns = jnp.concatenate([query, extra], axis=1)
        table_row = tables[8 * side : 8 * side + 1]
        for start, stop in row_blocks(rows, 256):
            size = stop - start
            scores[0:size, 0:length] = wide_dot(query_columns[start:stop], key_columns, NT)
            for tile in range(start // LANES, -(-stop // LANES)):
                first, final = tile * LANES, min(tile * LANES + LANES, rows)
                for slot in range(3):
                    other = tile + slot - 1
                    if other >= layout.query_tiles:
                        continue
                    low, high = first, final
                    if slot == 0:
                        high = min(first + 32, final)
                    if slot == 2:
                        low = first + LANES - 32
                    if low >= high:
                        continue
                    place = layout.tile_start(other)
                    width = min(LANES, length - place)
                    bins = bins_ref[low:high, slot * LANES : (slot + 1) * LANES]
                    bias = look_up(table_row, bins)[:, :width]
                    scores[low - start : high - start, place : place + width] += bias
            block = scores[0:size, 0:length]
            top = jnp.max(block, axis=1, keepdims=True)
            weights = jnp.exp2((block - top) * factor).astype(jnp.bfloat16)
            sums = wide_dot(weights, value_columns)
            total = sums[:, LANES:]
            result = sums[:, :LANES] / total
            if side == 0:
                out_ref[start:stop] = result
            else:
                out_ref[start:stop] += result
            log_total = top + jnp.log(total) * (1.0 / scale)
            log_ref[start:stop] = jnp.where(
                lane == 2 * pair + side, log_total, log_ref[start:stop]
            )


def backward_kernel(layout, scale, first_pair, *refs):
    count = len(layout.pieces)
    query_ref, grad_ref, out_ref, log_ref = refs[:4]
    key_refs = refs[4 : 4 + count]
    value_refs = refs[4 + count : 4 + 2 * count]
    rest = refs[4 + 2 * count :]
    members_ref, kinds_ref, bins_ref, places_ref, tables_ref = rest[:5]
    grad_query_ref = rest[5]
    grad_pair_refs = rest[6 : 6 + count]
    grad_table_ref = rest[6 + count]
    query_wide, grad_wide, query_half, grad_half, scores, slopes, slopes_low = rest[7 + count :]
    pair = pl.program_id(1) + first_pair
    rows, length, padded = layout.block_rows, layout.length, layout.padded
    factor = scale * LOG2E
    lane = lax.broadcasted_iota(jnp.int32, (1, LANES), 1)
    keys = jnp.concatenate([ref[...] for ref in key_refs], axis=0)
    values = jnp.concatenate([ref[...] for ref in value_refs], axis=0)
    members = members_ref[...]
    kinds = kinds_ref[...]
    tables = tables_ref[...]
    query = query_ref[...]
    grad = grad_ref[...]
    grad_full = grad.astype(jnp.float32)
    product = grad_full * out_ref[...]
    log_all = log_ref[...]
    tail = 2 * layout.groups
    ones = jnp.broadcast_to(jnp.where(lane < 3, 1.0, 0.0), (length, LANES)).astype(jnp.bfloat16)

    def three_parts(values):
        upper = values.astype(jnp.bfloat16).astype(jnp.float32)
        values = values - upper
        middle = values.astype(jnp.bfloat16).astype(jnp.float32)
        return upper, middle, values - middle

    def in_lanes(parts, first):
        return jnp.where(
            lane == first,
            parts[0],
            jnp.where(lane == first + 1, parts[1], jnp.where(lane == first + 2, parts[2], 0.0)),
        )

    if padded > rows:
        for ref in (query_wide, grad_wide, query_half, grad_half):
            for side in range(2):
                ref[side, rows:padded] = jnp.zeros((padded - rows, ref.shape[2]), jnp.bfloat16)
    for side in range(2):
        log_total = jnp.sum(
            jnp.where(lane == 2 * pair + side, log_all, 0.0), axis=1, keepdims=True
        )
        extra = group_columns(kinds, tables, side) + in_lanes(three_parts(log_total), tail)
        query_wide[side, 0:rows, 0:LANES] = query
        query_wide[side, 0:rows, LANES:] = extra.astype(jnp.bfloat16)
        delta = jnp.sum(half_of(product, lane, side), axis=1, keepdims=True)
        grad_wide[side, 0:rows, 0:LANES] = grad
        grad_wide[side, 0:rows, LANES:] = in_lanes(three_parts(-delta), 0).astype(jnp.bfloat16)
        query_half[side, 0:rows] = half_of(query, lane, side)
        grad_half[side, 0:rows] = half_of(grad, lane, side)

    key_columns = [
        jnp.concatenate([half_of(keys, lane, side), members], axis=1) for side in range(2)
    ]
    value_columns = [
        jnp.concatenate([half_of(values, lane, side), ones], axis=1) for side in range(2)
    ]
    inner_sums = [jnp.zeros((1, LANES), jnp.float32) for _ in range(2)]
    low_sums = [jnp.zeros((1, LANES), jnp.float32) for _ in range(2)]
    high_sums = [jnp.zeros((1, LANES), jnp.float32) for _ in range(2)]
    reach_tiles = list(range(layout.query_tiles)) + [-1]

    def put(which, start, stop, result):
        begin = 0
        for ref, size in zip(grad_pair_refs, layout.pieces):
            low, high = max(start, begin), min(stop, begin + size)
            if low < high:
                ref[which, low - begin : high - begin] = result[low - start : high - start]
            begin += size

    for start, stop in row_blocks(length, 384):
        size = stop - start
        grad_key = grad_value = None
        for side in range(2):
            table_row = tables[8 * side : 8 * side + 1]
            scores[0:size] = wide_dot(key_columns[side][start:stop], query_wide[side], NT)
            near = []
            for index, tile in enumerate(reach_tiles):
                place = layout.tile_start(tile)
                if start <= place < stop:
                    near.append((index, tile, place, min(place + LANES, length)))
            for index, tile, place, final in near:
                for slot in range(3):
                    other = tile + slot - 1
                    if not 0 <= other < layout.query_tiles:
                        continue
                    bins = bins_ref[
                        index * LANES : index * LANES + final - place,
                        slot * LANES : (slot + 1) * LANES,
                    ]
                    scores[
                        place - start : final - start, other * LANES : (other + 1) * LANES
                    ] += look_up(table_row, bins)
            probs = jnp.exp2(scores[0:size] * factor)
            grad_probs = wide_dot(value_columns[side][start:stop], grad_wide[side], NT)
            slope = probs * grad_probs
            if near:
                slopes[0:size] = slope
            low = slope.astype(jnp.bfloat16)
            slopes_low[side, start:stop] = low
            part = wide_dot(low, query_half[side])
            grad_key = part if grad_key is None else grad_key + part
            part = wide_dot(probs.astype(jnp.bfloat16), grad_half[side])
            grad_value = part if grad_value is None else grad_value + part
            for index, tile, place, final in near:
                for slot in range(3):
                    other = tile + slot - 1
                    if not 0 <= other < layout.query_tiles:
                        continue
                    bins = bins_ref[
                        index * LANES : index * LANES + final - place,
                        slot * LANES : (slot + 1) * LANES,
                    ]
                    cut = slopes[place - start : final - start, other * LANES : (other + 1) * LANES]
                    low_sums[side] += jnp.sum(
                        jnp.where(bins == 0, cut, 0.0), axis=0, keepdims=True
                    )
                    high_sums[side] += jnp.sum(
                        jnp.where(bins == 2 * (NEAR + 1), cut, 0.0), axis=0, keepdims=True
                    )
                for half in range(2):
                    begin, end = half * 64, min(half * 64 + 64, final - place)
                    if begin >= end:
                        continue
                    base = 0 if tile < 0 else tile - 1 + half
                    where = places_ref[index * LANES + begin : index * LANES + end]
                    spot = where & (LANES - 1)
                    for step in range(2):
                        other = base + step
                        if not 0 <= other < layout.query_tiles or (tile < 0 and step):
                            continue
                        cut = slopes[
                            place - start + begin : place - start + end,
                            other * LANES : (other + 1) * LANES,
                        ]
                        picked = jnp.take_along_axis(cut, spot, axis=1, mode="promise_in_bounds")
                        picked = jnp.where((where >> 7) == step, picked, 0.0)
                        inner_sums[side] += jnp.sum(picked, axis=0, keepdims=True)
        put(0, start, stop, (grad_key * scale).astype(jnp.bfloat16))
        put(1, start, stop, grad_value.astype(jnp.bfloat16))

    grad_query = None
    for side in range(2):
        both = wide_dot(slopes_low[side], key_columns[side], TN)[0:rows]
        part = both[:, :LANES]
        grad_query = part if grad_query is None else grad_query + part
        sums = jnp.where(lane < layout.groups, both[:, LANES:], 0.0)

        def total(kind):
            return jnp.sum(jnp.where(kinds == kind, sums, 0.0))

        right = total(RIGHT) + jnp.sum(high_sums[side])
        left = total(LEFT) + jnp.sum(low_sums[side])
        apart = total(APART)
        grad_table_ref[side : side + 1] = jnp.where(
            lane == 0,
            left,
            jnp.where(
                lane == 2 * (NEAR + 1),
                right,
                jnp.where(lane == 2 * (NEAR + 1) + 1, apart, inner_sums[side]),
            ),
        )
    grad_query_ref[...] = (grad_query * scale).astype(jnp.bfloat16)


def tile_columns(rows, offset=0):
    return pl.BlockSpec((None, rows, LANES), lambda crop, pair: (crop, 0, pair + offset))


def per_crop(rows, width):
    return pl.BlockSpec((None, rows, width), lambda crop, pair: (crop, 0, 0))


def kernel_params():
    return pltpu.CompilerParams(
        vmem_limit_bytes=VMEM_BYTES, dimension_semantics=("arbitrary", "arbitrary")
    )


def attention_forward(layout, scale, projected, key_values, members, kinds, bins, tables):
    crops, rows, _ = projected.shape
    pairs = tables.shape[0]
    specs = [tile_columns(rows)]
    operands = [projected]
    for place in (1, 2):
        for piece in key_values:
            specs.append(tile_columns(piece[0].shape[1], piece[place]))
            operands.append(piece[0])
    specs += [
        per_crop(layout.length, LANES),
        per_crop(rows, LANES),
        per_crop(layout.padded, 3 * LANES),
        pl.BlockSpec((None, 16, LANES), lambda crop, pair: (pair, 0, 0)),
    ]
    flops = 2 * crops * pairs * 2 * rows * layout.length * 256 * 2
    return pl.pallas_call(
        functools.partial(forward_kernel, layout, scale),
        grid=(crops, pairs),
        in_specs=specs,
        out_specs=(tile_columns(rows), per_crop(rows, LANES)),
        out_shape=(
            jax.ShapeDtypeStruct((crops, rows, pairs * LANES), jnp.float32),
            jax.ShapeDtypeStruct((crops, rows, LANES), jnp.float32),
        ),
        scratch_shapes=[pltpu.VMEM((256, layout.wide), jnp.float32)],
        compiler_params=kernel_params(),
        cost_estimate=pl.CostEstimate(
            flops=flops,
            bytes_accessed=12 * crops * rows * pairs * LANES,
            transcendentals=crops * pairs * 2 * rows * layout.length,
        ),
        name="attention_forward",
    )(*operands, members, kinds, bins, tables)


def attention_backward(
    layout,
    scale,
    first_pair,
    pairs,
    projected,
    grad_out,
    attended,
    logs,
    key_values,
    members,
    kinds,
    bins,
    places,
    tables,
):
    crops, rows, _ = projected.shape
    specs = [tile_columns(rows, first_pair)] * 3 + [per_crop(rows, LANES)]
    operands = [projected, grad_out, attended, logs]
    for place in (1, 2):
        for piece in key_values:
            specs.append(tile_columns(piece[0].shape[1], piece[place] + first_pair))
            operands.append(piece[0])
    specs += [
        per_crop(layout.length, LANES),
        per_crop(rows, LANES),
        per_crop(bins.shape[1], 3 * LANES),
        per_crop(places.shape[1], LANES),
        pl.BlockSpec((None, 16, LANES), lambda crop, pair: (pair + first_pair, 0, 0)),
    ]
    out_specs = [tile_columns(rows)]
    out_shapes = [jax.ShapeDtypeStruct((crops, rows, pairs * LANES), jnp.bfloat16)]
    for piece in key_values:
        size = piece[0].shape[1]
        out_specs.append(
            pl.BlockSpec((None, 2, size, LANES), lambda crop, pair: (crop, 0, 0, pair))
        )
        out_shapes.append(jax.ShapeDtypeStruct((crops, 2, size, pairs * LANES), jnp.bfloat16))
    out_specs.append(pl.BlockSpec((None, None, 8, LANES), lambda crop, pair: (crop, pair, 0, 0)))
    out_shapes.append(jax.ShapeDtypeStruct((crops, pairs, 8, LANES), jnp.float32))
    padded, block = layout.padded, 384
    return pl.pallas_call(
        functools.partial(backward_kernel, layout, scale, first_pair),
        grid=(crops, pairs),
        in_specs=specs,
        out_specs=tuple(out_specs),
        out_shape=tuple(out_shapes),
        scratch_shapes=[
            pltpu.VMEM((2, padded, 2 * LANES), jnp.bfloat16),
            pltpu.VMEM((2, padded, 2 * LANES), jnp.bfloat16),
            pltpu.VMEM((2, padded, LANES), jnp.bfloat16),
            pltpu.VMEM((2, padded, LANES), jnp.bfloat16),
            pltpu.VMEM((block, padded), jnp.float32),
            pltpu.VMEM((block, padded), jnp.float32),
            pltpu.VMEM((2, layout.length, padded), jnp.bfloat16),
        ],
        compiler_params=kernel_params(),
        cost_estimate=pl.CostEstimate(
            flops=2 * crops * pairs * 2 * rows * layout.length * 256 * 5,
            bytes_accessed=20 * crops * rows * pairs * LANES,
            transcendentals=crops * pairs * 2 * rows * layout.length,
        ),
        name="attention_backward",
    )(*operands, members, kinds, bins, places, tables)


def sigmoid(values):
    return 1.0 / (1.0 + jnp.exp(-values))


def fold_rows(values):
    return jnp.sum(values.reshape(values.shape[0] // 8, 8, values.shape[1]), axis=0)


def feed_kernel(split, chunks, here_ref, *refs):
    (attended_ref, gate_pre_ref, tokens_ref, upstream_ref, normed_a_ref, mod_ref, output_ref) = refs[:7]
    gate_ref, up_ref, down_ref = refs[7:10]
    layer_ref, grad_middle_ref, grad_att_ref, grad_pre_ref, sums_ref = refs[10:15]
    grads = refs[15:-10]
    gated, grad_ff, normed, branch, middle, total, grad_normed, hidden, both, grad_branch = refs[-10:]
    step = pl.program_id(0)
    here = here_ref[0]
    rows, width = tokens_ref.shape
    size = gate_ref.shape[1]
    strip = 32
    strips = rows // strip
    shift_f, scale_f = mod_ref[3:4], mod_ref[4:5]
    open_a, open_f = sigmoid(mod_ref[2:3]), sigmoid(mod_ref[5:6])

    def strip_of(index):
        return pl.ds(pl.multiple_of(index * strip, strip), strip)

    def norm_of(values):
        mean_value = jnp.mean(values, axis=1, keepdims=True)
        centred = values - mean_value
        spread = jnp.mean(centred * centred, axis=1, keepdims=True)
        root = lax.rsqrt(spread + 1e-06)
        return centred * root, root

    @pl.when(step == 0)
    def _():
        @pl.loop(0, strips)
        def _(index):
            cut = strip_of(index)
            gated[cut] = (attended_ref[cut] * sigmoid(gate_pre_ref[cut])).astype(jnp.bfloat16)
            grad_ff[cut] = (upstream_ref[cut].astype(jnp.float32) * open_f).astype(jnp.bfloat16)

        branch[...] = wide_dot(gated[...], output_ref[...])

        @pl.loop(0, strips)
        def _(index):
            cut = strip_of(index)
            values = tokens_ref[cut].astype(jnp.float32) + open_a * branch[cut]
            middle[cut] = values
            normed[cut] = (norm_of(values)[0] * (1.0 + scale_f) + shift_f).astype(jnp.bfloat16)
            total[cut] = jnp.zeros((strip, width), jnp.float32)
            grad_normed[cut] = jnp.zeros((strip, width), jnp.float32)

    block = rows if rows <= 384 else rows // 2
    for start in range(0, rows, block):
        cut = slice(start, start + block)
        before = wide_dot(normed[cut], gate_ref[...])
        lifted = wide_dot(normed[cut], up_ref[...])
        grad_hidden = wide_dot(grad_ff[cut], down_ref[...], NT)
        switch = sigmoid(before)
        silu = before * switch
        part = (silu * lifted).astype(jnp.bfloat16)
        hidden[cut] = part
        grad_up = (grad_hidden * silu).astype(jnp.bfloat16)
        grad_gate = (grad_hidden * lifted * (switch + silu * (1.0 - switch))).astype(jnp.bfloat16)
        both[cut, :size] = grad_gate
        both[cut, size:] = grad_up
        total[cut] += wide_dot(part, down_ref[...])
        grad_normed[cut] += wide_dot(grad_gate, gate_ref[...], NT) + wide_dot(
            grad_up, up_ref[...], NT
        )

    pair = wide_dot(normed[...], both[...], TN).astype(jnp.bfloat16)
    if split:
        gate_send, gate_keep, up_send, up_keep, down_send, down_keep, small_send, small_keep = grads
        half = width // 2
        away = pl.ds(pl.multiple_of((1 - here) * half, LANES), half)
        home = pl.ds(pl.multiple_of(here * half, LANES), half)
        down_send[...] = wide_dot(hidden[...], grad_ff[:, away], TN).astype(jnp.bfloat16)
        down_keep[...] = wide_dot(hidden[...], grad_ff[:, home], TN).astype(jnp.bfloat16)

        @pl.when(step < chunks // 2)
        def _():
            gate_send[...] = pair[:, :size]
            up_send[...] = pair[:, size:]

        @pl.when(step >= chunks // 2)
        def _():
            gate_keep[...] = pair[:, :size]
            up_keep[...] = pair[:, size:]
    else:
        gate_all, up_all, down_all, small_all = grads
        gate_all[...] = pair[:, :size]
        up_all[...] = pair[:, size:]
        down_all[...] = wide_dot(hidden[...], grad_ff[...], TN).astype(jnp.bfloat16)

    @pl.when(step == chunks - 1)
    def _():
        def finish(index, sums):
            gate_f_sum, shift_sum, scale_sum, gate_a_sum = sums
            cut = strip_of(index)
            values = middle[cut]
            fed = total[cut]
            upstream = upstream_ref[cut].astype(jnp.float32)
            layer_ref[cut] = (values + open_f * fed).astype(jnp.bfloat16)
            normal, root = norm_of(values)
            grad = grad_normed[cut]
            scaled = grad * (1.0 + scale_f)
            grad_middle = upstream + root * (
                scaled
                - jnp.mean(scaled, axis=1, keepdims=True)
                - normal * jnp.mean(scaled * normal, axis=1, keepdims=True)
            )
            grad_middle_ref[cut] = grad_middle
            grad_branch[cut] = (grad_middle * open_a).astype(jnp.bfloat16)
            return (
                gate_f_sum + fold_rows(upstream * fed),
                shift_sum + fold_rows(grad),
                scale_sum + fold_rows(grad * normal),
                gate_a_sum + fold_rows(grad_middle * branch[cut]),
            )

        zero = jnp.zeros((8, width), jnp.float32)
        sums = lax.fori_loop(0, strips, finish, (zero, zero, zero, zero))
        gate_f_sum, shift_sum, scale_sum, gate_a_sum = [
            jnp.sum(value, axis=0, keepdims=True) for value in sums
        ]
        none = jnp.zeros((1, width), jnp.float32)
        sums_ref[...] = jnp.concatenate(
            [
                none,
                none,
                gate_a_sum * open_a * (1.0 - open_a),
                shift_sum,
                scale_sum,
                gate_f_sum * open_f * (1.0 - open_f),
                none,
                none,
            ],
            axis=0,
        )
        total[...] = wide_dot(grad_branch[...], output_ref[...], NT)

        @pl.loop(0, strips)
        def _(index):
            cut = strip_of(index)
            grad_gated = total[cut]
            opened = sigmoid(gate_pre_ref[cut])
            grad_att_ref[cut] = (grad_gated * opened).astype(jnp.bfloat16)
            grad_pre_ref[cut] = (
                grad_gated * attended_ref[cut] * (opened * (1.0 - opened))
            ).astype(jnp.bfloat16)

        if split:
            for side, ref in ((away, small_send), (home, small_keep)):
                ref[:, :half] = wide_dot(gated[...], grad_branch[:, side], TN).astype(jnp.bfloat16)
                ref[:, half:] = wide_dot(normed_a_ref[...], grad_pre_ref[:, side], TN).astype(
                    jnp.bfloat16
                )
        else:
            small_all[:, :width] = wide_dot(gated[...], grad_branch[...], TN).astype(jnp.bfloat16)
            small_all[:, width:] = wide_dot(normed_a_ref[...], grad_pre_ref[...], TN).astype(
                jnp.bfloat16
            )


def feed_layer(
    split, here, attended, gate_pre, tokens, upstream, normed_a, mod_rows, output_weight, feed_gate, feed_up, feed_down
):
    rows, width = tokens.shape
    inner = feed_gate.shape[1]
    size = 512
    chunks = inner // size
    half = chunks // 2

    def turn(step, here_ref):
        return (step + half * (1 - here_ref[0])) % chunks if split else step

    def fixed(shape):
        return pl.BlockSpec(shape, lambda step, here_ref: (0, 0), pipeline_mode=pl.Buffered(1))

    def columns(step, here_ref):
        return (0, turn(step, here_ref))

    def strips(step, here_ref):
        return (turn(step, here_ref), 0)

    whole = (rows, width)
    in_specs = [fixed(whole)] * 5 + [
        fixed((8, width)),
        fixed((width, width)),
        pl.BlockSpec((width, size), columns),
        pl.BlockSpec((width, size), columns),
        pl.BlockSpec((size, width), strips),
    ]
    out_specs = [fixed(whole)] * 4 + [fixed((8, width))]
    bf16, f32 = jnp.bfloat16, jnp.float32
    out_shapes = [(whole, bf16), (whole, f32), (whole, bf16), (whole, bf16), ((8, width), f32)]
    if split:
        first = pl.BlockSpec((width, size), lambda step, here_ref: (0, jnp.minimum(step, half - 1)))
        second = pl.BlockSpec((width, size), lambda step, here_ref: (0, jnp.maximum(step - half, 0)))
        out_specs += [first, second, first, second]
        out_shapes += [((width, inner // 2), bf16)] * 4
        out_specs += [pl.BlockSpec((size, width // 2), strips)] * 2
        out_shapes += [((inner, width // 2), bf16)] * 2
        out_specs += [fixed((width, width))] * 2
        out_shapes += [((width, width), bf16)] * 2
    else:
        out_specs += [pl.BlockSpec((width, size), columns)] * 2
        out_shapes += [((width, inner), bf16)] * 2
        out_specs += [pl.BlockSpec((size, width), strips), fixed((width, 2 * width))]
        out_shapes += [((inner, width), bf16), ((width, 2 * width), bf16)]
    return pl.pallas_call(
        functools.partial(feed_kernel, split, chunks),
        grid_spec=pltpu.PrefetchScalarGridSpec(
            num_scalar_prefetch=1,
            grid=(chunks,),
            in_specs=in_specs,
            out_specs=tuple(out_specs),
            scratch_shapes=[
                pltpu.VMEM(whole, bf16),
                pltpu.VMEM(whole, bf16),
                pltpu.VMEM(whole, bf16),
                pltpu.VMEM(whole, f32),
                pltpu.VMEM(whole, f32),
                pltpu.VMEM(whole, f32),
                pltpu.VMEM(whole, f32),
                pltpu.VMEM((rows, size), bf16),
                pltpu.VMEM((rows, 2 * size), bf16),
                pltpu.VMEM(whole, bf16),
            ],
        ),
        out_shape=tuple(jax.ShapeDtypeStruct(shape, kind) for shape, kind in out_shapes),
        compiler_params=pltpu.CompilerParams(vmem_limit_bytes=VMEM_BYTES),
        cost_estimate=pl.CostEstimate(
            flops=2 * rows * width * (9 * inner + 4 * width),
            bytes_accessed=12 * width * inner + 24 * rows * width,
            transcendentals=2 * rows * inner,
        ),
        name="feed_layer",
    )(
        jnp.reshape(here, (1,)).astype(jnp.int32),
        attended,
        gate_pre,
        tokens,
        upstream,
        normed_a,
        mod_rows,
        output_weight,
        feed_gate,
        feed_up,
        feed_down,
    )


AXES = ("u", "v", "y", "x")
MASKS = {"u": 8, "v": 4, "y": 2, "x": 1}


def exchange(values, mask):
    return lax.ppermute(values, "crop", [(i, i ^ mask) for i in range(16)])


def add_low(former, latter, kind=jnp.bfloat16):
    return (former.astype(jnp.float32) + latter.astype(jnp.float32)).astype(kind)


def swap_res(values):
    return lax.ppermute(values, "res", [(0, 1), (1, 0)])


class Halving:
    def __init__(self, values, order):
        self.left = list(AXES)
        self.order = list(order)
        self.values = values.reshape(2, 2, 2, 2, values.shape[0] // 16, values.shape[1])

    def split(self):
        axis = self.order.pop(0)
        self.mask = MASKS[axis]
        dim = self.left.index(axis)
        self.left.pop(dim)
        bit = (lax.axis_index("crop") // self.mask) % 2
        self.kept = lax.dynamic_index_in_dim(self.values, bit, dim, keepdims=False)
        return lax.dynamic_index_in_dim(self.values, 1 - bit, dim, keepdims=False)

    def send(self, sent):
        return exchange(sent, self.mask)

    def join(self, came):
        self.values = add_low(self.kept, came, jnp.bfloat16 if self.left else jnp.float32)


def advance(streams):
    for stream, came in [(stream, stream.send(stream.split())) for stream in streams]:
        stream.join(came)


def share_columns(values, parts):
    if parts == 1:
        return values.astype(jnp.bfloat16)
    return lax.psum_scatter(values.astype(jnp.bfloat16), "res", scatter_dimension=1, tiled=True)


def scatter_crops(values):
    return lax.psum_scatter(values, "crop", scatter_dimension=0, tiled=True).astype(jnp.float32)


def gather_crops(values, crop_parts):
    if crop_parts != 16:
        return lax.all_gather(values, "crop", axis=0, tiled=True)
    index = lax.axis_index("crop")
    for mask in (1, 2, 4, 8):
        other = exchange(values, mask)
        low = (index // mask) % 2 == 0
        values = jnp.concatenate(
            [jnp.where(low, values, other), jnp.where(low, other, values)], axis=0
        )
    return values


def sum_res(values, parts):
    if parts == 1:
        return values
    if parts != 2:
        return lax.psum(values, "res")
    return values + swap_res(values)


def per_device(
    crop_parts,
    res_parts,
    tokens,
    cotangent,
    time_levels,
    cath_ids,
    residue_numbers,
    chain_mask,
    time_weight,
    label_table,
    modulation_weight,
    projection_weight,
    gate_weight,
    output_weight,
    relative_table,
    pair_gain,
    pair_weight,
    feed_gate,
    feed_up,
    feed_down,
):
    crop_count, row_count, model_width = tokens.shape
    crop_length = residue_numbers.shape[1]
    head_count = pair_weight.shape[1]
    head_width = model_width // head_count
    bin_count = relative_table.shape[0]
    label_count = label_table.shape[0]
    token_count = crop_count * row_count
    score_scale = head_width ** (-0.5)
    pairs = head_count // 2
    layout = Layout(row_count, crop_length)
    query_start = lax.axis_index("res") * row_count

    def conditioning(features, onehot):
        return jnp.dot(features, time_weight, preferred_element_type=jnp.float32) + jnp.dot(
            onehot, label_table, preferred_element_type=jnp.float32
        )

    features = time_features(time_levels, time_weight.shape[0]).astype(jnp.bfloat16)
    label_onehot = (cath_ids[:, None] == jnp.arange(label_count, dtype=jnp.int32)[None, :]).astype(
        jnp.bfloat16
    )
    cond_act = jax.nn.silu(conditioning(features, label_onehot)).astype(jnp.bfloat16)
    modulation = jnp.dot(cond_act, modulation_weight, preferred_element_type=jnp.float32)
    modulation = modulation.reshape(crop_count, 6, 1, model_width)
    shift_a, scale_a = modulation[:, 0], modulation[:, 1]
    mod_rows = pad_to(modulation[:, :, 0], 1, 8, 0.0)

    rotated = lax.dynamic_slice_in_dim(
        jnp.concatenate([jnp.stack([residue_numbers, chain_mask])] * 2, 2), query_start, crop_length, 2
    )
    members, kinds, forward_bins, backward_bins, places = attention_tables(
        layout, rotated[0], rotated[1], query_start, bin_count
    )
    relative_values = relative_table.astype(jnp.float32)
    gain_values = pair_gain.astype(jnp.float32)
    pair_norm = normalize_rows(relative_values, gain_values).astype(jnp.bfloat16)
    bias_rows = jnp.dot(pair_norm, pair_weight, preferred_element_type=jnp.float32)
    tables = head_tables(layout, bias_rows, score_scale)

    token_values = tokens.astype(jnp.float32)
    normed_a = (
        modulate(token_values, shift_a, scale_a)
        .astype(jnp.bfloat16)
        .reshape(token_count, model_width)
    )
    projected = jnp.dot(normed_a, projection_weight, preferred_element_type=jnp.float32).astype(
        jnp.bfloat16
    )
    projected = projected.reshape(crop_count, row_count, 3 * model_width)
    gate_pre = jnp.dot(normed_a, gate_weight, preferred_element_type=jnp.float32)
    gate_pre = gate_pre.reshape(crop_count, row_count, model_width)
    key_values = projected[:, :, model_width:]
    others = [
        lax.ppermute(
            key_values, "res", [((r + step) % res_parts, r) for r in range(res_parts)]
        )
        for step in range(1, res_parts)
    ]
    if len(layout.pieces) == 2:
        other = others[0] if len(others) == 1 else jnp.concatenate(others, axis=1)
        pieces = [(projected, pairs, 2 * pairs), (other, 0, pairs)]
    else:
        pieces = [(jnp.concatenate([key_values] + others, axis=1), 0, pairs)]

    def block_rows(values):
        return pad_to(values, 1, layout.block_rows, 0)

    attended, logs = attention_forward(
        layout,
        score_scale,
        block_rows(projected),
        pieces,
        members,
        kinds,
        forward_bins,
        tables,
    )
    here = lax.axis_index("res")
    split = res_parts == 2 and crop_parts == 16
    per_crop_results = [
        feed_layer(
            split,
            here,
            attended[crop],
            block_rows(gate_pre)[crop],
            block_rows(tokens)[crop],
            block_rows(cotangent)[crop],
            block_rows(normed_a.reshape(tokens.shape))[crop],
            mod_rows[crop],
            output_weight,
            feed_gate,
            feed_up,
            feed_down,
        )
        for crop in range(crop_count)
    ]
    layer_out, grad_middle, grad_attended, grad_gate_pre, feed_sums = (
        jnp.stack([result[place] for result in per_crop_results]) for place in range(5)
    )
    layer_out, grad_middle = layer_out[:, :row_count], grad_middle[:, :row_count]
    grad_gate_pre = grad_gate_pre[:, :row_count].reshape(token_count, model_width)
    weight_grads = [
        sum(result[place].astype(jnp.float32) for result in per_crop_results).astype(jnp.bfloat16)
        if crop_count > 1
        else per_crop_results[0][place]
        for place in range(5, len(per_crop_results[0]))
    ]

    def backward_of(first_pair, count, grad_now):
        return attention_backward(
            layout,
            score_scale,
            first_pair,
            count,
            block_rows(projected),
            grad_now,
            attended,
            logs,
            pieces,
            members,
            kinds,
            backward_bins,
            places,
            tables,
        )

    def own_sum(parts):
        if len(parts) == 2:
            total, away = parts[0].astype(jnp.float32), parts[1]
        else:
            total, away = parts[0][:, :, :row_count].astype(jnp.float32), parts[0][:, :, row_count:]
        for step in range(1, res_parts):
            sent = away[:, :, (step - 1) * row_count : step * row_count]
            pairs_to = [(r, (r + step) % res_parts) for r in range(res_parts)]
            total = total + lax.ppermute(sent, "res", pairs_to).astype(jnp.float32)
        return total.astype(jnp.bfloat16)

    first_count = 2
    if split:
        arrivals = [swap_res(weight_grads[place]) for place in (0, 2, 4, 6)]
        first = backward_of(0, first_count, grad_attended)
        arrivals, grad_attended = lax.optimization_barrier((arrivals, grad_attended))
        kept = [weight_grads[place] for place in (1, 3, 5, 7)]
        sums = [add_low(mine, came) for mine, came in zip(kept, arrivals)]
        streams = [Halving(value, order) for value, order in zip(sums, ("xyvu", "yvxu", "vxyu"))]
        small_stream = Halving(sums[3], "yxvu")
        sent = [stream.split() for stream in streams]
        sent, grad_attended = lax.optimization_barrier((sent, grad_attended))
        came = [stream.send(value) for stream, value in zip(streams, sent)]
        second = backward_of(first_count, pairs - first_count, grad_attended)
        for stream, value in zip(streams, came):
            stream.join(value)
    else:
        first = backward_of(0, first_count, grad_attended)
        second = backward_of(first_count, pairs - first_count, grad_attended)
    grad_query = jnp.concatenate([first[0], second[0]], axis=-1)[:, :row_count]
    grad_pairs = jnp.concatenate([own_sum(first[1:-1]), own_sum(second[1:-1])], axis=-1)
    grad_table = jnp.concatenate([first[-1], second[-1]], axis=1)[:, :, :2].sum(0)
    grad_table = grad_table.reshape(head_count, LANES)
    grad_projected = jnp.concatenate([grad_query, grad_pairs[:, 0], grad_pairs[:, 1]], axis=-1)
    grad_projected = grad_projected.reshape(token_count, 3 * model_width)

    if split:
        width = 3 * model_width // 2

        def projection_half(side):
            columns = lax.dynamic_slice_in_dim(grad_projected, side * width, width, 1)
            return across_rows(normed_a, columns).astype(jnp.bfloat16)

        came = swap_res(projection_half(1 - here))
        projection_sum = add_low(projection_half(here), came)
    grad_normed_a = against_columns(grad_projected, projection_weight) + against_columns(
        grad_gate_pre, gate_weight
    )
    norm_back_a = jax.vjp(modulate, token_values, shift_a, scale_a)[1]
    grad_tokens, grad_shift_a, grad_scale_a = norm_back_a(
        grad_normed_a.reshape(crop_count, row_count, model_width)
    )
    tokens_grad = (grad_middle + grad_tokens).astype(jnp.bfloat16)
    if split:
        cut = 2 * LANES * 3
        streams += [
            small_stream,
            Halving(projection_sum[:, :cut], "xyvu"),
            Halving(projection_sum[:, cut:], "yvxu"),
        ]
        while any(stream.order for stream in streams):
            advance([stream for stream in streams if stream.order])
        feed_gate_grad, feed_up_grad, feed_down_grad, small, left, right = (
            stream.values for stream in streams
        )
        output_weight_grad, gate_weight_grad = (
            small[:, : model_width // 2],
            small[:, model_width // 2 :],
        )
        projection_weight_grad = jnp.concatenate([left, right], axis=1)
    else:
        feed_gate_grad, feed_up_grad, feed_down_grad = (
            scatter_crops(share_columns(value, res_parts)) for value in weight_grads[:3]
        )
        output_weight_grad, gate_weight_grad = (
            scatter_crops(share_columns(value, res_parts))
            for value in (weight_grads[3][:, :model_width], weight_grads[3][:, model_width:])
        )
        projection_weight_grad = scatter_crops(
            share_columns(across_rows(normed_a, grad_projected), res_parts)
        )

    grad_modulation = jnp.concatenate([grad_shift_a, grad_scale_a, feed_sums[:, 2:6]], axis=1)
    grad_modulation = grad_modulation.reshape(crop_count, 6 * model_width)
    table_row = grad_table.reshape(1, head_count * LANES)
    first_row = (jnp.arange(crop_count) == 0).astype(jnp.float32)[:, None]
    small_here = jnp.concatenate([grad_modulation, first_row * table_row], axis=1)
    levels_here = jnp.stack([time_levels, cath_ids.astype(jnp.float32)], axis=1)
    levels_here = pad_to(levels_here, 1, LANES, 0.0)
    small_all = gather_crops(
        jnp.concatenate([levels_here, sum_res(small_here, res_parts)], axis=1), crop_parts
    )
    levels_all, small_all = small_all[:, :2], small_all[:, LANES:]
    grad_modulation = small_all[:, : 6 * model_width]
    grad_table = jnp.sum(small_all[:, 6 * model_width :], axis=0).reshape(head_count, LANES)
    grad_table = grad_table[:, :bin_count]
    features_all = time_features(levels_all[:, 0], time_weight.shape[0]).astype(jnp.bfloat16)
    onehot_all = (
        levels_all[:, 1].astype(jnp.int32)[:, None]
        == jnp.arange(label_count, dtype=jnp.int32)[None, :]
    ).astype(jnp.bfloat16)
    condition = conditioning(features_all, onehot_all)
    cond_act = jax.nn.silu(condition).astype(jnp.bfloat16)
    modulation_weight_grad = split_left(cond_act, grad_modulation, 0, 0)
    grad_condition = split_left(modulation_weight, grad_modulation, 1, 1).T * silu_slope(condition)
    time_weight_grad = split_left(features_all, grad_condition, 0, 0)
    label_table_grad = split_left(onehot_all, grad_condition, 0, 0)
    pair_weight_grad = split_left(pair_norm, grad_table, 0, 1)
    grad_pair_norm = split_right(grad_table, pair_weight, 0, 1)
    pair_back = jax.vjp(normalize_rows, relative_values, gain_values)[1]
    relative_table_grad, pair_gain_grad = pair_back(grad_pair_norm)
    return (
        layer_out,
        tokens_grad,
        time_weight_grad,
        label_table_grad,
        modulation_weight_grad,
        projection_weight_grad,
        gate_weight_grad,
        output_weight_grad,
        relative_table_grad,
        pair_gain_grad,
        pair_weight_grad,
        feed_gate_grad,
        feed_up_grad,
        feed_down_grad,
    )


def solution(mesh):
    return jax.shard_map(
        functools.partial(per_device, mesh.shape["crop"], mesh.shape["res"]),
        mesh=mesh,
        in_specs=(
            P("crop", "res", None),
            P("crop", "res", None),
            P("crop"),
            P("crop"),
            P("crop", None),
            P("crop", None),
            P(),
            P(),
            P(),
            P(),
            P(),
            P(),
            P(),
            P(),
            P(),
            P(),
            P(),
            P(),
        ),
        out_specs=(
            P("crop", "res", None),
            P("crop", "res", None),
            P(),
            P(),
            P(),
            P("crop", "res"),
            P("crop", "res"),
            P("crop", "res"),
            P(),
            P(),
            P(),
            P("crop", "res"),
            P("crop", "res"),
            P("crop", "res"),
        ),
        check_vma=False,
    )
```

```python
import functools
import math

import jax
import jax.numpy as jnp
from jax import lax
from jax.experimental import pallas as pl
from jax.experimental.pallas import tpu as pltpu
from jax.sharding import PartitionSpec as P

LANES = 128
NEAR = 31
VMEM_BYTES = 56 * 1024 * 1024
LOG2E = 1.4426950408889634
NONE, RIGHT, LEFT, APART = 0, 1, 2, 3


def layer_norm(inputs):
    mean_value = jnp.mean(inputs, axis=-1, keepdims=True)
    centred = inputs - mean_value
    spread = jnp.mean(centred * centred, axis=-1, keepdims=True)
    return centred * lax.rsqrt(spread + 1e-06)


def modulate(inputs, shift_row, scale_row):
    return layer_norm(inputs) * (1.0 + scale_row) + shift_row


def normalize_rows(table_rows, gain_row):
    return layer_norm(table_rows) * gain_row


def time_features(time_levels, feature_width):
    half_width = feature_width // 2
    frequency = jnp.exp(-math.log(10000.0) * jnp.arange(half_width, dtype=jnp.float32) / half_width)
    angles = 1000.0 * time_levels[:, None] * frequency[None, :]
    return jnp.concatenate([jnp.sin(angles), jnp.cos(angles)], axis=-1)


def across_rows(former, latter):
    return lax.dot_general(
        former, latter, (((0,), (0,)), ((), ())), preferred_element_type=jnp.float32
    )


def against_columns(former, latter):
    return lax.dot_general(
        former, latter, (((1,), (1,)), ((), ())), preferred_element_type=jnp.float32
    )


def split_parts(values):
    upper = lax.reduce_precision(values, 8, 7)
    return (upper.astype(jnp.bfloat16), (values - upper).astype(jnp.bfloat16))


def split_left(narrow, values, former_dim, latter_dim):
    upper, rest = split_parts(values)
    numbers = (((former_dim,), (latter_dim,)), ((), ()))
    return lax.dot_general(
        narrow, upper, numbers, preferred_element_type=jnp.float32
    ) + lax.dot_general(narrow, rest, numbers, preferred_element_type=jnp.float32)


def split_right(values, narrow, former_dim, latter_dim):
    upper, rest = split_parts(values)
    numbers = (((former_dim,), (latter_dim,)), ((), ()))
    return lax.dot_general(
        upper, narrow, numbers, preferred_element_type=jnp.float32
    ) + lax.dot_general(rest, narrow, numbers, preferred_element_type=jnp.float32)


def sigmoid_slope(inputs):
    gate_value = jax.nn.sigmoid(inputs)
    return gate_value * (1.0 - gate_value)


def silu_slope(inputs):
    gate_value = jax.nn.sigmoid(inputs)
    return gate_value * (1.0 + inputs * (1.0 - gate_value))


class Layout:
    def __init__(self, rows, length):
        self.rows = rows
        self.length = length
        self.query_tiles = -(-rows // LANES)
        self.key_tiles = -(-length // LANES)
        self.padded = self.query_tiles * LANES
        self.wide = self.key_tiles * LANES
        self.last = self.key_tiles - 1
        self.groups = (self.query_tiles + 4) * 4
        assert 2 * self.groups + 3 <= LANES
        assert rows - 1 + NEAR < self.padded and length - NEAR >= self.last * LANES
        assert rows % 8 == 0 and self.last > self.query_tiles
        self.block_rows = rows if rows % 16 == 0 else self.padded
        self.pieces = [rows, length - rows] if rows % 16 == 0 else [length]

    def tile_start(self, tile):
        return self.last * LANES if tile < 0 else tile * LANES


def pad_to(values, axis, size, fill):
    widths = [(0, 0)] * values.ndim
    widths[axis] = (0, size - values.shape[axis])
    return jnp.pad(values, widths, constant_values=fill)


def tables_kernel(layout, bin_count, start_ref, pairs_ref, *out_refs):
    members_ref, kinds_ref, forward_ref, backward_ref, places_ref, codes = out_refs
    rows, length, queries, groups = layout.rows, layout.length, layout.query_tiles, layout.groups
    wrap = length - start_ref[0]
    reach = (bin_count - 2) // 2
    zero_bin = LANES - 1
    shape = (LANES, LANES)
    lane = lax.broadcasted_iota(jnp.int32, shape, 1)
    row = lax.broadcasted_iota(jnp.int32, shape, 0)
    last_start = layout.last * LANES

    tiles = pairs_ref.shape[1]
    marks = pairs_ref[1].astype(jnp.float32)
    place = lax.broadcasted_iota(jnp.int32, marks.shape, 0) * LANES + lax.broadcasted_iota(
        jnp.int32, marks.shape, 1
    )
    before = jnp.sum(jnp.where(place < wrap, marks, 0.0), keepdims=True)
    every = jnp.sum(marks, keepdims=True)
    triangle = jnp.where(row <= lane, 1.0, 0.0).astype(jnp.bfloat16)
    running = jnp.dot(marks.astype(jnp.bfloat16), triangle, preferred_element_type=jnp.float32)
    numbers, chains = [], []
    carry = jnp.zeros((1, 1), jnp.float32)
    for tile in range(layout.key_tiles):
        count = running[tile : tile + 1] + carry
        carry = carry + running[tile : tile + 1, LANES - 1 :]
        count = count + jnp.where(place[tile : tile + 1] < wrap, every - before, -before)
        chains.append(jnp.broadcast_to(count.astype(jnp.int32), shape))
        numbers.append(jnp.broadcast_to(pairs_ref[0, tile : tile + 1], shape))
    number_rows = [value.T for value in numbers]
    chain_rows = [value.T for value in chains]

    def bins_of(key_number, key_chain, query_number, query_chain):
        offset = jnp.clip(key_number - query_number, -reach, reach) + reach
        return jnp.where(key_chain == query_chain, offset, bin_count - 1)

    def touches(query, tile):
        begin = -LANES if tile < 0 else tile * LANES
        return (begin <= query + NEAR) & (query - NEAR <= begin + LANES - 1)

    for tile in range(layout.key_tiles):
        size = min(LANES, length - tile * LANES)
        key = tile * LANES + row
        if tile == layout.last:
            other = jnp.full(shape, queries + 3, jnp.int32)
        elif tile == queries - 1:
            other = jnp.full(shape, queries, jnp.int32)
        else:
            other = jnp.where(key < wrap, queries + 1, queries + 2)
        group = jnp.where(key < rows, tile, other)
        slot = group * 4 + chain_rows[tile] - 1
        hit = (lane == slot) | (lane == slot + groups)
        tail = (lane >= 2 * groups) & (lane < 2 * groups + 3)
        values = jnp.where(hit, 1.0, jnp.where(tail, -1.0, 0.0)).astype(jnp.bfloat16)
        members_ref[tile * LANES : tile * LANES + size] = values[:size]

    local = jnp.where(lane >= groups, lane - groups, lane)
    lane_group = local >> 2
    lane_chain = (local & 3) + 1
    lane_begin = jnp.where(
        lane_group < queries,
        lane_group * LANES,
        jnp.where(lane_group == queries, (queries - 1) * LANES, -LANES),
    )
    has_band = (lane_group <= queries) | (lane_group == queries + 3)
    other_right = jnp.where(
        lane_group == queries,
        rows,
        jnp.where(
            lane_group == queries + 3,
            last_start,
            jnp.where(lane_group == queries + 1, 0, 2 * length),
        ),
    )
    right_limit = jnp.where(lane_group > queries, jnp.where(lane_group == queries + 3, wrap, length), wrap)
    for tile in range(queries):
        size = min(LANES, layout.block_rows - tile * LANES)
        query = tile * LANES + row
        near = (lane_begin <= query + NEAR) & (query - NEAR <= lane_begin + LANES - 1) & has_band
        right = jnp.where(lane_group < queries, lane_group - tile, right_limit - other_right) > 0
        same = chain_rows[tile] == lane_chain
        kinds = jnp.where(same, jnp.where(near, NONE, jnp.where(right, RIGHT, LEFT)), APART)
        kinds = jnp.where((lane < 2 * groups) & (query < rows), kinds, NONE)
        kinds_ref[tile * LANES : tile * LANES + size] = kinds[:size]
        for step in range(3):
            near_tile = tile + step - 1
            index = layout.last if near_tile < 0 else near_tile
            if near_tile < queries:
                inside = touches(query, near_tile) & (query < rows)
                inside &= lane < length - index * LANES
                found = bins_of(
                    numbers[index], chains[index], number_rows[tile], chain_rows[tile]
                )
                found = jnp.where(inside, found, zero_bin)
            else:
                found = jnp.full(shape, zero_bin, jnp.int32)
            forward_ref[
                tile * LANES : (tile + 1) * LANES, step * LANES : (step + 1) * LANES
            ] = found

    codes[...] = jnp.full(codes.shape, -1, jnp.int32)
    for tile in range(queries):
        size = min(LANES, rows - tile * LANES)
        code = number_rows[tile] * 8 + chain_rows[tile]
        codes[(tile + 1) * LANES : (tile + 1) * LANES + size] = code[:size]

    for index, tile in enumerate(list(range(queries)) + [-1]):
        source = layout.last if tile < 0 else tile
        key_row = (row - (length - last_start)) if tile < 0 else tile * LANES + row
        present = row < length - source * LANES
        for step in range(3):
            near_tile = tile + step - 1
            if 0 <= near_tile < queries:
                near_query = near_tile * LANES + lane
                inside = touches(near_query, tile) & (near_query < rows) & present
                found = bins_of(
                    number_rows[source], chain_rows[source], numbers[near_tile], chains[near_tile]
                )
                found = jnp.where(inside, found, zero_bin)
            else:
                found = jnp.full(shape, zero_bin, jnp.int32)
            backward_ref[
                index * LANES : (index + 1) * LANES, step * LANES : (step + 1) * LANES
            ] = found
        target = (number_rows[source] + reach - lane) * 8 + chain_rows[source]
        target = jnp.where(present & (lane > 0) & (lane < 2 * reach), target, -9)
        offset = (LANES - (length - last_start)) if tile < 0 else (tile + 1) * LANES
        far = 4 * LANES
        shift = jnp.full(shape, far, jnp.int32)
        for distance in range(-NEAR, NEAR + 1):
            other = codes[offset - distance : offset - distance + LANES]
            shift = jnp.where(other == target, distance, shift)
        if tile < 0:
            base = jnp.zeros(shape, jnp.int32)
        else:
            base = jnp.where(row < LANES // 2, tile - 1, tile) * LANES
        places_ref[index * LANES : (index + 1) * LANES] = jnp.where(
            shift == far, far - 1, key_row - shift - base
        )


def attention_tables(layout, numbers, marks, query_start, bin_count):
    crops = numbers.shape[0]
    pairs = jnp.stack([numbers, marks], axis=1)
    pairs = pad_to(pairs, 2, layout.wide, 0).reshape(crops, 2, layout.key_tiles, LANES)
    spots = (layout.query_tiles + 1) * LANES
    shapes = [
        ((layout.length, LANES), jnp.bfloat16),
        ((layout.block_rows, LANES), jnp.int32),
        ((layout.padded, 3 * LANES), jnp.int32),
        ((spots, 3 * LANES), jnp.int32),
        ((spots, LANES), jnp.int32),
    ]
    return pl.pallas_call(
        functools.partial(tables_kernel, layout, bin_count),
        grid=(crops,),
        in_specs=[
            pl.BlockSpec(memory_space=pltpu.SMEM),
            pl.BlockSpec((None, 2, layout.key_tiles, LANES), lambda crop: (crop, 0, 0, 0)),
        ],
        out_specs=tuple(pl.BlockSpec((None, *shape), lambda crop: (crop, 0, 0)) for shape, _ in shapes),
        out_shape=tuple(jax.ShapeDtypeStruct((crops, *shape), kind) for shape, kind in shapes),
        scratch_shapes=[pltpu.VMEM((layout.padded + 2 * LANES, LANES), jnp.int32)],
        compiler_params=pltpu.CompilerParams(vmem_limit_bytes=VMEM_BYTES),
        cost_estimate=pl.CostEstimate(
            flops=40000000 * crops, bytes_accessed=4000000 * crops, transcendentals=0
        ),
        name="pair_tables",
    )(jnp.reshape(query_start, (1,)).astype(jnp.int32), pairs)


def head_tables(layout, bias_rows, scale):
    bin_count, heads = bias_rows.shape
    table = (bias_rows - bias_rows[bin_count - 1 :]).T / scale
    lane = jnp.arange(LANES, dtype=jnp.int32)
    groups = layout.groups

    def columns(values):
        upper = lax.reduce_precision(values, 8, 7)
        rest = values - upper
        return jnp.where(
            lane < groups, upper[:, None], jnp.where(lane < 2 * groups, rest[:, None], 0.0)
        )

    lookup = pad_to(table, 1, LANES, 0.0)
    stacked = jnp.stack([lookup, columns(table[:, bin_count - 2]), columns(table[:, 0])], 1)
    stacked = pad_to(stacked, 1, 8, 0.0)
    return stacked.reshape(heads // 2, 16, LANES)


NT = (((1,), (1,)), ((), ()))
TN = (((0,), (0,)), ((), ()))


def wide_dot(former, latter, numbers=(((1,), (0,)), ((), ()))):
    return lax.dot_general(former, latter, numbers, preferred_element_type=jnp.float32)


def look_up(table_row, bins):
    table = jnp.broadcast_to(table_row, bins.shape)
    return jnp.take_along_axis(table, bins, axis=1, mode="promise_in_bounds")


def half_of(values, lane, side):
    return jnp.where((lane >= 64) == (side == 1), values, jnp.zeros_like(values))


def row_blocks(total, size):
    return [(start, min(start + size, total)) for start in range(0, total, size)]


def group_columns(kinds, tables, side):
    right = tables[8 * side + 1 : 8 * side + 2]
    left = tables[8 * side + 2 : 8 * side + 3]
    return jnp.where(kinds == RIGHT, right, jnp.where(kinds == LEFT, left, 0.0))


def forward_kernel(layout, scale, *refs):
    count = len(layout.pieces)
    query_ref = refs[0]
    key_refs = refs[1 : 1 + count]
    value_refs = refs[1 + count : 1 + 2 * count]
    members_ref, kinds_ref, bins_ref, tables_ref, out_ref, log_ref = refs[1 + 2 * count : -1]
    scores = refs[-1]
    pair = pl.program_id(1)
    rows, length = layout.block_rows, layout.length
    factor = scale * LOG2E
    lane = lax.broadcasted_iota(jnp.int32, (1, LANES), 1)
    query = query_ref[...]
    keys = jnp.concatenate([ref[...] for ref in key_refs], axis=0)
    values = jnp.concatenate([ref[...] for ref in value_refs], axis=0)
    members = members_ref[...]
    kinds = kinds_ref[...]
    tables = tables_ref[...]
    ones = jnp.ones((length, LANES), jnp.bfloat16)

    @pl.when(pair == 0)
    def _():
        log_ref[...] = jnp.zeros_like(log_ref)

    for side in range(2):
        key_columns = jnp.concatenate([half_of(keys, lane, side), members], axis=1)
        value_columns = jnp.concatenate([half_of(values, lane, side), ones], axis=1)
        extra = group_columns(kinds, tables, side).astype(jnp.bfloat16)
        query_columns = jnp.concatenate([query, extra], axis=1)
        table_row = tables[8 * side : 8 * side + 1]
        for start, stop in row_blocks(rows, 256):
            size = stop - start
            scores[0:size, 0:length] = wide_dot(query_columns[start:stop], key_columns, NT)
            for tile in range(start // LANES, -(-stop // LANES)):
                first, final = tile * LANES, min(tile * LANES + LANES, rows)
                for slot in range(3):
                    other = tile + slot - 1
                    if other >= layout.query_tiles:
                        continue
                    low, high = first, final
                    if slot == 0:
                        high = min(first + 32, final)
                    if slot == 2:
                        low = first + LANES - 32
                    if low >= high:
                        continue
                    place = layout.tile_start(other)
                    width = min(LANES, length - place)
                    bins = bins_ref[low:high, slot * LANES : (slot + 1) * LANES]
                    bias = look_up(table_row, bins)[:, :width]
                    scores[low - start : high - start, place : place + width] += bias
            block = scores[0:size, 0:length]
            top = jnp.max(block, axis=1, keepdims=True)
            weights = jnp.exp2((block - top) * factor).astype(jnp.bfloat16)
            sums = wide_dot(weights, value_columns)
            total = sums[:, LANES:]
            result = sums[:, :LANES] / total
            if side == 0:
                out_ref[start:stop] = result
            else:
                out_ref[start:stop] += result
            log_total = top + jnp.log(total) * (1.0 / scale)
            log_ref[start:stop] = jnp.where(
                lane == 2 * pair + side, log_total, log_ref[start:stop]
            )


def backward_kernel(layout, scale, first_pair, *refs):
    count = len(layout.pieces)
    query_ref, grad_ref, out_ref, log_ref = refs[:4]
    key_refs = refs[4 : 4 + count]
    value_refs = refs[4 + count : 4 + 2 * count]
    rest = refs[4 + 2 * count :]
    members_ref, kinds_ref, bins_ref, places_ref, tables_ref = rest[:5]
    grad_query_ref = rest[5]
    grad_pair_refs = rest[6 : 6 + count]
    grad_table_ref = rest[6 + count]
    query_wide, grad_wide, query_half, grad_half, scores, slopes, slopes_low = rest[7 + count :]
    pair = pl.program_id(1) + first_pair
    rows, length, padded = layout.block_rows, layout.length, layout.padded
    factor = scale * LOG2E
    lane = lax.broadcasted_iota(jnp.int32, (1, LANES), 1)
    keys = jnp.concatenate([ref[...] for ref in key_refs], axis=0)
    values = jnp.concatenate([ref[...] for ref in value_refs], axis=0)
    members = members_ref[...]
    kinds = kinds_ref[...]
    tables = tables_ref[...]
    query = query_ref[...]
    grad = grad_ref[...]
    grad_full = grad.astype(jnp.float32)
    product = grad_full * out_ref[...]
    log_all = log_ref[...]
    tail = 2 * layout.groups
    ones = jnp.broadcast_to(jnp.where(lane < 3, 1.0, 0.0), (length, LANES)).astype(jnp.bfloat16)

    def three_parts(values):
        upper = values.astype(jnp.bfloat16).astype(jnp.float32)
        values = values - upper
        middle = values.astype(jnp.bfloat16).astype(jnp.float32)
        return upper, middle, values - middle

    def in_lanes(parts, first):
        return jnp.where(
            lane == first,
            parts[0],
            jnp.where(lane == first + 1, parts[1], jnp.where(lane == first + 2, parts[2], 0.0)),
        )

    if padded > rows:
        for ref in (query_wide, grad_wide, query_half, grad_half):
            for side in range(2):
                ref[side, rows:padded] = jnp.zeros((padded - rows, ref.shape[2]), jnp.bfloat16)
    for side in range(2):
        log_total = jnp.sum(
            jnp.where(lane == 2 * pair + side, log_all, 0.0), axis=1, keepdims=True
        )
        extra = group_columns(kinds, tables, side) + in_lanes(three_parts(log_total), tail)
        query_wide[side, 0:rows, 0:LANES] = query
        query_wide[side, 0:rows, LANES:] = extra.astype(jnp.bfloat16)
        delta = jnp.sum(half_of(product, lane, side), axis=1, keepdims=True)
        grad_wide[side, 0:rows, 0:LANES] = grad
        grad_wide[side, 0:rows, LANES:] = in_lanes(three_parts(-delta), 0).astype(jnp.bfloat16)
        query_half[side, 0:rows] = half_of(query, lane, side)
        grad_half[side, 0:rows] = half_of(grad, lane, side)

    key_columns = [
        jnp.concatenate([half_of(keys, lane, side), members], axis=1) for side in range(2)
    ]
    value_columns = [
        jnp.concatenate([half_of(values, lane, side), ones], axis=1) for side in range(2)
    ]
    inner_sums = [jnp.zeros((1, LANES), jnp.float32) for _ in range(2)]
    low_sums = [jnp.zeros((1, LANES), jnp.float32) for _ in range(2)]
    high_sums = [jnp.zeros((1, LANES), jnp.float32) for _ in range(2)]
    reach_tiles = list(range(layout.query_tiles)) + [-1]

    def put(which, start, stop, result):
        begin = 0
        for ref, size in zip(grad_pair_refs, layout.pieces):
            low, high = max(start, begin), min(stop, begin + size)
            if low < high:
                ref[which, low - begin : high - begin] = result[low - start : high - start]
            begin += size

    for start, stop in row_blocks(length, 384):
        size = stop - start
        grad_key = grad_value = None
        for side in range(2):
            table_row = tables[8 * side : 8 * side + 1]
            scores[0:size] = wide_dot(key_columns[side][start:stop], query_wide[side], NT)
            near = []
            for index, tile in enumerate(reach_tiles):
                place = layout.tile_start(tile)
                if start <= place < stop:
                    near.append((index, tile, place, min(place + LANES, length)))
            for index, tile, place, final in near:
                for slot in range(3):
                    other = tile + slot - 1
                    if not 0 <= other < layout.query_tiles:
                        continue
                    bins = bins_ref[
                        index * LANES : index * LANES + final - place,
                        slot * LANES : (slot + 1) * LANES,
                    ]
                    scores[
                        place - start : final - start, other * LANES : (other + 1) * LANES
                    ] += look_up(table_row, bins)
            probs = jnp.exp2(scores[0:size] * factor)
            grad_probs = wide_dot(value_columns[side][start:stop], grad_wide[side], NT)
            slope = probs * grad_probs
            if near:
                slopes[0:size] = slope
            low = slope.astype(jnp.bfloat16)
            slopes_low[side, start:stop] = low
            part = wide_dot(low, query_half[side])
            grad_key = part if grad_key is None else grad_key + part
            part = wide_dot(probs.astype(jnp.bfloat16), grad_half[side])
            grad_value = part if grad_value is None else grad_value + part
            for index, tile, place, final in near:
                for slot in range(3):
                    other = tile + slot - 1
                    if not 0 <= other < layout.query_tiles:
                        continue
                    bins = bins_ref[
                        index * LANES : index * LANES + final - place,
                        slot * LANES : (slot + 1) * LANES,
                    ]
                    cut = slopes[place - start : final - start, other * LANES : (other + 1) * LANES]
                    low_sums[side] += jnp.sum(
                        jnp.where(bins == 0, cut, 0.0), axis=0, keepdims=True
                    )
                    high_sums[side] += jnp.sum(
                        jnp.where(bins == 2 * (NEAR + 1), cut, 0.0), axis=0, keepdims=True
                    )
                for half in range(2):
                    begin, end = half * 64, min(half * 64 + 64, final - place)
                    if begin >= end:
                        continue
                    base = 0 if tile < 0 else tile - 1 + half
                    where = places_ref[index * LANES + begin : index * LANES + end]
                    spot = where & (LANES - 1)
                    for step in range(2):
                        other = base + step
                        if not 0 <= other < layout.query_tiles or (tile < 0 and step):
                            continue
                        cut = slopes[
                            place - start + begin : place - start + end,
                            other * LANES : (other + 1) * LANES,
                        ]
                        picked = jnp.take_along_axis(cut, spot, axis=1, mode="promise_in_bounds")
                        picked = jnp.where((where >> 7) == step, picked, 0.0)
                        inner_sums[side] += jnp.sum(picked, axis=0, keepdims=True)
        put(0, start, stop, (grad_key * scale).astype(jnp.bfloat16))
        put(1, start, stop, grad_value.astype(jnp.bfloat16))

    grad_query = None
    for side in range(2):
        both = wide_dot(slopes_low[side], key_columns[side], TN)[0:rows]
        part = both[:, :LANES]
        grad_query = part if grad_query is None else grad_query + part
        sums = jnp.where(lane < layout.groups, both[:, LANES:], 0.0)

        def total(kind):
            return jnp.sum(jnp.where(kinds == kind, sums, 0.0))

        right = total(RIGHT) + jnp.sum(high_sums[side])
        left = total(LEFT) + jnp.sum(low_sums[side])
        apart = total(APART)
        grad_table_ref[side : side + 1] = jnp.where(
            lane == 0,
            left,
            jnp.where(
                lane == 2 * (NEAR + 1),
                right,
                jnp.where(lane == 2 * (NEAR + 1) + 1, apart, inner_sums[side]),
            ),
        )
    grad_query_ref[...] = (grad_query * scale).astype(jnp.bfloat16)


def tile_columns(rows, offset=0):
    return pl.BlockSpec((None, rows, LANES), lambda crop, pair: (crop, 0, pair + offset))


def per_crop(rows, width):
    return pl.BlockSpec((None, rows, width), lambda crop, pair: (crop, 0, 0))


def kernel_params():
    return pltpu.CompilerParams(
        vmem_limit_bytes=VMEM_BYTES, dimension_semantics=("arbitrary", "arbitrary")
    )


def attention_forward(layout, scale, projected, key_values, members, kinds, bins, tables):
    crops, rows, _ = projected.shape
    pairs = tables.shape[0]
    specs = [tile_columns(rows)]
    operands = [projected]
    for place in (1, 2):
        for piece in key_values:
            specs.append(tile_columns(piece[0].shape[1], piece[place]))
            operands.append(piece[0])
    specs += [
        per_crop(layout.length, LANES),
        per_crop(rows, LANES),
        per_crop(layout.padded, 3 * LANES),
        pl.BlockSpec((None, 16, LANES), lambda crop, pair: (pair, 0, 0)),
    ]
    flops = 2 * crops * pairs * 2 * rows * layout.length * 256 * 2
    return pl.pallas_call(
        functools.partial(forward_kernel, layout, scale),
        grid=(crops, pairs),
        in_specs=specs,
        out_specs=(tile_columns(rows), per_crop(rows, LANES)),
        out_shape=(
            jax.ShapeDtypeStruct((crops, rows, pairs * LANES), jnp.float32),
            jax.ShapeDtypeStruct((crops, rows, LANES), jnp.float32),
        ),
        scratch_shapes=[pltpu.VMEM((256, layout.wide), jnp.float32)],
        compiler_params=kernel_params(),
        cost_estimate=pl.CostEstimate(
            flops=flops,
            bytes_accessed=12 * crops * rows * pairs * LANES,
            transcendentals=crops * pairs * 2 * rows * layout.length,
        ),
        name="attention_forward",
    )(*operands, members, kinds, bins, tables)


def attention_backward(
    layout,
    scale,
    first_pair,
    pairs,
    projected,
    grad_out,
    attended,
    logs,
    key_values,
    members,
    kinds,
    bins,
    places,
    tables,
):
    crops, rows, _ = projected.shape
    specs = [tile_columns(rows, first_pair)] * 3 + [per_crop(rows, LANES)]
    operands = [projected, grad_out, attended, logs]
    for place in (1, 2):
        for piece in key_values:
            specs.append(tile_columns(piece[0].shape[1], piece[place] + first_pair))
            operands.append(piece[0])
    specs += [
        per_crop(layout.length, LANES),
        per_crop(rows, LANES),
        per_crop(bins.shape[1], 3 * LANES),
        per_crop(places.shape[1], LANES),
        pl.BlockSpec((None, 16, LANES), lambda crop, pair: (pair + first_pair, 0, 0)),
    ]
    out_specs = [tile_columns(rows)]
    out_shapes = [jax.ShapeDtypeStruct((crops, rows, pairs * LANES), jnp.bfloat16)]
    for piece in key_values:
        size = piece[0].shape[1]
        out_specs.append(
            pl.BlockSpec((None, 2, size, LANES), lambda crop, pair: (crop, 0, 0, pair))
        )
        out_shapes.append(jax.ShapeDtypeStruct((crops, 2, size, pairs * LANES), jnp.bfloat16))
    out_specs.append(pl.BlockSpec((None, None, 8, LANES), lambda crop, pair: (crop, pair, 0, 0)))
    out_shapes.append(jax.ShapeDtypeStruct((crops, pairs, 8, LANES), jnp.float32))
    padded, block = layout.padded, 384
    return pl.pallas_call(
        functools.partial(backward_kernel, layout, scale, first_pair),
        grid=(crops, pairs),
        in_specs=specs,
        out_specs=tuple(out_specs),
        out_shape=tuple(out_shapes),
        scratch_shapes=[
            pltpu.VMEM((2, padded, 2 * LANES), jnp.bfloat16),
            pltpu.VMEM((2, padded, 2 * LANES), jnp.bfloat16),
            pltpu.VMEM((2, padded, LANES), jnp.bfloat16),
            pltpu.VMEM((2, padded, LANES), jnp.bfloat16),
            pltpu.VMEM((block, padded), jnp.float32),
            pltpu.VMEM((block, padded), jnp.float32),
            pltpu.VMEM((2, layout.length, padded), jnp.bfloat16),
        ],
        compiler_params=kernel_params(),
        cost_estimate=pl.CostEstimate(
            flops=2 * crops * pairs * 2 * rows * layout.length * 256 * 5,
            bytes_accessed=20 * crops * rows * pairs * LANES,
            transcendentals=crops * pairs * 2 * rows * layout.length,
        ),
        name="attention_backward",
    )(*operands, members, kinds, bins, places, tables)


def sigmoid(values):
    return 1.0 / (1.0 + jnp.exp(-values))


def fold_rows(values):
    return jnp.sum(values.reshape(values.shape[0] // 8, 8, values.shape[1]), axis=0)


def feed_kernel(split, chunks, here_ref, *refs):
    (attended_ref, gate_pre_ref, tokens_ref, upstream_ref, normed_a_ref, mod_ref, output_ref) = refs[:7]
    gate_ref, up_ref, down_ref = refs[7:10]
    layer_ref, grad_middle_ref, grad_att_ref, grad_pre_ref, sums_ref = refs[10:15]
    grads = refs[15:-10]
    gated, grad_ff, normed, branch, middle, total, grad_normed, hidden, both, grad_branch = refs[-10:]
    step = pl.program_id(0)
    here = here_ref[0]
    rows, width = tokens_ref.shape
    size = gate_ref.shape[1]
    strip = 32
    strips = rows // strip
    shift_f, scale_f = mod_ref[3:4], mod_ref[4:5]
    open_a, open_f = sigmoid(mod_ref[2:3]), sigmoid(mod_ref[5:6])

    def strip_of(index):
        return pl.ds(pl.multiple_of(index * strip, strip), strip)

    def norm_of(values):
        mean_value = jnp.mean(values, axis=1, keepdims=True)
        centred = values - mean_value
        spread = jnp.mean(centred * centred, axis=1, keepdims=True)
        root = lax.rsqrt(spread + 1e-06)
        return centred * root, root

    @pl.when(step == 0)
    def _():
        @pl.loop(0, strips)
        def _(index):
            cut = strip_of(index)
            gated[cut] = (attended_ref[cut] * sigmoid(gate_pre_ref[cut])).astype(jnp.bfloat16)
            grad_ff[cut] = (upstream_ref[cut].astype(jnp.float32) * open_f).astype(jnp.bfloat16)

        branch[...] = wide_dot(gated[...], output_ref[...])

        @pl.loop(0, strips)
        def _(index):
            cut = strip_of(index)
            values = tokens_ref[cut].astype(jnp.float32) + open_a * branch[cut]
            middle[cut] = values
            normed[cut] = (norm_of(values)[0] * (1.0 + scale_f) + shift_f).astype(jnp.bfloat16)
            total[cut] = jnp.zeros((strip, width), jnp.float32)
            grad_normed[cut] = jnp.zeros((strip, width), jnp.float32)

    block = rows if rows <= 384 else rows // 2
    for start in range(0, rows, block):
        cut = slice(start, start + block)
        before = wide_dot(normed[cut], gate_ref[...])
        lifted = wide_dot(normed[cut], up_ref[...])
        grad_hidden = wide_dot(grad_ff[cut], down_ref[...], NT)
        switch = sigmoid(before)
        silu = before * switch
        part = (silu * lifted).astype(jnp.bfloat16)
        hidden[cut] = part
        grad_up = (grad_hidden * silu).astype(jnp.bfloat16)
        grad_gate = (grad_hidden * lifted * (switch + silu * (1.0 - switch))).astype(jnp.bfloat16)
        both[cut, :size] = grad_gate
        both[cut, size:] = grad_up
        total[cut] += wide_dot(part, down_ref[...])
        grad_normed[cut] += wide_dot(grad_gate, gate_ref[...], NT) + wide_dot(
            grad_up, up_ref[...], NT
        )

    pair = wide_dot(normed[...], both[...], TN).astype(jnp.bfloat16)
    if split:
        gate_send, gate_keep, up_send, up_keep, down_send, down_keep, small_send, small_keep = grads
        half = width // 2
        away = pl.ds(pl.multiple_of((1 - here) * half, LANES), half)
        home = pl.ds(pl.multiple_of(here * half, LANES), half)
        down_send[...] = wide_dot(hidden[...], grad_ff[:, away], TN).astype(jnp.bfloat16)
        down_keep[...] = wide_dot(hidden[...], grad_ff[:, home], TN).astype(jnp.bfloat16)

        @pl.when(step < chunks // 2)
        def _():
            gate_send[...] = pair[:, :size]
            up_send[...] = pair[:, size:]

        @pl.when(step >= chunks // 2)
        def _():
            gate_keep[...] = pair[:, :size]
            up_keep[...] = pair[:, size:]
    else:
        gate_all, up_all, down_all, small_all = grads
        gate_all[...] = pair[:, :size]
        up_all[...] = pair[:, size:]
        down_all[...] = wide_dot(hidden[...], grad_ff[...], TN).astype(jnp.bfloat16)

    @pl.when(step == chunks - 1)
    def _():
        def finish(index, sums):
            gate_f_sum, shift_sum, scale_sum, gate_a_sum = sums
            cut = strip_of(index)
            values = middle[cut]
            fed = total[cut]
            upstream = upstream_ref[cut].astype(jnp.float32)
            layer_ref[cut] = (values + open_f * fed).astype(jnp.bfloat16)
            normal, root = norm_of(values)
            grad = grad_normed[cut]
            scaled = grad * (1.0 + scale_f)
            grad_middle = upstream + root * (
                scaled
                - jnp.mean(scaled, axis=1, keepdims=True)
                - normal * jnp.mean(scaled * normal, axis=1, keepdims=True)
            )
            grad_middle_ref[cut] = grad_middle
            grad_branch[cut] = (grad_middle * open_a).astype(jnp.bfloat16)
            return (
                gate_f_sum + fold_rows(upstream * fed),
                shift_sum + fold_rows(grad),
                scale_sum + fold_rows(grad * normal),
                gate_a_sum + fold_rows(grad_middle * branch[cut]),
            )

        zero = jnp.zeros((8, width), jnp.float32)
        sums = lax.fori_loop(0, strips, finish, (zero, zero, zero, zero))
        gate_f_sum, shift_sum, scale_sum, gate_a_sum = [
            jnp.sum(value, axis=0, keepdims=True) for value in sums
        ]
        none = jnp.zeros((1, width), jnp.float32)
        sums_ref[...] = jnp.concatenate(
            [
                none,
                none,
                gate_a_sum * open_a * (1.0 - open_a),
                shift_sum,
                scale_sum,
                gate_f_sum * open_f * (1.0 - open_f),
                none,
                none,
            ],
            axis=0,
        )
        total[...] = wide_dot(grad_branch[...], output_ref[...], NT)

        @pl.loop(0, strips)
        def _(index):
            cut = strip_of(index)
            grad_gated = total[cut]
            opened = sigmoid(gate_pre_ref[cut])
            grad_att_ref[cut] = (grad_gated * opened).astype(jnp.bfloat16)
            grad_pre_ref[cut] = (
                grad_gated * attended_ref[cut] * (opened * (1.0 - opened))
            ).astype(jnp.bfloat16)

        if split:
            for side, ref in ((away, small_send), (home, small_keep)):
                ref[:, :half] = wide_dot(gated[...], grad_branch[:, side], TN).astype(jnp.bfloat16)
                ref[:, half:] = wide_dot(normed_a_ref[...], grad_pre_ref[:, side], TN).astype(
                    jnp.bfloat16
                )
        else:
            small_all[:, :width] = wide_dot(gated[...], grad_branch[...], TN).astype(jnp.bfloat16)
            small_all[:, width:] = wide_dot(normed_a_ref[...], grad_pre_ref[...], TN).astype(
                jnp.bfloat16
            )


def feed_layer(
    split, here, attended, gate_pre, tokens, upstream, normed_a, mod_rows, output_weight, feed_gate, feed_up, feed_down
):
    rows, width = tokens.shape
    inner = feed_gate.shape[1]
    size = 512
    chunks = inner // size
    half = chunks // 2

    def turn(step, here_ref):
        return (step + half * (1 - here_ref[0])) % chunks if split else step

    def fixed(shape):
        return pl.BlockSpec(shape, lambda step, here_ref: (0, 0), pipeline_mode=pl.Buffered(1))

    def columns(step, here_ref):
        return (0, turn(step, here_ref))

    def strips(step, here_ref):
        return (turn(step, here_ref), 0)

    whole = (rows, width)
    in_specs = [fixed(whole)] * 5 + [
        fixed((8, width)),
        fixed((width, width)),
        pl.BlockSpec((width, size), columns),
        pl.BlockSpec((width, size), columns),
        pl.BlockSpec((size, width), strips),
    ]
    out_specs = [fixed(whole)] * 4 + [fixed((8, width))]
    bf16, f32 = jnp.bfloat16, jnp.float32
    out_shapes = [(whole, bf16), (whole, f32), (whole, bf16), (whole, bf16), ((8, width), f32)]
    if split:
        first = pl.BlockSpec((width, size), lambda step, here_ref: (0, jnp.minimum(step, half - 1)))
        second = pl.BlockSpec((width, size), lambda step, here_ref: (0, jnp.maximum(step - half, 0)))
        out_specs += [first, second, first, second]
        out_shapes += [((width, inner // 2), bf16)] * 4
        out_specs += [pl.BlockSpec((size, width // 2), strips)] * 2
        out_shapes += [((inner, width // 2), bf16)] * 2
        out_specs += [fixed((width, width))] * 2
        out_shapes += [((width, width), bf16)] * 2
    else:
        out_specs += [pl.BlockSpec((width, size), columns)] * 2
        out_shapes += [((width, inner), bf16)] * 2
        out_specs += [pl.BlockSpec((size, width), strips), fixed((width, 2 * width))]
        out_shapes += [((inner, width), bf16), ((width, 2 * width), bf16)]
    return pl.pallas_call(
        functools.partial(feed_kernel, split, chunks),
        grid_spec=pltpu.PrefetchScalarGridSpec(
            num_scalar_prefetch=1,
            grid=(chunks,),
            in_specs=in_specs,
            out_specs=tuple(out_specs),
            scratch_shapes=[
                pltpu.VMEM(whole, bf16),
                pltpu.VMEM(whole, bf16),
                pltpu.VMEM(whole, bf16),
                pltpu.VMEM(whole, f32),
                pltpu.VMEM(whole, f32),
                pltpu.VMEM(whole, f32),
                pltpu.VMEM(whole, f32),
                pltpu.VMEM((rows, size), bf16),
                pltpu.VMEM((rows, 2 * size), bf16),
                pltpu.VMEM(whole, bf16),
            ],
        ),
        out_shape=tuple(jax.ShapeDtypeStruct(shape, kind) for shape, kind in out_shapes),
        compiler_params=pltpu.CompilerParams(vmem_limit_bytes=VMEM_BYTES),
        cost_estimate=pl.CostEstimate(
            flops=2 * rows * width * (9 * inner + 4 * width),
            bytes_accessed=12 * width * inner + 24 * rows * width,
            transcendentals=2 * rows * inner,
        ),
        name="feed_layer",
    )(
        jnp.reshape(here, (1,)).astype(jnp.int32),
        attended,
        gate_pre,
        tokens,
        upstream,
        normed_a,
        mod_rows,
        output_weight,
        feed_gate,
        feed_up,
        feed_down,
    )


MASKS = {"u": 8, "v": 4, "y": 2, "x": 1}


def exchange(values, mask):
    return lax.ppermute(values, "crop", [(i, i ^ mask) for i in range(16)])


def swap_res(values):
    return lax.ppermute(values, "res", [(0, 1), (1, 0)])


def tie(*values):
    return lax.optimization_barrier(values)


def add_low(former, latter, kind=jnp.bfloat16):
    return (former.astype(jnp.float32) + latter.astype(jnp.float32)).astype(kind)


def stage_kernel(part_counts, bits_ref, *refs):
    total = sum(part_counts)
    inputs, outputs = refs[: 4 * total], refs[4 * total :]
    place = 0
    for stream, parts in enumerate(part_counts):
        for side in range(2):
            out_ref = outputs[2 * stream + side]
            column = 0
            for part in range(parts):
                kept_ref, came_ref = inputs[4 * (place + part) + 2 * side :][:2]
                width = kept_ref.shape[-1]
                out_ref[:, :, column : column + width] = add_low(kept_ref[...], came_ref[...])
                column += width
        place += parts


class Halving:
    def __init__(self, orders):
        self.orders = [list(order) for order in orders]
        self.left = [list(MASKS) for _ in orders]

    def stage(self, streams):
        index = lax.axis_index("crop")
        self.masks, bits, places = [], [], []
        for order, left in zip(self.orders, self.left):
            axis = order.pop(0)
            places.append(len(left) - 1 - left.index(axis))
            left.remove(axis)
            self.masks.append(MASKS[axis])
            bits.append((index // MASKS[axis]) % 2)
        bits = jnp.stack(bits).astype(jnp.int32)
        chunks = 2 ** (len(self.left[0]) + 1)
        specs, operands, out_specs, out_shapes = [], [], [], []
        for stream, (parts, place) in enumerate(zip(streams, places)):
            for kept, came, block, width in parts:
                rows = kept.shape[0] // chunks
                for side in range(2):

                    def chunk(step, bits_ref, stream=stream, place=place, side=side, block=block):
                        bit = bits_ref[stream] if side else 1 - bits_ref[stream]
                        low = step & ((1 << place) - 1)
                        return (((step >> place) << (place + 1)) | (bit << place) | low, 0, block)

                    for value in (kept, came):
                        operands.append(value.reshape(chunks, rows, value.shape[1]))
                        specs.append(pl.BlockSpec((1, rows, width), chunk))
            wide = sum(part[3] for part in parts)
            for side in range(2):
                out_specs.append(
                    pl.BlockSpec((1, rows, wide), lambda step, bits_ref: (step, 0, 0))
                )
                out_shapes.append(jax.ShapeDtypeStruct((chunks // 2, rows, wide), jnp.bfloat16))
        results = pl.pallas_call(
            functools.partial(stage_kernel, [len(parts) for parts in streams]),
            grid_spec=pltpu.PrefetchScalarGridSpec(
                num_scalar_prefetch=1,
                grid=(chunks // 2,),
                in_specs=specs,
                out_specs=tuple(out_specs),
            ),
            out_shape=tuple(out_shapes),
            compiler_params=pltpu.CompilerParams(vmem_limit_bytes=24 * 1024 * 1024),
            cost_estimate=pl.CostEstimate(
                flops=sum(4 * math.prod(shape.shape) for shape in out_shapes),
                bytes_accessed=sum(6 * math.prod(shape.shape) for shape in out_shapes),
                transcendentals=0,
            ),
            name="halving_stage",
        )(bits, *operands)
        flat = [value.reshape(-1, value.shape[2]) for value in results]
        return flat[0::2], flat[1::2]

    def send(self, values):
        return [exchange(value, mask) for value, mask in zip(values, self.masks)]


def parts_of(kept, came):
    return [[(mine, other, 0, mine.shape[1])] for mine, other in zip(kept, came)]


def share_columns(values, parts):
    if parts == 1:
        return values.astype(jnp.bfloat16)
    return lax.psum_scatter(values.astype(jnp.bfloat16), "res", scatter_dimension=1, tiled=True)


def scatter_crops(values):
    return lax.psum_scatter(values, "crop", scatter_dimension=0, tiled=True).astype(jnp.float32)


def gather_crops(values, crop_parts):
    if crop_parts != 16:
        return lax.all_gather(values, "crop", axis=0, tiled=True)
    index = lax.axis_index("crop")
    for mask in (1, 2, 4, 8):
        other = exchange(values, mask)
        low = (index // mask) % 2 == 0
        values = jnp.concatenate(
            [jnp.where(low, values, other), jnp.where(low, other, values)], axis=0
        )
    return values


def sum_res(values, parts):
    if parts == 1:
        return values
    if parts != 2:
        return lax.psum(values, "res")
    return values + swap_res(values)


def projection_kernel(counts, here_ref, normed_ref, *refs):
    calls = len(counts)
    parts, (joined_ref, send_ref, keep_ref) = refs[: 3 * calls], refs[3 * calls :]
    width = joined_ref.shape[1] // 3
    column = 0
    for call, pairs in enumerate(counts):
        size = pairs * LANES
        query_ref, own_ref, came_ref = parts[3 * call : 3 * call + 3]
        joined_ref[:, column : column + size] = query_ref[...]
        for which in range(2):
            first = (1 + which) * width + column
            joined_ref[:, first : first + size] = add_low(own_ref[which], came_ref[which])
        column += size
    half = send_ref.shape[1]
    for side, ref in ((1 - here_ref[0], send_ref), (here_ref[0], keep_ref)):
        columns = pl.ds(pl.multiple_of(side * half, LANES), half)
        ref[...] = wide_dot(normed_ref[...], joined_ref[:, columns], TN).astype(jnp.bfloat16)


def projection_gradient(here, normed_a, calls):
    rows, width = normed_a.shape
    counts = [call[0].shape[-1] // LANES for call in calls]
    vmem = pl.BlockSpec(memory_space=pltpu.VMEM)
    return pl.pallas_call(
        functools.partial(projection_kernel, counts),
        in_specs=[pl.BlockSpec(memory_space=pltpu.SMEM)] + [vmem] * (1 + 3 * len(calls)),
        out_specs=(vmem, vmem, vmem),
        out_shape=(
            jax.ShapeDtypeStruct((rows, 3 * width), jnp.bfloat16),
            jax.ShapeDtypeStruct((width, 3 * width // 2), jnp.bfloat16),
            jax.ShapeDtypeStruct((width, 3 * width // 2), jnp.bfloat16),
        ),
        compiler_params=pltpu.CompilerParams(vmem_limit_bytes=40 * 1024 * 1024),
        cost_estimate=pl.CostEstimate(
            flops=6 * rows * width * width, bytes_accessed=24 * rows * width, transcendentals=0
        ),
        name="projection_gradient",
    )(jnp.reshape(here, (1,)).astype(jnp.int32), normed_a, *sum(([*call] for call in calls), []))


def finish_kernel(
    joined_ref, weight_ref, pre_ref, gate_ref, tokens_ref, middle_ref, mod_ref, out_ref, sums_ref, total
):
    step = pl.program_id(0)
    rows, width = tokens_ref.shape
    part = wide_dot(joined_ref[...], weight_ref[...], NT)

    @pl.when(step == 0)
    def _():
        total[...] = part + wide_dot(pre_ref[...], gate_ref[...], NT)

    @pl.when(step > 0)
    def _():
        total[...] += part

    @pl.when(step == pl.num_programs(0) - 1)
    def _():
        strip = 32
        scale = mod_ref[1:2]

        def finish(index, sums):
            shift_sum, scale_sum = sums
            cut = pl.ds(pl.multiple_of(index * strip, strip), strip)
            values = tokens_ref[cut].astype(jnp.float32)
            centred = values - jnp.mean(values, axis=1, keepdims=True)
            root = lax.rsqrt(jnp.mean(centred * centred, axis=1, keepdims=True) + 1e-06)
            normal = centred * root
            grad = total[cut]
            scaled = grad * (1.0 + scale)
            out_ref[cut] = (
                middle_ref[cut]
                + root
                * (
                    scaled
                    - jnp.mean(scaled, axis=1, keepdims=True)
                    - normal * jnp.mean(scaled * normal, axis=1, keepdims=True)
                )
            ).astype(jnp.bfloat16)
            return shift_sum + fold_rows(grad), scale_sum + fold_rows(grad * normal)

        zero = jnp.zeros((8, width), jnp.float32)
        shift_sum, scale_sum = lax.fori_loop(0, rows // strip, finish, (zero, zero))
        sums_ref[0:1] = jnp.sum(shift_sum, axis=0, keepdims=True)
        sums_ref[1:2] = jnp.sum(scale_sum, axis=0, keepdims=True)
        sums_ref[2:8] = jnp.zeros((6, width), jnp.float32)


def finish_layer(joined, weight, grad_pre, gate_weight, tokens, grad_middle, mod_rows):
    rows, width = tokens.shape

    def fixed(shape):
        return pl.BlockSpec(shape, lambda step: (0, 0), pipeline_mode=pl.Buffered(1))

    return pl.pallas_call(
        finish_kernel,
        grid=(3,),
        in_specs=[
            pl.BlockSpec((rows, width), lambda step: (0, step)),
            pl.BlockSpec((width, width), lambda step: (0, step)),
            fixed((rows, width)),
            fixed((width, width)),
            fixed((rows, width)),
            fixed((rows, width)),
            fixed((8, width)),
        ],
        out_specs=(fixed((rows, width)), fixed((8, width))),
        out_shape=(
            jax.ShapeDtypeStruct((rows, width), jnp.bfloat16),
            jax.ShapeDtypeStruct((8, width), jnp.float32),
        ),
        scratch_shapes=[pltpu.VMEM((rows, width), jnp.float32)],
        compiler_params=pltpu.CompilerParams(vmem_limit_bytes=40 * 1024 * 1024),
        cost_estimate=pl.CostEstimate(
            flops=8 * rows * width * width, bytes_accessed=24 * rows * width, transcendentals=0
        ),
        name="finish_layer",
    )(joined, weight, grad_pre, gate_weight, tokens, grad_middle, mod_rows)


def per_device(
    crop_parts,
    res_parts,
    tokens,
    cotangent,
    time_levels,
    cath_ids,
    residue_numbers,
    chain_mask,
    time_weight,
    label_table,
    modulation_weight,
    projection_weight,
    gate_weight,
    output_weight,
    relative_table,
    pair_gain,
    pair_weight,
    feed_gate,
    feed_up,
    feed_down,
):
    crop_count, row_count, model_width = tokens.shape
    crop_length = residue_numbers.shape[1]
    head_count = pair_weight.shape[1]
    head_width = model_width // head_count
    bin_count = relative_table.shape[0]
    label_count = label_table.shape[0]
    token_count = crop_count * row_count
    score_scale = head_width ** (-0.5)
    pairs = head_count // 2
    layout = Layout(row_count, crop_length)
    query_start = lax.axis_index("res") * row_count

    def conditioning(features, onehot):
        return jnp.dot(features, time_weight, preferred_element_type=jnp.float32) + jnp.dot(
            onehot, label_table, preferred_element_type=jnp.float32
        )

    features = time_features(time_levels, time_weight.shape[0]).astype(jnp.bfloat16)
    label_onehot = (cath_ids[:, None] == jnp.arange(label_count, dtype=jnp.int32)[None, :]).astype(
        jnp.bfloat16
    )
    cond_act = jax.nn.silu(conditioning(features, label_onehot)).astype(jnp.bfloat16)
    modulation = jnp.dot(cond_act, modulation_weight, preferred_element_type=jnp.float32)
    modulation = modulation.reshape(crop_count, 6, 1, model_width)
    shift_a, scale_a = modulation[:, 0], modulation[:, 1]
    mod_rows = pad_to(modulation[:, :, 0], 1, 8, 0.0)

    rotated = lax.dynamic_slice_in_dim(
        jnp.concatenate([jnp.stack([residue_numbers, chain_mask])] * 2, 2), query_start, crop_length, 2
    )
    members, kinds, forward_bins, backward_bins, places = attention_tables(
        layout, rotated[0], rotated[1], query_start, bin_count
    )
    relative_values = relative_table.astype(jnp.float32)
    gain_values = pair_gain.astype(jnp.float32)
    pair_norm = normalize_rows(relative_values, gain_values).astype(jnp.bfloat16)
    bias_rows = jnp.dot(pair_norm, pair_weight, preferred_element_type=jnp.float32)
    tables = head_tables(layout, bias_rows, score_scale)

    token_values = tokens.astype(jnp.float32)
    normed_a = (
        modulate(token_values, shift_a, scale_a)
        .astype(jnp.bfloat16)
        .reshape(token_count, model_width)
    )
    projected = jnp.dot(normed_a, projection_weight, preferred_element_type=jnp.float32).astype(
        jnp.bfloat16
    )
    projected = projected.reshape(crop_count, row_count, 3 * model_width)
    gate_pre = jnp.dot(normed_a, gate_weight, preferred_element_type=jnp.float32)
    gate_pre = gate_pre.reshape(crop_count, row_count, model_width)
    key_values = projected[:, :, model_width:]
    others = [
        lax.ppermute(
            key_values, "res", [((r + step) % res_parts, r) for r in range(res_parts)]
        )
        for step in range(1, res_parts)
    ]
    if len(layout.pieces) == 2:
        other = others[0] if len(others) == 1 else jnp.concatenate(others, axis=1)
        pieces = [(projected, pairs, 2 * pairs), (other, 0, pairs)]
    else:
        pieces = [(jnp.concatenate([key_values] + others, axis=1), 0, pairs)]

    def block_rows(values):
        return pad_to(values, 1, layout.block_rows, 0)

    attended, logs = attention_forward(
        layout,
        score_scale,
        block_rows(projected),
        pieces,
        members,
        kinds,
        forward_bins,
        tables,
    )
    here = lax.axis_index("res")
    split = res_parts == 2 and crop_parts == 16 and crop_count == 1
    per_crop_results = [
        feed_layer(
            split,
            here,
            attended[crop],
            block_rows(gate_pre)[crop],
            block_rows(tokens)[crop],
            block_rows(cotangent)[crop],
            block_rows(normed_a.reshape(tokens.shape))[crop],
            mod_rows[crop],
            output_weight,
            feed_gate,
            feed_up,
            feed_down,
        )
        for crop in range(crop_count)
    ]
    layer_out, grad_middle, grad_attended, grad_gate_pre, feed_sums = (
        jnp.stack([result[place] for result in per_crop_results]) for place in range(5)
    )
    layer_out, grad_middle = layer_out[:, :row_count], grad_middle[:, :row_count]
    grad_gate_pre = grad_gate_pre[:, :row_count].reshape(token_count, model_width)
    weight_grads = [
        sum(result[place].astype(jnp.float32) for result in per_crop_results).astype(jnp.bfloat16)
        if crop_count > 1
        else per_crop_results[0][place]
        for place in range(5, len(per_crop_results[0]))
    ]

    def backward_of(first_pair, count, grad_now):
        return attention_backward(
            layout,
            score_scale,
            first_pair,
            count,
            block_rows(projected),
            grad_now,
            attended,
            logs,
            pieces,
            members,
            kinds,
            backward_bins,
            places,
            tables,
        )

    if split:
        arrivals = [swap_res(weight_grads[place]) for place in (0, 2, 4, 6)]
        kept = [weight_grads[place] for place in (1, 3, 5, 7)]
        halving = Halving(["xyvu", "yvxu", "vxyu"])
        half = model_width // 2
        calls = [list(backward_of(0, 1, grad_attended))]
        arrivals, calls[0] = tie(arrivals, calls[0])
        (gate_w, up_w, down_w, small_w) = zip(kept, arrivals)
        streams = [
            [(*gate_w, 0, gate_w[0].shape[1]), (*small_w, 0, half)],
            [(*up_w, 0, up_w[0].shape[1]), (*small_w, 1, half)],
            [(*down_w, 0, half)],
        ]
        for first_pair, count in ((1, 3), (4, 2)):
            sent, kept = halving.stage(streams)
            sent, grad_attended = tie(sent, grad_attended)
            came = halving.send(sent)
            calls.append(list(backward_of(first_pair, count, grad_attended)))
            came, calls[-1] = tie(came, calls[-1])
            streams = parts_of(kept, came)
        grad_table = jnp.concatenate([call[-1] for call in calls], axis=1)
        sent, kept = halving.stage(streams)
        came = halving.send(sent)
        joined, proj_send, proj_keep = projection_gradient(
            here, normed_a, [(call[0][0], call[1][0], swap_res(call[2][0])) for call in calls]
        )
        proj_came = swap_res(proj_send)
        tokens_grad, norm_sums = finish_layer(
            joined,
            projection_weight,
            grad_gate_pre,
            gate_weight,
            tokens[0],
            grad_middle[0],
            mod_rows[0],
        )
        tokens_grad = tokens_grad[None]
        grad_shift_a, grad_scale_a = norm_sums[None, 0:1], norm_sums[None, 1:2]
        sent, kept = halving.stage(parts_of(kept, came))
        came = halving.send(sent)
        last = Halving(["xyvu", "yvxu"])
        streams = [[(proj_keep, proj_came, 0, 2 * half)], [(proj_keep, proj_came, 2, half)]]
        for _ in range(4):
            last_sent, last_kept = last.stage(streams)
            last_came = last.send(last_sent)
            streams = parts_of(last_kept, last_came)
        gate_and_out, up_and_gate, feed_down_grad = (
            add_low(mine, other, jnp.float32) for mine, other in zip(kept, came)
        )
        inner = feed_gate.shape[1] // 2
        feed_gate_grad, output_weight_grad = gate_and_out[:, :inner], gate_and_out[:, inner:]
        feed_up_grad, gate_weight_grad = up_and_gate[:, :inner], up_and_gate[:, inner:]
        projection_weight_grad = jnp.concatenate(
            [add_low(mine, other, jnp.float32) for mine, other in zip(last_kept, last_came)], axis=1
        )
    else:
        results = backward_of(0, pairs, grad_attended)
        grad_table = results[-1]
        grad_pairs = results[1:-1]
        if len(grad_pairs) == 2:
            total, away = grad_pairs[0].astype(jnp.float32), grad_pairs[1]
        else:
            total = grad_pairs[0][:, :, :row_count].astype(jnp.float32)
            away = grad_pairs[0][:, :, row_count:]
        for step in range(1, res_parts):
            sent = away[:, :, (step - 1) * row_count : step * row_count]
            pairs_to = [(r, (r + step) % res_parts) for r in range(res_parts)]
            total = total + lax.ppermute(sent, "res", pairs_to).astype(jnp.float32)
        total = total.astype(jnp.bfloat16)
        grad_projected = jnp.concatenate(
            [results[0][:, :row_count], total[:, 0], total[:, 1]], axis=-1
        ).reshape(token_count, 3 * model_width)
        grad_normed_a = against_columns(grad_projected, projection_weight) + against_columns(
            grad_gate_pre, gate_weight
        )
        norm_back_a = jax.vjp(modulate, token_values, shift_a, scale_a)[1]
        grad_tokens, grad_shift_a, grad_scale_a = norm_back_a(
            grad_normed_a.reshape(crop_count, row_count, model_width)
        )
        tokens_grad = (grad_middle + grad_tokens).astype(jnp.bfloat16)
        feed_gate_grad, feed_up_grad, feed_down_grad = (
            scatter_crops(share_columns(value, res_parts)) for value in weight_grads[:3]
        )
        output_weight_grad, gate_weight_grad = (
            scatter_crops(share_columns(value, res_parts))
            for value in (weight_grads[3][:, :model_width], weight_grads[3][:, model_width:])
        )
        projection_weight_grad = scatter_crops(
            share_columns(across_rows(normed_a, grad_projected), res_parts)
        )
    grad_table = grad_table[:, :, :2].sum(0).reshape(head_count, LANES)

    grad_modulation = jnp.concatenate([grad_shift_a, grad_scale_a, feed_sums[:, 2:6]], axis=1)
    grad_modulation = grad_modulation.reshape(crop_count, 6 * model_width)
    table_row = grad_table.reshape(1, head_count * LANES)
    first_row = (jnp.arange(crop_count) == 0).astype(jnp.float32)[:, None]
    small_here = jnp.concatenate([grad_modulation, first_row * table_row], axis=1)
    levels_here = jnp.stack([time_levels, cath_ids.astype(jnp.float32)], axis=1)
    levels_here = pad_to(levels_here, 1, LANES, 0.0)
    small_all = gather_crops(
        jnp.concatenate([levels_here, sum_res(small_here, res_parts)], axis=1), crop_parts
    )
    levels_all, small_all = small_all[:, :2], small_all[:, LANES:]
    grad_modulation = small_all[:, : 6 * model_width]
    grad_table = jnp.sum(small_all[:, 6 * model_width :], axis=0).reshape(head_count, LANES)
    grad_table = grad_table[:, :bin_count]
    features_all = time_features(levels_all[:, 0], time_weight.shape[0]).astype(jnp.bfloat16)
    onehot_all = (
        levels_all[:, 1].astype(jnp.int32)[:, None]
        == jnp.arange(label_count, dtype=jnp.int32)[None, :]
    ).astype(jnp.bfloat16)
    condition = conditioning(features_all, onehot_all)
    cond_act = jax.nn.silu(condition).astype(jnp.bfloat16)
    modulation_weight_grad = split_left(cond_act, grad_modulation, 0, 0)
    grad_condition = split_left(modulation_weight, grad_modulation, 1, 1).T * silu_slope(condition)
    time_weight_grad = split_left(features_all, grad_condition, 0, 0)
    label_table_grad = split_left(onehot_all, grad_condition, 0, 0)
    pair_weight_grad = split_left(pair_norm, grad_table, 0, 1)
    grad_pair_norm = split_right(grad_table, pair_weight, 0, 1)
    pair_back = jax.vjp(normalize_rows, relative_values, gain_values)[1]
    relative_table_grad, pair_gain_grad = pair_back(grad_pair_norm)
    return (
        layer_out,
        tokens_grad,
        time_weight_grad,
        label_table_grad,
        modulation_weight_grad,
        projection_weight_grad,
        gate_weight_grad,
        output_weight_grad,
        relative_table_grad,
        pair_gain_grad,
        pair_weight_grad,
        feed_gate_grad,
        feed_up_grad,
        feed_down_grad,
    )


def solution(mesh):
    return jax.shard_map(
        functools.partial(per_device, mesh.shape["crop"], mesh.shape["res"]),
        mesh=mesh,
        in_specs=(
            P("crop", "res", None),
            P("crop", "res", None),
            P("crop"),
            P("crop"),
            P("crop", None),
            P("crop", None),
            P(),
            P(),
            P(),
            P(),
            P(),
            P(),
            P(),
            P(),
            P(),
            P(),
            P(),
            P(),
        ),
        out_specs=(
            P("crop", "res", None),
            P("crop", "res", None),
            P(),
            P(),
            P(),
            P("crop", "res"),
            P("crop", "res"),
            P("crop", "res"),
            P(),
            P(),
            P(),
            P("crop", "res"),
            P("crop", "res"),
            P("crop", "res"),
        ),
        check_vma=False,
    )
```

```python
import functools
import math

import jax
import jax.numpy as jnp
from jax import lax
from jax.experimental import pallas as pl
from jax.experimental.pallas import tpu as pltpu
from jax.sharding import PartitionSpec as P

LANES = 128
NEAR = 31
VMEM_BYTES = 56 * 1024 * 1024
LOG2E = 1.4426950408889634
NONE, RIGHT, LEFT, APART = 0, 1, 2, 3


def layer_norm(inputs):
    mean_value = jnp.mean(inputs, axis=-1, keepdims=True)
    centred = inputs - mean_value
    spread = jnp.mean(centred * centred, axis=-1, keepdims=True)
    return centred * lax.rsqrt(spread + 1e-06)


def modulate(inputs, shift_row, scale_row):
    return layer_norm(inputs) * (1.0 + scale_row) + shift_row


def normalize_rows(table_rows, gain_row):
    return layer_norm(table_rows) * gain_row


def time_features(time_levels, feature_width):
    half_width = feature_width // 2
    frequency = jnp.exp(-math.log(10000.0) * jnp.arange(half_width, dtype=jnp.float32) / half_width)
    angles = 1000.0 * time_levels[:, None] * frequency[None, :]
    return jnp.concatenate([jnp.sin(angles), jnp.cos(angles)], axis=-1)


def across_rows(former, latter):
    return lax.dot_general(
        former, latter, (((0,), (0,)), ((), ())), preferred_element_type=jnp.float32
    )


def against_columns(former, latter):
    return lax.dot_general(
        former, latter, (((1,), (1,)), ((), ())), preferred_element_type=jnp.float32
    )


def split_parts(values):
    upper = lax.reduce_precision(values, 8, 7)
    return (upper.astype(jnp.bfloat16), (values - upper).astype(jnp.bfloat16))


def split_left(narrow, values, former_dim, latter_dim):
    upper, rest = split_parts(values)
    numbers = (((former_dim,), (latter_dim,)), ((), ()))
    return lax.dot_general(
        narrow, upper, numbers, preferred_element_type=jnp.float32
    ) + lax.dot_general(narrow, rest, numbers, preferred_element_type=jnp.float32)


def split_right(values, narrow, former_dim, latter_dim):
    upper, rest = split_parts(values)
    numbers = (((former_dim,), (latter_dim,)), ((), ()))
    return lax.dot_general(
        upper, narrow, numbers, preferred_element_type=jnp.float32
    ) + lax.dot_general(rest, narrow, numbers, preferred_element_type=jnp.float32)


def sigmoid_slope(inputs):
    gate_value = jax.nn.sigmoid(inputs)
    return gate_value * (1.0 - gate_value)


def silu_slope(inputs):
    gate_value = jax.nn.sigmoid(inputs)
    return gate_value * (1.0 + inputs * (1.0 - gate_value))


class Layout:
    def __init__(self, rows, length):
        self.rows = rows
        self.length = length
        self.query_tiles = -(-rows // LANES)
        self.key_tiles = -(-length // LANES)
        self.padded = self.query_tiles * LANES
        self.wide = self.key_tiles * LANES
        self.last = self.key_tiles - 1
        self.groups = (self.query_tiles + 4) * 4
        assert 2 * self.groups + 3 <= LANES
        assert rows - 1 + NEAR < self.padded and length - NEAR >= self.last * LANES
        assert rows % 8 == 0 and self.last > self.query_tiles
        self.block_rows = rows if rows % 16 == 0 else self.padded
        self.pieces = [rows, length - rows] if rows % 16 == 0 else [length]

    def tile_start(self, tile):
        return self.last * LANES if tile < 0 else tile * LANES


def pad_to(values, axis, size, fill):
    widths = [(0, 0)] * values.ndim
    widths[axis] = (0, size - values.shape[axis])
    return jnp.pad(values, widths, constant_values=fill)


def tables_kernel(layout, bin_count, start_ref, pairs_ref, *out_refs):
    members_ref, kinds_ref, forward_ref, backward_ref, places_ref, codes = out_refs
    rows, length, queries, groups = layout.rows, layout.length, layout.query_tiles, layout.groups
    wrap = length - start_ref[0]
    reach = (bin_count - 2) // 2
    zero_bin = LANES - 1
    shape = (LANES, LANES)
    lane = lax.broadcasted_iota(jnp.int32, shape, 1)
    row = lax.broadcasted_iota(jnp.int32, shape, 0)
    last_start = layout.last * LANES

    tiles = pairs_ref.shape[1]
    marks = pairs_ref[1].astype(jnp.float32)
    place = lax.broadcasted_iota(jnp.int32, marks.shape, 0) * LANES + lax.broadcasted_iota(
        jnp.int32, marks.shape, 1
    )
    before = jnp.sum(jnp.where(place < wrap, marks, 0.0), keepdims=True)
    every = jnp.sum(marks, keepdims=True)
    triangle = jnp.where(row <= lane, 1.0, 0.0).astype(jnp.bfloat16)
    running = jnp.dot(marks.astype(jnp.bfloat16), triangle, preferred_element_type=jnp.float32)
    numbers, chains = [], []
    carry = jnp.zeros((1, 1), jnp.float32)
    for tile in range(layout.key_tiles):
        count = running[tile : tile + 1] + carry
        carry = carry + running[tile : tile + 1, LANES - 1 :]
        count = count + jnp.where(place[tile : tile + 1] < wrap, every - before, -before)
        chains.append(jnp.broadcast_to(count.astype(jnp.int32), shape))
        numbers.append(jnp.broadcast_to(pairs_ref[0, tile : tile + 1], shape))
    number_rows = [value.T for value in numbers]
    chain_rows = [value.T for value in chains]

    def bins_of(key_number, key_chain, query_number, query_chain):
        offset = jnp.clip(key_number - query_number, -reach, reach) + reach
        return jnp.where(key_chain == query_chain, offset, bin_count - 1)

    def touches(query, tile):
        begin = -LANES if tile < 0 else tile * LANES
        return (begin <= query + NEAR) & (query - NEAR <= begin + LANES - 1)

    for tile in range(layout.key_tiles):
        size = min(LANES, length - tile * LANES)
        key = tile * LANES + row
        if tile == layout.last:
            other = jnp.full(shape, queries + 3, jnp.int32)
        elif tile == queries - 1:
            other = jnp.full(shape, queries, jnp.int32)
        else:
            other = jnp.where(key < wrap, queries + 1, queries + 2)
        group = jnp.where(key < rows, tile, other)
        slot = group * 4 + chain_rows[tile] - 1
        hit = (lane == slot) | (lane == slot + groups)
        tail = (lane >= 2 * groups) & (lane < 2 * groups + 3)
        values = jnp.where(hit, 1.0, jnp.where(tail, -1.0, 0.0)).astype(jnp.bfloat16)
        members_ref[tile * LANES : tile * LANES + size] = values[:size]

    local = jnp.where(lane >= groups, lane - groups, lane)
    lane_group = local >> 2
    lane_chain = (local & 3) + 1
    lane_begin = jnp.where(
        lane_group < queries,
        lane_group * LANES,
        jnp.where(lane_group == queries, (queries - 1) * LANES, -LANES),
    )
    has_band = (lane_group <= queries) | (lane_group == queries + 3)
    other_right = jnp.where(
        lane_group == queries,
        rows,
        jnp.where(
            lane_group == queries + 3,
            last_start,
            jnp.where(lane_group == queries + 1, 0, 2 * length),
        ),
    )
    right_limit = jnp.where(lane_group > queries, jnp.where(lane_group == queries + 3, wrap, length), wrap)
    for tile in range(queries):
        size = min(LANES, layout.block_rows - tile * LANES)
        query = tile * LANES + row
        near = (lane_begin <= query + NEAR) & (query - NEAR <= lane_begin + LANES - 1) & has_band
        right = jnp.where(lane_group < queries, lane_group - tile, right_limit - other_right) > 0
        same = chain_rows[tile] == lane_chain
        kinds = jnp.where(same, jnp.where(near, NONE, jnp.where(right, RIGHT, LEFT)), APART)
        kinds = jnp.where((lane < 2 * groups) & (query < rows), kinds, NONE)
        kinds_ref[tile * LANES : tile * LANES + size] = kinds[:size]
        for step in range(3):
            near_tile = tile + step - 1
            index = layout.last if near_tile < 0 else near_tile
            if near_tile < queries:
                inside = touches(query, near_tile) & (query < rows)
                inside &= lane < length - index * LANES
                found = bins_of(
                    numbers[index], chains[index], number_rows[tile], chain_rows[tile]
                )
                found = jnp.where(inside, found, zero_bin)
            else:
                found = jnp.full(shape, zero_bin, jnp.int32)
            forward_ref[
                tile * LANES : (tile + 1) * LANES, step * LANES : (step + 1) * LANES
            ] = found

    codes[...] = jnp.full(codes.shape, -1, jnp.int32)
    for tile in range(queries):
        size = min(LANES, rows - tile * LANES)
        code = number_rows[tile] * 8 + chain_rows[tile]
        codes[(tile + 1) * LANES : (tile + 1) * LANES + size] = code[:size]

    for index, tile in enumerate(list(range(queries)) + [-1]):
        source = layout.last if tile < 0 else tile
        key_row = (row - (length - last_start)) if tile < 0 else tile * LANES + row
        present = row < length - source * LANES
        for step in range(3):
            near_tile = tile + step - 1
            if 0 <= near_tile < queries:
                near_query = near_tile * LANES + lane
                inside = touches(near_query, tile) & (near_query < rows) & present
                found = bins_of(
                    number_rows[source], chain_rows[source], numbers[near_tile], chains[near_tile]
                )
                found = jnp.where(inside, found, zero_bin)
            else:
                found = jnp.full(shape, zero_bin, jnp.int32)
            backward_ref[
                index * LANES : (index + 1) * LANES, step * LANES : (step + 1) * LANES
            ] = found
        target = (number_rows[source] + reach - lane) * 8 + chain_rows[source]
        target = jnp.where(present & (lane > 0) & (lane < 2 * reach), target, -9)
        offset = (LANES - (length - last_start)) if tile < 0 else (tile + 1) * LANES
        far = 4 * LANES
        shift = jnp.full(shape, far, jnp.int32)
        for distance in range(-NEAR, NEAR + 1):
            other = codes[offset - distance : offset - distance + LANES]
            shift = jnp.where(other == target, distance, shift)
        if tile < 0:
            base = jnp.zeros(shape, jnp.int32)
        else:
            base = jnp.where(row < LANES // 2, tile - 1, tile) * LANES
        places_ref[index * LANES : (index + 1) * LANES] = jnp.where(
            shift == far, far - 1, key_row - shift - base
        )


def attention_tables(layout, numbers, marks, query_start, bin_count):
    crops = numbers.shape[0]
    pairs = jnp.stack([numbers, marks], axis=1)
    pairs = pad_to(pairs, 2, layout.wide, 0).reshape(crops, 2, layout.key_tiles, LANES)
    spots = (layout.query_tiles + 1) * LANES
    shapes = [
        ((layout.length, LANES), jnp.bfloat16),
        ((layout.block_rows, LANES), jnp.int32),
        ((layout.padded, 3 * LANES), jnp.int32),
        ((spots, 3 * LANES), jnp.int32),
        ((spots, LANES), jnp.int32),
    ]
    return pl.pallas_call(
        functools.partial(tables_kernel, layout, bin_count),
        grid=(crops,),
        in_specs=[
            pl.BlockSpec(memory_space=pltpu.SMEM),
            pl.BlockSpec((None, 2, layout.key_tiles, LANES), lambda crop: (crop, 0, 0, 0)),
        ],
        out_specs=tuple(pl.BlockSpec((None, *shape), lambda crop: (crop, 0, 0)) for shape, _ in shapes),
        out_shape=tuple(jax.ShapeDtypeStruct((crops, *shape), kind) for shape, kind in shapes),
        scratch_shapes=[pltpu.VMEM((layout.padded + 2 * LANES, LANES), jnp.int32)],
        compiler_params=pltpu.CompilerParams(vmem_limit_bytes=VMEM_BYTES),
        cost_estimate=pl.CostEstimate(
            flops=40000000 * crops, bytes_accessed=4000000 * crops, transcendentals=0
        ),
        name="pair_tables",
    )(jnp.reshape(query_start, (1,)).astype(jnp.int32), pairs)


def head_tables(layout, bias_rows, scale):
    bin_count, heads = bias_rows.shape
    table = (bias_rows - bias_rows[bin_count - 1 :]).T / scale
    lane = jnp.arange(LANES, dtype=jnp.int32)
    groups = layout.groups

    def columns(values):
        upper = lax.reduce_precision(values, 8, 7)
        rest = values - upper
        return jnp.where(
            lane < groups, upper[:, None], jnp.where(lane < 2 * groups, rest[:, None], 0.0)
        )

    lookup = pad_to(table, 1, LANES, 0.0)
    stacked = jnp.stack([lookup, columns(table[:, bin_count - 2]), columns(table[:, 0])], 1)
    stacked = pad_to(stacked, 1, 8, 0.0)
    return stacked.reshape(heads // 2, 16, LANES)


NT = (((1,), (1,)), ((), ()))
TN = (((0,), (0,)), ((), ()))


def wide_dot(former, latter, numbers=(((1,), (0,)), ((), ()))):
    return lax.dot_general(former, latter, numbers, preferred_element_type=jnp.float32)


def look_up(table_row, bins):
    table = jnp.broadcast_to(table_row, bins.shape)
    return jnp.take_along_axis(table, bins, axis=1, mode="promise_in_bounds")


def half_of(values, lane, side):
    return jnp.where((lane >= 64) == (side == 1), values, jnp.zeros_like(values))


def row_blocks(total, size):
    return [(start, min(start + size, total)) for start in range(0, total, size)]


def group_columns(kinds, tables, side):
    right = tables[8 * side + 1 : 8 * side + 2]
    left = tables[8 * side + 2 : 8 * side + 3]
    return jnp.where(kinds == RIGHT, right, jnp.where(kinds == LEFT, left, 0.0))


def forward_kernel(layout, scale, *refs):
    count = len(layout.pieces)
    query_ref = refs[0]
    key_refs = refs[1 : 1 + count]
    value_refs = refs[1 + count : 1 + 2 * count]
    members_ref, kinds_ref, bins_ref, tables_ref, out_ref, log_ref = refs[1 + 2 * count : -1]
    scores = refs[-1]
    pair = pl.program_id(1)
    rows, length = layout.block_rows, layout.length
    factor = scale * LOG2E
    lane = lax.broadcasted_iota(jnp.int32, (1, LANES), 1)
    query = query_ref[...]
    keys = jnp.concatenate([ref[...] for ref in key_refs], axis=0)
    values = jnp.concatenate([ref[...] for ref in value_refs], axis=0)
    members = members_ref[...]
    kinds = kinds_ref[...]
    tables = tables_ref[...]
    ones = jnp.ones((length, LANES), jnp.bfloat16)

    @pl.when(pair == 0)
    def _():
        log_ref[...] = jnp.zeros_like(log_ref)

    for side in range(2):
        key_columns = jnp.concatenate([half_of(keys, lane, side), members], axis=1)
        value_columns = jnp.concatenate([half_of(values, lane, side), ones], axis=1)
        extra = group_columns(kinds, tables, side).astype(jnp.bfloat16)
        query_columns = jnp.concatenate([query, extra], axis=1)
        table_row = tables[8 * side : 8 * side + 1]
        for start, stop in row_blocks(rows, 256):
            size = stop - start
            scores[0:size, 0:length] = wide_dot(query_columns[start:stop], key_columns, NT)
            for tile in range(start // LANES, -(-stop // LANES)):
                first, final = tile * LANES, min(tile * LANES + LANES, rows)
                for slot in range(3):
                    other = tile + slot - 1
                    if other >= layout.query_tiles:
                        continue
                    low, high = first, final
                    if slot == 0:
                        high = min(first + 32, final)
                    if slot == 2:
                        low = first + LANES - 32
                    if low >= high:
                        continue
                    place = layout.tile_start(other)
                    width = min(LANES, length - place)
                    bins = bins_ref[low:high, slot * LANES : (slot + 1) * LANES]
                    bias = look_up(table_row, bins)[:, :width]
                    scores[low - start : high - start, place : place + width] += bias
            block = scores[0:size, 0:length]
            top = jnp.max(block, axis=1, keepdims=True)
            weights = jnp.exp2((block - top) * factor).astype(jnp.bfloat16)
            sums = wide_dot(weights, value_columns)
            total = sums[:, LANES:]
            result = sums[:, :LANES] / total
            if side == 0:
                out_ref[start:stop] = result
            else:
                out_ref[start:stop] += result
            log_total = top + jnp.log(total) * (1.0 / scale)
            log_ref[start:stop] = jnp.where(
                lane == 2 * pair + side, log_total, log_ref[start:stop]
            )


def backward_kernel(layout, scale, first_pair, *refs):
    count = len(layout.pieces)
    query_ref, grad_ref, out_ref, log_ref = refs[:4]
    key_refs = refs[4 : 4 + count]
    value_refs = refs[4 + count : 4 + 2 * count]
    rest = refs[4 + 2 * count :]
    members_ref, kinds_ref, bins_ref, places_ref, tables_ref = rest[:5]
    grad_query_ref = rest[5]
    grad_pair_refs = rest[6 : 6 + count]
    grad_table_ref = rest[6 + count]
    query_wide, grad_wide, query_half, grad_half, scores, slopes, slopes_low = rest[7 + count :]
    pair = pl.program_id(1) + first_pair
    rows, length, padded = layout.block_rows, layout.length, layout.padded
    factor = scale * LOG2E
    lane = lax.broadcasted_iota(jnp.int32, (1, LANES), 1)
    keys = jnp.concatenate([ref[...] for ref in key_refs], axis=0)
    values = jnp.concatenate([ref[...] for ref in value_refs], axis=0)
    members = members_ref[...]
    kinds = kinds_ref[...]
    tables = tables_ref[...]
    query = query_ref[...]
    grad = grad_ref[...]
    grad_full = grad.astype(jnp.float32)
    product = grad_full * out_ref[...]
    log_all = log_ref[...]
    tail = 2 * layout.groups
    ones = jnp.broadcast_to(jnp.where(lane < 3, 1.0, 0.0), (length, LANES)).astype(jnp.bfloat16)

    def three_parts(values):
        upper = values.astype(jnp.bfloat16).astype(jnp.float32)
        values = values - upper
        middle = values.astype(jnp.bfloat16).astype(jnp.float32)
        return upper, middle, values - middle

    def in_lanes(parts, first):
        return jnp.where(
            lane == first,
            parts[0],
            jnp.where(lane == first + 1, parts[1], jnp.where(lane == first + 2, parts[2], 0.0)),
        )

    if padded > rows:
        for ref in (query_wide, grad_wide, query_half, grad_half):
            for side in range(2):
                ref[side, rows:padded] = jnp.zeros((padded - rows, ref.shape[2]), jnp.bfloat16)
    for side in range(2):
        log_total = jnp.sum(
            jnp.where(lane == 2 * pair + side, log_all, 0.0), axis=1, keepdims=True
        )
        extra = group_columns(kinds, tables, side) + in_lanes(three_parts(log_total), tail)
        query_wide[side, 0:rows, 0:LANES] = query
        query_wide[side, 0:rows, LANES:] = extra.astype(jnp.bfloat16)
        delta = jnp.sum(half_of(product, lane, side), axis=1, keepdims=True)
        grad_wide[side, 0:rows, 0:LANES] = grad
        grad_wide[side, 0:rows, LANES:] = in_lanes(three_parts(-delta), 0).astype(jnp.bfloat16)
        query_half[side, 0:rows] = half_of(query, lane, side)
        grad_half[side, 0:rows] = half_of(grad, lane, side)

    key_columns = [
        jnp.concatenate([half_of(keys, lane, side), members], axis=1) for side in range(2)
    ]
    value_columns = [
        jnp.concatenate([half_of(values, lane, side), ones], axis=1) for side in range(2)
    ]
    inner_sums = [jnp.zeros((1, LANES), jnp.float32) for _ in range(2)]
    low_sums = [jnp.zeros((1, LANES), jnp.float32) for _ in range(2)]
    high_sums = [jnp.zeros((1, LANES), jnp.float32) for _ in range(2)]
    reach_tiles = list(range(layout.query_tiles)) + [-1]

    def put(which, start, stop, result):
        begin = 0
        for ref, size in zip(grad_pair_refs, layout.pieces):
            low, high = max(start, begin), min(stop, begin + size)
            if low < high:
                ref[which, low - begin : high - begin] = result[low - start : high - start]
            begin += size

    for start, stop in row_blocks(length, 384):
        size = stop - start
        grad_key = grad_value = None
        for side in range(2):
            table_row = tables[8 * side : 8 * side + 1]
            scores[0:size] = wide_dot(key_columns[side][start:stop], query_wide[side], NT)
            near = []
            for index, tile in enumerate(reach_tiles):
                place = layout.tile_start(tile)
                if start <= place < stop:
                    near.append((index, tile, place, min(place + LANES, length)))
            for index, tile, place, final in near:
                for slot in range(3):
                    other = tile + slot - 1
                    if not 0 <= other < layout.query_tiles:
                        continue
                    bins = bins_ref[
                        index * LANES : index * LANES + final - place,
                        slot * LANES : (slot + 1) * LANES,
                    ]
                    scores[
                        place - start : final - start, other * LANES : (other + 1) * LANES
                    ] += look_up(table_row, bins)
            probs = jnp.exp2(scores[0:size] * factor)
            grad_probs = wide_dot(value_columns[side][start:stop], grad_wide[side], NT)
            slope = probs * grad_probs
            if near:
                slopes[0:size] = slope
            low = slope.astype(jnp.bfloat16)
            slopes_low[side, start:stop] = low
            part = wide_dot(low, query_half[side])
            grad_key = part if grad_key is None else grad_key + part
            part = wide_dot(probs.astype(jnp.bfloat16), grad_half[side])
            grad_value = part if grad_value is None else grad_value + part
            for index, tile, place, final in near:
                for slot in range(3):
                    other = tile + slot - 1
                    if not 0 <= other < layout.query_tiles:
                        continue
                    bins = bins_ref[
                        index * LANES : index * LANES + final - place,
                        slot * LANES : (slot + 1) * LANES,
                    ]
                    cut = slopes[place - start : final - start, other * LANES : (other + 1) * LANES]
                    low_sums[side] += jnp.sum(
                        jnp.where(bins == 0, cut, 0.0), axis=0, keepdims=True
                    )
                    high_sums[side] += jnp.sum(
                        jnp.where(bins == 2 * (NEAR + 1), cut, 0.0), axis=0, keepdims=True
                    )
                for half in range(2):
                    begin, end = half * 64, min(half * 64 + 64, final - place)
                    if begin >= end:
                        continue
                    base = 0 if tile < 0 else tile - 1 + half
                    where = places_ref[index * LANES + begin : index * LANES + end]
                    spot = where & (LANES - 1)
                    for step in range(2):
                        other = base + step
                        if not 0 <= other < layout.query_tiles or (tile < 0 and step):
                            continue
                        cut = slopes[
                            place - start + begin : place - start + end,
                            other * LANES : (other + 1) * LANES,
                        ]
                        picked = jnp.take_along_axis(cut, spot, axis=1, mode="promise_in_bounds")
                        picked = jnp.where((where >> 7) == step, picked, 0.0)
                        inner_sums[side] += jnp.sum(picked, axis=0, keepdims=True)
        put(0, start, stop, (grad_key * scale).astype(jnp.bfloat16))
        put(1, start, stop, grad_value.astype(jnp.bfloat16))

    grad_query = None
    for side in range(2):
        both = wide_dot(slopes_low[side], key_columns[side], TN)[0:rows]
        part = both[:, :LANES]
        grad_query = part if grad_query is None else grad_query + part
        sums = jnp.where(lane < layout.groups, both[:, LANES:], 0.0)

        def total(kind):
            return jnp.sum(jnp.where(kinds == kind, sums, 0.0))

        right = total(RIGHT) + jnp.sum(high_sums[side])
        left = total(LEFT) + jnp.sum(low_sums[side])
        apart = total(APART)
        grad_table_ref[side : side + 1] = jnp.where(
            lane == 0,
            left,
            jnp.where(
                lane == 2 * (NEAR + 1),
                right,
                jnp.where(lane == 2 * (NEAR + 1) + 1, apart, inner_sums[side]),
            ),
        )
    grad_query_ref[...] = (grad_query * scale).astype(jnp.bfloat16)


def tile_columns(rows, offset=0):
    return pl.BlockSpec((None, rows, LANES), lambda crop, pair: (crop, 0, pair + offset))


def per_crop(rows, width):
    return pl.BlockSpec((None, rows, width), lambda crop, pair: (crop, 0, 0))


def kernel_params():
    return pltpu.CompilerParams(
        vmem_limit_bytes=VMEM_BYTES, dimension_semantics=("arbitrary", "arbitrary")
    )


def attention_forward(layout, scale, projected, key_values, members, kinds, bins, tables):
    crops, rows, _ = projected.shape
    pairs = tables.shape[0]
    specs = [tile_columns(rows)]
    operands = [projected]
    for place in (1, 2):
        for piece in key_values:
            specs.append(tile_columns(piece[0].shape[1], piece[place]))
            operands.append(piece[0])
    specs += [
        per_crop(layout.length, LANES),
        per_crop(rows, LANES),
        per_crop(layout.padded, 3 * LANES),
        pl.BlockSpec((None, 16, LANES), lambda crop, pair: (pair, 0, 0)),
    ]
    flops = 2 * crops * pairs * 2 * rows * layout.length * 256 * 2
    return pl.pallas_call(
        functools.partial(forward_kernel, layout, scale),
        grid=(crops, pairs),
        in_specs=specs,
        out_specs=(tile_columns(rows), per_crop(rows, LANES)),
        out_shape=(
            jax.ShapeDtypeStruct((crops, rows, pairs * LANES), jnp.float32),
            jax.ShapeDtypeStruct((crops, rows, LANES), jnp.float32),
        ),
        scratch_shapes=[pltpu.VMEM((256, layout.wide), jnp.float32)],
        compiler_params=kernel_params(),
        cost_estimate=pl.CostEstimate(
            flops=flops,
            bytes_accessed=12 * crops * rows * pairs * LANES,
            transcendentals=crops * pairs * 2 * rows * layout.length,
        ),
        name="attention_forward",
    )(*operands, members, kinds, bins, tables)


def attention_backward(
    layout,
    scale,
    first_pair,
    pairs,
    projected,
    grad_out,
    attended,
    logs,
    key_values,
    members,
    kinds,
    bins,
    places,
    tables,
):
    crops, rows, _ = projected.shape
    specs = [tile_columns(rows, first_pair)] * 3 + [per_crop(rows, LANES)]
    operands = [projected, grad_out, attended, logs]
    for place in (1, 2):
        for piece in key_values:
            specs.append(tile_columns(piece[0].shape[1], piece[place] + first_pair))
            operands.append(piece[0])
    specs += [
        per_crop(layout.length, LANES),
        per_crop(rows, LANES),
        per_crop(bins.shape[1], 3 * LANES),
        per_crop(places.shape[1], LANES),
        pl.BlockSpec((None, 16, LANES), lambda crop, pair: (pair + first_pair, 0, 0)),
    ]
    out_specs = [tile_columns(rows)]
    out_shapes = [jax.ShapeDtypeStruct((crops, rows, pairs * LANES), jnp.bfloat16)]
    for piece in key_values:
        size = piece[0].shape[1]
        out_specs.append(
            pl.BlockSpec((None, 2, size, LANES), lambda crop, pair: (crop, 0, 0, pair))
        )
        out_shapes.append(jax.ShapeDtypeStruct((crops, 2, size, pairs * LANES), jnp.bfloat16))
    out_specs.append(pl.BlockSpec((None, None, 8, LANES), lambda crop, pair: (crop, pair, 0, 0)))
    out_shapes.append(jax.ShapeDtypeStruct((crops, pairs, 8, LANES), jnp.float32))
    padded, block = layout.padded, 384
    return pl.pallas_call(
        functools.partial(backward_kernel, layout, scale, first_pair),
        grid=(crops, pairs),
        in_specs=specs,
        out_specs=tuple(out_specs),
        out_shape=tuple(out_shapes),
        scratch_shapes=[
            pltpu.VMEM((2, padded, 2 * LANES), jnp.bfloat16),
            pltpu.VMEM((2, padded, 2 * LANES), jnp.bfloat16),
            pltpu.VMEM((2, padded, LANES), jnp.bfloat16),
            pltpu.VMEM((2, padded, LANES), jnp.bfloat16),
            pltpu.VMEM((block, padded), jnp.float32),
            pltpu.VMEM((block, padded), jnp.float32),
            pltpu.VMEM((2, layout.length, padded), jnp.bfloat16),
        ],
        compiler_params=kernel_params(),
        cost_estimate=pl.CostEstimate(
            flops=2 * crops * pairs * 2 * rows * layout.length * 256 * 5,
            bytes_accessed=20 * crops * rows * pairs * LANES,
            transcendentals=crops * pairs * 2 * rows * layout.length,
        ),
        name="attention_backward",
    )(*operands, members, kinds, bins, places, tables)


def sigmoid(values):
    return 1.0 / (1.0 + jnp.exp(-values))


def fold_rows(values):
    return jnp.sum(values.reshape(values.shape[0] // 8, 8, values.shape[1]), axis=0)


def feed_kernel(split, chunks, here_ref, *refs):
    (attended_ref, gate_pre_ref, tokens_ref, upstream_ref, normed_a_ref, mod_ref, output_ref) = refs[:7]
    gate_ref, up_ref, down_ref = refs[7:10]
    layer_ref, grad_middle_ref, grad_att_ref, grad_pre_ref, sums_ref = refs[10:15]
    grads = refs[15:-10]
    gated, grad_ff, normed, branch, middle, total, grad_normed, hidden, both, grad_branch = refs[-10:]
    step = pl.program_id(0)
    here = here_ref[0]
    rows, width = tokens_ref.shape
    size = gate_ref.shape[1]
    strip = 32
    strips = rows // strip
    shift_f, scale_f = mod_ref[3:4], mod_ref[4:5]
    open_a, open_f = sigmoid(mod_ref[2:3]), sigmoid(mod_ref[5:6])

    def strip_of(index):
        return pl.ds(pl.multiple_of(index * strip, strip), strip)

    def norm_of(values):
        mean_value = jnp.mean(values, axis=1, keepdims=True)
        centred = values - mean_value
        spread = jnp.mean(centred * centred, axis=1, keepdims=True)
        root = lax.rsqrt(spread + 1e-06)
        return centred * root, root

    @pl.when(step == 0)
    def _():
        @pl.loop(0, strips)
        def _(index):
            cut = strip_of(index)
            gated[cut] = (attended_ref[cut] * sigmoid(gate_pre_ref[cut])).astype(jnp.bfloat16)
            grad_ff[cut] = (upstream_ref[cut].astype(jnp.float32) * open_f).astype(jnp.bfloat16)

        branch[...] = wide_dot(gated[...], output_ref[...])

        @pl.loop(0, strips)
        def _(index):
            cut = strip_of(index)
            values = tokens_ref[cut].astype(jnp.float32) + open_a * branch[cut]
            middle[cut] = values
            normed[cut] = (norm_of(values)[0] * (1.0 + scale_f) + shift_f).astype(jnp.bfloat16)
            total[cut] = jnp.zeros((strip, width), jnp.float32)
            grad_normed[cut] = jnp.zeros((strip, width), jnp.float32)

    block = rows if rows <= 384 else rows // 2
    for start in range(0, rows, block):
        cut = slice(start, start + block)
        before = wide_dot(normed[cut], gate_ref[...])
        lifted = wide_dot(normed[cut], up_ref[...])
        grad_hidden = wide_dot(grad_ff[cut], down_ref[...], NT)
        switch = sigmoid(before)
        silu = before * switch
        part = (silu * lifted).astype(jnp.bfloat16)
        hidden[cut] = part
        grad_up = (grad_hidden * silu).astype(jnp.bfloat16)
        grad_gate = (grad_hidden * lifted * (switch + silu * (1.0 - switch))).astype(jnp.bfloat16)
        both[cut, :size] = grad_gate
        both[cut, size:] = grad_up
        total[cut] += wide_dot(part, down_ref[...])
        grad_normed[cut] += wide_dot(grad_gate, gate_ref[...], NT) + wide_dot(
            grad_up, up_ref[...], NT
        )

    pair = wide_dot(normed[...], both[...], TN).astype(jnp.bfloat16)
    if split:
        gate_send, gate_keep, up_send, up_keep, down_send, down_keep, small_send, small_keep = grads
        half = width // 2
        away = pl.ds(pl.multiple_of((1 - here) * half, LANES), half)
        home = pl.ds(pl.multiple_of(here * half, LANES), half)
        down_send[...] = wide_dot(hidden[...], grad_ff[:, away], TN).astype(jnp.bfloat16)
        down_keep[...] = wide_dot(hidden[...], grad_ff[:, home], TN).astype(jnp.bfloat16)

        @pl.when(step < chunks // 2)
        def _():
            gate_send[...] = pair[:, :size]
            up_send[...] = pair[:, size:]

        @pl.when(step >= chunks // 2)
        def _():
            gate_keep[...] = pair[:, :size]
            up_keep[...] = pair[:, size:]
    else:
        gate_all, up_all, down_all, small_all = grads
        gate_all[...] = pair[:, :size]
        up_all[...] = pair[:, size:]
        down_all[...] = wide_dot(hidden[...], grad_ff[...], TN).astype(jnp.bfloat16)

    @pl.when(step == chunks - 1)
    def _():
        def finish(index, sums):
            gate_f_sum, shift_sum, scale_sum, gate_a_sum = sums
            cut = strip_of(index)
            values = middle[cut]
            fed = total[cut]
            upstream = upstream_ref[cut].astype(jnp.float32)
            layer_ref[cut] = (values + open_f * fed).astype(jnp.bfloat16)
            normal, root = norm_of(values)
            grad = grad_normed[cut]
            scaled = grad * (1.0 + scale_f)
            grad_middle = upstream + root * (
                scaled
                - jnp.mean(scaled, axis=1, keepdims=True)
                - normal * jnp.mean(scaled * normal, axis=1, keepdims=True)
            )
            grad_middle_ref[cut] = grad_middle
            grad_branch[cut] = (grad_middle * open_a).astype(jnp.bfloat16)
            return (
                gate_f_sum + fold_rows(upstream * fed),
                shift_sum + fold_rows(grad),
                scale_sum + fold_rows(grad * normal),
                gate_a_sum + fold_rows(grad_middle * branch[cut]),
            )

        zero = jnp.zeros((8, width), jnp.float32)
        sums = lax.fori_loop(0, strips, finish, (zero, zero, zero, zero))
        gate_f_sum, shift_sum, scale_sum, gate_a_sum = [
            jnp.sum(value, axis=0, keepdims=True) for value in sums
        ]
        none = jnp.zeros((1, width), jnp.float32)
        sums_ref[...] = jnp.concatenate(
            [
                none,
                none,
                gate_a_sum * open_a * (1.0 - open_a),
                shift_sum,
                scale_sum,
                gate_f_sum * open_f * (1.0 - open_f),
                none,
                none,
            ],
            axis=0,
        )
        total[...] = wide_dot(grad_branch[...], output_ref[...], NT)

        @pl.loop(0, strips)
        def _(index):
            cut = strip_of(index)
            grad_gated = total[cut]
            opened = sigmoid(gate_pre_ref[cut])
            grad_att_ref[cut] = (grad_gated * opened).astype(jnp.bfloat16)
            grad_pre_ref[cut] = (
                grad_gated * attended_ref[cut] * (opened * (1.0 - opened))
            ).astype(jnp.bfloat16)

        if split:
            for side, ref in ((away, small_send), (home, small_keep)):
                ref[:, :half] = wide_dot(gated[...], grad_branch[:, side], TN).astype(jnp.bfloat16)
                ref[:, half:] = wide_dot(normed_a_ref[...], grad_pre_ref[:, side], TN).astype(
                    jnp.bfloat16
                )
        else:
            small_all[:, :width] = wide_dot(gated[...], grad_branch[...], TN).astype(jnp.bfloat16)
            small_all[:, width:] = wide_dot(normed_a_ref[...], grad_pre_ref[...], TN).astype(
                jnp.bfloat16
            )


def feed_layer(
    split, here, attended, gate_pre, tokens, upstream, normed_a, mod_rows, output_weight, feed_gate, feed_up, feed_down
):
    rows, width = tokens.shape
    inner = feed_gate.shape[1]
    size = 512
    chunks = inner // size
    half = chunks // 2

    def turn(step, here_ref):
        return (step + half * (1 - here_ref[0])) % chunks if split else step

    def fixed(shape):
        return pl.BlockSpec(shape, lambda step, here_ref: (0, 0), pipeline_mode=pl.Buffered(1))

    def columns(step, here_ref):
        return (0, turn(step, here_ref))

    def strips(step, here_ref):
        return (turn(step, here_ref), 0)

    whole = (rows, width)
    in_specs = [fixed(whole)] * 5 + [
        fixed((8, width)),
        fixed((width, width)),
        pl.BlockSpec((width, size), columns),
        pl.BlockSpec((width, size), columns),
        pl.BlockSpec((size, width), strips),
    ]
    out_specs = [fixed(whole)] * 4 + [fixed((8, width))]
    bf16, f32 = jnp.bfloat16, jnp.float32
    out_shapes = [(whole, bf16), (whole, f32), (whole, bf16), (whole, bf16), ((8, width), f32)]
    if split:
        first = pl.BlockSpec((width, size), lambda step, here_ref: (0, jnp.minimum(step, half - 1)))
        second = pl.BlockSpec((width, size), lambda step, here_ref: (0, jnp.maximum(step - half, 0)))
        out_specs += [first, second, first, second]
        out_shapes += [((width, inner // 2), bf16)] * 4
        out_specs += [pl.BlockSpec((size, width // 2), strips)] * 2
        out_shapes += [((inner, width // 2), bf16)] * 2
        out_specs += [fixed((width, width))] * 2
        out_shapes += [((width, width), bf16)] * 2
    else:
        out_specs += [pl.BlockSpec((width, size), columns)] * 2
        out_shapes += [((width, inner), bf16)] * 2
        out_specs += [pl.BlockSpec((size, width), strips), fixed((width, 2 * width))]
        out_shapes += [((inner, width), bf16), ((width, 2 * width), bf16)]
    return pl.pallas_call(
        functools.partial(feed_kernel, split, chunks),
        grid_spec=pltpu.PrefetchScalarGridSpec(
            num_scalar_prefetch=1,
            grid=(chunks,),
            in_specs=in_specs,
            out_specs=tuple(out_specs),
            scratch_shapes=[
                pltpu.VMEM(whole, bf16),
                pltpu.VMEM(whole, bf16),
                pltpu.VMEM(whole, bf16),
                pltpu.VMEM(whole, f32),
                pltpu.VMEM(whole, f32),
                pltpu.VMEM(whole, f32),
                pltpu.VMEM(whole, f32),
                pltpu.VMEM((rows, size), bf16),
                pltpu.VMEM((rows, 2 * size), bf16),
                pltpu.VMEM(whole, bf16),
            ],
        ),
        out_shape=tuple(jax.ShapeDtypeStruct(shape, kind) for shape, kind in out_shapes),
        compiler_params=pltpu.CompilerParams(vmem_limit_bytes=VMEM_BYTES),
        cost_estimate=pl.CostEstimate(
            flops=2 * rows * width * (9 * inner + 4 * width),
            bytes_accessed=12 * width * inner + 24 * rows * width,
            transcendentals=2 * rows * inner,
        ),
        name="feed_layer",
    )(
        jnp.reshape(here, (1,)).astype(jnp.int32),
        attended,
        gate_pre,
        tokens,
        upstream,
        normed_a,
        mod_rows,
        output_weight,
        feed_gate,
        feed_up,
        feed_down,
    )


MASKS = {"u": 8, "v": 4, "y": 2, "x": 1}


def exchange(values, mask):
    return lax.ppermute(values, "crop", [(i, i ^ mask) for i in range(16)])


def swap_res(values):
    return lax.ppermute(values, "res", [(0, 1), (1, 0)])


def tie(*values):
    return lax.optimization_barrier(values)


def add_low(former, latter, kind=jnp.bfloat16):
    return (former.astype(jnp.float32) + latter.astype(jnp.float32)).astype(kind)


def stage_kernel(part_counts, bits_ref, *refs):
    total = sum(part_counts)
    inputs, outputs = refs[: 4 * total], refs[4 * total :]
    place = 0
    for stream, parts in enumerate(part_counts):
        for side in range(2):
            out_ref = outputs[2 * stream + side]
            column = 0
            for part in range(parts):
                kept_ref, came_ref = inputs[4 * (place + part) + 2 * side :][:2]
                width = kept_ref.shape[-1]
                out_ref[:, :, column : column + width] = add_low(kept_ref[...], came_ref[...])
                column += width
        place += parts


class Halving:
    def __init__(self, orders):
        self.orders = [list(order) for order in orders]
        self.left = [list(MASKS) for _ in orders]

    def stage(self, streams):
        index = lax.axis_index("crop")
        self.masks, bits, places = [], [], []
        for order, left in zip(self.orders, self.left):
            axis = order.pop(0)
            places.append(len(left) - 1 - left.index(axis))
            left.remove(axis)
            self.masks.append(MASKS[axis])
            bits.append((index // MASKS[axis]) % 2)
        bits = jnp.stack(bits).astype(jnp.int32)
        chunks = 2 ** (len(self.left[0]) + 1)
        specs, operands, out_specs, out_shapes = [], [], [], []
        for stream, (parts, place) in enumerate(zip(streams, places)):
            for kept, came, block, width in parts:
                rows = kept.shape[0] // chunks
                for side in range(2):

                    def chunk(step, bits_ref, stream=stream, place=place, side=side, block=block):
                        bit = bits_ref[stream] if side else 1 - bits_ref[stream]
                        low = step & ((1 << place) - 1)
                        return (((step >> place) << (place + 1)) | (bit << place) | low, 0, block)

                    for value in (kept, came):
                        operands.append(value.reshape(chunks, rows, value.shape[1]))
                        specs.append(pl.BlockSpec((1, rows, width), chunk))
            wide = sum(part[3] for part in parts)
            for side in range(2):
                out_specs.append(
                    pl.BlockSpec((1, rows, wide), lambda step, bits_ref: (step, 0, 0))
                )
                out_shapes.append(jax.ShapeDtypeStruct((chunks // 2, rows, wide), jnp.bfloat16))
        results = pl.pallas_call(
            functools.partial(stage_kernel, [len(parts) for parts in streams]),
            grid_spec=pltpu.PrefetchScalarGridSpec(
                num_scalar_prefetch=1,
                grid=(chunks // 2,),
                in_specs=specs,
                out_specs=tuple(out_specs),
            ),
            out_shape=tuple(out_shapes),
            compiler_params=pltpu.CompilerParams(vmem_limit_bytes=VMEM_BYTES),
            cost_estimate=pl.CostEstimate(
                flops=sum(4 * math.prod(shape.shape) for shape in out_shapes),
                bytes_accessed=sum(6 * math.prod(shape.shape) for shape in out_shapes),
                transcendentals=0,
            ),
            name="halving_stage",
        )(bits, *operands)
        flat = [value.reshape(-1, value.shape[2]) for value in results]
        return flat[0::2], flat[1::2]

    def send(self, values):
        return [exchange(value, mask) for value, mask in zip(values, self.masks)]


def parts_of(kept, came):
    return [[(mine, other, 0, mine.shape[1])] for mine, other in zip(kept, came)]


def share_columns(values, parts):
    if parts == 1:
        return values.astype(jnp.bfloat16)
    return lax.psum_scatter(values.astype(jnp.bfloat16), "res", scatter_dimension=1, tiled=True)


def scatter_crops(values):
    return lax.psum_scatter(values, "crop", scatter_dimension=0, tiled=True).astype(jnp.float32)


def gather_crops(values, crop_parts):
    if crop_parts != 16:
        return lax.all_gather(values, "crop", axis=0, tiled=True)
    index = lax.axis_index("crop")
    for mask in (1, 2, 4, 8):
        other = exchange(values, mask)
        low = (index // mask) % 2 == 0
        values = jnp.concatenate(
            [jnp.where(low, values, other), jnp.where(low, other, values)], axis=0
        )
    return values


def sum_res(values, parts):
    if parts == 1:
        return values
    if parts != 2:
        return lax.psum(values, "res")
    return values + swap_res(values)


PACK = 1152
SIDE = 384


def whole_vmem(count):
    return [pl.BlockSpec(memory_space=pltpu.VMEM)] * count


def scalars(*values):
    return jnp.stack([jnp.asarray(value, jnp.int32) for value in values])


def local_call(kernel, numbers, operands, shapes, name, flops=0):
    return pl.pallas_call(
        kernel,
        in_specs=[pl.BlockSpec(memory_space=pltpu.SMEM)] + whole_vmem(len(operands)),
        out_specs=tuple(whole_vmem(len(shapes))),
        out_shape=tuple(jax.ShapeDtypeStruct(shape, kind) for shape, kind in shapes),
        compiler_params=pltpu.CompilerParams(vmem_limit_bytes=VMEM_BYTES),
        cost_estimate=pl.CostEstimate(
            flops=flops,
            bytes_accessed=sum(value.size * value.dtype.itemsize for value in operands)
            + sum(4 * math.prod(shape) for shape, _ in shapes),
            transcendentals=0,
        ),
        name=name,
    )(numbers, *operands)


def projection_kernel(counts, here_ref, normed_ref, *refs):
    calls = len(counts)
    parts, (joined_ref, send_ref, keep_ref) = refs[: 3 * calls], refs[3 * calls :]
    width = joined_ref.shape[1] // 3
    column = 0
    for call, pairs in enumerate(counts):
        size = pairs * LANES
        query_ref, own_ref, came_ref = parts[3 * call : 3 * call + 3]
        joined_ref[:, column : column + size] = query_ref[...]
        for which in range(2):
            first = (1 + which) * width + column
            joined_ref[:, first : first + size] = add_low(own_ref[which], came_ref[which])
        column += size
    half = send_ref.shape[1]
    for side, ref in ((1 - here_ref[0], send_ref), (here_ref[0], keep_ref)):
        columns = pl.ds(pl.multiple_of(side * half, LANES), half)
        ref[...] = wide_dot(normed_ref[...], joined_ref[:, columns], TN).astype(jnp.bfloat16)


def projection_gradient(here, normed_a, calls):
    rows, width = normed_a.shape
    counts = [call[0].shape[-1] // LANES for call in calls]
    return local_call(
        functools.partial(projection_kernel, counts),
        scalars(here),
        [normed_a] + [value for call in calls for value in call],
        [
            ((rows, 3 * width), jnp.bfloat16),
            ((width, 3 * width // 2), jnp.bfloat16),
            ((width, 3 * width // 2), jnp.bfloat16),
        ],
        "projection_gradient",
        6 * rows * width * width,
    )


def finish_kernel(counts, joined_ref, weight_ref, pre_ref, gate_ref, tokens_ref, middle_ref, mod_ref, *refs):
    feed_sums_ref, extra_ref = refs[:2]
    table_refs = refs[2 : 2 + len(counts)]
    out_ref, pack_ref, total = refs[2 + len(counts) :]
    step = pl.program_id(0)
    rows, width = tokens_ref.shape
    part = wide_dot(joined_ref[...], weight_ref[...], NT)

    @pl.when(step == 0)
    def _():
        total[...] = part + wide_dot(pre_ref[...], gate_ref[...], NT)

    @pl.when(step > 0)
    def _():
        total[...] += part

    @pl.when(step == pl.num_programs(0) - 1)
    def _():
        strip = 32
        scale = mod_ref[1:2]

        def finish(index, sums):
            shift_sum, scale_sum = sums
            cut = pl.ds(pl.multiple_of(index * strip, strip), strip)
            values = tokens_ref[cut].astype(jnp.float32)
            centred = values - jnp.mean(values, axis=1, keepdims=True)
            root = lax.rsqrt(jnp.mean(centred * centred, axis=1, keepdims=True) + 1e-06)
            normal = centred * root
            grad = total[cut]
            scaled = grad * (1.0 + scale)
            out_ref[cut] = (
                middle_ref[cut]
                + root
                * (
                    scaled
                    - jnp.mean(scaled, axis=1, keepdims=True)
                    - normal * jnp.mean(scaled * normal, axis=1, keepdims=True)
                )
            ).astype(jnp.bfloat16)
            return shift_sum + fold_rows(grad), scale_sum + fold_rows(grad * normal)

        zero = jnp.zeros((8, width), jnp.float32)
        shift_sum, scale_sum = lax.fori_loop(0, rows // strip, finish, (zero, zero))
        left = jnp.concatenate(
            [
                jnp.sum(shift_sum, axis=0, keepdims=True),
                jnp.sum(scale_sum, axis=0, keepdims=True),
                feed_sums_ref[2:8],
            ],
            axis=0,
        )
        heads = []
        for ref, pairs in zip(table_refs, counts):
            for pair in range(pairs):
                heads += [ref[pair, 0:1], ref[pair, 1:2]]
        lines = [jnp.concatenate(heads[3 * i : 3 * i + 3], axis=1) for i in range(4)]
        right = jnp.concatenate(lines + [extra_ref[4:8]], axis=0)
        pack = jnp.concatenate([left, right], axis=1)
        upper = pack.astype(jnp.bfloat16)
        rest = (pack - upper.astype(jnp.float32)).astype(jnp.bfloat16)
        pack_ref[...] = jnp.concatenate([upper, rest], axis=0)


def finish_layer(
    joined, weight, grad_pre, gate_weight, tokens, grad_middle, mod_rows, feed_sums, extra, grad_tables
):
    rows, width = tokens.shape
    counts = [table.shape[0] for table in grad_tables]

    def fixed(shape):
        return pl.BlockSpec(shape, lambda step: (0,) * len(shape), pipeline_mode=pl.Buffered(1))

    return pl.pallas_call(
        functools.partial(finish_kernel, counts),
        grid=(3,),
        in_specs=[
            pl.BlockSpec((rows, width), lambda step: (0, step)),
            pl.BlockSpec((width, width), lambda step: (0, step)),
            fixed((rows, width)),
            fixed((width, width)),
            fixed((rows, width)),
            fixed((rows, width)),
            fixed((8, width)),
            fixed((8, width)),
            fixed((8, SIDE)),
        ]
        + [fixed((count, 8, LANES)) for count in counts],
        out_specs=(fixed((rows, width)), fixed((16, PACK))),
        out_shape=(
            jax.ShapeDtypeStruct((rows, width), jnp.bfloat16),
            jax.ShapeDtypeStruct((16, PACK), jnp.bfloat16),
        ),
        scratch_shapes=[pltpu.VMEM((rows, width), jnp.float32)],
        compiler_params=pltpu.CompilerParams(vmem_limit_bytes=VMEM_BYTES),
        cost_estimate=pl.CostEstimate(
            flops=8 * rows * width * width, bytes_accessed=24 * rows * width, transcendentals=0
        ),
        name="finish_layer",
    )(
        joined,
        weight,
        grad_pre,
        gate_weight,
        tokens,
        grad_middle,
        mod_rows,
        feed_sums,
        extra,
        *grad_tables,
    )


def fan_first_kernel(bits_ref, keep_ref, came_ref, pack_ref, mine_ref, *send_refs):
    chunk = keep_ref.shape[0] // 16
    for other, ref in enumerate((mine_ref, *send_refs)):
        for level in range(4):
            start = (level * 4 + (bits_ref[0] ^ other)) * chunk
            cut = pl.ds(pl.multiple_of(start, 16), chunk)
            ref[level * chunk : (level + 1) * chunk] = add_low(keep_ref[cut], came_ref[cut])
        if other:
            ref[4 * chunk : 4 * chunk + 16] = pack_ref[...]


def fan_second_kernel(bits_ref, mine_ref, *refs):
    came_refs, pack_ref = refs[:3], refs[3]
    out_ref, *send_refs = refs[4:8]
    packs_ref = refs[8]
    chunk = mine_ref.shape[0] // 4
    packs_ref[0:16] = pack_ref[...]
    for other, ref in enumerate(came_refs):
        packs_ref[16 * other + 16 : 16 * other + 32] = ref[4 * chunk : 4 * chunk + 16]
    for other, ref in enumerate((out_ref, *send_refs)):
        cut = pl.ds(pl.multiple_of((bits_ref[0] ^ other) * chunk, 16), chunk)
        total = mine_ref[cut].astype(jnp.float32)
        for came_ref in came_refs:
            total = total + came_ref[cut].astype(jnp.float32)
        ref[0:chunk] = total.astype(jnp.bfloat16)
        if other:
            ref[chunk : chunk + 64] = packs_ref[...]


def fan_third_kernel(bits_ref, mine_ref, *refs):
    came_refs, packs_ref, (out_ref, all_ref) = refs[:3], refs[3], refs[4:]
    chunk = mine_ref.shape[0]
    total = mine_ref[...].astype(jnp.float32)
    all_ref[0:64] = packs_ref[...]
    for other, ref in enumerate(came_refs):
        total = total + ref[0:chunk].astype(jnp.float32)
        all_ref[64 * other + 64 : 64 * other + 128] = ref[chunk : chunk + 64]
    out_ref[...] = total


def last_sums_kernel(widths, bits_ref, *refs):
    count = len(widths)
    outputs = list(refs[2 * count :])
    for stream, cuts in enumerate(widths):
        kept_ref, came_ref = refs[2 * stream], refs[2 * stream + 1]
        column = 0
        for width in cuts:
            columns = slice(column, column + width)
            outputs.pop(0)[...] = add_low(kept_ref[:, columns], came_ref[:, columns], jnp.float32)
            column += width


def last_sums(kept, came, widths):
    operands = [value for pair in zip(kept, came) for value in pair]
    shapes = [
        ((mine.shape[0], width), jnp.float32) for mine, cuts in zip(kept, widths) for width in cuts
    ]
    return local_call(
        functools.partial(last_sums_kernel, widths), scalars(0), operands, shapes, "last_sums"
    )


def small_kernel(
    heads,
    here_ref,
    mine_ref,
    came_ref,
    modulation_ref,
    pair_norm_ref,
    relative_ref,
    gain_ref,
    pair_weight_ref,
    mod_grad_ref,
    time_ref,
    label_ref,
    relative_grad_ref,
    gain_grad_ref,
    pair_grad_ref,
    grad_condition,
):
    step = pl.program_id(0)
    crops = mine_ref.shape[0] // 16
    width = modulation_ref.shape[1]
    shape = (crops, mine_ref.shape[0])
    row = lax.broadcasted_iota(jnp.int32, shape, 1)
    crop = lax.broadcasted_iota(jnp.int32, shape, 0)

    def chosen(line):
        local = row - crop * 16
        return jnp.where((local == line) | (local == line + 8), 1.0, 0.0).astype(jnp.bfloat16)

    def parts_split(values):
        upper = values.astype(jnp.bfloat16)
        return upper, (values - upper.astype(jnp.float32)).astype(jnp.bfloat16)

    def dot_left(narrow, values, numbers):
        upper, rest = parts_split(values)
        return wide_dot(narrow, upper, numbers) + wide_dot(narrow, rest, numbers)

    def dot_right(values, narrow, numbers):
        upper, rest = parts_split(values)
        return wide_dot(upper, narrow, numbers) + wide_dot(rest, narrow, numbers)

    cond_line = wide_dot(chosen(5), mine_ref[:, width:])
    condition = cond_line[:, :256]
    gate_value = sigmoid(condition)
    cond_act = (condition * gate_value).astype(jnp.bfloat16)
    pick = chosen(step)
    grad_mod = wide_dot(pick, mine_ref[:, :width]) + wide_dot(pick, came_ref[:, :width])
    mod_grad_ref[...] = dot_left(cond_act, grad_mod, TN)
    part = dot_right(grad_mod, modulation_ref[...], NT)

    @pl.when(step == 0)
    def _():
        grad_condition[...] = part
        line = lax.broadcasted_iota(jnp.int32, (8, shape[1]), 0)
        local = lax.broadcasted_iota(jnp.int32, (8, shape[1]), 1) & 15
        every = jnp.where((local == line) | (local == line + 8), 1.0, 0.0).astype(jnp.bfloat16)
        lines = wide_dot(every, mine_ref[:, width:]) + wide_dot(every, came_ref[:, width:])
        table = jnp.concatenate(
            [
                lines[head // 3 : head // 3 + 1, (head % 3) * LANES : (head % 3 + 1) * LANES]
                for head in range(heads)
            ]
            + [jnp.zeros((16 - heads, LANES), jnp.float32)],
            axis=0,
        )
        bins = relative_ref.shape[0]
        pair_grad_ref[...] = dot_left(pair_norm_ref[...], table, (((0,), (1,)), ((), ())))[:, :heads]
        grad_norm = dot_right(table, pair_weight_ref[...], (((0,), (1,)), ((), ())))[:bins]
        values = relative_ref[...]
        centred = values - jnp.mean(values, axis=1, keepdims=True)
        root = lax.rsqrt(jnp.mean(centred * centred, axis=1, keepdims=True) + 1e-06)
        normal = centred * root
        gain_grad_ref[...] = jnp.sum(grad_norm * normal, axis=0, keepdims=True)
        scaled = grad_norm * gain_ref[...]
        relative_grad_ref[...] = root * (
            scaled
            - jnp.mean(scaled, axis=1, keepdims=True)
            - normal * jnp.mean(scaled * normal, axis=1, keepdims=True)
        )

    @pl.when(step > 0)
    def _():
        grad_condition[...] += part

    @pl.when(step == pl.num_programs(0) - 1)
    def _():
        final = grad_condition[...] * (gate_value * (1.0 + condition * (1.0 - gate_value)))
        features = wide_dot(chosen(4), mine_ref[:, width:])[:, :256].astype(jnp.bfloat16)
        time_ref[...] = dot_left(features, final, TN)
        label = lax.broadcasted_iota(jnp.int32, (crops, label_ref.shape[0]), 1)
        number = cond_line[:, 256:257].astype(jnp.int32)
        onehot = jnp.where(label == number, 1.0, 0.0).astype(jnp.bfloat16)
        label_ref[...] = dot_left(onehot, final, TN)


def small_gradients(mine, came, modulation_weight, pair_norm, relative, gain, pair_weight, labels):
    conds, wide = modulation_weight.shape
    width = wide // 6
    bins = relative.shape[0]
    heads = pair_weight.shape[1]
    rows = mine.shape[0]

    def fixed(shape):
        return pl.BlockSpec(shape, lambda step: (0, 0))

    shapes = [(conds, wide), (conds, conds), (labels, conds), (bins, conds), (1, conds), (conds, heads)]
    return pl.pallas_call(
        functools.partial(small_kernel, heads),
        grid=(6,),
        in_specs=[
            pl.BlockSpec(memory_space=pltpu.SMEM),
            fixed((rows, PACK)),
            fixed((rows, PACK)),
            pl.BlockSpec((conds, width), lambda step: (0, step)),
            fixed((LANES, conds)),
            fixed((bins, conds)),
            fixed((1, conds)),
            fixed((conds, 16)),
        ],
        out_specs=tuple(
            [pl.BlockSpec((conds, width), lambda step: (0, step))] + [fixed(s) for s in shapes[1:]]
        ),
        out_shape=tuple(jax.ShapeDtypeStruct(shape, jnp.float32) for shape in shapes),
        scratch_shapes=[pltpu.VMEM((rows // 16, conds), jnp.float32)],
        compiler_params=pltpu.CompilerParams(vmem_limit_bytes=VMEM_BYTES),
        cost_estimate=pl.CostEstimate(
            flops=100000000, bytes_accessed=10000000, transcendentals=0
        ),
        name="small_gradients",
    )(
        scalars(0),
        mine,
        came,
        modulation_weight,
        pad_to(pair_norm, 0, LANES, 0.0),
        relative,
        gain.reshape(1, -1),
        pad_to(pair_weight, 1, 16, 0.0),
    )


def per_device(
    crop_parts,
    res_parts,
    tokens,
    cotangent,
    time_levels,
    cath_ids,
    residue_numbers,
    chain_mask,
    time_weight,
    label_table,
    modulation_weight,
    projection_weight,
    gate_weight,
    output_weight,
    relative_table,
    pair_gain,
    pair_weight,
    feed_gate,
    feed_up,
    feed_down,
):
    crop_count, row_count, model_width = tokens.shape
    crop_length = residue_numbers.shape[1]
    head_count = pair_weight.shape[1]
    head_width = model_width // head_count
    bin_count = relative_table.shape[0]
    label_count = label_table.shape[0]
    token_count = crop_count * row_count
    score_scale = head_width ** (-0.5)
    pairs = head_count // 2
    layout = Layout(row_count, crop_length)
    query_start = lax.axis_index("res") * row_count

    def conditioning(features, onehot):
        return jnp.dot(features, time_weight, preferred_element_type=jnp.float32) + jnp.dot(
            onehot, label_table, preferred_element_type=jnp.float32
        )

    features = time_features(time_levels, time_weight.shape[0]).astype(jnp.bfloat16)
    label_onehot = (cath_ids[:, None] == jnp.arange(label_count, dtype=jnp.int32)[None, :]).astype(
        jnp.bfloat16
    )
    condition = conditioning(features, label_onehot)
    cond_act = jax.nn.silu(condition).astype(jnp.bfloat16)
    modulation = jnp.dot(cond_act, modulation_weight, preferred_element_type=jnp.float32)
    modulation = modulation.reshape(crop_count, 6, 1, model_width)
    shift_a, scale_a = modulation[:, 0], modulation[:, 1]
    mod_rows = pad_to(modulation[:, :, 0], 1, 8, 0.0)

    rotated = lax.dynamic_slice_in_dim(
        jnp.concatenate([jnp.stack([residue_numbers, chain_mask])] * 2, 2), query_start, crop_length, 2
    )
    members, kinds, forward_bins, backward_bins, places = attention_tables(
        layout, rotated[0], rotated[1], query_start, bin_count
    )
    relative_values = relative_table.astype(jnp.float32)
    gain_values = pair_gain.astype(jnp.float32)
    pair_norm = normalize_rows(relative_values, gain_values).astype(jnp.bfloat16)
    bias_rows = jnp.dot(pair_norm, pair_weight, preferred_element_type=jnp.float32)
    tables = head_tables(layout, bias_rows, score_scale)

    token_values = tokens.astype(jnp.float32)
    normed_a = (
        modulate(token_values, shift_a, scale_a)
        .astype(jnp.bfloat16)
        .reshape(token_count, model_width)
    )
    projected = jnp.dot(normed_a, projection_weight, preferred_element_type=jnp.float32).astype(
        jnp.bfloat16
    )
    projected = projected.reshape(crop_count, row_count, 3 * model_width)
    gate_pre = jnp.dot(normed_a, gate_weight, preferred_element_type=jnp.float32)
    gate_pre = gate_pre.reshape(crop_count, row_count, model_width)
    key_values = projected[:, :, model_width:]
    others = [
        lax.ppermute(
            key_values, "res", [((r + step) % res_parts, r) for r in range(res_parts)]
        )
        for step in range(1, res_parts)
    ]
    if len(layout.pieces) == 2:
        other = others[0] if len(others) == 1 else jnp.concatenate(others, axis=1)
        pieces = [(projected, pairs, 2 * pairs), (other, 0, pairs)]
    else:
        pieces = [(jnp.concatenate([key_values] + others, axis=1), 0, pairs)]

    def block_rows(values):
        return pad_to(values, 1, layout.block_rows, 0)

    attended, logs = attention_forward(
        layout,
        score_scale,
        block_rows(projected),
        pieces,
        members,
        kinds,
        forward_bins,
        tables,
    )
    here = lax.axis_index("res")
    split = res_parts == 2 and crop_parts == 16 and crop_count == 1
    per_crop_results = [
        feed_layer(
            split,
            here,
            attended[crop],
            block_rows(gate_pre)[crop],
            block_rows(tokens)[crop],
            block_rows(cotangent)[crop],
            block_rows(normed_a.reshape(tokens.shape))[crop],
            mod_rows[crop],
            output_weight,
            feed_gate,
            feed_up,
            feed_down,
        )
        for crop in range(crop_count)
    ]
    layer_out, grad_middle, grad_attended, grad_gate_pre, feed_sums = (
        jnp.stack([result[place] for result in per_crop_results]) for place in range(5)
    )
    layer_out, grad_middle = layer_out[:, :row_count], grad_middle[:, :row_count]
    grad_gate_pre = grad_gate_pre[:, :row_count].reshape(token_count, model_width)
    weight_grads = [
        sum(result[place].astype(jnp.float32) for result in per_crop_results).astype(jnp.bfloat16)
        if crop_count > 1
        else per_crop_results[0][place]
        for place in range(5, len(per_crop_results[0]))
    ]

    def backward_of(first_pair, count, grad_now):
        return attention_backward(
            layout,
            score_scale,
            first_pair,
            count,
            block_rows(projected),
            grad_now,
            attended,
            logs,
            pieces,
            members,
            kinds,
            backward_bins,
            places,
            tables,
        )

    if split:
        arrivals = [swap_res(weight_grads[place]) for place in (0, 2, 4, 6)]
        kept = [weight_grads[place] for place in (1, 3, 5, 7)]
        halving = Halving(["xyvu", "yvxu", "vxyu"])
        half = model_width // 2
        calls = [list(backward_of(0, 1, grad_attended))]
        arrivals, calls[0] = tie(arrivals, calls[0])
        (gate_w, up_w, down_w, small_w) = zip(kept, arrivals)
        streams = [
            [(*gate_w, 0, gate_w[0].shape[1]), (*small_w, 0, half)],
            [(*up_w, 0, up_w[0].shape[1]), (*small_w, 1, half)],
            [(*down_w, 0, half)],
        ]
        arrived = []
        for first_pair, count in ((1, 4), (5, 1)):
            arrived.append(swap_res(calls[-1][2][0]))
            sent, kept = halving.stage(streams)
            sent, grad_attended = tie(sent, grad_attended)
            came = halving.send(sent)
            calls.append(list(backward_of(first_pair, count, grad_attended)))
            came, calls[-1], arrived[-1] = tie(came, calls[-1], arrived[-1])
            streams = parts_of(kept, came)
        index = lax.axis_index("crop")
        away = swap_res(calls[2][2][0])
        sent, kept = halving.stage(streams)
        sent, calls[2][1] = tie(sent, calls[2][1])
        came = halving.send(sent)
        joined, proj_send, proj_keep = projection_gradient(
            here,
            normed_a,
            [
                (calls[0][0][0], calls[0][1][0], arrived[0]),
                (calls[1][0][0], calls[1][1][0], arrived[1]),
                (calls[2][0][0], calls[2][1][0], away),
            ],
        )
        proj_came = swap_res(proj_send)
        extra = jnp.concatenate(
            [
                pad_to(features.astype(jnp.float32), 1, SIDE, 0.0),
                jnp.concatenate(
                    [condition, pad_to(cath_ids.astype(jnp.float32)[:, None], 1, LANES, 0.0)], axis=1
                ),
            ],
            axis=0,
        )
        tokens_grad, pack = finish_layer(
            joined,
            projection_weight,
            grad_gate_pre,
            gate_weight,
            tokens[0],
            grad_middle[0],
            mod_rows[0],
            feed_sums[0],
            jnp.pad(extra, ((4, 2), (0, 0))),
            [call[-1][0] for call in calls],
        )
        tokens_grad = tokens_grad[None]
        came, proj_came, pack = tie(came, proj_came, pack)
        sent, kept = halving.stage(parts_of(kept, came))
        bf16 = jnp.bfloat16
        share = model_width // 16
        mine, *fan = local_call(
            fan_first_kernel,
            scalars(index % 4),
            [proj_keep, proj_came, pack],
            [((4 * share, PACK), bf16)] + [((4 * share + 16, PACK), bf16)] * 3,
            "fan_first",
        )
        sent, fan = tie(sent, fan)
        fan_came = [exchange(value, mask + 1) for mask, value in enumerate(fan)]
        came = halving.send(sent)
        fan_came, mine = tie(fan_came, mine)
        mine, *fan, packs = local_call(
            fan_second_kernel,
            scalars(index // 4),
            [mine, *fan_came, pack],
            [((share, PACK), bf16)] + [((share + 64, PACK), bf16)] * 3 + [((64, PACK), bf16)],
            "fan_second",
        )
        came, fan = tie(came, fan)
        fan_came = [exchange(value, 4 * (mask + 1)) for mask, value in enumerate(fan)]
        inner = feed_gate.shape[1] // 2
        finals = last_sums(kept, came, [[inner, half], [inner, half], [half]])
        fan_came, finals = tie(fan_came, finals)
        feed_gate_grad, output_weight_grad, feed_up_grad, gate_weight_grad, feed_down_grad = finals
        projection_weight_grad, packs = local_call(
            fan_third_kernel,
            scalars(0),
            [mine, *fan_came, packs],
            [((share, PACK), jnp.float32), ((256, PACK), bf16)],
            "fan_third",
        )
        (
            modulation_weight_grad,
            time_weight_grad,
            label_table_grad,
            relative_table_grad,
            pair_gain_grad,
            pair_weight_grad,
        ) = small_gradients(
            packs,
            swap_res(packs),
            modulation_weight,
            pair_norm,
            relative_values,
            gain_values,
            pair_weight,
            label_count,
        )
        pair_gain_grad = pair_gain_grad[0]
    else:
        results = backward_of(0, pairs, grad_attended)
        grad_table = results[-1]
        grad_pairs = results[1:-1]
        if len(grad_pairs) == 2:
            total, away = grad_pairs[0].astype(jnp.float32), grad_pairs[1]
        else:
            total = grad_pairs[0][:, :, :row_count].astype(jnp.float32)
            away = grad_pairs[0][:, :, row_count:]
        for step in range(1, res_parts):
            sent = away[:, :, (step - 1) * row_count : step * row_count]
            pairs_to = [(r, (r + step) % res_parts) for r in range(res_parts)]
            total = total + lax.ppermute(sent, "res", pairs_to).astype(jnp.float32)
        total = total.astype(jnp.bfloat16)
        grad_projected = jnp.concatenate(
            [results[0][:, :row_count], total[:, 0], total[:, 1]], axis=-1
        ).reshape(token_count, 3 * model_width)
        grad_normed_a = against_columns(grad_projected, projection_weight) + against_columns(
            grad_gate_pre, gate_weight
        )
        norm_back_a = jax.vjp(modulate, token_values, shift_a, scale_a)[1]
        grad_tokens, grad_shift_a, grad_scale_a = norm_back_a(
            grad_normed_a.reshape(crop_count, row_count, model_width)
        )
        tokens_grad = (grad_middle + grad_tokens).astype(jnp.bfloat16)
        feed_gate_grad, feed_up_grad, feed_down_grad = (
            scatter_crops(share_columns(value, res_parts)) for value in weight_grads[:3]
        )
        output_weight_grad, gate_weight_grad = (
            scatter_crops(share_columns(value, res_parts))
            for value in (weight_grads[3][:, :model_width], weight_grads[3][:, model_width:])
        )
        projection_weight_grad = scatter_crops(
            share_columns(across_rows(normed_a, grad_projected), res_parts)
        )
        grad_table = grad_table[:, :, :2].sum(0).reshape(head_count, LANES)

        grad_modulation = jnp.concatenate([grad_shift_a, grad_scale_a, feed_sums[:, 2:6]], axis=1)
        grad_modulation = grad_modulation.reshape(crop_count, 6 * model_width)
        table_row = grad_table.reshape(1, head_count * LANES)
        first_row = (jnp.arange(crop_count) == 0).astype(jnp.float32)[:, None]
        small_here = jnp.concatenate([grad_modulation, first_row * table_row], axis=1)
        levels_here = jnp.stack([time_levels, cath_ids.astype(jnp.float32)], axis=1)
        levels_here = pad_to(levels_here, 1, LANES, 0.0)
        small_all = gather_crops(
            jnp.concatenate([levels_here, sum_res(small_here, res_parts)], axis=1), crop_parts
        )
        levels_all, small_all = small_all[:, :2], small_all[:, LANES:]
        grad_modulation = small_all[:, : 6 * model_width]
        grad_table = jnp.sum(small_all[:, 6 * model_width :], axis=0).reshape(head_count, LANES)
        grad_table = grad_table[:, :bin_count]
        features_all = time_features(levels_all[:, 0], time_weight.shape[0]).astype(jnp.bfloat16)
        onehot_all = (
            levels_all[:, 1].astype(jnp.int32)[:, None]
            == jnp.arange(label_count, dtype=jnp.int32)[None, :]
        ).astype(jnp.bfloat16)
        condition = conditioning(features_all, onehot_all)
        cond_act = jax.nn.silu(condition).astype(jnp.bfloat16)
        modulation_weight_grad = split_left(cond_act, grad_modulation, 0, 0)
        grad_condition = split_left(modulation_weight, grad_modulation, 1, 1).T * silu_slope(condition)
        time_weight_grad = split_left(features_all, grad_condition, 0, 0)
        label_table_grad = split_left(onehot_all, grad_condition, 0, 0)
        pair_weight_grad = split_left(pair_norm, grad_table, 0, 1)
        grad_pair_norm = split_right(grad_table, pair_weight, 0, 1)
        pair_back = jax.vjp(normalize_rows, relative_values, gain_values)[1]
        relative_table_grad, pair_gain_grad = pair_back(grad_pair_norm)
    return (
        layer_out,
        tokens_grad,
        time_weight_grad,
        label_table_grad,
        modulation_weight_grad,
        projection_weight_grad,
        gate_weight_grad,
        output_weight_grad,
        relative_table_grad,
        pair_gain_grad,
        pair_weight_grad,
        feed_gate_grad,
        feed_up_grad,
        feed_down_grad,
    )


def solution(mesh):
    return jax.shard_map(
        functools.partial(per_device, mesh.shape["crop"], mesh.shape["res"]),
        mesh=mesh,
        in_specs=(
            P("crop", "res", None),
            P("crop", "res", None),
            P("crop"),
            P("crop"),
            P("crop", None),
            P("crop", None),
            P(),
            P(),
            P(),
            P(),
            P(),
            P(),
            P(),
            P(),
            P(),
            P(),
            P(),
            P(),
        ),
        out_specs=(
            P("crop", "res", None),
            P("crop", "res", None),
            P(),
            P(),
            P(),
            P("crop", "res"),
            P("crop", "res"),
            P("crop", "res"),
            P(),
            P(),
            P(),
            P("crop", "res"),
            P("crop", "res"),
            P("crop", "res"),
        ),
        check_vma=False,
    )
```

```python
import functools
import math

import jax
import jax.numpy as jnp
from jax import lax
from jax.experimental import pallas as pl
from jax.experimental.pallas import tpu as pltpu
from jax.sharding import PartitionSpec as P

LANES = 128
NEAR = 31
VMEM_BYTES = 56 * 1024 * 1024
LOG2E = 1.4426950408889634
NONE, RIGHT, LEFT, APART = 0, 1, 2, 3


def layer_norm(inputs):
    mean_value = jnp.mean(inputs, axis=-1, keepdims=True)
    centred = inputs - mean_value
    spread = jnp.mean(centred * centred, axis=-1, keepdims=True)
    return centred * lax.rsqrt(spread + 1e-06)


def modulate(inputs, shift_row, scale_row):
    return layer_norm(inputs) * (1.0 + scale_row) + shift_row


def normalize_rows(table_rows, gain_row):
    return layer_norm(table_rows) * gain_row


def time_features(time_levels, feature_width):
    half_width = feature_width // 2
    frequency = jnp.exp(-math.log(10000.0) * jnp.arange(half_width, dtype=jnp.float32) / half_width)
    angles = 1000.0 * time_levels[:, None] * frequency[None, :]
    return jnp.concatenate([jnp.sin(angles), jnp.cos(angles)], axis=-1)


def across_rows(former, latter):
    return lax.dot_general(
        former, latter, (((0,), (0,)), ((), ())), preferred_element_type=jnp.float32
    )


def against_columns(former, latter):
    return lax.dot_general(
        former, latter, (((1,), (1,)), ((), ())), preferred_element_type=jnp.float32
    )


def split_parts(values):
    upper = lax.reduce_precision(values, 8, 7)
    return (upper.astype(jnp.bfloat16), (values - upper).astype(jnp.bfloat16))


def split_left(narrow, values, former_dim, latter_dim):
    upper, rest = split_parts(values)
    numbers = (((former_dim,), (latter_dim,)), ((), ()))
    return lax.dot_general(
        narrow, upper, numbers, preferred_element_type=jnp.float32
    ) + lax.dot_general(narrow, rest, numbers, preferred_element_type=jnp.float32)


def split_right(values, narrow, former_dim, latter_dim):
    upper, rest = split_parts(values)
    numbers = (((former_dim,), (latter_dim,)), ((), ()))
    return lax.dot_general(
        upper, narrow, numbers, preferred_element_type=jnp.float32
    ) + lax.dot_general(rest, narrow, numbers, preferred_element_type=jnp.float32)


def sigmoid_slope(inputs):
    gate_value = jax.nn.sigmoid(inputs)
    return gate_value * (1.0 - gate_value)


def silu_slope(inputs):
    gate_value = jax.nn.sigmoid(inputs)
    return gate_value * (1.0 + inputs * (1.0 - gate_value))


class Layout:
    def __init__(self, rows, length):
        self.rows = rows
        self.length = length
        self.query_tiles = -(-rows // LANES)
        self.key_tiles = -(-length // LANES)
        self.padded = self.query_tiles * LANES
        self.wide = self.key_tiles * LANES
        self.last = self.key_tiles - 1
        self.groups = (self.query_tiles + 4) * 4
        assert 2 * self.groups + 3 <= LANES
        assert rows - 1 + NEAR < self.padded and length - NEAR >= self.last * LANES
        assert rows % 8 == 0 and self.last > self.query_tiles
        self.block_rows = rows if rows % 16 == 0 else self.padded
        self.pieces = [rows, length - rows] if rows % 16 == 0 else [length]

    def tile_start(self, tile):
        return self.last * LANES if tile < 0 else tile * LANES


def pad_to(values, axis, size, fill):
    widths = [(0, 0)] * values.ndim
    widths[axis] = (0, size - values.shape[axis])
    return jnp.pad(values, widths, constant_values=fill)


def tables_kernel(layout, bin_count, start_ref, pairs_ref, *out_refs):
    members_ref, kinds_ref, forward_ref, backward_ref, places_ref, codes = out_refs
    rows, length, queries, groups = layout.rows, layout.length, layout.query_tiles, layout.groups
    wrap = length - start_ref[0]
    reach = (bin_count - 2) // 2
    zero_bin = LANES - 1
    shape = (LANES, LANES)
    lane = lax.broadcasted_iota(jnp.int32, shape, 1)
    row = lax.broadcasted_iota(jnp.int32, shape, 0)
    last_start = layout.last * LANES

    tiles = pairs_ref.shape[1]
    marks = pairs_ref[1].astype(jnp.float32)
    place = lax.broadcasted_iota(jnp.int32, marks.shape, 0) * LANES + lax.broadcasted_iota(
        jnp.int32, marks.shape, 1
    )
    before = jnp.sum(jnp.where(place < wrap, marks, 0.0), keepdims=True)
    every = jnp.sum(marks, keepdims=True)
    triangle = jnp.where(row <= lane, 1.0, 0.0).astype(jnp.bfloat16)
    running = jnp.dot(marks.astype(jnp.bfloat16), triangle, preferred_element_type=jnp.float32)
    numbers, chains = [], []
    carry = jnp.zeros((1, 1), jnp.float32)
    for tile in range(layout.key_tiles):
        count = running[tile : tile + 1] + carry
        carry = carry + running[tile : tile + 1, LANES - 1 :]
        count = count + jnp.where(place[tile : tile + 1] < wrap, every - before, -before)
        chains.append(jnp.broadcast_to(count.astype(jnp.int32), shape))
        numbers.append(jnp.broadcast_to(pairs_ref[0, tile : tile + 1], shape))
    number_rows = [value.T for value in numbers]
    chain_rows = [value.T for value in chains]

    def bins_of(key_number, key_chain, query_number, query_chain):
        offset = jnp.clip(key_number - query_number, -reach, reach) + reach
        return jnp.where(key_chain == query_chain, offset, bin_count - 1)

    def touches(query, tile):
        begin = -LANES if tile < 0 else tile * LANES
        return (begin <= query + NEAR) & (query - NEAR <= begin + LANES - 1)

    for tile in range(layout.key_tiles):
        size = min(LANES, length - tile * LANES)
        key = tile * LANES + row
        if tile == layout.last:
            other = jnp.full(shape, queries + 3, jnp.int32)
        elif tile == queries - 1:
            other = jnp.full(shape, queries, jnp.int32)
        else:
            other = jnp.where(key < wrap, queries + 1, queries + 2)
        group = jnp.where(key < rows, tile, other)
        slot = group * 4 + chain_rows[tile] - 1
        hit = (lane == slot) | (lane == slot + groups)
        tail = (lane >= 2 * groups) & (lane < 2 * groups + 3)
        values = jnp.where(hit, 1.0, jnp.where(tail, -1.0, 0.0)).astype(jnp.bfloat16)
        members_ref[tile * LANES : tile * LANES + size] = values[:size]

    local = jnp.where(lane >= groups, lane - groups, lane)
    lane_group = local >> 2
    lane_chain = (local & 3) + 1
    lane_begin = jnp.where(
        lane_group < queries,
        lane_group * LANES,
        jnp.where(lane_group == queries, (queries - 1) * LANES, -LANES),
    )
    has_band = (lane_group <= queries) | (lane_group == queries + 3)
    other_right = jnp.where(
        lane_group == queries,
        rows,
        jnp.where(
            lane_group == queries + 3,
            last_start,
            jnp.where(lane_group == queries + 1, 0, 2 * length),
        ),
    )
    right_limit = jnp.where(lane_group > queries, jnp.where(lane_group == queries + 3, wrap, length), wrap)
    for tile in range(queries):
        size = min(LANES, layout.block_rows - tile * LANES)
        query = tile * LANES + row
        near = (lane_begin <= query + NEAR) & (query - NEAR <= lane_begin + LANES - 1) & has_band
        right = jnp.where(lane_group < queries, lane_group - tile, right_limit - other_right) > 0
        same = chain_rows[tile] == lane_chain
        kinds = jnp.where(same, jnp.where(near, NONE, jnp.where(right, RIGHT, LEFT)), APART)
        kinds = jnp.where((lane < 2 * groups) & (query < rows), kinds, NONE)
        kinds_ref[tile * LANES : tile * LANES + size] = kinds[:size]
        for step in range(3):
            near_tile = tile + step - 1
            index = layout.last if near_tile < 0 else near_tile
            if near_tile < queries:
                inside = touches(query, near_tile) & (query < rows)
                inside &= lane < length - index * LANES
                found = bins_of(
                    numbers[index], chains[index], number_rows[tile], chain_rows[tile]
                )
                found = jnp.where(inside, found, zero_bin)
            else:
                found = jnp.full(shape, zero_bin, jnp.int32)
            forward_ref[
                tile * LANES : (tile + 1) * LANES, step * LANES : (step + 1) * LANES
            ] = found

    codes[...] = jnp.full(codes.shape, -1, jnp.int32)
    for tile in range(queries):
        size = min(LANES, rows - tile * LANES)
        code = number_rows[tile] * 8 + chain_rows[tile]
        codes[(tile + 1) * LANES : (tile + 1) * LANES + size] = code[:size]

    for index, tile in enumerate(list(range(queries)) + [-1]):
        source = layout.last if tile < 0 else tile
        key_row = (row - (length - last_start)) if tile < 0 else tile * LANES + row
        present = row < length - source * LANES
        for step in range(3):
            near_tile = tile + step - 1
            if 0 <= near_tile < queries:
                near_query = near_tile * LANES + lane
                inside = touches(near_query, tile) & (near_query < rows) & present
                found = bins_of(
                    number_rows[source], chain_rows[source], numbers[near_tile], chains[near_tile]
                )
                found = jnp.where(inside, found, zero_bin)
            else:
                found = jnp.full(shape, zero_bin, jnp.int32)
            backward_ref[
                index * LANES : (index + 1) * LANES, step * LANES : (step + 1) * LANES
            ] = found
        target = (number_rows[source] + reach - lane) * 8 + chain_rows[source]
        target = jnp.where(present & (lane > 0) & (lane < 2 * reach), target, -9)
        offset = (LANES - (length - last_start)) if tile < 0 else (tile + 1) * LANES
        far = 4 * LANES
        shift = jnp.full(shape, far, jnp.int32)
        for distance in range(-NEAR, NEAR + 1):
            other = codes[offset - distance : offset - distance + LANES]
            shift = jnp.where(other == target, distance, shift)
        if tile < 0:
            base = jnp.zeros(shape, jnp.int32)
        else:
            base = jnp.where(row < LANES // 2, tile - 1, tile) * LANES
        places_ref[index * LANES : (index + 1) * LANES] = jnp.where(
            shift == far, far - 1, key_row - shift - base
        )


def attention_tables(layout, numbers, marks, query_start, bin_count):
    crops = numbers.shape[0]
    pairs = jnp.stack([numbers, marks], axis=1)
    pairs = pad_to(pairs, 2, layout.wide, 0).reshape(crops, 2, layout.key_tiles, LANES)
    spots = (layout.query_tiles + 1) * LANES
    shapes = [
        ((layout.length, LANES), jnp.bfloat16),
        ((layout.block_rows, LANES), jnp.int32),
        ((layout.padded, 3 * LANES), jnp.int32),
        ((spots, 3 * LANES), jnp.int32),
        ((spots, LANES), jnp.int32),
    ]
    return pl.pallas_call(
        functools.partial(tables_kernel, layout, bin_count),
        grid=(crops,),
        in_specs=[
            pl.BlockSpec(memory_space=pltpu.SMEM),
            pl.BlockSpec((None, 2, layout.key_tiles, LANES), lambda crop: (crop, 0, 0, 0)),
        ],
        out_specs=tuple(pl.BlockSpec((None, *shape), lambda crop: (crop, 0, 0)) for shape, _ in shapes),
        out_shape=tuple(jax.ShapeDtypeStruct((crops, *shape), kind) for shape, kind in shapes),
        scratch_shapes=[pltpu.VMEM((layout.padded + 2 * LANES, LANES), jnp.int32)],
        compiler_params=pltpu.CompilerParams(vmem_limit_bytes=VMEM_BYTES),
        cost_estimate=pl.CostEstimate(
            flops=40000000 * crops, bytes_accessed=4000000 * crops, transcendentals=0
        ),
        name="pair_tables",
    )(jnp.reshape(query_start, (1,)).astype(jnp.int32), pairs)


def head_tables(layout, bias_rows, scale):
    bin_count, heads = bias_rows.shape
    table = (bias_rows - bias_rows[bin_count - 1 :]).T / scale
    lane = jnp.arange(LANES, dtype=jnp.int32)
    groups = layout.groups

    def columns(values):
        upper = lax.reduce_precision(values, 8, 7)
        rest = values - upper
        return jnp.where(
            lane < groups, upper[:, None], jnp.where(lane < 2 * groups, rest[:, None], 0.0)
        )

    lookup = pad_to(table, 1, LANES, 0.0)
    stacked = jnp.stack([lookup, columns(table[:, bin_count - 2]), columns(table[:, 0])], 1)
    stacked = pad_to(stacked, 1, 8, 0.0)
    return stacked.reshape(heads // 2, 16, LANES)


NT = (((1,), (1,)), ((), ()))
TN = (((0,), (0,)), ((), ()))


def wide_dot(former, latter, numbers=(((1,), (0,)), ((), ()))):
    return lax.dot_general(former, latter, numbers, preferred_element_type=jnp.float32)


def look_up(table_row, bins):
    table = jnp.broadcast_to(table_row, bins.shape)
    return jnp.take_along_axis(table, bins, axis=1, mode="promise_in_bounds")


def half_of(values, lane, side):
    return jnp.where((lane >= 64) == (side == 1), values, jnp.zeros_like(values))


def row_blocks(total, size):
    return [(start, min(start + size, total)) for start in range(0, total, size)]


def group_columns(kinds, tables, side):
    right = tables[8 * side + 1 : 8 * side + 2]
    left = tables[8 * side + 2 : 8 * side + 3]
    return jnp.where(kinds == RIGHT, right, jnp.where(kinds == LEFT, left, 0.0))


def forward_kernel(layout, scale, *refs):
    count = len(layout.pieces)
    query_ref = refs[0]
    key_refs = refs[1 : 1 + count]
    value_refs = refs[1 + count : 1 + 2 * count]
    members_ref, kinds_ref, bins_ref, tables_ref, out_ref, log_ref = refs[1 + 2 * count : -1]
    all_scores = refs[-1]
    pair = pl.program_id(1)
    rows, length = layout.block_rows, layout.length
    turn = 0
    factor = scale * LOG2E
    lane = lax.broadcasted_iota(jnp.int32, (1, LANES), 1)
    query = query_ref[...]
    keys = jnp.concatenate([ref[...] for ref in key_refs], axis=0)
    values = jnp.concatenate([ref[...] for ref in value_refs], axis=0)
    members = members_ref[...]
    kinds = kinds_ref[...]
    tables = tables_ref[...]
    ones = jnp.ones((length, LANES), jnp.bfloat16)

    @pl.when(pair == 0)
    def _():
        log_ref[...] = jnp.zeros_like(log_ref)

    for side in range(2):
        key_columns = jnp.concatenate([half_of(keys, lane, side), members], axis=1)
        value_columns = jnp.concatenate([half_of(values, lane, side), ones], axis=1)
        extra = group_columns(kinds, tables, side).astype(jnp.bfloat16)
        query_columns = jnp.concatenate([query, extra], axis=1)
        table_row = tables[8 * side : 8 * side + 1]
        for start, stop in row_blocks(rows, 256):
            size = stop - start
            scores = all_scores.at[turn % 2]
            turn += 1
            scores[0:size, 0:length] = wide_dot(query_columns[start:stop], key_columns, NT)
            for tile in range(start // LANES, -(-stop // LANES)):
                first, final = tile * LANES, min(tile * LANES + LANES, rows)
                for slot in range(3):
                    other = tile + slot - 1
                    if other >= layout.query_tiles:
                        continue
                    low, high = first, final
                    if slot == 0:
                        high = min(first + 32, final)
                    if slot == 2:
                        low = first + LANES - 32
                    if low >= high:
                        continue
                    place = layout.tile_start(other)
                    width = min(LANES, length - place)
                    bins = bins_ref[low:high, slot * LANES : (slot + 1) * LANES]
                    bias = look_up(table_row, bins)[:, :width]
                    scores[low - start : high - start, place : place + width] += bias
            block = scores[0:size, 0:length]
            top = jnp.max(block, axis=1, keepdims=True)
            weights = jnp.exp2((block - top) * factor).astype(jnp.bfloat16)
            sums = wide_dot(weights, value_columns)
            total = sums[:, LANES:]
            result = sums[:, :LANES] / total
            if side == 0:
                out_ref[start:stop] = result
            else:
                out_ref[start:stop] += result
            log_total = top + jnp.log(total) * (1.0 / scale)
            log_ref[start:stop] = jnp.where(
                lane == 2 * pair + side, log_total, log_ref[start:stop]
            )


def backward_kernel(layout, scale, first_pair, *refs):
    count = len(layout.pieces)
    query_ref, grad_ref, out_ref, log_ref = refs[:4]
    key_refs = refs[4 : 4 + count]
    value_refs = refs[4 + count : 4 + 2 * count]
    rest = refs[4 + 2 * count :]
    members_ref, kinds_ref, bins_ref, places_ref, tables_ref = rest[:5]
    grad_query_ref = rest[5]
    grad_pair_refs = rest[6 : 6 + count]
    grad_table_ref = rest[6 + count]
    query_wide, grad_wide, query_half, grad_half, all_scores, all_slopes, slopes_low = rest[7 + count :]
    pair = pl.program_id(1) + first_pair
    rows, length, padded = layout.block_rows, layout.length, layout.padded
    factor = scale * LOG2E
    lane = lax.broadcasted_iota(jnp.int32, (1, LANES), 1)
    keys = jnp.concatenate([ref[...] for ref in key_refs], axis=0)
    values = jnp.concatenate([ref[...] for ref in value_refs], axis=0)
    members = members_ref[...]
    kinds = kinds_ref[...]
    tables = tables_ref[...]
    query = query_ref[...]
    grad = grad_ref[...]
    grad_full = grad.astype(jnp.float32)
    product = grad_full * out_ref[...]
    log_all = log_ref[...]
    tail = 2 * layout.groups
    ones = jnp.broadcast_to(jnp.where(lane < 3, 1.0, 0.0), (length, LANES)).astype(jnp.bfloat16)

    def three_parts(values):
        upper = values.astype(jnp.bfloat16).astype(jnp.float32)
        values = values - upper
        middle = values.astype(jnp.bfloat16).astype(jnp.float32)
        return upper, middle, values - middle

    def in_lanes(parts, first):
        return jnp.where(
            lane == first,
            parts[0],
            jnp.where(lane == first + 1, parts[1], jnp.where(lane == first + 2, parts[2], 0.0)),
        )

    if padded > rows:
        for ref in (query_wide, grad_wide, query_half, grad_half):
            for side in range(2):
                ref[side, rows:padded] = jnp.zeros((padded - rows, ref.shape[2]), jnp.bfloat16)
    for side in range(2):
        log_total = jnp.sum(
            jnp.where(lane == 2 * pair + side, log_all, 0.0), axis=1, keepdims=True
        )
        extra = group_columns(kinds, tables, side) + in_lanes(three_parts(log_total), tail)
        query_wide[side, 0:rows, 0:LANES] = query
        query_wide[side, 0:rows, LANES:] = extra.astype(jnp.bfloat16)
        delta = jnp.sum(half_of(product, lane, side), axis=1, keepdims=True)
        grad_wide[side, 0:rows, 0:LANES] = grad
        grad_wide[side, 0:rows, LANES:] = in_lanes(three_parts(-delta), 0).astype(jnp.bfloat16)
        query_half[side, 0:rows] = half_of(query, lane, side)
        grad_half[side, 0:rows] = half_of(grad, lane, side)

    key_columns = [
        jnp.concatenate([half_of(keys, lane, side), members], axis=1) for side in range(2)
    ]
    value_columns = [
        jnp.concatenate([half_of(values, lane, side), ones], axis=1) for side in range(2)
    ]
    inner_sums = [jnp.zeros((1, LANES), jnp.float32) for _ in range(2)]
    low_sums = [jnp.zeros((1, LANES), jnp.float32) for _ in range(2)]
    high_sums = [jnp.zeros((1, LANES), jnp.float32) for _ in range(2)]
    reach_tiles = list(range(layout.query_tiles)) + [-1]

    def put(which, start, stop, result):
        begin = 0
        for ref, size in zip(grad_pair_refs, layout.pieces):
            low, high = max(start, begin), min(stop, begin + size)
            if low < high:
                ref[which, low - begin : high - begin] = result[low - start : high - start]
            begin += size

    for start, stop in row_blocks(length, 384):
        size = stop - start
        grad_key = grad_value = None
        for side in range(2):
            table_row = tables[8 * side : 8 * side + 1]
            scores, slopes = all_scores.at[side], all_slopes.at[side]
            scores[0:size] = wide_dot(key_columns[side][start:stop], query_wide[side], NT)
            near = []
            for index, tile in enumerate(reach_tiles):
                place = layout.tile_start(tile)
                if start <= place < stop:
                    near.append((index, tile, place, min(place + LANES, length)))
            for index, tile, place, final in near:
                for slot in range(3):
                    other = tile + slot - 1
                    if not 0 <= other < layout.query_tiles:
                        continue
                    bins = bins_ref[
                        index * LANES : index * LANES + final - place,
                        slot * LANES : (slot + 1) * LANES,
                    ]
                    scores[
                        place - start : final - start, other * LANES : (other + 1) * LANES
                    ] += look_up(table_row, bins)
            probs = jnp.exp2(scores[0:size] * factor)
            grad_probs = wide_dot(value_columns[side][start:stop], grad_wide[side], NT)
            slope = probs * grad_probs
            if near:
                slopes[0:size] = slope
            low = slope.astype(jnp.bfloat16)
            slopes_low[side, start:stop] = low
            part = wide_dot(low, query_half[side])
            grad_key = part if grad_key is None else grad_key + part
            part = wide_dot(probs.astype(jnp.bfloat16), grad_half[side])
            grad_value = part if grad_value is None else grad_value + part
            for index, tile, place, final in near:
                for slot in range(3):
                    other = tile + slot - 1
                    if not 0 <= other < layout.query_tiles:
                        continue
                    bins = bins_ref[
                        index * LANES : index * LANES + final - place,
                        slot * LANES : (slot + 1) * LANES,
                    ]
                    cut = slopes[place - start : final - start, other * LANES : (other + 1) * LANES]
                    low_sums[side] += jnp.sum(
                        jnp.where(bins == 0, cut, 0.0), axis=0, keepdims=True
                    )
                    high_sums[side] += jnp.sum(
                        jnp.where(bins == 2 * (NEAR + 1), cut, 0.0), axis=0, keepdims=True
                    )
                for half in range(2):
                    begin, end = half * 64, min(half * 64 + 64, final - place)
                    if begin >= end:
                        continue
                    base = 0 if tile < 0 else tile - 1 + half
                    where = places_ref[index * LANES + begin : index * LANES + end]
                    spot = where & (LANES - 1)
                    for step in range(2):
                        other = base + step
                        if not 0 <= other < layout.query_tiles or (tile < 0 and step):
                            continue
                        cut = slopes[
                            place - start + begin : place - start + end,
                            other * LANES : (other + 1) * LANES,
                        ]
                        picked = jnp.take_along_axis(cut, spot, axis=1, mode="promise_in_bounds")
                        picked = jnp.where((where >> 7) == step, picked, 0.0)
                        inner_sums[side] += jnp.sum(picked, axis=0, keepdims=True)
        put(0, start, stop, (grad_key * scale).astype(jnp.bfloat16))
        put(1, start, stop, grad_value.astype(jnp.bfloat16))

    grad_query = None
    for side in range(2):
        both = wide_dot(slopes_low[side], key_columns[side], TN)[0:rows]
        part = both[:, :LANES]
        grad_query = part if grad_query is None else grad_query + part
        sums = jnp.where(lane < layout.groups, both[:, LANES:], 0.0)

        def total(kind):
            return jnp.sum(jnp.where(kinds == kind, sums, 0.0))

        right = total(RIGHT) + jnp.sum(high_sums[side])
        left = total(LEFT) + jnp.sum(low_sums[side])
        apart = total(APART)
        grad_table_ref[side : side + 1] = jnp.where(
            lane == 0,
            left,
            jnp.where(
                lane == 2 * (NEAR + 1),
                right,
                jnp.where(lane == 2 * (NEAR + 1) + 1, apart, inner_sums[side]),
            ),
        )
    grad_query_ref[...] = (grad_query * scale).astype(jnp.bfloat16)


def tile_columns(rows, offset=0):
    return pl.BlockSpec((None, rows, LANES), lambda crop, pair: (crop, 0, pair + offset))


def per_crop(rows, width):
    return pl.BlockSpec((None, rows, width), lambda crop, pair: (crop, 0, 0))


def kernel_params():
    return pltpu.CompilerParams(
        vmem_limit_bytes=VMEM_BYTES, dimension_semantics=("arbitrary", "arbitrary")
    )


def attention_forward(layout, scale, projected, key_values, members, kinds, bins, tables):
    crops, rows, _ = projected.shape
    pairs = tables.shape[0]
    specs = [tile_columns(rows)]
    operands = [projected]
    for place in (1, 2):
        for piece in key_values:
            specs.append(tile_columns(piece[0].shape[1], piece[place]))
            operands.append(piece[0])
    specs += [
        per_crop(layout.length, LANES),
        per_crop(rows, LANES),
        per_crop(layout.padded, 3 * LANES),
        pl.BlockSpec((None, 16, LANES), lambda crop, pair: (pair, 0, 0)),
    ]
    flops = 2 * crops * pairs * 2 * rows * layout.length * 256 * 2
    return pl.pallas_call(
        functools.partial(forward_kernel, layout, scale),
        grid=(crops, pairs),
        in_specs=specs,
        out_specs=(tile_columns(rows), per_crop(rows, LANES)),
        out_shape=(
            jax.ShapeDtypeStruct((crops, rows, pairs * LANES), jnp.float32),
            jax.ShapeDtypeStruct((crops, rows, LANES), jnp.float32),
        ),
        scratch_shapes=[pltpu.VMEM((2, 256, layout.wide), jnp.float32)],
        compiler_params=kernel_params(),
        cost_estimate=pl.CostEstimate(
            flops=flops,
            bytes_accessed=12 * crops * rows * pairs * LANES,
            transcendentals=crops * pairs * 2 * rows * layout.length,
        ),
        name="attention_forward",
    )(*operands, members, kinds, bins, tables)


def attention_backward(
    layout,
    scale,
    first_pair,
    pairs,
    projected,
    grad_out,
    attended,
    logs,
    key_values,
    members,
    kinds,
    bins,
    places,
    tables,
):
    crops, rows, _ = projected.shape
    specs = [tile_columns(rows, first_pair)] * 3 + [per_crop(rows, LANES)]
    operands = [projected, grad_out, attended, logs]
    for place in (1, 2):
        for piece in key_values:
            specs.append(tile_columns(piece[0].shape[1], piece[place] + first_pair))
            operands.append(piece[0])
    specs += [
        per_crop(layout.length, LANES),
        per_crop(rows, LANES),
        per_crop(bins.shape[1], 3 * LANES),
        per_crop(places.shape[1], LANES),
        pl.BlockSpec((None, 16, LANES), lambda crop, pair: (pair + first_pair, 0, 0)),
    ]
    out_specs = [tile_columns(rows)]
    out_shapes = [jax.ShapeDtypeStruct((crops, rows, pairs * LANES), jnp.bfloat16)]
    for piece in key_values:
        size = piece[0].shape[1]
        out_specs.append(
            pl.BlockSpec((None, 2, size, LANES), lambda crop, pair: (crop, 0, 0, pair))
        )
        out_shapes.append(jax.ShapeDtypeStruct((crops, 2, size, pairs * LANES), jnp.bfloat16))
    out_specs.append(pl.BlockSpec((None, None, 8, LANES), lambda crop, pair: (crop, pair, 0, 0)))
    out_shapes.append(jax.ShapeDtypeStruct((crops, pairs, 8, LANES), jnp.float32))
    padded, block = layout.padded, 384
    return pl.pallas_call(
        functools.partial(backward_kernel, layout, scale, first_pair),
        grid=(crops, pairs),
        in_specs=specs,
        out_specs=tuple(out_specs),
        out_shape=tuple(out_shapes),
        scratch_shapes=[
            pltpu.VMEM((2, padded, 2 * LANES), jnp.bfloat16),
            pltpu.VMEM((2, padded, 2 * LANES), jnp.bfloat16),
            pltpu.VMEM((2, padded, LANES), jnp.bfloat16),
            pltpu.VMEM((2, padded, LANES), jnp.bfloat16),
            pltpu.VMEM((2, block, padded), jnp.float32),
            pltpu.VMEM((2, block, padded), jnp.float32),
            pltpu.VMEM((2, layout.length, padded), jnp.bfloat16),
        ],
        compiler_params=kernel_params(),
        cost_estimate=pl.CostEstimate(
            flops=2 * crops * pairs * 2 * rows * layout.length * 256 * 5,
            bytes_accessed=20 * crops * rows * pairs * LANES,
            transcendentals=crops * pairs * 2 * rows * layout.length,
        ),
        name="attention_backward",
    )(*operands, members, kinds, bins, places, tables)


def sigmoid(values):
    return 0.5 * jnp.tanh(0.5 * values) + 0.5


def fold_rows(values):
    return jnp.sum(values.reshape(values.shape[0] // 8, 8, values.shape[1]), axis=0)


def feed_kernel(split, chunks, here_ref, *refs):
    (attended_ref, tokens_ref, upstream_ref, normed_a_ref, mod_ref, gate_weight_ref, output_ref) = refs[:7]
    gate_ref, up_ref, down_ref = refs[7:10]
    layer_ref, grad_middle_ref, grad_att_ref, grad_pre_ref, sums_ref = refs[10:15]
    grads = refs[15:-12]
    gated, grad_ff, normed, branch, middle, total, grad_normed, hidden, both, grad_branch = refs[-12:-2]
    gate_pre, turned = refs[-2:]
    step = pl.program_id(0)
    here = here_ref[0]
    rows, width = tokens_ref.shape
    size = gate_ref.shape[1]
    strip = 112 if rows % 112 == 0 else 64
    strips = rows // strip
    shift_f, scale_f = mod_ref[3:4], mod_ref[4:5]
    open_a, open_f = sigmoid(mod_ref[2:3]), sigmoid(mod_ref[5:6])

    def strip_of(index):
        return pl.ds(pl.multiple_of(index * strip, strip), strip)

    def norm_of(values):
        mean_value = jnp.mean(values, axis=1, keepdims=True)
        centred = values - mean_value
        spread = jnp.mean(centred * centred, axis=1, keepdims=True)
        root = lax.rsqrt(spread + 1e-06)
        return centred * root, root

    @pl.when(step == 0)
    def _():
        gate_pre[...] = wide_dot(normed_a_ref[...], gate_weight_ref[...])

        @pl.loop(0, strips)
        def _(index):
            cut = strip_of(index)
            gated[cut] = (attended_ref[cut] * sigmoid(gate_pre[cut])).astype(jnp.bfloat16)
            grad_ff[cut] = (upstream_ref[cut].astype(jnp.float32) * open_f).astype(jnp.bfloat16)

        branch[...] = wide_dot(gated[...], output_ref[...])

        @pl.loop(0, strips)
        def _(index):
            cut = strip_of(index)
            values = tokens_ref[cut].astype(jnp.float32) + open_a * branch[cut]
            middle[cut] = values
            normed[cut] = (norm_of(values)[0] * (1.0 + scale_f) + shift_f).astype(jnp.bfloat16)
            total[cut] = jnp.zeros((strip, width), jnp.float32)
            grad_normed[cut] = jnp.zeros((strip, width), jnp.float32)

        turned[...] = normed[...].T

    block = rows if rows <= 384 else rows // 2
    for start in range(0, rows, block):
        cut = slice(start, start + block)
        before = wide_dot(normed[cut], gate_ref[...])
        lifted = wide_dot(normed[cut], up_ref[...])
        grad_hidden = wide_dot(grad_ff[cut], down_ref[...], NT)
        switch = sigmoid(before)
        silu = before * switch
        part = (silu * lifted).astype(jnp.bfloat16)
        hidden[cut] = part
        grad_up = (grad_hidden * silu).astype(jnp.bfloat16)
        grad_gate = (grad_hidden * lifted * (switch + silu * (1.0 - switch))).astype(jnp.bfloat16)
        both[cut, :size] = grad_gate
        both[cut, size:] = grad_up
        total[cut] += wide_dot(part, down_ref[...])
        grad_normed[cut] += wide_dot(grad_gate, gate_ref[...], NT) + wide_dot(
            grad_up, up_ref[...], NT
        )

    pair = wide_dot(turned[...], both[...]).astype(jnp.bfloat16)
    if split:
        gate_send, gate_keep, up_send, up_keep, down_send, down_keep, small_send, small_keep = grads
        half = width // 2
        away = pl.ds(pl.multiple_of((1 - here) * half, LANES), half)
        home = pl.ds(pl.multiple_of(here * half, LANES), half)
        down_send[...] = wide_dot(hidden[...], grad_ff[:, away], TN).astype(jnp.bfloat16)
        down_keep[...] = wide_dot(hidden[...], grad_ff[:, home], TN).astype(jnp.bfloat16)

        @pl.when(step < chunks // 2)
        def _():
            gate_send[...] = pair[:, :size]
            up_send[...] = pair[:, size:]

        @pl.when(step >= chunks // 2)
        def _():
            gate_keep[...] = pair[:, :size]
            up_keep[...] = pair[:, size:]
    else:
        gate_all, up_all, down_all, small_all = grads
        gate_all[...] = pair[:, :size]
        up_all[...] = pair[:, size:]
        down_all[...] = wide_dot(hidden[...], grad_ff[...], TN).astype(jnp.bfloat16)

    @pl.when(step == chunks - 1)
    def _():
        def finish(index, sums):
            gate_f_sum, shift_sum, scale_sum, gate_a_sum = sums
            cut = strip_of(index)
            values = middle[cut]
            fed = total[cut]
            upstream = upstream_ref[cut].astype(jnp.float32)
            layer_ref[cut] = (values + open_f * fed).astype(jnp.bfloat16)
            normal, root = norm_of(values)
            grad = grad_normed[cut]
            scaled = grad * (1.0 + scale_f)
            grad_middle = upstream + root * (
                scaled
                - jnp.mean(scaled, axis=1, keepdims=True)
                - normal * jnp.mean(scaled * normal, axis=1, keepdims=True)
            )
            grad_middle_ref[cut] = grad_middle
            grad_branch[cut] = (grad_middle * open_a).astype(jnp.bfloat16)
            return (
                gate_f_sum + fold_rows(upstream * fed),
                shift_sum + fold_rows(grad),
                scale_sum + fold_rows(grad * normal),
                gate_a_sum + fold_rows(grad_middle * branch[cut]),
            )

        zero = jnp.zeros((8, width), jnp.float32)
        sums = lax.fori_loop(0, strips, finish, (zero, zero, zero, zero))
        gate_f_sum, shift_sum, scale_sum, gate_a_sum = [
            jnp.sum(value, axis=0, keepdims=True) for value in sums
        ]
        none = jnp.zeros((1, width), jnp.float32)
        sums_ref[...] = jnp.concatenate(
            [
                none,
                none,
                gate_a_sum * open_a * (1.0 - open_a),
                shift_sum,
                scale_sum,
                gate_f_sum * open_f * (1.0 - open_f),
                none,
                none,
            ],
            axis=0,
        )
        total[...] = wide_dot(grad_branch[...], output_ref[...], NT)

        @pl.loop(0, strips)
        def _(index):
            cut = strip_of(index)
            grad_gated = total[cut]
            opened = sigmoid(gate_pre[cut])
            grad_att_ref[cut] = (grad_gated * opened).astype(jnp.bfloat16)
            grad_pre_ref[cut] = (
                grad_gated * attended_ref[cut] * (opened * (1.0 - opened))
            ).astype(jnp.bfloat16)

        if split:
            for side, ref in ((away, small_send), (home, small_keep)):
                ref[:, :half] = wide_dot(gated[...], grad_branch[:, side], TN).astype(jnp.bfloat16)
                ref[:, half:] = wide_dot(normed_a_ref[...], grad_pre_ref[:, side], TN).astype(
                    jnp.bfloat16
                )
        else:
            small_all[:, :width] = wide_dot(gated[...], grad_branch[...], TN).astype(jnp.bfloat16)
            small_all[:, width:] = wide_dot(normed_a_ref[...], grad_pre_ref[...], TN).astype(
                jnp.bfloat16
            )


def feed_layer(
    split, here, attended, tokens, upstream, normed_a, mod_rows, gate_weight, output_weight, feed_gate, feed_up, feed_down
):
    rows, width = tokens.shape
    inner = feed_gate.shape[1]
    size = 512
    chunks = inner // size
    half = chunks // 2

    def turn(step, here_ref):
        return (step + half * (1 - here_ref[0])) % chunks if split else step

    def fixed(shape):
        return pl.BlockSpec(shape, lambda step, here_ref: (0, 0), pipeline_mode=pl.Buffered(1))

    def columns(step, here_ref):
        return (0, turn(step, here_ref))

    def strips(step, here_ref):
        return (turn(step, here_ref), 0)

    whole = (rows, width)
    in_specs = [fixed(whole)] * 4 + [
        fixed((8, width)),
        fixed((width, width)),
        fixed((width, width)),
        pl.BlockSpec((width, size), columns),
        pl.BlockSpec((width, size), columns),
        pl.BlockSpec((size, width), strips),
    ]
    out_specs = [fixed(whole)] * 4 + [fixed((8, width))]
    bf16, f32 = jnp.bfloat16, jnp.float32
    out_shapes = [(whole, bf16), (whole, f32), (whole, bf16), (whole, bf16), ((8, width), f32)]
    if split:
        first = pl.BlockSpec((width, size), lambda step, here_ref: (0, jnp.minimum(step, half - 1)))
        second = pl.BlockSpec((width, size), lambda step, here_ref: (0, jnp.maximum(step - half, 0)))
        out_specs += [first, second, first, second]
        out_shapes += [((width, inner // 2), bf16)] * 4
        out_specs += [pl.BlockSpec((size, width // 2), strips)] * 2
        out_shapes += [((inner, width // 2), bf16)] * 2
        out_specs += [fixed((width, width))] * 2
        out_shapes += [((width, width), bf16)] * 2
    else:
        out_specs += [pl.BlockSpec((width, size), columns)] * 2
        out_shapes += [((width, inner), bf16)] * 2
        out_specs += [pl.BlockSpec((size, width), strips), fixed((width, 2 * width))]
        out_shapes += [((inner, width), bf16), ((width, 2 * width), bf16)]
    return pl.pallas_call(
        functools.partial(feed_kernel, split, chunks),
        grid_spec=pltpu.PrefetchScalarGridSpec(
            num_scalar_prefetch=1,
            grid=(chunks,),
            in_specs=in_specs,
            out_specs=tuple(out_specs),
            scratch_shapes=[
                pltpu.VMEM(whole, bf16),
                pltpu.VMEM(whole, bf16),
                pltpu.VMEM(whole, bf16),
                pltpu.VMEM(whole, f32),
                pltpu.VMEM(whole, f32),
                pltpu.VMEM(whole, f32),
                pltpu.VMEM(whole, f32),
                pltpu.VMEM((rows, size), bf16),
                pltpu.VMEM((rows, 2 * size), bf16),
                pltpu.VMEM(whole, bf16),
                pltpu.VMEM(whole, f32),
                pltpu.VMEM((width, rows), bf16),
            ],
        ),
        out_shape=tuple(jax.ShapeDtypeStruct(shape, kind) for shape, kind in out_shapes),
        compiler_params=pltpu.CompilerParams(vmem_limit_bytes=VMEM_BYTES),
        cost_estimate=pl.CostEstimate(
            flops=2 * rows * width * (9 * inner + 5 * width),
            bytes_accessed=12 * width * inner + 24 * rows * width,
            transcendentals=2 * rows * inner,
        ),
        name="feed_layer",
    )(
        jnp.reshape(here, (1,)).astype(jnp.int32),
        attended,
        tokens,
        upstream,
        normed_a,
        mod_rows,
        gate_weight,
        output_weight,
        feed_gate,
        feed_up,
        feed_down,
    )


MASKS = {"u": 8, "v": 4, "y": 2, "x": 1}


def exchange(values, mask):
    return lax.ppermute(values, "crop", [(i, i ^ mask) for i in range(16)])


def swap_res(values):
    return lax.ppermute(values, "res", [(0, 1), (1, 0)])


def tie(*values):
    return lax.optimization_barrier(values)


def add_low(former, latter, kind=jnp.bfloat16):
    return (former.astype(jnp.float32) + latter.astype(jnp.float32)).astype(kind)


def stage_kernel(part_counts, bits_ref, *refs):
    total = sum(part_counts)
    inputs, outputs = refs[: 4 * total], refs[4 * total :]
    place = 0
    for stream, parts in enumerate(part_counts):
        for side in range(2):
            out_ref = outputs[2 * stream + side]
            column = 0
            for part in range(parts):
                kept_ref, came_ref = inputs[4 * (place + part) + 2 * side :][:2]
                width = kept_ref.shape[-1]
                out_ref[..., column : column + width] = add_low(kept_ref[...], came_ref[...])
                column += width
        place += parts


class Halving:
    def __init__(self, orders):
        self.orders = [list(order) for order in orders]
        self.left = [list(MASKS) for _ in orders]

    def stage(self, streams):
        index = lax.axis_index("crop")
        self.masks, bits, places = [], [], []
        for order, left in zip(self.orders, self.left):
            axis = order.pop(0)
            places.append(len(left) - 1 - left.index(axis))
            left.remove(axis)
            self.masks.append(MASKS[axis])
            bits.append((index // MASKS[axis]) % 2)
        bits = jnp.stack(bits).astype(jnp.int32)
        chunks = 2 ** (len(self.left[0]) + 1)
        steps = min(2, chunks // 2)
        specs, operands, out_specs, out_shapes = [], [], [], []
        for stream, (parts, place) in enumerate(zip(streams, places)):
            low, high = 1 << place, chunks >> (place + 1)
            by_group = high >= steps
            block_high, block_low = (high // steps, low) if by_group else (high, low // steps)
            for kept, came, block, width in parts:
                rows = kept.shape[0] // chunks
                for side in range(2):

                    def cut(step, bits_ref, stream=stream, side=side, block=block, by_group=by_group):
                        bit = bits_ref[stream] if side else 1 - bits_ref[stream]
                        return (step, bit, 0, 0, block) if by_group else (0, bit, step, 0, block)

                    for value in (kept, came):
                        operands.append(value.reshape(high, 2, low, rows, value.shape[1]))
                        specs.append(
                            pl.BlockSpec((block_high, None, block_low, rows, width), cut)
                        )
            wide = sum(part[3] for part in parts)

            def out_cut(step, bits_ref, by_group=by_group):
                return (step, 0, 0, 0) if by_group else (0, step, 0, 0)

            for side in range(2):
                out_specs.append(pl.BlockSpec((block_high, block_low, rows, wide), out_cut))
                out_shapes.append(jax.ShapeDtypeStruct((high, low, rows, wide), jnp.bfloat16))
        results = pl.pallas_call(
            functools.partial(stage_kernel, [len(parts) for parts in streams]),
            grid_spec=pltpu.PrefetchScalarGridSpec(
                num_scalar_prefetch=1,
                grid=(steps,),
                in_specs=specs,
                out_specs=tuple(out_specs),
            ),
            out_shape=tuple(out_shapes),
            compiler_params=pltpu.CompilerParams(vmem_limit_bytes=VMEM_BYTES),
            cost_estimate=pl.CostEstimate(
                flops=sum(4 * math.prod(shape.shape) for shape in out_shapes),
                bytes_accessed=sum(6 * math.prod(shape.shape) for shape in out_shapes),
                transcendentals=0,
            ),
            name="halving_stage",
        )(bits, *operands)
        flat = [value.reshape(-1, value.shape[3]) for value in results]
        return flat[0::2], flat[1::2]

    def send(self, values):
        return [exchange(value, mask) for value, mask in zip(values, self.masks)]


def parts_of(kept, came):
    return [[(mine, other, 0, mine.shape[1])] for mine, other in zip(kept, came)]


def share_columns(values, parts):
    if parts == 1:
        return values.astype(jnp.bfloat16)
    return lax.psum_scatter(values.astype(jnp.bfloat16), "res", scatter_dimension=1, tiled=True)


def scatter_crops(values):
    return lax.psum_scatter(values, "crop", scatter_dimension=0, tiled=True).astype(jnp.float32)


def gather_crops(values, crop_parts):
    if crop_parts != 16:
        return lax.all_gather(values, "crop", axis=0, tiled=True)
    index = lax.axis_index("crop")
    for mask in (1, 2, 4, 8):
        other = exchange(values, mask)
        low = (index // mask) % 2 == 0
        values = jnp.concatenate(
            [jnp.where(low, values, other), jnp.where(low, other, values)], axis=0
        )
    return values


def sum_res(values, parts):
    if parts == 1:
        return values
    if parts != 2:
        return lax.psum(values, "res")
    return values + swap_res(values)


PACK = 1152
SIDE = 384


def whole_vmem(count):
    return [pl.BlockSpec(memory_space=pltpu.VMEM)] * count


def scalars(*values):
    return jnp.stack([jnp.asarray(value, jnp.int32) for value in values])


def local_call(kernel, numbers, operands, shapes, name, flops=0):
    return pl.pallas_call(
        kernel,
        in_specs=[pl.BlockSpec(memory_space=pltpu.SMEM)] + whole_vmem(len(operands)),
        out_specs=tuple(whole_vmem(len(shapes))),
        out_shape=tuple(jax.ShapeDtypeStruct(shape, kind) for shape, kind in shapes),
        compiler_params=pltpu.CompilerParams(vmem_limit_bytes=VMEM_BYTES),
        cost_estimate=pl.CostEstimate(
            flops=flops,
            bytes_accessed=sum(value.size * value.dtype.itemsize for value in operands)
            + sum(4 * math.prod(shape) for shape, _ in shapes),
            transcendentals=0,
        ),
        name=name,
    )(numbers, *operands)


def projection_kernel(counts, here_ref, normed_ref, *refs):
    calls = len(counts)
    parts, (joined_ref, send_ref, keep_ref) = refs[: 3 * calls], refs[3 * calls :]
    width = joined_ref.shape[1] // 3
    column = 0
    for call, pairs in enumerate(counts):
        size = pairs * LANES
        query_ref, own_ref, came_ref = parts[3 * call : 3 * call + 3]
        joined_ref[:, column : column + size] = query_ref[...]
        for which in range(2):
            first = (1 + which) * width + column
            joined_ref[:, first : first + size] = add_low(own_ref[which], came_ref[which])
        column += size
    half = send_ref.shape[1]
    for side, ref in ((1 - here_ref[0], send_ref), (here_ref[0], keep_ref)):
        columns = pl.ds(pl.multiple_of(side * half, LANES), half)
        ref[...] = wide_dot(normed_ref[...], joined_ref[:, columns], TN).astype(jnp.bfloat16)


def projection_gradient(here, normed_a, calls):
    rows, width = normed_a.shape
    counts = [call[0].shape[-1] // LANES for call in calls]
    return local_call(
        functools.partial(projection_kernel, counts),
        scalars(here),
        [normed_a] + [value for call in calls for value in call],
        [
            ((rows, 3 * width), jnp.bfloat16),
            ((width, 3 * width // 2), jnp.bfloat16),
            ((width, 3 * width // 2), jnp.bfloat16),
        ],
        "projection_gradient",
        6 * rows * width * width,
    )


def finish_kernel(counts, joined_ref, weight_ref, pre_ref, gate_ref, tokens_ref, middle_ref, mod_ref, *refs):
    feed_sums_ref, extra_ref = refs[:2]
    table_refs = refs[2 : 2 + len(counts)]
    out_ref, pack_ref, total = refs[2 + len(counts) :]
    step = pl.program_id(0)
    rows, width = tokens_ref.shape
    part = wide_dot(joined_ref[...], weight_ref[...], NT)

    @pl.when(step == 0)
    def _():
        total[...] = part + wide_dot(pre_ref[...], gate_ref[...], NT)

    @pl.when(step > 0)
    def _():
        total[...] += part

    @pl.when(step == pl.num_programs(0) - 1)
    def _():
        strip = 112 if rows % 112 == 0 else 64
        scale = mod_ref[1:2]

        def finish(index, sums):
            shift_sum, scale_sum = sums
            cut = pl.ds(pl.multiple_of(index * strip, strip), strip)
            values = tokens_ref[cut].astype(jnp.float32)
            centred = values - jnp.mean(values, axis=1, keepdims=True)
            root = lax.rsqrt(jnp.mean(centred * centred, axis=1, keepdims=True) + 1e-06)
            normal = centred * root
            grad = total[cut]
            scaled = grad * (1.0 + scale)
            out_ref[cut] = (
                middle_ref[cut]
                + root
                * (
                    scaled
                    - jnp.mean(scaled, axis=1, keepdims=True)
                    - normal * jnp.mean(scaled * normal, axis=1, keepdims=True)
                )
            ).astype(jnp.bfloat16)
            return shift_sum + fold_rows(grad), scale_sum + fold_rows(grad * normal)

        zero = jnp.zeros((8, width), jnp.float32)
        shift_sum, scale_sum = lax.fori_loop(0, rows // strip, finish, (zero, zero))
        heads = []
        for ref, pairs in zip(table_refs, counts):
            for pair in range(pairs):
                heads += [ref[pair, 0:1], ref[pair, 1:2]]

        def upper_of(values):
            return values.astype(jnp.bfloat16).astype(jnp.float32)

        rests = [head - upper_of(head) for head in heads]
        count = width // LANES
        left = [
            jnp.sum(shift_sum, axis=0, keepdims=True),
            jnp.sum(scale_sum, axis=0, keepdims=True),
            feed_sums_ref[2:6],
        ]
        left += [
            jnp.concatenate(rests[i : i + count], axis=1) for i in range(0, len(heads), count)
        ]
        right = [jnp.concatenate(heads[3 * i : 3 * i + 3], axis=1) for i in range(4)]
        line = extra_ref[5:6]
        right += [extra_ref[4:5], line, line - upper_of(line), extra_ref[7:8]]
        pack = jnp.concatenate(
            [jnp.concatenate(left, axis=0), jnp.concatenate(right, axis=0)], axis=1
        )
        pack_ref[...] = jnp.concatenate([pack, jnp.zeros_like(pack)], axis=0).astype(jnp.bfloat16)


def finish_layer(
    joined, weight, grad_pre, gate_weight, tokens, grad_middle, mod_rows, feed_sums, extra, grad_tables
):
    rows, width = tokens.shape
    counts = [table.shape[0] for table in grad_tables]

    def fixed(shape):
        return pl.BlockSpec(shape, lambda step: (0,) * len(shape), pipeline_mode=pl.Buffered(1))

    return pl.pallas_call(
        functools.partial(finish_kernel, counts),
        grid=(3,),
        in_specs=[
            pl.BlockSpec((rows, width), lambda step: (0, step)),
            pl.BlockSpec((width, width), lambda step: (0, step)),
            fixed((rows, width)),
            fixed((width, width)),
            fixed((rows, width)),
            fixed((rows, width)),
            fixed((8, width)),
            fixed((8, width)),
            fixed((8, SIDE)),
        ]
        + [fixed((count, 8, LANES)) for count in counts],
        out_specs=(fixed((rows, width)), fixed((16, PACK))),
        out_shape=(
            jax.ShapeDtypeStruct((rows, width), jnp.bfloat16),
            jax.ShapeDtypeStruct((16, PACK), jnp.bfloat16),
        ),
        scratch_shapes=[pltpu.VMEM((rows, width), jnp.float32)],
        compiler_params=pltpu.CompilerParams(vmem_limit_bytes=VMEM_BYTES),
        cost_estimate=pl.CostEstimate(
            flops=8 * rows * width * width, bytes_accessed=24 * rows * width, transcendentals=0
        ),
        name="finish_layer",
    )(
        joined,
        weight,
        grad_pre,
        gate_weight,
        tokens,
        grad_middle,
        mod_rows,
        feed_sums,
        extra,
        *grad_tables,
    )


def fan_first_kernel(bits_ref, keep_ref, came_ref, mine_ref, *send_refs):
    chunk = keep_ref.shape[0] // 16
    for other, ref in enumerate((mine_ref, *send_refs)):
        for level in range(4):
            start = (level * 4 + (bits_ref[0] ^ other)) * chunk
            cut = pl.ds(pl.multiple_of(start, 16), chunk)
            ref[level * chunk : (level + 1) * chunk] = add_low(keep_ref[cut], came_ref[cut])


def fan_second_kernel(bits_ref, mine_ref, *refs):
    came_refs, pack_refs = refs[:3], refs[3:7]
    out_ref, *send_refs = refs[7:11]
    packs_ref = refs[11]
    chunk = mine_ref.shape[0] // 4
    packs = [ref[...].astype(jnp.float32)[0:8] for ref in pack_refs]
    packs_ref[...] = jnp.concatenate(packs, axis=0).astype(jnp.bfloat16)
    for other, ref in enumerate((out_ref, *send_refs)):
        cut = pl.ds(pl.multiple_of((bits_ref[0] ^ other) * chunk, 16), chunk)
        total = mine_ref[cut].astype(jnp.float32)
        for came_ref in came_refs:
            total = total + came_ref[cut].astype(jnp.float32)
        ref[0:chunk] = total.astype(jnp.bfloat16)
        if other:
            ref[chunk : chunk + 32] = packs_ref[...]


def fan_third_kernel(bits_ref, mine_ref, *refs):
    came_refs, packs_ref, (out_ref, all_ref) = refs[:3], refs[3], refs[4:]
    chunk = mine_ref.shape[0]
    total = mine_ref[...].astype(jnp.float32)
    all_ref[0:32] = packs_ref[...]
    for other, ref in enumerate(came_refs):
        total = total + ref[0:chunk].astype(jnp.float32)
        all_ref[32 * other + 32 : 32 * other + 64] = ref[chunk : chunk + 32]
    out_ref[...] = total


def last_sums_kernel(widths, bits_ref, *refs):
    count = len(widths)
    outputs = list(refs[2 * count :])
    for stream, cuts in enumerate(widths):
        kept_ref, came_ref = refs[2 * stream], refs[2 * stream + 1]
        column = 0
        for width in cuts:
            columns = slice(column, column + width)
            outputs.pop(0)[...] = add_low(kept_ref[:, columns], came_ref[:, columns], jnp.float32)
            column += width


def last_sums(kept, came, widths):
    operands = [value for pair in zip(kept, came) for value in pair]
    shapes = [
        ((mine.shape[0], width), jnp.float32) for mine, cuts in zip(kept, widths) for width in cuts
    ]
    return local_call(
        functools.partial(last_sums_kernel, widths), scalars(0), operands, shapes, "last_sums"
    )


def small_kernel(
    heads,
    here_ref,
    mine_ref,
    came_ref,
    modulation_ref,
    pair_norm_ref,
    relative_ref,
    gain_ref,
    pair_weight_ref,
    mod_grad_ref,
    time_ref,
    label_ref,
    relative_grad_ref,
    gain_grad_ref,
    pair_grad_ref,
    grad_condition,
):
    step = pl.program_id(0)
    crops = mine_ref.shape[0] // 8
    width = mine_ref.shape[1] - SIDE
    shape = (crops, mine_ref.shape[0])
    row = lax.broadcasted_iota(jnp.int32, shape, 1)
    crop = lax.broadcasted_iota(jnp.int32, shape, 0)

    def chosen(*lines):
        local = row - crop * 8
        hit = functools.reduce(jnp.logical_or, [local == line for line in lines])
        return jnp.where(hit, 1.0, 0.0).astype(jnp.bfloat16)

    def parts_split(values):
        upper = values.astype(jnp.bfloat16)
        return upper, (values - upper.astype(jnp.float32)).astype(jnp.bfloat16)

    def dot_left(narrow, values, numbers):
        upper, rest = parts_split(values)
        return wide_dot(narrow, upper, numbers) + wide_dot(narrow, rest, numbers)

    def dot_right(values, narrow, numbers):
        upper, rest = parts_split(values)
        return wide_dot(upper, narrow, numbers) + wide_dot(rest, narrow, numbers)

    cond_line = wide_dot(chosen(5, 6), mine_ref[:, width:])
    condition = cond_line[:, :256]
    gate_value = sigmoid(condition)
    cond_act = (condition * gate_value).astype(jnp.bfloat16)
    part = None
    for turn in range(mod_grad_ref.shape[1] // width):
        pick = chosen(step * (mod_grad_ref.shape[1] // width) + turn)
        columns = slice(turn * width, (turn + 1) * width)
        grad_mod = wide_dot(pick, mine_ref[:, :width]) + wide_dot(pick, came_ref[:, :width])
        mod_grad_ref[:, columns] = dot_left(cond_act, grad_mod, TN)
        more = dot_right(grad_mod, modulation_ref[:, columns], NT)
        part = more if part is None else part + more

    @pl.when(step == 0)
    def _():
        grad_condition[...] = part
        line = lax.broadcasted_iota(jnp.int32, (8, shape[1]), 0)
        local = lax.broadcasted_iota(jnp.int32, (8, shape[1]), 1) & 7
        every = jnp.where(local == line, 1.0, 0.0).astype(jnp.bfloat16)
        lines = wide_dot(every, mine_ref[...]) + wide_dot(every, came_ref[...])

        def of_head(head):
            upper = width + (head % 3) * LANES
            rest = (head % (width // LANES)) * LANES
            low = 6 + head // (width // LANES)
            return (
                lines[head // 3 : head // 3 + 1, upper : upper + LANES]
                + lines[low : low + 1, rest : rest + LANES]
            )

        table = jnp.concatenate(
            [of_head(head) for head in range(heads)]
            + [jnp.zeros((16 - heads, LANES), jnp.float32)],
            axis=0,
        )
        bins = relative_ref.shape[0]
        pair_grad_ref[...] = dot_left(pair_norm_ref[...], table, (((0,), (1,)), ((), ())))[:, :heads]
        grad_norm = dot_right(table, pair_weight_ref[...], (((0,), (1,)), ((), ())))[:bins]
        values = relative_ref[...]
        centred = values - jnp.mean(values, axis=1, keepdims=True)
        root = lax.rsqrt(jnp.mean(centred * centred, axis=1, keepdims=True) + 1e-06)
        normal = centred * root
        gain_grad_ref[...] = jnp.sum(grad_norm * normal, axis=0, keepdims=True)
        scaled = grad_norm * gain_ref[...]
        relative_grad_ref[...] = root * (
            scaled
            - jnp.mean(scaled, axis=1, keepdims=True)
            - normal * jnp.mean(scaled * normal, axis=1, keepdims=True)
        )

    @pl.when(step > 0)
    def _():
        grad_condition[...] += part

    @pl.when(step == pl.num_programs(0) - 1)
    def _():
        final = grad_condition[...] * (gate_value * (1.0 + condition * (1.0 - gate_value)))
        features = wide_dot(chosen(4), mine_ref[:, width:])[:, :256].astype(jnp.bfloat16)
        time_ref[...] = dot_left(features, final, TN)
        label = lax.broadcasted_iota(jnp.int32, (crops, label_ref.shape[0]), 1)
        number = cond_line[:, 256:257].astype(jnp.int32)
        onehot = jnp.where(label == number, 1.0, 0.0).astype(jnp.bfloat16)
        label_ref[...] = dot_left(onehot, final, TN)


def small_gradients(mine, came, modulation_weight, pair_norm, relative, gain, pair_weight, labels):
    conds, wide = modulation_weight.shape
    bins = relative.shape[0]
    heads = pair_weight.shape[1]
    rows = mine.shape[0]
    steps = 3

    def fixed(shape):
        return pl.BlockSpec(shape, lambda step: (0, 0))

    shapes = [(conds, wide), (conds, conds), (labels, conds), (bins, conds), (1, conds), (conds, heads)]
    return pl.pallas_call(
        functools.partial(small_kernel, heads),
        grid=(steps,),
        in_specs=[
            pl.BlockSpec(memory_space=pltpu.SMEM),
            fixed((rows, PACK)),
            fixed((rows, PACK)),
            pl.BlockSpec((conds, wide // steps), lambda step: (0, step)),
            fixed((LANES, conds)),
            fixed((bins, conds)),
            fixed((1, conds)),
            fixed((conds, 16)),
        ],
        out_specs=tuple(
            [pl.BlockSpec((conds, wide // steps), lambda step: (0, step))]
            + [fixed(s) for s in shapes[1:]]
        ),
        out_shape=tuple(jax.ShapeDtypeStruct(shape, jnp.float32) for shape in shapes),
        scratch_shapes=[pltpu.VMEM((rows // 8, conds), jnp.float32)],
        compiler_params=pltpu.CompilerParams(vmem_limit_bytes=VMEM_BYTES),
        cost_estimate=pl.CostEstimate(
            flops=100000000, bytes_accessed=10000000, transcendentals=0
        ),
        name="small_gradients",
    )(
        scalars(0),
        mine,
        came,
        modulation_weight,
        pad_to(pair_norm, 0, LANES, 0.0),
        relative,
        gain.reshape(1, -1),
        pad_to(pair_weight, 1, 16, 0.0),
    )


def per_device(
    crop_parts,
    res_parts,
    tokens,
    cotangent,
    time_levels,
    cath_ids,
    residue_numbers,
    chain_mask,
    time_weight,
    label_table,
    modulation_weight,
    projection_weight,
    gate_weight,
    output_weight,
    relative_table,
    pair_gain,
    pair_weight,
    feed_gate,
    feed_up,
    feed_down,
):
    crop_count, row_count, model_width = tokens.shape
    crop_length = residue_numbers.shape[1]
    head_count = pair_weight.shape[1]
    head_width = model_width // head_count
    bin_count = relative_table.shape[0]
    label_count = label_table.shape[0]
    token_count = crop_count * row_count
    score_scale = head_width ** (-0.5)
    pairs = head_count // 2
    layout = Layout(row_count, crop_length)
    query_start = lax.axis_index("res") * row_count

    def conditioning(features, onehot):
        return jnp.dot(features, time_weight, preferred_element_type=jnp.float32) + jnp.dot(
            onehot, label_table, preferred_element_type=jnp.float32
        )

    features = time_features(time_levels, time_weight.shape[0]).astype(jnp.bfloat16)
    label_onehot = (cath_ids[:, None] == jnp.arange(label_count, dtype=jnp.int32)[None, :]).astype(
        jnp.bfloat16
    )
    condition = conditioning(features, label_onehot)
    cond_act = jax.nn.silu(condition).astype(jnp.bfloat16)
    modulation = jnp.dot(cond_act, modulation_weight, preferred_element_type=jnp.float32)
    modulation = modulation.reshape(crop_count, 6, 1, model_width)
    shift_a, scale_a = modulation[:, 0], modulation[:, 1]
    mod_rows = pad_to(modulation[:, :, 0], 1, 8, 0.0)

    rotated = lax.dynamic_slice_in_dim(
        jnp.concatenate([jnp.stack([residue_numbers, chain_mask])] * 2, 2), query_start, crop_length, 2
    )
    members, kinds, forward_bins, backward_bins, places = attention_tables(
        layout, rotated[0], rotated[1], query_start, bin_count
    )
    relative_values = relative_table.astype(jnp.float32)
    gain_values = pair_gain.astype(jnp.float32)
    pair_norm = normalize_rows(relative_values, gain_values).astype(jnp.bfloat16)
    bias_rows = jnp.dot(pair_norm, pair_weight, preferred_element_type=jnp.float32)
    tables = head_tables(layout, bias_rows, score_scale)

    token_values = tokens.astype(jnp.float32)
    normed_a = (
        modulate(token_values, shift_a, scale_a)
        .astype(jnp.bfloat16)
        .reshape(token_count, model_width)
    )
    def project(weight):
        rows = jnp.dot(normed_a, weight, preferred_element_type=jnp.float32)
        return rows.astype(jnp.bfloat16).reshape(crop_count, row_count, -1)

    key_values = project(projection_weight[:, model_width:])
    queries = project(projection_weight[:, :model_width])
    others = [
        lax.ppermute(
            key_values, "res", [((r + step) % res_parts, r) for r in range(res_parts)]
        )
        for step in range(1, res_parts)
    ]
    if len(layout.pieces) == 2:
        other = others[0] if len(others) == 1 else jnp.concatenate(others, axis=1)
        pieces = [(key_values, 0, pairs), (other, 0, pairs)]
    else:
        pieces = [(jnp.concatenate([key_values] + others, axis=1), 0, pairs)]

    def block_rows(values):
        return pad_to(values, 1, layout.block_rows, 0)

    attended, logs = attention_forward(
        layout,
        score_scale,
        block_rows(queries),
        pieces,
        members,
        kinds,
        forward_bins,
        tables,
    )
    here = lax.axis_index("res")
    split = res_parts == 2 and crop_parts == 16
    per_crop_results = [
        feed_layer(
            split,
            here,
            attended[crop],
            block_rows(tokens)[crop],
            block_rows(cotangent)[crop],
            block_rows(normed_a.reshape(tokens.shape))[crop],
            mod_rows[crop],
            gate_weight,
            output_weight,
            feed_gate,
            feed_up,
            feed_down,
        )
        for crop in range(crop_count)
    ]
    layer_out, grad_middle, grad_attended, grad_gate_pre, feed_sums = (
        jnp.stack([result[place] for result in per_crop_results]) for place in range(5)
    )
    layer_out, grad_middle = layer_out[:, :row_count], grad_middle[:, :row_count]
    grad_gate_pre = grad_gate_pre[:, :row_count].reshape(token_count, model_width)
    weight_grads = [
        sum(result[place].astype(jnp.float32) for result in per_crop_results).astype(jnp.bfloat16)
        if crop_count > 1
        else per_crop_results[0][place]
        for place in range(5, len(per_crop_results[0]))
    ]

    def backward_of(first_pair, count, grad_now):
        return attention_backward(
            layout,
            score_scale,
            first_pair,
            count,
            block_rows(queries),
            grad_now,
            attended,
            logs,
            pieces,
            members,
            kinds,
            backward_bins,
            places,
            tables,
        )

    if split:
        arrivals = [swap_res(weight_grads[place]) for place in (0, 2, 4, 6)]
        kept = [weight_grads[place] for place in (1, 3, 5, 7)]
        halving = Halving(["xyvu", "yvxu", "vxyu"])
        half = model_width // 2
        calls = [list(backward_of(0, 1, grad_attended))]
        arrivals, calls[0] = tie(arrivals, calls[0])
        (gate_w, up_w, down_w, small_w) = zip(kept, arrivals)
        streams = [
            [(*gate_w, 0, gate_w[0].shape[1]), (*small_w, 0, half)],
            [(*up_w, 0, up_w[0].shape[1]), (*small_w, 1, half)],
            [(*down_w, 0, half)],
        ]
        arrived = []
        for first_pair, count in ((1, 4), (5, 1)):
            arrived.append(swap_res(calls[-1][2][0]))
            sent, kept = halving.stage(streams if isinstance(streams, list) else parts_of(*streams))
            sent, grad_attended = tie(sent, grad_attended)
            came = halving.send(sent)
            calls.append(list(backward_of(first_pair, count, grad_attended)))
            came, calls[-1], arrived[-1] = tie(came, calls[-1], arrived[-1])
            streams = (kept, came)
        index = lax.axis_index("crop")
        bf16 = jnp.bfloat16
        share = model_width // 16
        away = swap_res(calls[2][2][0])
        joined, proj_send, proj_keep = projection_gradient(
            here,
            normed_a,
            [
                (calls[0][0][0], calls[0][1][0], arrived[0]),
                (calls[1][0][0], calls[1][1][0], arrived[1]),
                (calls[2][0][0], calls[2][1][0], away),
            ],
        )
        proj_came = swap_res(proj_send)
        streams, proj_keep = tie(streams, proj_keep)
        sent, kept = halving.stage(parts_of(*streams))
        sent, proj_came = tie(sent, proj_came)
        came = halving.send(sent)
        mine, *fan = local_call(
            fan_first_kernel,
            scalars(index % 4),
            [proj_keep, proj_came],
            [((4 * share, PACK), bf16)] * 4,
            "fan_first",
        )
        fan, joined = tie(fan, joined)
        fan_came = [exchange(value, mask + 1) for mask, value in enumerate(fan)]
        extra = jnp.concatenate(
            [
                pad_to(features.astype(jnp.float32), 1, SIDE, 0.0),
                jnp.concatenate(
                    [condition, pad_to(cath_ids.astype(jnp.float32)[:, None], 1, LANES, 0.0)], axis=1
                ),
            ],
            axis=0,
        )
        tokens_grad, pack = finish_layer(
            joined,
            projection_weight,
            grad_gate_pre,
            gate_weight,
            tokens[0],
            grad_middle[0],
            mod_rows[0],
            feed_sums[0],
            jnp.pad(extra, ((4, 2), (0, 0))),
            [call[-1][0] for call in calls],
        )
        tokens_grad = tokens_grad[None]
        came, pack = tie(came, pack)
        packs = [pack] + [exchange(pack, mask + 1) for mask in range(3)]
        sent, kept = halving.stage(parts_of(kept, came))
        came = halving.send(sent)
        fan_came, packs, sent = tie(fan_came, packs, sent)
        mine, *fan, packs = local_call(
            fan_second_kernel,
            scalars(index // 4),
            [mine, *fan_came, *packs],
            [((share, PACK), bf16)] + [((share + 32, PACK), bf16)] * 3 + [((32, PACK), bf16)],
            "fan_second",
        )
        came, fan = tie(came, fan)
        fan_came = [exchange(value, 4 * (mask + 1)) for mask, value in enumerate(fan)]
        inner = feed_gate.shape[1] // 2
        finals = last_sums(kept, came, [[inner, half], [inner, half], [half]])
        fan_came, finals = tie(fan_came, finals)
        feed_gate_grad, output_weight_grad, feed_up_grad, gate_weight_grad, feed_down_grad = finals
        projection_weight_grad, packs = local_call(
            fan_third_kernel,
            scalars(0),
            [mine, *fan_came, packs],
            [((share, PACK), jnp.float32), ((128, PACK), bf16)],
            "fan_third",
        )
        (
            modulation_weight_grad,
            time_weight_grad,
            label_table_grad,
            relative_table_grad,
            pair_gain_grad,
            pair_weight_grad,
        ) = small_gradients(
            packs,
            swap_res(packs),
            modulation_weight,
            pair_norm,
            relative_values,
            gain_values,
            pair_weight,
            label_count,
        )
        pair_gain_grad = pair_gain_grad[0]
    else:
        results = backward_of(0, pairs, grad_attended)
        grad_table = results[-1]
        grad_pairs = results[1:-1]
        if len(grad_pairs) == 2:
            total, away = grad_pairs[0].astype(jnp.float32), grad_pairs[1]
        else:
            total = grad_pairs[0][:, :, :row_count].astype(jnp.float32)
            away = grad_pairs[0][:, :, row_count:]
        for step in range(1, res_parts):
            sent = away[:, :, (step - 1) * row_count : step * row_count]
            pairs_to = [(r, (r + step) % res_parts) for r in range(res_parts)]
            total = total + lax.ppermute(sent, "res", pairs_to).astype(jnp.float32)
        total = total.astype(jnp.bfloat16)
        grad_projected = jnp.concatenate(
            [results[0][:, :row_count], total[:, 0], total[:, 1]], axis=-1
        ).reshape(token_count, 3 * model_width)
        grad_normed_a = against_columns(grad_projected, projection_weight) + against_columns(
            grad_gate_pre, gate_weight
        )
        norm_back_a = jax.vjp(modulate, token_values, shift_a, scale_a)[1]
        grad_tokens, grad_shift_a, grad_scale_a = norm_back_a(
            grad_normed_a.reshape(crop_count, row_count, model_width)
        )
        tokens_grad = (grad_middle + grad_tokens).astype(jnp.bfloat16)
        feed_gate_grad, feed_up_grad, feed_down_grad = (
            scatter_crops(share_columns(value, res_parts)) for value in weight_grads[:3]
        )
        output_weight_grad, gate_weight_grad = (
            scatter_crops(share_columns(value, res_parts))
            for value in (weight_grads[3][:, :model_width], weight_grads[3][:, model_width:])
        )
        projection_weight_grad = scatter_crops(
            share_columns(across_rows(normed_a, grad_projected), res_parts)
        )
        grad_table = grad_table[:, :, :2].sum(0).reshape(head_count, LANES)

        grad_modulation = jnp.concatenate([grad_shift_a, grad_scale_a, feed_sums[:, 2:6]], axis=1)
        grad_modulation = grad_modulation.reshape(crop_count, 6 * model_width)
        table_row = grad_table.reshape(1, head_count * LANES)
        first_row = (jnp.arange(crop_count) == 0).astype(jnp.float32)[:, None]
        small_here = jnp.concatenate([grad_modulation, first_row * table_row], axis=1)
        levels_here = jnp.stack([time_levels, cath_ids.astype(jnp.float32)], axis=1)
        levels_here = pad_to(levels_here, 1, LANES, 0.0)
        small_all = gather_crops(
            jnp.concatenate([levels_here, sum_res(small_here, res_parts)], axis=1), crop_parts
        )
        levels_all, small_all = small_all[:, :2], small_all[:, LANES:]
        grad_modulation = small_all[:, : 6 * model_width]
        grad_table = jnp.sum(small_all[:, 6 * model_width :], axis=0).reshape(head_count, LANES)
        grad_table = grad_table[:, :bin_count]
        features_all = time_features(levels_all[:, 0], time_weight.shape[0]).astype(jnp.bfloat16)
        onehot_all = (
            levels_all[:, 1].astype(jnp.int32)[:, None]
            == jnp.arange(label_count, dtype=jnp.int32)[None, :]
        ).astype(jnp.bfloat16)
        condition = conditioning(features_all, onehot_all)
        cond_act = jax.nn.silu(condition).astype(jnp.bfloat16)
        modulation_weight_grad = split_left(cond_act, grad_modulation, 0, 0)
        grad_condition = split_left(modulation_weight, grad_modulation, 1, 1).T * silu_slope(condition)
        time_weight_grad = split_left(features_all, grad_condition, 0, 0)
        label_table_grad = split_left(onehot_all, grad_condition, 0, 0)
        pair_weight_grad = split_left(pair_norm, grad_table, 0, 1)
        grad_pair_norm = split_right(grad_table, pair_weight, 0, 1)
        pair_back = jax.vjp(normalize_rows, relative_values, gain_values)[1]
        relative_table_grad, pair_gain_grad = pair_back(grad_pair_norm)
    return (
        layer_out,
        tokens_grad,
        time_weight_grad,
        label_table_grad,
        modulation_weight_grad,
        projection_weight_grad,
        gate_weight_grad,
        output_weight_grad,
        relative_table_grad,
        pair_gain_grad,
        pair_weight_grad,
        feed_gate_grad,
        feed_up_grad,
        feed_down_grad,
    )


def solution(mesh):
    return jax.shard_map(
        functools.partial(per_device, mesh.shape["crop"], mesh.shape["res"]),
        mesh=mesh,
        in_specs=(
            P("crop", "res", None),
            P("crop", "res", None),
            P("crop"),
            P("crop"),
            P("crop", None),
            P("crop", None),
            P(),
            P(),
            P(),
            P(),
            P(),
            P(),
            P(),
            P(),
            P(),
            P(),
            P(),
            P(),
        ),
        out_specs=(
            P("crop", "res", None),
            P("crop", "res", None),
            P(),
            P(),
            P(),
            P("crop", "res"),
            P("crop", "res"),
            P("crop", "res"),
            P(),
            P(),
            P(),
            P("crop", "res"),
            P("crop", "res"),
            P("crop", "res"),
        ),
        check_vma=False,
    )
```

```python
import functools
import math

import jax
import jax.numpy as jnp
from jax import lax
from jax.experimental import pallas as pl
from jax.experimental.pallas import tpu as pltpu
from jax.sharding import PartitionSpec as P

LANES = 128
NEAR = 31
VMEM_BYTES = 56 * 1024 * 1024
LOG2E = 1.4426950408889634
NONE, RIGHT, LEFT, APART = 0, 1, 2, 3


def layer_norm(inputs):
    mean_value = jnp.mean(inputs, axis=-1, keepdims=True)
    centred = inputs - mean_value
    spread = jnp.mean(centred * centred, axis=-1, keepdims=True)
    return centred * lax.rsqrt(spread + 1e-06)


def modulate(inputs, shift_row, scale_row):
    return layer_norm(inputs) * (1.0 + scale_row) + shift_row


def normalize_rows(table_rows, gain_row):
    return layer_norm(table_rows) * gain_row


def time_features(time_levels, feature_width):
    half_width = feature_width // 2
    frequency = jnp.exp(-math.log(10000.0) * jnp.arange(half_width, dtype=jnp.float32) / half_width)
    angles = 1000.0 * time_levels[:, None] * frequency[None, :]
    return jnp.concatenate([jnp.sin(angles), jnp.cos(angles)], axis=-1)


def across_rows(former, latter):
    return lax.dot_general(
        former, latter, (((0,), (0,)), ((), ())), preferred_element_type=jnp.float32
    )


def against_columns(former, latter):
    return lax.dot_general(
        former, latter, (((1,), (1,)), ((), ())), preferred_element_type=jnp.float32
    )


def split_parts(values):
    upper = lax.reduce_precision(values, 8, 7)
    return (upper.astype(jnp.bfloat16), (values - upper).astype(jnp.bfloat16))


def split_left(narrow, values, former_dim, latter_dim):
    upper, rest = split_parts(values)
    numbers = (((former_dim,), (latter_dim,)), ((), ()))
    return lax.dot_general(
        narrow, upper, numbers, preferred_element_type=jnp.float32
    ) + lax.dot_general(narrow, rest, numbers, preferred_element_type=jnp.float32)


def split_right(values, narrow, former_dim, latter_dim):
    upper, rest = split_parts(values)
    numbers = (((former_dim,), (latter_dim,)), ((), ()))
    return lax.dot_general(
        upper, narrow, numbers, preferred_element_type=jnp.float32
    ) + lax.dot_general(rest, narrow, numbers, preferred_element_type=jnp.float32)


def sigmoid_slope(inputs):
    gate_value = jax.nn.sigmoid(inputs)
    return gate_value * (1.0 - gate_value)


def silu_slope(inputs):
    gate_value = jax.nn.sigmoid(inputs)
    return gate_value * (1.0 + inputs * (1.0 - gate_value))


class Layout:
    def __init__(self, rows, length):
        self.rows = rows
        self.length = length
        self.query_tiles = -(-rows // LANES)
        self.key_tiles = -(-length // LANES)
        self.padded = self.query_tiles * LANES
        self.wide = self.key_tiles * LANES
        self.last = self.key_tiles - 1
        self.groups = (self.query_tiles + 4) * 4
        assert 2 * self.groups + 3 <= LANES
        assert rows - 1 + NEAR < self.padded and length - NEAR >= self.last * LANES
        assert rows % 8 == 0 and self.last > self.query_tiles
        self.block_rows = rows if rows % 16 == 0 else self.padded
        self.pieces = [rows, length - rows] if rows % 16 == 0 else [length]

    def tile_start(self, tile):
        return self.last * LANES if tile < 0 else tile * LANES


def pad_to(values, axis, size, fill):
    widths = [(0, 0)] * values.ndim
    widths[axis] = (0, size - values.shape[axis])
    return jnp.pad(values, widths, constant_values=fill)


def tables_kernel(layout, bin_count, start_ref, pairs_ref, *out_refs):
    members_ref, kinds_ref, forward_ref, backward_ref, places_ref, codes = out_refs
    rows, length, queries, groups = layout.rows, layout.length, layout.query_tiles, layout.groups
    wrap = length - start_ref[0]
    reach = (bin_count - 2) // 2
    zero_bin = LANES - 1
    shape = (LANES, LANES)
    lane = lax.broadcasted_iota(jnp.int32, shape, 1)
    row = lax.broadcasted_iota(jnp.int32, shape, 0)
    last_start = layout.last * LANES

    tiles = pairs_ref.shape[1]
    marks = pairs_ref[1].astype(jnp.float32)
    place = lax.broadcasted_iota(jnp.int32, marks.shape, 0) * LANES + lax.broadcasted_iota(
        jnp.int32, marks.shape, 1
    )
    before = jnp.sum(jnp.where(place < wrap, marks, 0.0), keepdims=True)
    every = jnp.sum(marks, keepdims=True)
    triangle = jnp.where(row <= lane, 1.0, 0.0).astype(jnp.bfloat16)
    running = jnp.dot(marks.astype(jnp.bfloat16), triangle, preferred_element_type=jnp.float32)
    numbers, chains = [], []
    carry = jnp.zeros((1, 1), jnp.float32)
    for tile in range(layout.key_tiles):
        count = running[tile : tile + 1] + carry
        carry = carry + running[tile : tile + 1, LANES - 1 :]
        count = count + jnp.where(place[tile : tile + 1] < wrap, every - before, -before)
        chains.append(jnp.broadcast_to(count.astype(jnp.int32), shape))
        numbers.append(jnp.broadcast_to(pairs_ref[0, tile : tile + 1], shape))
    number_rows = [value.T for value in numbers]
    chain_rows = [value.T for value in chains]

    def bins_of(key_number, key_chain, query_number, query_chain):
        offset = jnp.clip(key_number - query_number, -reach, reach) + reach
        return jnp.where(key_chain == query_chain, offset, bin_count - 1)

    def touches(query, tile):
        begin = -LANES if tile < 0 else tile * LANES
        return (begin <= query + NEAR) & (query - NEAR <= begin + LANES - 1)

    for tile in range(layout.key_tiles):
        size = min(LANES, length - tile * LANES)
        key = tile * LANES + row
        if tile == layout.last:
            other = jnp.full(shape, queries + 3, jnp.int32)
        elif tile == queries - 1:
            other = jnp.full(shape, queries, jnp.int32)
        else:
            other = jnp.where(key < wrap, queries + 1, queries + 2)
        group = jnp.where(key < rows, tile, other)
        slot = group * 4 + chain_rows[tile] - 1
        hit = (lane == slot) | (lane == slot + groups)
        tail = (lane >= 2 * groups) & (lane < 2 * groups + 3)
        values = jnp.where(hit, 1.0, jnp.where(tail, -1.0, 0.0)).astype(jnp.bfloat16)
        members_ref[tile * LANES : tile * LANES + size] = values[:size]

    local = jnp.where(lane >= groups, lane - groups, lane)
    lane_group = local >> 2
    lane_chain = (local & 3) + 1
    lane_begin = jnp.where(
        lane_group < queries,
        lane_group * LANES,
        jnp.where(lane_group == queries, (queries - 1) * LANES, -LANES),
    )
    has_band = (lane_group <= queries) | (lane_group == queries + 3)
    other_right = jnp.where(
        lane_group == queries,
        rows,
        jnp.where(
            lane_group == queries + 3,
            last_start,
            jnp.where(lane_group == queries + 1, 0, 2 * length),
        ),
    )
    right_limit = jnp.where(lane_group > queries, jnp.where(lane_group == queries + 3, wrap, length), wrap)
    for tile in range(queries):
        size = min(LANES, layout.block_rows - tile * LANES)
        query = tile * LANES + row
        near = (lane_begin <= query + NEAR) & (query - NEAR <= lane_begin + LANES - 1) & has_band
        right = jnp.where(lane_group < queries, lane_group - tile, right_limit - other_right) > 0
        same = chain_rows[tile] == lane_chain
        kinds = jnp.where(same, jnp.where(near, NONE, jnp.where(right, RIGHT, LEFT)), APART)
        kinds = jnp.where((lane < 2 * groups) & (query < rows), kinds, NONE)
        kinds_ref[tile * LANES : tile * LANES + size] = kinds[:size]
        for step in range(3):
            near_tile = tile + step - 1
            index = layout.last if near_tile < 0 else near_tile
            if near_tile < queries:
                inside = touches(query, near_tile) & (query < rows)
                inside &= lane < length - index * LANES
                found = bins_of(
                    numbers[index], chains[index], number_rows[tile], chain_rows[tile]
                )
                found = jnp.where(inside, found, zero_bin)
            else:
                found = jnp.full(shape, zero_bin, jnp.int32)
            forward_ref[
                tile * LANES : (tile + 1) * LANES, step * LANES : (step + 1) * LANES
            ] = found

    codes[...] = jnp.full(codes.shape, -1, jnp.int32)
    for tile in range(queries):
        size = min(LANES, rows - tile * LANES)
        code = number_rows[tile] * 8 + chain_rows[tile]
        codes[(tile + 1) * LANES : (tile + 1) * LANES + size] = code[:size]

    for index, tile in enumerate(list(range(queries)) + [-1]):
        source = layout.last if tile < 0 else tile
        key_row = (row - (length - last_start)) if tile < 0 else tile * LANES + row
        present = row < length - source * LANES
        for step in range(3):
            near_tile = tile + step - 1
            if 0 <= near_tile < queries:
                near_query = near_tile * LANES + lane
                inside = touches(near_query, tile) & (near_query < rows) & present
                found = bins_of(
                    number_rows[source], chain_rows[source], numbers[near_tile], chains[near_tile]
                )
                found = jnp.where(inside, found, zero_bin)
            else:
                found = jnp.full(shape, zero_bin, jnp.int32)
            backward_ref[
                index * LANES : (index + 1) * LANES, step * LANES : (step + 1) * LANES
            ] = found
        target = (number_rows[source] + reach - lane) * 8 + chain_rows[source]
        target = jnp.where(present & (lane > 0) & (lane < 2 * reach), target, -9)
        offset = (LANES - (length - last_start)) if tile < 0 else (tile + 1) * LANES
        far = 4 * LANES
        shift = jnp.full(shape, far, jnp.int32)
        for distance in range(-NEAR, NEAR + 1):
            other = codes[offset - distance : offset - distance + LANES]
            shift = jnp.where(other == target, distance, shift)
        if tile < 0:
            base = jnp.zeros(shape, jnp.int32)
        else:
            base = jnp.where(row < LANES // 2, tile - 1, tile) * LANES
        places_ref[index * LANES : (index + 1) * LANES] = jnp.where(
            shift == far, far - 1, key_row - shift - base
        )


def attention_tables(layout, numbers, marks, query_start, bin_count):
    crops = numbers.shape[0]
    pairs = jnp.stack([numbers, marks], axis=1)
    pairs = pad_to(pairs, 2, layout.wide, 0).reshape(crops, 2, layout.key_tiles, LANES)
    spots = (layout.query_tiles + 1) * LANES
    shapes = [
        ((layout.length, LANES), jnp.bfloat16),
        ((layout.block_rows, LANES), jnp.int32),
        ((layout.padded, 3 * LANES), jnp.int32),
        ((spots, 3 * LANES), jnp.int32),
        ((spots, LANES), jnp.int32),
    ]
    return pl.pallas_call(
        functools.partial(tables_kernel, layout, bin_count),
        grid=(crops,),
        in_specs=[
            pl.BlockSpec(memory_space=pltpu.SMEM),
            pl.BlockSpec((None, 2, layout.key_tiles, LANES), lambda crop: (crop, 0, 0, 0)),
        ],
        out_specs=tuple(pl.BlockSpec((None, *shape), lambda crop: (crop, 0, 0)) for shape, _ in shapes),
        out_shape=tuple(jax.ShapeDtypeStruct((crops, *shape), kind) for shape, kind in shapes),
        scratch_shapes=[pltpu.VMEM((layout.padded + 2 * LANES, LANES), jnp.int32)],
        compiler_params=pltpu.CompilerParams(vmem_limit_bytes=VMEM_BYTES),
        cost_estimate=pl.CostEstimate(
            flops=40000000 * crops, bytes_accessed=4000000 * crops, transcendentals=0
        ),
        name="pair_tables",
    )(jnp.reshape(query_start, (1,)).astype(jnp.int32), pairs)


def head_tables(layout, bias_rows, scale):
    bin_count, heads = bias_rows.shape
    table = (bias_rows - bias_rows[bin_count - 1 :]).T / scale
    lane = jnp.arange(LANES, dtype=jnp.int32)
    groups = layout.groups

    def columns(values):
        upper = lax.reduce_precision(values, 8, 7)
        rest = values - upper
        return jnp.where(
            lane < groups, upper[:, None], jnp.where(lane < 2 * groups, rest[:, None], 0.0)
        )

    lookup = pad_to(table, 1, LANES, 0.0)
    stacked = jnp.stack([lookup, columns(table[:, bin_count - 2]), columns(table[:, 0])], 1)
    stacked = pad_to(stacked, 1, 8, 0.0)
    return stacked.reshape(heads // 2, 16, LANES)


NT = (((1,), (1,)), ((), ()))
TN = (((0,), (0,)), ((), ()))


def wide_dot(former, latter, numbers=(((1,), (0,)), ((), ()))):
    return lax.dot_general(former, latter, numbers, preferred_element_type=jnp.float32)


def look_up(table_row, bins):
    table = jnp.broadcast_to(table_row, bins.shape)
    return jnp.take_along_axis(table, bins, axis=1, mode="promise_in_bounds")


def half_of(values, lane, side):
    return jnp.where((lane >= 64) == (side == 1), values, jnp.zeros_like(values))


def row_blocks(total, size):
    return [(start, min(start + size, total)) for start in range(0, total, size)]


def group_columns(kinds, tables, side):
    right = tables[8 * side + 1 : 8 * side + 2]
    left = tables[8 * side + 2 : 8 * side + 3]
    return jnp.where(kinds == RIGHT, right, jnp.where(kinds == LEFT, left, 0.0))


def forward_kernel(layout, scale, *refs):
    count = len(layout.pieces)
    query_ref = refs[0]
    key_refs = refs[1 : 1 + count]
    value_refs = refs[1 + count : 1 + 2 * count]
    members_ref, kinds_ref, bins_ref, tables_ref, out_ref, log_ref = refs[1 + 2 * count : -1]
    all_scores = refs[-1]
    pair = pl.program_id(1)
    rows, length = layout.block_rows, layout.length
    turn = 0
    factor = scale * LOG2E
    lane = lax.broadcasted_iota(jnp.int32, (1, LANES), 1)
    query = query_ref[...]
    keys = jnp.concatenate([ref[...] for ref in key_refs], axis=0)
    values = jnp.concatenate([ref[...] for ref in value_refs], axis=0)
    members = members_ref[...]
    kinds = kinds_ref[...]
    tables = tables_ref[...]
    ones = jnp.ones((length, LANES), jnp.bfloat16)

    @pl.when(pair == 0)
    def _():
        log_ref[...] = jnp.zeros_like(log_ref)

    for side in range(2):
        key_columns = jnp.concatenate([half_of(keys, lane, side), members], axis=1)
        value_columns = jnp.concatenate([half_of(values, lane, side), ones], axis=1)
        extra = group_columns(kinds, tables, side).astype(jnp.bfloat16)
        query_columns = jnp.concatenate([query, extra], axis=1)
        table_row = tables[8 * side : 8 * side + 1]
        for start, stop in row_blocks(rows, 256):
            size = stop - start
            scores = all_scores.at[turn % 2]
            turn += 1
            scores[0:size, 0:length] = wide_dot(query_columns[start:stop], key_columns, NT)
            for tile in range(start // LANES, -(-stop // LANES)):
                first, final = tile * LANES, min(tile * LANES + LANES, rows)
                for slot in range(3):
                    other = tile + slot - 1
                    if other >= layout.query_tiles:
                        continue
                    low, high = first, final
                    if slot == 0:
                        high = min(first + 32, final)
                    if slot == 2:
                        low = first + LANES - 32
                    if low >= high:
                        continue
                    place = layout.tile_start(other)
                    width = min(LANES, length - place)
                    bins = bins_ref[low:high, slot * LANES : (slot + 1) * LANES]
                    bias = look_up(table_row, bins)[:, :width]
                    scores[low - start : high - start, place : place + width] += bias
            block = scores[0:size, 0:length]
            top = jnp.max(block, axis=1, keepdims=True)
            weights = jnp.exp2((block - top) * factor).astype(jnp.bfloat16)
            sums = wide_dot(weights, value_columns)
            total = sums[:, LANES:]
            result = sums[:, :LANES] / total
            if side == 0:
                out_ref[start:stop] = result
            else:
                out_ref[start:stop] += result
            log_total = top + jnp.log(total) * (1.0 / scale)
            log_ref[start:stop] = jnp.where(
                lane == 2 * pair + side, log_total, log_ref[start:stop]
            )


def backward_kernel(layout, scale, first_pair, *refs):
    count = len(layout.pieces)
    query_ref, grad_ref, out_ref, log_ref = refs[:4]
    key_refs = refs[4 : 4 + count]
    value_refs = refs[4 + count : 4 + 2 * count]
    rest = refs[4 + 2 * count :]
    members_ref, kinds_ref, bins_ref, places_ref, tables_ref = rest[:5]
    grad_query_ref = rest[5]
    grad_pair_refs = rest[6 : 6 + count]
    grad_table_ref = rest[6 + count]
    query_wide, grad_wide, query_half, grad_half, all_scores, all_slopes, slopes_low = rest[7 + count :]
    pair = pl.program_id(1) + first_pair
    rows, length, padded = layout.block_rows, layout.length, layout.padded
    factor = scale * LOG2E
    lane = lax.broadcasted_iota(jnp.int32, (1, LANES), 1)
    keys = jnp.concatenate([ref[...] for ref in key_refs], axis=0)
    values = jnp.concatenate([ref[...] for ref in value_refs], axis=0)
    members = members_ref[...]
    kinds = kinds_ref[...]
    tables = tables_ref[...]
    query = query_ref[...]
    grad = grad_ref[...]
    grad_full = grad.astype(jnp.float32)
    product = grad_full * out_ref[...]
    log_all = log_ref[...]
    tail = 2 * layout.groups
    ones = jnp.broadcast_to(jnp.where(lane < 3, 1.0, 0.0), (length, LANES)).astype(jnp.bfloat16)

    def three_parts(values):
        upper = values.astype(jnp.bfloat16).astype(jnp.float32)
        values = values - upper
        middle = values.astype(jnp.bfloat16).astype(jnp.float32)
        return upper, middle, values - middle

    def in_lanes(parts, first):
        return jnp.where(
            lane == first,
            parts[0],
            jnp.where(lane == first + 1, parts[1], jnp.where(lane == first + 2, parts[2], 0.0)),
        )

    if padded > rows:
        for ref in (query_wide, grad_wide, query_half, grad_half):
            for side in range(2):
                ref[side, rows:padded] = jnp.zeros((padded - rows, ref.shape[2]), jnp.bfloat16)
    for side in range(2):
        log_total = jnp.sum(
            jnp.where(lane == 2 * pair + side, log_all, 0.0), axis=1, keepdims=True
        )
        extra = group_columns(kinds, tables, side) + in_lanes(three_parts(log_total), tail)
        query_wide[side, 0:rows, 0:LANES] = query
        query_wide[side, 0:rows, LANES:] = extra.astype(jnp.bfloat16)
        delta = jnp.sum(half_of(product, lane, side), axis=1, keepdims=True)
        grad_wide[side, 0:rows, 0:LANES] = grad
        grad_wide[side, 0:rows, LANES:] = in_lanes(three_parts(-delta), 0).astype(jnp.bfloat16)
        query_half[side, 0:rows] = half_of(query, lane, side)
        grad_half[side, 0:rows] = half_of(grad, lane, side)

    key_columns = [
        jnp.concatenate([half_of(keys, lane, side), members], axis=1) for side in range(2)
    ]
    value_columns = [
        jnp.concatenate([half_of(values, lane, side), ones], axis=1) for side in range(2)
    ]
    inner_sums = [jnp.zeros((1, LANES), jnp.float32) for _ in range(2)]
    low_sums = [jnp.zeros((1, LANES), jnp.float32) for _ in range(2)]
    high_sums = [jnp.zeros((1, LANES), jnp.float32) for _ in range(2)]
    reach_tiles = list(range(layout.query_tiles)) + [-1]

    def put(which, start, stop, result):
        begin = 0
        for ref, size in zip(grad_pair_refs, layout.pieces):
            low, high = max(start, begin), min(stop, begin + size)
            if low < high:
                ref[which, low - begin : high - begin] = result[low - start : high - start]
            begin += size

    for start, stop in row_blocks(length, 384):
        size = stop - start
        grad_key = grad_value = None
        for side in range(2):
            table_row = tables[8 * side : 8 * side + 1]
            scores, slopes = all_scores.at[side], all_slopes.at[side]
            scores[0:size] = wide_dot(key_columns[side][start:stop], query_wide[side], NT)
            near = []
            for index, tile in enumerate(reach_tiles):
                place = layout.tile_start(tile)
                if start <= place < stop:
                    near.append((index, tile, place, min(place + LANES, length)))
            for index, tile, place, final in near:
                for slot in range(3):
                    other = tile + slot - 1
                    if not 0 <= other < layout.query_tiles:
                        continue
                    bins = bins_ref[
                        index * LANES : index * LANES + final - place,
                        slot * LANES : (slot + 1) * LANES,
                    ]
                    scores[
                        place - start : final - start, other * LANES : (other + 1) * LANES
                    ] += look_up(table_row, bins)
            probs = jnp.exp2(scores[0:size] * factor)
            grad_probs = wide_dot(value_columns[side][start:stop], grad_wide[side], NT)
            slope = probs * grad_probs
            if near:
                slopes[0:size] = slope
            low = slope.astype(jnp.bfloat16)
            slopes_low[side, start:stop] = low
            part = wide_dot(low, query_half[side])
            grad_key = part if grad_key is None else grad_key + part
            part = wide_dot(probs.astype(jnp.bfloat16), grad_half[side])
            grad_value = part if grad_value is None else grad_value + part
            for index, tile, place, final in near:
                for slot in range(3):
                    other = tile + slot - 1
                    if not 0 <= other < layout.query_tiles:
                        continue
                    bins = bins_ref[
                        index * LANES : index * LANES + final - place,
                        slot * LANES : (slot + 1) * LANES,
                    ]
                    cut = slopes[place - start : final - start, other * LANES : (other + 1) * LANES]
                    low_sums[side] += jnp.sum(
                        jnp.where(bins == 0, cut, 0.0), axis=0, keepdims=True
                    )
                    high_sums[side] += jnp.sum(
                        jnp.where(bins == 2 * (NEAR + 1), cut, 0.0), axis=0, keepdims=True
                    )
                for half in range(2):
                    begin, end = half * 64, min(half * 64 + 64, final - place)
                    if begin >= end:
                        continue
                    base = 0 if tile < 0 else tile - 1 + half
                    where = places_ref[index * LANES + begin : index * LANES + end]
                    spot = where & (LANES - 1)
                    for step in range(2):
                        other = base + step
                        if not 0 <= other < layout.query_tiles or (tile < 0 and step):
                            continue
                        cut = slopes[
                            place - start + begin : place - start + end,
                            other * LANES : (other + 1) * LANES,
                        ]
                        picked = jnp.take_along_axis(cut, spot, axis=1, mode="promise_in_bounds")
                        picked = jnp.where((where >> 7) == step, picked, 0.0)
                        inner_sums[side] += jnp.sum(picked, axis=0, keepdims=True)
        put(0, start, stop, (grad_key * scale).astype(jnp.bfloat16))
        put(1, start, stop, grad_value.astype(jnp.bfloat16))

    grad_query = None
    for side in range(2):
        both = wide_dot(slopes_low[side], key_columns[side], TN)[0:rows]
        part = both[:, :LANES]
        grad_query = part if grad_query is None else grad_query + part
        sums = jnp.where(lane < layout.groups, both[:, LANES:], 0.0)

        def total(kind):
            return jnp.sum(jnp.where(kinds == kind, sums, 0.0))

        right = total(RIGHT) + jnp.sum(high_sums[side])
        left = total(LEFT) + jnp.sum(low_sums[side])
        apart = total(APART)
        grad_table_ref[side : side + 1] = jnp.where(
            lane == 0,
            left,
            jnp.where(
                lane == 2 * (NEAR + 1),
                right,
                jnp.where(lane == 2 * (NEAR + 1) + 1, apart, inner_sums[side]),
            ),
        )
    grad_query_ref[...] = (grad_query * scale).astype(jnp.bfloat16)


def tile_columns(rows, offset=0):
    return pl.BlockSpec((None, rows, LANES), lambda crop, pair: (crop, 0, pair + offset))


def per_crop(rows, width):
    return pl.BlockSpec((None, rows, width), lambda crop, pair: (crop, 0, 0))


def kernel_params():
    return pltpu.CompilerParams(
        vmem_limit_bytes=VMEM_BYTES, dimension_semantics=("arbitrary", "arbitrary")
    )


def attention_forward(layout, scale, projected, key_values, members, kinds, bins, tables):
    crops, rows, _ = projected.shape
    pairs = tables.shape[0]
    specs = [tile_columns(rows)]
    operands = [projected]
    for place in (1, 2):
        for piece in key_values:
            specs.append(tile_columns(piece[0].shape[1], piece[place]))
            operands.append(piece[0])
    specs += [
        per_crop(layout.length, LANES),
        per_crop(rows, LANES),
        per_crop(layout.padded, 3 * LANES),
        pl.BlockSpec((None, 16, LANES), lambda crop, pair: (pair, 0, 0)),
    ]
    flops = 2 * crops * pairs * 2 * rows * layout.length * 256 * 2
    return pl.pallas_call(
        functools.partial(forward_kernel, layout, scale),
        grid=(crops, pairs),
        in_specs=specs,
        out_specs=(tile_columns(rows), per_crop(rows, LANES)),
        out_shape=(
            jax.ShapeDtypeStruct((crops, rows, pairs * LANES), jnp.float32),
            jax.ShapeDtypeStruct((crops, rows, LANES), jnp.float32),
        ),
        scratch_shapes=[pltpu.VMEM((2, 256, layout.wide), jnp.float32)],
        compiler_params=kernel_params(),
        cost_estimate=pl.CostEstimate(
            flops=flops,
            bytes_accessed=12 * crops * rows * pairs * LANES,
            transcendentals=crops * pairs * 2 * rows * layout.length,
        ),
        name="attention_forward",
    )(*operands, members, kinds, bins, tables)


def attention_backward(
    layout,
    scale,
    first_pair,
    pairs,
    projected,
    grad_out,
    attended,
    logs,
    key_values,
    members,
    kinds,
    bins,
    places,
    tables,
):
    crops, rows, _ = projected.shape
    specs = [tile_columns(rows, first_pair)] * 3 + [per_crop(rows, LANES)]
    operands = [projected, grad_out, attended, logs]
    for place in (1, 2):
        for piece in key_values:
            specs.append(tile_columns(piece[0].shape[1], piece[place] + first_pair))
            operands.append(piece[0])
    specs += [
        per_crop(layout.length, LANES),
        per_crop(rows, LANES),
        per_crop(bins.shape[1], 3 * LANES),
        per_crop(places.shape[1], LANES),
        pl.BlockSpec((None, 16, LANES), lambda crop, pair: (pair + first_pair, 0, 0)),
    ]
    out_specs = [tile_columns(rows)]
    out_shapes = [jax.ShapeDtypeStruct((crops, rows, pairs * LANES), jnp.bfloat16)]
    for piece in key_values:
        size = piece[0].shape[1]
        out_specs.append(
            pl.BlockSpec((None, 2, size, LANES), lambda crop, pair: (crop, 0, 0, pair))
        )
        out_shapes.append(jax.ShapeDtypeStruct((crops, 2, size, pairs * LANES), jnp.bfloat16))
    out_specs.append(pl.BlockSpec((None, None, 8, LANES), lambda crop, pair: (crop, pair, 0, 0)))
    out_shapes.append(jax.ShapeDtypeStruct((crops, pairs, 8, LANES), jnp.float32))
    padded, block = layout.padded, 384
    return pl.pallas_call(
        functools.partial(backward_kernel, layout, scale, first_pair),
        grid=(crops, pairs),
        in_specs=specs,
        out_specs=tuple(out_specs),
        out_shape=tuple(out_shapes),
        scratch_shapes=[
            pltpu.VMEM((2, padded, 2 * LANES), jnp.bfloat16),
            pltpu.VMEM((2, padded, 2 * LANES), jnp.bfloat16),
            pltpu.VMEM((2, padded, LANES), jnp.bfloat16),
            pltpu.VMEM((2, padded, LANES), jnp.bfloat16),
            pltpu.VMEM((2, block, padded), jnp.float32),
            pltpu.VMEM((2, block, padded), jnp.float32),
            pltpu.VMEM((2, layout.length, padded), jnp.bfloat16),
        ],
        compiler_params=kernel_params(),
        cost_estimate=pl.CostEstimate(
            flops=2 * crops * pairs * 2 * rows * layout.length * 256 * 5,
            bytes_accessed=20 * crops * rows * pairs * LANES,
            transcendentals=crops * pairs * 2 * rows * layout.length,
        ),
        name="attention_backward",
    )(*operands, members, kinds, bins, places, tables)


def sigmoid(values):
    return 0.5 * jnp.tanh(0.5 * values) + 0.5


def fold_rows(values):
    return jnp.sum(values.reshape(values.shape[0] // 8, 8, values.shape[1]), axis=0)


def feed_kernel(split, chunks, here_ref, *refs):
    (attended_ref, tokens_ref, upstream_ref, normed_a_ref, mod_ref, gate_weight_ref, output_ref) = refs[:7]
    gate_ref, up_ref, down_ref = refs[7:10]
    layer_ref, grad_middle_ref, grad_att_ref, grad_pre_ref, sums_ref = refs[10:15]
    grads = refs[15:-12]
    gated, grad_ff, normed, branch, middle, total, grad_normed, hidden, both, grad_branch = refs[-12:-2]
    gate_pre, turned = refs[-2:]
    step = pl.program_id(0)
    here = here_ref[0]
    rows, width = tokens_ref.shape
    size = gate_ref.shape[1]
    strip = 112 if rows % 112 == 0 else 64
    strips = rows // strip
    shift_f, scale_f = mod_ref[3:4], mod_ref[4:5]
    open_a, open_f = sigmoid(mod_ref[2:3]), sigmoid(mod_ref[5:6])

    def strip_of(index):
        return pl.ds(pl.multiple_of(index * strip, strip), strip)

    def norm_of(values):
        mean_value = jnp.mean(values, axis=1, keepdims=True)
        centred = values - mean_value
        spread = jnp.mean(centred * centred, axis=1, keepdims=True)
        root = lax.rsqrt(spread + 1e-06)
        return centred * root, root

    @pl.when(step == 0)
    def _():
        gate_pre[...] = wide_dot(normed_a_ref[...], gate_weight_ref[...])

        @pl.loop(0, strips)
        def _(index):
            cut = strip_of(index)
            gated[cut] = (attended_ref[cut] * sigmoid(gate_pre[cut])).astype(jnp.bfloat16)
            grad_ff[cut] = (upstream_ref[cut].astype(jnp.float32) * open_f).astype(jnp.bfloat16)

        branch[...] = wide_dot(gated[...], output_ref[...])

        @pl.loop(0, strips)
        def _(index):
            cut = strip_of(index)
            values = tokens_ref[cut].astype(jnp.float32) + open_a * branch[cut]
            middle[cut] = values
            normed[cut] = (norm_of(values)[0] * (1.0 + scale_f) + shift_f).astype(jnp.bfloat16)
            total[cut] = jnp.zeros((strip, width), jnp.float32)
            grad_normed[cut] = jnp.zeros((strip, width), jnp.float32)

        turned[...] = normed[...].T

    block = rows if rows <= 384 else rows // 2
    for start in range(0, rows, block):
        cut = slice(start, start + block)
        before = wide_dot(normed[cut], gate_ref[...])
        lifted = wide_dot(normed[cut], up_ref[...])
        grad_hidden = wide_dot(grad_ff[cut], down_ref[...], NT)
        switch = sigmoid(before)
        silu = before * switch
        part = (silu * lifted).astype(jnp.bfloat16)
        hidden[cut] = part
        grad_up = (grad_hidden * silu).astype(jnp.bfloat16)
        grad_gate = (grad_hidden * lifted * (switch + silu * (1.0 - switch))).astype(jnp.bfloat16)
        both[cut, :size] = grad_gate
        both[cut, size:] = grad_up
        total[cut] += wide_dot(part, down_ref[...])
        grad_normed[cut] += wide_dot(grad_gate, gate_ref[...], NT) + wide_dot(
            grad_up, up_ref[...], NT
        )

    pair = wide_dot(turned[...], both[...]).astype(jnp.bfloat16)
    if split:
        gate_send, gate_keep, up_send, up_keep, down_send, down_keep, small_send, small_keep = grads
        half = width // 2
        away = pl.ds(pl.multiple_of((1 - here) * half, LANES), half)
        home = pl.ds(pl.multiple_of(here * half, LANES), half)
        down_send[...] = wide_dot(hidden[...], grad_ff[:, away], TN).astype(jnp.bfloat16)
        down_keep[...] = wide_dot(hidden[...], grad_ff[:, home], TN).astype(jnp.bfloat16)

        @pl.when(step < chunks // 2)
        def _():
            gate_send[...] = pair[:, :size]
            up_send[...] = pair[:, size:]

        @pl.when(step >= chunks // 2)
        def _():
            gate_keep[...] = pair[:, :size]
            up_keep[...] = pair[:, size:]
    else:
        gate_all, up_all, down_all, small_all = grads
        gate_all[...] = pair[:, :size]
        up_all[...] = pair[:, size:]
        down_all[...] = wide_dot(hidden[...], grad_ff[...], TN).astype(jnp.bfloat16)

    @pl.when(step == chunks - 1)
    def _():
        def finish(index, sums):
            gate_f_sum, shift_sum, scale_sum, gate_a_sum = sums
            cut = strip_of(index)
            values = middle[cut]
            fed = total[cut]
            upstream = upstream_ref[cut].astype(jnp.float32)
            layer_ref[cut] = (values + open_f * fed).astype(jnp.bfloat16)
            normal, root = norm_of(values)
            grad = grad_normed[cut]
            scaled = grad * (1.0 + scale_f)
            grad_middle = upstream + root * (
                scaled
                - jnp.mean(scaled, axis=1, keepdims=True)
                - normal * jnp.mean(scaled * normal, axis=1, keepdims=True)
            )
            grad_middle_ref[cut] = grad_middle
            grad_branch[cut] = (grad_middle * open_a).astype(jnp.bfloat16)
            return (
                gate_f_sum + fold_rows(upstream * fed),
                shift_sum + fold_rows(grad),
                scale_sum + fold_rows(grad * normal),
                gate_a_sum + fold_rows(grad_middle * branch[cut]),
            )

        zero = jnp.zeros((8, width), jnp.float32)
        sums = lax.fori_loop(0, strips, finish, (zero, zero, zero, zero))
        gate_f_sum, shift_sum, scale_sum, gate_a_sum = [
            jnp.sum(value, axis=0, keepdims=True) for value in sums
        ]
        none = jnp.zeros((1, width), jnp.float32)
        sums_ref[...] = jnp.concatenate(
            [
                none,
                none,
                gate_a_sum * open_a * (1.0 - open_a),
                shift_sum,
                scale_sum,
                gate_f_sum * open_f * (1.0 - open_f),
                none,
                none,
            ],
            axis=0,
        )
        total[...] = wide_dot(grad_branch[...], output_ref[...], NT)

        @pl.loop(0, strips)
        def _(index):
            cut = strip_of(index)
            grad_gated = total[cut]
            opened = sigmoid(gate_pre[cut])
            grad_att_ref[cut] = (grad_gated * opened).astype(jnp.bfloat16)
            grad_pre_ref[cut] = (
                grad_gated * attended_ref[cut] * (opened * (1.0 - opened))
            ).astype(jnp.bfloat16)

        if split:
            for side, ref in ((away, small_send), (home, small_keep)):
                ref[:, :half] = wide_dot(gated[...], grad_branch[:, side], TN).astype(jnp.bfloat16)
                ref[:, half:] = wide_dot(normed_a_ref[...], grad_pre_ref[:, side], TN).astype(
                    jnp.bfloat16
                )
        else:
            small_all[:, :width] = wide_dot(gated[...], grad_branch[...], TN).astype(jnp.bfloat16)
            small_all[:, width:] = wide_dot(normed_a_ref[...], grad_pre_ref[...], TN).astype(
                jnp.bfloat16
            )


def feed_layer(
    split, here, attended, tokens, upstream, normed_a, mod_rows, gate_weight, output_weight, feed_gate, feed_up, feed_down
):
    rows, width = tokens.shape
    inner = feed_gate.shape[1]
    size = 512
    chunks = inner // size
    half = chunks // 2

    def turn(step, here_ref):
        return (step + half * (1 - here_ref[0])) % chunks if split else step

    def fixed(shape):
        return pl.BlockSpec(shape, lambda step, here_ref: (0, 0), pipeline_mode=pl.Buffered(1))

    def columns(step, here_ref):
        return (0, turn(step, here_ref))

    def strips(step, here_ref):
        return (turn(step, here_ref), 0)

    whole = (rows, width)
    in_specs = [fixed(whole)] * 4 + [
        fixed((8, width)),
        fixed((width, width)),
        fixed((width, width)),
        pl.BlockSpec((width, size), columns),
        pl.BlockSpec((width, size), columns),
        pl.BlockSpec((size, width), strips),
    ]
    out_specs = [fixed(whole)] * 4 + [fixed((8, width))]
    bf16, f32 = jnp.bfloat16, jnp.float32
    out_shapes = [(whole, bf16), (whole, f32), (whole, bf16), (whole, bf16), ((8, width), f32)]
    if split:
        first = pl.BlockSpec((width, size), lambda step, here_ref: (0, jnp.minimum(step, half - 1)))
        second = pl.BlockSpec((width, size), lambda step, here_ref: (0, jnp.maximum(step - half, 0)))
        out_specs += [first, second, first, second]
        out_shapes += [((width, inner // 2), bf16)] * 4
        out_specs += [pl.BlockSpec((size, width // 2), strips)] * 2
        out_shapes += [((inner, width // 2), bf16)] * 2
        out_specs += [fixed((width, width))] * 2
        out_shapes += [((width, width), bf16)] * 2
    else:
        out_specs += [pl.BlockSpec((width, size), columns)] * 2
        out_shapes += [((width, inner), bf16)] * 2
        out_specs += [pl.BlockSpec((size, width), strips), fixed((width, 2 * width))]
        out_shapes += [((inner, width), bf16), ((width, 2 * width), bf16)]
    return pl.pallas_call(
        functools.partial(feed_kernel, split, chunks),
        grid_spec=pltpu.PrefetchScalarGridSpec(
            num_scalar_prefetch=1,
            grid=(chunks,),
            in_specs=in_specs,
            out_specs=tuple(out_specs),
            scratch_shapes=[
                pltpu.VMEM(whole, bf16),
                pltpu.VMEM(whole, bf16),
                pltpu.VMEM(whole, bf16),
                pltpu.VMEM(whole, f32),
                pltpu.VMEM(whole, f32),
                pltpu.VMEM(whole, f32),
                pltpu.VMEM(whole, f32),
                pltpu.VMEM((rows, size), bf16),
                pltpu.VMEM((rows, 2 * size), bf16),
                pltpu.VMEM(whole, bf16),
                pltpu.VMEM(whole, f32),
                pltpu.VMEM((width, rows), bf16),
            ],
        ),
        out_shape=tuple(jax.ShapeDtypeStruct(shape, kind) for shape, kind in out_shapes),
        compiler_params=pltpu.CompilerParams(vmem_limit_bytes=VMEM_BYTES),
        cost_estimate=pl.CostEstimate(
            flops=2 * rows * width * (9 * inner + 5 * width),
            bytes_accessed=12 * width * inner + 24 * rows * width,
            transcendentals=2 * rows * inner,
        ),
        name="feed_layer",
    )(
        jnp.reshape(here, (1,)).astype(jnp.int32),
        attended,
        tokens,
        upstream,
        normed_a,
        mod_rows,
        gate_weight,
        output_weight,
        feed_gate,
        feed_up,
        feed_down,
    )


MASKS = {"u": 8, "v": 4, "y": 2, "x": 1}


def exchange(values, mask):
    return lax.ppermute(values, "crop", [(i, i ^ mask) for i in range(16)])


def swap_res(values):
    return lax.ppermute(values, "res", [(0, 1), (1, 0)])


def tie(*values):
    return lax.optimization_barrier(values)


def add_low(former, latter, kind=jnp.bfloat16):
    return (former.astype(jnp.float32) + latter.astype(jnp.float32)).astype(kind)


def stage_kernel(plans, bits_ref, *refs):
    inputs = refs[: sum(plan["count"] for plan in plans)]
    outputs = list(refs[len(inputs) :])
    for plan in plans:
        mine, inputs = inputs[: plan["count"]], inputs[plan["count"] :]
        out_ref = None if plan["apart"] else outputs.pop(0)
        for column, width, own in plan["parts"]:
            total = None
            for index in own:
                value = mine[index][...].astype(jnp.float32)
                total = value if total is None else total + value
            for index in plan["spans"]:
                total = total + mine[index][..., column : column + width].astype(jnp.float32)
            if plan["apart"]:
                outputs.pop(0)[...] = total
            else:
                out_ref[..., column : column + width] = total.astype(jnp.bfloat16)


class Halving:
    def __init__(self, streams, orders):
        self.streams = streams
        self.orders = [list(order) for order in orders]
        self.past = [[] for _ in orders]
        self.came = [[] for _ in orders]

    def stage(self, last=False):
        index = lax.axis_index("crop")
        bits = scalars(*[(index // mask) % 2 for mask in MASKS.values()])
        self.masks, plans, specs, operands, out_specs, out_shapes = [], [], [], [], [], []
        left = 0 if last else len(self.orders[0]) - 1
        steps = {3: 4, 2: 2}.get(left, 1)
        for stream, (parts, order, past) in enumerate(zip(self.streams, self.orders, self.past)):
            now = None if last else order.pop(0)
            rest = [axis for axis in MASKS if axis in order]

            def spec_of(axes, rows, width, block, now=now, rest=rest):
                def index_map(step, bits_ref):
                    places = []
                    for axis in axes:
                        bit = bits_ref[list(MASKS).index(axis)]
                        if axis == now:
                            places.append(1 - bit)
                        elif axis not in rest:
                            places.append(bit)
                        elif axis == rest[0] and steps > 1:
                            places.append(step // (steps // 2))
                        elif len(rest) > 1 and axis == rest[1] and steps > 2:
                            places.append(step % 2)
                        else:
                            places.append(0)
                    return (*places, 0, block)

                sizes = [
                    2
                    if axis in rest
                    and not (axis == rest[0] and steps > 1)
                    and not (len(rest) > 1 and axis == rest[1] and steps > 2)
                    else None
                    for axis in axes
                ]
                return pl.BlockSpec((*sizes, rows, width), index_map)

            plan = {"parts": [], "spans": [], "count": 0, "apart": last}
            column = 0
            rows = parts[0][0][0].shape[0] // 16
            for arrays, block, width in parts:
                own = []
                for value in arrays:
                    operands.append(value.reshape(2, 2, 2, 2, rows, value.shape[1]))
                    specs.append(spec_of(list(MASKS), rows, width, block))
                    own.append(plan["count"])
                    plan["count"] += 1
                plan["parts"].append((column, width, own))
                column += width
            for axes, value in self.came[stream]:
                operands.append(value.reshape(*[2] * len(axes), rows, column))
                specs.append(spec_of(axes, rows, column, 0))
                plan["spans"].append(plan["count"])
                plan["count"] += 1
            plans.append(plan)
            if last:
                for _, width, _ in plan["parts"]:
                    out_specs.append(pl.BlockSpec((rows, width), lambda step, bits_ref: (0, 0)))
                    out_shapes.append(jax.ShapeDtypeStruct((rows, width), jnp.float32))
            else:
                past.append(now)
                self.masks.append(MASKS[now])
                out_specs.append(spec_of(rest, rows, column, 0))
                out_shapes.append(
                    jax.ShapeDtypeStruct((*[2] * len(rest), rows, column), jnp.bfloat16)
                )
        self.axes = [[axis for axis in MASKS if axis in order] for order in self.orders]
        results = pl.pallas_call(
            functools.partial(stage_kernel, plans),
            grid_spec=pltpu.PrefetchScalarGridSpec(
                num_scalar_prefetch=1, grid=(steps,), in_specs=specs, out_specs=tuple(out_specs)
            ),
            out_shape=tuple(out_shapes),
            compiler_params=pltpu.CompilerParams(vmem_limit_bytes=VMEM_BYTES),
            cost_estimate=pl.CostEstimate(
                flops=sum(4 * math.prod(shape.shape) for shape in out_shapes),
                bytes_accessed=sum(8 * math.prod(shape.shape) for shape in out_shapes),
                transcendentals=0,
            ),
            name="halving_stage",
        )(bits, *operands)
        return list(results) if last else [value.reshape(-1, value.shape[-1]) for value in results]

    def send(self, values):
        return [exchange(value, mask) for value, mask in zip(values, self.masks)]

    def take(self, values):
        for came, axes, value in zip(self.came, self.axes, values):
            came.append((axes, value))


def share_columns(values, parts):
    if parts == 1:
        return values.astype(jnp.bfloat16)
    return lax.psum_scatter(values.astype(jnp.bfloat16), "res", scatter_dimension=1, tiled=True)


def scatter_crops(values):
    return lax.psum_scatter(values, "crop", scatter_dimension=0, tiled=True).astype(jnp.float32)


def gather_crops(values, crop_parts):
    if crop_parts != 16:
        return lax.all_gather(values, "crop", axis=0, tiled=True)
    index = lax.axis_index("crop")
    for mask in (1, 2, 4, 8):
        other = exchange(values, mask)
        low = (index // mask) % 2 == 0
        values = jnp.concatenate(
            [jnp.where(low, values, other), jnp.where(low, other, values)], axis=0
        )
    return values


def sum_res(values, parts):
    if parts == 1:
        return values
    if parts != 2:
        return lax.psum(values, "res")
    return values + swap_res(values)


PACK = 1152
SIDE = 384


def whole_vmem(count):
    return [pl.BlockSpec(memory_space=pltpu.VMEM)] * count


def scalars(*values):
    return jnp.stack([jnp.asarray(value, jnp.int32) for value in values])


def local_call(kernel, numbers, operands, shapes, name, flops=0):
    return pl.pallas_call(
        kernel,
        in_specs=[pl.BlockSpec(memory_space=pltpu.SMEM)] + whole_vmem(len(operands)),
        out_specs=tuple(whole_vmem(len(shapes))),
        out_shape=tuple(jax.ShapeDtypeStruct(shape, kind) for shape, kind in shapes),
        compiler_params=pltpu.CompilerParams(vmem_limit_bytes=VMEM_BYTES),
        cost_estimate=pl.CostEstimate(
            flops=flops,
            bytes_accessed=sum(value.size * value.dtype.itemsize for value in operands)
            + sum(4 * math.prod(shape) for shape, _ in shapes),
            transcendentals=0,
        ),
        name=name,
    )(numbers, *operands)


def projection_kernel(counts, here_ref, normed_ref, *refs):
    calls = len(counts)
    parts, (joined_ref, send_ref, keep_ref) = refs[: 3 * calls], refs[3 * calls :]
    width = joined_ref.shape[1] // 3
    column = 0
    for call, pairs in enumerate(counts):
        size = pairs * LANES
        query_ref, own_ref, came_ref = parts[3 * call : 3 * call + 3]
        joined_ref[:, column : column + size] = query_ref[...]
        for which in range(2):
            first = (1 + which) * width + column
            joined_ref[:, first : first + size] = add_low(own_ref[which], came_ref[which])
        column += size
    half = send_ref.shape[1]
    for side, ref in ((1 - here_ref[0], send_ref), (here_ref[0], keep_ref)):
        columns = pl.ds(pl.multiple_of(side * half, LANES), half)
        ref[...] = wide_dot(normed_ref[...], joined_ref[:, columns], TN).astype(jnp.bfloat16)


def projection_gradient(here, normed_a, calls):
    rows, width = normed_a.shape
    counts = [call[0].shape[-1] // LANES for call in calls]
    return local_call(
        functools.partial(projection_kernel, counts),
        scalars(here),
        [normed_a] + [value for call in calls for value in call],
        [
            ((rows, 3 * width), jnp.bfloat16),
            ((width, 3 * width // 2), jnp.bfloat16),
            ((width, 3 * width // 2), jnp.bfloat16),
        ],
        "projection_gradient",
        6 * rows * width * width,
    )


def finish_kernel(counts, joined_ref, weight_ref, pre_ref, gate_ref, tokens_ref, middle_ref, mod_ref, *refs):
    feed_sums_ref, extra_ref = refs[:2]
    table_refs = refs[2 : 2 + len(counts)]
    out_ref, pack_ref, total = refs[2 + len(counts) :]
    step = pl.program_id(0)
    rows, width = tokens_ref.shape
    part = wide_dot(joined_ref[...], weight_ref[...], NT)

    @pl.when(step == 0)
    def _():
        total[...] = part + wide_dot(pre_ref[...], gate_ref[...], NT)

    @pl.when(step > 0)
    def _():
        total[...] += part

    @pl.when(step == pl.num_programs(0) - 1)
    def _():
        strip = 112 if rows % 112 == 0 else 64
        scale = mod_ref[1:2]

        def finish(index, sums):
            shift_sum, scale_sum = sums
            cut = pl.ds(pl.multiple_of(index * strip, strip), strip)
            values = tokens_ref[cut].astype(jnp.float32)
            centred = values - jnp.mean(values, axis=1, keepdims=True)
            root = lax.rsqrt(jnp.mean(centred * centred, axis=1, keepdims=True) + 1e-06)
            normal = centred * root
            grad = total[cut]
            scaled = grad * (1.0 + scale)
            out_ref[cut] = (
                middle_ref[cut]
                + root
                * (
                    scaled
                    - jnp.mean(scaled, axis=1, keepdims=True)
                    - normal * jnp.mean(scaled * normal, axis=1, keepdims=True)
                )
            ).astype(jnp.bfloat16)
            return shift_sum + fold_rows(grad), scale_sum + fold_rows(grad * normal)

        zero = jnp.zeros((8, width), jnp.float32)
        shift_sum, scale_sum = lax.fori_loop(0, rows // strip, finish, (zero, zero))
        heads = []
        for ref, pairs in zip(table_refs, counts):
            for pair in range(pairs):
                heads += [ref[pair, 0:1], ref[pair, 1:2]]

        def upper_of(values):
            return values.astype(jnp.bfloat16).astype(jnp.float32)

        rests = [head - upper_of(head) for head in heads]
        count = width // LANES
        left = [
            jnp.sum(shift_sum, axis=0, keepdims=True),
            jnp.sum(scale_sum, axis=0, keepdims=True),
            feed_sums_ref[2:6],
        ]
        left += [
            jnp.concatenate(rests[i : i + count], axis=1) for i in range(0, len(heads), count)
        ]
        right = [jnp.concatenate(heads[3 * i : 3 * i + 3], axis=1) for i in range(4)]
        line = extra_ref[5:6]
        right += [extra_ref[4:5], line, line - upper_of(line), extra_ref[7:8]]
        pack = jnp.concatenate(
            [jnp.concatenate(left, axis=0), jnp.concatenate(right, axis=0)], axis=1
        )
        pack_ref[...] = jnp.concatenate([pack, jnp.zeros_like(pack)], axis=0).astype(jnp.bfloat16)


def finish_layer(
    joined, weight, grad_pre, gate_weight, tokens, grad_middle, mod_rows, feed_sums, extra, grad_tables
):
    rows, width = tokens.shape
    counts = [table.shape[0] for table in grad_tables]

    def fixed(shape):
        return pl.BlockSpec(shape, lambda step: (0,) * len(shape), pipeline_mode=pl.Buffered(1))

    return pl.pallas_call(
        functools.partial(finish_kernel, counts),
        grid=(3,),
        in_specs=[
            pl.BlockSpec((rows, width), lambda step: (0, step)),
            pl.BlockSpec((width, width), lambda step: (0, step)),
            fixed((rows, width)),
            fixed((width, width)),
            fixed((rows, width)),
            fixed((rows, width)),
            fixed((8, width)),
            fixed((8, width)),
            fixed((8, SIDE)),
        ]
        + [fixed((count, 8, LANES)) for count in counts],
        out_specs=(fixed((rows, width)), fixed((16, PACK))),
        out_shape=(
            jax.ShapeDtypeStruct((rows, width), jnp.bfloat16),
            jax.ShapeDtypeStruct((16, PACK), jnp.bfloat16),
        ),
        scratch_shapes=[pltpu.VMEM((rows, width), jnp.float32)],
        compiler_params=pltpu.CompilerParams(vmem_limit_bytes=VMEM_BYTES),
        cost_estimate=pl.CostEstimate(
            flops=8 * rows * width * width, bytes_accessed=24 * rows * width, transcendentals=0
        ),
        name="finish_layer",
    )(
        joined,
        weight,
        grad_pre,
        gate_weight,
        tokens,
        grad_middle,
        mod_rows,
        feed_sums,
        extra,
        *grad_tables,
    )


def fan_first_kernel(bits_ref, keep_ref, came_ref, mine_ref, *send_refs):
    chunk = keep_ref.shape[0] // 16
    for other, ref in enumerate((mine_ref, *send_refs)):
        for level in range(4):
            start = (level * 4 + (bits_ref[0] ^ other)) * chunk
            cut = pl.ds(pl.multiple_of(start, 16), chunk)
            ref[level * chunk : (level + 1) * chunk] = add_low(keep_ref[cut], came_ref[cut])


def fan_v_kernel(bits_ref, mine_ref, *refs):
    came_refs, pack_refs = refs[:3], refs[3:7]
    send_ref, out_ref, packs_ref = refs[7:]
    chunk = mine_ref.shape[0] // 4
    packs = [ref[...].astype(jnp.float32)[0:8] for ref in pack_refs]
    packs = jnp.concatenate(packs, axis=0).astype(jnp.bfloat16)
    packs_ref[...] = packs
    send_ref[2 * chunk :] = packs
    for side, ref in ((1 - bits_ref[0], send_ref), (bits_ref[0], out_ref)):
        for far in range(2):
            cut = pl.ds(pl.multiple_of((2 * far + side) * chunk, 16), chunk)
            total = mine_ref[cut].astype(jnp.float32)
            for came_ref in came_refs:
                total = total + came_ref[cut].astype(jnp.float32)
            ref[far * chunk : (far + 1) * chunk] = total.astype(jnp.bfloat16)


def fan_u_kernel(bits_ref, mine_ref, came_ref, packs_ref, send_ref, out_ref, all_ref):
    chunk = mine_ref.shape[0] // 2
    packs = jnp.concatenate([packs_ref[...], came_ref[2 * chunk :]], axis=0)
    all_ref[...] = packs
    send_ref[chunk:] = packs
    for side, ref in ((1 - bits_ref[0], send_ref), (bits_ref[0], out_ref)):
        cut = pl.ds(pl.multiple_of(side * chunk, 16), chunk)
        ref[0:chunk] = add_low(mine_ref[cut], came_ref[cut])


def fan_last_kernel(bits_ref, mine_ref, came_ref, packs_ref, out_ref, all_ref):
    chunk = mine_ref.shape[0]
    out_ref[...] = add_low(mine_ref[...], came_ref[0:chunk], jnp.float32)
    all_ref[...] = jnp.concatenate([packs_ref[...], came_ref[chunk:]], axis=0)


def small_kernel(
    heads,
    here_ref,
    mine_ref,
    came_ref,
    modulation_ref,
    pair_norm_ref,
    relative_ref,
    gain_ref,
    pair_weight_ref,
    mod_grad_ref,
    time_ref,
    label_ref,
    relative_grad_ref,
    gain_grad_ref,
    pair_grad_ref,
    grad_condition,
    grad_mod,
    kept,
):
    step = pl.program_id(0)
    crops = mine_ref.shape[0] // 8
    width = mine_ref.shape[1] - SIDE
    conds = relative_ref.shape[1]
    parts = mod_grad_ref.shape[1] // width

    def parts_split(values):
        upper = values.astype(jnp.bfloat16)
        return upper, (values - upper.astype(jnp.float32)).astype(jnp.bfloat16)

    def dot_left(narrow, values, numbers):
        upper, rest = parts_split(values)
        return wide_dot(narrow, upper, numbers) + wide_dot(narrow, rest, numbers)

    def dot_right(values, narrow, numbers):
        upper, rest = parts_split(values)
        return wide_dot(upper, narrow, numbers) + wide_dot(rest, narrow, numbers)

    def both_twice(narrow):
        return jnp.concatenate([narrow, narrow], axis=0)

    def stacked(values):
        return jnp.concatenate(parts_split(values), axis=0)

    @pl.when(step == 0)
    def _():
        shape = (8 * crops, 8 * crops)
        picked = lax.broadcasted_iota(jnp.int32, shape, 0)
        source = lax.broadcasted_iota(jnp.int32, shape, 1)
        hit = ((source >> 3) == (picked & (crops - 1))) & ((source & 7) == (picked // crops))
        select = jnp.where(hit, 1.0, 0.0).astype(jnp.bfloat16)
        mine = wide_dot(select, mine_ref[...])
        grad_mod[...] = mine[: 6 * crops, :width] + wide_dot(select, came_ref[...])[: 6 * crops, :width]
        condition = (
            mine[5 * crops : 6 * crops, width : width + conds]
            + mine[6 * crops : 7 * crops, width : width + conds]
        )
        gate_value = sigmoid(condition)
        kept[0] = condition * gate_value
        kept[1] = gate_value * (1.0 + condition * (1.0 - gate_value))
        kept[2] = mine[4 * crops : 5 * crops, width : width + conds]
        kept[3] = jnp.broadcast_to(
            mine[5 * crops : 6 * crops, width + conds : width + conds + 1]
            + mine[6 * crops : 7 * crops, width + conds : width + conds + 1],
            (crops, conds),
        )
        grad_condition[...] = jnp.zeros_like(grad_condition)

    cond_act = both_twice(kept[0].astype(jnp.bfloat16))
    for turn in range(parts):
        columns = slice(turn * width, (turn + 1) * width)
        first = pl.multiple_of((step * parts + turn) * crops, crops)
        pair = stacked(grad_mod[pl.ds(first, crops)])
        mod_grad_ref[:, columns] = wide_dot(cond_act, pair, TN)
        more = wide_dot(pair, modulation_ref[:, columns], NT)
        grad_condition[...] += more[:crops] + more[crops:]

    @pl.when(step == 0)
    def _():
        shape = (8, 8 * crops)
        line = lax.broadcasted_iota(jnp.int32, shape, 0)
        local = lax.broadcasted_iota(jnp.int32, shape, 1) & 7
        every = jnp.where(local == line, 1.0, 0.0).astype(jnp.bfloat16)
        lines = wide_dot(every, mine_ref[...]) + wide_dot(every, came_ref[...])

        def of_head(head):
            upper = width + (head % 3) * LANES
            rest = (head % (width // LANES)) * LANES
            low = 6 + head // (width // LANES)
            return (
                lines[head // 3 : head // 3 + 1, upper : upper + LANES]
                + lines[low : low + 1, rest : rest + LANES]
            )

        table = jnp.concatenate(
            [of_head(head) for head in range(heads)]
            + [jnp.zeros((16 - heads, LANES), jnp.float32)],
            axis=0,
        )
        bins = relative_ref.shape[0]
        pair_grad_ref[...] = dot_right(table, pair_norm_ref[...], (((1,), (0,)), ((), ())))[:heads]
        grad_norm = dot_right(table, pair_weight_ref[...], (((0,), (1,)), ((), ())))[:bins]
        values = relative_ref[...]
        centred = values - jnp.mean(values, axis=1, keepdims=True)
        root = lax.rsqrt(jnp.mean(centred * centred, axis=1, keepdims=True) + 1e-06)
        normal = centred * root
        gain_grad_ref[...] = jnp.sum(grad_norm * normal, axis=0, keepdims=True)
        scaled = grad_norm * gain_ref[...]
        relative_grad_ref[...] = root * (
            scaled
            - jnp.mean(scaled, axis=1, keepdims=True)
            - normal * jnp.mean(scaled * normal, axis=1, keepdims=True)
        )

    @pl.when(step == pl.num_programs(0) - 1)
    def _():
        final = stacked(grad_condition[...] * kept[1])
        time_ref[...] = wide_dot(both_twice(kept[2].astype(jnp.bfloat16)), final, TN)
        label = lax.broadcasted_iota(jnp.int32, (crops, label_ref.shape[0]), 1)
        number = kept[3][:, 0:1].astype(jnp.int32)
        onehot = jnp.where(label == number, 1.0, 0.0).astype(jnp.bfloat16)
        label_ref[...] = wide_dot(both_twice(onehot), final, TN)


def small_gradients(heads, labels, mine, came, modulation_weight, pair_norm, relative, gain, pair_weight):
    conds, wide = modulation_weight.shape
    bins = relative.shape[0]
    rows = mine.shape[0]
    steps = 3

    def fixed(shape):
        return pl.BlockSpec(shape, lambda step: (0, 0))

    shapes = [(conds, wide), (conds, conds), (labels, conds), (bins, conds), (1, conds), (heads, conds)]
    return pl.pallas_call(
        functools.partial(small_kernel, heads),
        grid=(steps,),
        in_specs=[
            pl.BlockSpec(memory_space=pltpu.SMEM),
            fixed((rows, PACK)),
            fixed((rows, PACK)),
            pl.BlockSpec((conds, wide // steps), lambda step: (0, step)),
            fixed((LANES, conds)),
            fixed((bins, conds)),
            fixed((1, conds)),
            fixed((conds, 16)),
        ],
        out_specs=tuple(
            [pl.BlockSpec((conds, wide // steps), lambda step: (0, step))]
            + [fixed(s) for s in shapes[1:]]
        ),
        out_shape=tuple(jax.ShapeDtypeStruct(shape, jnp.float32) for shape in shapes),
        scratch_shapes=[
            pltpu.VMEM((rows // 8, conds), jnp.float32),
            pltpu.VMEM((6 * rows // 8, wide // 6), jnp.float32),
            pltpu.VMEM((4, rows // 8, conds), jnp.float32),
        ],
        compiler_params=pltpu.CompilerParams(vmem_limit_bytes=VMEM_BYTES),
        cost_estimate=pl.CostEstimate(
            flops=100000000, bytes_accessed=10000000, transcendentals=0
        ),
        name="small_gradients",
    )(
        scalars(0),
        mine,
        came,
        modulation_weight,
        pair_norm,
        relative,
        gain,
        pair_weight,
    )


def per_device(
    crop_parts,
    res_parts,
    tokens,
    cotangent,
    time_levels,
    cath_ids,
    residue_numbers,
    chain_mask,
    time_weight,
    label_table,
    modulation_weight,
    projection_weight,
    gate_weight,
    output_weight,
    relative_table,
    pair_gain,
    pair_weight,
    feed_gate,
    feed_up,
    feed_down,
):
    crop_count, row_count, model_width = tokens.shape
    crop_length = residue_numbers.shape[1]
    head_count = pair_weight.shape[1]
    head_width = model_width // head_count
    bin_count = relative_table.shape[0]
    label_count = label_table.shape[0]
    token_count = crop_count * row_count
    score_scale = head_width ** (-0.5)
    pairs = head_count // 2
    layout = Layout(row_count, crop_length)
    query_start = lax.axis_index("res") * row_count

    def conditioning(features, onehot):
        return jnp.dot(features, time_weight, preferred_element_type=jnp.float32) + jnp.dot(
            onehot, label_table, preferred_element_type=jnp.float32
        )

    features = time_features(time_levels, time_weight.shape[0]).astype(jnp.bfloat16)
    label_onehot = (cath_ids[:, None] == jnp.arange(label_count, dtype=jnp.int32)[None, :]).astype(
        jnp.bfloat16
    )
    condition = conditioning(features, label_onehot)
    cond_act = jax.nn.silu(condition).astype(jnp.bfloat16)
    modulation = jnp.dot(cond_act, modulation_weight, preferred_element_type=jnp.float32)
    modulation = modulation.reshape(crop_count, 6, 1, model_width)
    shift_a, scale_a = modulation[:, 0], modulation[:, 1]
    mod_rows = pad_to(modulation[:, :, 0], 1, 8, 0.0)

    rotated = lax.dynamic_slice_in_dim(
        jnp.concatenate([jnp.stack([residue_numbers, chain_mask])] * 2, 2), query_start, crop_length, 2
    )
    members, kinds, forward_bins, backward_bins, places = attention_tables(
        layout, rotated[0], rotated[1], query_start, bin_count
    )
    relative_values = relative_table.astype(jnp.float32)
    gain_values = pair_gain.astype(jnp.float32)
    pair_norm = normalize_rows(relative_values, gain_values).astype(jnp.bfloat16)
    bias_rows = jnp.dot(pair_norm, pair_weight, preferred_element_type=jnp.float32)
    tables = head_tables(layout, bias_rows, score_scale)

    token_values = tokens.astype(jnp.float32)
    normed_a = (
        modulate(token_values, shift_a, scale_a)
        .astype(jnp.bfloat16)
        .reshape(token_count, model_width)
    )
    def project(weight):
        rows = jnp.dot(normed_a, weight, preferred_element_type=jnp.float32)
        return rows.astype(jnp.bfloat16).reshape(crop_count, row_count, -1)

    key_values = project(projection_weight[:, model_width:])
    queries = project(projection_weight[:, :model_width])
    others = [
        lax.ppermute(
            key_values, "res", [((r + step) % res_parts, r) for r in range(res_parts)]
        )
        for step in range(1, res_parts)
    ]
    if len(layout.pieces) == 2:
        other = others[0] if len(others) == 1 else jnp.concatenate(others, axis=1)
        pieces = [(key_values, 0, pairs), (other, 0, pairs)]
    else:
        pieces = [(jnp.concatenate([key_values] + others, axis=1), 0, pairs)]

    def block_rows(values):
        return pad_to(values, 1, layout.block_rows, 0)

    attended, logs = attention_forward(
        layout,
        score_scale,
        block_rows(queries),
        pieces,
        members,
        kinds,
        forward_bins,
        tables,
    )
    here = lax.axis_index("res")
    split = res_parts == 2 and crop_parts == 16
    per_crop_results = [
        feed_layer(
            split,
            here,
            attended[crop],
            block_rows(tokens)[crop],
            block_rows(cotangent)[crop],
            block_rows(normed_a.reshape(tokens.shape))[crop],
            mod_rows[crop],
            gate_weight,
            output_weight,
            feed_gate,
            feed_up,
            feed_down,
        )
        for crop in range(crop_count)
    ]
    layer_out, grad_middle, grad_attended, grad_gate_pre, feed_sums = (
        jnp.stack([result[place] for result in per_crop_results]) for place in range(5)
    )
    layer_out, grad_middle = layer_out[:, :row_count], grad_middle[:, :row_count]
    grad_gate_pre = grad_gate_pre[:, :row_count].reshape(token_count, model_width)
    weight_grads = [
        sum(result[place].astype(jnp.float32) for result in per_crop_results).astype(jnp.bfloat16)
        if crop_count > 1
        else per_crop_results[0][place]
        for place in range(5, len(per_crop_results[0]))
    ]

    def backward_of(first_pair, count, grad_now):
        return attention_backward(
            layout,
            score_scale,
            first_pair,
            count,
            block_rows(queries),
            grad_now,
            attended,
            logs,
            pieces,
            members,
            kinds,
            backward_bins,
            places,
            tables,
        )

    if split:
        arrivals = [swap_res(weight_grads[place]) for place in (0, 2, 4, 6)]
        kept = [weight_grads[place] for place in (1, 3, 5, 7)]
        half = model_width // 2
        inner = feed_gate.shape[1] // 2
        small_operands = tie(
            pad_to(pair_norm, 0, LANES, 0.0),
            relative_values,
            gain_values.reshape(1, -1),
            pad_to(pair_weight, 1, 16, 0.0),
            grad_attended,
        )
        *small_operands, grad_attended = small_operands
        calls = [list(backward_of(0, 1, grad_attended))]
        arrivals, calls[0] = tie(arrivals, calls[0])
        gate_w, up_w, down_w, small_w = zip(kept, arrivals)
        halving = Halving(
            [
                [(gate_w, 0, inner), (small_w, 0, half)],
                [(up_w, 0, inner), (small_w, 1, half)],
                [(down_w, 0, half)],
            ],
            ["xyvu", "yvxu", "vxyu"],
        )
        arrived = []
        for first_pair, count in ((1, 3), (4, 2)):
            arrived.append(swap_res(calls[-1][2][0]))
            sent = halving.stage()
            sent, grad_attended = tie(sent, grad_attended)
            came = halving.send(sent)
            calls.append(list(backward_of(first_pair, count, grad_attended)))
            came, calls[-1], arrived[-1] = tie(came, calls[-1], arrived[-1])
            halving.take(came)
        index = lax.axis_index("crop")
        bf16 = jnp.bfloat16
        share = model_width // 16
        away = swap_res(calls[2][2][0])
        sent = halving.stage()
        sent, calls[2][1] = tie(sent, calls[2][1])
        came = halving.send(sent)
        joined, proj_send, proj_keep = projection_gradient(
            here,
            normed_a,
            [
                (calls[0][0][0], calls[0][1][0], arrived[0]),
                (calls[1][0][0], calls[1][1][0], arrived[1]),
                (calls[2][0][0], calls[2][1][0], away),
            ],
        )
        proj_came = swap_res(proj_send)
        came, proj_keep = tie(came, proj_keep)
        halving.take(came)
        sent = halving.stage()
        sent, proj_came = tie(sent, proj_came)
        came = halving.send(sent)
        mine, *fan = local_call(
            fan_first_kernel,
            scalars(index % 4),
            [proj_keep, proj_came],
            [((4 * share, PACK), bf16)] * 4,
            "fan_first",
        )
        fan, joined = tie(fan, joined)
        fan_came = [exchange(value, mask + 1) for mask, value in enumerate(fan)]
        extra = jnp.concatenate(
            [
                pad_to(features.astype(jnp.float32), 1, SIDE, 0.0),
                jnp.concatenate(
                    [condition, pad_to(cath_ids.astype(jnp.float32)[:, None], 1, LANES, 0.0)], axis=1
                ),
            ],
            axis=0,
        )
        tokens_grad, pack = finish_layer(
            joined,
            projection_weight,
            grad_gate_pre,
            gate_weight,
            tokens[0],
            grad_middle[0],
            mod_rows[0],
            feed_sums[0],
            jnp.pad(extra, ((4, 2), (0, 0))),
            [call[-1][0] for call in calls],
        )
        tokens_grad = tokens_grad[None]
        came, pack = tie(came, pack)
        packs = [pack] + [exchange(pack, mask + 1) for mask in range(3)]
        halving.take(came)
        finals = halving.stage(last=True)
        fan_came, packs, finals = tie(fan_came, packs, finals)
        feed_gate_grad, output_weight_grad, feed_up_grad, gate_weight_grad, feed_down_grad = finals
        sent, mine, packs = local_call(
            fan_v_kernel,
            scalars((index // 4) % 2),
            [mine, *fan_came, *packs],
            [((2 * share + 32, PACK), bf16), ((2 * share, PACK), bf16), ((32, PACK), bf16)],
            "fan_v",
        )
        sent, mine, packs = local_call(
            fan_u_kernel,
            scalars(index // 8),
            [mine, exchange(sent, MASKS["v"]), packs],
            [((share + 64, PACK), bf16), ((share, PACK), bf16), ((64, PACK), bf16)],
            "fan_u",
        )
        projection_weight_grad, packs = local_call(
            fan_last_kernel,
            scalars(0),
            [mine, exchange(sent, MASKS["u"]), packs],
            [((share, PACK), jnp.float32), ((128, PACK), bf16)],
            "fan_last",
        )
        (
            modulation_weight_grad,
            time_weight_grad,
            label_table_grad,
            relative_table_grad,
            pair_gain_grad,
            pair_weight_grad,
        ) = small_gradients(
            head_count, label_count, packs, swap_res(packs), modulation_weight, *small_operands
        )
        pair_weight_grad = pair_weight_grad.T
        pair_gain_grad = pair_gain_grad[0]
    else:
        results = backward_of(0, pairs, grad_attended)
        grad_table = results[-1]
        grad_pairs = results[1:-1]
        if len(grad_pairs) == 2:
            total, away = grad_pairs[0].astype(jnp.float32), grad_pairs[1]
        else:
            total = grad_pairs[0][:, :, :row_count].astype(jnp.float32)
            away = grad_pairs[0][:, :, row_count:]
        for step in range(1, res_parts):
            sent = away[:, :, (step - 1) * row_count : step * row_count]
            pairs_to = [(r, (r + step) % res_parts) for r in range(res_parts)]
            total = total + lax.ppermute(sent, "res", pairs_to).astype(jnp.float32)
        total = total.astype(jnp.bfloat16)
        grad_projected = jnp.concatenate(
            [results[0][:, :row_count], total[:, 0], total[:, 1]], axis=-1
        ).reshape(token_count, 3 * model_width)
        grad_normed_a = against_columns(grad_projected, projection_weight) + against_columns(
            grad_gate_pre, gate_weight
        )
        norm_back_a = jax.vjp(modulate, token_values, shift_a, scale_a)[1]
        grad_tokens, grad_shift_a, grad_scale_a = norm_back_a(
            grad_normed_a.reshape(crop_count, row_count, model_width)
        )
        tokens_grad = (grad_middle + grad_tokens).astype(jnp.bfloat16)
        feed_gate_grad, feed_up_grad, feed_down_grad = (
            scatter_crops(share_columns(value, res_parts)) for value in weight_grads[:3]
        )
        output_weight_grad, gate_weight_grad = (
            scatter_crops(share_columns(value, res_parts))
            for value in (weight_grads[3][:, :model_width], weight_grads[3][:, model_width:])
        )
        projection_weight_grad = scatter_crops(
            share_columns(across_rows(normed_a, grad_projected), res_parts)
        )
        grad_table = grad_table[:, :, :2].sum(0).reshape(head_count, LANES)

        grad_modulation = jnp.concatenate([grad_shift_a, grad_scale_a, feed_sums[:, 2:6]], axis=1)
        grad_modulation = grad_modulation.reshape(crop_count, 6 * model_width)
        table_row = grad_table.reshape(1, head_count * LANES)
        first_row = (jnp.arange(crop_count) == 0).astype(jnp.float32)[:, None]
        small_here = jnp.concatenate([grad_modulation, first_row * table_row], axis=1)
        levels_here = jnp.stack([time_levels, cath_ids.astype(jnp.float32)], axis=1)
        levels_here = pad_to(levels_here, 1, LANES, 0.0)
        small_all = gather_crops(
            jnp.concatenate([levels_here, sum_res(small_here, res_parts)], axis=1), crop_parts
        )
        levels_all, small_all = small_all[:, :2], small_all[:, LANES:]
        grad_modulation = small_all[:, : 6 * model_width]
        grad_table = jnp.sum(small_all[:, 6 * model_width :], axis=0).reshape(head_count, LANES)
        grad_table = grad_table[:, :bin_count]
        features_all = time_features(levels_all[:, 0], time_weight.shape[0]).astype(jnp.bfloat16)
        onehot_all = (
            levels_all[:, 1].astype(jnp.int32)[:, None]
            == jnp.arange(label_count, dtype=jnp.int32)[None, :]
        ).astype(jnp.bfloat16)
        condition = conditioning(features_all, onehot_all)
        cond_act = jax.nn.silu(condition).astype(jnp.bfloat16)
        modulation_weight_grad = split_left(cond_act, grad_modulation, 0, 0)
        grad_condition = split_left(modulation_weight, grad_modulation, 1, 1).T * silu_slope(condition)
        time_weight_grad = split_left(features_all, grad_condition, 0, 0)
        label_table_grad = split_left(onehot_all, grad_condition, 0, 0)
        pair_weight_grad = split_left(pair_norm, grad_table, 0, 1)
        grad_pair_norm = split_right(grad_table, pair_weight, 0, 1)
        pair_back = jax.vjp(normalize_rows, relative_values, gain_values)[1]
        relative_table_grad, pair_gain_grad = pair_back(grad_pair_norm)
    return (
        layer_out,
        tokens_grad,
        time_weight_grad,
        label_table_grad,
        modulation_weight_grad,
        projection_weight_grad,
        gate_weight_grad,
        output_weight_grad,
        relative_table_grad,
        pair_gain_grad,
        pair_weight_grad,
        feed_gate_grad,
        feed_up_grad,
        feed_down_grad,
    )


def solution(mesh):
    return jax.shard_map(
        functools.partial(per_device, mesh.shape["crop"], mesh.shape["res"]),
        mesh=mesh,
        in_specs=(
            P("crop", "res", None),
            P("crop", "res", None),
            P("crop"),
            P("crop"),
            P("crop", None),
            P("crop", None),
            P(),
            P(),
            P(),
            P(),
            P(),
            P(),
            P(),
            P(),
            P(),
            P(),
            P(),
            P(),
        ),
        out_specs=(
            P("crop", "res", None),
            P("crop", "res", None),
            P(),
            P(),
            P(),
            P("crop", "res"),
            P("crop", "res"),
            P("crop", "res"),
            P(),
            P(),
            P(),
            P("crop", "res"),
            P("crop", "res"),
            P("crop", "res"),
        ),
        check_vma=False,
    )
```

```python
import functools
import math

import jax
import jax.numpy as jnp
from jax import lax
from jax.experimental import pallas as pl
from jax.experimental.pallas import tpu as pltpu
from jax.sharding import PartitionSpec as P

LANES = 128
NEAR = 31
VMEM_BYTES = 56 * 1024 * 1024
LOG2E = 1.4426950408889634
NONE, RIGHT, LEFT, APART = 0, 1, 2, 3


def layer_norm(inputs):
    mean_value = jnp.mean(inputs, axis=-1, keepdims=True)
    centred = inputs - mean_value
    spread = jnp.mean(centred * centred, axis=-1, keepdims=True)
    return centred * lax.rsqrt(spread + 1e-06)


def modulate(inputs, shift_row, scale_row):
    return layer_norm(inputs) * (1.0 + scale_row) + shift_row


def normalize_rows(table_rows, gain_row):
    return layer_norm(table_rows) * gain_row


def time_features(time_levels, feature_width):
    half_width = feature_width // 2
    frequency = jnp.exp(-math.log(10000.0) * jnp.arange(half_width, dtype=jnp.float32) / half_width)
    angles = 1000.0 * time_levels[:, None] * frequency[None, :]
    return jnp.concatenate([jnp.sin(angles), jnp.cos(angles)], axis=-1)


def across_rows(former, latter):
    return lax.dot_general(
        former, latter, (((0,), (0,)), ((), ())), preferred_element_type=jnp.float32
    )


def against_columns(former, latter):
    return lax.dot_general(
        former, latter, (((1,), (1,)), ((), ())), preferred_element_type=jnp.float32
    )


def split_parts(values):
    upper = lax.reduce_precision(values, 8, 7)
    return (upper.astype(jnp.bfloat16), (values - upper).astype(jnp.bfloat16))


def split_left(narrow, values, former_dim, latter_dim):
    upper, rest = split_parts(values)
    numbers = (((former_dim,), (latter_dim,)), ((), ()))
    return lax.dot_general(
        narrow, upper, numbers, preferred_element_type=jnp.float32
    ) + lax.dot_general(narrow, rest, numbers, preferred_element_type=jnp.float32)


def split_right(values, narrow, former_dim, latter_dim):
    upper, rest = split_parts(values)
    numbers = (((former_dim,), (latter_dim,)), ((), ()))
    return lax.dot_general(
        upper, narrow, numbers, preferred_element_type=jnp.float32
    ) + lax.dot_general(rest, narrow, numbers, preferred_element_type=jnp.float32)


def sigmoid_slope(inputs):
    gate_value = jax.nn.sigmoid(inputs)
    return gate_value * (1.0 - gate_value)


def silu_slope(inputs):
    gate_value = jax.nn.sigmoid(inputs)
    return gate_value * (1.0 + inputs * (1.0 - gate_value))


class Layout:
    def __init__(self, rows, length):
        self.rows = rows
        self.length = length
        self.query_tiles = -(-rows // LANES)
        self.key_tiles = -(-length // LANES)
        self.padded = self.query_tiles * LANES
        self.wide = self.key_tiles * LANES
        self.last = self.key_tiles - 1
        self.groups = (self.query_tiles + 4) * 4
        assert 2 * self.groups + 3 <= LANES and self.groups <= 64
        assert rows - 1 + NEAR < self.padded and length - NEAR >= self.last * LANES
        assert rows % 8 == 0 and self.last > self.query_tiles
        self.block_rows = rows if rows % 16 == 0 else self.padded
        self.pieces = [rows, length - rows] if rows % 16 == 0 else [length]

    def tile_start(self, tile):
        return self.last * LANES if tile < 0 else tile * LANES


def pad_to(values, axis, size, fill):
    widths = [(0, 0)] * values.ndim
    widths[axis] = (0, size - values.shape[axis])
    return jnp.pad(values, widths, constant_values=fill)


def tables_kernel(layout, bin_count, start_ref, pairs_ref, *out_refs):
    members_ref, kinds_ref, forward_ref, backward_ref, places_ref = out_refs[:5]
    members_turned, kinds_turned, codes = out_refs[5:]
    rows, length, queries, groups = layout.rows, layout.length, layout.query_tiles, layout.groups
    wrap = length - start_ref[0]
    reach = (bin_count - 2) // 2
    zero_bin = LANES - 1
    shape = (LANES, LANES)
    lane = lax.broadcasted_iota(jnp.int32, shape, 1)
    row = lax.broadcasted_iota(jnp.int32, shape, 0)
    last_start = layout.last * LANES

    tiles = pairs_ref.shape[1]
    marks = pairs_ref[1].astype(jnp.float32)
    place = lax.broadcasted_iota(jnp.int32, marks.shape, 0) * LANES + lax.broadcasted_iota(
        jnp.int32, marks.shape, 1
    )
    before = jnp.sum(jnp.where(place < wrap, marks, 0.0), keepdims=True)
    every = jnp.sum(marks, keepdims=True)
    triangle = jnp.where(row <= lane, 1.0, 0.0).astype(jnp.bfloat16)
    running = jnp.dot(marks.astype(jnp.bfloat16), triangle, preferred_element_type=jnp.float32)
    numbers, chains = [], []
    carry = jnp.zeros((1, 1), jnp.float32)
    for tile in range(layout.key_tiles):
        count = running[tile : tile + 1] + carry
        carry = carry + running[tile : tile + 1, LANES - 1 :]
        count = count + jnp.where(place[tile : tile + 1] < wrap, every - before, -before)
        chains.append(jnp.broadcast_to(count.astype(jnp.int32), shape))
        numbers.append(jnp.broadcast_to(pairs_ref[0, tile : tile + 1], shape))
    number_rows = [value.T for value in numbers]
    chain_rows = [value.T for value in chains]

    def bins_of(key_number, key_chain, query_number, query_chain):
        offset = jnp.clip(key_number - query_number, -reach, reach) + reach
        return jnp.where(key_chain == query_chain, offset, bin_count - 1)

    def touches(query, tile):
        begin = -LANES if tile < 0 else tile * LANES
        return (begin <= query + NEAR) & (query - NEAR <= begin + LANES - 1)

    for tile in range(layout.key_tiles):
        size = min(LANES, length - tile * LANES)
        key = tile * LANES + row
        if tile == layout.last:
            other = jnp.full(shape, queries + 3, jnp.int32)
        elif tile == queries - 1:
            other = jnp.full(shape, queries, jnp.int32)
        else:
            other = jnp.where(key < wrap, queries + 1, queries + 2)
        group = jnp.where(key < rows, tile, other)
        slot = group * 4 + chain_rows[tile] - 1
        hit = (lane == slot) | (lane == slot + groups)
        tail = (lane >= 2 * groups) & (lane < 2 * groups + 3)
        values = jnp.where(hit, 1.0, jnp.where(tail, -1.0, 0.0)).astype(jnp.bfloat16)
        members_ref[tile * LANES : tile * LANES + size] = values[:size]
        turned = jnp.where(hit & (lane < groups), 1.0, 0.0).T
        members_turned[:, tile * LANES : tile * LANES + size] = turned[:64, :size].astype(jnp.bfloat16)

    local = jnp.where(lane >= groups, lane - groups, lane)
    lane_group = local >> 2
    lane_chain = (local & 3) + 1
    lane_begin = jnp.where(
        lane_group < queries,
        lane_group * LANES,
        jnp.where(lane_group == queries, (queries - 1) * LANES, -LANES),
    )
    has_band = (lane_group <= queries) | (lane_group == queries + 3)
    other_right = jnp.where(
        lane_group == queries,
        rows,
        jnp.where(
            lane_group == queries + 3,
            last_start,
            jnp.where(lane_group == queries + 1, 0, 2 * length),
        ),
    )
    right_limit = jnp.where(lane_group > queries, jnp.where(lane_group == queries + 3, wrap, length), wrap)
    for tile in range(queries):
        size = min(LANES, layout.block_rows - tile * LANES)
        query = tile * LANES + row
        near = (lane_begin <= query + NEAR) & (query - NEAR <= lane_begin + LANES - 1) & has_band
        right = jnp.where(lane_group < queries, lane_group - tile, right_limit - other_right) > 0
        same = chain_rows[tile] == lane_chain
        kinds = jnp.where(same, jnp.where(near, NONE, jnp.where(right, RIGHT, LEFT)), APART)
        kinds = jnp.where((lane < 2 * groups) & (query < rows), kinds, NONE)
        kinds_ref[tile * LANES : tile * LANES + size] = kinds[:size]
        kinds_turned[:, tile * LANES : (tile + 1) * LANES] = jnp.where(lane < groups, kinds, NONE).T[:64]
        for step in range(3):
            near_tile = tile + step - 1
            index = layout.last if near_tile < 0 else near_tile
            if near_tile < queries:
                inside = touches(query, near_tile) & (query < rows)
                inside &= lane < length - index * LANES
                found = bins_of(
                    numbers[index], chains[index], number_rows[tile], chain_rows[tile]
                )
                found = jnp.where(inside, found, zero_bin)
            else:
                found = jnp.full(shape, zero_bin, jnp.int32)
            forward_ref[
                tile * LANES : (tile + 1) * LANES, step * LANES : (step + 1) * LANES
            ] = found

    codes[...] = jnp.full(codes.shape, -1, jnp.int32)
    for tile in range(queries):
        size = min(LANES, rows - tile * LANES)
        code = number_rows[tile] * 8 + chain_rows[tile]
        codes[(tile + 1) * LANES : (tile + 1) * LANES + size] = code[:size]

    for index, tile in enumerate(list(range(queries)) + [-1]):
        source = layout.last if tile < 0 else tile
        key_row = (row - (length - last_start)) if tile < 0 else tile * LANES + row
        present = row < length - source * LANES
        for step in range(3):
            near_tile = tile + step - 1
            if 0 <= near_tile < queries:
                near_query = near_tile * LANES + lane
                inside = touches(near_query, tile) & (near_query < rows) & present
                found = bins_of(
                    number_rows[source], chain_rows[source], numbers[near_tile], chains[near_tile]
                )
                found = jnp.where(inside, found, zero_bin)
            else:
                found = jnp.full(shape, zero_bin, jnp.int32)
            backward_ref[
                index * LANES : (index + 1) * LANES, step * LANES : (step + 1) * LANES
            ] = found
        target = (number_rows[source] + reach - lane) * 8 + chain_rows[source]
        target = jnp.where(present & (lane > 0) & (lane < 2 * reach), target, -9)
        offset = (LANES - (length - last_start)) if tile < 0 else (tile + 1) * LANES
        far = 4 * LANES
        shift = jnp.full(shape, far, jnp.int32)
        for distance in range(-NEAR, NEAR + 1):
            other = codes[offset - distance : offset - distance + LANES]
            shift = jnp.where(other == target, distance, shift)
        if tile < 0:
            base = jnp.zeros(shape, jnp.int32)
        else:
            base = jnp.where(row < LANES // 2, tile - 1, tile) * LANES
        places_ref[index * LANES : (index + 1) * LANES] = jnp.where(
            shift == far, far - 1, key_row - shift - base
        )


def attention_tables(layout, numbers, marks, query_start, bin_count):
    crops = numbers.shape[0]
    pairs = jnp.stack([numbers, marks], axis=1)
    pairs = pad_to(pairs, 2, layout.wide, 0).reshape(crops, 2, layout.key_tiles, LANES)
    spots = (layout.query_tiles + 1) * LANES
    shapes = [
        ((layout.length, LANES), jnp.bfloat16),
        ((layout.block_rows, LANES), jnp.int32),
        ((layout.padded, 3 * LANES), jnp.int32),
        ((spots, 3 * LANES), jnp.int32),
        ((spots, LANES), jnp.int32),
        ((64, layout.length), jnp.bfloat16),
        ((64, layout.padded), jnp.int32),
    ]
    return pl.pallas_call(
        functools.partial(tables_kernel, layout, bin_count),
        grid=(crops,),
        in_specs=[
            pl.BlockSpec(memory_space=pltpu.SMEM),
            pl.BlockSpec((None, 2, layout.key_tiles, LANES), lambda crop: (crop, 0, 0, 0)),
        ],
        out_specs=tuple(pl.BlockSpec((None, *shape), lambda crop: (crop, 0, 0)) for shape, _ in shapes),
        out_shape=tuple(jax.ShapeDtypeStruct((crops, *shape), kind) for shape, kind in shapes),
        scratch_shapes=[pltpu.VMEM((layout.padded + 2 * LANES, LANES), jnp.int32)],
        compiler_params=pltpu.CompilerParams(vmem_limit_bytes=VMEM_BYTES),
        cost_estimate=pl.CostEstimate(
            flops=40000000 * crops, bytes_accessed=4000000 * crops, transcendentals=0
        ),
        name="pair_tables",
    )(jnp.reshape(query_start, (1,)).astype(jnp.int32), pairs)


def head_tables(layout, bias_rows, scale):
    bin_count, heads = bias_rows.shape
    table = (bias_rows - bias_rows[bin_count - 1 :]).T / scale
    lane = jnp.arange(LANES, dtype=jnp.int32)
    groups = layout.groups

    def columns(values):
        upper = lax.reduce_precision(values, 8, 7)
        rest = values - upper
        return jnp.where(
            lane < groups, upper[:, None], jnp.where(lane < 2 * groups, rest[:, None], 0.0)
        )

    lookup = pad_to(table, 1, LANES, 0.0)
    stacked = jnp.stack([lookup, columns(table[:, bin_count - 2]), columns(table[:, 0])], 1)
    stacked = pad_to(stacked, 1, 8, 0.0)
    return stacked.reshape(heads // 2, 16, LANES)


NT = (((1,), (1,)), ((), ()))
TN = (((0,), (0,)), ((), ()))


def wide_dot(former, latter, numbers=(((1,), (0,)), ((), ()))):
    return lax.dot_general(former, latter, numbers, preferred_element_type=jnp.float32)


def look_up(table_row, bins):
    table = jnp.broadcast_to(table_row, bins.shape)
    return jnp.take_along_axis(table, bins, axis=1, mode="promise_in_bounds")


def half_of(values, lane, side):
    return jnp.where((lane >= 64) == (side == 1), values, jnp.zeros_like(values))


def row_blocks(total, size):
    return [(start, min(start + size, total)) for start in range(0, total, size)]


def group_columns(kinds, tables, side):
    right = tables[8 * side + 1 : 8 * side + 2]
    left = tables[8 * side + 2 : 8 * side + 3]
    return jnp.where(kinds == RIGHT, right, jnp.where(kinds == LEFT, left, 0.0))


def forward_kernel(layout, scale, *refs):
    count = len(layout.pieces)
    query_ref = refs[0]
    key_refs = refs[1 : 1 + count]
    value_refs = refs[1 + count : 1 + 2 * count]
    members_ref, kinds_ref, bins_ref, tables_ref, out_ref, log_ref = refs[1 + 2 * count : -1]
    all_scores = refs[-1]
    pair = pl.program_id(1)
    rows, length = layout.block_rows, layout.length
    turn = 0
    factor = scale * LOG2E
    lane = lax.broadcasted_iota(jnp.int32, (1, LANES), 1)
    query = query_ref[...]
    keys = jnp.concatenate([ref[...] for ref in key_refs], axis=0)
    values = jnp.concatenate([ref[...] for ref in value_refs], axis=0)
    members = members_ref[...]
    kinds = kinds_ref[...]
    tables = tables_ref[...]
    values_turned = values.T
    blocks = row_blocks(rows, 256)
    turned = [[None, None] for _ in blocks]
    totals = [[None, None] for _ in blocks]

    @pl.when(pair == 0)
    def _():
        log_ref[...] = jnp.zeros_like(log_ref)

    for side in range(2):
        key_columns = jnp.concatenate([half_of(keys, lane, side), members], axis=1)
        extra = group_columns(kinds, tables, side).astype(jnp.bfloat16)
        query_columns = jnp.concatenate([query, extra], axis=1)
        table_row = tables[8 * side : 8 * side + 1]
        for number, (start, stop) in enumerate(blocks):
            size = stop - start
            scores = all_scores.at[turn % 2]
            turn += 1
            scores[0:size, 0:length] = wide_dot(query_columns[start:stop], key_columns, NT)
            for tile in range(start // LANES, -(-stop // LANES)):
                first, final = tile * LANES, min(tile * LANES + LANES, rows)
                for slot in range(3):
                    other = tile + slot - 1
                    if other >= layout.query_tiles:
                        continue
                    low, high = first, final
                    if slot == 0:
                        high = min(first + 32, final)
                    if slot == 2:
                        low = first + LANES - 32
                    if low >= high:
                        continue
                    place = layout.tile_start(other)
                    width = min(LANES, length - place)
                    bins = bins_ref[low:high, slot * LANES : (slot + 1) * LANES]
                    bias = look_up(table_row, bins)[:, :width]
                    scores[low - start : high - start, place : place + width] += bias
            block = scores[0:size, 0:length]
            top = jnp.max(block, axis=1, keepdims=True)
            weights = jnp.exp2((block - top) * factor)
            total = jnp.sum(weights, axis=1, keepdims=True)
            turned[number][side] = wide_dot(
                values_turned[64 * side : 64 * side + 64], weights.astype(jnp.bfloat16), NT
            )
            totals[number][side] = total
            log_total = top + jnp.log(total) * (1.0 / scale)
            log_ref[start:stop] = jnp.where(
                lane == 2 * pair + side, log_total, log_ref[start:stop]
            )
    for number, (start, stop) in enumerate(blocks):
        result = jnp.concatenate(turned[number], axis=0).T
        out_ref[start:stop] = result / jnp.where(lane < 64, *totals[number])


def backward_kernel(layout, scale, first_pair, *refs):
    count = len(layout.pieces)
    query_ref, grad_ref, out_ref, log_ref = refs[:4]
    key_refs = refs[4 : 4 + count]
    value_refs = refs[4 + count : 4 + 2 * count]
    rest = refs[4 + 2 * count :]
    members_ref, kinds_ref, bins_ref, places_ref, tables_ref = rest[:5]
    members_turned_ref, kinds_turned_ref = rest[5:7]
    grad_query_ref = rest[7]
    grad_pair_refs = rest[8 : 8 + count]
    grad_table_ref = rest[8 + count]
    query_wide, grad_wide, query_turned, grad_turned = rest[9 + count : 13 + count]
    all_scores, all_slopes, slopes_low, probs_low = rest[13 + count :]
    pair = pl.program_id(1) + first_pair
    rows, length, padded = layout.block_rows, layout.length, layout.padded
    factor = scale * LOG2E
    lane = lax.broadcasted_iota(jnp.int32, (1, LANES), 1)
    keys = jnp.concatenate([ref[...] for ref in key_refs], axis=0)
    values = jnp.concatenate([ref[...] for ref in value_refs], axis=0)
    members = members_ref[...]
    kinds = kinds_ref[...]
    tables = tables_ref[...]
    query = query_ref[...]
    grad = grad_ref[...]
    grad_full = grad.astype(jnp.float32)
    product = grad_full * out_ref[...]
    log_all = log_ref[...]
    tail = 2 * layout.groups
    ones = jnp.broadcast_to(jnp.where(lane < 3, 1.0, 0.0), (length, LANES)).astype(jnp.bfloat16)

    def three_parts(values):
        upper = values.astype(jnp.bfloat16).astype(jnp.float32)
        values = values - upper
        middle = values.astype(jnp.bfloat16).astype(jnp.float32)
        return upper, middle, values - middle

    def in_lanes(parts, first):
        return jnp.where(
            lane == first,
            parts[0],
            jnp.where(lane == first + 1, parts[1], jnp.where(lane == first + 2, parts[2], 0.0)),
        )

    if padded > rows:
        for ref in (query_wide, grad_wide):
            for side in range(2):
                ref[side, rows:padded] = jnp.zeros((padded - rows, ref.shape[2]), jnp.bfloat16)
        for ref in (query_turned, grad_turned):
            ref[:, rows:padded] = jnp.zeros((LANES, padded - rows), jnp.bfloat16)
    query_turned[:, 0:rows] = query.T
    grad_turned[:, 0:rows] = grad.T
    for side in range(2):
        log_total = jnp.sum(
            jnp.where(lane == 2 * pair + side, log_all, 0.0), axis=1, keepdims=True
        )
        extra = group_columns(kinds, tables, side) + in_lanes(three_parts(log_total), tail)
        query_wide[side, 0:rows, 0:LANES] = query
        query_wide[side, 0:rows, LANES:] = extra.astype(jnp.bfloat16)
        delta = jnp.sum(half_of(product, lane, side), axis=1, keepdims=True)
        grad_wide[side, 0:rows, 0:LANES] = grad
        grad_wide[side, 0:rows, LANES:] = in_lanes(three_parts(-delta), 0).astype(jnp.bfloat16)

    key_columns = [
        jnp.concatenate([half_of(keys, lane, side), members], axis=1) for side in range(2)
    ]
    value_columns = [
        jnp.concatenate([half_of(values, lane, side), ones], axis=1) for side in range(2)
    ]
    inner_sums = [jnp.zeros((1, LANES), jnp.float32) for _ in range(2)]
    low_sums = [jnp.zeros((1, LANES), jnp.float32) for _ in range(2)]
    high_sums = [jnp.zeros((1, LANES), jnp.float32) for _ in range(2)]
    reach_tiles = list(range(layout.query_tiles)) + [-1]

    def put(which, start, stop, result):
        begin = 0
        for ref, size in zip(grad_pair_refs, layout.pieces):
            low, high = max(start, begin), min(stop, begin + size)
            if low < high:
                ref[which, low - begin : high - begin] = result[low - start : high - start]
            begin += size

    for start, stop in row_blocks(length, 384):
        size = stop - start
        for side in range(2):
            table_row = tables[8 * side : 8 * side + 1]
            scores, slopes = all_scores.at[side], all_slopes.at[side]
            scores[0:size] = wide_dot(key_columns[side][start:stop], query_wide[side], NT)
            near = []
            for index, tile in enumerate(reach_tiles):
                place = layout.tile_start(tile)
                if start <= place < stop:
                    near.append((index, tile, place, min(place + LANES, length)))
            for index, tile, place, final in near:
                for slot in range(3):
                    other = tile + slot - 1
                    if not 0 <= other < layout.query_tiles:
                        continue
                    bins = bins_ref[
                        index * LANES : index * LANES + final - place,
                        slot * LANES : (slot + 1) * LANES,
                    ]
                    scores[
                        place - start : final - start, other * LANES : (other + 1) * LANES
                    ] += look_up(table_row, bins)
            probs = jnp.exp2(scores[0:size] * factor)
            grad_probs = wide_dot(value_columns[side][start:stop], grad_wide[side], NT)
            slope = probs * grad_probs
            if near:
                slopes[0:size] = slope
            low = slope.astype(jnp.bfloat16)
            slopes_low[side, start:stop] = low
            probs_low[side, start:stop] = probs.astype(jnp.bfloat16)
            for index, tile, place, final in near:
                for slot in range(3):
                    other = tile + slot - 1
                    if not 0 <= other < layout.query_tiles:
                        continue
                    bins = bins_ref[
                        index * LANES : index * LANES + final - place,
                        slot * LANES : (slot + 1) * LANES,
                    ]
                    cut = slopes[place - start : final - start, other * LANES : (other + 1) * LANES]
                    low_sums[side] += jnp.sum(
                        jnp.where(bins == 0, cut, 0.0), axis=0, keepdims=True
                    )
                    high_sums[side] += jnp.sum(
                        jnp.where(bins == 2 * (NEAR + 1), cut, 0.0), axis=0, keepdims=True
                    )
                for half in range(2):
                    begin, end = half * 64, min(half * 64 + 64, final - place)
                    if begin >= end:
                        continue
                    base = 0 if tile < 0 else tile - 1 + half
                    where = places_ref[index * LANES + begin : index * LANES + end]
                    spot = where & (LANES - 1)
                    for step in range(2):
                        other = base + step
                        if not 0 <= other < layout.query_tiles or (tile < 0 and step):
                            continue
                        cut = slopes[
                            place - start + begin : place - start + end,
                            other * LANES : (other + 1) * LANES,
                        ]
                        picked = jnp.take_along_axis(cut, spot, axis=1, mode="promise_in_bounds")
                        picked = jnp.where((where >> 7) == step, picked, 0.0)
                        inner_sums[side] += jnp.sum(picked, axis=0, keepdims=True)

    keys_turned = keys.T
    grad_keys, grad_values, grad_queries = [], [], []
    kinds_turned = kinds_turned_ref[...]
    for side in range(2):
        cut = slice(64 * side, 64 * side + 64)
        grad_values.append(wide_dot(grad_turned[cut], probs_low[side], NT))
        grad_keys.append(wide_dot(query_turned[cut], slopes_low[side], NT))
        left = jnp.concatenate([keys_turned[cut], members_turned_ref[...]], axis=0)
        both = wide_dot(left, slopes_low[side])
        grad_queries.append(both[:64])
        sums = both[64:]

        def total(kind):
            return jnp.sum(jnp.where(kinds_turned == kind, sums, 0.0))

        right = total(RIGHT) + jnp.sum(high_sums[side])
        left = total(LEFT) + jnp.sum(low_sums[side])
        apart = total(APART)
        grad_table_ref[side : side + 1] = jnp.where(
            lane == 0,
            left,
            jnp.where(
                lane == 2 * (NEAR + 1),
                right,
                jnp.where(lane == 2 * (NEAR + 1) + 1, apart, inner_sums[side]),
            ),
        )
    put(0, 0, length, (jnp.concatenate(grad_keys, axis=0) * scale).T.astype(jnp.bfloat16))
    put(1, 0, length, jnp.concatenate(grad_values, axis=0).T.astype(jnp.bfloat16))
    turned = jnp.concatenate(grad_queries, axis=0) * scale
    grad_query_ref[...] = turned.T[0:rows].astype(jnp.bfloat16)


def tile_columns(rows, offset=0):
    return pl.BlockSpec((None, rows, LANES), lambda crop, pair: (crop, 0, pair + offset))


def per_crop(rows, width):
    return pl.BlockSpec((None, rows, width), lambda crop, pair: (crop, 0, 0))


def kernel_params():
    return pltpu.CompilerParams(
        vmem_limit_bytes=VMEM_BYTES, dimension_semantics=("arbitrary", "arbitrary")
    )


def attention_forward(layout, scale, projected, key_values, members, kinds, bins, tables):
    crops, rows, _ = projected.shape
    pairs = tables.shape[0]
    specs = [tile_columns(rows)]
    operands = [projected]
    for place in (1, 2):
        for piece in key_values:
            specs.append(tile_columns(piece[0].shape[1], piece[place]))
            operands.append(piece[0])
    specs += [
        per_crop(layout.length, LANES),
        per_crop(rows, LANES),
        per_crop(layout.padded, 3 * LANES),
        pl.BlockSpec((None, 16, LANES), lambda crop, pair: (pair, 0, 0)),
    ]
    flops = 2 * crops * pairs * 2 * rows * layout.length * 256 * 2
    return pl.pallas_call(
        functools.partial(forward_kernel, layout, scale),
        grid=(crops, pairs),
        in_specs=specs,
        out_specs=(tile_columns(rows), per_crop(rows, LANES)),
        out_shape=(
            jax.ShapeDtypeStruct((crops, rows, pairs * LANES), jnp.float32),
            jax.ShapeDtypeStruct((crops, rows, LANES), jnp.float32),
        ),
        scratch_shapes=[pltpu.VMEM((2, 256, layout.wide), jnp.float32)],
        compiler_params=kernel_params(),
        cost_estimate=pl.CostEstimate(
            flops=flops,
            bytes_accessed=12 * crops * rows * pairs * LANES,
            transcendentals=crops * pairs * 2 * rows * layout.length,
        ),
        name="attention_forward",
    )(*operands, members, kinds, bins, tables)


def attention_backward(
    layout,
    scale,
    first_pair,
    pairs,
    projected,
    grad_out,
    attended,
    logs,
    key_values,
    members,
    kinds,
    bins,
    places,
    members_turned,
    kinds_turned,
    tables,
):
    crops, rows, _ = projected.shape
    specs = [tile_columns(rows, first_pair)] * 3 + [per_crop(rows, LANES)]
    operands = [projected, grad_out, attended, logs]
    for place in (1, 2):
        for piece in key_values:
            specs.append(tile_columns(piece[0].shape[1], piece[place] + first_pair))
            operands.append(piece[0])
    specs += [
        per_crop(layout.length, LANES),
        per_crop(rows, LANES),
        per_crop(bins.shape[1], 3 * LANES),
        per_crop(places.shape[1], LANES),
        pl.BlockSpec((None, 16, LANES), lambda crop, pair: (pair + first_pair, 0, 0)),
        per_crop(64, layout.length),
        per_crop(64, layout.padded),
    ]
    out_specs = [tile_columns(rows)]
    out_shapes = [jax.ShapeDtypeStruct((crops, rows, pairs * LANES), jnp.bfloat16)]
    for piece in key_values:
        size = piece[0].shape[1]
        out_specs.append(
            pl.BlockSpec((None, 2, size, LANES), lambda crop, pair: (crop, 0, 0, pair))
        )
        out_shapes.append(jax.ShapeDtypeStruct((crops, 2, size, pairs * LANES), jnp.bfloat16))
    out_specs.append(pl.BlockSpec((None, None, 8, LANES), lambda crop, pair: (crop, pair, 0, 0)))
    out_shapes.append(jax.ShapeDtypeStruct((crops, pairs, 8, LANES), jnp.float32))
    padded, block = layout.padded, 384
    return pl.pallas_call(
        functools.partial(backward_kernel, layout, scale, first_pair),
        grid=(crops, pairs),
        in_specs=specs,
        out_specs=tuple(out_specs),
        out_shape=tuple(out_shapes),
        scratch_shapes=[
            pltpu.VMEM((2, padded, 2 * LANES), jnp.bfloat16),
            pltpu.VMEM((2, padded, 2 * LANES), jnp.bfloat16),
            pltpu.VMEM((LANES, padded), jnp.bfloat16),
            pltpu.VMEM((LANES, padded), jnp.bfloat16),
            pltpu.VMEM((2, block, padded), jnp.float32),
            pltpu.VMEM((2, block, padded), jnp.float32),
            pltpu.VMEM((2, layout.length, padded), jnp.bfloat16),
            pltpu.VMEM((2, layout.length, padded), jnp.bfloat16),
        ],
        compiler_params=kernel_params(),
        cost_estimate=pl.CostEstimate(
            flops=2 * crops * pairs * 2 * rows * layout.length * 256 * 5,
            bytes_accessed=20 * crops * rows * pairs * LANES,
            transcendentals=crops * pairs * 2 * rows * layout.length,
        ),
        name="attention_backward",
    )(*operands, members, kinds, bins, places, tables, members_turned, kinds_turned)


def sigmoid(values):
    return 0.5 * jnp.tanh(0.5 * values) + 0.5


def fold_rows(values):
    return jnp.sum(values.reshape(values.shape[0] // 8, 8, values.shape[1]), axis=0)


def feed_kernel(split, chunks, here_ref, *refs):
    (attended_ref, tokens_ref, upstream_ref, normed_a_ref, mod_ref, gate_weight_ref, output_ref) = refs[:7]
    gate_ref, up_ref, down_ref = refs[7:10]
    layer_ref, grad_middle_ref, grad_att_ref, grad_pre_ref, sums_ref = refs[10:15]
    grads = refs[15:-12]
    gated, grad_ff, normed, branch, middle, total, grad_normed, hidden, both, grad_branch = refs[-12:-2]
    gate_pre, turned = refs[-2:]
    step = pl.program_id(0)
    here = here_ref[0]
    rows, width = tokens_ref.shape
    size = gate_ref.shape[1]
    strip = 112 if rows % 112 == 0 else 64
    strips = rows // strip
    shift_f, scale_f = mod_ref[3:4], mod_ref[4:5]
    open_a, open_f = sigmoid(mod_ref[2:3]), sigmoid(mod_ref[5:6])

    def strip_of(index):
        return pl.ds(pl.multiple_of(index * strip, strip), strip)

    def norm_of(values):
        mean_value = jnp.mean(values, axis=1, keepdims=True)
        centred = values - mean_value
        spread = jnp.mean(centred * centred, axis=1, keepdims=True)
        root = lax.rsqrt(spread + 1e-06)
        return centred * root, root

    @pl.when(step == 0)
    def _():
        gate_pre[...] = wide_dot(normed_a_ref[...], gate_weight_ref[...])

        @pl.loop(0, strips)
        def _(index):
            cut = strip_of(index)
            gated[cut] = (attended_ref[cut] * sigmoid(gate_pre[cut])).astype(jnp.bfloat16)
            grad_ff[cut] = (upstream_ref[cut].astype(jnp.float32) * open_f).astype(jnp.bfloat16)

        branch[...] = wide_dot(gated[...], output_ref[...])

        @pl.loop(0, strips)
        def _(index):
            cut = strip_of(index)
            values = tokens_ref[cut].astype(jnp.float32) + open_a * branch[cut]
            middle[cut] = values
            normed[cut] = (norm_of(values)[0] * (1.0 + scale_f) + shift_f).astype(jnp.bfloat16)
            total[cut] = jnp.zeros((strip, width), jnp.float32)
            grad_normed[cut] = jnp.zeros((strip, width), jnp.float32)

        turned[...] = normed[...].T

    block = rows if rows <= 384 else rows // 2
    for start in range(0, rows, block):
        cut = slice(start, start + block)
        before = wide_dot(normed[cut], gate_ref[...])
        lifted = wide_dot(normed[cut], up_ref[...])
        grad_hidden = wide_dot(grad_ff[cut], down_ref[...], NT)
        switch = sigmoid(before)
        silu = before * switch
        part = (silu * lifted).astype(jnp.bfloat16)
        hidden[cut] = part
        grad_up = (grad_hidden * silu).astype(jnp.bfloat16)
        grad_gate = (grad_hidden * lifted * (switch + silu * (1.0 - switch))).astype(jnp.bfloat16)
        both[cut, :size] = grad_gate
        both[cut, size:] = grad_up
        total[cut] += wide_dot(part, down_ref[...])
        grad_normed[cut] += wide_dot(grad_gate, gate_ref[...], NT) + wide_dot(
            grad_up, up_ref[...], NT
        )

    pair = wide_dot(turned[...], both[...]).astype(jnp.bfloat16)
    if split:
        gate_send, gate_keep, up_send, up_keep, down_send, down_keep, small_send, small_keep = grads
        half = width // 2
        away = pl.ds(pl.multiple_of((1 - here) * half, LANES), half)
        home = pl.ds(pl.multiple_of(here * half, LANES), half)
        down_send[...] = wide_dot(hidden[...], grad_ff[:, away], TN).astype(jnp.bfloat16)
        down_keep[...] = wide_dot(hidden[...], grad_ff[:, home], TN).astype(jnp.bfloat16)

        @pl.when(step < chunks // 2)
        def _():
            gate_send[...] = pair[:, :size]
            up_send[...] = pair[:, size:]

        @pl.when(step >= chunks // 2)
        def _():
            gate_keep[...] = pair[:, :size]
            up_keep[...] = pair[:, size:]
    else:
        gate_all, up_all, down_all, small_all = grads
        gate_all[...] = pair[:, :size]
        up_all[...] = pair[:, size:]
        down_all[...] = wide_dot(hidden[...], grad_ff[...], TN).astype(jnp.bfloat16)

    @pl.when(step == chunks - 1)
    def _():
        def finish(index, sums):
            gate_f_sum, shift_sum, scale_sum, gate_a_sum = sums
            cut = strip_of(index)
            values = middle[cut]
            fed = total[cut]
            upstream = upstream_ref[cut].astype(jnp.float32)
            layer_ref[cut] = (values + open_f * fed).astype(jnp.bfloat16)
            normal, root = norm_of(values)
            grad = grad_normed[cut]
            scaled = grad * (1.0 + scale_f)
            grad_middle = upstream + root * (
                scaled
                - jnp.mean(scaled, axis=1, keepdims=True)
                - normal * jnp.mean(scaled * normal, axis=1, keepdims=True)
            )
            grad_middle_ref[cut] = grad_middle
            grad_branch[cut] = (grad_middle * open_a).astype(jnp.bfloat16)
            return (
                gate_f_sum + fold_rows(upstream * fed),
                shift_sum + fold_rows(grad),
                scale_sum + fold_rows(grad * normal),
                gate_a_sum + fold_rows(grad_middle * branch[cut]),
            )

        zero = jnp.zeros((8, width), jnp.float32)
        sums = lax.fori_loop(0, strips, finish, (zero, zero, zero, zero))
        gate_f_sum, shift_sum, scale_sum, gate_a_sum = [
            jnp.sum(value, axis=0, keepdims=True) for value in sums
        ]
        none = jnp.zeros((1, width), jnp.float32)
        sums_ref[...] = jnp.concatenate(
            [
                none,
                none,
                gate_a_sum * open_a * (1.0 - open_a),
                shift_sum,
                scale_sum,
                gate_f_sum * open_f * (1.0 - open_f),
                none,
                none,
            ],
            axis=0,
        )
        total[...] = wide_dot(grad_branch[...], output_ref[...], NT)

        @pl.loop(0, strips)
        def _(index):
            cut = strip_of(index)
            grad_gated = total[cut]
            opened = sigmoid(gate_pre[cut])
            grad_att_ref[cut] = (grad_gated * opened).astype(jnp.bfloat16)
            grad_pre_ref[cut] = (
                grad_gated * attended_ref[cut] * (opened * (1.0 - opened))
            ).astype(jnp.bfloat16)

        if split:
            for side, ref in ((away, small_send), (home, small_keep)):
                ref[:, :half] = wide_dot(gated[...], grad_branch[:, side], TN).astype(jnp.bfloat16)
                ref[:, half:] = wide_dot(normed_a_ref[...], grad_pre_ref[:, side], TN).astype(
                    jnp.bfloat16
                )
        else:
            small_all[:, :width] = wide_dot(gated[...], grad_branch[...], TN).astype(jnp.bfloat16)
            small_all[:, width:] = wide_dot(normed_a_ref[...], grad_pre_ref[...], TN).astype(
                jnp.bfloat16
            )


def feed_layer(
    split, here, attended, tokens, upstream, normed_a, mod_rows, gate_weight, output_weight, feed_gate, feed_up, feed_down
):
    rows, width = tokens.shape
    inner = feed_gate.shape[1]
    size = 512
    chunks = inner // size
    half = chunks // 2

    def turn(step, here_ref):
        return (step + half * (1 - here_ref[0])) % chunks if split else step

    def fixed(shape):
        return pl.BlockSpec(shape, lambda step, here_ref: (0, 0), pipeline_mode=pl.Buffered(1))

    def columns(step, here_ref):
        return (0, turn(step, here_ref))

    def strips(step, here_ref):
        return (turn(step, here_ref), 0)

    whole = (rows, width)
    in_specs = [fixed(whole)] * 4 + [
        fixed((8, width)),
        fixed((width, width)),
        fixed((width, width)),
        pl.BlockSpec((width, size), columns),
        pl.BlockSpec((width, size), columns),
        pl.BlockSpec((size, width), strips),
    ]
    out_specs = [fixed(whole)] * 4 + [fixed((8, width))]
    bf16, f32 = jnp.bfloat16, jnp.float32
    out_shapes = [(whole, bf16), (whole, f32), (whole, bf16), (whole, bf16), ((8, width), f32)]
    if split:
        first = pl.BlockSpec((width, size), lambda step, here_ref: (0, jnp.minimum(step, half - 1)))
        second = pl.BlockSpec((width, size), lambda step, here_ref: (0, jnp.maximum(step - half, 0)))
        out_specs += [first, second, first, second]
        out_shapes += [((width, inner // 2), bf16)] * 4
        out_specs += [pl.BlockSpec((size, width // 2), strips)] * 2
        out_shapes += [((inner, width // 2), bf16)] * 2
        out_specs += [fixed((width, width))] * 2
        out_shapes += [((width, width), bf16)] * 2
    else:
        out_specs += [pl.BlockSpec((width, size), columns)] * 2
        out_shapes += [((width, inner), bf16)] * 2
        out_specs += [pl.BlockSpec((size, width), strips), fixed((width, 2 * width))]
        out_shapes += [((inner, width), bf16), ((width, 2 * width), bf16)]
    return pl.pallas_call(
        functools.partial(feed_kernel, split, chunks),
        grid_spec=pltpu.PrefetchScalarGridSpec(
            num_scalar_prefetch=1,
            grid=(chunks,),
            in_specs=in_specs,
            out_specs=tuple(out_specs),
            scratch_shapes=[
                pltpu.VMEM(whole, bf16),
                pltpu.VMEM(whole, bf16),
                pltpu.VMEM(whole, bf16),
                pltpu.VMEM(whole, f32),
                pltpu.VMEM(whole, f32),
                pltpu.VMEM(whole, f32),
                pltpu.VMEM(whole, f32),
                pltpu.VMEM((rows, size), bf16),
                pltpu.VMEM((rows, 2 * size), bf16),
                pltpu.VMEM(whole, bf16),
                pltpu.VMEM(whole, f32),
                pltpu.VMEM((width, rows), bf16),
            ],
        ),
        out_shape=tuple(jax.ShapeDtypeStruct(shape, kind) for shape, kind in out_shapes),
        compiler_params=pltpu.CompilerParams(vmem_limit_bytes=VMEM_BYTES),
        cost_estimate=pl.CostEstimate(
            flops=2 * rows * width * (9 * inner + 5 * width),
            bytes_accessed=12 * width * inner + 24 * rows * width,
            transcendentals=2 * rows * inner,
        ),
        name="feed_layer",
    )(
        jnp.reshape(here, (1,)).astype(jnp.int32),
        attended,
        tokens,
        upstream,
        normed_a,
        mod_rows,
        gate_weight,
        output_weight,
        feed_gate,
        feed_up,
        feed_down,
    )


MASKS = {"u": 8, "v": 4, "y": 2, "x": 1}


def exchange(values, mask):
    return lax.ppermute(values, "crop", [(i, i ^ mask) for i in range(16)])


def swap_res(values):
    return lax.ppermute(values, "res", [(0, 1), (1, 0)])


def tie(*values):
    return lax.optimization_barrier(values)


def add_low(former, latter, kind=jnp.bfloat16):
    return (former.astype(jnp.float32) + latter.astype(jnp.float32)).astype(kind)


def stage_kernel(plans, bits_ref, *refs):
    inputs = refs[: sum(plan["count"] for plan in plans)]
    outputs = list(refs[len(inputs) :])
    for plan in plans:
        mine, inputs = inputs[: plan["count"]], inputs[plan["count"] :]
        out_ref = None if plan["apart"] else outputs.pop(0)
        for column, width, own in plan["parts"]:
            total = None
            for index in own:
                value = mine[index][...].astype(jnp.float32)
                total = value if total is None else total + value
            for index in plan["spans"]:
                total = total + mine[index][..., column : column + width].astype(jnp.float32)
            if plan["apart"]:
                outputs.pop(0)[...] = total
            else:
                out_ref[..., column : column + width] = total.astype(jnp.bfloat16)


class Halving:
    def __init__(self, streams, orders):
        self.streams = streams
        self.orders = [list(order) for order in orders]
        self.past = [[] for _ in orders]
        self.came = [[] for _ in orders]

    def stage(self, last=False):
        index = lax.axis_index("crop")
        bits = scalars(*[(index // mask) % 2 for mask in MASKS.values()])
        self.masks, plans, specs, operands, out_specs, out_shapes = [], [], [], [], [], []
        left = 0 if last else len(self.orders[0]) - 1
        steps = {3: 4, 2: 2}.get(left, 1)
        for stream, (parts, order, past) in enumerate(zip(self.streams, self.orders, self.past)):
            now = None if last else order.pop(0)
            rest = [axis for axis in MASKS if axis in order]

            def spec_of(axes, rows, width, block, now=now, rest=rest):
                def index_map(step, bits_ref):
                    places = []
                    for axis in axes:
                        bit = bits_ref[list(MASKS).index(axis)]
                        if axis == now:
                            places.append(1 - bit)
                        elif axis not in rest:
                            places.append(bit)
                        elif axis == rest[0] and steps > 1:
                            places.append(step // (steps // 2))
                        elif len(rest) > 1 and axis == rest[1] and steps > 2:
                            places.append(step % 2)
                        else:
                            places.append(0)
                    return (*places, 0, block)

                sizes = [
                    2
                    if axis in rest
                    and not (axis == rest[0] and steps > 1)
                    and not (len(rest) > 1 and axis == rest[1] and steps > 2)
                    else None
                    for axis in axes
                ]
                return pl.BlockSpec((*sizes, rows, width), index_map)

            plan = {"parts": [], "spans": [], "count": 0, "apart": last}
            column = 0
            rows = parts[0][0][0].shape[0] // 16
            for arrays, block, width in parts:
                own = []
                for value in arrays:
                    operands.append(value.reshape(2, 2, 2, 2, rows, value.shape[1]))
                    specs.append(spec_of(list(MASKS), rows, width, block))
                    own.append(plan["count"])
                    plan["count"] += 1
                plan["parts"].append((column, width, own))
                column += width
            for axes, value in self.came[stream]:
                operands.append(value.reshape(*[2] * len(axes), rows, column))
                specs.append(spec_of(axes, rows, column, 0))
                plan["spans"].append(plan["count"])
                plan["count"] += 1
            plans.append(plan)
            if last:
                for _, width, _ in plan["parts"]:
                    out_specs.append(pl.BlockSpec((rows, width), lambda step, bits_ref: (0, 0)))
                    out_shapes.append(jax.ShapeDtypeStruct((rows, width), jnp.float32))
            else:
                past.append(now)
                self.masks.append(MASKS[now])
                out_specs.append(spec_of(rest, rows, column, 0))
                out_shapes.append(
                    jax.ShapeDtypeStruct((*[2] * len(rest), rows, column), jnp.bfloat16)
                )
        self.axes = [[axis for axis in MASKS if axis in order] for order in self.orders]
        results = pl.pallas_call(
            functools.partial(stage_kernel, plans),
            grid_spec=pltpu.PrefetchScalarGridSpec(
                num_scalar_prefetch=1, grid=(steps,), in_specs=specs, out_specs=tuple(out_specs)
            ),
            out_shape=tuple(out_shapes),
            compiler_params=pltpu.CompilerParams(vmem_limit_bytes=VMEM_BYTES),
            cost_estimate=pl.CostEstimate(
                flops=sum(4 * math.prod(shape.shape) for shape in out_shapes),
                bytes_accessed=sum(8 * math.prod(shape.shape) for shape in out_shapes),
                transcendentals=0,
            ),
            name="halving_stage",
        )(bits, *operands)
        return list(results) if last else [value.reshape(-1, value.shape[-1]) for value in results]

    def send(self, values):
        return [exchange(value, mask) for value, mask in zip(values, self.masks)]

    def take(self, values):
        for came, axes, value in zip(self.came, self.axes, values):
            came.append((axes, value))


def share_columns(values, parts):
    if parts == 1:
        return values.astype(jnp.bfloat16)
    return lax.psum_scatter(values.astype(jnp.bfloat16), "res", scatter_dimension=1, tiled=True)


def scatter_crops(values):
    return lax.psum_scatter(values, "crop", scatter_dimension=0, tiled=True).astype(jnp.float32)


def gather_crops(values, crop_parts):
    if crop_parts != 16:
        return lax.all_gather(values, "crop", axis=0, tiled=True)
    index = lax.axis_index("crop")
    for mask in (1, 2, 4, 8):
        other = exchange(values, mask)
        low = (index // mask) % 2 == 0
        values = jnp.concatenate(
            [jnp.where(low, values, other), jnp.where(low, other, values)], axis=0
        )
    return values


def sum_res(values, parts):
    if parts == 1:
        return values
    if parts != 2:
        return lax.psum(values, "res")
    return values + swap_res(values)


PACK = 1152
SIDE = 384


def whole_vmem(count):
    return [pl.BlockSpec(memory_space=pltpu.VMEM)] * count


def scalars(*values):
    return jnp.stack([jnp.asarray(value, jnp.int32) for value in values])


def local_call(kernel, numbers, operands, shapes, name, flops=0):
    return pl.pallas_call(
        kernel,
        in_specs=[pl.BlockSpec(memory_space=pltpu.SMEM)] + whole_vmem(len(operands)),
        out_specs=tuple(whole_vmem(len(shapes))),
        out_shape=tuple(jax.ShapeDtypeStruct(shape, kind) for shape, kind in shapes),
        compiler_params=pltpu.CompilerParams(vmem_limit_bytes=VMEM_BYTES),
        cost_estimate=pl.CostEstimate(
            flops=flops,
            bytes_accessed=sum(value.size * value.dtype.itemsize for value in operands)
            + sum(4 * math.prod(shape) for shape, _ in shapes),
            transcendentals=0,
        ),
        name=name,
    )(numbers, *operands)


def projection_kernel(counts, here_ref, normed_ref, *refs):
    calls = len(counts)
    parts, (joined_ref, send_ref, keep_ref) = refs[: 3 * calls], refs[3 * calls :]
    width = joined_ref.shape[1] // 3
    column = 0
    for call, pairs in enumerate(counts):
        size = pairs * LANES
        query_ref, own_ref, came_ref = parts[3 * call : 3 * call + 3]
        joined_ref[:, column : column + size] = query_ref[...]
        for which in range(2):
            first = (1 + which) * width + column
            joined_ref[:, first : first + size] = add_low(own_ref[which], came_ref[which])
        column += size
    half = send_ref.shape[1]
    for side, ref in ((1 - here_ref[0], send_ref), (here_ref[0], keep_ref)):
        columns = pl.ds(pl.multiple_of(side * half, LANES), half)
        ref[...] = wide_dot(normed_ref[...], joined_ref[:, columns], TN).astype(jnp.bfloat16)


def projection_gradient(here, normed_a, calls):
    rows, width = normed_a.shape
    counts = [call[0].shape[-1] // LANES for call in calls]
    return local_call(
        functools.partial(projection_kernel, counts),
        scalars(here),
        [normed_a] + [value for call in calls for value in call],
        [
            ((rows, 3 * width), jnp.bfloat16),
            ((width, 3 * width // 2), jnp.bfloat16),
            ((width, 3 * width // 2), jnp.bfloat16),
        ],
        "projection_gradient",
        6 * rows * width * width,
    )


def finish_kernel(counts, joined_ref, weight_ref, pre_ref, gate_ref, tokens_ref, middle_ref, mod_ref, *refs):
    feed_sums_ref, extra_ref = refs[:2]
    table_refs = refs[2 : 2 + len(counts)]
    out_ref, pack_ref, total = refs[2 + len(counts) :]
    step = pl.program_id(0)
    rows, width = tokens_ref.shape
    part = wide_dot(joined_ref[...], weight_ref[...], NT)

    @pl.when(step == 0)
    def _():
        total[...] = part + wide_dot(pre_ref[...], gate_ref[...], NT)

    @pl.when(step > 0)
    def _():
        total[...] += part

    @pl.when(step == pl.num_programs(0) - 1)
    def _():
        strip = 112 if rows % 112 == 0 else 64
        scale = mod_ref[1:2]

        def finish(index, sums):
            shift_sum, scale_sum = sums
            cut = pl.ds(pl.multiple_of(index * strip, strip), strip)
            values = tokens_ref[cut].astype(jnp.float32)
            centred = values - jnp.mean(values, axis=1, keepdims=True)
            root = lax.rsqrt(jnp.mean(centred * centred, axis=1, keepdims=True) + 1e-06)
            normal = centred * root
            grad = total[cut]
            scaled = grad * (1.0 + scale)
            out_ref[cut] = (
                middle_ref[cut]
                + root
                * (
                    scaled
                    - jnp.mean(scaled, axis=1, keepdims=True)
                    - normal * jnp.mean(scaled * normal, axis=1, keepdims=True)
                )
            ).astype(jnp.bfloat16)
            return shift_sum + fold_rows(grad), scale_sum + fold_rows(grad * normal)

        zero = jnp.zeros((8, width), jnp.float32)
        shift_sum, scale_sum = lax.fori_loop(0, rows // strip, finish, (zero, zero))
        heads = []
        for ref, pairs in zip(table_refs, counts):
            for pair in range(pairs):
                heads += [ref[pair, 0:1], ref[pair, 1:2]]

        def upper_of(values):
            return values.astype(jnp.bfloat16).astype(jnp.float32)

        rests = [head - upper_of(head) for head in heads]
        count = width // LANES
        left = [
            jnp.sum(shift_sum, axis=0, keepdims=True),
            jnp.sum(scale_sum, axis=0, keepdims=True),
            feed_sums_ref[2:6],
        ]
        left += [
            jnp.concatenate(rests[i : i + count], axis=1) for i in range(0, len(heads), count)
        ]
        right = [jnp.concatenate(heads[3 * i : 3 * i + 3], axis=1) for i in range(4)]
        line = extra_ref[5:6]
        right += [extra_ref[4:5], line, line - upper_of(line), extra_ref[7:8]]
        pack = jnp.concatenate(
            [jnp.concatenate(left, axis=0), jnp.concatenate(right, axis=0)], axis=1
        )
        pack_ref[...] = jnp.concatenate([pack, jnp.zeros_like(pack)], axis=0).astype(jnp.bfloat16)


def finish_layer(
    joined, weight, grad_pre, gate_weight, tokens, grad_middle, mod_rows, feed_sums, extra, grad_tables
):
    rows, width = tokens.shape
    counts = [table.shape[0] for table in grad_tables]

    def fixed(shape):
        return pl.BlockSpec(shape, lambda step: (0,) * len(shape), pipeline_mode=pl.Buffered(1))

    return pl.pallas_call(
        functools.partial(finish_kernel, counts),
        grid=(3,),
        in_specs=[
            pl.BlockSpec((rows, width), lambda step: (0, step)),
            pl.BlockSpec((width, width), lambda step: (0, step)),
            fixed((rows, width)),
            fixed((width, width)),
            fixed((rows, width)),
            fixed((rows, width)),
            fixed((8, width)),
            fixed((8, width)),
            fixed((8, SIDE)),
        ]
        + [fixed((count, 8, LANES)) for count in counts],
        out_specs=(fixed((rows, width)), fixed((16, PACK))),
        out_shape=(
            jax.ShapeDtypeStruct((rows, width), jnp.bfloat16),
            jax.ShapeDtypeStruct((16, PACK), jnp.bfloat16),
        ),
        scratch_shapes=[pltpu.VMEM((rows, width), jnp.float32)],
        compiler_params=pltpu.CompilerParams(vmem_limit_bytes=VMEM_BYTES),
        cost_estimate=pl.CostEstimate(
            flops=8 * rows * width * width, bytes_accessed=24 * rows * width, transcendentals=0
        ),
        name="finish_layer",
    )(
        joined,
        weight,
        grad_pre,
        gate_weight,
        tokens,
        grad_middle,
        mod_rows,
        feed_sums,
        extra,
        *grad_tables,
    )


def fan_first_kernel(bits_ref, keep_ref, came_ref, mine_ref, *send_refs):
    chunk = keep_ref.shape[0] // 16
    for other, ref in enumerate((mine_ref, *send_refs)):
        for level in range(4):
            start = (level * 4 + (bits_ref[0] ^ other)) * chunk
            cut = pl.ds(pl.multiple_of(start, 16), chunk)
            ref[level * chunk : (level + 1) * chunk] = add_low(keep_ref[cut], came_ref[cut])


def fan_v_kernel(bits_ref, mine_ref, *refs):
    came_refs, (send_ref, out_ref) = refs[:3], refs[3:]
    chunk = mine_ref.shape[0] // 4
    for side, ref in ((1 - bits_ref[0], send_ref), (bits_ref[0], out_ref)):
        for far in range(2):
            cut = pl.ds(pl.multiple_of((2 * far + side) * chunk, 16), chunk)
            total = mine_ref[cut].astype(jnp.float32)
            for came_ref in came_refs:
                total = total + came_ref[cut].astype(jnp.float32)
            ref[far * chunk : (far + 1) * chunk] = total.astype(jnp.bfloat16)


def fan_u_kernel(bits_ref, mine_ref, came_ref, send_ref, out_ref):
    chunk = mine_ref.shape[0] // 2
    for side, ref in ((1 - bits_ref[0], send_ref), (bits_ref[0], out_ref)):
        cut = pl.ds(pl.multiple_of(side * chunk, 16), chunk)
        ref[...] = add_low(mine_ref[cut], came_ref[cut])


def join_packs_kernel(bits_ref, *refs):
    packs = [ref[...].astype(jnp.float32)[0:8] for ref in refs[:4]]
    refs[4][...] = jnp.concatenate(packs, axis=0).astype(jnp.bfloat16)


def small_kernel(
    heads,
    here_ref,
    mine_ref,
    came_ref,
    modulation_ref,
    pair_norm_ref,
    relative_ref,
    gain_ref,
    pair_weight_ref,
    mod_grad_ref,
    time_ref,
    label_ref,
    relative_grad_ref,
    gain_grad_ref,
    pair_grad_ref,
    grad_condition,
    grad_mod,
    kept,
):
    step = pl.program_id(0)
    crops = mine_ref.shape[0] // 8
    width = mine_ref.shape[1] - SIDE
    conds = relative_ref.shape[1]
    parts = mod_grad_ref.shape[1] // width

    def parts_split(values):
        upper = values.astype(jnp.bfloat16)
        return upper, (values - upper.astype(jnp.float32)).astype(jnp.bfloat16)

    def dot_left(narrow, values, numbers):
        upper, rest = parts_split(values)
        return wide_dot(narrow, upper, numbers) + wide_dot(narrow, rest, numbers)

    def dot_right(values, narrow, numbers):
        upper, rest = parts_split(values)
        return wide_dot(upper, narrow, numbers) + wide_dot(rest, narrow, numbers)

    def both_twice(narrow):
        return jnp.concatenate([narrow, narrow], axis=0)

    def stacked(values):
        return jnp.concatenate(parts_split(values), axis=0)

    @pl.when(step == 0)
    def _():
        shape = (8 * crops, 8 * crops)
        picked = lax.broadcasted_iota(jnp.int32, shape, 0)
        source = lax.broadcasted_iota(jnp.int32, shape, 1)
        hit = ((source >> 3) == (picked & (crops - 1))) & ((source & 7) == (picked // crops))
        select = jnp.where(hit, 1.0, 0.0).astype(jnp.bfloat16)
        mine = wide_dot(select, mine_ref[...])
        grad_mod[...] = mine[: 6 * crops, :width] + wide_dot(select, came_ref[...])[: 6 * crops, :width]
        condition = (
            mine[5 * crops : 6 * crops, width : width + conds]
            + mine[6 * crops : 7 * crops, width : width + conds]
        )
        gate_value = sigmoid(condition)
        kept[0] = condition * gate_value
        kept[1] = gate_value * (1.0 + condition * (1.0 - gate_value))
        kept[2] = mine[4 * crops : 5 * crops, width : width + conds]
        kept[3] = jnp.broadcast_to(
            mine[5 * crops : 6 * crops, width + conds : width + conds + 1]
            + mine[6 * crops : 7 * crops, width + conds : width + conds + 1],
            (crops, conds),
        )
        grad_condition[...] = jnp.zeros_like(grad_condition)

    cond_act = both_twice(kept[0].astype(jnp.bfloat16))
    for turn in range(parts):
        columns = slice(turn * width, (turn + 1) * width)
        first = pl.multiple_of((step * parts + turn) * crops, crops)
        pair = stacked(grad_mod[pl.ds(first, crops)])
        mod_grad_ref[:, columns] = wide_dot(cond_act, pair, TN)
        more = wide_dot(pair, modulation_ref[:, columns], NT)
        grad_condition[...] += more[:crops] + more[crops:]

    @pl.when(step == 0)
    def _():
        shape = (8, 8 * crops)
        line = lax.broadcasted_iota(jnp.int32, shape, 0)
        local = lax.broadcasted_iota(jnp.int32, shape, 1) & 7
        every = jnp.where(local == line, 1.0, 0.0).astype(jnp.bfloat16)
        lines = wide_dot(every, mine_ref[...]) + wide_dot(every, came_ref[...])

        def of_head(head):
            upper = width + (head % 3) * LANES
            rest = (head % (width // LANES)) * LANES
            low = 6 + head // (width // LANES)
            return (
                lines[head // 3 : head // 3 + 1, upper : upper + LANES]
                + lines[low : low + 1, rest : rest + LANES]
            )

        table = jnp.concatenate(
            [of_head(head) for head in range(heads)]
            + [jnp.zeros((16 - heads, LANES), jnp.float32)],
            axis=0,
        )
        bins = relative_ref.shape[0]
        pair_grad_ref[...] = dot_right(table, pair_norm_ref[...], (((1,), (0,)), ((), ())))[:heads]
        grad_norm = dot_right(table, pair_weight_ref[...], (((0,), (1,)), ((), ())))[:bins]
        values = relative_ref[...]
        centred = values - jnp.mean(values, axis=1, keepdims=True)
        root = lax.rsqrt(jnp.mean(centred * centred, axis=1, keepdims=True) + 1e-06)
        normal = centred * root
        gain_grad_ref[...] = jnp.sum(grad_norm * normal, axis=0, keepdims=True)
        scaled = grad_norm * gain_ref[...]
        relative_grad_ref[...] = root * (
            scaled
            - jnp.mean(scaled, axis=1, keepdims=True)
            - normal * jnp.mean(scaled * normal, axis=1, keepdims=True)
        )

    @pl.when(step == pl.num_programs(0) - 1)
    def _():
        final = stacked(grad_condition[...] * kept[1])
        time_ref[...] = wide_dot(both_twice(kept[2].astype(jnp.bfloat16)), final, TN)
        label = lax.broadcasted_iota(jnp.int32, (crops, label_ref.shape[0]), 1)
        number = kept[3][:, 0:1].astype(jnp.int32)
        onehot = jnp.where(label == number, 1.0, 0.0).astype(jnp.bfloat16)
        label_ref[...] = wide_dot(both_twice(onehot), final, TN)


def small_gradients(heads, labels, mine, came, modulation_weight, pair_norm, relative, gain, pair_weight):
    conds, wide = modulation_weight.shape
    bins = relative.shape[0]
    rows = mine.shape[0]
    steps = 3

    def fixed(shape):
        return pl.BlockSpec(shape, lambda step: (0, 0))

    shapes = [(conds, wide), (conds, conds), (labels, conds), (bins, conds), (1, conds), (heads, conds)]
    return pl.pallas_call(
        functools.partial(small_kernel, heads),
        grid=(steps,),
        in_specs=[
            pl.BlockSpec(memory_space=pltpu.SMEM),
            fixed((rows, PACK)),
            fixed((rows, PACK)),
            pl.BlockSpec((conds, wide // steps), lambda step: (0, step)),
            fixed((LANES, conds)),
            fixed((bins, conds)),
            fixed((1, conds)),
            fixed((conds, 16)),
        ],
        out_specs=tuple(
            [pl.BlockSpec((conds, wide // steps), lambda step: (0, step))]
            + [fixed(s) for s in shapes[1:]]
        ),
        out_shape=tuple(jax.ShapeDtypeStruct(shape, jnp.float32) for shape in shapes),
        scratch_shapes=[
            pltpu.VMEM((rows // 8, conds), jnp.float32),
            pltpu.VMEM((6 * rows // 8, wide // 6), jnp.float32),
            pltpu.VMEM((4, rows // 8, conds), jnp.float32),
        ],
        compiler_params=pltpu.CompilerParams(vmem_limit_bytes=VMEM_BYTES),
        cost_estimate=pl.CostEstimate(
            flops=100000000, bytes_accessed=10000000, transcendentals=0
        ),
        name="small_gradients",
    )(
        scalars(0),
        mine,
        came,
        modulation_weight,
        pair_norm,
        relative,
        gain,
        pair_weight,
    )


def per_device(
    crop_parts,
    res_parts,
    tokens,
    cotangent,
    time_levels,
    cath_ids,
    residue_numbers,
    chain_mask,
    time_weight,
    label_table,
    modulation_weight,
    projection_weight,
    gate_weight,
    output_weight,
    relative_table,
    pair_gain,
    pair_weight,
    feed_gate,
    feed_up,
    feed_down,
):
    crop_count, row_count, model_width = tokens.shape
    crop_length = residue_numbers.shape[1]
    head_count = pair_weight.shape[1]
    head_width = model_width // head_count
    bin_count = relative_table.shape[0]
    label_count = label_table.shape[0]
    token_count = crop_count * row_count
    score_scale = head_width ** (-0.5)
    pairs = head_count // 2
    layout = Layout(row_count, crop_length)
    query_start = lax.axis_index("res") * row_count

    def conditioning(features, onehot):
        return jnp.dot(features, time_weight, preferred_element_type=jnp.float32) + jnp.dot(
            onehot, label_table, preferred_element_type=jnp.float32
        )

    features = time_features(time_levels, time_weight.shape[0]).astype(jnp.bfloat16)
    label_onehot = (cath_ids[:, None] == jnp.arange(label_count, dtype=jnp.int32)[None, :]).astype(
        jnp.bfloat16
    )
    condition = conditioning(features, label_onehot)
    cond_act = jax.nn.silu(condition).astype(jnp.bfloat16)
    modulation = jnp.dot(cond_act, modulation_weight, preferred_element_type=jnp.float32)
    modulation = modulation.reshape(crop_count, 6, 1, model_width)
    shift_a, scale_a = modulation[:, 0], modulation[:, 1]
    mod_rows = pad_to(modulation[:, :, 0], 1, 8, 0.0)

    rotated = lax.dynamic_slice_in_dim(
        jnp.concatenate([jnp.stack([residue_numbers, chain_mask])] * 2, 2), query_start, crop_length, 2
    )
    members, kinds, forward_bins, backward_bins, places, *turned = attention_tables(
        layout, rotated[0], rotated[1], query_start, bin_count
    )
    relative_values = relative_table.astype(jnp.float32)
    gain_values = pair_gain.astype(jnp.float32)
    pair_norm = normalize_rows(relative_values, gain_values).astype(jnp.bfloat16)
    bias_rows = jnp.dot(pair_norm, pair_weight, preferred_element_type=jnp.float32)
    tables = head_tables(layout, bias_rows, score_scale)

    token_values = tokens.astype(jnp.float32)
    normed_a = (
        modulate(token_values, shift_a, scale_a)
        .astype(jnp.bfloat16)
        .reshape(token_count, model_width)
    )
    def project(weight):
        rows = jnp.dot(normed_a, weight, preferred_element_type=jnp.float32)
        return rows.astype(jnp.bfloat16).reshape(crop_count, row_count, -1)

    key_values = project(projection_weight[:, model_width:])
    queries = project(projection_weight[:, :model_width])
    others = [
        lax.ppermute(
            key_values, "res", [((r + step) % res_parts, r) for r in range(res_parts)]
        )
        for step in range(1, res_parts)
    ]
    small_operands = (
        pad_to(pair_norm, 0, LANES, 0.0),
        relative_values,
        gain_values.reshape(1, -1),
        pad_to(pair_weight, 1, 16, 0.0),
    )
    if others:
        others, small_operands = tie(others, small_operands)
    if len(layout.pieces) == 2:
        other = others[0] if len(others) == 1 else jnp.concatenate(others, axis=1)
        pieces = [(key_values, 0, pairs), (other, 0, pairs)]
    else:
        pieces = [(jnp.concatenate([key_values] + others, axis=1), 0, pairs)]

    def block_rows(values):
        return pad_to(values, 1, layout.block_rows, 0)

    attended, logs = attention_forward(
        layout,
        score_scale,
        block_rows(queries),
        pieces,
        members,
        kinds,
        forward_bins,
        tables,
    )
    here = lax.axis_index("res")
    split = res_parts == 2 and crop_parts == 16
    per_crop_results = [
        feed_layer(
            split,
            here,
            attended[crop],
            block_rows(tokens)[crop],
            block_rows(cotangent)[crop],
            block_rows(normed_a.reshape(tokens.shape))[crop],
            mod_rows[crop],
            gate_weight,
            output_weight,
            feed_gate,
            feed_up,
            feed_down,
        )
        for crop in range(crop_count)
    ]
    layer_out, grad_middle, grad_attended, grad_gate_pre, feed_sums = (
        jnp.stack([result[place] for result in per_crop_results]) for place in range(5)
    )
    layer_out, grad_middle = layer_out[:, :row_count], grad_middle[:, :row_count]
    grad_gate_pre = grad_gate_pre[:, :row_count].reshape(token_count, model_width)
    weight_grads = [
        sum(result[place].astype(jnp.float32) for result in per_crop_results).astype(jnp.bfloat16)
        if crop_count > 1
        else per_crop_results[0][place]
        for place in range(5, len(per_crop_results[0]))
    ]

    def backward_of(first_pair, count, grad_now):
        return attention_backward(
            layout,
            score_scale,
            first_pair,
            count,
            block_rows(queries),
            grad_now,
            attended,
            logs,
            pieces,
            members,
            kinds,
            backward_bins,
            places,
            *turned,
            tables,
        )

    if split:
        arrivals = [swap_res(weight_grads[place]) for place in (0, 2, 4, 6)]
        kept = [weight_grads[place] for place in (1, 3, 5, 7)]
        half = model_width // 2
        inner = feed_gate.shape[1] // 2
        calls = [list(backward_of(0, 1, grad_attended))]
        arrivals, calls[0] = tie(arrivals, calls[0])
        gate_w, up_w, down_w, small_w = zip(kept, arrivals)
        halving = Halving(
            [
                [(gate_w, 0, inner), (small_w, 0, half)],
                [(up_w, 0, inner), (small_w, 1, half)],
                [(down_w, 0, half)],
            ],
            ["xyvu", "yvxu", "vxyu"],
        )
        arrived = []
        for first_pair, count in ((1, 3), (4, 2)):
            arrived.append(swap_res(calls[-1][2][0]))
            sent = halving.stage()
            sent, grad_attended = tie(sent, grad_attended)
            came = halving.send(sent)
            calls.append(list(backward_of(first_pair, count, grad_attended)))
            came, calls[-1], arrived[-1] = tie(came, calls[-1], arrived[-1])
            halving.take(came)
        index = lax.axis_index("crop")
        bf16 = jnp.bfloat16
        share = model_width // 16
        away = swap_res(calls[2][2][0])
        sent = halving.stage()
        sent, calls[2][1] = tie(sent, calls[2][1])
        came = halving.send(sent)
        joined, proj_send, proj_keep = projection_gradient(
            here,
            normed_a,
            [
                (calls[0][0][0], calls[0][1][0], arrived[0]),
                (calls[1][0][0], calls[1][1][0], arrived[1]),
                (calls[2][0][0], calls[2][1][0], away),
            ],
        )
        came, proj_send, proj_keep = tie(came, proj_send, proj_keep)
        proj_came = swap_res(proj_send)
        halving.take(came)
        sent = halving.stage()
        sent, proj_came = tie(sent, proj_came)
        came = halving.send(sent)
        mine, *fan = local_call(
            fan_first_kernel,
            scalars(index % 4),
            [proj_keep, proj_came],
            [((4 * share, PACK), bf16)] * 4,
            "fan_first",
        )
        fan, joined = tie(fan, joined)
        fan_came = [exchange(value, mask + 1) for mask, value in enumerate(fan)]
        extra = jnp.concatenate(
            [
                pad_to(features.astype(jnp.float32), 1, SIDE, 0.0),
                jnp.concatenate(
                    [condition, pad_to(cath_ids.astype(jnp.float32)[:, None], 1, LANES, 0.0)], axis=1
                ),
            ],
            axis=0,
        )
        tokens_grad, pack = finish_layer(
            joined,
            projection_weight,
            grad_gate_pre,
            gate_weight,
            tokens[0],
            grad_middle[0],
            mod_rows[0],
            feed_sums[0],
            jnp.pad(extra, ((4, 2), (0, 0))),
            [call[-1][0] for call in calls],
        )
        tokens_grad = tokens_grad[None]
        came, pack = tie(came, pack)
        packs = [pack] + [exchange(pack, mask + 1) for mask in range(3)]
        halving.take(came)
        finals = halving.stage(last=True)
        feed_gate_grad, output_weight_grad, feed_up_grad, gate_weight_grad, feed_down_grad = finals
        packs, finals = tie(packs, finals)
        (packs,) = local_call(join_packs_kernel, scalars(0), packs, [((32, PACK), bf16)], "join_packs")
        far_packs = exchange(packs, MASKS["v"])
        packs, fan_came, far_packs = tie(packs, fan_came, far_packs)
        sent, mine = local_call(
            fan_v_kernel,
            scalars((index // 4) % 2),
            [mine, *fan_came],
            [((2 * share, PACK), bf16), ((2 * share, PACK), bf16)],
            "fan_v",
        )
        packs = jnp.concatenate([packs, far_packs], axis=0)
        sent, packs = tie(sent, packs)
        came = exchange(sent, MASKS["v"])
        far_packs = exchange(packs, MASKS["u"])
        came, far_packs = tie(came, far_packs)
        packs = jnp.concatenate([packs, far_packs], axis=0)
        sent, mine = local_call(
            fan_u_kernel,
            scalars(index // 8),
            [mine, came],
            [((share, PACK), bf16), ((share, PACK), bf16)],
            "fan_u",
        )
        sent, packs = tie(sent, packs)
        came = exchange(sent, MASKS["u"])
        (
            modulation_weight_grad,
            time_weight_grad,
            label_table_grad,
            relative_table_grad,
            pair_gain_grad,
            pair_weight_grad,
        ) = small_gradients(
            head_count, label_count, packs, swap_res(packs), modulation_weight, *small_operands
        )
        pair_weight_grad = pair_weight_grad.T
        came, pair_weight_grad = tie(came, pair_weight_grad)
        projection_weight_grad = add_low(mine, came, jnp.float32)
        pair_gain_grad = pair_gain_grad[0]
    else:
        results = backward_of(0, pairs, grad_attended)
        grad_table = results[-1]
        grad_pairs = results[1:-1]
        if len(grad_pairs) == 2:
            total, away = grad_pairs[0].astype(jnp.float32), grad_pairs[1]
        else:
            total = grad_pairs[0][:, :, :row_count].astype(jnp.float32)
            away = grad_pairs[0][:, :, row_count:]
        for step in range(1, res_parts):
            sent = away[:, :, (step - 1) * row_count : step * row_count]
            pairs_to = [(r, (r + step) % res_parts) for r in range(res_parts)]
            total = total + lax.ppermute(sent, "res", pairs_to).astype(jnp.float32)
        total = total.astype(jnp.bfloat16)
        grad_projected = jnp.concatenate(
            [results[0][:, :row_count], total[:, 0], total[:, 1]], axis=-1
        ).reshape(token_count, 3 * model_width)
        grad_normed_a = against_columns(grad_projected, projection_weight) + against_columns(
            grad_gate_pre, gate_weight
        )
        norm_back_a = jax.vjp(modulate, token_values, shift_a, scale_a)[1]
        grad_tokens, grad_shift_a, grad_scale_a = norm_back_a(
            grad_normed_a.reshape(crop_count, row_count, model_width)
        )
        tokens_grad = (grad_middle + grad_tokens).astype(jnp.bfloat16)
        feed_gate_grad, feed_up_grad, feed_down_grad = (
            scatter_crops(share_columns(value, res_parts)) for value in weight_grads[:3]
        )
        output_weight_grad, gate_weight_grad = (
            scatter_crops(share_columns(value, res_parts))
            for value in (weight_grads[3][:, :model_width], weight_grads[3][:, model_width:])
        )
        projection_weight_grad = scatter_crops(
            share_columns(across_rows(normed_a, grad_projected), res_parts)
        )
        grad_table = grad_table[:, :, :2].sum(0).reshape(head_count, LANES)

        grad_modulation = jnp.concatenate([grad_shift_a, grad_scale_a, feed_sums[:, 2:6]], axis=1)
        grad_modulation = grad_modulation.reshape(crop_count, 6 * model_width)
        table_row = grad_table.reshape(1, head_count * LANES)
        first_row = (jnp.arange(crop_count) == 0).astype(jnp.float32)[:, None]
        small_here = jnp.concatenate([grad_modulation, first_row * table_row], axis=1)
        levels_here = jnp.stack([time_levels, cath_ids.astype(jnp.float32)], axis=1)
        levels_here = pad_to(levels_here, 1, LANES, 0.0)
        small_all = gather_crops(
            jnp.concatenate([levels_here, sum_res(small_here, res_parts)], axis=1), crop_parts
        )
        levels_all, small_all = small_all[:, :2], small_all[:, LANES:]
        grad_modulation = small_all[:, : 6 * model_width]
        grad_table = jnp.sum(small_all[:, 6 * model_width :], axis=0).reshape(head_count, LANES)
        grad_table = grad_table[:, :bin_count]
        features_all = time_features(levels_all[:, 0], time_weight.shape[0]).astype(jnp.bfloat16)
        onehot_all = (
            levels_all[:, 1].astype(jnp.int32)[:, None]
            == jnp.arange(label_count, dtype=jnp.int32)[None, :]
        ).astype(jnp.bfloat16)
        condition = conditioning(features_all, onehot_all)
        cond_act = jax.nn.silu(condition).astype(jnp.bfloat16)
        modulation_weight_grad = split_left(cond_act, grad_modulation, 0, 0)
        grad_condition = split_left(modulation_weight, grad_modulation, 1, 1).T * silu_slope(condition)
        time_weight_grad = split_left(features_all, grad_condition, 0, 0)
        label_table_grad = split_left(onehot_all, grad_condition, 0, 0)
        pair_weight_grad = split_left(pair_norm, grad_table, 0, 1)
        grad_pair_norm = split_right(grad_table, pair_weight, 0, 1)
        pair_back = jax.vjp(normalize_rows, relative_values, gain_values)[1]
        relative_table_grad, pair_gain_grad = pair_back(grad_pair_norm)
    return (
        layer_out,
        tokens_grad,
        time_weight_grad,
        label_table_grad,
        modulation_weight_grad,
        projection_weight_grad,
        gate_weight_grad,
        output_weight_grad,
        relative_table_grad,
        pair_gain_grad,
        pair_weight_grad,
        feed_gate_grad,
        feed_up_grad,
        feed_down_grad,
    )


def solution(mesh):
    return jax.shard_map(
        functools.partial(per_device, mesh.shape["crop"], mesh.shape["res"]),
        mesh=mesh,
        in_specs=(
            P("crop", "res", None),
            P("crop", "res", None),
            P("crop"),
            P("crop"),
            P("crop", None),
            P("crop", None),
            P(),
            P(),
            P(),
            P(),
            P(),
            P(),
            P(),
            P(),
            P(),
            P(),
            P(),
            P(),
        ),
        out_specs=(
            P("crop", "res", None),
            P("crop", "res", None),
            P(),
            P(),
            P(),
            P("crop", "res"),
            P("crop", "res"),
            P("crop", "res"),
            P(),
            P(),
            P(),
            P("crop", "res"),
            P("crop", "res"),
            P("crop", "res"),
        ),
        check_vma=False,
    )
```

```python
import functools
import itertools
import math

import jax
import jax.numpy as jnp
from jax import lax
from jax.experimental import pallas as pl
from jax.experimental.pallas import tpu as pltpu
from jax.sharding import PartitionSpec as P

LANES = 128
NEAR = 31
VMEM_BYTES = 56 * 1024 * 1024
LOG2E = 1.4426950408889634
NONE, RIGHT, LEFT, APART = 0, 1, 2, 3


def layer_norm(inputs):
    mean_value = jnp.mean(inputs, axis=-1, keepdims=True)
    centred = inputs - mean_value
    spread = jnp.mean(centred * centred, axis=-1, keepdims=True)
    return centred * lax.rsqrt(spread + 1e-06)


def modulate(inputs, shift_row, scale_row):
    return layer_norm(inputs) * (1.0 + scale_row) + shift_row


def normalize_rows(table_rows, gain_row):
    return layer_norm(table_rows) * gain_row


def time_features(time_levels, feature_width):
    half_width = feature_width // 2
    frequency = jnp.exp(-math.log(10000.0) * jnp.arange(half_width, dtype=jnp.float32) / half_width)
    angles = 1000.0 * time_levels[:, None] * frequency[None, :]
    return jnp.concatenate([jnp.sin(angles), jnp.cos(angles)], axis=-1)


def across_rows(former, latter):
    return lax.dot_general(
        former, latter, (((0,), (0,)), ((), ())), preferred_element_type=jnp.float32
    )


def against_columns(former, latter):
    return lax.dot_general(
        former, latter, (((1,), (1,)), ((), ())), preferred_element_type=jnp.float32
    )


def split_parts(values):
    upper = lax.reduce_precision(values, 8, 7)
    return (upper.astype(jnp.bfloat16), (values - upper).astype(jnp.bfloat16))


def split_left(narrow, values, former_dim, latter_dim):
    upper, rest = split_parts(values)
    numbers = (((former_dim,), (latter_dim,)), ((), ()))
    return lax.dot_general(
        narrow, upper, numbers, preferred_element_type=jnp.float32
    ) + lax.dot_general(narrow, rest, numbers, preferred_element_type=jnp.float32)


def split_right(values, narrow, former_dim, latter_dim):
    upper, rest = split_parts(values)
    numbers = (((former_dim,), (latter_dim,)), ((), ()))
    return lax.dot_general(
        upper, narrow, numbers, preferred_element_type=jnp.float32
    ) + lax.dot_general(rest, narrow, numbers, preferred_element_type=jnp.float32)


def sigmoid_slope(inputs):
    gate_value = jax.nn.sigmoid(inputs)
    return gate_value * (1.0 - gate_value)


def silu_slope(inputs):
    gate_value = jax.nn.sigmoid(inputs)
    return gate_value * (1.0 + inputs * (1.0 - gate_value))


class Layout:
    def __init__(self, rows, length):
        self.rows = rows
        self.length = length
        self.query_tiles = -(-rows // LANES)
        self.key_tiles = -(-length // LANES)
        self.padded = self.query_tiles * LANES
        self.wide = self.key_tiles * LANES
        self.last = self.key_tiles - 1
        self.groups = (self.query_tiles + 4) * 4
        assert 2 * self.groups + 3 <= LANES and self.groups <= 64
        assert rows - 1 + NEAR < self.padded and length - NEAR >= self.last * LANES
        assert rows % 8 == 0 and self.last > self.query_tiles
        self.block_rows = rows if rows % 16 == 0 else self.padded
        self.pieces = [rows, length - rows] if rows % 16 == 0 else [length]

    def tile_start(self, tile):
        return self.last * LANES if tile < 0 else tile * LANES


def pad_to(values, axis, size, fill):
    widths = [(0, 0)] * values.ndim
    widths[axis] = (0, size - values.shape[axis])
    return jnp.pad(values, widths, constant_values=fill)


def tables_kernel(layout, bin_count, start_ref, pairs_ref, *out_refs):
    members_ref, kinds_ref, forward_ref, backward_ref, places_ref = out_refs[:5]
    members_turned, kinds_turned, codes = out_refs[5:]
    rows, length, queries, groups = layout.rows, layout.length, layout.query_tiles, layout.groups
    wrap = length - start_ref[0]
    reach = (bin_count - 2) // 2
    zero_bin = LANES - 1
    shape = (LANES, LANES)
    lane = lax.broadcasted_iota(jnp.int32, shape, 1)
    row = lax.broadcasted_iota(jnp.int32, shape, 0)
    last_start = layout.last * LANES

    tiles = pairs_ref.shape[1]
    marks = pairs_ref[1].astype(jnp.float32)
    place = lax.broadcasted_iota(jnp.int32, marks.shape, 0) * LANES + lax.broadcasted_iota(
        jnp.int32, marks.shape, 1
    )
    before = jnp.sum(jnp.where(place < wrap, marks, 0.0), keepdims=True)
    every = jnp.sum(marks, keepdims=True)
    triangle = jnp.where(row <= lane, 1.0, 0.0).astype(jnp.bfloat16)
    running = jnp.dot(marks.astype(jnp.bfloat16), triangle, preferred_element_type=jnp.float32)
    numbers, chains = [], []
    carry = jnp.zeros((1, 1), jnp.float32)
    for tile in range(layout.key_tiles):
        count = running[tile : tile + 1] + carry
        carry = carry + running[tile : tile + 1, LANES - 1 :]
        count = count + jnp.where(place[tile : tile + 1] < wrap, every - before, -before)
        chains.append(jnp.broadcast_to(count.astype(jnp.int32), shape))
        numbers.append(jnp.broadcast_to(pairs_ref[0, tile : tile + 1], shape))
    number_rows = [value.T for value in numbers]
    chain_rows = [value.T for value in chains]

    def bins_of(key_number, key_chain, query_number, query_chain):
        offset = jnp.clip(key_number - query_number, -reach, reach) + reach
        return jnp.where(key_chain == query_chain, offset, bin_count - 1)

    def touches(query, tile):
        begin = -LANES if tile < 0 else tile * LANES
        return (begin <= query + NEAR) & (query - NEAR <= begin + LANES - 1)

    for tile in range(layout.key_tiles):
        size = min(LANES, length - tile * LANES)
        key = tile * LANES + row
        if tile == layout.last:
            other = jnp.full(shape, queries + 3, jnp.int32)
        elif tile == queries - 1:
            other = jnp.full(shape, queries, jnp.int32)
        else:
            other = jnp.where(key < wrap, queries + 1, queries + 2)
        group = jnp.where(key < rows, tile, other)
        slot = group * 4 + chain_rows[tile] - 1
        hit = (lane == slot) | (lane == slot + groups)
        tail = (lane >= 2 * groups) & (lane < 2 * groups + 3)
        values = jnp.where(hit, 1.0, jnp.where(tail, -1.0, 0.0)).astype(jnp.bfloat16)
        members_ref[tile * LANES : tile * LANES + size] = values[:size]
        turned = jnp.where(hit & (lane < groups), 1.0, 0.0).T
        members_turned[:, tile * LANES : tile * LANES + size] = turned[:64, :size].astype(jnp.bfloat16)

    local = jnp.where(lane >= groups, lane - groups, lane)
    lane_group = local >> 2
    lane_chain = (local & 3) + 1
    lane_begin = jnp.where(
        lane_group < queries,
        lane_group * LANES,
        jnp.where(lane_group == queries, (queries - 1) * LANES, -LANES),
    )
    has_band = (lane_group <= queries) | (lane_group == queries + 3)
    other_right = jnp.where(
        lane_group == queries,
        rows,
        jnp.where(
            lane_group == queries + 3,
            last_start,
            jnp.where(lane_group == queries + 1, 0, 2 * length),
        ),
    )
    right_limit = jnp.where(lane_group > queries, jnp.where(lane_group == queries + 3, wrap, length), wrap)
    for tile in range(queries):
        size = min(LANES, layout.block_rows - tile * LANES)
        query = tile * LANES + row
        near = (lane_begin <= query + NEAR) & (query - NEAR <= lane_begin + LANES - 1) & has_band
        right = jnp.where(lane_group < queries, lane_group - tile, right_limit - other_right) > 0
        same = chain_rows[tile] == lane_chain
        kinds = jnp.where(same, jnp.where(near, NONE, jnp.where(right, RIGHT, LEFT)), APART)
        kinds = jnp.where((lane < 2 * groups) & (query < rows), kinds, NONE)
        kinds_ref[tile * LANES : tile * LANES + size] = kinds[:size]
        kinds_turned[:, tile * LANES : (tile + 1) * LANES] = jnp.where(lane < groups, kinds, NONE).T[:64]
        for step in range(3):
            near_tile = tile + step - 1
            index = layout.last if near_tile < 0 else near_tile
            if near_tile < queries:
                inside = touches(query, near_tile) & (query < rows)
                inside &= lane < length - index * LANES
                found = bins_of(
                    numbers[index], chains[index], number_rows[tile], chain_rows[tile]
                )
                found = jnp.where(inside, found, zero_bin)
            else:
                found = jnp.full(shape, zero_bin, jnp.int32)
            forward_ref[
                tile * LANES : (tile + 1) * LANES, step * LANES : (step + 1) * LANES
            ] = found

    codes[...] = jnp.full(codes.shape, -1, jnp.int32)
    for tile in range(queries):
        size = min(LANES, rows - tile * LANES)
        code = number_rows[tile] * 8 + chain_rows[tile]
        codes[(tile + 1) * LANES : (tile + 1) * LANES + size] = code[:size]

    for index, tile in enumerate(list(range(queries)) + [-1]):
        source = layout.last if tile < 0 else tile
        key_row = (row - (length - last_start)) if tile < 0 else tile * LANES + row
        present = row < length - source * LANES
        for step in range(3):
            near_tile = tile + step - 1
            if 0 <= near_tile < queries:
                near_query = near_tile * LANES + lane
                inside = touches(near_query, tile) & (near_query < rows) & present
                found = bins_of(
                    number_rows[source], chain_rows[source], numbers[near_tile], chains[near_tile]
                )
                found = jnp.where(inside, found, zero_bin)
            else:
                found = jnp.full(shape, zero_bin, jnp.int32)
            backward_ref[
                index * LANES : (index + 1) * LANES, step * LANES : (step + 1) * LANES
            ] = found
        target = (number_rows[source] + reach - lane) * 8 + chain_rows[source]
        target = jnp.where(present & (lane > 0) & (lane < 2 * reach), target, -9)
        offset = (LANES - (length - last_start)) if tile < 0 else (tile + 1) * LANES
        far = 4 * LANES
        shift = jnp.full(shape, far, jnp.int32)
        for distance in range(-NEAR, NEAR + 1):
            other = codes[offset - distance : offset - distance + LANES]
            shift = jnp.where(other == target, distance, shift)
        if tile < 0:
            base = jnp.zeros(shape, jnp.int32)
        else:
            base = jnp.where(row < LANES // 2, tile - 1, tile) * LANES
        places_ref[index * LANES : (index + 1) * LANES] = jnp.where(
            shift == far, far - 1, key_row - shift - base
        )


def attention_tables(layout, numbers, marks, query_start, bin_count):
    crops = numbers.shape[0]
    pairs = jnp.stack([numbers, marks], axis=1)
    pairs = pad_to(pairs, 2, layout.wide, 0).reshape(crops, 2, layout.key_tiles, LANES)
    spots = (layout.query_tiles + 1) * LANES
    shapes = [
        ((layout.length, LANES), jnp.bfloat16),
        ((layout.block_rows, LANES), jnp.int32),
        ((layout.padded, 3 * LANES), jnp.int32),
        ((spots, 3 * LANES), jnp.int32),
        ((spots, LANES), jnp.int32),
        ((64, layout.length), jnp.bfloat16),
        ((64, layout.padded), jnp.int32),
    ]
    return pl.pallas_call(
        functools.partial(tables_kernel, layout, bin_count),
        grid=(crops,),
        in_specs=[
            pl.BlockSpec(memory_space=pltpu.SMEM),
            pl.BlockSpec((None, 2, layout.key_tiles, LANES), lambda crop: (crop, 0, 0, 0)),
        ],
        out_specs=tuple(pl.BlockSpec((None, *shape), lambda crop: (crop, 0, 0)) for shape, _ in shapes),
        out_shape=tuple(jax.ShapeDtypeStruct((crops, *shape), kind) for shape, kind in shapes),
        scratch_shapes=[pltpu.VMEM((layout.padded + 2 * LANES, LANES), jnp.int32)],
        compiler_params=pltpu.CompilerParams(vmem_limit_bytes=VMEM_BYTES),
        cost_estimate=pl.CostEstimate(
            flops=40000000 * crops, bytes_accessed=4000000 * crops, transcendentals=0
        ),
        name="pair_tables",
    )(jnp.reshape(query_start, (1,)).astype(jnp.int32), pairs)


def head_tables(layout, bias_rows, scale):
    bin_count, heads = bias_rows.shape
    table = (bias_rows - bias_rows[bin_count - 1 :]).T / scale
    lane = jnp.arange(LANES, dtype=jnp.int32)
    groups = layout.groups

    def columns(values):
        upper = lax.reduce_precision(values, 8, 7)
        rest = values - upper
        return jnp.where(
            lane < groups, upper[:, None], jnp.where(lane < 2 * groups, rest[:, None], 0.0)
        )

    lookup = pad_to(table, 1, LANES, 0.0)
    stacked = jnp.stack([lookup, columns(table[:, bin_count - 2]), columns(table[:, 0])], 1)
    stacked = pad_to(stacked, 1, 8, 0.0)
    return stacked.reshape(heads // 2, 16, LANES)


NT = (((1,), (1,)), ((), ()))
TN = (((0,), (0,)), ((), ()))


def wide_dot(former, latter, numbers=(((1,), (0,)), ((), ()))):
    return lax.dot_general(former, latter, numbers, preferred_element_type=jnp.float32)


def look_up(table_row, bins):
    table = jnp.broadcast_to(table_row, bins.shape)
    return jnp.take_along_axis(table, bins, axis=1, mode="promise_in_bounds")


def half_of(values, lane, side):
    return jnp.where((lane >= 64) == (side == 1), values, jnp.zeros_like(values))


def row_blocks(total, size):
    return [(start, min(start + size, total)) for start in range(0, total, size)]


def group_columns(kinds, tables, side):
    right = tables[8 * side + 1 : 8 * side + 2]
    left = tables[8 * side + 2 : 8 * side + 3]
    return jnp.where(kinds == RIGHT, right, jnp.where(kinds == LEFT, left, 0.0))


def forward_kernel(layout, scale, *refs):
    count = len(layout.pieces)
    query_ref = refs[0]
    key_refs = refs[1 : 1 + count]
    value_refs = refs[1 + count : 1 + 2 * count]
    members_ref, kinds_ref, bins_ref, tables_ref, out_ref, log_ref = refs[1 + 2 * count : -3]
    all_scores, all_weights, tops = refs[-3:]
    pair = pl.program_id(1)
    rows, length = layout.block_rows, layout.length
    turn = 0
    factor = scale * LOG2E
    lane = lax.broadcasted_iota(jnp.int32, (1, LANES), 1)
    query = query_ref[...]
    keys = jnp.concatenate([ref[...] for ref in key_refs], axis=0)
    values = jnp.concatenate([ref[...] for ref in value_refs], axis=0)
    members = members_ref[...]
    kinds = kinds_ref[...]
    tables = tables_ref[...]
    ones = jnp.ones((length, LANES), jnp.bfloat16)

    @pl.when(pair == 0)
    def _():
        log_ref[...] = jnp.zeros_like(log_ref)

    for side in range(2):
        key_columns = jnp.concatenate([half_of(keys, lane, side), members], axis=1)
        value_columns = jnp.concatenate([half_of(values, lane, side), ones], axis=1)
        extra = group_columns(kinds, tables, side).astype(jnp.bfloat16)
        query_columns = jnp.concatenate([query, extra], axis=1)
        table_row = tables[8 * side : 8 * side + 1]
        for start, stop in row_blocks(rows, 256):
            size = stop - start
            scores = all_scores.at[turn % 2]
            turn += 1
            scores[0:size, 0:length] = wide_dot(query_columns[start:stop], key_columns, NT)
            for tile in range(start // LANES, -(-stop // LANES)):
                first, final = tile * LANES, min(tile * LANES + LANES, rows)
                for slot in range(3):
                    other = tile + slot - 1
                    if other >= layout.query_tiles:
                        continue
                    low, high = first, final
                    if slot == 0:
                        high = min(first + 32, final)
                    if slot == 2:
                        low = first + LANES - 32
                    if low >= high:
                        continue
                    place = layout.tile_start(other)
                    width = min(LANES, length - place)
                    bins = bins_ref[low:high, slot * LANES : (slot + 1) * LANES]
                    bias = look_up(table_row, bins)[:, :width]
                    scores[low - start : high - start, place : place + width] += bias
            weights = all_weights.at[turn % 2]
            for strip in range(0, size, 16):
                rows_now = slice(strip, strip + 16)
                block = scores[rows_now, 0:length]
                top = jnp.max(block, axis=1, keepdims=True)
                weights[rows_now, 0:length] = jnp.exp2((block - top) * factor).astype(jnp.bfloat16)
                tops[rows_now] = jnp.broadcast_to(top, (16, LANES))
            sums = wide_dot(weights[0:size, 0:length], value_columns)
            total = sums[:, LANES:]
            result = sums[:, :LANES] / total
            if side == 0:
                out_ref[start:stop] = result
            else:
                out_ref[start:stop] += result
            log_total = tops[0:size] + jnp.log(total) * (1.0 / scale)
            log_ref[start:stop] = jnp.where(
                lane == 2 * pair + side, log_total, log_ref[start:stop]
            )


def backward_kernel(layout, scale, first_pair, *refs):
    count = len(layout.pieces)
    query_ref, grad_ref, out_ref, log_ref = refs[:4]
    key_refs = refs[4 : 4 + count]
    value_refs = refs[4 + count : 4 + 2 * count]
    rest = refs[4 + 2 * count :]
    members_ref, kinds_ref, bins_ref, places_ref, tables_ref = rest[:5]
    members_turned_ref, kinds_turned_ref = rest[5:7]
    grad_query_ref = rest[7]
    grad_pair_refs = rest[8 : 8 + count]
    grad_table_ref = rest[8 + count]
    query_wide, grad_wide, query_turned, grad_turned = rest[9 + count : 13 + count]
    all_scores, all_slopes, slopes_low, probs_low = rest[13 + count :]
    pair = pl.program_id(1) + first_pair
    rows, length, padded = layout.block_rows, layout.length, layout.padded
    factor = scale * LOG2E
    lane = lax.broadcasted_iota(jnp.int32, (1, LANES), 1)
    keys = jnp.concatenate([ref[...] for ref in key_refs], axis=0)
    values = jnp.concatenate([ref[...] for ref in value_refs], axis=0)
    members = members_ref[...]
    kinds = kinds_ref[...]
    tables = tables_ref[...]
    query = query_ref[...]
    grad = grad_ref[...]
    grad_full = grad.astype(jnp.float32)
    product = grad_full * out_ref[...]
    log_all = log_ref[...]
    tail = 2 * layout.groups
    ones = jnp.broadcast_to(jnp.where(lane < 3, 1.0, 0.0), (length, LANES)).astype(jnp.bfloat16)

    def three_parts(values):
        upper = values.astype(jnp.bfloat16).astype(jnp.float32)
        values = values - upper
        middle = values.astype(jnp.bfloat16).astype(jnp.float32)
        return upper, middle, values - middle

    def in_lanes(parts, first):
        return jnp.where(
            lane == first,
            parts[0],
            jnp.where(lane == first + 1, parts[1], jnp.where(lane == first + 2, parts[2], 0.0)),
        )

    if padded > rows:
        for ref in (query_wide, grad_wide):
            for side in range(2):
                ref[side, rows:padded] = jnp.zeros((padded - rows, ref.shape[2]), jnp.bfloat16)
        for ref in (query_turned, grad_turned):
            ref[:, rows:padded] = jnp.zeros((LANES, padded - rows), jnp.bfloat16)
    query_turned[:, 0:rows] = query.T
    grad_turned[:, 0:rows] = grad.T
    for side in range(2):
        log_total = jnp.sum(
            jnp.where(lane == 2 * pair + side, log_all, 0.0), axis=1, keepdims=True
        )
        extra = group_columns(kinds, tables, side) + in_lanes(three_parts(log_total), tail)
        query_wide[side, 0:rows, 0:LANES] = query
        query_wide[side, 0:rows, LANES:] = extra.astype(jnp.bfloat16)
        delta = jnp.sum(half_of(product, lane, side), axis=1, keepdims=True)
        grad_wide[side, 0:rows, 0:LANES] = grad
        grad_wide[side, 0:rows, LANES:] = in_lanes(three_parts(-delta), 0).astype(jnp.bfloat16)

    key_columns = [
        jnp.concatenate([half_of(keys, lane, side), members], axis=1) for side in range(2)
    ]
    value_columns = [
        jnp.concatenate([half_of(values, lane, side), ones], axis=1) for side in range(2)
    ]
    inner_sums = [jnp.zeros((1, LANES), jnp.float32) for _ in range(2)]
    low_sums = [jnp.zeros((1, LANES), jnp.float32) for _ in range(2)]
    high_sums = [jnp.zeros((1, LANES), jnp.float32) for _ in range(2)]
    reach_tiles = list(range(layout.query_tiles)) + [-1]

    def put(which, start, stop, result):
        begin = 0
        for ref, size in zip(grad_pair_refs, layout.pieces):
            low, high = max(start, begin), min(stop, begin + size)
            if low < high:
                ref[which, low - begin : high - begin] = result[low - start : high - start]
            begin += size

    for start, stop in row_blocks(length, 384):
        size = stop - start
        for side in range(2):
            table_row = tables[8 * side : 8 * side + 1]
            scores, slopes = all_scores.at[side], all_slopes.at[side]
            scores[0:size] = wide_dot(key_columns[side][start:stop], query_wide[side], NT)
            near = []
            for index, tile in enumerate(reach_tiles):
                place = layout.tile_start(tile)
                if start <= place < stop:
                    near.append((index, tile, place, min(place + LANES, length)))
            for index, tile, place, final in near:
                for slot in range(3):
                    other = tile + slot - 1
                    if not 0 <= other < layout.query_tiles:
                        continue
                    bins = bins_ref[
                        index * LANES : index * LANES + final - place,
                        slot * LANES : (slot + 1) * LANES,
                    ]
                    scores[
                        place - start : final - start, other * LANES : (other + 1) * LANES
                    ] += look_up(table_row, bins)
            slopes[0:size] = wide_dot(value_columns[side][start:stop], grad_wide[side], NT)
            for strip in range(0, size, 16):
                rows_now = slice(strip, strip + 16)
                rows_all = slice(start + strip, start + strip + 16)
                probs = jnp.exp2(scores[rows_now] * factor)
                probs_low[side, rows_all] = probs.astype(jnp.bfloat16)
                slopes_low[side, rows_all] = (probs * slopes[rows_now]).astype(jnp.bfloat16)
            for index, tile, place, final in near:
                for slot in range(3):
                    other = tile + slot - 1
                    if not 0 <= other < layout.query_tiles:
                        continue
                    bins = bins_ref[
                        index * LANES : index * LANES + final - place,
                        slot * LANES : (slot + 1) * LANES,
                    ]
                    cut = slopes_low[side, place:final, other * LANES : (other + 1) * LANES].astype(
                        jnp.float32
                    )
                    low_sums[side] += jnp.sum(
                        jnp.where(bins == 0, cut, 0.0), axis=0, keepdims=True
                    )
                    high_sums[side] += jnp.sum(
                        jnp.where(bins == 2 * (NEAR + 1), cut, 0.0), axis=0, keepdims=True
                    )
                for half in range(2):
                    begin, end = half * 64, min(half * 64 + 64, final - place)
                    if begin >= end:
                        continue
                    base = 0 if tile < 0 else tile - 1 + half
                    where = places_ref[index * LANES + begin : index * LANES + end]
                    spot = where & (LANES - 1)
                    for step in range(2):
                        other = base + step
                        if not 0 <= other < layout.query_tiles or (tile < 0 and step):
                            continue
                        cut = slopes_low[
                            side, place + begin : place + end, other * LANES : (other + 1) * LANES
                        ].astype(jnp.float32)
                        picked = jnp.take_along_axis(cut, spot, axis=1, mode="promise_in_bounds")
                        picked = jnp.where((where >> 7) == step, picked, 0.0)
                        inner_sums[side] += jnp.sum(picked, axis=0, keepdims=True)

    keys_turned = keys.T
    grad_keys, grad_values, grad_queries = [], [], []
    kinds_turned = kinds_turned_ref[...]
    for side in range(2):
        cut = slice(64 * side, 64 * side + 64)
        grad_values.append(wide_dot(grad_turned[cut], probs_low[side], NT))
        grad_keys.append(wide_dot(query_turned[cut], slopes_low[side], NT))
        left = jnp.concatenate([keys_turned[cut], members_turned_ref[...]], axis=0)
        both = wide_dot(left, slopes_low[side])
        grad_queries.append(both[:64])
        sums = both[64:]

        def total(kind):
            return jnp.sum(jnp.where(kinds_turned == kind, sums, 0.0))

        right = total(RIGHT) + jnp.sum(high_sums[side])
        left = total(LEFT) + jnp.sum(low_sums[side])
        apart = total(APART)
        grad_table_ref[side : side + 1] = jnp.where(
            lane == 0,
            left,
            jnp.where(
                lane == 2 * (NEAR + 1),
                right,
                jnp.where(lane == 2 * (NEAR + 1) + 1, apart, inner_sums[side]),
            ),
        )
    put(0, 0, length, (jnp.concatenate(grad_keys, axis=0) * scale).T.astype(jnp.bfloat16))
    put(1, 0, length, jnp.concatenate(grad_values, axis=0).T.astype(jnp.bfloat16))
    turned = jnp.concatenate(grad_queries, axis=0) * scale
    grad_query_ref[...] = turned.T[0:rows].astype(jnp.bfloat16)


def tile_columns(rows, offset=0):
    return pl.BlockSpec((None, rows, LANES), lambda crop, pair: (crop, 0, pair + offset))


def per_crop(rows, width):
    return pl.BlockSpec((None, rows, width), lambda crop, pair: (crop, 0, 0))


def kernel_params():
    return pltpu.CompilerParams(
        vmem_limit_bytes=VMEM_BYTES, dimension_semantics=("arbitrary", "arbitrary")
    )


def attention_forward(layout, scale, projected, key_values, members, kinds, bins, tables):
    crops, rows, _ = projected.shape
    pairs = tables.shape[0]
    specs = [tile_columns(rows)]
    operands = [projected]
    for place in (1, 2):
        for piece in key_values:
            specs.append(tile_columns(piece[0].shape[1], piece[place]))
            operands.append(piece[0])
    specs += [
        per_crop(layout.length, LANES),
        per_crop(rows, LANES),
        per_crop(layout.padded, 3 * LANES),
        pl.BlockSpec((None, 16, LANES), lambda crop, pair: (pair, 0, 0)),
    ]
    flops = 2 * crops * pairs * 2 * rows * layout.length * 256 * 2
    return pl.pallas_call(
        functools.partial(forward_kernel, layout, scale),
        grid=(crops, pairs),
        in_specs=specs,
        out_specs=(tile_columns(rows), per_crop(rows, LANES)),
        out_shape=(
            jax.ShapeDtypeStruct((crops, rows, pairs * LANES), jnp.float32),
            jax.ShapeDtypeStruct((crops, rows, LANES), jnp.float32),
        ),
        scratch_shapes=[
            pltpu.VMEM((2, 256, layout.wide), jnp.float32),
            pltpu.VMEM((2, 256, layout.wide), jnp.bfloat16),
            pltpu.VMEM((256, LANES), jnp.float32),
        ],
        compiler_params=kernel_params(),
        cost_estimate=pl.CostEstimate(
            flops=flops,
            bytes_accessed=12 * crops * rows * pairs * LANES,
            transcendentals=crops * pairs * 2 * rows * layout.length,
        ),
        name="attention_forward",
    )(*operands, members, kinds, bins, tables)


def attention_backward(
    layout,
    scale,
    first_pair,
    pairs,
    projected,
    grad_out,
    attended,
    logs,
    key_values,
    members,
    kinds,
    bins,
    places,
    members_turned,
    kinds_turned,
    tables,
):
    crops, rows, _ = projected.shape
    specs = [tile_columns(rows, first_pair)] * 3 + [per_crop(rows, LANES)]
    operands = [projected, grad_out, attended, logs]
    for place in (1, 2):
        for piece in key_values:
            specs.append(tile_columns(piece[0].shape[1], piece[place] + first_pair))
            operands.append(piece[0])
    specs += [
        per_crop(layout.length, LANES),
        per_crop(rows, LANES),
        per_crop(bins.shape[1], 3 * LANES),
        per_crop(places.shape[1], LANES),
        pl.BlockSpec((None, 16, LANES), lambda crop, pair: (pair + first_pair, 0, 0)),
        per_crop(64, layout.length),
        per_crop(64, layout.padded),
    ]
    out_specs = [tile_columns(rows)]
    out_shapes = [jax.ShapeDtypeStruct((crops, rows, pairs * LANES), jnp.bfloat16)]
    for piece in key_values:
        size = piece[0].shape[1]
        out_specs.append(
            pl.BlockSpec((None, 2, size, LANES), lambda crop, pair: (crop, 0, 0, pair))
        )
        out_shapes.append(jax.ShapeDtypeStruct((crops, 2, size, pairs * LANES), jnp.bfloat16))
    out_specs.append(pl.BlockSpec((None, None, 8, LANES), lambda crop, pair: (crop, pair, 0, 0)))
    out_shapes.append(jax.ShapeDtypeStruct((crops, pairs, 8, LANES), jnp.float32))
    padded, block = layout.padded, 384
    return pl.pallas_call(
        functools.partial(backward_kernel, layout, scale, first_pair),
        grid=(crops, pairs),
        in_specs=specs,
        out_specs=tuple(out_specs),
        out_shape=tuple(out_shapes),
        scratch_shapes=[
            pltpu.VMEM((2, padded, 2 * LANES), jnp.bfloat16),
            pltpu.VMEM((2, padded, 2 * LANES), jnp.bfloat16),
            pltpu.VMEM((LANES, padded), jnp.bfloat16),
            pltpu.VMEM((LANES, padded), jnp.bfloat16),
            pltpu.VMEM((2, block, padded), jnp.float32),
            pltpu.VMEM((2, block, padded), jnp.float32),
            pltpu.VMEM((2, layout.length, padded), jnp.bfloat16),
            pltpu.VMEM((2, layout.length, padded), jnp.bfloat16),
        ],
        compiler_params=kernel_params(),
        cost_estimate=pl.CostEstimate(
            flops=2 * crops * pairs * 2 * rows * layout.length * 256 * 5,
            bytes_accessed=20 * crops * rows * pairs * LANES,
            transcendentals=crops * pairs * 2 * rows * layout.length,
        ),
        name="attention_backward",
    )(*operands, members, kinds, bins, places, tables, members_turned, kinds_turned)


def sigmoid(values):
    return 0.5 * jnp.tanh(0.5 * values) + 0.5


def each_strip(rows, body, size=16):
    count = rows // size
    group = max(number for number in range(1, 9) if count % number == 0)

    @pl.loop(0, count // group)
    def _(index):
        for part in range(group):
            body(pl.ds(pl.multiple_of((index * group + part) * size, size), size))


def fold_rows(values):
    return jnp.sum(values.reshape(values.shape[0] // 8, 8, values.shape[1]), axis=0)


def feed_kernel(split, chunks, here_ref, *refs):
    (attended_ref, tokens_ref, upstream_ref, normed_a_ref, mod_ref, gate_weight_ref, output_ref) = refs[:7]
    gate_ref, up_ref, down_ref = refs[7:10]
    layer_ref, grad_middle_ref, grad_att_ref, grad_pre_ref, sums_ref = refs[10:15]
    grads = refs[15:-16]
    gated, grad_ff, normed, branch, middle, total, grad_normed, hidden, both, grad_branch = refs[-16:-6]
    gate_pre, turned, before, lifted, grad_hidden, folded = refs[-6:]
    step = pl.program_id(0)
    here = here_ref[0]
    rows, width = tokens_ref.shape
    size = gate_ref.shape[1]
    shift_f, scale_f = mod_ref[3:4], mod_ref[4:5]
    open_a, open_f = sigmoid(mod_ref[2:3]), sigmoid(mod_ref[5:6])

    def norm_of(values):
        mean_value = jnp.mean(values, axis=1, keepdims=True)
        centred = values - mean_value
        spread = jnp.mean(centred * centred, axis=1, keepdims=True)
        root = lax.rsqrt(spread + 1e-06)
        return centred * root, root

    @pl.when(step == 0)
    def _():
        gate_pre[...] = wide_dot(normed_a_ref[...], gate_weight_ref[...])

        def open_gates(cut):
            gated[cut] = (attended_ref[cut] * sigmoid(gate_pre[cut])).astype(jnp.bfloat16)
            grad_ff[cut] = (upstream_ref[cut].astype(jnp.float32) * open_f).astype(jnp.bfloat16)

        each_strip(rows, open_gates)
        branch[...] = wide_dot(gated[...], output_ref[...])

        def norm_in(cut):
            values = tokens_ref[cut].astype(jnp.float32) + open_a * branch[cut]
            middle[cut] = values
            normed[cut] = (norm_of(values)[0] * (1.0 + scale_f) + shift_f).astype(jnp.bfloat16)
            total[cut] = jnp.zeros((16, width), jnp.float32)
            grad_normed[cut] = jnp.zeros((16, width), jnp.float32)

        each_strip(rows, norm_in)
        turned[...] = normed[...].T

    block = rows if rows <= 384 else rows // 2
    for start in range(0, rows, block):
        cut = slice(start, start + block)
        before[cut] = wide_dot(normed[cut], gate_ref[...])
        lifted[cut] = wide_dot(normed[cut], up_ref[...])
        grad_hidden[cut] = wide_dot(grad_ff[cut], down_ref[...], NT)
        for first in range(start, start + block, 16):
            now = slice(first, first + 16)
            value, up, grad = before[now], lifted[now], grad_hidden[now]
            switch = sigmoid(value)
            silu = value * switch
            hidden[now] = (silu * up).astype(jnp.bfloat16)
            both[now, :size] = (grad * up * (switch + silu * (1.0 - switch))).astype(jnp.bfloat16)
            both[now, size:] = (grad * silu).astype(jnp.bfloat16)
        total[cut] += wide_dot(hidden[cut], down_ref[...])
        grad_normed[cut] += wide_dot(both[cut, :size], gate_ref[...], NT) + wide_dot(
            both[cut, size:], up_ref[...], NT
        )

    pair = wide_dot(turned[...], both[...]).astype(jnp.bfloat16)
    if split:
        gate_send, gate_keep, up_send, up_keep, down_send, down_keep, small_send, small_keep = grads
        half = width // 2
        away = pl.ds(pl.multiple_of((1 - here) * half, LANES), half)
        home = pl.ds(pl.multiple_of(here * half, LANES), half)
        down_send[...] = wide_dot(hidden[...], grad_ff[:, away], TN).astype(jnp.bfloat16)
        down_keep[...] = wide_dot(hidden[...], grad_ff[:, home], TN).astype(jnp.bfloat16)

        @pl.when(step < chunks // 2)
        def _():
            gate_send[...] = pair[:, :size]
            up_send[...] = pair[:, size:]

        @pl.when(step >= chunks // 2)
        def _():
            gate_keep[...] = pair[:, :size]
            up_keep[...] = pair[:, size:]
    else:
        gate_all, up_all, down_all, small_all = grads
        gate_all[...] = pair[:, :size]
        up_all[...] = pair[:, size:]
        down_all[...] = wide_dot(hidden[...], grad_ff[...], TN).astype(jnp.bfloat16)

    @pl.when(step == chunks - 1)
    def _():
        folded[...] = jnp.zeros_like(folded)

        def finish(cut):
            values = middle[cut]
            fed = total[cut]
            upstream = upstream_ref[cut].astype(jnp.float32)
            layer_ref[cut] = (values + open_f * fed).astype(jnp.bfloat16)
            folded[0] += fold_rows(upstream * fed)
            normal, root = norm_of(values)
            grad = grad_normed[cut]
            folded[1] += fold_rows(grad)
            folded[2] += fold_rows(grad * normal)
            scaled = grad * (1.0 + scale_f)
            grad_middle = upstream + root * (
                scaled
                - jnp.mean(scaled, axis=1, keepdims=True)
                - normal * jnp.mean(scaled * normal, axis=1, keepdims=True)
            )
            grad_middle_ref[cut] = grad_middle
            grad_branch[cut] = (grad_middle * open_a).astype(jnp.bfloat16)
            folded[3] += fold_rows(grad_middle * branch[cut])

        each_strip(rows, finish)
        gate_f_sum, shift_sum, scale_sum, gate_a_sum = [
            jnp.sum(folded[place], axis=0, keepdims=True) for place in range(4)
        ]
        none = jnp.zeros((1, width), jnp.float32)
        sums_ref[...] = jnp.concatenate(
            [
                none,
                none,
                gate_a_sum * open_a * (1.0 - open_a),
                shift_sum,
                scale_sum,
                gate_f_sum * open_f * (1.0 - open_f),
                none,
                none,
            ],
            axis=0,
        )
        total[...] = wide_dot(grad_branch[...], output_ref[...], NT)

        def gates_back(cut):
            grad_gated = total[cut]
            opened = sigmoid(gate_pre[cut])
            grad_att_ref[cut] = (grad_gated * opened).astype(jnp.bfloat16)
            grad_pre_ref[cut] = (
                grad_gated * attended_ref[cut] * (opened * (1.0 - opened))
            ).astype(jnp.bfloat16)

        each_strip(rows, gates_back)

        if split:
            for side, ref in ((away, small_send), (home, small_keep)):
                ref[:, :half] = wide_dot(gated[...], grad_branch[:, side], TN).astype(jnp.bfloat16)
                ref[:, half:] = wide_dot(normed_a_ref[...], grad_pre_ref[:, side], TN).astype(
                    jnp.bfloat16
                )
        else:
            small_all[:, :width] = wide_dot(gated[...], grad_branch[...], TN).astype(jnp.bfloat16)
            small_all[:, width:] = wide_dot(normed_a_ref[...], grad_pre_ref[...], TN).astype(
                jnp.bfloat16
            )


def feed_layer(
    split, here, attended, tokens, upstream, normed_a, mod_rows, gate_weight, output_weight, feed_gate, feed_up, feed_down
):
    rows, width = tokens.shape
    inner = feed_gate.shape[1]
    size = 512
    chunks = inner // size
    half = chunks // 2

    def turn(step, here_ref):
        return (step + half * (1 - here_ref[0])) % chunks if split else step

    def fixed(shape):
        return pl.BlockSpec(shape, lambda step, here_ref: (0, 0), pipeline_mode=pl.Buffered(1))

    def columns(step, here_ref):
        return (0, turn(step, here_ref))

    def strips(step, here_ref):
        return (turn(step, here_ref), 0)

    whole = (rows, width)
    in_specs = [fixed(whole)] * 4 + [
        fixed((8, width)),
        fixed((width, width)),
        fixed((width, width)),
        pl.BlockSpec((width, size), columns),
        pl.BlockSpec((width, size), columns),
        pl.BlockSpec((size, width), strips),
    ]
    out_specs = [fixed(whole)] * 4 + [fixed((8, width))]
    bf16, f32 = jnp.bfloat16, jnp.float32
    out_shapes = [(whole, bf16), (whole, f32), (whole, bf16), (whole, bf16), ((8, width), f32)]
    if split:
        first = pl.BlockSpec((width, size), lambda step, here_ref: (0, jnp.minimum(step, half - 1)))
        second = pl.BlockSpec((width, size), lambda step, here_ref: (0, jnp.maximum(step - half, 0)))
        out_specs += [first, second, first, second]
        out_shapes += [((width, inner // 2), bf16)] * 4
        out_specs += [pl.BlockSpec((size, width // 2), strips)] * 2
        out_shapes += [((inner, width // 2), bf16)] * 2
        out_specs += [fixed((width, width))] * 2
        out_shapes += [((width, width), bf16)] * 2
    else:
        out_specs += [pl.BlockSpec((width, size), columns)] * 2
        out_shapes += [((width, inner), bf16)] * 2
        out_specs += [pl.BlockSpec((size, width), strips), fixed((width, 2 * width))]
        out_shapes += [((inner, width), bf16), ((width, 2 * width), bf16)]
    return pl.pallas_call(
        functools.partial(feed_kernel, split, chunks),
        grid_spec=pltpu.PrefetchScalarGridSpec(
            num_scalar_prefetch=1,
            grid=(chunks,),
            in_specs=in_specs,
            out_specs=tuple(out_specs),
            scratch_shapes=[
                pltpu.VMEM(whole, bf16),
                pltpu.VMEM(whole, bf16),
                pltpu.VMEM(whole, bf16),
                pltpu.VMEM(whole, f32),
                pltpu.VMEM(whole, f32),
                pltpu.VMEM(whole, f32),
                pltpu.VMEM(whole, f32),
                pltpu.VMEM((rows, size), bf16),
                pltpu.VMEM((rows, 2 * size), bf16),
                pltpu.VMEM(whole, bf16),
                pltpu.VMEM(whole, f32),
                pltpu.VMEM((width, rows), bf16),
                pltpu.VMEM((rows, size), f32),
                pltpu.VMEM((rows, size), f32),
                pltpu.VMEM((rows, size), f32),
                pltpu.VMEM((4, 8, width), f32),
            ],
        ),
        out_shape=tuple(jax.ShapeDtypeStruct(shape, kind) for shape, kind in out_shapes),
        compiler_params=pltpu.CompilerParams(vmem_limit_bytes=VMEM_BYTES),
        cost_estimate=pl.CostEstimate(
            flops=2 * rows * width * (9 * inner + 5 * width),
            bytes_accessed=12 * width * inner + 24 * rows * width,
            transcendentals=2 * rows * inner,
        ),
        name="feed_layer",
    )(
        jnp.reshape(here, (1,)).astype(jnp.int32),
        attended,
        tokens,
        upstream,
        normed_a,
        mod_rows,
        gate_weight,
        output_weight,
        feed_gate,
        feed_up,
        feed_down,
    )


MASKS = {"u": 8, "v": 4, "y": 2, "x": 1}


def exchange(values, mask):
    return lax.ppermute(values, "crop", [(i, i ^ mask) for i in range(16)])


def swap_res(values):
    return lax.ppermute(values, "res", [(0, 1), (1, 0)])


def tie(*values):
    return lax.optimization_barrier(values)


def add_low(former, latter, kind=jnp.bfloat16):
    return (former.astype(jnp.float32) + latter.astype(jnp.float32)).astype(kind)


def stage_kernel(plans, bits_ref, *refs):
    inputs = refs[: sum(plan["count"] for plan in plans)]
    outputs = list(refs[len(inputs) :])
    for plan in plans:
        mine, inputs = inputs[: plan["count"]], inputs[plan["count"] :]
        out_ref = None if plan["apart"] else outputs.pop(0)
        for column, width, own in plan["parts"]:
            result = outputs.pop(0) if plan["apart"] else out_ref
            target = 0 if plan["apart"] else column
            rows = result.shape[-2]
            for lead in itertools.product(*[range(size) for size in result.shape[:-2]]):
                for first in range(0, rows, 16):
                    cut = (*lead, slice(first, first + 16))
                    total = None
                    for index in own:
                        value = mine[index][(*cut, slice(0, width))].astype(jnp.float32)
                        total = value if total is None else total + value
                    for index in plan["spans"]:
                        value = mine[index][(*cut, slice(column, column + width))]
                        total = total + value.astype(jnp.float32)
                    result[(*cut, slice(target, target + width))] = total.astype(result.dtype)


class Halving:
    def __init__(self, streams, orders):
        self.streams = streams
        self.orders = [list(order) for order in orders]
        self.past = [[] for _ in orders]
        self.came = [[] for _ in orders]

    def stage(self, last=False):
        index = lax.axis_index("crop")
        bits = scalars(*[(index // mask) % 2 for mask in MASKS.values()])
        self.masks, plans, specs, operands, out_specs, out_shapes = [], [], [], [], [], []
        left = 0 if last else len(self.orders[0]) - 1
        steps = {3: 4, 2: 2}.get(left, 1)
        for stream, (parts, order, past) in enumerate(zip(self.streams, self.orders, self.past)):
            now = None if last else order.pop(0)
            rest = [axis for axis in MASKS if axis in order]

            def spec_of(axes, rows, width, block, now=now, rest=rest):
                def index_map(step, bits_ref):
                    places = []
                    for axis in axes:
                        bit = bits_ref[list(MASKS).index(axis)]
                        if axis == now:
                            places.append(1 - bit)
                        elif axis not in rest:
                            places.append(bit)
                        elif axis == rest[0] and steps > 1:
                            places.append(step // (steps // 2))
                        elif len(rest) > 1 and axis == rest[1] and steps > 2:
                            places.append(step % 2)
                        else:
                            places.append(0)
                    return (*places, 0, block)

                sizes = [
                    2
                    if axis in rest
                    and not (axis == rest[0] and steps > 1)
                    and not (len(rest) > 1 and axis == rest[1] and steps > 2)
                    else None
                    for axis in axes
                ]
                return pl.BlockSpec((*sizes, rows, width), index_map)

            plan = {"parts": [], "spans": [], "count": 0, "apart": last}
            column = 0
            rows = parts[0][0][0].shape[0] // 16
            for arrays, block, width in parts:
                own = []
                for value in arrays:
                    operands.append(value.reshape(2, 2, 2, 2, rows, value.shape[1]))
                    specs.append(spec_of(list(MASKS), rows, width, block))
                    own.append(plan["count"])
                    plan["count"] += 1
                plan["parts"].append((column, width, own))
                column += width
            for axes, value in self.came[stream]:
                operands.append(value.reshape(*[2] * len(axes), rows, column))
                specs.append(spec_of(axes, rows, column, 0))
                plan["spans"].append(plan["count"])
                plan["count"] += 1
            plans.append(plan)
            if last:
                for _, width, _ in plan["parts"]:
                    out_specs.append(pl.BlockSpec((rows, width), lambda step, bits_ref: (0, 0)))
                    out_shapes.append(jax.ShapeDtypeStruct((rows, width), jnp.float32))
            else:
                past.append(now)
                self.masks.append(MASKS[now])
                out_specs.append(spec_of(rest, rows, column, 0))
                out_shapes.append(
                    jax.ShapeDtypeStruct((*[2] * len(rest), rows, column), jnp.bfloat16)
                )
        self.axes = [[axis for axis in MASKS if axis in order] for order in self.orders]
        results = pl.pallas_call(
            functools.partial(stage_kernel, plans),
            grid_spec=pltpu.PrefetchScalarGridSpec(
                num_scalar_prefetch=1, grid=(steps,), in_specs=specs, out_specs=tuple(out_specs)
            ),
            out_shape=tuple(out_shapes),
            compiler_params=pltpu.CompilerParams(vmem_limit_bytes=VMEM_BYTES),
            cost_estimate=pl.CostEstimate(
                flops=sum(4 * math.prod(shape.shape) for shape in out_shapes),
                bytes_accessed=sum(8 * math.prod(shape.shape) for shape in out_shapes),
                transcendentals=0,
            ),
            name="halving_stage",
        )(bits, *operands)
        return list(results) if last else [value.reshape(-1, value.shape[-1]) for value in results]

    def send(self, values):
        return [exchange(value, mask) for value, mask in zip(values, self.masks)]

    def take(self, values):
        for came, axes, value in zip(self.came, self.axes, values):
            came.append((axes, value))


def share_columns(values, parts):
    if parts == 1:
        return values.astype(jnp.bfloat16)
    return lax.psum_scatter(values.astype(jnp.bfloat16), "res", scatter_dimension=1, tiled=True)


def scatter_crops(values):
    return lax.psum_scatter(values, "crop", scatter_dimension=0, tiled=True).astype(jnp.float32)


def gather_crops(values, crop_parts):
    if crop_parts != 16:
        return lax.all_gather(values, "crop", axis=0, tiled=True)
    index = lax.axis_index("crop")
    for mask in (1, 2, 4, 8):
        other = exchange(values, mask)
        low = (index // mask) % 2 == 0
        values = jnp.concatenate(
            [jnp.where(low, values, other), jnp.where(low, other, values)], axis=0
        )
    return values


def sum_res(values, parts):
    if parts == 1:
        return values
    if parts != 2:
        return lax.psum(values, "res")
    return values + swap_res(values)


PACK = 1152
SIDE = 384


def whole_vmem(count):
    return [pl.BlockSpec(memory_space=pltpu.VMEM)] * count


def scalars(*values):
    return jnp.stack([jnp.asarray(value, jnp.int32) for value in values])


def local_call(kernel, numbers, operands, shapes, name, flops=0):
    return pl.pallas_call(
        kernel,
        in_specs=[pl.BlockSpec(memory_space=pltpu.SMEM)] + whole_vmem(len(operands)),
        out_specs=tuple(whole_vmem(len(shapes))),
        out_shape=tuple(jax.ShapeDtypeStruct(shape, kind) for shape, kind in shapes),
        compiler_params=pltpu.CompilerParams(vmem_limit_bytes=VMEM_BYTES),
        cost_estimate=pl.CostEstimate(
            flops=flops,
            bytes_accessed=sum(value.size * value.dtype.itemsize for value in operands)
            + sum(4 * math.prod(shape) for shape, _ in shapes),
            transcendentals=0,
        ),
        name=name,
    )(numbers, *operands)


def projection_kernel(counts, here_ref, normed_ref, *refs):
    calls = len(counts)
    parts, (joined_ref, send_ref, keep_ref) = refs[: 3 * calls], refs[3 * calls :]
    width = joined_ref.shape[1] // 3
    column = 0
    for call, pairs in enumerate(counts):
        size = pairs * LANES
        query_ref, own_ref, came_ref = parts[3 * call : 3 * call + 3]
        joined_ref[:, column : column + size] = query_ref[...]
        for start in range(0, joined_ref.shape[0], 16):
            cut = slice(start, start + 16)
            for which in range(2):
                first = (1 + which) * width + column
                joined_ref[cut, first : first + size] = add_low(
                    own_ref[which, cut], came_ref[which, cut]
                )
        column += size
    half = send_ref.shape[1]
    for side, ref in ((1 - here_ref[0], send_ref), (here_ref[0], keep_ref)):
        columns = pl.ds(pl.multiple_of(side * half, LANES), half)
        ref[...] = wide_dot(normed_ref[...], joined_ref[:, columns], TN).astype(jnp.bfloat16)


def projection_gradient(here, normed_a, calls):
    rows, width = normed_a.shape
    counts = [call[0].shape[-1] // LANES for call in calls]
    return local_call(
        functools.partial(projection_kernel, counts),
        scalars(here),
        [normed_a] + [value for call in calls for value in call],
        [
            ((rows, 3 * width), jnp.bfloat16),
            ((width, 3 * width // 2), jnp.bfloat16),
            ((width, 3 * width // 2), jnp.bfloat16),
        ],
        "projection_gradient",
        6 * rows * width * width,
    )


def finish_kernel(counts, joined_ref, weight_ref, pre_ref, gate_ref, tokens_ref, middle_ref, mod_ref, *refs):
    feed_sums_ref, extra_ref = refs[:2]
    table_refs = refs[2 : 2 + len(counts)]
    out_ref, pack_ref, total, folded = refs[2 + len(counts) :]
    step = pl.program_id(0)
    rows, width = tokens_ref.shape
    part = wide_dot(joined_ref[...], weight_ref[...], NT)

    @pl.when(step == 0)
    def _():
        total[...] = part + wide_dot(pre_ref[...], gate_ref[...], NT)

    @pl.when(step > 0)
    def _():
        total[...] += part

    @pl.when(step == pl.num_programs(0) - 1)
    def _():
        scale = mod_ref[1:2]
        folded[...] = jnp.zeros_like(folded)

        def finish(cut):
            values = tokens_ref[cut].astype(jnp.float32)
            centred = values - jnp.mean(values, axis=1, keepdims=True)
            root = lax.rsqrt(jnp.mean(centred * centred, axis=1, keepdims=True) + 1e-06)
            normal = centred * root
            grad = total[cut]
            folded[0] += fold_rows(grad)
            folded[1] += fold_rows(grad * normal)
            scaled = grad * (1.0 + scale)
            out_ref[cut] = (
                middle_ref[cut]
                + root
                * (
                    scaled
                    - jnp.mean(scaled, axis=1, keepdims=True)
                    - normal * jnp.mean(scaled * normal, axis=1, keepdims=True)
                )
            ).astype(jnp.bfloat16)

        each_strip(rows, finish)
        shift_sum, scale_sum = folded[0], folded[1]
        heads = []
        for ref, pairs in zip(table_refs, counts):
            for pair in range(pairs):
                heads += [ref[pair, 0:1], ref[pair, 1:2]]

        def upper_of(values):
            return values.astype(jnp.bfloat16).astype(jnp.float32)

        rests = [head - upper_of(head) for head in heads]
        count = width // LANES
        left = [
            jnp.sum(shift_sum, axis=0, keepdims=True),
            jnp.sum(scale_sum, axis=0, keepdims=True),
            feed_sums_ref[2:6],
        ]
        left += [
            jnp.concatenate(rests[i : i + count], axis=1) for i in range(0, len(heads), count)
        ]
        right = [jnp.concatenate(heads[3 * i : 3 * i + 3], axis=1) for i in range(4)]
        line = extra_ref[5:6]
        right += [extra_ref[4:5], line, line - upper_of(line), extra_ref[7:8]]
        pack = jnp.concatenate(
            [jnp.concatenate(left, axis=0), jnp.concatenate(right, axis=0)], axis=1
        )
        pack_ref[...] = jnp.concatenate([pack, jnp.zeros_like(pack)], axis=0).astype(jnp.bfloat16)


def finish_layer(
    joined, weight, grad_pre, gate_weight, tokens, grad_middle, mod_rows, feed_sums, extra, grad_tables
):
    rows, width = tokens.shape
    counts = [table.shape[0] for table in grad_tables]

    def fixed(shape):
        return pl.BlockSpec(shape, lambda step: (0,) * len(shape), pipeline_mode=pl.Buffered(1))

    return pl.pallas_call(
        functools.partial(finish_kernel, counts),
        grid=(3,),
        in_specs=[
            pl.BlockSpec((rows, width), lambda step: (0, step)),
            pl.BlockSpec((width, width), lambda step: (0, step)),
            fixed((rows, width)),
            fixed((width, width)),
            fixed((rows, width)),
            fixed((rows, width)),
            fixed((8, width)),
            fixed((8, width)),
            fixed((8, SIDE)),
        ]
        + [fixed((count, 8, LANES)) for count in counts],
        out_specs=(fixed((rows, width)), fixed((16, PACK))),
        out_shape=(
            jax.ShapeDtypeStruct((rows, width), jnp.bfloat16),
            jax.ShapeDtypeStruct((16, PACK), jnp.bfloat16),
        ),
        scratch_shapes=[
            pltpu.VMEM((rows, width), jnp.float32),
            pltpu.VMEM((2, 8, width), jnp.float32),
        ],
        compiler_params=pltpu.CompilerParams(vmem_limit_bytes=VMEM_BYTES),
        cost_estimate=pl.CostEstimate(
            flops=8 * rows * width * width, bytes_accessed=24 * rows * width, transcendentals=0
        ),
        name="finish_layer",
    )(
        joined,
        weight,
        grad_pre,
        gate_weight,
        tokens,
        grad_middle,
        mod_rows,
        feed_sums,
        extra,
        *grad_tables,
    )


def fan_first_kernel(bits_ref, keep_ref, came_ref, mine_ref, *send_refs):
    chunk = keep_ref.shape[0] // 16
    for other, ref in enumerate((mine_ref, *send_refs)):
        for level in range(4):
            start = (level * 4 + (bits_ref[0] ^ other)) * chunk
            for first in range(0, chunk, 16):
                cut = pl.ds(pl.multiple_of(start + first, 16), 16)
                place = level * chunk + first
                ref[place : place + 16] = add_low(keep_ref[cut], came_ref[cut])


def fan_v_kernel(bits_ref, mine_ref, *refs):
    came_refs, (send_ref, out_ref) = refs[:3], refs[3:]
    chunk = mine_ref.shape[0] // 4
    for side, ref in ((1 - bits_ref[0], send_ref), (bits_ref[0], out_ref)):
        for far in range(2):
            for first in range(0, chunk, 16):
                cut = pl.ds(pl.multiple_of((2 * far + side) * chunk + first, 16), 16)
                total = mine_ref[cut].astype(jnp.float32)
                for came_ref in came_refs:
                    total = total + came_ref[cut].astype(jnp.float32)
                place = far * chunk + first
                ref[place : place + 16] = total.astype(jnp.bfloat16)


def fan_u_kernel(bits_ref, mine_ref, came_ref, send_ref, out_ref):
    chunk = mine_ref.shape[0] // 2
    for side, ref in ((1 - bits_ref[0], send_ref), (bits_ref[0], out_ref)):
        for first in range(0, chunk, 16):
            cut = pl.ds(pl.multiple_of(side * chunk + first, 16), 16)
            ref[first : first + 16] = add_low(mine_ref[cut], came_ref[cut])


def join_packs_kernel(bits_ref, *refs):
    packs = [ref[...].astype(jnp.float32)[0:8] for ref in refs[:4]]
    refs[4][...] = jnp.concatenate(packs, axis=0).astype(jnp.bfloat16)


def small_kernel(
    heads,
    here_ref,
    mine_ref,
    came_ref,
    modulation_ref,
    pair_norm_ref,
    relative_ref,
    gain_ref,
    pair_weight_ref,
    mod_grad_ref,
    time_ref,
    label_ref,
    relative_grad_ref,
    gain_grad_ref,
    pair_grad_ref,
    grad_condition,
    grad_mod,
    kept,
):
    step = pl.program_id(0)
    crops = mine_ref.shape[0] // 8
    width = mine_ref.shape[1] - SIDE
    conds = relative_ref.shape[1]
    parts = mod_grad_ref.shape[1] // width

    def parts_split(values):
        upper = values.astype(jnp.bfloat16)
        return upper, (values - upper.astype(jnp.float32)).astype(jnp.bfloat16)

    def dot_left(narrow, values, numbers):
        upper, rest = parts_split(values)
        return wide_dot(narrow, upper, numbers) + wide_dot(narrow, rest, numbers)

    def dot_right(values, narrow, numbers):
        upper, rest = parts_split(values)
        return wide_dot(upper, narrow, numbers) + wide_dot(rest, narrow, numbers)

    def both_twice(narrow):
        return jnp.concatenate([narrow, narrow], axis=0)

    def stacked(values):
        return jnp.concatenate(parts_split(values), axis=0)

    @pl.when(step == 0)
    def _():
        shape = (8 * crops, 8 * crops)
        picked = lax.broadcasted_iota(jnp.int32, shape, 0)
        source = lax.broadcasted_iota(jnp.int32, shape, 1)
        hit = ((source >> 3) == (picked & (crops - 1))) & ((source & 7) == (picked // crops))
        select = jnp.where(hit, 1.0, 0.0).astype(jnp.bfloat16)
        mine = wide_dot(select, mine_ref[...])
        grad_mod[...] = mine[: 6 * crops, :width] + wide_dot(select, came_ref[...])[: 6 * crops, :width]
        condition = (
            mine[5 * crops : 6 * crops, width : width + conds]
            + mine[6 * crops : 7 * crops, width : width + conds]
        )
        gate_value = sigmoid(condition)
        kept[0] = condition * gate_value
        kept[1] = gate_value * (1.0 + condition * (1.0 - gate_value))
        kept[2] = mine[4 * crops : 5 * crops, width : width + conds]
        kept[3] = jnp.broadcast_to(
            mine[5 * crops : 6 * crops, width + conds : width + conds + 1]
            + mine[6 * crops : 7 * crops, width + conds : width + conds + 1],
            (crops, conds),
        )
        grad_condition[...] = jnp.zeros_like(grad_condition)

    cond_act = both_twice(kept[0].astype(jnp.bfloat16))
    for turn in range(parts):
        columns = slice(turn * width, (turn + 1) * width)
        first = pl.multiple_of((step * parts + turn) * crops, crops)
        pair = stacked(grad_mod[pl.ds(first, crops)])
        mod_grad_ref[:, columns] = wide_dot(cond_act, pair, TN)
        more = wide_dot(pair, modulation_ref[:, columns], NT)
        grad_condition[...] += more[:crops] + more[crops:]

    @pl.when(step == 0)
    def _():
        shape = (8, 8 * crops)
        line = lax.broadcasted_iota(jnp.int32, shape, 0)
        local = lax.broadcasted_iota(jnp.int32, shape, 1) & 7
        every = jnp.where(local == line, 1.0, 0.0).astype(jnp.bfloat16)
        lines = wide_dot(every, mine_ref[...]) + wide_dot(every, came_ref[...])

        def of_head(head):
            upper = width + (head % 3) * LANES
            rest = (head % (width // LANES)) * LANES
            low = 6 + head // (width // LANES)
            return (
                lines[head // 3 : head // 3 + 1, upper : upper + LANES]
                + lines[low : low + 1, rest : rest + LANES]
            )

        table = jnp.concatenate(
            [of_head(head) for head in range(heads)]
            + [jnp.zeros((16 - heads, LANES), jnp.float32)],
            axis=0,
        )
        bins = relative_ref.shape[0]
        pair_grad_ref[...] = dot_right(table, pair_norm_ref[...], (((1,), (0,)), ((), ())))[:heads]
        grad_norm = dot_right(table, pair_weight_ref[...], (((0,), (1,)), ((), ())))[:bins]
        values = relative_ref[...]
        centred = values - jnp.mean(values, axis=1, keepdims=True)
        root = lax.rsqrt(jnp.mean(centred * centred, axis=1, keepdims=True) + 1e-06)
        normal = centred * root
        gain_grad_ref[...] = jnp.sum(grad_norm * normal, axis=0, keepdims=True)
        scaled = grad_norm * gain_ref[...]
        relative_grad_ref[...] = root * (
            scaled
            - jnp.mean(scaled, axis=1, keepdims=True)
            - normal * jnp.mean(scaled * normal, axis=1, keepdims=True)
        )

    @pl.when(step == pl.num_programs(0) - 1)
    def _():
        final = stacked(grad_condition[...] * kept[1])
        time_ref[...] = wide_dot(both_twice(kept[2].astype(jnp.bfloat16)), final, TN)
        label = lax.broadcasted_iota(jnp.int32, (crops, label_ref.shape[0]), 1)
        number = kept[3][:, 0:1].astype(jnp.int32)
        onehot = jnp.where(label == number, 1.0, 0.0).astype(jnp.bfloat16)
        label_ref[...] = wide_dot(both_twice(onehot), final, TN)


def small_gradients(heads, labels, mine, came, modulation_weight, pair_norm, relative, gain, pair_weight):
    conds, wide = modulation_weight.shape
    bins = relative.shape[0]
    rows = mine.shape[0]
    steps = 3

    def fixed(shape):
        return pl.BlockSpec(shape, lambda step: (0, 0))

    shapes = [(conds, wide), (conds, conds), (labels, conds), (bins, conds), (1, conds), (heads, conds)]
    return pl.pallas_call(
        functools.partial(small_kernel, heads),
        grid=(steps,),
        in_specs=[
            pl.BlockSpec(memory_space=pltpu.SMEM),
            fixed((rows, PACK)),
            fixed((rows, PACK)),
            pl.BlockSpec((conds, wide // steps), lambda step: (0, step)),
            fixed((LANES, conds)),
            fixed((bins, conds)),
            fixed((1, conds)),
            fixed((conds, 16)),
        ],
        out_specs=tuple(
            [pl.BlockSpec((conds, wide // steps), lambda step: (0, step))]
            + [fixed(s) for s in shapes[1:]]
        ),
        out_shape=tuple(jax.ShapeDtypeStruct(shape, jnp.float32) for shape in shapes),
        scratch_shapes=[
            pltpu.VMEM((rows // 8, conds), jnp.float32),
            pltpu.VMEM((6 * rows // 8, wide // 6), jnp.float32),
            pltpu.VMEM((4, rows // 8, conds), jnp.float32),
        ],
        compiler_params=pltpu.CompilerParams(vmem_limit_bytes=VMEM_BYTES),
        cost_estimate=pl.CostEstimate(
            flops=100000000, bytes_accessed=10000000, transcendentals=0
        ),
        name="small_gradients",
    )(
        scalars(0),
        mine,
        came,
        modulation_weight,
        pair_norm,
        relative,
        gain,
        pair_weight,
    )


def per_device(
    crop_parts,
    res_parts,
    tokens,
    cotangent,
    time_levels,
    cath_ids,
    residue_numbers,
    chain_mask,
    time_weight,
    label_table,
    modulation_weight,
    projection_weight,
    gate_weight,
    output_weight,
    relative_table,
    pair_gain,
    pair_weight,
    feed_gate,
    feed_up,
    feed_down,
):
    crop_count, row_count, model_width = tokens.shape
    crop_length = residue_numbers.shape[1]
    head_count = pair_weight.shape[1]
    head_width = model_width // head_count
    bin_count = relative_table.shape[0]
    label_count = label_table.shape[0]
    token_count = crop_count * row_count
    score_scale = head_width ** (-0.5)
    pairs = head_count // 2
    layout = Layout(row_count, crop_length)
    query_start = lax.axis_index("res") * row_count

    def conditioning(features, onehot):
        return jnp.dot(features, time_weight, preferred_element_type=jnp.float32) + jnp.dot(
            onehot, label_table, preferred_element_type=jnp.float32
        )

    features = time_features(time_levels, time_weight.shape[0]).astype(jnp.bfloat16)
    label_onehot = (cath_ids[:, None] == jnp.arange(label_count, dtype=jnp.int32)[None, :]).astype(
        jnp.bfloat16
    )
    condition = conditioning(features, label_onehot)
    cond_act = jax.nn.silu(condition).astype(jnp.bfloat16)
    modulation = jnp.dot(cond_act, modulation_weight, preferred_element_type=jnp.float32)
    modulation = modulation.reshape(crop_count, 6, 1, model_width)
    shift_a, scale_a = modulation[:, 0], modulation[:, 1]
    mod_rows = pad_to(modulation[:, :, 0], 1, 8, 0.0)

    rotated = lax.dynamic_slice_in_dim(
        jnp.concatenate([jnp.stack([residue_numbers, chain_mask])] * 2, 2), query_start, crop_length, 2
    )
    members, kinds, forward_bins, backward_bins, places, *turned = attention_tables(
        layout, rotated[0], rotated[1], query_start, bin_count
    )
    relative_values = relative_table.astype(jnp.float32)
    gain_values = pair_gain.astype(jnp.float32)
    pair_norm = normalize_rows(relative_values, gain_values).astype(jnp.bfloat16)
    bias_rows = jnp.dot(pair_norm, pair_weight, preferred_element_type=jnp.float32)
    tables = head_tables(layout, bias_rows, score_scale)

    token_values = tokens.astype(jnp.float32)
    normed_a = (
        modulate(token_values, shift_a, scale_a)
        .astype(jnp.bfloat16)
        .reshape(token_count, model_width)
    )
    def project(weight):
        rows = jnp.dot(normed_a, weight, preferred_element_type=jnp.float32)
        return rows.astype(jnp.bfloat16).reshape(crop_count, row_count, -1)

    key_values = project(projection_weight[:, model_width:])
    queries = project(projection_weight[:, :model_width])
    others = [
        lax.ppermute(
            key_values, "res", [((r + step) % res_parts, r) for r in range(res_parts)]
        )
        for step in range(1, res_parts)
    ]
    small_operands = (
        pad_to(pair_norm, 0, LANES, 0.0),
        relative_values,
        gain_values.reshape(1, -1),
        pad_to(pair_weight, 1, 16, 0.0),
    )
    if others:
        others, small_operands = tie(others, small_operands)
    if len(layout.pieces) == 2:
        other = others[0] if len(others) == 1 else jnp.concatenate(others, axis=1)
        pieces = [(key_values, 0, pairs), (other, 0, pairs)]
    else:
        pieces = [(jnp.concatenate([key_values] + others, axis=1), 0, pairs)]

    def block_rows(values):
        return pad_to(values, 1, layout.block_rows, 0)

    attended, logs = attention_forward(
        layout,
        score_scale,
        block_rows(queries),
        pieces,
        members,
        kinds,
        forward_bins,
        tables,
    )
    here = lax.axis_index("res")
    split = res_parts == 2 and crop_parts == 16
    per_crop_results = [
        feed_layer(
            split,
            here,
            attended[crop],
            block_rows(tokens)[crop],
            block_rows(cotangent)[crop],
            block_rows(normed_a.reshape(tokens.shape))[crop],
            mod_rows[crop],
            gate_weight,
            output_weight,
            feed_gate,
            feed_up,
            feed_down,
        )
        for crop in range(crop_count)
    ]
    layer_out, grad_middle, grad_attended, grad_gate_pre, feed_sums = (
        jnp.stack([result[place] for result in per_crop_results]) for place in range(5)
    )
    layer_out, grad_middle = layer_out[:, :row_count], grad_middle[:, :row_count]
    grad_gate_pre = grad_gate_pre[:, :row_count].reshape(token_count, model_width)
    weight_grads = [
        sum(result[place].astype(jnp.float32) for result in per_crop_results).astype(jnp.bfloat16)
        if crop_count > 1
        else per_crop_results[0][place]
        for place in range(5, len(per_crop_results[0]))
    ]

    def backward_of(first_pair, count, grad_now):
        return attention_backward(
            layout,
            score_scale,
            first_pair,
            count,
            block_rows(queries),
            grad_now,
            attended,
            logs,
            pieces,
            members,
            kinds,
            backward_bins,
            places,
            *turned,
            tables,
        )

    if split:
        arrivals = [swap_res(weight_grads[place]) for place in (0, 2, 4, 6)]
        kept = [weight_grads[place] for place in (1, 3, 5, 7)]
        half = model_width // 2
        inner = feed_gate.shape[1] // 2
        calls = [list(backward_of(0, 1, grad_attended))]
        arrivals, calls[0] = tie(arrivals, calls[0])
        gate_w, up_w, down_w, small_w = zip(kept, arrivals)
        halving = Halving(
            [
                [(gate_w, 0, inner), (small_w, 0, half)],
                [(up_w, 0, inner), (small_w, 1, half)],
                [(down_w, 0, half)],
            ],
            ["xyvu", "yvxu", "vxyu"],
        )
        arrived = []
        for first_pair, count in ((1, 3), (4, 2)):
            arrived.append(swap_res(calls[-1][2][0]))
            sent = halving.stage()
            sent, grad_attended = tie(sent, grad_attended)
            came = halving.send(sent)
            calls.append(list(backward_of(first_pair, count, grad_attended)))
            came, calls[-1], arrived[-1] = tie(came, calls[-1], arrived[-1])
            halving.take(came)
        index = lax.axis_index("crop")
        bf16 = jnp.bfloat16
        share = model_width // 16
        away = swap_res(calls[2][2][0])
        sent = halving.stage()
        sent, calls[2][1] = tie(sent, calls[2][1])
        came = halving.send(sent)
        joined, proj_send, proj_keep = projection_gradient(
            here,
            normed_a,
            [
                (calls[0][0][0], calls[0][1][0], arrived[0]),
                (calls[1][0][0], calls[1][1][0], arrived[1]),
                (calls[2][0][0], calls[2][1][0], away),
            ],
        )
        came, proj_send, proj_keep = tie(came, proj_send, proj_keep)
        proj_came = swap_res(proj_send)
        halving.take(came)
        sent = halving.stage()
        sent, proj_came = tie(sent, proj_came)
        came = halving.send(sent)
        mine, *fan = local_call(
            fan_first_kernel,
            scalars(index % 4),
            [proj_keep, proj_came],
            [((4 * share, PACK), bf16)] * 4,
            "fan_first",
        )
        fan, joined = tie(fan, joined)
        fan_came = [exchange(value, mask + 1) for mask, value in enumerate(fan)]
        extra = jnp.concatenate(
            [
                pad_to(features.astype(jnp.float32), 1, SIDE, 0.0),
                jnp.concatenate(
                    [condition, pad_to(cath_ids.astype(jnp.float32)[:, None], 1, LANES, 0.0)], axis=1
                ),
            ],
            axis=0,
        )
        tokens_grad, pack = finish_layer(
            joined,
            projection_weight,
            grad_gate_pre,
            gate_weight,
            tokens[0],
            grad_middle[0],
            mod_rows[0],
            feed_sums[0],
            jnp.pad(extra, ((4, 2), (0, 0))),
            [call[-1][0] for call in calls],
        )
        tokens_grad = tokens_grad[None]
        came, pack = tie(came, pack)
        packs = [pack] + [exchange(pack, mask + 1) for mask in range(3)]
        halving.take(came)
        finals = halving.stage(last=True)
        feed_gate_grad, output_weight_grad, feed_up_grad, gate_weight_grad, feed_down_grad = finals
        packs, finals = tie(packs, finals)
        (packs,) = local_call(join_packs_kernel, scalars(0), packs, [((32, PACK), bf16)], "join_packs")
        far_packs = exchange(packs, MASKS["v"])
        packs, fan_came, far_packs = tie(packs, fan_came, far_packs)
        sent, mine = local_call(
            fan_v_kernel,
            scalars((index // 4) % 2),
            [mine, *fan_came],
            [((2 * share, PACK), bf16), ((2 * share, PACK), bf16)],
            "fan_v",
        )
        packs = jnp.concatenate([packs, far_packs], axis=0)
        sent, packs = tie(sent, packs)
        came = exchange(sent, MASKS["v"])
        far_packs = exchange(packs, MASKS["u"])
        came, far_packs = tie(came, far_packs)
        packs = jnp.concatenate([packs, far_packs], axis=0)
        sent, mine = local_call(
            fan_u_kernel,
            scalars(index // 8),
            [mine, came],
            [((share, PACK), bf16), ((share, PACK), bf16)],
            "fan_u",
        )
        sent, packs = tie(sent, packs)
        came = exchange(sent, MASKS["u"])
        (
            modulation_weight_grad,
            time_weight_grad,
            label_table_grad,
            relative_table_grad,
            pair_gain_grad,
            pair_weight_grad,
        ) = small_gradients(
            head_count, label_count, packs, swap_res(packs), modulation_weight, *small_operands
        )
        pair_weight_grad = pair_weight_grad.T
        came, pair_weight_grad = tie(came, pair_weight_grad)
        projection_weight_grad = add_low(mine, came, jnp.float32)
        pair_gain_grad = pair_gain_grad[0]
    else:
        results = backward_of(0, pairs, grad_attended)
        grad_table = results[-1]
        grad_pairs = results[1:-1]
        if len(grad_pairs) == 2:
            total, away = grad_pairs[0].astype(jnp.float32), grad_pairs[1]
        else:
            total = grad_pairs[0][:, :, :row_count].astype(jnp.float32)
            away = grad_pairs[0][:, :, row_count:]
        for step in range(1, res_parts):
            sent = away[:, :, (step - 1) * row_count : step * row_count]
            pairs_to = [(r, (r + step) % res_parts) for r in range(res_parts)]
            total = total + lax.ppermute(sent, "res", pairs_to).astype(jnp.float32)
        total = total.astype(jnp.bfloat16)
        grad_projected = jnp.concatenate(
            [results[0][:, :row_count], total[:, 0], total[:, 1]], axis=-1
        ).reshape(token_count, 3 * model_width)
        grad_normed_a = against_columns(grad_projected, projection_weight) + against_columns(
            grad_gate_pre, gate_weight
        )
        norm_back_a = jax.vjp(modulate, token_values, shift_a, scale_a)[1]
        grad_tokens, grad_shift_a, grad_scale_a = norm_back_a(
            grad_normed_a.reshape(crop_count, row_count, model_width)
        )
        tokens_grad = (grad_middle + grad_tokens).astype(jnp.bfloat16)
        feed_gate_grad, feed_up_grad, feed_down_grad = (
            scatter_crops(share_columns(value, res_parts)) for value in weight_grads[:3]
        )
        output_weight_grad, gate_weight_grad = (
            scatter_crops(share_columns(value, res_parts))
            for value in (weight_grads[3][:, :model_width], weight_grads[3][:, model_width:])
        )
        projection_weight_grad = scatter_crops(
            share_columns(across_rows(normed_a, grad_projected), res_parts)
        )
        grad_table = grad_table[:, :, :2].sum(0).reshape(head_count, LANES)

        grad_modulation = jnp.concatenate([grad_shift_a, grad_scale_a, feed_sums[:, 2:6]], axis=1)
        grad_modulation = grad_modulation.reshape(crop_count, 6 * model_width)
        table_row = grad_table.reshape(1, head_count * LANES)
        first_row = (jnp.arange(crop_count) == 0).astype(jnp.float32)[:, None]
        small_here = jnp.concatenate([grad_modulation, first_row * table_row], axis=1)
        levels_here = jnp.stack([time_levels, cath_ids.astype(jnp.float32)], axis=1)
        levels_here = pad_to(levels_here, 1, LANES, 0.0)
        small_all = gather_crops(
            jnp.concatenate([levels_here, sum_res(small_here, res_parts)], axis=1), crop_parts
        )
        levels_all, small_all = small_all[:, :2], small_all[:, LANES:]
        grad_modulation = small_all[:, : 6 * model_width]
        grad_table = jnp.sum(small_all[:, 6 * model_width :], axis=0).reshape(head_count, LANES)
        grad_table = grad_table[:, :bin_count]
        features_all = time_features(levels_all[:, 0], time_weight.shape[0]).astype(jnp.bfloat16)
        onehot_all = (
            levels_all[:, 1].astype(jnp.int32)[:, None]
            == jnp.arange(label_count, dtype=jnp.int32)[None, :]
        ).astype(jnp.bfloat16)
        condition = conditioning(features_all, onehot_all)
        cond_act = jax.nn.silu(condition).astype(jnp.bfloat16)
        modulation_weight_grad = split_left(cond_act, grad_modulation, 0, 0)
        grad_condition = split_left(modulation_weight, grad_modulation, 1, 1).T * silu_slope(condition)
        time_weight_grad = split_left(features_all, grad_condition, 0, 0)
        label_table_grad = split_left(onehot_all, grad_condition, 0, 0)
        pair_weight_grad = split_left(pair_norm, grad_table, 0, 1)
        grad_pair_norm = split_right(grad_table, pair_weight, 0, 1)
        pair_back = jax.vjp(normalize_rows, relative_values, gain_values)[1]
        relative_table_grad, pair_gain_grad = pair_back(grad_pair_norm)
    return (
        layer_out,
        tokens_grad,
        time_weight_grad,
        label_table_grad,
        modulation_weight_grad,
        projection_weight_grad,
        gate_weight_grad,
        output_weight_grad,
        relative_table_grad,
        pair_gain_grad,
        pair_weight_grad,
        feed_gate_grad,
        feed_up_grad,
        feed_down_grad,
    )


def solution(mesh):
    return jax.shard_map(
        functools.partial(per_device, mesh.shape["crop"], mesh.shape["res"]),
        mesh=mesh,
        in_specs=(
            P("crop", "res", None),
            P("crop", "res", None),
            P("crop"),
            P("crop"),
            P("crop", None),
            P("crop", None),
            P(),
            P(),
            P(),
            P(),
            P(),
            P(),
            P(),
            P(),
            P(),
            P(),
            P(),
            P(),
        ),
        out_specs=(
            P("crop", "res", None),
            P("crop", "res", None),
            P(),
            P(),
            P(),
            P("crop", "res"),
            P("crop", "res"),
            P("crop", "res"),
            P(),
            P(),
            P(),
            P("crop", "res"),
            P("crop", "res"),
            P("crop", "res"),
        ),
        check_vma=False,
    )
```

```python
import functools
import itertools
import math

import jax
import jax.numpy as jnp
from jax import lax
from jax.experimental import pallas as pl
from jax.experimental.pallas import tpu as pltpu
from jax.sharding import PartitionSpec as P

LANES = 128
NEAR = 31
VMEM_BYTES = 56 * 1024 * 1024
LOG2E = 1.4426950408889634
NONE, RIGHT, LEFT, APART = 0, 1, 2, 3


def layer_norm(inputs):
    mean_value = jnp.mean(inputs, axis=-1, keepdims=True)
    centred = inputs - mean_value
    spread = jnp.mean(centred * centred, axis=-1, keepdims=True)
    return centred * lax.rsqrt(spread + 1e-06)


def modulate(inputs, shift_row, scale_row):
    return layer_norm(inputs) * (1.0 + scale_row) + shift_row


def normalize_rows(table_rows, gain_row):
    return layer_norm(table_rows) * gain_row


def time_features(time_levels, feature_width):
    half_width = feature_width // 2
    frequency = jnp.exp(-math.log(10000.0) * jnp.arange(half_width, dtype=jnp.float32) / half_width)
    angles = 1000.0 * time_levels[:, None] * frequency[None, :]
    return jnp.concatenate([jnp.sin(angles), jnp.cos(angles)], axis=-1)


def across_rows(former, latter):
    return lax.dot_general(
        former, latter, (((0,), (0,)), ((), ())), preferred_element_type=jnp.float32
    )


def against_columns(former, latter):
    return lax.dot_general(
        former, latter, (((1,), (1,)), ((), ())), preferred_element_type=jnp.float32
    )


def split_parts(values):
    upper = lax.reduce_precision(values, 8, 7)
    return (upper.astype(jnp.bfloat16), (values - upper).astype(jnp.bfloat16))


def split_left(narrow, values, former_dim, latter_dim):
    upper, rest = split_parts(values)
    numbers = (((former_dim,), (latter_dim,)), ((), ()))
    return lax.dot_general(
        narrow, upper, numbers, preferred_element_type=jnp.float32
    ) + lax.dot_general(narrow, rest, numbers, preferred_element_type=jnp.float32)


def split_right(values, narrow, former_dim, latter_dim):
    upper, rest = split_parts(values)
    numbers = (((former_dim,), (latter_dim,)), ((), ()))
    return lax.dot_general(
        upper, narrow, numbers, preferred_element_type=jnp.float32
    ) + lax.dot_general(rest, narrow, numbers, preferred_element_type=jnp.float32)


def sigmoid_slope(inputs):
    gate_value = jax.nn.sigmoid(inputs)
    return gate_value * (1.0 - gate_value)


def silu_slope(inputs):
    gate_value = jax.nn.sigmoid(inputs)
    return gate_value * (1.0 + inputs * (1.0 - gate_value))


class Layout:
    def __init__(self, rows, length):
        self.rows = rows
        self.length = length
        self.query_tiles = -(-rows // LANES)
        self.key_tiles = -(-length // LANES)
        self.padded = self.query_tiles * LANES
        self.wide = self.key_tiles * LANES
        self.last = self.key_tiles - 1
        self.groups = (self.query_tiles + 4) * 4
        assert 2 * self.groups + 3 <= LANES and self.groups <= 64
        assert rows - 1 + NEAR < self.padded and length - NEAR >= self.last * LANES
        assert rows % 8 == 0 and self.last > self.query_tiles
        self.block_rows = rows if rows % 16 == 0 else self.padded
        self.pieces = [rows, length - rows] if rows % 16 == 0 else [length]

    def tile_start(self, tile):
        return self.last * LANES if tile < 0 else tile * LANES


def pad_to(values, axis, size, fill):
    widths = [(0, 0)] * values.ndim
    widths[axis] = (0, size - values.shape[axis])
    return jnp.pad(values, widths, constant_values=fill)


def tables_kernel(layout, bin_count, start_ref, pairs_ref, *out_refs):
    members_ref, kinds_ref, forward_ref, backward_ref, places_ref = out_refs[:5]
    members_turned, kinds_turned, codes = out_refs[5:]
    rows, length, queries, groups = layout.rows, layout.length, layout.query_tiles, layout.groups
    wrap = length - start_ref[0]
    reach = (bin_count - 2) // 2
    zero_bin = LANES - 1
    shape = (LANES, LANES)
    lane = lax.broadcasted_iota(jnp.int32, shape, 1)
    row = lax.broadcasted_iota(jnp.int32, shape, 0)
    last_start = layout.last * LANES

    tiles = pairs_ref.shape[1]
    marks = pairs_ref[1].astype(jnp.float32)
    place = lax.broadcasted_iota(jnp.int32, marks.shape, 0) * LANES + lax.broadcasted_iota(
        jnp.int32, marks.shape, 1
    )
    before = jnp.sum(jnp.where(place < wrap, marks, 0.0), keepdims=True)
    every = jnp.sum(marks, keepdims=True)
    triangle = jnp.where(row <= lane, 1.0, 0.0).astype(jnp.bfloat16)
    running = jnp.dot(marks.astype(jnp.bfloat16), triangle, preferred_element_type=jnp.float32)
    numbers, chains = [], []
    carry = jnp.zeros((1, 1), jnp.float32)
    for tile in range(layout.key_tiles):
        count = running[tile : tile + 1] + carry
        carry = carry + running[tile : tile + 1, LANES - 1 :]
        count = count + jnp.where(place[tile : tile + 1] < wrap, every - before, -before)
        chains.append(jnp.broadcast_to(count.astype(jnp.int32), shape))
        numbers.append(jnp.broadcast_to(pairs_ref[0, tile : tile + 1], shape))
    number_rows = [value.T for value in numbers]
    chain_rows = [value.T for value in chains]

    def bins_of(key_number, key_chain, query_number, query_chain):
        offset = jnp.clip(key_number - query_number, -reach, reach) + reach
        return jnp.where(key_chain == query_chain, offset, bin_count - 1)

    def touches(query, tile):
        begin = -LANES if tile < 0 else tile * LANES
        return (begin <= query + NEAR) & (query - NEAR <= begin + LANES - 1)

    for tile in range(layout.key_tiles):
        size = min(LANES, length - tile * LANES)
        key = tile * LANES + row
        if tile == layout.last:
            other = jnp.full(shape, queries + 3, jnp.int32)
        elif tile == queries - 1:
            other = jnp.full(shape, queries, jnp.int32)
        else:
            other = jnp.where(key < wrap, queries + 1, queries + 2)
        group = jnp.where(key < rows, tile, other)
        slot = group * 4 + chain_rows[tile] - 1
        hit = (lane == slot) | (lane == slot + groups)
        tail = (lane >= 2 * groups) & (lane < 2 * groups + 3)
        values = jnp.where(hit, 1.0, jnp.where(tail, -1.0, 0.0)).astype(jnp.bfloat16)
        members_ref[tile * LANES : tile * LANES + size] = values[:size]
        turned = jnp.where(hit & (lane < groups), 1.0, 0.0).T
        members_turned[:, tile * LANES : tile * LANES + size] = turned[:64, :size].astype(jnp.bfloat16)

    local = jnp.where(lane >= groups, lane - groups, lane)
    lane_group = local >> 2
    lane_chain = (local & 3) + 1
    lane_begin = jnp.where(
        lane_group < queries,
        lane_group * LANES,
        jnp.where(lane_group == queries, (queries - 1) * LANES, -LANES),
    )
    has_band = (lane_group <= queries) | (lane_group == queries + 3)
    other_right = jnp.where(
        lane_group == queries,
        rows,
        jnp.where(
            lane_group == queries + 3,
            last_start,
            jnp.where(lane_group == queries + 1, 0, 2 * length),
        ),
    )
    right_limit = jnp.where(lane_group > queries, jnp.where(lane_group == queries + 3, wrap, length), wrap)
    for tile in range(queries):
        size = min(LANES, layout.block_rows - tile * LANES)
        query = tile * LANES + row
        near = (lane_begin <= query + NEAR) & (query - NEAR <= lane_begin + LANES - 1) & has_band
        right = jnp.where(lane_group < queries, lane_group - tile, right_limit - other_right) > 0
        same = chain_rows[tile] == lane_chain
        kinds = jnp.where(same, jnp.where(near, NONE, jnp.where(right, RIGHT, LEFT)), APART)
        kinds = jnp.where((lane < 2 * groups) & (query < rows), kinds, NONE)
        kinds_ref[tile * LANES : tile * LANES + size] = kinds[:size]
        kinds_turned[:, tile * LANES : (tile + 1) * LANES] = jnp.where(lane < groups, kinds, NONE).T[:64]
        for step in range(3):
            near_tile = tile + step - 1
            index = layout.last if near_tile < 0 else near_tile
            if near_tile < queries:
                inside = touches(query, near_tile) & (query < rows)
                inside &= lane < length - index * LANES
                found = bins_of(
                    numbers[index], chains[index], number_rows[tile], chain_rows[tile]
                )
                found = jnp.where(inside, found, zero_bin)
            else:
                found = jnp.full(shape, zero_bin, jnp.int32)
            forward_ref[
                tile * LANES : (tile + 1) * LANES, step * LANES : (step + 1) * LANES
            ] = found

    codes[...] = jnp.full(codes.shape, -1, jnp.int32)
    for tile in range(queries):
        size = min(LANES, rows - tile * LANES)
        code = number_rows[tile] * 8 + chain_rows[tile]
        codes[(tile + 1) * LANES : (tile + 1) * LANES + size] = code[:size]

    for index, tile in enumerate(list(range(queries)) + [-1]):
        source = layout.last if tile < 0 else tile
        key_row = (row - (length - last_start)) if tile < 0 else tile * LANES + row
        present = row < length - source * LANES
        for step in range(3):
            near_tile = tile + step - 1
            if 0 <= near_tile < queries:
                near_query = near_tile * LANES + lane
                inside = touches(near_query, tile) & (near_query < rows) & present
                found = bins_of(
                    number_rows[source], chain_rows[source], numbers[near_tile], chains[near_tile]
                )
                found = jnp.where(inside, found, zero_bin)
            else:
                found = jnp.full(shape, zero_bin, jnp.int32)
            backward_ref[
                index * LANES : (index + 1) * LANES, step * LANES : (step + 1) * LANES
            ] = found
        target = (number_rows[source] + reach - lane) * 8 + chain_rows[source]
        target = jnp.where(present & (lane > 0) & (lane < 2 * reach), target, -9)
        offset = (LANES - (length - last_start)) if tile < 0 else (tile + 1) * LANES
        far = 4 * LANES
        shift = jnp.full(shape, far, jnp.int32)
        for distance in range(-NEAR, NEAR + 1):
            other = codes[offset - distance : offset - distance + LANES]
            shift = jnp.where(other == target, distance, shift)
        if tile < 0:
            base = jnp.zeros(shape, jnp.int32)
        else:
            base = jnp.where(row < LANES // 2, tile - 1, tile) * LANES
        places_ref[index * LANES : (index + 1) * LANES] = jnp.where(
            shift == far, far - 1, key_row - shift - base
        )


def attention_tables(layout, numbers, marks, query_start, bin_count):
    crops = numbers.shape[0]
    pairs = jnp.stack([numbers, marks], axis=1)
    pairs = pad_to(pairs, 2, layout.wide, 0).reshape(crops, 2, layout.key_tiles, LANES)
    spots = (layout.query_tiles + 1) * LANES
    shapes = [
        ((layout.length, LANES), jnp.bfloat16),
        ((layout.block_rows, LANES), jnp.int32),
        ((layout.padded, 3 * LANES), jnp.int32),
        ((spots, 3 * LANES), jnp.int32),
        ((spots, LANES), jnp.int32),
        ((64, layout.length), jnp.bfloat16),
        ((64, layout.padded), jnp.int32),
    ]
    return pl.pallas_call(
        functools.partial(tables_kernel, layout, bin_count),
        grid=(crops,),
        in_specs=[
            pl.BlockSpec(memory_space=pltpu.SMEM),
            pl.BlockSpec((None, 2, layout.key_tiles, LANES), lambda crop: (crop, 0, 0, 0)),
        ],
        out_specs=tuple(pl.BlockSpec((None, *shape), lambda crop: (crop, 0, 0)) for shape, _ in shapes),
        out_shape=tuple(jax.ShapeDtypeStruct((crops, *shape), kind) for shape, kind in shapes),
        scratch_shapes=[pltpu.VMEM((layout.padded + 2 * LANES, LANES), jnp.int32)],
        compiler_params=pltpu.CompilerParams(vmem_limit_bytes=VMEM_BYTES),
        cost_estimate=pl.CostEstimate(
            flops=40000000 * crops, bytes_accessed=4000000 * crops, transcendentals=0
        ),
        name="pair_tables",
    )(jnp.reshape(query_start, (1,)).astype(jnp.int32), pairs)


def head_tables(layout, bias_rows, scale):
    bin_count, heads = bias_rows.shape
    table = (bias_rows - bias_rows[bin_count - 1 :]).T / scale
    lane = jnp.arange(LANES, dtype=jnp.int32)
    groups = layout.groups

    def columns(values):
        upper = lax.reduce_precision(values, 8, 7)
        rest = values - upper
        return jnp.where(
            lane < groups, upper[:, None], jnp.where(lane < 2 * groups, rest[:, None], 0.0)
        )

    lookup = pad_to(table, 1, LANES, 0.0)
    stacked = jnp.stack([lookup, columns(table[:, bin_count - 2]), columns(table[:, 0])], 1)
    stacked = pad_to(stacked, 1, 8, 0.0)
    return stacked.reshape(heads // 2, 16, LANES)


NT = (((1,), (1,)), ((), ()))
TN = (((0,), (0,)), ((), ()))


def wide_dot(former, latter, numbers=(((1,), (0,)), ((), ()))):
    return lax.dot_general(former, latter, numbers, preferred_element_type=jnp.float32)


def look_up(table_row, bins):
    table = jnp.broadcast_to(table_row, bins.shape)
    return jnp.take_along_axis(table, bins, axis=1, mode="promise_in_bounds")


def half_of(values, lane, side):
    return jnp.where((lane >= 64) == (side == 1), values, jnp.zeros_like(values))


def row_blocks(total, size):
    return [(start, min(start + size, total)) for start in range(0, total, size)]


def group_columns(kinds, tables, side):
    right = tables[8 * side + 1 : 8 * side + 2]
    left = tables[8 * side + 2 : 8 * side + 3]
    return jnp.where(kinds == RIGHT, right, jnp.where(kinds == LEFT, left, 0.0))


def forward_kernel(layout, scale, *refs):
    count = len(layout.pieces)
    query_ref = refs[0]
    key_refs = refs[1 : 1 + count]
    value_refs = refs[1 + count : 1 + 2 * count]
    members_ref, kinds_ref, bins_ref, tables_ref, out_ref, log_ref = refs[1 + 2 * count : -1]
    all_scores = refs[-1]
    pair = pl.program_id(1)
    rows, length = layout.block_rows, layout.length
    turn = 0
    factor = scale * LOG2E
    lane = lax.broadcasted_iota(jnp.int32, (1, LANES), 1)
    query = query_ref[...]
    keys = jnp.concatenate([ref[...] for ref in key_refs], axis=0)
    values = jnp.concatenate([ref[...] for ref in value_refs], axis=0)
    members = members_ref[...]
    kinds = kinds_ref[...]
    tables = tables_ref[...]
    ones = jnp.ones((length, LANES), jnp.bfloat16)

    @pl.when(pair == 0)
    def _():
        log_ref[...] = jnp.zeros_like(log_ref)

    for side in range(2):
        key_columns = jnp.concatenate([half_of(keys, lane, side), members], axis=1)
        value_columns = jnp.concatenate([half_of(values, lane, side), ones], axis=1)
        extra = group_columns(kinds, tables, side).astype(jnp.bfloat16)
        query_columns = jnp.concatenate([query, extra], axis=1)
        table_row = tables[8 * side : 8 * side + 1]
        for start, stop in row_blocks(rows, 256):
            size = stop - start
            scores = all_scores.at[turn % 2]
            turn += 1
            scores[0:size, 0:length] = wide_dot(query_columns[start:stop], key_columns, NT)
            for tile in range(start // LANES, -(-stop // LANES)):
                first, final = tile * LANES, min(tile * LANES + LANES, rows)
                for slot in range(3):
                    other = tile + slot - 1
                    if other >= layout.query_tiles:
                        continue
                    low, high = first, final
                    if slot == 0:
                        high = min(first + 32, final)
                    if slot == 2:
                        low = first + LANES - 32
                    if low >= high:
                        continue
                    place = layout.tile_start(other)
                    width = min(LANES, length - place)
                    bins = bins_ref[low:high, slot * LANES : (slot + 1) * LANES]
                    bias = look_up(table_row, bins)[:, :width]
                    scores[low - start : high - start, place : place + width] += bias
            block = scores[0:size, 0:length]
            top = jnp.max(block, axis=1, keepdims=True)
            weights = jnp.exp2(((block - top) * factor).astype(jnp.bfloat16))
            sums = wide_dot(weights, value_columns)
            total = sums[:, LANES:]
            result = sums[:, :LANES] / total
            if side == 0:
                out_ref[start:stop] = result
            else:
                out_ref[start:stop] += result
            log_total = top + jnp.log(total) * (1.0 / scale)
            log_ref[start:stop] = jnp.where(
                lane == 2 * pair + side, log_total, log_ref[start:stop]
            )


def backward_kernel(layout, scale, first_pair, *refs):
    count = len(layout.pieces)
    query_ref, grad_ref, out_ref, log_ref = refs[:4]
    key_refs = refs[4 : 4 + count]
    value_refs = refs[4 + count : 4 + 2 * count]
    rest = refs[4 + 2 * count :]
    members_ref, kinds_ref, bins_ref, places_ref, tables_ref = rest[:5]
    members_turned_ref, kinds_turned_ref = rest[5:7]
    grad_query_ref = rest[7]
    grad_pair_refs = rest[8 : 8 + count]
    grad_table_ref = rest[8 + count]
    query_wide, grad_wide, query_turned, grad_turned = rest[9 + count : 13 + count]
    all_scores, slopes_low, probs_low = rest[13 + count :]
    pair = pl.program_id(1) + first_pair
    rows, length, padded = layout.block_rows, layout.length, layout.padded
    factor = scale * LOG2E
    lane = lax.broadcasted_iota(jnp.int32, (1, LANES), 1)
    keys = jnp.concatenate([ref[...] for ref in key_refs], axis=0)
    values = jnp.concatenate([ref[...] for ref in value_refs], axis=0)
    members = members_ref[...]
    kinds = kinds_ref[...]
    tables = tables_ref[...]
    query = query_ref[...]
    grad = grad_ref[...]
    grad_full = grad.astype(jnp.float32)
    product = grad_full * out_ref[...]
    log_all = log_ref[...]
    tail = 2 * layout.groups
    ones = jnp.broadcast_to(jnp.where(lane < 3, 1.0, 0.0), (length, LANES)).astype(jnp.bfloat16)

    def three_parts(values):
        upper = values.astype(jnp.bfloat16).astype(jnp.float32)
        values = values - upper
        middle = values.astype(jnp.bfloat16).astype(jnp.float32)
        return upper, middle, values - middle

    def in_lanes(parts, first):
        return jnp.where(
            lane == first,
            parts[0],
            jnp.where(lane == first + 1, parts[1], jnp.where(lane == first + 2, parts[2], 0.0)),
        )

    if padded > rows:
        for ref in (query_wide, grad_wide):
            for side in range(2):
                ref[side, rows:padded] = jnp.zeros((padded - rows, ref.shape[2]), jnp.bfloat16)
        for ref in (query_turned, grad_turned):
            ref[:, rows:padded] = jnp.zeros((LANES, padded - rows), jnp.bfloat16)
    query_turned[:, 0:rows] = query.T
    grad_turned[:, 0:rows] = grad.T
    for side in range(2):
        log_total = jnp.sum(
            jnp.where(lane == 2 * pair + side, log_all, 0.0), axis=1, keepdims=True
        )
        extra = group_columns(kinds, tables, side) + in_lanes(three_parts(log_total), tail)
        query_wide[side, 0:rows, 0:LANES] = query
        query_wide[side, 0:rows, LANES:] = extra.astype(jnp.bfloat16)
        delta = jnp.sum(half_of(product, lane, side), axis=1, keepdims=True)
        grad_wide[side, 0:rows, 0:LANES] = grad
        grad_wide[side, 0:rows, LANES:] = in_lanes(three_parts(-delta), 0).astype(jnp.bfloat16)

    key_columns = [
        jnp.concatenate([half_of(keys, lane, side), members], axis=1) for side in range(2)
    ]
    value_columns = [
        jnp.concatenate([half_of(values, lane, side), ones], axis=1) for side in range(2)
    ]
    inner_sums = [jnp.zeros((1, LANES), jnp.float32) for _ in range(2)]
    low_sums = [jnp.zeros((1, LANES), jnp.float32) for _ in range(2)]
    high_sums = [jnp.zeros((1, LANES), jnp.float32) for _ in range(2)]
    reach_tiles = list(range(layout.query_tiles)) + [-1]

    def put(which, start, stop, result):
        begin = 0
        for ref, size in zip(grad_pair_refs, layout.pieces):
            low, high = max(start, begin), min(stop, begin + size)
            if low < high:
                ref[which, low - begin : high - begin] = result[low - start : high - start]
            begin += size

    for start, stop in row_blocks(length, 384):
        size = stop - start
        for side in range(2):
            table_row = tables[8 * side : 8 * side + 1]
            scores = all_scores.at[side]
            scores[0:size] = wide_dot(key_columns[side][start:stop], query_wide[side], NT)
            near = []
            for index, tile in enumerate(reach_tiles):
                place = layout.tile_start(tile)
                if start <= place < stop:
                    near.append((index, tile, place, min(place + LANES, length)))
            for index, tile, place, final in near:
                for slot in range(3):
                    other = tile + slot - 1
                    if not 0 <= other < layout.query_tiles:
                        continue
                    bins = bins_ref[
                        index * LANES : index * LANES + final - place,
                        slot * LANES : (slot + 1) * LANES,
                    ]
                    scores[
                        place - start : final - start, other * LANES : (other + 1) * LANES
                    ] += look_up(table_row, bins)
            probs = jnp.exp2((scores[0:size] * factor).astype(jnp.bfloat16))
            grad_probs = wide_dot(value_columns[side][start:stop], grad_wide[side], NT)
            probs_low[side, start:stop] = probs
            slopes_low[side, start:stop] = probs * grad_probs.astype(jnp.bfloat16)
            for index, tile, place, final in near:
                for slot in range(3):
                    other = tile + slot - 1
                    if not 0 <= other < layout.query_tiles:
                        continue
                    bins = bins_ref[
                        index * LANES : index * LANES + final - place,
                        slot * LANES : (slot + 1) * LANES,
                    ]
                    cut = slopes_low[side, place:final, other * LANES : (other + 1) * LANES].astype(
                        jnp.float32
                    )
                    low_sums[side] += jnp.sum(
                        jnp.where(bins == 0, cut, 0.0), axis=0, keepdims=True
                    )
                    high_sums[side] += jnp.sum(
                        jnp.where(bins == 2 * (NEAR + 1), cut, 0.0), axis=0, keepdims=True
                    )
                for half in range(2):
                    begin, end = half * 64, min(half * 64 + 64, final - place)
                    if begin >= end:
                        continue
                    base = 0 if tile < 0 else tile - 1 + half
                    where = places_ref[index * LANES + begin : index * LANES + end]
                    spot = where & (LANES - 1)
                    for step in range(2):
                        other = base + step
                        if not 0 <= other < layout.query_tiles or (tile < 0 and step):
                            continue
                        cut = slopes_low[
                            side, place + begin : place + end, other * LANES : (other + 1) * LANES
                        ].astype(jnp.float32)
                        picked = jnp.take_along_axis(cut, spot, axis=1, mode="promise_in_bounds")
                        picked = jnp.where((where >> 7) == step, picked, 0.0)
                        inner_sums[side] += jnp.sum(picked, axis=0, keepdims=True)

    keys_turned = keys.T
    grad_keys, grad_values, grad_queries = [], [], []
    kinds_turned = kinds_turned_ref[...]
    for side in range(2):
        cut = slice(64 * side, 64 * side + 64)
        grad_values.append(wide_dot(grad_turned[cut], probs_low[side], NT))
        grad_keys.append(wide_dot(query_turned[cut], slopes_low[side], NT))
        left = jnp.concatenate([keys_turned[cut], members_turned_ref[...]], axis=0)
        both = wide_dot(left, slopes_low[side])
        grad_queries.append(both[:64])
        sums = both[64:]

        def total(kind):
            return jnp.sum(jnp.where(kinds_turned == kind, sums, 0.0))

        right = total(RIGHT) + jnp.sum(high_sums[side])
        left = total(LEFT) + jnp.sum(low_sums[side])
        apart = total(APART)
        grad_table_ref[side : side + 1] = jnp.where(
            lane == 0,
            left,
            jnp.where(
                lane == 2 * (NEAR + 1),
                right,
                jnp.where(lane == 2 * (NEAR + 1) + 1, apart, inner_sums[side]),
            ),
        )
    put(0, 0, length, (jnp.concatenate(grad_keys, axis=0) * scale).T.astype(jnp.bfloat16))
    put(1, 0, length, jnp.concatenate(grad_values, axis=0).T.astype(jnp.bfloat16))
    turned = jnp.concatenate(grad_queries, axis=0) * scale
    grad_query_ref[...] = turned.T[0:rows].astype(jnp.bfloat16)


def tile_columns(rows, offset=0):
    return pl.BlockSpec((None, rows, LANES), lambda crop, pair: (crop, 0, pair + offset))


def per_crop(rows, width):
    return pl.BlockSpec((None, rows, width), lambda crop, pair: (crop, 0, 0))


def kernel_params():
    return pltpu.CompilerParams(
        vmem_limit_bytes=VMEM_BYTES, dimension_semantics=("arbitrary", "arbitrary")
    )


def attention_forward(layout, scale, projected, key_values, members, kinds, bins, tables):
    crops, rows, _ = projected.shape
    pairs = tables.shape[0]
    specs = [tile_columns(rows)]
    operands = [projected]
    for place in (1, 2):
        for piece in key_values:
            specs.append(tile_columns(piece[0].shape[1], piece[place]))
            operands.append(piece[0])
    specs += [
        per_crop(layout.length, LANES),
        per_crop(rows, LANES),
        per_crop(layout.padded, 3 * LANES),
        pl.BlockSpec((None, 16, LANES), lambda crop, pair: (pair, 0, 0)),
    ]
    flops = 2 * crops * pairs * 2 * rows * layout.length * 256 * 2
    return pl.pallas_call(
        functools.partial(forward_kernel, layout, scale),
        grid=(crops, pairs),
        in_specs=specs,
        out_specs=(tile_columns(rows), per_crop(rows, LANES)),
        out_shape=(
            jax.ShapeDtypeStruct((crops, rows, pairs * LANES), jnp.float32),
            jax.ShapeDtypeStruct((crops, rows, LANES), jnp.float32),
        ),
        scratch_shapes=[pltpu.VMEM((2, 256, layout.wide), jnp.float32)],
        compiler_params=kernel_params(),
        cost_estimate=pl.CostEstimate(
            flops=flops,
            bytes_accessed=12 * crops * rows * pairs * LANES,
            transcendentals=crops * pairs * 2 * rows * layout.length,
        ),
        name="attention_forward",
    )(*operands, members, kinds, bins, tables)


def attention_backward(
    layout,
    scale,
    first_pair,
    pairs,
    projected,
    grad_out,
    attended,
    logs,
    key_values,
    members,
    kinds,
    bins,
    places,
    members_turned,
    kinds_turned,
    tables,
):
    crops, rows, _ = projected.shape
    specs = [tile_columns(rows, first_pair)] * 3 + [per_crop(rows, LANES)]
    operands = [projected, grad_out, attended, logs]
    for place in (1, 2):
        for piece in key_values:
            specs.append(tile_columns(piece[0].shape[1], piece[place] + first_pair))
            operands.append(piece[0])
    specs += [
        per_crop(layout.length, LANES),
        per_crop(rows, LANES),
        per_crop(bins.shape[1], 3 * LANES),
        per_crop(places.shape[1], LANES),
        pl.BlockSpec((None, 16, LANES), lambda crop, pair: (pair + first_pair, 0, 0)),
        per_crop(64, layout.length),
        per_crop(64, layout.padded),
    ]
    out_specs = [tile_columns(rows)]
    out_shapes = [jax.ShapeDtypeStruct((crops, rows, pairs * LANES), jnp.bfloat16)]
    for piece in key_values:
        size = piece[0].shape[1]
        out_specs.append(
            pl.BlockSpec((None, 2, size, LANES), lambda crop, pair: (crop, 0, 0, pair))
        )
        out_shapes.append(jax.ShapeDtypeStruct((crops, 2, size, pairs * LANES), jnp.bfloat16))
    out_specs.append(pl.BlockSpec((None, None, 8, LANES), lambda crop, pair: (crop, pair, 0, 0)))
    out_shapes.append(jax.ShapeDtypeStruct((crops, pairs, 8, LANES), jnp.float32))
    padded, block = layout.padded, 384
    return pl.pallas_call(
        functools.partial(backward_kernel, layout, scale, first_pair),
        grid=(crops, pairs),
        in_specs=specs,
        out_specs=tuple(out_specs),
        out_shape=tuple(out_shapes),
        scratch_shapes=[
            pltpu.VMEM((2, padded, 2 * LANES), jnp.bfloat16),
            pltpu.VMEM((2, padded, 2 * LANES), jnp.bfloat16),
            pltpu.VMEM((LANES, padded), jnp.bfloat16),
            pltpu.VMEM((LANES, padded), jnp.bfloat16),
            pltpu.VMEM((2, block, padded), jnp.float32),
            pltpu.VMEM((2, layout.length, padded), jnp.bfloat16),
            pltpu.VMEM((2, layout.length, padded), jnp.bfloat16),
        ],
        compiler_params=kernel_params(),
        cost_estimate=pl.CostEstimate(
            flops=2 * crops * pairs * 2 * rows * layout.length * 256 * 5,
            bytes_accessed=20 * crops * rows * pairs * LANES,
            transcendentals=crops * pairs * 2 * rows * layout.length,
        ),
        name="attention_backward",
    )(*operands, members, kinds, bins, places, tables, members_turned, kinds_turned)


def sigmoid(values):
    return 0.5 * jnp.tanh(0.5 * values) + 0.5


def each_strip(rows, body, size=16):
    count = rows // size
    group = max(number for number in range(1, 9) if count % number == 0)

    @pl.loop(0, count // group)
    def _(index):
        for part in range(group):
            body(pl.ds(pl.multiple_of((index * group + part) * size, size), size))


def fold_rows(values):
    return jnp.sum(values.reshape(values.shape[0] // 8, 8, values.shape[1]), axis=0)


def feed_kernel(split, chunks, here_ref, *refs):
    (attended_ref, tokens_ref, upstream_ref, normed_a_ref, mod_ref, gate_weight_ref, output_ref) = refs[:7]
    gate_ref, up_ref, down_ref = refs[7:10]
    layer_ref, grad_middle_ref, grad_att_ref, grad_pre_ref, sums_ref = refs[10:15]
    grads = refs[15:-12]
    gated, grad_ff, normed, branch, middle, total, grad_normed, hidden, both, grad_branch = refs[-12:-2]
    gate_pre, turned = refs[-2:]
    step = pl.program_id(0)
    here = here_ref[0]
    rows, width = tokens_ref.shape
    size = gate_ref.shape[1]
    strip = 112 if rows % 112 == 0 else 64
    strips = rows // strip
    shift_f, scale_f = mod_ref[3:4], mod_ref[4:5]
    open_a, open_f = sigmoid(mod_ref[2:3]), sigmoid(mod_ref[5:6])

    def strip_of(index):
        return pl.ds(pl.multiple_of(index * strip, strip), strip)

    def norm_of(values):
        mean_value = jnp.mean(values, axis=1, keepdims=True)
        centred = values - mean_value
        spread = jnp.mean(centred * centred, axis=1, keepdims=True)
        root = lax.rsqrt(spread + 1e-06)
        return centred * root, root

    @pl.when(step == 0)
    def _():
        gate_pre[...] = wide_dot(normed_a_ref[...], gate_weight_ref[...])

        @pl.loop(0, strips)
        def _(index):
            cut = strip_of(index)
            gated[cut] = (attended_ref[cut] * sigmoid(gate_pre[cut])).astype(jnp.bfloat16)
            grad_ff[cut] = (upstream_ref[cut].astype(jnp.float32) * open_f).astype(jnp.bfloat16)

        branch[...] = wide_dot(gated[...], output_ref[...])

        @pl.loop(0, strips)
        def _(index):
            cut = strip_of(index)
            values = tokens_ref[cut].astype(jnp.float32) + open_a * branch[cut]
            middle[cut] = values
            normed[cut] = (norm_of(values)[0] * (1.0 + scale_f) + shift_f).astype(jnp.bfloat16)
            total[cut] = jnp.zeros((strip, width), jnp.float32)
            grad_normed[cut] = jnp.zeros((strip, width), jnp.float32)

        turned[...] = normed[...].T

    block = rows if rows <= 384 else rows // 2
    for start in range(0, rows, block):
        cut = slice(start, start + block)
        before = wide_dot(normed[cut], gate_ref[...])
        lifted = wide_dot(normed[cut], up_ref[...])
        grad_hidden = wide_dot(grad_ff[cut], down_ref[...], NT)
        switch = sigmoid(before)
        silu = before * switch
        part = (silu * lifted).astype(jnp.bfloat16)
        hidden[cut] = part
        grad_up = (grad_hidden * silu).astype(jnp.bfloat16)
        grad_gate = (grad_hidden * lifted * (switch + silu * (1.0 - switch))).astype(jnp.bfloat16)
        both[cut, :size] = grad_gate
        both[cut, size:] = grad_up
        total[cut] += wide_dot(part, down_ref[...])
        grad_normed[cut] += wide_dot(grad_gate, gate_ref[...], NT) + wide_dot(
            grad_up, up_ref[...], NT
        )

    pair = wide_dot(turned[...], both[...]).astype(jnp.bfloat16)
    if split:
        gate_send, gate_keep, up_send, up_keep, down_send, down_keep, small_send, small_keep = grads
        half = width // 2
        away = pl.ds(pl.multiple_of((1 - here) * half, LANES), half)
        home = pl.ds(pl.multiple_of(here * half, LANES), half)
        down_send[...] = wide_dot(hidden[...], grad_ff[:, away], TN).astype(jnp.bfloat16)
        down_keep[...] = wide_dot(hidden[...], grad_ff[:, home], TN).astype(jnp.bfloat16)

        @pl.when(step < chunks // 2)
        def _():
            gate_send[...] = pair[:, :size]
            up_send[...] = pair[:, size:]

        @pl.when(step >= chunks // 2)
        def _():
            gate_keep[...] = pair[:, :size]
            up_keep[...] = pair[:, size:]
    else:
        gate_all, up_all, down_all, small_all = grads
        gate_all[...] = pair[:, :size]
        up_all[...] = pair[:, size:]
        down_all[...] = wide_dot(hidden[...], grad_ff[...], TN).astype(jnp.bfloat16)

    @pl.when(step == chunks - 1)
    def _():
        def finish(index, sums):
            gate_f_sum, shift_sum, scale_sum, gate_a_sum = sums
            cut = strip_of(index)
            values = middle[cut]
            fed = total[cut]
            upstream = upstream_ref[cut].astype(jnp.float32)
            layer_ref[cut] = (values + open_f * fed).astype(jnp.bfloat16)
            normal, root = norm_of(values)
            grad = grad_normed[cut]
            scaled = grad * (1.0 + scale_f)
            grad_middle = upstream + root * (
                scaled
                - jnp.mean(scaled, axis=1, keepdims=True)
                - normal * jnp.mean(scaled * normal, axis=1, keepdims=True)
            )
            grad_middle_ref[cut] = grad_middle
            grad_branch[cut] = (grad_middle * open_a).astype(jnp.bfloat16)
            return (
                gate_f_sum + fold_rows(upstream * fed),
                shift_sum + fold_rows(grad),
                scale_sum + fold_rows(grad * normal),
                gate_a_sum + fold_rows(grad_middle * branch[cut]),
            )

        zero = jnp.zeros((8, width), jnp.float32)
        sums = lax.fori_loop(0, strips, finish, (zero, zero, zero, zero))
        gate_f_sum, shift_sum, scale_sum, gate_a_sum = [
            jnp.sum(value, axis=0, keepdims=True) for value in sums
        ]
        none = jnp.zeros((1, width), jnp.float32)
        sums_ref[...] = jnp.concatenate(
            [
                none,
                none,
                gate_a_sum * open_a * (1.0 - open_a),
                shift_sum,
                scale_sum,
                gate_f_sum * open_f * (1.0 - open_f),
                none,
                none,
            ],
            axis=0,
        )
        total[...] = wide_dot(grad_branch[...], output_ref[...], NT)

        @pl.loop(0, strips)
        def _(index):
            cut = strip_of(index)
            grad_gated = total[cut]
            opened = sigmoid(gate_pre[cut])
            grad_att_ref[cut] = (grad_gated * opened).astype(jnp.bfloat16)
            grad_pre_ref[cut] = (
                grad_gated * attended_ref[cut] * (opened * (1.0 - opened))
            ).astype(jnp.bfloat16)

        if split:
            for side, ref in ((away, small_send), (home, small_keep)):
                ref[:, :half] = wide_dot(gated[...], grad_branch[:, side], TN).astype(jnp.bfloat16)
                ref[:, half:] = wide_dot(normed_a_ref[...], grad_pre_ref[:, side], TN).astype(
                    jnp.bfloat16
                )
        else:
            small_all[:, :width] = wide_dot(gated[...], grad_branch[...], TN).astype(jnp.bfloat16)
            small_all[:, width:] = wide_dot(normed_a_ref[...], grad_pre_ref[...], TN).astype(
                jnp.bfloat16
            )


def feed_layer(
    split, here, attended, tokens, upstream, normed_a, mod_rows, gate_weight, output_weight, feed_gate, feed_up, feed_down
):
    rows, width = tokens.shape
    inner = feed_gate.shape[1]
    size = 512
    chunks = inner // size
    half = chunks // 2

    def turn(step, here_ref):
        return (step + half * (1 - here_ref[0])) % chunks if split else step

    def fixed(shape):
        return pl.BlockSpec(shape, lambda step, here_ref: (0, 0), pipeline_mode=pl.Buffered(1))

    def columns(step, here_ref):
        return (0, turn(step, here_ref))

    def strips(step, here_ref):
        return (turn(step, here_ref), 0)

    whole = (rows, width)
    in_specs = [fixed(whole)] * 4 + [
        fixed((8, width)),
        fixed((width, width)),
        fixed((width, width)),
        pl.BlockSpec((width, size), columns),
        pl.BlockSpec((width, size), columns),
        pl.BlockSpec((size, width), strips),
    ]
    out_specs = [fixed(whole)] * 4 + [fixed((8, width))]
    bf16, f32 = jnp.bfloat16, jnp.float32
    out_shapes = [(whole, bf16), (whole, f32), (whole, bf16), (whole, bf16), ((8, width), f32)]
    if split:
        first = pl.BlockSpec((width, size), lambda step, here_ref: (0, jnp.minimum(step, half - 1)))
        second = pl.BlockSpec((width, size), lambda step, here_ref: (0, jnp.maximum(step - half, 0)))
        out_specs += [first, second, first, second]
        out_shapes += [((width, inner // 2), bf16)] * 4
        out_specs += [pl.BlockSpec((size, width // 2), strips)] * 2
        out_shapes += [((inner, width // 2), bf16)] * 2
        out_specs += [fixed((width, width))] * 2
        out_shapes += [((width, width), bf16)] * 2
    else:
        out_specs += [pl.BlockSpec((width, size), columns)] * 2
        out_shapes += [((width, inner), bf16)] * 2
        out_specs += [pl.BlockSpec((size, width), strips), fixed((width, 2 * width))]
        out_shapes += [((inner, width), bf16), ((width, 2 * width), bf16)]
    return pl.pallas_call(
        functools.partial(feed_kernel, split, chunks),
        grid_spec=pltpu.PrefetchScalarGridSpec(
            num_scalar_prefetch=1,
            grid=(chunks,),
            in_specs=in_specs,
            out_specs=tuple(out_specs),
            scratch_shapes=[
                pltpu.VMEM(whole, bf16),
                pltpu.VMEM(whole, bf16),
                pltpu.VMEM(whole, bf16),
                pltpu.VMEM(whole, f32),
                pltpu.VMEM(whole, f32),
                pltpu.VMEM(whole, f32),
                pltpu.VMEM(whole, f32),
                pltpu.VMEM((rows, size), bf16),
                pltpu.VMEM((rows, 2 * size), bf16),
                pltpu.VMEM(whole, bf16),
                pltpu.VMEM(whole, f32),
                pltpu.VMEM((width, rows), bf16),
            ],
        ),
        out_shape=tuple(jax.ShapeDtypeStruct(shape, kind) for shape, kind in out_shapes),
        compiler_params=pltpu.CompilerParams(vmem_limit_bytes=VMEM_BYTES),
        cost_estimate=pl.CostEstimate(
            flops=2 * rows * width * (9 * inner + 5 * width),
            bytes_accessed=12 * width * inner + 24 * rows * width,
            transcendentals=2 * rows * inner,
        ),
        name="feed_layer",
    )(
        jnp.reshape(here, (1,)).astype(jnp.int32),
        attended,
        tokens,
        upstream,
        normed_a,
        mod_rows,
        gate_weight,
        output_weight,
        feed_gate,
        feed_up,
        feed_down,
    )


MASKS = {"u": 8, "v": 4, "y": 2, "x": 1}


def exchange(values, mask):
    return lax.ppermute(values, "crop", [(i, i ^ mask) for i in range(16)])


def swap_res(values):
    return lax.ppermute(values, "res", [(0, 1), (1, 0)])


def tie(*values):
    return lax.optimization_barrier(values)


def add_low(former, latter, kind=jnp.bfloat16):
    return (former.astype(jnp.float32) + latter.astype(jnp.float32)).astype(kind)


def stage_kernel(plans, bits_ref, *refs):
    inputs = refs[: sum(plan["count"] for plan in plans)]
    outputs = list(refs[len(inputs) :])
    for plan in plans:
        mine, inputs = inputs[: plan["count"]], inputs[plan["count"] :]
        out_ref = None if plan["apart"] else outputs[0]
        if not plan["apart"] and plan["merge"] is None:
            outputs.pop(0)
        for column, width, own in plan["parts"]:
            result = outputs.pop(0) if plan["apart"] else out_ref
            target = 0 if plan["apart"] else column
            lead_sizes = () if plan["merge"] is not None else result.shape[:-2]
            for lead in itertools.product(*[range(size) for size in lead_sizes]):
                for first in range(0, plan["rows"], 16):
                    cut = (*lead, slice(first, first + 16))
                    across = slice(column, column + width)
                    total = None
                    for index in own:
                        value = mine[index][(*cut, slice(0, width))].astype(jnp.float32)
                        total = value if total is None else total + value
                    for index in plan["spans"]:
                        total = total + mine[index][(*cut, across)].astype(jnp.float32)
                    fold, local = first // plan["block"], first % plan["block"]
                    if plan["folds"]:
                        value = mine[plan["folds"][fold]][local : local + 16, across]
                        total = total + value.astype(jnp.float32)
                    if plan["merge"] is None:
                        result[(*cut, slice(target, target + width))] = total.astype(result.dtype)
                    else:
                        begin = plan["merge"] + fold * plan["wide"] + column
                        result[local : local + 16, begin : begin + width] = total.astype(result.dtype)


class Halving:
    def __init__(self, streams, orders):
        self.streams = streams
        self.orders = [list(order) for order in orders]
        self.past = [[] for _ in orders]
        self.came = [[] for _ in orders]

    def stage(self, last=False, merge=False, merged=None):
        index = lax.axis_index("crop")
        bits = scalars(*[(index // mask) % 2 for mask in MASKS.values()])
        self.masks, plans, specs, operands, out_specs, out_shapes = [], [], [], [], [], []
        left = 0 if last else len(self.orders[0]) - 1
        fewest = min(parts[0][0][0].shape[0] for parts in self.streams) // 16
        begin = 0
        steps = {3: 4, 2: 2}.get(left, 1)
        for stream, (parts, order, past) in enumerate(zip(self.streams, self.orders, self.past)):
            now = None if last else order.pop(0)
            rest = [axis for axis in MASKS if axis in order]

            def spec_of(axes, rows, width, block, now=now, rest=rest):
                def index_map(step, bits_ref):
                    places = []
                    for axis in axes:
                        bit = bits_ref[list(MASKS).index(axis)]
                        if axis == now:
                            places.append(1 - bit)
                        elif axis not in rest:
                            places.append(bit)
                        elif axis == rest[0] and steps > 1:
                            places.append(step // (steps // 2))
                        elif len(rest) > 1 and axis == rest[1] and steps > 2:
                            places.append(step % 2)
                        else:
                            places.append(0)
                    return (*places, 0, block)

                sizes = [
                    2
                    if axis in rest
                    and not (axis == rest[0] and steps > 1)
                    and not (len(rest) > 1 and axis == rest[1] and steps > 2)
                    else None
                    for axis in axes
                ]
                return pl.BlockSpec((*sizes, rows, width), index_map)

            column = 0
            rows = parts[0][0][0].shape[0] // 16
            wide = sum(width for _, _, width in parts)
            plan = {
                "parts": [],
                "spans": [],
                "folds": [],
                "count": 0,
                "apart": last,
                "rows": rows,
                "block": fewest,
                "wide": wide,
                "merge": begin if merge else None,
            }
            for arrays, block, width in parts:
                own = []
                for value in arrays:
                    operands.append(value.reshape(2, 2, 2, 2, rows, value.shape[1]))
                    specs.append(spec_of(list(MASKS), rows, width, block))
                    own.append(plan["count"])
                    plan["count"] += 1
                plan["parts"].append((column, width, own))
                column += width
            for axes, value in self.came[stream]:
                operands.append(value.reshape(*[2] * len(axes), rows, column))
                specs.append(spec_of(axes, rows, column, 0))
                plan["spans"].append(plan["count"])
                plan["count"] += 1
            if merged is not None:
                for fold in range(rows // fewest):
                    place = (begin + fold * wide) // wide
                    operands.append(merged)
                    specs.append(
                        pl.BlockSpec((fewest, wide), lambda step, bits_ref, place=place: (0, place))
                    )
                    plan["folds"].append(plan["count"])
                    plan["count"] += 1
            begin += wide * (rows // fewest)
            plans.append(plan)
            if last:
                for _, width, _ in plan["parts"]:
                    out_specs.append(pl.BlockSpec((rows, width), lambda step, bits_ref: (0, 0)))
                    out_shapes.append(jax.ShapeDtypeStruct((rows, width), jnp.float32))
            else:
                past.append(now)
                self.masks.append(MASKS[now])
                if not merge:
                    out_specs.append(spec_of(rest, rows, column, 0))
                    out_shapes.append(
                        jax.ShapeDtypeStruct((*[2] * len(rest), rows, column), jnp.bfloat16)
                    )
        if merge:
            out_specs.append(pl.BlockSpec((fewest, begin), lambda step, bits_ref: (0, 0)))
            out_shapes.append(jax.ShapeDtypeStruct((fewest, begin), jnp.bfloat16))
        self.axes = [[axis for axis in MASKS if axis in order] for order in self.orders]
        results = pl.pallas_call(
            functools.partial(stage_kernel, plans),
            grid_spec=pltpu.PrefetchScalarGridSpec(
                num_scalar_prefetch=1, grid=(steps,), in_specs=specs, out_specs=tuple(out_specs)
            ),
            out_shape=tuple(out_shapes),
            compiler_params=pltpu.CompilerParams(vmem_limit_bytes=VMEM_BYTES),
            cost_estimate=pl.CostEstimate(
                flops=sum(4 * math.prod(shape.shape) for shape in out_shapes),
                bytes_accessed=sum(8 * math.prod(shape.shape) for shape in out_shapes),
                transcendentals=0,
            ),
            name="halving_stage",
        )(bits, *operands)
        if merge or last:
            return list(results)
        return [value.reshape(-1, value.shape[-1]) for value in results]

    def send(self, values):
        return [exchange(value, mask) for value, mask in zip(values, self.masks)]

    def take(self, values):
        for came, axes, value in zip(self.came, self.axes, values):
            came.append((axes, value))


def share_columns(values, parts):
    if parts == 1:
        return values.astype(jnp.bfloat16)
    return lax.psum_scatter(values.astype(jnp.bfloat16), "res", scatter_dimension=1, tiled=True)


def scatter_crops(values):
    return lax.psum_scatter(values, "crop", scatter_dimension=0, tiled=True).astype(jnp.float32)


def gather_crops(values, crop_parts):
    if crop_parts != 16:
        return lax.all_gather(values, "crop", axis=0, tiled=True)
    index = lax.axis_index("crop")
    for mask in (1, 2, 4, 8):
        other = exchange(values, mask)
        low = (index // mask) % 2 == 0
        values = jnp.concatenate(
            [jnp.where(low, values, other), jnp.where(low, other, values)], axis=0
        )
    return values


def sum_res(values, parts):
    if parts == 1:
        return values
    if parts != 2:
        return lax.psum(values, "res")
    return values + swap_res(values)


PACK = 1152
SIDE = 384


def whole_vmem(count):
    return [pl.BlockSpec(memory_space=pltpu.VMEM)] * count


def scalars(*values):
    return jnp.stack([jnp.asarray(value, jnp.int32) for value in values])


def local_call(kernel, numbers, operands, shapes, name, flops=0):
    return pl.pallas_call(
        kernel,
        in_specs=[pl.BlockSpec(memory_space=pltpu.SMEM)] + whole_vmem(len(operands)),
        out_specs=tuple(whole_vmem(len(shapes))),
        out_shape=tuple(jax.ShapeDtypeStruct(shape, kind) for shape, kind in shapes),
        compiler_params=pltpu.CompilerParams(vmem_limit_bytes=VMEM_BYTES),
        cost_estimate=pl.CostEstimate(
            flops=flops,
            bytes_accessed=sum(value.size * value.dtype.itemsize for value in operands)
            + sum(4 * math.prod(shape) for shape, _ in shapes),
            transcendentals=0,
        ),
        name=name,
    )(numbers, *operands)


def projection_kernel(counts, here_ref, normed_ref, *refs):
    calls = len(counts)
    parts, (joined_ref, send_ref, keep_ref) = refs[: 3 * calls], refs[3 * calls :]
    width = joined_ref.shape[1] // 3
    column = 0
    for call, pairs in enumerate(counts):
        size = pairs * LANES
        query_ref, own_ref, came_ref = parts[3 * call : 3 * call + 3]
        joined_ref[:, column : column + size] = query_ref[...]
        for start in range(0, joined_ref.shape[0], 16):
            cut = slice(start, start + 16)
            for which in range(2):
                first = (1 + which) * width + column
                joined_ref[cut, first : first + size] = add_low(
                    own_ref[which, cut], came_ref[which, cut]
                )
        column += size
    half = send_ref.shape[1]
    for side, ref in ((1 - here_ref[0], send_ref), (here_ref[0], keep_ref)):
        columns = pl.ds(pl.multiple_of(side * half, LANES), half)
        ref[...] = wide_dot(normed_ref[...], joined_ref[:, columns], TN).astype(jnp.bfloat16)


def projection_gradient(here, normed_a, calls):
    rows, width = normed_a.shape
    counts = [call[0].shape[-1] // LANES for call in calls]
    return local_call(
        functools.partial(projection_kernel, counts),
        scalars(here),
        [normed_a] + [value for call in calls for value in call],
        [
            ((rows, 3 * width), jnp.bfloat16),
            ((width, 3 * width // 2), jnp.bfloat16),
            ((width, 3 * width // 2), jnp.bfloat16),
        ],
        "projection_gradient",
        6 * rows * width * width,
    )


def finish_kernel(counts, joined_ref, weight_ref, pre_ref, gate_ref, tokens_ref, middle_ref, mod_ref, *refs):
    feed_sums_ref, extra_ref = refs[:2]
    table_refs = refs[2 : 2 + len(counts)]
    out_ref, pack_ref, total, folded = refs[2 + len(counts) :]
    step = pl.program_id(0)
    rows, width = tokens_ref.shape
    part = wide_dot(joined_ref[...], weight_ref[...], NT)

    @pl.when(step == 0)
    def _():
        total[...] = part + wide_dot(pre_ref[...], gate_ref[...], NT)

    @pl.when(step > 0)
    def _():
        total[...] += part

    @pl.when(step == pl.num_programs(0) - 1)
    def _():
        scale = mod_ref[1:2]
        folded[...] = jnp.zeros_like(folded)

        def finish(cut):
            values = tokens_ref[cut].astype(jnp.float32)
            centred = values - jnp.mean(values, axis=1, keepdims=True)
            root = lax.rsqrt(jnp.mean(centred * centred, axis=1, keepdims=True) + 1e-06)
            normal = centred * root
            grad = total[cut]
            folded[0] += fold_rows(grad)
            folded[1] += fold_rows(grad * normal)
            scaled = grad * (1.0 + scale)
            out_ref[cut] = (
                middle_ref[cut]
                + root
                * (
                    scaled
                    - jnp.mean(scaled, axis=1, keepdims=True)
                    - normal * jnp.mean(scaled * normal, axis=1, keepdims=True)
                )
            ).astype(jnp.bfloat16)

        each_strip(rows, finish)
        shift_sum, scale_sum = folded[0], folded[1]
        heads = []
        for ref, pairs in zip(table_refs, counts):
            for pair in range(pairs):
                heads += [ref[pair, 0:1], ref[pair, 1:2]]

        def upper_of(values):
            return values.astype(jnp.bfloat16).astype(jnp.float32)

        rests = [head - upper_of(head) for head in heads]
        count = width // LANES
        left = [
            jnp.sum(shift_sum, axis=0, keepdims=True),
            jnp.sum(scale_sum, axis=0, keepdims=True),
            feed_sums_ref[2:6],
        ]
        left += [
            jnp.concatenate(rests[i : i + count], axis=1) for i in range(0, len(heads), count)
        ]
        right = [jnp.concatenate(heads[3 * i : 3 * i + 3], axis=1) for i in range(4)]
        line = extra_ref[5:6]
        right += [extra_ref[4:5], line, line - upper_of(line), extra_ref[7:8]]
        pack = jnp.concatenate(
            [jnp.concatenate(left, axis=0), jnp.concatenate(right, axis=0)], axis=1
        )
        pack_ref[...] = jnp.concatenate([pack, jnp.zeros_like(pack)], axis=0).astype(jnp.bfloat16)


def finish_layer(
    joined, weight, grad_pre, gate_weight, tokens, grad_middle, mod_rows, feed_sums, extra, grad_tables
):
    rows, width = tokens.shape
    counts = [table.shape[0] for table in grad_tables]

    def fixed(shape):
        return pl.BlockSpec(shape, lambda step: (0,) * len(shape), pipeline_mode=pl.Buffered(1))

    return pl.pallas_call(
        functools.partial(finish_kernel, counts),
        grid=(3,),
        in_specs=[
            pl.BlockSpec((rows, width), lambda step: (0, step)),
            pl.BlockSpec((width, width), lambda step: (0, step)),
            fixed((rows, width)),
            fixed((width, width)),
            fixed((rows, width)),
            fixed((rows, width)),
            fixed((8, width)),
            fixed((8, width)),
            fixed((8, SIDE)),
        ]
        + [fixed((count, 8, LANES)) for count in counts],
        out_specs=(fixed((rows, width)), fixed((16, PACK))),
        out_shape=(
            jax.ShapeDtypeStruct((rows, width), jnp.bfloat16),
            jax.ShapeDtypeStruct((16, PACK), jnp.bfloat16),
        ),
        scratch_shapes=[
            pltpu.VMEM((rows, width), jnp.float32),
            pltpu.VMEM((2, 8, width), jnp.float32),
        ],
        compiler_params=pltpu.CompilerParams(vmem_limit_bytes=VMEM_BYTES),
        cost_estimate=pl.CostEstimate(
            flops=8 * rows * width * width, bytes_accessed=24 * rows * width, transcendentals=0
        ),
        name="finish_layer",
    )(
        joined,
        weight,
        grad_pre,
        gate_weight,
        tokens,
        grad_middle,
        mod_rows,
        feed_sums,
        extra,
        *grad_tables,
    )


def fan_first_kernel(bits_ref, keep_ref, came_ref, mine_ref, *send_refs):
    chunk = keep_ref.shape[0] // 16
    for other, ref in enumerate((mine_ref, *send_refs)):
        for level in range(4):
            start = (level * 4 + (bits_ref[0] ^ other)) * chunk
            for first in range(0, chunk, 16):
                cut = pl.ds(pl.multiple_of(start + first, 16), 16)
                place = level * chunk + first
                ref[place : place + 16] = add_low(keep_ref[cut], came_ref[cut])


def fan_v_kernel(bits_ref, mine_ref, *refs):
    came_refs, (send_ref, out_ref) = refs[:3], refs[3:]
    chunk = mine_ref.shape[0] // 4
    for side, ref in ((1 - bits_ref[0], send_ref), (bits_ref[0], out_ref)):
        for far in range(2):
            for first in range(0, chunk, 16):
                cut = pl.ds(pl.multiple_of((2 * far + side) * chunk + first, 16), 16)
                total = mine_ref[cut].astype(jnp.float32)
                for came_ref in came_refs:
                    total = total + came_ref[cut].astype(jnp.float32)
                place = far * chunk + first
                ref[place : place + 16] = total.astype(jnp.bfloat16)


def fan_u_kernel(bits_ref, mine_ref, came_ref, send_ref, out_ref):
    chunk = mine_ref.shape[0] // 2
    for side, ref in ((1 - bits_ref[0], send_ref), (bits_ref[0], out_ref)):
        for first in range(0, chunk, 16):
            cut = pl.ds(pl.multiple_of(side * chunk + first, 16), 16)
            ref[first : first + 16] = add_low(mine_ref[cut], came_ref[cut])


def join_packs_kernel(bits_ref, *refs):
    packs = [ref[...].astype(jnp.float32)[0:8] for ref in refs[:4]]
    refs[4][...] = jnp.concatenate(packs, axis=0).astype(jnp.bfloat16)


def small_kernel(
    heads,
    here_ref,
    mine_ref,
    came_ref,
    modulation_ref,
    pair_norm_ref,
    relative_ref,
    gain_ref,
    pair_weight_ref,
    mod_grad_ref,
    time_ref,
    label_ref,
    relative_grad_ref,
    gain_grad_ref,
    pair_grad_ref,
    grad_condition,
    grad_mod,
    kept,
):
    step = pl.program_id(0)
    crops = mine_ref.shape[0] // 8
    width = mine_ref.shape[1] - SIDE
    conds = relative_ref.shape[1]
    parts = mod_grad_ref.shape[1] // width

    def parts_split(values):
        upper = values.astype(jnp.bfloat16)
        return upper, (values - upper.astype(jnp.float32)).astype(jnp.bfloat16)

    def dot_left(narrow, values, numbers):
        upper, rest = parts_split(values)
        return wide_dot(narrow, upper, numbers) + wide_dot(narrow, rest, numbers)

    def dot_right(values, narrow, numbers):
        upper, rest = parts_split(values)
        return wide_dot(upper, narrow, numbers) + wide_dot(rest, narrow, numbers)

    def both_twice(narrow):
        return jnp.concatenate([narrow, narrow], axis=0)

    def stacked(values):
        return jnp.concatenate(parts_split(values), axis=0)

    @pl.when(step == 0)
    def _():
        shape = (8 * crops, 8 * crops)
        picked = lax.broadcasted_iota(jnp.int32, shape, 0)
        source = lax.broadcasted_iota(jnp.int32, shape, 1)
        hit = ((source >> 3) == (picked & (crops - 1))) & ((source & 7) == (picked // crops))
        select = jnp.where(hit, 1.0, 0.0).astype(jnp.bfloat16)
        mine = wide_dot(select, mine_ref[...])
        grad_mod[...] = mine[: 6 * crops, :width] + wide_dot(select, came_ref[...])[: 6 * crops, :width]
        condition = (
            mine[5 * crops : 6 * crops, width : width + conds]
            + mine[6 * crops : 7 * crops, width : width + conds]
        )
        gate_value = sigmoid(condition)
        kept[0] = condition * gate_value
        kept[1] = gate_value * (1.0 + condition * (1.0 - gate_value))
        kept[2] = mine[4 * crops : 5 * crops, width : width + conds]
        kept[3] = jnp.broadcast_to(
            mine[5 * crops : 6 * crops, width + conds : width + conds + 1]
            + mine[6 * crops : 7 * crops, width + conds : width + conds + 1],
            (crops, conds),
        )
        grad_condition[...] = jnp.zeros_like(grad_condition)

    cond_act = both_twice(kept[0].astype(jnp.bfloat16))
    for turn in range(parts):
        columns = slice(turn * width, (turn + 1) * width)
        first = pl.multiple_of((step * parts + turn) * crops, crops)
        pair = stacked(grad_mod[pl.ds(first, crops)])
        mod_grad_ref[:, columns] = wide_dot(cond_act, pair, TN)
        more = wide_dot(pair, modulation_ref[:, columns], NT)
        grad_condition[...] += more[:crops] + more[crops:]

    @pl.when(step == 0)
    def _():
        shape = (8, 8 * crops)
        line = lax.broadcasted_iota(jnp.int32, shape, 0)
        local = lax.broadcasted_iota(jnp.int32, shape, 1) & 7
        every = jnp.where(local == line, 1.0, 0.0).astype(jnp.bfloat16)
        lines = wide_dot(every, mine_ref[...]) + wide_dot(every, came_ref[...])

        def of_head(head):
            upper = width + (head % 3) * LANES
            rest = (head % (width // LANES)) * LANES
            low = 6 + head // (width // LANES)
            return (
                lines[head // 3 : head // 3 + 1, upper : upper + LANES]
                + lines[low : low + 1, rest : rest + LANES]
            )

        table = jnp.concatenate(
            [of_head(head) for head in range(heads)]
            + [jnp.zeros((16 - heads, LANES), jnp.float32)],
            axis=0,
        )
        bins = relative_ref.shape[0]
        pair_grad_ref[...] = dot_right(table, pair_norm_ref[...], (((1,), (0,)), ((), ())))[:heads]
        grad_norm = dot_right(table, pair_weight_ref[...], (((0,), (1,)), ((), ())))[:bins]
        values = relative_ref[...]
        centred = values - jnp.mean(values, axis=1, keepdims=True)
        root = lax.rsqrt(jnp.mean(centred * centred, axis=1, keepdims=True) + 1e-06)
        normal = centred * root
        gain_grad_ref[...] = jnp.sum(grad_norm * normal, axis=0, keepdims=True)
        scaled = grad_norm * gain_ref[...]
        relative_grad_ref[...] = root * (
            scaled
            - jnp.mean(scaled, axis=1, keepdims=True)
            - normal * jnp.mean(scaled * normal, axis=1, keepdims=True)
        )

    @pl.when(step == pl.num_programs(0) - 1)
    def _():
        final = stacked(grad_condition[...] * kept[1])
        time_ref[...] = wide_dot(both_twice(kept[2].astype(jnp.bfloat16)), final, TN)
        label = lax.broadcasted_iota(jnp.int32, (crops, label_ref.shape[0]), 1)
        number = kept[3][:, 0:1].astype(jnp.int32)
        onehot = jnp.where(label == number, 1.0, 0.0).astype(jnp.bfloat16)
        label_ref[...] = wide_dot(both_twice(onehot), final, TN)


def small_gradients(heads, labels, mine, came, modulation_weight, pair_norm, relative, gain, pair_weight):
    conds, wide = modulation_weight.shape
    bins = relative.shape[0]
    rows = mine.shape[0]
    steps = 3

    def fixed(shape):
        return pl.BlockSpec(shape, lambda step: (0, 0))

    shapes = [(conds, wide), (conds, conds), (labels, conds), (bins, conds), (1, conds), (heads, conds)]
    return pl.pallas_call(
        functools.partial(small_kernel, heads),
        grid=(steps,),
        in_specs=[
            pl.BlockSpec(memory_space=pltpu.SMEM),
            fixed((rows, PACK)),
            fixed((rows, PACK)),
            pl.BlockSpec((conds, wide // steps), lambda step: (0, step)),
            fixed((LANES, conds)),
            fixed((bins, conds)),
            fixed((1, conds)),
            fixed((conds, 16)),
        ],
        out_specs=tuple(
            [pl.BlockSpec((conds, wide // steps), lambda step: (0, step))]
            + [fixed(s) for s in shapes[1:]]
        ),
        out_shape=tuple(jax.ShapeDtypeStruct(shape, jnp.float32) for shape in shapes),
        scratch_shapes=[
            pltpu.VMEM((rows // 8, conds), jnp.float32),
            pltpu.VMEM((6 * rows // 8, wide // 6), jnp.float32),
            pltpu.VMEM((4, rows // 8, conds), jnp.float32),
        ],
        compiler_params=pltpu.CompilerParams(vmem_limit_bytes=VMEM_BYTES),
        cost_estimate=pl.CostEstimate(
            flops=100000000, bytes_accessed=10000000, transcendentals=0
        ),
        name="small_gradients",
    )(
        scalars(0),
        mine,
        came,
        modulation_weight,
        pair_norm,
        relative,
        gain,
        pair_weight,
    )


def per_device(
    crop_parts,
    res_parts,
    tokens,
    cotangent,
    time_levels,
    cath_ids,
    residue_numbers,
    chain_mask,
    time_weight,
    label_table,
    modulation_weight,
    projection_weight,
    gate_weight,
    output_weight,
    relative_table,
    pair_gain,
    pair_weight,
    feed_gate,
    feed_up,
    feed_down,
):
    crop_count, row_count, model_width = tokens.shape
    crop_length = residue_numbers.shape[1]
    head_count = pair_weight.shape[1]
    head_width = model_width // head_count
    bin_count = relative_table.shape[0]
    label_count = label_table.shape[0]
    token_count = crop_count * row_count
    score_scale = head_width ** (-0.5)
    pairs = head_count // 2
    layout = Layout(row_count, crop_length)
    query_start = lax.axis_index("res") * row_count

    def conditioning(features, onehot):
        return jnp.dot(features, time_weight, preferred_element_type=jnp.float32) + jnp.dot(
            onehot, label_table, preferred_element_type=jnp.float32
        )

    features = time_features(time_levels, time_weight.shape[0]).astype(jnp.bfloat16)
    label_onehot = (cath_ids[:, None] == jnp.arange(label_count, dtype=jnp.int32)[None, :]).astype(
        jnp.bfloat16
    )
    condition = conditioning(features, label_onehot)
    cond_act = jax.nn.silu(condition).astype(jnp.bfloat16)
    modulation = jnp.dot(cond_act, modulation_weight, preferred_element_type=jnp.float32)
    modulation = modulation.reshape(crop_count, 6, 1, model_width)
    shift_a, scale_a = modulation[:, 0], modulation[:, 1]
    mod_rows = pad_to(modulation[:, :, 0], 1, 8, 0.0)

    rotated = lax.dynamic_slice_in_dim(
        jnp.concatenate([jnp.stack([residue_numbers, chain_mask])] * 2, 2), query_start, crop_length, 2
    )
    members, kinds, forward_bins, backward_bins, places, *turned = attention_tables(
        layout, rotated[0], rotated[1], query_start, bin_count
    )
    relative_values = relative_table.astype(jnp.float32)
    gain_values = pair_gain.astype(jnp.float32)
    pair_norm = normalize_rows(relative_values, gain_values).astype(jnp.bfloat16)
    bias_rows = jnp.dot(pair_norm, pair_weight, preferred_element_type=jnp.float32)
    tables = head_tables(layout, bias_rows, score_scale)

    token_values = tokens.astype(jnp.float32)
    normed_a = (
        modulate(token_values, shift_a, scale_a)
        .astype(jnp.bfloat16)
        .reshape(token_count, model_width)
    )
    def project(weight):
        rows = jnp.dot(normed_a, weight, preferred_element_type=jnp.float32)
        return rows.astype(jnp.bfloat16).reshape(crop_count, row_count, -1)

    key_values = project(projection_weight[:, model_width:])
    queries = project(projection_weight[:, :model_width])
    others = [
        lax.ppermute(
            key_values, "res", [((r + step) % res_parts, r) for r in range(res_parts)]
        )
        for step in range(1, res_parts)
    ]
    small_operands = (
        pad_to(pair_norm, 0, LANES, 0.0),
        relative_values,
        gain_values.reshape(1, -1),
        pad_to(pair_weight, 1, 16, 0.0),
    )
    if others:
        others, small_operands = tie(others, small_operands)
    if len(layout.pieces) == 2:
        other = others[0] if len(others) == 1 else jnp.concatenate(others, axis=1)
        pieces = [(key_values, 0, pairs), (other, 0, pairs)]
    else:
        pieces = [(jnp.concatenate([key_values] + others, axis=1), 0, pairs)]

    def block_rows(values):
        return pad_to(values, 1, layout.block_rows, 0)

    attended, logs = attention_forward(
        layout,
        score_scale,
        block_rows(queries),
        pieces,
        members,
        kinds,
        forward_bins,
        tables,
    )
    here = lax.axis_index("res")
    split = res_parts == 2 and crop_parts == 16
    per_crop_results = [
        feed_layer(
            split,
            here,
            attended[crop],
            block_rows(tokens)[crop],
            block_rows(cotangent)[crop],
            block_rows(normed_a.reshape(tokens.shape))[crop],
            mod_rows[crop],
            gate_weight,
            output_weight,
            feed_gate,
            feed_up,
            feed_down,
        )
        for crop in range(crop_count)
    ]
    layer_out, grad_middle, grad_attended, grad_gate_pre, feed_sums = (
        jnp.stack([result[place] for result in per_crop_results]) for place in range(5)
    )
    layer_out, grad_middle = layer_out[:, :row_count], grad_middle[:, :row_count]
    grad_gate_pre = grad_gate_pre[:, :row_count].reshape(token_count, model_width)
    weight_grads = [
        sum(result[place].astype(jnp.float32) for result in per_crop_results).astype(jnp.bfloat16)
        if crop_count > 1
        else per_crop_results[0][place]
        for place in range(5, len(per_crop_results[0]))
    ]

    def backward_of(first_pair, count, grad_now):
        return attention_backward(
            layout,
            score_scale,
            first_pair,
            count,
            block_rows(queries),
            grad_now,
            attended,
            logs,
            pieces,
            members,
            kinds,
            backward_bins,
            places,
            *turned,
            tables,
        )

    if split:
        arrivals = [swap_res(weight_grads[place]) for place in (0, 2, 4, 6)]
        kept = [weight_grads[place] for place in (1, 3, 5, 7)]
        half = model_width // 2
        inner = feed_gate.shape[1] // 2
        calls = [list(backward_of(0, 1, grad_attended))]
        arrivals, calls[0] = tie(arrivals, calls[0])
        gate_w, up_w, down_w, small_w = zip(kept, arrivals)
        halving = Halving(
            [
                [(gate_w, 0, inner), (small_w, 0, half)],
                [(up_w, 0, inner), (small_w, 1, half)],
                [(down_w, 0, half)],
            ],
            ["xyvu", "yvxu", "vxyu"],
        )
        arrived = []
        for first_pair, count in ((1, 4), (5, 1)):
            arrived.append(swap_res(calls[-1][2][0]))
            sent = halving.stage()
            sent, grad_attended = tie(sent, grad_attended)
            came = halving.send(sent)
            calls.append(list(backward_of(first_pair, count, grad_attended)))
            came, calls[-1], arrived[-1] = tie(came, calls[-1], arrived[-1])
            halving.take(came)
        index = lax.axis_index("crop")
        bf16 = jnp.bfloat16
        share = model_width // 16
        away = swap_res(calls[2][2][0])
        sent = halving.stage()
        sent, calls[2][1] = tie(sent, calls[2][1])
        came = halving.send(sent)
        joined, proj_send, proj_keep = projection_gradient(
            here,
            normed_a,
            [
                (calls[0][0][0], calls[0][1][0], arrived[0]),
                (calls[1][0][0], calls[1][1][0], arrived[1]),
                (calls[2][0][0], calls[2][1][0], away),
            ],
        )
        came, proj_send, proj_keep = tie(came, proj_send, proj_keep)
        proj_came = swap_res(proj_send)
        halving.take(came)
        (sent,) = halving.stage(merge=True)
        sent, proj_came = tie(sent, proj_came)
        came = exchange(sent, MASKS["u"])
        mine, *fan = local_call(
            fan_first_kernel,
            scalars(index % 4),
            [proj_keep, proj_came],
            [((4 * share, PACK), bf16)] * 4,
            "fan_first",
        )
        fan, joined = tie(fan, joined)
        fan_came = [exchange(value, mask + 1) for mask, value in enumerate(fan)]
        extra = jnp.concatenate(
            [
                pad_to(features.astype(jnp.float32), 1, SIDE, 0.0),
                jnp.concatenate(
                    [condition, pad_to(cath_ids.astype(jnp.float32)[:, None], 1, LANES, 0.0)], axis=1
                ),
            ],
            axis=0,
        )
        tokens_grad, pack = finish_layer(
            joined,
            projection_weight,
            grad_gate_pre,
            gate_weight,
            tokens[0],
            grad_middle[0],
            mod_rows[0],
            feed_sums[0],
            jnp.pad(extra, ((4, 2), (0, 0))),
            [call[-1][0] for call in calls],
        )
        tokens_grad = tokens_grad[None]
        came, pack = tie(came, pack)
        packs = [pack] + [exchange(pack, mask + 1) for mask in range(3)]
        finals = halving.stage(last=True, merged=came)
        feed_gate_grad, output_weight_grad, feed_up_grad, gate_weight_grad, feed_down_grad = finals
        packs, finals = tie(packs, finals)
        (packs,) = local_call(join_packs_kernel, scalars(0), packs, [((32, PACK), bf16)], "join_packs")
        far_packs = exchange(packs, MASKS["v"])
        packs, fan_came, far_packs = tie(packs, fan_came, far_packs)
        sent, mine = local_call(
            fan_v_kernel,
            scalars((index // 4) % 2),
            [mine, *fan_came],
            [((2 * share, PACK), bf16), ((2 * share, PACK), bf16)],
            "fan_v",
        )
        packs = jnp.concatenate([packs, far_packs], axis=0)
        sent, packs = tie(sent, packs)
        came = exchange(sent, MASKS["v"])
        far_packs = exchange(packs, MASKS["u"])
        came, far_packs = tie(came, far_packs)
        packs = jnp.concatenate([packs, far_packs], axis=0)
        sent, mine = local_call(
            fan_u_kernel,
            scalars(index // 8),
            [mine, came],
            [((share, PACK), bf16), ((share, PACK), bf16)],
            "fan_u",
        )
        sent, packs = tie(sent, packs)
        came = exchange(sent, MASKS["u"])
        (
            modulation_weight_grad,
            time_weight_grad,
            label_table_grad,
            relative_table_grad,
            pair_gain_grad,
            pair_weight_grad,
        ) = small_gradients(
            head_count, label_count, packs, swap_res(packs), modulation_weight, *small_operands
        )
        pair_weight_grad = pair_weight_grad.T
        came, pair_weight_grad = tie(came, pair_weight_grad)
        projection_weight_grad = add_low(mine, came, jnp.float32)
        pair_gain_grad = pair_gain_grad[0]
    else:
        results = backward_of(0, pairs, grad_attended)
        grad_table = results[-1]
        grad_pairs = results[1:-1]
        if len(grad_pairs) == 2:
            total, away = grad_pairs[0].astype(jnp.float32), grad_pairs[1]
        else:
            total = grad_pairs[0][:, :, :row_count].astype(jnp.float32)
            away = grad_pairs[0][:, :, row_count:]
        for step in range(1, res_parts):
            sent = away[:, :, (step - 1) * row_count : step * row_count]
            pairs_to = [(r, (r + step) % res_parts) for r in range(res_parts)]
            total = total + lax.ppermute(sent, "res", pairs_to).astype(jnp.float32)
        total = total.astype(jnp.bfloat16)
        grad_projected = jnp.concatenate(
            [results[0][:, :row_count], total[:, 0], total[:, 1]], axis=-1
        ).reshape(token_count, 3 * model_width)
        grad_normed_a = against_columns(grad_projected, projection_weight) + against_columns(
            grad_gate_pre, gate_weight
        )
        norm_back_a = jax.vjp(modulate, token_values, shift_a, scale_a)[1]
        grad_tokens, grad_shift_a, grad_scale_a = norm_back_a(
            grad_normed_a.reshape(crop_count, row_count, model_width)
        )
        tokens_grad = (grad_middle + grad_tokens).astype(jnp.bfloat16)
        feed_gate_grad, feed_up_grad, feed_down_grad = (
            scatter_crops(share_columns(value, res_parts)) for value in weight_grads[:3]
        )
        output_weight_grad, gate_weight_grad = (
            scatter_crops(share_columns(value, res_parts))
            for value in (weight_grads[3][:, :model_width], weight_grads[3][:, model_width:])
        )
        projection_weight_grad = scatter_crops(
            share_columns(across_rows(normed_a, grad_projected), res_parts)
        )
        grad_table = grad_table[:, :, :2].sum(0).reshape(head_count, LANES)

        grad_modulation = jnp.concatenate([grad_shift_a, grad_scale_a, feed_sums[:, 2:6]], axis=1)
        grad_modulation = grad_modulation.reshape(crop_count, 6 * model_width)
        table_row = grad_table.reshape(1, head_count * LANES)
        first_row = (jnp.arange(crop_count) == 0).astype(jnp.float32)[:, None]
        small_here = jnp.concatenate([grad_modulation, first_row * table_row], axis=1)
        levels_here = jnp.stack([time_levels, cath_ids.astype(jnp.float32)], axis=1)
        levels_here = pad_to(levels_here, 1, LANES, 0.0)
        small_all = gather_crops(
            jnp.concatenate([levels_here, sum_res(small_here, res_parts)], axis=1), crop_parts
        )
        levels_all, small_all = small_all[:, :2], small_all[:, LANES:]
        grad_modulation = small_all[:, : 6 * model_width]
        grad_table = jnp.sum(small_all[:, 6 * model_width :], axis=0).reshape(head_count, LANES)
        grad_table = grad_table[:, :bin_count]
        features_all = time_features(levels_all[:, 0], time_weight.shape[0]).astype(jnp.bfloat16)
        onehot_all = (
            levels_all[:, 1].astype(jnp.int32)[:, None]
            == jnp.arange(label_count, dtype=jnp.int32)[None, :]
        ).astype(jnp.bfloat16)
        condition = conditioning(features_all, onehot_all)
        cond_act = jax.nn.silu(condition).astype(jnp.bfloat16)
        modulation_weight_grad = split_left(cond_act, grad_modulation, 0, 0)
        grad_condition = split_left(modulation_weight, grad_modulation, 1, 1).T * silu_slope(condition)
        time_weight_grad = split_left(features_all, grad_condition, 0, 0)
        label_table_grad = split_left(onehot_all, grad_condition, 0, 0)
        pair_weight_grad = split_left(pair_norm, grad_table, 0, 1)
        grad_pair_norm = split_right(grad_table, pair_weight, 0, 1)
        pair_back = jax.vjp(normalize_rows, relative_values, gain_values)[1]
        relative_table_grad, pair_gain_grad = pair_back(grad_pair_norm)
    return (
        layer_out,
        tokens_grad,
        time_weight_grad,
        label_table_grad,
        modulation_weight_grad,
        projection_weight_grad,
        gate_weight_grad,
        output_weight_grad,
        relative_table_grad,
        pair_gain_grad,
        pair_weight_grad,
        feed_gate_grad,
        feed_up_grad,
        feed_down_grad,
    )


def solution(mesh):
    return jax.shard_map(
        functools.partial(per_device, mesh.shape["crop"], mesh.shape["res"]),
        mesh=mesh,
        in_specs=(
            P("crop", "res", None),
            P("crop", "res", None),
            P("crop"),
            P("crop"),
            P("crop", None),
            P("crop", None),
            P(),
            P(),
            P(),
            P(),
            P(),
            P(),
            P(),
            P(),
            P(),
            P(),
            P(),
            P(),
        ),
        out_specs=(
            P("crop", "res", None),
            P("crop", "res", None),
            P(),
            P(),
            P(),
            P("crop", "res"),
            P("crop", "res"),
            P("crop", "res"),
            P(),
            P(),
            P(),
            P("crop", "res"),
            P("crop", "res"),
            P("crop", "res"),
        ),
        check_vma=False,
    )
```

```python
import functools
import itertools
import math

import jax
import jax.numpy as jnp
from jax import lax
from jax.experimental import pallas as pl
from jax.experimental.pallas import tpu as pltpu
from jax.sharding import PartitionSpec as P

LANES = 128
NEAR = 31
VMEM_BYTES = 62 * 1024 * 1024
LOG2E = 1.4426950408889634
NONE, RIGHT, LEFT, APART = 0, 1, 2, 3


def layer_norm(inputs):
    mean_value = jnp.mean(inputs, axis=-1, keepdims=True)
    centred = inputs - mean_value
    spread = jnp.mean(centred * centred, axis=-1, keepdims=True)
    return centred * lax.rsqrt(spread + 1e-06)


def modulate(inputs, shift_row, scale_row):
    return layer_norm(inputs) * (1.0 + scale_row) + shift_row


def normalize_rows(table_rows, gain_row):
    return layer_norm(table_rows) * gain_row


def time_features(time_levels, feature_width):
    half_width = feature_width // 2
    frequency = jnp.exp(-math.log(10000.0) * jnp.arange(half_width, dtype=jnp.float32) / half_width)
    angles = 1000.0 * time_levels[:, None] * frequency[None, :]
    return jnp.concatenate([jnp.sin(angles), jnp.cos(angles)], axis=-1)


def across_rows(former, latter):
    return lax.dot_general(
        former, latter, (((0,), (0,)), ((), ())), preferred_element_type=jnp.float32
    )


def against_columns(former, latter):
    return lax.dot_general(
        former, latter, (((1,), (1,)), ((), ())), preferred_element_type=jnp.float32
    )


def split_parts(values):
    upper = lax.reduce_precision(values, 8, 7)
    return (upper.astype(jnp.bfloat16), (values - upper).astype(jnp.bfloat16))


def split_left(narrow, values, former_dim, latter_dim):
    upper, rest = split_parts(values)
    numbers = (((former_dim,), (latter_dim,)), ((), ()))
    return lax.dot_general(
        narrow, upper, numbers, preferred_element_type=jnp.float32
    ) + lax.dot_general(narrow, rest, numbers, preferred_element_type=jnp.float32)


def split_right(values, narrow, former_dim, latter_dim):
    upper, rest = split_parts(values)
    numbers = (((former_dim,), (latter_dim,)), ((), ()))
    return lax.dot_general(
        upper, narrow, numbers, preferred_element_type=jnp.float32
    ) + lax.dot_general(rest, narrow, numbers, preferred_element_type=jnp.float32)


def sigmoid_slope(inputs):
    gate_value = jax.nn.sigmoid(inputs)
    return gate_value * (1.0 - gate_value)


def silu_slope(inputs):
    gate_value = jax.nn.sigmoid(inputs)
    return gate_value * (1.0 + inputs * (1.0 - gate_value))


class Layout:
    def __init__(self, rows, length):
        self.rows = rows
        self.length = length
        self.query_tiles = -(-rows // LANES)
        self.key_tiles = -(-length // LANES)
        self.padded = self.query_tiles * LANES
        self.wide = self.key_tiles * LANES
        self.last = self.key_tiles - 1
        self.groups = (self.query_tiles + 4) * 4
        assert 2 * self.groups + 3 <= LANES and self.groups <= 64
        assert rows - 1 + NEAR < self.padded and length - NEAR >= self.last * LANES
        assert rows % 8 == 0 and self.last > self.query_tiles
        self.block_rows = rows if rows % 16 == 0 else self.padded
        self.pieces = [rows, length - rows] if rows % 16 == 0 else [length]

    def tile_start(self, tile):
        return self.last * LANES if tile < 0 else tile * LANES


def pad_to(values, axis, size, fill):
    widths = [(0, 0)] * values.ndim
    widths[axis] = (0, size - values.shape[axis])
    return jnp.pad(values, widths, constant_values=fill)


def tables_kernel(
    layout, bin_count, heads, scale, start_ref, pairs_ref, relative_ref, gain_ref, weight_ref, *out_refs
):
    members_ref, kinds_ref, forward_ref, backward_ref, places_ref = out_refs[:5]
    members_turned, kinds_turned, tables_ref, norm_ref, codes = out_refs[5:]
    rows, length, queries, groups = layout.rows, layout.length, layout.query_tiles, layout.groups
    wrap = length - start_ref[0]
    reach = (bin_count - 2) // 2
    zero_bin = LANES - 1
    shape = (LANES, LANES)
    lane = lax.broadcasted_iota(jnp.int32, shape, 1)
    row = lax.broadcasted_iota(jnp.int32, shape, 0)
    last_start = layout.last * LANES

    values = relative_ref[...].astype(jnp.float32)
    centred = values - jnp.mean(values, axis=1, keepdims=True)
    root = lax.rsqrt(jnp.mean(centred * centred, axis=1, keepdims=True) + 1e-06)
    pair_norm = (centred * root * gain_ref[...].astype(jnp.float32)).astype(jnp.bfloat16)
    norm_ref[...] = pair_norm
    bias = lax.dot_general(
        weight_ref[...], pair_norm, (((0,), (1,)), ((), ())), preferred_element_type=jnp.float32
    )
    head_lane = lax.broadcasted_iota(jnp.int32, bias.shape, 1)
    final = jnp.sum(jnp.where(head_lane == bin_count - 1, bias, 0.0), axis=1, keepdims=True)
    table = jnp.where(head_lane < bin_count, (bias - final) * (1.0 / scale), 0.0)

    def columns(number):
        value = jnp.sum(jnp.where(head_lane == number, table, 0.0), axis=1, keepdims=True)
        upper = value.astype(jnp.bfloat16).astype(jnp.float32)
        return jnp.where(
            head_lane < groups, upper, jnp.where(head_lane < 2 * groups, value - upper, 0.0)
        )

    right_columns, left_columns = columns(bin_count - 2), columns(0)
    for head in range(heads):
        line = 8 * (head % 2)
        for place, rows_of in enumerate((table, right_columns, left_columns)):
            tables_ref[head // 2, line + place : line + place + 1] = rows_of[head : head + 1]

    tiles = pairs_ref.shape[1]
    marks = pairs_ref[1].astype(jnp.float32)
    place = lax.broadcasted_iota(jnp.int32, marks.shape, 0) * LANES + lax.broadcasted_iota(
        jnp.int32, marks.shape, 1
    )
    before = jnp.sum(jnp.where(place < wrap, marks, 0.0), keepdims=True)
    every = jnp.sum(marks, keepdims=True)
    triangle = jnp.where(row <= lane, 1.0, 0.0).astype(jnp.bfloat16)
    running = jnp.dot(marks.astype(jnp.bfloat16), triangle, preferred_element_type=jnp.float32)
    numbers, chains = [], []
    carry = jnp.zeros((1, 1), jnp.float32)
    for tile in range(layout.key_tiles):
        count = running[tile : tile + 1] + carry
        carry = carry + running[tile : tile + 1, LANES - 1 :]
        count = count + jnp.where(place[tile : tile + 1] < wrap, every - before, -before)
        chains.append(jnp.broadcast_to(count.astype(jnp.int32), shape))
        numbers.append(jnp.broadcast_to(pairs_ref[0, tile : tile + 1], shape))
    number_rows = [value.T for value in numbers]
    chain_rows = [value.T for value in chains]

    def bins_of(key_number, key_chain, query_number, query_chain):
        offset = jnp.clip(key_number - query_number, -reach, reach) + reach
        return jnp.where(key_chain == query_chain, offset, bin_count - 1)

    def touches(query, tile):
        begin = -LANES if tile < 0 else tile * LANES
        return (begin <= query + NEAR) & (query - NEAR <= begin + LANES - 1)

    for tile in range(layout.key_tiles):
        size = min(LANES, length - tile * LANES)
        key = tile * LANES + row
        if tile == layout.last:
            other = jnp.full(shape, queries + 3, jnp.int32)
        elif tile == queries - 1:
            other = jnp.full(shape, queries, jnp.int32)
        else:
            other = jnp.where(key < wrap, queries + 1, queries + 2)
        group = jnp.where(key < rows, tile, other)
        slot = group * 4 + chain_rows[tile] - 1
        hit = (lane == slot) | (lane == slot + groups)
        tail = (lane >= 2 * groups) & (lane < 2 * groups + 3)
        values = jnp.where(hit, 1.0, jnp.where(tail, -1.0, 0.0)).astype(jnp.bfloat16)
        members_ref[tile * LANES : tile * LANES + size] = values[:size]
        turned = jnp.where(hit & (lane < groups), 1.0, 0.0).T
        members_turned[:, tile * LANES : tile * LANES + size] = turned[:64, :size].astype(jnp.bfloat16)

    local = jnp.where(lane >= groups, lane - groups, lane)
    lane_group = local >> 2
    lane_chain = (local & 3) + 1
    lane_begin = jnp.where(
        lane_group < queries,
        lane_group * LANES,
        jnp.where(lane_group == queries, (queries - 1) * LANES, -LANES),
    )
    has_band = (lane_group <= queries) | (lane_group == queries + 3)
    other_right = jnp.where(
        lane_group == queries,
        rows,
        jnp.where(
            lane_group == queries + 3,
            last_start,
            jnp.where(lane_group == queries + 1, 0, 2 * length),
        ),
    )
    right_limit = jnp.where(lane_group > queries, jnp.where(lane_group == queries + 3, wrap, length), wrap)
    for tile in range(queries):
        size = min(LANES, layout.block_rows - tile * LANES)
        query = tile * LANES + row
        near = (lane_begin <= query + NEAR) & (query - NEAR <= lane_begin + LANES - 1) & has_band
        right = jnp.where(lane_group < queries, lane_group - tile, right_limit - other_right) > 0
        same = chain_rows[tile] == lane_chain
        kinds = jnp.where(same, jnp.where(near, NONE, jnp.where(right, RIGHT, LEFT)), APART)
        kinds = jnp.where((lane < 2 * groups) & (query < rows), kinds, NONE)
        kinds_ref[tile * LANES : tile * LANES + size] = kinds[:size]
        kinds_turned[:, tile * LANES : (tile + 1) * LANES] = jnp.where(lane < groups, kinds, NONE).T[:64]
        for step in range(3):
            near_tile = tile + step - 1
            index = layout.last if near_tile < 0 else near_tile
            if near_tile < queries:
                inside = touches(query, near_tile) & (query < rows)
                inside &= lane < length - index * LANES
                found = bins_of(
                    numbers[index], chains[index], number_rows[tile], chain_rows[tile]
                )
                found = jnp.where(inside, found, zero_bin)
            else:
                found = jnp.full(shape, zero_bin, jnp.int32)
            forward_ref[
                tile * LANES : (tile + 1) * LANES, step * LANES : (step + 1) * LANES
            ] = found

    codes[...] = jnp.full(codes.shape, -1, jnp.int32)
    for tile in range(queries):
        size = min(LANES, rows - tile * LANES)
        code = number_rows[tile] * 8 + chain_rows[tile]
        codes[(tile + 1) * LANES : (tile + 1) * LANES + size] = code[:size]

    for index, tile in enumerate(list(range(queries)) + [-1]):
        source = layout.last if tile < 0 else tile
        key_row = (row - (length - last_start)) if tile < 0 else tile * LANES + row
        present = row < length - source * LANES
        for step in range(3):
            near_tile = tile + step - 1
            if 0 <= near_tile < queries:
                near_query = near_tile * LANES + lane
                inside = touches(near_query, tile) & (near_query < rows) & present
                found = bins_of(
                    number_rows[source], chain_rows[source], numbers[near_tile], chains[near_tile]
                )
                found = jnp.where(inside, found, zero_bin)
            else:
                found = jnp.full(shape, zero_bin, jnp.int32)
            backward_ref[
                index * LANES : (index + 1) * LANES, step * LANES : (step + 1) * LANES
            ] = found
        target = (number_rows[source] + reach - lane) * 8 + chain_rows[source]
        target = jnp.where(present & (lane > 0) & (lane < 2 * reach), target, -9)
        offset = (LANES - (length - last_start)) if tile < 0 else (tile + 1) * LANES
        far = 4 * LANES
        shift = jnp.full(shape, far, jnp.int32)
        for distance in range(-NEAR, NEAR + 1):
            other = codes[offset - distance : offset - distance + LANES]
            shift = jnp.where(other == target, distance, shift)
        if tile < 0:
            base = jnp.zeros(shape, jnp.int32)
        else:
            base = jnp.where(row < LANES // 2, tile - 1, tile) * LANES
        places_ref[index * LANES : (index + 1) * LANES] = jnp.where(
            shift == far, far - 1, key_row - shift - base
        )


def attention_tables(layout, scale, numbers, marks, query_start, relative_table, pair_gain, pair_weight):
    crops = numbers.shape[0]
    bin_count, width = relative_table.shape
    heads = pair_weight.shape[1]
    pairs = jnp.stack([numbers, marks], axis=1)
    pairs = pad_to(pairs, 2, layout.wide, 0).reshape(crops, 2, layout.key_tiles, LANES)
    spots = (layout.query_tiles + 1) * LANES
    shapes = [
        ((layout.length, LANES), jnp.bfloat16),
        ((layout.block_rows, LANES), jnp.int32),
        ((layout.padded, 3 * LANES), jnp.int32),
        ((spots, 3 * LANES), jnp.int32),
        ((spots, LANES), jnp.int32),
        ((64, layout.length), jnp.bfloat16),
        ((64, layout.padded), jnp.int32),
    ]
    shared = [((heads // 2, 16, LANES), jnp.float32), ((LANES, width), jnp.bfloat16)]

    def whole(shape):
        return pl.BlockSpec(shape, lambda crop: (0,) * len(shape))

    return pl.pallas_call(
        functools.partial(tables_kernel, layout, bin_count, heads, scale),
        grid=(crops,),
        in_specs=[
            pl.BlockSpec(memory_space=pltpu.SMEM),
            pl.BlockSpec((None, 2, layout.key_tiles, LANES), lambda crop: (crop, 0, 0, 0)),
            whole((LANES, width)),
            whole((1, width)),
            whole((width, 16)),
        ],
        out_specs=tuple(
            [pl.BlockSpec((None, *shape), lambda crop: (crop, 0, 0)) for shape, _ in shapes]
            + [whole(shape) for shape, _ in shared]
        ),
        out_shape=tuple(
            [jax.ShapeDtypeStruct((crops, *shape), kind) for shape, kind in shapes]
            + [jax.ShapeDtypeStruct(shape, kind) for shape, kind in shared]
        ),
        scratch_shapes=[pltpu.VMEM((layout.padded + 2 * LANES, LANES), jnp.int32)],
        compiler_params=pltpu.CompilerParams(vmem_limit_bytes=VMEM_BYTES),
        cost_estimate=pl.CostEstimate(
            flops=40000000 * crops, bytes_accessed=4000000 * crops, transcendentals=0
        ),
        name="pair_tables",
    )(
        jnp.reshape(query_start, (1,)).astype(jnp.int32),
        pairs,
        pad_to(relative_table, 0, LANES, 0.0),
        pair_gain.reshape(1, -1),
        pad_to(pair_weight, 1, 16, 0.0),
    )


NT = (((1,), (1,)), ((), ()))
TN = (((0,), (0,)), ((), ()))


def wide_dot(former, latter, numbers=(((1,), (0,)), ((), ()))):
    return lax.dot_general(former, latter, numbers, preferred_element_type=jnp.float32)


def look_up(table_row, bins):
    table = jnp.broadcast_to(table_row, bins.shape)
    return jnp.take_along_axis(table, bins, axis=1, mode="promise_in_bounds")


def half_of(values, lane, side):
    return jnp.where((lane >= 64) == (side == 1), values, jnp.zeros_like(values))


def row_blocks(total, size):
    return [(start, min(start + size, total)) for start in range(0, total, size)]


def group_columns(kinds, tables, side):
    right = tables[8 * side + 1 : 8 * side + 2]
    left = tables[8 * side + 2 : 8 * side + 3]
    return jnp.where(kinds == RIGHT, right, jnp.where(kinds == LEFT, left, 0.0))


def forward_kernel(layout, scale, *refs):
    count = len(layout.pieces)
    normed_ref, weight_ref = refs[:2]
    key_refs = refs[2 : 2 + count]
    value_refs = refs[2 + count : 2 + 2 * count]
    members_ref, kinds_ref, bins_ref, tables_ref, query_ref, out_ref, log_ref = refs[
        2 + 2 * count : -1
    ]
    all_scores = refs[-1]
    pair = pl.program_id(1)
    rows, length = layout.block_rows, layout.length
    turn = 0
    factor = scale * LOG2E
    lane = lax.broadcasted_iota(jnp.int32, (1, LANES), 1)
    query = wide_dot(normed_ref[...], weight_ref[...]).astype(jnp.bfloat16)
    query_ref[...] = query
    keys = jnp.concatenate([ref[...] for ref in key_refs], axis=0)
    values = jnp.concatenate([ref[...] for ref in value_refs], axis=0)
    members = members_ref[...]
    kinds = kinds_ref[...]
    tables = tables_ref[...]
    ones = jnp.ones((length, LANES), jnp.bfloat16)

    @pl.when(pair == 0)
    def _():
        log_ref[...] = jnp.zeros_like(log_ref)

    for side in range(2):
        key_columns = jnp.concatenate([half_of(keys, lane, side), members], axis=1)
        value_columns = jnp.concatenate([half_of(values, lane, side), ones], axis=1)
        extra = group_columns(kinds, tables, side).astype(jnp.bfloat16)
        query_columns = jnp.concatenate([query, extra], axis=1)
        table_row = tables[8 * side : 8 * side + 1]
        for start, stop in row_blocks(rows, 256):
            size = stop - start
            scores = all_scores.at[turn % 2]
            turn += 1
            scores[0:size, 0:length] = wide_dot(query_columns[start:stop], key_columns, NT)
            for tile in range(start // LANES, -(-stop // LANES)):
                first, final = tile * LANES, min(tile * LANES + LANES, rows)
                for slot in range(3):
                    other = tile + slot - 1
                    if other >= layout.query_tiles:
                        continue
                    low, high = first, final
                    if slot == 0:
                        high = min(first + 32, final)
                    if slot == 2:
                        low = first + LANES - 32
                    if low >= high:
                        continue
                    place = layout.tile_start(other)
                    width = min(LANES, length - place)
                    bins = bins_ref[low:high, slot * LANES : (slot + 1) * LANES]
                    bias = look_up(table_row, bins)[:, :width]
                    scores[low - start : high - start, place : place + width] += bias
            block = scores[0:size, 0:length]
            top = jnp.max(block, axis=1, keepdims=True)
            weights = jnp.exp2((block - top) * factor).astype(jnp.bfloat16)
            sums = wide_dot(weights, value_columns)
            total = sums[:, LANES:]
            result = sums[:, :LANES] / total
            if side == 0:
                out_ref[start:stop] = result
            else:
                out_ref[start:stop] += result
            log_total = top + jnp.log(total) * (1.0 / scale)
            log_ref[start:stop] = jnp.where(
                lane == 2 * pair + side, log_total, log_ref[start:stop]
            )


def backward_kernel(layout, scale, first_pair, *refs):
    count = len(layout.pieces)
    query_ref, grad_ref, out_ref, log_ref = refs[:4]
    key_refs = refs[4 : 4 + count]
    value_refs = refs[4 + count : 4 + 2 * count]
    rest = refs[4 + 2 * count :]
    members_ref, kinds_ref, bins_ref, places_ref, tables_ref = rest[:5]
    members_turned_ref, kinds_turned_ref = rest[5:7]
    grad_query_ref = rest[7]
    grad_pair_refs = rest[8 : 8 + count]
    grad_table_ref = rest[8 + count]
    query_wide, grad_wide, query_turned, grad_turned = rest[9 + count : 13 + count]
    all_scores, slopes_low, probs_low = rest[13 + count :]
    pair = pl.program_id(1) + first_pair
    rows, length, padded = layout.block_rows, layout.length, layout.padded
    factor = scale * LOG2E
    lane = lax.broadcasted_iota(jnp.int32, (1, LANES), 1)
    keys = jnp.concatenate([ref[...] for ref in key_refs], axis=0)
    values = jnp.concatenate([ref[...] for ref in value_refs], axis=0)
    members = members_ref[...]
    kinds = kinds_ref[...]
    tables = tables_ref[...]
    query = query_ref[...]
    grad = grad_ref[...]
    grad_full = grad.astype(jnp.float32)
    product = grad_full * out_ref[...]
    log_all = log_ref[...]
    tail = 2 * layout.groups
    ones = jnp.broadcast_to(jnp.where(lane < 3, 1.0, 0.0), (length, LANES)).astype(jnp.bfloat16)

    def three_parts(values):
        upper = values.astype(jnp.bfloat16).astype(jnp.float32)
        values = values - upper
        middle = values.astype(jnp.bfloat16).astype(jnp.float32)
        return upper, middle, values - middle

    def in_lanes(parts, first):
        return jnp.where(
            lane == first,
            parts[0],
            jnp.where(lane == first + 1, parts[1], jnp.where(lane == first + 2, parts[2], 0.0)),
        )

    if padded > rows:
        for ref in (query_wide, grad_wide):
            for side in range(2):
                ref[side, rows:padded] = jnp.zeros((padded - rows, ref.shape[2]), jnp.bfloat16)
        for ref in (query_turned, grad_turned):
            ref[:, rows:padded] = jnp.zeros((LANES, padded - rows), jnp.bfloat16)
    query_turned[:, 0:rows] = query.T
    grad_turned[:, 0:rows] = grad.T
    for side in range(2):
        log_total = jnp.sum(
            jnp.where(lane == 2 * pair + side, log_all, 0.0), axis=1, keepdims=True
        )
        extra = group_columns(kinds, tables, side) + in_lanes(three_parts(log_total), tail)
        query_wide[side, 0:rows, 0:LANES] = query
        query_wide[side, 0:rows, LANES:] = extra.astype(jnp.bfloat16)
        delta = jnp.sum(half_of(product, lane, side), axis=1, keepdims=True)
        grad_wide[side, 0:rows, 0:LANES] = grad
        grad_wide[side, 0:rows, LANES:] = in_lanes(three_parts(-delta), 0).astype(jnp.bfloat16)

    key_columns = [
        jnp.concatenate([half_of(keys, lane, side), members], axis=1) for side in range(2)
    ]
    value_columns = [
        jnp.concatenate([half_of(values, lane, side), ones], axis=1) for side in range(2)
    ]
    inner_sums = [jnp.zeros((1, LANES), jnp.float32) for _ in range(2)]
    low_sums = [jnp.zeros((1, LANES), jnp.float32) for _ in range(2)]
    high_sums = [jnp.zeros((1, LANES), jnp.float32) for _ in range(2)]
    reach_tiles = list(range(layout.query_tiles)) + [-1]

    def put(which, start, stop, result):
        begin = 0
        for ref, size in zip(grad_pair_refs, layout.pieces):
            low, high = max(start, begin), min(stop, begin + size)
            if low < high:
                ref[which, low - begin : high - begin] = result[low - start : high - start]
            begin += size

    for start, stop in row_blocks(length, 384):
        size = stop - start
        for side in range(2):
            table_row = tables[8 * side : 8 * side + 1]
            scores = all_scores.at[side]
            scores[0:size] = wide_dot(key_columns[side][start:stop], query_wide[side], NT)
            near = []
            for index, tile in enumerate(reach_tiles):
                place = layout.tile_start(tile)
                if start <= place < stop:
                    near.append((index, tile, place, min(place + LANES, length)))
            for index, tile, place, final in near:
                for slot in range(3):
                    other = tile + slot - 1
                    if not 0 <= other < layout.query_tiles:
                        continue
                    across = slice(other * LANES, (other + 1) * LANES)
                    rows_here = final - place
                    if slot == 1:
                        parts = [(0, rows_here, True)]
                    elif slot == 0:
                        parts = [(0, min(32, rows_here), True), (32, rows_here, False)]
                    else:
                        near_from = max(rows_here - 32, 0)
                        parts = [(0, near_from, False), (near_from, rows_here, True)]
                    for low_row, high_row, inner in parts:
                        if low_row >= high_row:
                            continue
                        bins = bins_ref[
                            index * LANES + low_row : index * LANES + high_row,
                            slot * LANES : (slot + 1) * LANES,
                        ]
                        if inner:
                            bias = look_up(table_row, bins)
                        else:
                            top_bin = 2 * (NEAR + 1)
                            bias = jnp.where(
                                bins == top_bin,
                                table_row[:, top_bin : top_bin + 1],
                                jnp.where(bins == 0, table_row[:, 0:1], 0.0),
                            )
                        scores[place - start + low_row : place - start + high_row, across] += bias
            probs = jnp.exp2(scores[0:size] * factor)
            grad_probs = wide_dot(value_columns[side][start:stop], grad_wide[side], NT)
            probs_low[side, start:stop] = probs.astype(jnp.bfloat16)
            slopes_low[side, start:stop] = (probs * grad_probs).astype(jnp.bfloat16)
            for index, tile, place, final in near:
                for slot in range(3):
                    other = tile + slot - 1
                    if not 0 <= other < layout.query_tiles:
                        continue
                    bins = bins_ref[
                        index * LANES : index * LANES + final - place,
                        slot * LANES : (slot + 1) * LANES,
                    ]
                    cut = slopes_low[side, place:final, other * LANES : (other + 1) * LANES].astype(
                        jnp.float32
                    )
                    low_sums[side] += jnp.sum(
                        jnp.where(bins == 0, cut, 0.0), axis=0, keepdims=True
                    )
                    high_sums[side] += jnp.sum(
                        jnp.where(bins == 2 * (NEAR + 1), cut, 0.0), axis=0, keepdims=True
                    )
                for half in range(2):
                    base = 0 if tile < 0 else tile - 1 + half
                    for step in range(2):
                        other = base + step
                        if not 0 <= other < layout.query_tiles or (tile < 0 and step):
                            continue
                        begin, end = half * 64, half * 64 + 64
                        if tile >= 0 and other == tile - 1:
                            end = begin + 32
                        if tile >= 0 and other == tile + 1:
                            begin = end - 32
                        end = min(end, final - place)
                        if begin >= end:
                            continue
                        where = places_ref[index * LANES + begin : index * LANES + end]
                        spot = where & (LANES - 1)
                        cut = slopes_low[
                            side, place + begin : place + end, other * LANES : (other + 1) * LANES
                        ].astype(jnp.float32)
                        picked = jnp.take_along_axis(cut, spot, axis=1, mode="promise_in_bounds")
                        picked = jnp.where((where >> 7) == step, picked, 0.0)
                        inner_sums[side] += jnp.sum(picked, axis=0, keepdims=True)

    keys_turned = keys.T
    grad_keys, grad_values, grad_queries = [], [], []
    kinds_turned = kinds_turned_ref[...]
    for side in range(2):
        cut = slice(64 * side, 64 * side + 64)
        grad_values.append(wide_dot(grad_turned[cut], probs_low[side], NT))
        grad_keys.append(wide_dot(query_turned[cut], slopes_low[side], NT))
        left = jnp.concatenate([keys_turned[cut], members_turned_ref[...]], axis=0)
        both = wide_dot(left, slopes_low[side])
        grad_queries.append(both[:64])
        sums = both[64:]

        def total(kind):
            return jnp.sum(jnp.where(kinds_turned == kind, sums, 0.0))

        right = total(RIGHT) + jnp.sum(high_sums[side])
        left = total(LEFT) + jnp.sum(low_sums[side])
        apart = total(APART)
        grad_table_ref[side : side + 1] = jnp.where(
            lane == 0,
            left,
            jnp.where(
                lane == 2 * (NEAR + 1),
                right,
                jnp.where(lane == 2 * (NEAR + 1) + 1, apart, inner_sums[side]),
            ),
        )
    put(0, 0, length, (jnp.concatenate(grad_keys, axis=0) * scale).T.astype(jnp.bfloat16))
    put(1, 0, length, jnp.concatenate(grad_values, axis=0).T.astype(jnp.bfloat16))
    turned = jnp.concatenate(grad_queries, axis=0) * scale
    grad_query_ref[...] = turned.T[0:rows].astype(jnp.bfloat16)


def tile_columns(rows, offset=0):
    return pl.BlockSpec((None, rows, LANES), lambda crop, pair: (crop, 0, pair + offset))


def per_crop(rows, width):
    return pl.BlockSpec((None, rows, width), lambda crop, pair: (crop, 0, 0))


def kernel_params():
    return pltpu.CompilerParams(
        vmem_limit_bytes=VMEM_BYTES, dimension_semantics=("arbitrary", "arbitrary")
    )


def attention_forward(layout, scale, normed, weight, key_values, members, kinds, bins, tables):
    crops, rows, width = normed.shape
    pairs = tables.shape[0]
    specs = [per_crop(rows, width), pl.BlockSpec((width, LANES), lambda crop, pair: (0, pair))]
    operands = [normed, weight]
    for place in (1, 2):
        for piece in key_values:
            specs.append(tile_columns(piece[0].shape[1], piece[place]))
            operands.append(piece[0])
    specs += [
        per_crop(layout.length, LANES),
        per_crop(rows, LANES),
        per_crop(layout.padded, 3 * LANES),
        pl.BlockSpec((None, 16, LANES), lambda crop, pair: (pair, 0, 0)),
    ]
    flops = 2 * crops * pairs * 2 * rows * layout.length * 256 * 2
    return pl.pallas_call(
        functools.partial(forward_kernel, layout, scale),
        grid=(crops, pairs),
        in_specs=specs,
        out_specs=(tile_columns(rows), tile_columns(rows), per_crop(rows, LANES)),
        out_shape=(
            jax.ShapeDtypeStruct((crops, rows, pairs * LANES), jnp.bfloat16),
            jax.ShapeDtypeStruct((crops, rows, pairs * LANES), jnp.float32),
            jax.ShapeDtypeStruct((crops, rows, LANES), jnp.float32),
        ),
        scratch_shapes=[pltpu.VMEM((2, 256, layout.wide), jnp.float32)],
        compiler_params=kernel_params(),
        cost_estimate=pl.CostEstimate(
            flops=flops,
            bytes_accessed=12 * crops * rows * pairs * LANES,
            transcendentals=crops * pairs * 2 * rows * layout.length,
        ),
        name="attention_forward",
    )(*operands, members, kinds, bins, tables)


def attention_backward(
    layout,
    scale,
    first_pair,
    pairs,
    projected,
    grad_out,
    attended,
    logs,
    key_values,
    members,
    kinds,
    bins,
    places,
    members_turned,
    kinds_turned,
    tables,
):
    crops, rows, _ = projected.shape
    specs = [tile_columns(rows, first_pair)] * 3 + [per_crop(rows, LANES)]
    operands = [projected, grad_out, attended, logs]
    for place in (1, 2):
        for piece in key_values:
            specs.append(tile_columns(piece[0].shape[1], piece[place] + first_pair))
            operands.append(piece[0])
    specs += [
        per_crop(layout.length, LANES),
        per_crop(rows, LANES),
        per_crop(bins.shape[1], 3 * LANES),
        per_crop(places.shape[1], LANES),
        pl.BlockSpec((None, 16, LANES), lambda crop, pair: (pair + first_pair, 0, 0)),
        per_crop(64, layout.length),
        per_crop(64, layout.padded),
    ]
    out_specs = [tile_columns(rows)]
    out_shapes = [jax.ShapeDtypeStruct((crops, rows, pairs * LANES), jnp.bfloat16)]
    for piece in key_values:
        size = piece[0].shape[1]
        out_specs.append(
            pl.BlockSpec((None, 2, size, LANES), lambda crop, pair: (crop, 0, 0, pair))
        )
        out_shapes.append(jax.ShapeDtypeStruct((crops, 2, size, pairs * LANES), jnp.bfloat16))
    out_specs.append(pl.BlockSpec((None, None, 8, LANES), lambda crop, pair: (crop, pair, 0, 0)))
    out_shapes.append(jax.ShapeDtypeStruct((crops, pairs, 8, LANES), jnp.float32))
    padded, block = layout.padded, 384
    return pl.pallas_call(
        functools.partial(backward_kernel, layout, scale, first_pair),
        grid=(crops, pairs),
        in_specs=specs,
        out_specs=tuple(out_specs),
        out_shape=tuple(out_shapes),
        scratch_shapes=[
            pltpu.VMEM((2, padded, 2 * LANES), jnp.bfloat16),
            pltpu.VMEM((2, padded, 2 * LANES), jnp.bfloat16),
            pltpu.VMEM((LANES, padded), jnp.bfloat16),
            pltpu.VMEM((LANES, padded), jnp.bfloat16),
            pltpu.VMEM((2, block, padded), jnp.float32),
            pltpu.VMEM((2, layout.length, padded), jnp.bfloat16),
            pltpu.VMEM((2, layout.length, padded), jnp.bfloat16),
        ],
        compiler_params=kernel_params(),
        cost_estimate=pl.CostEstimate(
            flops=2 * crops * pairs * 2 * rows * layout.length * 256 * 5,
            bytes_accessed=20 * crops * rows * pairs * LANES,
            transcendentals=crops * pairs * 2 * rows * layout.length,
        ),
        name="attention_backward",
    )(*operands, members, kinds, bins, places, tables, members_turned, kinds_turned)


def sigmoid(values):
    return 0.5 * jnp.tanh(0.5 * values) + 0.5


def each_strip(rows, body, size=16):
    count = rows // size
    group = max(number for number in range(1, 9) if count % number == 0)

    @pl.loop(0, count // group)
    def _(index):
        for part in range(group):
            body(pl.ds(pl.multiple_of((index * group + part) * size, size), size))


def fold_rows(values):
    return jnp.sum(values.reshape(values.shape[0] // 8, 8, values.shape[1]), axis=0)


def feed_kernel(split, chunks, here_ref, *refs):
    (attended_ref, tokens_ref, upstream_ref, normed_a_ref, mod_ref, gate_weight_ref, output_ref) = refs[:7]
    gate_ref, up_ref, down_ref = refs[7:10]
    layer_ref, grad_middle_ref, grad_att_ref, grad_pre_ref, sums_ref = refs[10:15]
    grads = refs[15:-12]
    gated, grad_ff, normed, branch, middle, total, grad_normed, hidden, both, grad_branch = refs[-12:-2]
    gate_pre, turned = refs[-2:]
    step = pl.program_id(0)
    here = here_ref[0]
    rows, width = tokens_ref.shape
    size = gate_ref.shape[1]
    strip = 112 if rows % 112 == 0 else 64
    strips = rows // strip
    shift_f, scale_f = mod_ref[3:4], mod_ref[4:5]
    open_a, open_f = sigmoid(mod_ref[2:3]), sigmoid(mod_ref[5:6])

    def strip_of(index):
        return pl.ds(pl.multiple_of(index * strip, strip), strip)

    def norm_of(values):
        mean_value = jnp.mean(values, axis=1, keepdims=True)
        centred = values - mean_value
        spread = jnp.mean(centred * centred, axis=1, keepdims=True)
        root = lax.rsqrt(spread + 1e-06)
        return centred * root, root

    @pl.when(step == 0)
    def _():
        gate_pre[...] = wide_dot(normed_a_ref[...], gate_weight_ref[...])

        @pl.loop(0, strips)
        def _(index):
            cut = strip_of(index)
            gated[cut] = (attended_ref[cut] * sigmoid(gate_pre[cut])).astype(jnp.bfloat16)
            grad_ff[cut] = (upstream_ref[cut].astype(jnp.float32) * open_f).astype(jnp.bfloat16)

        branch[...] = wide_dot(gated[...], output_ref[...])

        @pl.loop(0, strips)
        def _(index):
            cut = strip_of(index)
            values = tokens_ref[cut].astype(jnp.float32) + open_a * branch[cut]
            middle[cut] = values
            normed[cut] = (norm_of(values)[0] * (1.0 + scale_f) + shift_f).astype(jnp.bfloat16)
            total[cut] = jnp.zeros((strip, width), jnp.float32)
            grad_normed[cut] = jnp.zeros((strip, width), jnp.float32)

        turned[...] = normed[...].T

    block = rows if rows <= 384 else rows // 2
    cuts = [slice(start, start + block) for start in range(0, rows, block)]
    firsts = [
        (
            wide_dot(normed[cut], gate_ref[...]),
            wide_dot(normed[cut], up_ref[...]),
            wide_dot(grad_ff[cut], down_ref[...], NT),
        )
        for cut in cuts
    ]
    for cut, (before, lifted, grad_hidden) in zip(cuts, firsts):
        switch = sigmoid(before)
        silu = before * switch
        hidden[cut] = (silu * lifted).astype(jnp.bfloat16)
        both[cut, :size] = (
            grad_hidden * lifted * (switch + silu * (1.0 - switch))
        ).astype(jnp.bfloat16)
        both[cut, size:] = (grad_hidden * silu).astype(jnp.bfloat16)
    for cut in cuts:
        total[cut] += wide_dot(hidden[cut], down_ref[...])
        grad_normed[cut] += wide_dot(both[cut, :size], gate_ref[...], NT) + wide_dot(
            both[cut, size:], up_ref[...], NT
        )

    pair = wide_dot(turned[...], both[...]).astype(jnp.bfloat16)
    if split:
        gate_send, gate_keep, up_send, up_keep, down_send, down_keep, small_send, small_keep = grads
        half = width // 2
        away = pl.ds(pl.multiple_of((1 - here) * half, LANES), half)
        home = pl.ds(pl.multiple_of(here * half, LANES), half)
        down_send[...] = wide_dot(hidden[...], grad_ff[:, away], TN).astype(jnp.bfloat16)
        down_keep[...] = wide_dot(hidden[...], grad_ff[:, home], TN).astype(jnp.bfloat16)

        @pl.when(step < chunks // 2)
        def _():
            gate_send[...] = pair[:, :size]
            up_send[...] = pair[:, size:]

        @pl.when(step >= chunks // 2)
        def _():
            gate_keep[...] = pair[:, :size]
            up_keep[...] = pair[:, size:]
    else:
        gate_all, up_all, down_all, small_all = grads
        gate_all[...] = pair[:, :size]
        up_all[...] = pair[:, size:]
        down_all[...] = wide_dot(hidden[...], grad_ff[...], TN).astype(jnp.bfloat16)

    @pl.when(step == chunks - 1)
    def _():
        def finish(index, sums):
            gate_f_sum, shift_sum, scale_sum, gate_a_sum = sums
            cut = strip_of(index)
            values = middle[cut]
            fed = total[cut]
            upstream = upstream_ref[cut].astype(jnp.float32)
            layer_ref[cut] = (values + open_f * fed).astype(jnp.bfloat16)
            normal, root = norm_of(values)
            grad = grad_normed[cut]
            scaled = grad * (1.0 + scale_f)
            grad_middle = upstream + root * (
                scaled
                - jnp.mean(scaled, axis=1, keepdims=True)
                - normal * jnp.mean(scaled * normal, axis=1, keepdims=True)
            )
            grad_middle_ref[cut] = grad_middle
            grad_branch[cut] = (grad_middle * open_a).astype(jnp.bfloat16)
            return (
                gate_f_sum + fold_rows(upstream * fed),
                shift_sum + fold_rows(grad),
                scale_sum + fold_rows(grad * normal),
                gate_a_sum + fold_rows(grad_middle * branch[cut]),
            )

        zero = jnp.zeros((8, width), jnp.float32)
        sums = lax.fori_loop(0, strips, finish, (zero, zero, zero, zero))
        gate_f_sum, shift_sum, scale_sum, gate_a_sum = [
            jnp.sum(value, axis=0, keepdims=True) for value in sums
        ]
        none = jnp.zeros((1, width), jnp.float32)
        sums_ref[...] = jnp.concatenate(
            [
                none,
                none,
                gate_a_sum * open_a * (1.0 - open_a),
                shift_sum,
                scale_sum,
                gate_f_sum * open_f * (1.0 - open_f),
                none,
                none,
            ],
            axis=0,
        )
        total[...] = wide_dot(grad_branch[...], output_ref[...], NT)

        @pl.loop(0, strips)
        def _(index):
            cut = strip_of(index)
            grad_gated = total[cut]
            opened = sigmoid(gate_pre[cut])
            grad_att_ref[cut] = (grad_gated * opened).astype(jnp.bfloat16)
            grad_pre_ref[cut] = (
                grad_gated * attended_ref[cut] * (opened * (1.0 - opened))
            ).astype(jnp.bfloat16)

        if split:
            for side, ref in ((away, small_send), (home, small_keep)):
                ref[:, :half] = wide_dot(gated[...], grad_branch[:, side], TN).astype(jnp.bfloat16)
                ref[:, half:] = wide_dot(normed_a_ref[...], grad_pre_ref[:, side], TN).astype(
                    jnp.bfloat16
                )
        else:
            small_all[:, :width] = wide_dot(gated[...], grad_branch[...], TN).astype(jnp.bfloat16)
            small_all[:, width:] = wide_dot(normed_a_ref[...], grad_pre_ref[...], TN).astype(
                jnp.bfloat16
            )


def feed_layer(
    split, here, attended, tokens, upstream, normed_a, mod_rows, gate_weight, output_weight, feed_gate, feed_up, feed_down
):
    rows, width = tokens.shape
    inner = feed_gate.shape[1]
    size = 512
    chunks = inner // size
    half = chunks // 2

    def turn(step, here_ref):
        return (step + half * (1 - here_ref[0])) % chunks if split else step

    def fixed(shape):
        return pl.BlockSpec(shape, lambda step, here_ref: (0, 0), pipeline_mode=pl.Buffered(1))

    def columns(step, here_ref):
        return (0, turn(step, here_ref))

    def strips(step, here_ref):
        return (turn(step, here_ref), 0)

    whole = (rows, width)
    in_specs = [fixed(whole)] * 4 + [
        fixed((8, width)),
        fixed((width, width)),
        fixed((width, width)),
        pl.BlockSpec((width, size), columns),
        pl.BlockSpec((width, size), columns),
        pl.BlockSpec((size, width), strips),
    ]
    out_specs = [fixed(whole)] * 4 + [fixed((8, width))]
    bf16, f32 = jnp.bfloat16, jnp.float32
    out_shapes = [(whole, bf16), (whole, f32), (whole, bf16), (whole, bf16), ((8, width), f32)]
    if split:
        first = pl.BlockSpec((width, size), lambda step, here_ref: (0, jnp.minimum(step, half - 1)))
        second = pl.BlockSpec((width, size), lambda step, here_ref: (0, jnp.maximum(step - half, 0)))
        out_specs += [first, second, first, second]
        out_shapes += [((width, inner // 2), bf16)] * 4
        out_specs += [pl.BlockSpec((size, width // 2), strips)] * 2
        out_shapes += [((inner, width // 2), bf16)] * 2
        out_specs += [fixed((width, width))] * 2
        out_shapes += [((width, width), bf16)] * 2
    else:
        out_specs += [pl.BlockSpec((width, size), columns)] * 2
        out_shapes += [((width, inner), bf16)] * 2
        out_specs += [pl.BlockSpec((size, width), strips), fixed((width, 2 * width))]
        out_shapes += [((inner, width), bf16), ((width, 2 * width), bf16)]
    return pl.pallas_call(
        functools.partial(feed_kernel, split, chunks),
        grid_spec=pltpu.PrefetchScalarGridSpec(
            num_scalar_prefetch=1,
            grid=(chunks,),
            in_specs=in_specs,
            out_specs=tuple(out_specs),
            scratch_shapes=[
                pltpu.VMEM(whole, bf16),
                pltpu.VMEM(whole, bf16),
                pltpu.VMEM(whole, bf16),
                pltpu.VMEM(whole, f32),
                pltpu.VMEM(whole, f32),
                pltpu.VMEM(whole, f32),
                pltpu.VMEM(whole, f32),
                pltpu.VMEM((rows, size), bf16),
                pltpu.VMEM((rows, 2 * size), bf16),
                pltpu.VMEM(whole, bf16),
                pltpu.VMEM(whole, f32),
                pltpu.VMEM((width, rows), bf16),
            ],
        ),
        out_shape=tuple(jax.ShapeDtypeStruct(shape, kind) for shape, kind in out_shapes),
        compiler_params=pltpu.CompilerParams(vmem_limit_bytes=VMEM_BYTES),
        cost_estimate=pl.CostEstimate(
            flops=2 * rows * width * (9 * inner + 5 * width),
            bytes_accessed=12 * width * inner + 24 * rows * width,
            transcendentals=2 * rows * inner,
        ),
        name="feed_layer",
    )(
        jnp.reshape(here, (1,)).astype(jnp.int32),
        attended,
        tokens,
        upstream,
        normed_a,
        mod_rows,
        gate_weight,
        output_weight,
        feed_gate,
        feed_up,
        feed_down,
    )


MASKS = {"u": 8, "v": 4, "y": 2, "x": 1}


def exchange(values, mask):
    return lax.ppermute(values, "crop", [(i, i ^ mask) for i in range(16)])


def swap_res(values):
    return lax.ppermute(values, "res", [(0, 1), (1, 0)])


def tie(*values):
    return lax.optimization_barrier(values)


def add_low(former, latter, kind=jnp.bfloat16):
    return (former.astype(jnp.float32) + latter.astype(jnp.float32)).astype(kind)


def stage_kernel(plans, bits_ref, *refs):
    inputs = refs[: sum(plan["count"] for plan in plans)]
    outputs = list(refs[len(inputs) :])
    for plan in plans:
        mine, inputs = inputs[: plan["count"]], inputs[plan["count"] :]
        out_ref = None if plan["apart"] else outputs[0]
        if not plan["apart"] and plan["merge"] is None:
            outputs.pop(0)
        for column, width, own in plan["parts"]:
            result = outputs.pop(0) if plan["apart"] else out_ref
            target = 0 if plan["apart"] else column
            lead_sizes = () if plan["merge"] is not None else result.shape[:-2]
            for lead in itertools.product(*[range(size) for size in lead_sizes]):
                for first in range(0, plan["rows"], 16):
                    cut = (*lead, slice(first, first + 16))
                    across = slice(column, column + width)
                    total = None
                    for index in own:
                        value = mine[index][(*cut, slice(0, width))].astype(jnp.float32)
                        total = value if total is None else total + value
                    for index in plan["spans"]:
                        total = total + mine[index][(*cut, across)].astype(jnp.float32)
                    fold, local = first // plan["block"], first % plan["block"]
                    if plan["folds"]:
                        value = mine[plan["folds"][fold]][local : local + 16, across]
                        total = total + value.astype(jnp.float32)
                    if plan["merge"] is None:
                        result[(*cut, slice(target, target + width))] = total.astype(result.dtype)
                    else:
                        begin = plan["merge"] + fold * plan["wide"] + column
                        result[local : local + 16, begin : begin + width] = total.astype(result.dtype)


class Halving:
    def __init__(self, streams, orders):
        self.streams = streams
        self.orders = [list(order) for order in orders]
        self.past = [[] for _ in orders]
        self.came = [[] for _ in orders]

    def stage(self, last=False, merge=False, merged=None):
        index = lax.axis_index("crop")
        bits = scalars(*[(index // mask) % 2 for mask in MASKS.values()])
        self.masks, plans, specs, operands, out_specs, out_shapes = [], [], [], [], [], []
        left = 0 if last else len(self.orders[0]) - 1
        fewest = min(parts[0][0][0].shape[0] for parts in self.streams) // 16
        begin = 0
        steps = {3: 4, 2: 2}.get(left, 1)
        for stream, (parts, order, past) in enumerate(zip(self.streams, self.orders, self.past)):
            now = None if last else order.pop(0)
            rest = [axis for axis in MASKS if axis in order]

            def spec_of(axes, rows, width, block, now=now, rest=rest):
                def index_map(step, bits_ref):
                    places = []
                    for axis in axes:
                        bit = bits_ref[list(MASKS).index(axis)]
                        if axis == now:
                            places.append(1 - bit)
                        elif axis not in rest:
                            places.append(bit)
                        elif axis == rest[0] and steps > 1:
                            places.append(step // (steps // 2))
                        elif len(rest) > 1 and axis == rest[1] and steps > 2:
                            places.append(step % 2)
                        else:
                            places.append(0)
                    return (*places, 0, block)

                sizes = [
                    2
                    if axis in rest
                    and not (axis == rest[0] and steps > 1)
                    and not (len(rest) > 1 and axis == rest[1] and steps > 2)
                    else None
                    for axis in axes
                ]
                return pl.BlockSpec((*sizes, rows, width), index_map)

            column = 0
            rows = parts[0][0][0].shape[0] // 16
            wide = sum(width for _, _, width in parts)
            plan = {
                "parts": [],
                "spans": [],
                "folds": [],
                "count": 0,
                "apart": last,
                "rows": rows,
                "block": fewest,
                "wide": wide,
                "merge": begin if merge else None,
            }
            for arrays, block, width in parts:
                own = []
                for value in arrays:
                    operands.append(value.reshape(2, 2, 2, 2, rows, value.shape[1]))
                    specs.append(spec_of(list(MASKS), rows, width, block))
                    own.append(plan["count"])
                    plan["count"] += 1
                plan["parts"].append((column, width, own))
                column += width
            for axes, value in self.came[stream]:
                operands.append(value.reshape(*[2] * len(axes), rows, column))
                specs.append(spec_of(axes, rows, column, 0))
                plan["spans"].append(plan["count"])
                plan["count"] += 1
            if merged is not None:
                for fold in range(rows // fewest):
                    place = (begin + fold * wide) // wide
                    operands.append(merged)
                    specs.append(
                        pl.BlockSpec((fewest, wide), lambda step, bits_ref, place=place: (0, place))
                    )
                    plan["folds"].append(plan["count"])
                    plan["count"] += 1
            begin += wide * (rows // fewest)
            plans.append(plan)
            if last:
                for _, width, _ in plan["parts"]:
                    out_specs.append(pl.BlockSpec((rows, width), lambda step, bits_ref: (0, 0)))
                    out_shapes.append(jax.ShapeDtypeStruct((rows, width), jnp.float32))
            else:
                past.append(now)
                self.masks.append(MASKS[now])
                if not merge:
                    out_specs.append(spec_of(rest, rows, column, 0))
                    out_shapes.append(
                        jax.ShapeDtypeStruct((*[2] * len(rest), rows, column), jnp.bfloat16)
                    )
        if merge:
            out_specs.append(pl.BlockSpec((fewest, begin), lambda step, bits_ref: (0, 0)))
            out_shapes.append(jax.ShapeDtypeStruct((fewest, begin), jnp.bfloat16))
        self.axes = [[axis for axis in MASKS if axis in order] for order in self.orders]
        results = pl.pallas_call(
            functools.partial(stage_kernel, plans),
            grid_spec=pltpu.PrefetchScalarGridSpec(
                num_scalar_prefetch=1, grid=(steps,), in_specs=specs, out_specs=tuple(out_specs)
            ),
            out_shape=tuple(out_shapes),
            compiler_params=pltpu.CompilerParams(vmem_limit_bytes=VMEM_BYTES),
            cost_estimate=pl.CostEstimate(
                flops=sum(4 * math.prod(shape.shape) for shape in out_shapes),
                bytes_accessed=sum(8 * math.prod(shape.shape) for shape in out_shapes),
                transcendentals=0,
            ),
            name="halving_stage",
        )(bits, *operands)
        if merge or last:
            return list(results)
        return [value.reshape(-1, value.shape[-1]) for value in results]

    def send(self, values):
        return [exchange(value, mask) for value, mask in zip(values, self.masks)]

    def take(self, values):
        for came, axes, value in zip(self.came, self.axes, values):
            came.append((axes, value))


def share_columns(values, parts):
    if parts == 1:
        return values.astype(jnp.bfloat16)
    return lax.psum_scatter(values.astype(jnp.bfloat16), "res", scatter_dimension=1, tiled=True)


def scatter_crops(values):
    return lax.psum_scatter(values, "crop", scatter_dimension=0, tiled=True).astype(jnp.float32)


def gather_crops(values, crop_parts):
    if crop_parts != 16:
        return lax.all_gather(values, "crop", axis=0, tiled=True)
    index = lax.axis_index("crop")
    for mask in (1, 2, 4, 8):
        other = exchange(values, mask)
        low = (index // mask) % 2 == 0
        values = jnp.concatenate(
            [jnp.where(low, values, other), jnp.where(low, other, values)], axis=0
        )
    return values


def sum_res(values, parts):
    if parts == 1:
        return values
    if parts != 2:
        return lax.psum(values, "res")
    return values + swap_res(values)


PACK = 1152
SIDE = 384


def whole_vmem(count):
    return [pl.BlockSpec(memory_space=pltpu.VMEM)] * count


def scalars(*values):
    return jnp.stack([jnp.asarray(value, jnp.int32) for value in values])


def local_call(kernel, numbers, operands, shapes, name, flops=0):
    return pl.pallas_call(
        kernel,
        in_specs=[pl.BlockSpec(memory_space=pltpu.SMEM)] + whole_vmem(len(operands)),
        out_specs=tuple(whole_vmem(len(shapes))),
        out_shape=tuple(jax.ShapeDtypeStruct(shape, kind) for shape, kind in shapes),
        compiler_params=pltpu.CompilerParams(vmem_limit_bytes=VMEM_BYTES),
        cost_estimate=pl.CostEstimate(
            flops=flops,
            bytes_accessed=sum(value.size * value.dtype.itemsize for value in operands)
            + sum(4 * math.prod(shape) for shape, _ in shapes),
            transcendentals=0,
        ),
        name=name,
    )(numbers, *operands)


def projection_kernel(counts, here_ref, normed_ref, *refs):
    calls = len(counts)
    parts, (joined_ref, send_ref, keep_ref) = refs[: 3 * calls], refs[3 * calls :]
    width = joined_ref.shape[1] // 3
    column = 0
    for call, pairs in enumerate(counts):
        size = pairs * LANES
        query_ref, own_ref, came_ref = parts[3 * call : 3 * call + 3]
        joined_ref[:, column : column + size] = query_ref[...]
        for start in range(0, joined_ref.shape[0], 16):
            cut = slice(start, start + 16)
            for which in range(2):
                first = (1 + which) * width + column
                joined_ref[cut, first : first + size] = add_low(
                    own_ref[which, cut], came_ref[which, cut]
                )
        column += size
    half = send_ref.shape[1]
    for side, ref in ((1 - here_ref[0], send_ref), (here_ref[0], keep_ref)):
        columns = pl.ds(pl.multiple_of(side * half, LANES), half)
        ref[...] = wide_dot(normed_ref[...], joined_ref[:, columns], TN).astype(jnp.bfloat16)


def projection_gradient(here, normed_a, calls):
    rows, width = normed_a.shape
    counts = [call[0].shape[-1] // LANES for call in calls]
    return local_call(
        functools.partial(projection_kernel, counts),
        scalars(here),
        [normed_a] + [value for call in calls for value in call],
        [
            ((rows, 3 * width), jnp.bfloat16),
            ((width, 3 * width // 2), jnp.bfloat16),
            ((width, 3 * width // 2), jnp.bfloat16),
        ],
        "projection_gradient",
        6 * rows * width * width,
    )


def finish_kernel(counts, joined_ref, weight_ref, pre_ref, gate_ref, tokens_ref, middle_ref, mod_ref, *refs):
    feed_sums_ref, extra_ref = refs[:2]
    table_refs = refs[2 : 2 + len(counts)]
    out_ref, pack_ref, total, folded = refs[2 + len(counts) :]
    step = pl.program_id(0)
    rows, width = tokens_ref.shape
    part = wide_dot(joined_ref[...], weight_ref[...], NT)

    @pl.when(step == 0)
    def _():
        total[...] = part + wide_dot(pre_ref[...], gate_ref[...], NT)

    @pl.when(step > 0)
    def _():
        total[...] += part

    @pl.when(step == pl.num_programs(0) - 1)
    def _():
        scale = mod_ref[1:2]
        folded[...] = jnp.zeros_like(folded)

        def finish(cut):
            values = tokens_ref[cut].astype(jnp.float32)
            centred = values - jnp.mean(values, axis=1, keepdims=True)
            root = lax.rsqrt(jnp.mean(centred * centred, axis=1, keepdims=True) + 1e-06)
            normal = centred * root
            grad = total[cut]
            folded[0] += fold_rows(grad)
            folded[1] += fold_rows(grad * normal)
            scaled = grad * (1.0 + scale)
            out_ref[cut] = (
                middle_ref[cut]
                + root
                * (
                    scaled
                    - jnp.mean(scaled, axis=1, keepdims=True)
                    - normal * jnp.mean(scaled * normal, axis=1, keepdims=True)
                )
            ).astype(jnp.bfloat16)

        each_strip(rows, finish)
        shift_sum, scale_sum = folded[0], folded[1]
        heads = []
        for ref, pairs in zip(table_refs, counts):
            for pair in range(pairs):
                heads += [ref[pair, 0:1], ref[pair, 1:2]]

        def upper_of(values):
            return values.astype(jnp.bfloat16).astype(jnp.float32)

        rests = [head - upper_of(head) for head in heads]
        count = width // LANES
        left = [
            jnp.sum(shift_sum, axis=0, keepdims=True),
            jnp.sum(scale_sum, axis=0, keepdims=True),
            feed_sums_ref[2:6],
        ]
        left += [
            jnp.concatenate(rests[i : i + count], axis=1) for i in range(0, len(heads), count)
        ]
        right = [jnp.concatenate(heads[3 * i : 3 * i + 3], axis=1) for i in range(4)]
        line = extra_ref[5:6]
        right += [extra_ref[4:5], line, line - upper_of(line), extra_ref[7:8]]
        pack = jnp.concatenate(
            [jnp.concatenate(left, axis=0), jnp.concatenate(right, axis=0)], axis=1
        )
        pack_ref[...] = jnp.concatenate([pack, jnp.zeros_like(pack)], axis=0).astype(jnp.bfloat16)


def finish_layer(
    joined, weight, grad_pre, gate_weight, tokens, grad_middle, mod_rows, feed_sums, extra, grad_tables
):
    rows, width = tokens.shape
    counts = [table.shape[0] for table in grad_tables]

    def fixed(shape):
        return pl.BlockSpec(shape, lambda step: (0,) * len(shape), pipeline_mode=pl.Buffered(1))

    return pl.pallas_call(
        functools.partial(finish_kernel, counts),
        grid=(3,),
        in_specs=[
            pl.BlockSpec((rows, width), lambda step: (0, step)),
            pl.BlockSpec((width, width), lambda step: (0, step)),
            fixed((rows, width)),
            fixed((width, width)),
            fixed((rows, width)),
            fixed((rows, width)),
            fixed((8, width)),
            fixed((8, width)),
            fixed((8, SIDE)),
        ]
        + [fixed((count, 8, LANES)) for count in counts],
        out_specs=(fixed((rows, width)), fixed((16, PACK))),
        out_shape=(
            jax.ShapeDtypeStruct((rows, width), jnp.bfloat16),
            jax.ShapeDtypeStruct((16, PACK), jnp.bfloat16),
        ),
        scratch_shapes=[
            pltpu.VMEM((rows, width), jnp.float32),
            pltpu.VMEM((2, 8, width), jnp.float32),
        ],
        compiler_params=pltpu.CompilerParams(vmem_limit_bytes=VMEM_BYTES),
        cost_estimate=pl.CostEstimate(
            flops=8 * rows * width * width, bytes_accessed=24 * rows * width, transcendentals=0
        ),
        name="finish_layer",
    )(
        joined,
        weight,
        grad_pre,
        gate_weight,
        tokens,
        grad_middle,
        mod_rows,
        feed_sums,
        extra,
        *grad_tables,
    )


def fan_first_kernel(bits_ref, keep_ref, came_ref, mine_ref, *send_refs):
    chunk = keep_ref.shape[0] // 16
    for other, ref in enumerate((mine_ref, *send_refs)):
        for level in range(4):
            start = (level * 4 + (bits_ref[0] ^ other)) * chunk
            for first in range(0, chunk, 16):
                cut = pl.ds(pl.multiple_of(start + first, 16), 16)
                place = level * chunk + first
                ref[place : place + 16] = add_low(keep_ref[cut], came_ref[cut])


def fan_v_kernel(bits_ref, mine_ref, *refs):
    came_refs, (send_ref, out_ref) = refs[:3], refs[3:]
    chunk = mine_ref.shape[0] // 4
    for side, ref in ((1 - bits_ref[0], send_ref), (bits_ref[0], out_ref)):
        for far in range(2):
            for first in range(0, chunk, 16):
                cut = pl.ds(pl.multiple_of((2 * far + side) * chunk + first, 16), 16)
                total = mine_ref[cut].astype(jnp.float32)
                for came_ref in came_refs:
                    total = total + came_ref[cut].astype(jnp.float32)
                place = far * chunk + first
                ref[place : place + 16] = total.astype(jnp.bfloat16)


def fan_u_kernel(bits_ref, mine_ref, came_ref, send_ref, out_ref):
    chunk = mine_ref.shape[0] // 2
    for side, ref in ((1 - bits_ref[0], send_ref), (bits_ref[0], out_ref)):
        for first in range(0, chunk, 16):
            cut = pl.ds(pl.multiple_of(side * chunk + first, 16), 16)
            ref[first : first + 16] = add_low(mine_ref[cut], came_ref[cut])


def join_packs_kernel(bits_ref, *refs):
    packs = [ref[...].astype(jnp.float32)[0:8] for ref in refs[:4]]
    refs[4][...] = jnp.concatenate(packs, axis=0).astype(jnp.bfloat16)


def small_kernel(
    heads,
    here_ref,
    mine_ref,
    came_ref,
    modulation_ref,
    pair_norm_ref,
    relative_ref,
    gain_ref,
    pair_weight_ref,
    mod_grad_ref,
    time_ref,
    label_ref,
    relative_grad_ref,
    gain_grad_ref,
    pair_grad_ref,
    grad_condition,
    grad_mod,
    kept,
):
    step = pl.program_id(0)
    crops = mine_ref.shape[0] // 8
    width = mine_ref.shape[1] - SIDE
    conds = relative_ref.shape[1]
    parts = mod_grad_ref.shape[1] // width

    def parts_split(values):
        upper = values.astype(jnp.bfloat16)
        return upper, (values - upper.astype(jnp.float32)).astype(jnp.bfloat16)

    def dot_left(narrow, values, numbers):
        upper, rest = parts_split(values)
        return wide_dot(narrow, upper, numbers) + wide_dot(narrow, rest, numbers)

    def dot_right(values, narrow, numbers):
        upper, rest = parts_split(values)
        return wide_dot(upper, narrow, numbers) + wide_dot(rest, narrow, numbers)

    def both_twice(narrow):
        return jnp.concatenate([narrow, narrow], axis=0)

    def stacked(values):
        return jnp.concatenate(parts_split(values), axis=0)

    @pl.when(step == 0)
    def _():
        shape = (8 * crops, 8 * crops)
        picked = lax.broadcasted_iota(jnp.int32, shape, 0)
        source = lax.broadcasted_iota(jnp.int32, shape, 1)
        hit = ((source >> 3) == (picked & (crops - 1))) & ((source & 7) == (picked // crops))
        select = jnp.where(hit, 1.0, 0.0).astype(jnp.bfloat16)
        mine = wide_dot(select, mine_ref[...])
        grad_mod[...] = mine[: 6 * crops, :width] + wide_dot(select, came_ref[...])[: 6 * crops, :width]
        condition = (
            mine[5 * crops : 6 * crops, width : width + conds]
            + mine[6 * crops : 7 * crops, width : width + conds]
        )
        gate_value = sigmoid(condition)
        kept[0] = condition * gate_value
        kept[1] = gate_value * (1.0 + condition * (1.0 - gate_value))
        kept[2] = mine[4 * crops : 5 * crops, width : width + conds]
        kept[3] = jnp.broadcast_to(
            mine[5 * crops : 6 * crops, width + conds : width + conds + 1]
            + mine[6 * crops : 7 * crops, width + conds : width + conds + 1],
            (crops, conds),
        )
        grad_condition[...] = jnp.zeros_like(grad_condition)

    cond_act = both_twice(kept[0].astype(jnp.bfloat16))
    for turn in range(parts):
        columns = slice(turn * width, (turn + 1) * width)
        first = pl.multiple_of((step * parts + turn) * crops, crops)
        pair = stacked(grad_mod[pl.ds(first, crops)])
        mod_grad_ref[:, columns] = wide_dot(cond_act, pair, TN)
        more = wide_dot(pair, modulation_ref[:, columns], NT)
        grad_condition[...] += more[:crops] + more[crops:]

    @pl.when(step == 0)
    def _():
        shape = (8, 8 * crops)
        line = lax.broadcasted_iota(jnp.int32, shape, 0)
        local = lax.broadcasted_iota(jnp.int32, shape, 1) & 7
        every = jnp.where(local == line, 1.0, 0.0).astype(jnp.bfloat16)
        lines = wide_dot(every, mine_ref[...]) + wide_dot(every, came_ref[...])

        def of_head(head):
            upper = width + (head % 3) * LANES
            rest = (head % (width // LANES)) * LANES
            low = 6 + head // (width // LANES)
            return (
                lines[head // 3 : head // 3 + 1, upper : upper + LANES]
                + lines[low : low + 1, rest : rest + LANES]
            )

        table = jnp.concatenate(
            [of_head(head) for head in range(heads)]
            + [jnp.zeros((16 - heads, LANES), jnp.float32)],
            axis=0,
        )
        bins = relative_ref.shape[0]
        pair_grad_ref[...] = dot_right(table, pair_norm_ref[...], (((1,), (0,)), ((), ())))[:heads]
        grad_norm = dot_right(table, pair_weight_ref[...], (((0,), (1,)), ((), ())))[:bins]
        values = relative_ref[...].astype(jnp.float32)
        centred = values - jnp.mean(values, axis=1, keepdims=True)
        root = lax.rsqrt(jnp.mean(centred * centred, axis=1, keepdims=True) + 1e-06)
        normal = centred * root
        gain_grad_ref[...] = jnp.sum(grad_norm * normal, axis=0, keepdims=True)
        scaled = grad_norm * gain_ref[...].astype(jnp.float32)
        relative_grad_ref[...] = root * (
            scaled
            - jnp.mean(scaled, axis=1, keepdims=True)
            - normal * jnp.mean(scaled * normal, axis=1, keepdims=True)
        )

    @pl.when(step == pl.num_programs(0) - 1)
    def _():
        final = stacked(grad_condition[...] * kept[1])
        time_ref[...] = wide_dot(both_twice(kept[2].astype(jnp.bfloat16)), final, TN)
        label = lax.broadcasted_iota(jnp.int32, (crops, label_ref.shape[0]), 1)
        number = kept[3][:, 0:1].astype(jnp.int32)
        onehot = jnp.where(label == number, 1.0, 0.0).astype(jnp.bfloat16)
        label_ref[...] = wide_dot(both_twice(onehot), final, TN)


def small_gradients(heads, labels, mine, came, modulation_weight, pair_norm, relative, gain, pair_weight):
    conds, wide = modulation_weight.shape
    bins = relative.shape[0]
    rows = mine.shape[0]
    steps = 3

    def fixed(shape):
        return pl.BlockSpec(shape, lambda step: (0, 0))

    shapes = [(conds, wide), (conds, conds), (labels, conds), (bins, conds), (1, conds), (heads, conds)]
    return pl.pallas_call(
        functools.partial(small_kernel, heads),
        grid=(steps,),
        in_specs=[
            pl.BlockSpec(memory_space=pltpu.SMEM),
            fixed((rows, PACK)),
            fixed((rows, PACK)),
            pl.BlockSpec((conds, wide // steps), lambda step: (0, step)),
            fixed((LANES, conds)),
            fixed((bins, conds)),
            fixed((1, conds)),
            fixed((conds, 16)),
        ],
        out_specs=tuple(
            [pl.BlockSpec((conds, wide // steps), lambda step: (0, step))]
            + [fixed(s) for s in shapes[1:]]
        ),
        out_shape=tuple(jax.ShapeDtypeStruct(shape, jnp.float32) for shape in shapes),
        scratch_shapes=[
            pltpu.VMEM((rows // 8, conds), jnp.float32),
            pltpu.VMEM((6 * rows // 8, wide // 6), jnp.float32),
            pltpu.VMEM((4, rows // 8, conds), jnp.float32),
        ],
        compiler_params=pltpu.CompilerParams(vmem_limit_bytes=VMEM_BYTES),
        cost_estimate=pl.CostEstimate(
            flops=100000000, bytes_accessed=10000000, transcendentals=0
        ),
        name="small_gradients",
    )(
        scalars(0),
        mine,
        came,
        modulation_weight,
        pair_norm,
        relative,
        gain,
        pair_weight,
    )


def per_device(
    crop_parts,
    res_parts,
    tokens,
    cotangent,
    time_levels,
    cath_ids,
    residue_numbers,
    chain_mask,
    time_weight,
    label_table,
    modulation_weight,
    projection_weight,
    gate_weight,
    output_weight,
    relative_table,
    pair_gain,
    pair_weight,
    feed_gate,
    feed_up,
    feed_down,
):
    crop_count, row_count, model_width = tokens.shape
    crop_length = residue_numbers.shape[1]
    head_count = pair_weight.shape[1]
    head_width = model_width // head_count
    bin_count = relative_table.shape[0]
    label_count = label_table.shape[0]
    token_count = crop_count * row_count
    score_scale = head_width ** (-0.5)
    pairs = head_count // 2
    layout = Layout(row_count, crop_length)
    query_start = lax.axis_index("res") * row_count

    def conditioning(features, onehot):
        return jnp.dot(features, time_weight, preferred_element_type=jnp.float32) + jnp.dot(
            onehot, label_table, preferred_element_type=jnp.float32
        )

    features = time_features(time_levels, time_weight.shape[0]).astype(jnp.bfloat16)
    label_onehot = (cath_ids[:, None] == jnp.arange(label_count, dtype=jnp.int32)[None, :]).astype(
        jnp.bfloat16
    )
    condition = conditioning(features, label_onehot)
    cond_act = jax.nn.silu(condition).astype(jnp.bfloat16)
    modulation = jnp.dot(cond_act, modulation_weight, preferred_element_type=jnp.float32)
    modulation = modulation.reshape(crop_count, 6, 1, model_width)
    shift_a, scale_a = modulation[:, 0], modulation[:, 1]
    mod_rows = pad_to(modulation[:, :, 0], 1, 8, 0.0)

    rotated = lax.dynamic_slice_in_dim(
        jnp.concatenate([jnp.stack([residue_numbers, chain_mask])] * 2, 2), query_start, crop_length, 2
    )
    members, kinds, forward_bins, backward_bins, places, *turned, tables, pair_norm = attention_tables(
        layout,
        score_scale,
        rotated[0],
        rotated[1],
        query_start,
        relative_table,
        pair_gain,
        pair_weight,
    )

    token_values = tokens.astype(jnp.float32)
    normed_a = (
        modulate(token_values, shift_a, scale_a)
        .astype(jnp.bfloat16)
        .reshape(token_count, model_width)
    )
    def project(weight):
        rows = jnp.dot(normed_a, weight, preferred_element_type=jnp.float32)
        return rows.astype(jnp.bfloat16).reshape(crop_count, row_count, -1)

    key_values = project(projection_weight[:, model_width:])
    others = [
        lax.ppermute(
            key_values, "res", [((r + step) % res_parts, r) for r in range(res_parts)]
        )
        for step in range(1, res_parts)
    ]
    if len(layout.pieces) == 2:
        other = others[0] if len(others) == 1 else jnp.concatenate(others, axis=1)
        pieces = [(key_values, 0, pairs), (other, 0, pairs)]
    else:
        pieces = [(jnp.concatenate([key_values] + others, axis=1), 0, pairs)]

    def block_rows(values):
        return pad_to(values, 1, layout.block_rows, 0)

    queries, attended, logs = attention_forward(
        layout,
        score_scale,
        block_rows(normed_a.reshape(tokens.shape)),
        projection_weight,
        pieces,
        members,
        kinds,
        forward_bins,
        tables,
    )
    here = lax.axis_index("res")
    split = res_parts == 2 and crop_parts == 16
    per_crop_results = [
        feed_layer(
            split,
            here,
            attended[crop],
            block_rows(tokens)[crop],
            block_rows(cotangent)[crop],
            block_rows(normed_a.reshape(tokens.shape))[crop],
            mod_rows[crop],
            gate_weight,
            output_weight,
            feed_gate,
            feed_up,
            feed_down,
        )
        for crop in range(crop_count)
    ]
    layer_out, grad_middle, grad_attended, grad_gate_pre, feed_sums = (
        jnp.stack([result[place] for result in per_crop_results]) for place in range(5)
    )
    layer_out, grad_middle = layer_out[:, :row_count], grad_middle[:, :row_count]
    grad_gate_pre = grad_gate_pre[:, :row_count].reshape(token_count, model_width)
    weight_grads = [
        sum(result[place].astype(jnp.float32) for result in per_crop_results).astype(jnp.bfloat16)
        if crop_count > 1
        else per_crop_results[0][place]
        for place in range(5, len(per_crop_results[0]))
    ]

    def backward_of(first_pair, count, grad_now):
        return attention_backward(
            layout,
            score_scale,
            first_pair,
            count,
            queries,
            grad_now,
            attended,
            logs,
            pieces,
            members,
            kinds,
            backward_bins,
            places,
            *turned,
            tables,
        )

    if split:
        arrivals = [swap_res(weight_grads[place]) for place in (0, 2, 4, 6)]
        kept = [weight_grads[place] for place in (1, 3, 5, 7)]
        half = model_width // 2
        inner = feed_gate.shape[1] // 2
        calls = [list(backward_of(0, 1, grad_attended))]
        arrivals, calls[0] = tie(arrivals, calls[0])
        gate_w, up_w, down_w, small_w = zip(kept, arrivals)
        halving = Halving(
            [
                [(gate_w, 0, inner), (small_w, 0, half)],
                [(up_w, 0, inner), (small_w, 1, half)],
                [(down_w, 0, half)],
            ],
            ["xyvu", "yvxu", "vxyu"],
        )
        arrived = []
        for first_pair, count in ((1, 4), (5, 1)):
            arrived.append(swap_res(calls[-1][2][0]))
            sent = halving.stage()
            sent, grad_attended = tie(sent, grad_attended)
            came = halving.send(sent)
            calls.append(list(backward_of(first_pair, count, grad_attended)))
            came, calls[-1], arrived[-1] = tie(came, calls[-1], arrived[-1])
            halving.take(came)
        index = lax.axis_index("crop")
        bf16 = jnp.bfloat16
        share = model_width // 16
        away = swap_res(calls[2][2][0])
        sent = halving.stage()
        sent, calls[2][1] = tie(sent, calls[2][1])
        came = halving.send(sent)
        joined, proj_send, proj_keep = projection_gradient(
            here,
            normed_a,
            [
                (calls[0][0][0], calls[0][1][0], arrived[0]),
                (calls[1][0][0], calls[1][1][0], arrived[1]),
                (calls[2][0][0], calls[2][1][0], away),
            ],
        )
        came, proj_send, proj_keep = tie(came, proj_send, proj_keep)
        proj_came = swap_res(proj_send)
        halving.take(came)
        (sent,) = halving.stage(merge=True)
        sent, proj_came = tie(sent, proj_came)
        came = exchange(sent, MASKS["u"])
        mine, *fan = local_call(
            fan_first_kernel,
            scalars(index % 4),
            [proj_keep, proj_came],
            [((4 * share, PACK), bf16)] * 4,
            "fan_first",
        )
        fan, joined = tie(fan, joined)
        fan_came = [exchange(value, mask + 1) for mask, value in enumerate(fan)]
        extra = jnp.concatenate(
            [
                pad_to(features.astype(jnp.float32), 1, SIDE, 0.0),
                jnp.concatenate(
                    [condition, pad_to(cath_ids.astype(jnp.float32)[:, None], 1, LANES, 0.0)], axis=1
                ),
            ],
            axis=0,
        )
        tokens_grad, pack = finish_layer(
            joined,
            projection_weight,
            grad_gate_pre,
            gate_weight,
            tokens[0],
            grad_middle[0],
            mod_rows[0],
            feed_sums[0],
            jnp.pad(extra, ((4, 2), (0, 0))),
            [call[-1][0] for call in calls],
        )
        tokens_grad = tokens_grad[None]
        came, pack = tie(came, pack)
        packs = [pack] + [exchange(pack, mask + 1) for mask in range(3)]
        finals = halving.stage(last=True, merged=came)
        feed_gate_grad, output_weight_grad, feed_up_grad, gate_weight_grad, feed_down_grad = finals
        packs, finals = tie(packs, finals)
        (packs,) = local_call(join_packs_kernel, scalars(0), packs, [((32, PACK), bf16)], "join_packs")
        far_packs = exchange(packs, MASKS["v"])
        packs, fan_came, far_packs = tie(packs, fan_came, far_packs)
        sent, mine = local_call(
            fan_v_kernel,
            scalars((index // 4) % 2),
            [mine, *fan_came],
            [((2 * share, PACK), bf16), ((2 * share, PACK), bf16)],
            "fan_v",
        )
        packs = jnp.concatenate([packs, far_packs], axis=0)
        sent, packs = tie(sent, packs)
        came = exchange(sent, MASKS["v"])
        far_packs = exchange(packs, MASKS["u"])
        came, far_packs = tie(came, far_packs)
        packs = jnp.concatenate([packs, far_packs], axis=0)
        sent, mine = local_call(
            fan_u_kernel,
            scalars(index // 8),
            [mine, came],
            [((share, PACK), bf16), ((share, PACK), bf16)],
            "fan_u",
        )
        sent, packs = tie(sent, packs)
        came = exchange(sent, MASKS["u"])
        (
            modulation_weight_grad,
            time_weight_grad,
            label_table_grad,
            relative_table_grad,
            pair_gain_grad,
            pair_weight_grad,
        ) = small_gradients(
            head_count,
            label_count,
            packs,
            swap_res(packs),
            modulation_weight,
            pair_norm,
            relative_table,
            pair_gain.reshape(1, -1),
            pad_to(pair_weight, 1, 16, 0.0),
        )
        pair_weight_grad = pair_weight_grad.T
        came, pair_weight_grad = tie(came, pair_weight_grad)
        projection_weight_grad = add_low(mine, came, jnp.float32)
        pair_gain_grad = pair_gain_grad[0]
    else:
        results = backward_of(0, pairs, grad_attended)
        grad_table = results[-1]
        grad_pairs = results[1:-1]
        if len(grad_pairs) == 2:
            total, away = grad_pairs[0].astype(jnp.float32), grad_pairs[1]
        else:
            total = grad_pairs[0][:, :, :row_count].astype(jnp.float32)
            away = grad_pairs[0][:, :, row_count:]
        for step in range(1, res_parts):
            sent = away[:, :, (step - 1) * row_count : step * row_count]
            pairs_to = [(r, (r + step) % res_parts) for r in range(res_parts)]
            total = total + lax.ppermute(sent, "res", pairs_to).astype(jnp.float32)
        total = total.astype(jnp.bfloat16)
        grad_projected = jnp.concatenate(
            [results[0][:, :row_count], total[:, 0], total[:, 1]], axis=-1
        ).reshape(token_count, 3 * model_width)
        grad_normed_a = against_columns(grad_projected, projection_weight) + against_columns(
            grad_gate_pre, gate_weight
        )
        norm_back_a = jax.vjp(modulate, token_values, shift_a, scale_a)[1]
        grad_tokens, grad_shift_a, grad_scale_a = norm_back_a(
            grad_normed_a.reshape(crop_count, row_count, model_width)
        )
        tokens_grad = (grad_middle + grad_tokens).astype(jnp.bfloat16)
        feed_gate_grad, feed_up_grad, feed_down_grad = (
            scatter_crops(share_columns(value, res_parts)) for value in weight_grads[:3]
        )
        output_weight_grad, gate_weight_grad = (
            scatter_crops(share_columns(value, res_parts))
            for value in (weight_grads[3][:, :model_width], weight_grads[3][:, model_width:])
        )
        projection_weight_grad = scatter_crops(
            share_columns(across_rows(normed_a, grad_projected), res_parts)
        )
        grad_table = grad_table[:, :, :2].sum(0).reshape(head_count, LANES)

        grad_modulation = jnp.concatenate([grad_shift_a, grad_scale_a, feed_sums[:, 2:6]], axis=1)
        grad_modulation = grad_modulation.reshape(crop_count, 6 * model_width)
        table_row = grad_table.reshape(1, head_count * LANES)
        first_row = (jnp.arange(crop_count) == 0).astype(jnp.float32)[:, None]
        small_here = jnp.concatenate([grad_modulation, first_row * table_row], axis=1)
        levels_here = jnp.stack([time_levels, cath_ids.astype(jnp.float32)], axis=1)
        levels_here = pad_to(levels_here, 1, LANES, 0.0)
        small_all = gather_crops(
            jnp.concatenate([levels_here, sum_res(small_here, res_parts)], axis=1), crop_parts
        )
        levels_all, small_all = small_all[:, :2], small_all[:, LANES:]
        grad_modulation = small_all[:, : 6 * model_width]
        grad_table = jnp.sum(small_all[:, 6 * model_width :], axis=0).reshape(head_count, LANES)
        grad_table = grad_table[:, :bin_count]
        features_all = time_features(levels_all[:, 0], time_weight.shape[0]).astype(jnp.bfloat16)
        onehot_all = (
            levels_all[:, 1].astype(jnp.int32)[:, None]
            == jnp.arange(label_count, dtype=jnp.int32)[None, :]
        ).astype(jnp.bfloat16)
        condition = conditioning(features_all, onehot_all)
        cond_act = jax.nn.silu(condition).astype(jnp.bfloat16)
        modulation_weight_grad = split_left(cond_act, grad_modulation, 0, 0)
        grad_condition = split_left(modulation_weight, grad_modulation, 1, 1).T * silu_slope(condition)
        time_weight_grad = split_left(features_all, grad_condition, 0, 0)
        label_table_grad = split_left(onehot_all, grad_condition, 0, 0)
        relative_values = relative_table.astype(jnp.float32)
        gain_values = pair_gain.astype(jnp.float32)
        pair_norm = pair_norm[:bin_count]
        pair_weight_grad = split_left(pair_norm, grad_table, 0, 1)
        grad_pair_norm = split_right(grad_table, pair_weight, 0, 1)
        pair_back = jax.vjp(normalize_rows, relative_values, gain_values)[1]
        relative_table_grad, pair_gain_grad = pair_back(grad_pair_norm)
    return (
        layer_out,
        tokens_grad,
        time_weight_grad,
        label_table_grad,
        modulation_weight_grad,
        projection_weight_grad,
        gate_weight_grad,
        output_weight_grad,
        relative_table_grad,
        pair_gain_grad,
        pair_weight_grad,
        feed_gate_grad,
        feed_up_grad,
        feed_down_grad,
    )


def solution(mesh):
    return jax.shard_map(
        functools.partial(per_device, mesh.shape["crop"], mesh.shape["res"]),
        mesh=mesh,
        in_specs=(
            P("crop", "res", None),
            P("crop", "res", None),
            P("crop"),
            P("crop"),
            P("crop", None),
            P("crop", None),
            P(),
            P(),
            P(),
            P(),
            P(),
            P(),
            P(),
            P(),
            P(),
            P(),
            P(),
            P(),
        ),
        out_specs=(
            P("crop", "res", None),
            P("crop", "res", None),
            P(),
            P(),
            P(),
            P("crop", "res"),
            P("crop", "res"),
            P("crop", "res"),
            P(),
            P(),
            P(),
            P("crop", "res"),
            P("crop", "res"),
            P("crop", "res"),
        ),
        check_vma=False,
    )
```

```python
import functools
import itertools
import math

import jax
import jax.numpy as jnp
from jax import lax
from jax.experimental import pallas as pl
from jax.experimental.pallas import tpu as pltpu
from jax.sharding import PartitionSpec as P

LANES = 128
NEAR = 31
VMEM_BYTES = 62 * 1024 * 1024
LOG2E = 1.4426950408889634
NONE, RIGHT, LEFT, APART = 0, 1, 2, 3


def layer_norm(inputs):
    mean_value = jnp.mean(inputs, axis=-1, keepdims=True)
    centred = inputs - mean_value
    spread = jnp.mean(centred * centred, axis=-1, keepdims=True)
    return centred * lax.rsqrt(spread + 1e-06)


def modulate(inputs, shift_row, scale_row):
    return layer_norm(inputs) * (1.0 + scale_row) + shift_row


def normalize_rows(table_rows, gain_row):
    return layer_norm(table_rows) * gain_row


def time_features(time_levels, feature_width):
    half_width = feature_width // 2
    frequency = jnp.exp(-math.log(10000.0) * jnp.arange(half_width, dtype=jnp.float32) / half_width)
    angles = 1000.0 * time_levels[:, None] * frequency[None, :]
    return jnp.concatenate([jnp.sin(angles), jnp.cos(angles)], axis=-1)


def across_rows(former, latter):
    return lax.dot_general(
        former, latter, (((0,), (0,)), ((), ())), preferred_element_type=jnp.float32
    )


def against_columns(former, latter):
    return lax.dot_general(
        former, latter, (((1,), (1,)), ((), ())), preferred_element_type=jnp.float32
    )


def split_parts(values):
    upper = lax.reduce_precision(values, 8, 7)
    return (upper.astype(jnp.bfloat16), (values - upper).astype(jnp.bfloat16))


def split_left(narrow, values, former_dim, latter_dim):
    upper, rest = split_parts(values)
    numbers = (((former_dim,), (latter_dim,)), ((), ()))
    return lax.dot_general(
        narrow, upper, numbers, preferred_element_type=jnp.float32
    ) + lax.dot_general(narrow, rest, numbers, preferred_element_type=jnp.float32)


def split_right(values, narrow, former_dim, latter_dim):
    upper, rest = split_parts(values)
    numbers = (((former_dim,), (latter_dim,)), ((), ()))
    return lax.dot_general(
        upper, narrow, numbers, preferred_element_type=jnp.float32
    ) + lax.dot_general(rest, narrow, numbers, preferred_element_type=jnp.float32)


def sigmoid_slope(inputs):
    gate_value = jax.nn.sigmoid(inputs)
    return gate_value * (1.0 - gate_value)


def silu_slope(inputs):
    gate_value = jax.nn.sigmoid(inputs)
    return gate_value * (1.0 + inputs * (1.0 - gate_value))


class Layout:
    def __init__(self, rows, length):
        self.rows = rows
        self.length = length
        self.query_tiles = -(-rows // LANES)
        self.key_tiles = -(-length // LANES)
        self.padded = self.query_tiles * LANES
        self.wide = self.key_tiles * LANES
        self.last = self.key_tiles - 1
        self.groups = (self.query_tiles + 4) * 4
        assert 2 * self.groups + 3 <= LANES and self.groups <= 64
        assert rows - 1 + NEAR < self.padded and length - NEAR >= self.last * LANES
        assert rows % 8 == 0 and self.last > self.query_tiles
        self.block_rows = rows if rows % 16 == 0 else self.padded
        self.pieces = [rows, length - rows] if rows % 16 == 0 else [length]

    def tile_start(self, tile):
        return self.last * LANES if tile < 0 else tile * LANES


def pad_to(values, axis, size, fill):
    widths = [(0, 0)] * values.ndim
    widths[axis] = (0, size - values.shape[axis])
    return jnp.pad(values, widths, constant_values=fill)


def tables_kernel(
    layout, bin_count, heads, scale, start_ref, pairs_ref, relative_ref, gain_ref, weight_ref, *out_refs
):
    members_ref, kinds_ref, forward_ref, backward_ref, places_ref = out_refs[:5]
    members_turned, kinds_turned, tables_ref, norm_ref, codes = out_refs[5:]
    rows, length, queries, groups = layout.rows, layout.length, layout.query_tiles, layout.groups
    wrap = length - start_ref[0]
    reach = (bin_count - 2) // 2
    zero_bin = LANES - 1
    shape = (LANES, LANES)
    lane = lax.broadcasted_iota(jnp.int32, shape, 1)
    row = lax.broadcasted_iota(jnp.int32, shape, 0)
    last_start = layout.last * LANES

    values = relative_ref[...].astype(jnp.float32)
    centred = values - jnp.mean(values, axis=1, keepdims=True)
    root = lax.rsqrt(jnp.mean(centred * centred, axis=1, keepdims=True) + 1e-06)
    pair_norm = (centred * root * gain_ref[...].astype(jnp.float32)).astype(jnp.bfloat16)
    norm_ref[...] = pair_norm
    bias = lax.dot_general(
        weight_ref[...], pair_norm, (((0,), (1,)), ((), ())), preferred_element_type=jnp.float32
    )
    head_lane = lax.broadcasted_iota(jnp.int32, bias.shape, 1)
    final = jnp.sum(jnp.where(head_lane == bin_count - 1, bias, 0.0), axis=1, keepdims=True)
    table = jnp.where(head_lane < bin_count, (bias - final) * (1.0 / scale), 0.0)

    def columns(number):
        value = jnp.sum(jnp.where(head_lane == number, table, 0.0), axis=1, keepdims=True)
        upper = value.astype(jnp.bfloat16).astype(jnp.float32)
        return jnp.where(
            head_lane < groups, upper, jnp.where(head_lane < 2 * groups, value - upper, 0.0)
        )

    right_columns, left_columns = columns(bin_count - 2), columns(0)
    for head in range(heads):
        line = 8 * (head % 2)
        for place, rows_of in enumerate((table, right_columns, left_columns)):
            tables_ref[head // 2, line + place : line + place + 1] = rows_of[head : head + 1]

    tiles = pairs_ref.shape[1]
    marks = pairs_ref[1].astype(jnp.float32)
    place = lax.broadcasted_iota(jnp.int32, marks.shape, 0) * LANES + lax.broadcasted_iota(
        jnp.int32, marks.shape, 1
    )
    before = jnp.sum(jnp.where(place < wrap, marks, 0.0), keepdims=True)
    every = jnp.sum(marks, keepdims=True)
    triangle = jnp.where(row <= lane, 1.0, 0.0).astype(jnp.bfloat16)
    running = jnp.dot(marks.astype(jnp.bfloat16), triangle, preferred_element_type=jnp.float32)
    numbers, chains = [], []
    carry = jnp.zeros((1, 1), jnp.float32)
    for tile in range(layout.key_tiles):
        count = running[tile : tile + 1] + carry
        carry = carry + running[tile : tile + 1, LANES - 1 :]
        count = count + jnp.where(place[tile : tile + 1] < wrap, every - before, -before)
        chains.append(jnp.broadcast_to(count.astype(jnp.int32), shape))
        numbers.append(jnp.broadcast_to(pairs_ref[0, tile : tile + 1], shape))
    number_rows = [value.T for value in numbers]
    chain_rows = [value.T for value in chains]

    def bins_of(key_number, key_chain, query_number, query_chain):
        offset = jnp.clip(key_number - query_number, -reach, reach) + reach
        return jnp.where(key_chain == query_chain, offset, bin_count - 1)

    def touches(query, tile):
        begin = -LANES if tile < 0 else tile * LANES
        return (begin <= query + NEAR) & (query - NEAR <= begin + LANES - 1)

    for tile in range(layout.key_tiles):
        size = min(LANES, length - tile * LANES)
        key = tile * LANES + row
        if tile == layout.last:
            other = jnp.full(shape, queries + 3, jnp.int32)
        elif tile == queries - 1:
            other = jnp.full(shape, queries, jnp.int32)
        else:
            other = jnp.where(key < wrap, queries + 1, queries + 2)
        group = jnp.where(key < rows, tile, other)
        slot = group * 4 + chain_rows[tile] - 1
        hit = (lane == slot) | (lane == slot + groups)
        tail = (lane >= 2 * groups) & (lane < 2 * groups + 3)
        values = jnp.where(hit, 1.0, jnp.where(tail, -1.0, 0.0)).astype(jnp.bfloat16)
        members_ref[tile * LANES : tile * LANES + size] = values[:size]
        turned = jnp.where(hit & (lane < groups), 1.0, 0.0).T
        members_turned[:, tile * LANES : tile * LANES + size] = turned[:64, :size].astype(jnp.bfloat16)

    local = jnp.where(lane >= groups, lane - groups, lane)
    lane_group = local >> 2
    lane_chain = (local & 3) + 1
    lane_begin = jnp.where(
        lane_group < queries,
        lane_group * LANES,
        jnp.where(lane_group == queries, (queries - 1) * LANES, -LANES),
    )
    has_band = (lane_group <= queries) | (lane_group == queries + 3)
    other_right = jnp.where(
        lane_group == queries,
        rows,
        jnp.where(
            lane_group == queries + 3,
            last_start,
            jnp.where(lane_group == queries + 1, 0, 2 * length),
        ),
    )
    right_limit = jnp.where(lane_group > queries, jnp.where(lane_group == queries + 3, wrap, length), wrap)
    for tile in range(queries):
        size = min(LANES, layout.block_rows - tile * LANES)
        query = tile * LANES + row
        near = (lane_begin <= query + NEAR) & (query - NEAR <= lane_begin + LANES - 1) & has_band
        right = jnp.where(lane_group < queries, lane_group - tile, right_limit - other_right) > 0
        same = chain_rows[tile] == lane_chain
        kinds = jnp.where(same, jnp.where(near, NONE, jnp.where(right, RIGHT, LEFT)), APART)
        kinds = jnp.where((lane < 2 * groups) & (query < rows), kinds, NONE)
        kinds_ref[tile * LANES : tile * LANES + size] = kinds[:size]
        kinds_turned[:, tile * LANES : (tile + 1) * LANES] = jnp.where(lane < groups, kinds, NONE).T[:64]
        for step in range(3):
            near_tile = tile + step - 1
            index = layout.last if near_tile < 0 else near_tile
            if near_tile < queries:
                inside = touches(query, near_tile) & (query < rows)
                inside &= lane < length - index * LANES
                found = bins_of(
                    numbers[index], chains[index], number_rows[tile], chain_rows[tile]
                )
                found = jnp.where(inside, found, zero_bin)
            else:
                found = jnp.full(shape, zero_bin, jnp.int32)
            forward_ref[
                tile * LANES : (tile + 1) * LANES, step * LANES : (step + 1) * LANES
            ] = found

    codes[...] = jnp.full(codes.shape, -1, jnp.int32)
    for tile in range(queries):
        size = min(LANES, rows - tile * LANES)
        code = number_rows[tile] * 8 + chain_rows[tile]
        codes[(tile + 1) * LANES : (tile + 1) * LANES + size] = code[:size]

    for index, tile in enumerate(list(range(queries)) + [-1]):
        source = layout.last if tile < 0 else tile
        key_row = (row - (length - last_start)) if tile < 0 else tile * LANES + row
        present = row < length - source * LANES
        for step in range(3):
            near_tile = tile + step - 1
            if 0 <= near_tile < queries:
                near_query = near_tile * LANES + lane
                inside = touches(near_query, tile) & (near_query < rows) & present
                found = bins_of(
                    number_rows[source], chain_rows[source], numbers[near_tile], chains[near_tile]
                )
                found = jnp.where(inside, found, zero_bin)
            else:
                found = jnp.full(shape, zero_bin, jnp.int32)
            backward_ref[
                index * LANES : (index + 1) * LANES, step * LANES : (step + 1) * LANES
            ] = found
        target = (number_rows[source] + reach - lane) * 8 + chain_rows[source]
        target = jnp.where(present & (lane > 0) & (lane < 2 * reach), target, -9)
        offset = (LANES - (length - last_start)) if tile < 0 else (tile + 1) * LANES
        far = 4 * LANES
        shift = jnp.full(shape, far, jnp.int32)
        for distance in range(-NEAR, NEAR + 1):
            other = codes[offset - distance : offset - distance + LANES]
            shift = jnp.where(other == target, distance, shift)
        if tile < 0:
            base = jnp.zeros(shape, jnp.int32)
        else:
            base = jnp.where(row < LANES // 2, tile - 1, tile) * LANES
        places_ref[index * LANES : (index + 1) * LANES] = jnp.where(
            shift == far, far - 1, key_row - shift - base
        )


def attention_tables(layout, scale, numbers, marks, query_start, relative_table, pair_gain, pair_weight):
    crops = numbers.shape[0]
    bin_count, width = relative_table.shape
    heads = pair_weight.shape[1]
    pairs = jnp.stack([numbers, marks], axis=1)
    pairs = pad_to(pairs, 2, layout.wide, 0).reshape(crops, 2, layout.key_tiles, LANES)
    spots = (layout.query_tiles + 1) * LANES
    shapes = [
        ((layout.length, LANES), jnp.bfloat16),
        ((layout.block_rows, LANES), jnp.int32),
        ((layout.padded, 3 * LANES), jnp.int32),
        ((spots, 3 * LANES), jnp.int32),
        ((spots, LANES), jnp.int32),
        ((64, layout.length), jnp.bfloat16),
        ((64, layout.padded), jnp.int32),
    ]
    shared = [((heads // 2, 16, LANES), jnp.float32), ((LANES, width), jnp.bfloat16)]

    def whole(shape):
        return pl.BlockSpec(shape, lambda crop: (0,) * len(shape))

    return pl.pallas_call(
        functools.partial(tables_kernel, layout, bin_count, heads, scale),
        grid=(crops,),
        in_specs=[
            pl.BlockSpec(memory_space=pltpu.SMEM),
            pl.BlockSpec((None, 2, layout.key_tiles, LANES), lambda crop: (crop, 0, 0, 0)),
            whole((LANES, width)),
            whole((1, width)),
            whole((width, 16)),
        ],
        out_specs=tuple(
            [pl.BlockSpec((None, *shape), lambda crop: (crop, 0, 0)) for shape, _ in shapes]
            + [whole(shape) for shape, _ in shared]
        ),
        out_shape=tuple(
            [jax.ShapeDtypeStruct((crops, *shape), kind) for shape, kind in shapes]
            + [jax.ShapeDtypeStruct(shape, kind) for shape, kind in shared]
        ),
        scratch_shapes=[pltpu.VMEM((layout.padded + 2 * LANES, LANES), jnp.int32)],
        compiler_params=pltpu.CompilerParams(vmem_limit_bytes=VMEM_BYTES),
        cost_estimate=pl.CostEstimate(
            flops=40000000 * crops, bytes_accessed=4000000 * crops, transcendentals=0
        ),
        name="pair_tables",
    )(
        jnp.reshape(query_start, (1,)).astype(jnp.int32),
        pairs,
        pad_to(relative_table, 0, LANES, 0.0),
        pair_gain.reshape(1, -1),
        pad_to(pair_weight, 1, 16, 0.0),
    )


NT = (((1,), (1,)), ((), ()))
TN = (((0,), (0,)), ((), ()))


def wide_dot(former, latter, numbers=(((1,), (0,)), ((), ()))):
    return lax.dot_general(former, latter, numbers, preferred_element_type=jnp.float32)


def look_up(table_row, bins):
    table = jnp.broadcast_to(table_row, bins.shape)
    return jnp.take_along_axis(table, bins, axis=1, mode="promise_in_bounds")


def half_of(values, lane, side):
    return jnp.where((lane >= 64) == (side == 1), values, jnp.zeros_like(values))


def row_blocks(total, size):
    return [(start, min(start + size, total)) for start in range(0, total, size)]


def group_columns(kinds, tables, side):
    right = tables[8 * side + 1 : 8 * side + 2]
    left = tables[8 * side + 2 : 8 * side + 3]
    return jnp.where(kinds == RIGHT, right, jnp.where(kinds == LEFT, left, 0.0))


def forward_kernel(layout, scale, *refs):
    count = len(layout.pieces)
    normed_ref, weight_ref = refs[:2]
    key_refs = refs[2 : 2 + count]
    value_refs = refs[2 + count : 2 + 2 * count]
    members_ref, kinds_ref, bins_ref, tables_ref, query_ref, out_ref, log_ref = refs[
        2 + 2 * count : -1
    ]
    all_scores = refs[-1]
    pair = pl.program_id(1)
    rows, length = layout.block_rows, layout.length
    turn = 0
    factor = scale * LOG2E
    lane = lax.broadcasted_iota(jnp.int32, (1, LANES), 1)
    query = wide_dot(normed_ref[...], weight_ref[...]).astype(jnp.bfloat16)
    query_ref[...] = query
    keys = jnp.concatenate([ref[...] for ref in key_refs], axis=0)
    values = jnp.concatenate([ref[...] for ref in value_refs], axis=0)
    members = members_ref[...]
    kinds = kinds_ref[...]
    tables = tables_ref[...]
    ones = jnp.ones((length, LANES), jnp.bfloat16)

    @pl.when(pair == 0)
    def _():
        log_ref[...] = jnp.zeros_like(log_ref)

    for side in range(2):
        key_columns = jnp.concatenate([half_of(keys, lane, side), members], axis=1)
        value_columns = jnp.concatenate([half_of(values, lane, side), ones], axis=1)
        extra = group_columns(kinds, tables, side).astype(jnp.bfloat16)
        query_columns = jnp.concatenate([query, extra], axis=1)
        table_row = tables[8 * side : 8 * side + 1]
        for start, stop in row_blocks(rows, 256):
            size = stop - start
            scores = all_scores.at[turn % 2]
            turn += 1
            scores[0:size, 0:length] = wide_dot(query_columns[start:stop], key_columns, NT)
            for tile in range(start // LANES, -(-stop // LANES)):
                first, final = tile * LANES, min(tile * LANES + LANES, rows)
                for slot in range(3):
                    other = tile + slot - 1
                    if other >= layout.query_tiles:
                        continue
                    low, high = first, final
                    if slot == 0:
                        high = min(first + 32, final)
                    if slot == 2:
                        low = first + LANES - 32
                    if low >= high:
                        continue
                    place = layout.tile_start(other)
                    width = min(LANES, length - place)
                    bins = bins_ref[low:high, slot * LANES : (slot + 1) * LANES]
                    bias = look_up(table_row, bins)[:, :width]
                    scores[low - start : high - start, place : place + width] += bias
            block = scores[0:size, 0:length]
            top = jnp.max(block, axis=1, keepdims=True)
            weights = jnp.exp2((block - top) * factor).astype(jnp.bfloat16)
            sums = wide_dot(weights, value_columns)
            total = sums[:, LANES:]
            result = sums[:, :LANES] / total
            if side == 0:
                out_ref[start:stop] = result
            else:
                out_ref[start:stop] += result
            log_total = top + jnp.log(total) * (1.0 / scale)
            log_ref[start:stop] = jnp.where(
                lane == 2 * pair + side, log_total, log_ref[start:stop]
            )


def backward_kernel(layout, scale, first_pair, *refs):
    count = len(layout.pieces)
    query_ref, grad_ref, out_ref, log_ref = refs[:4]
    key_refs = refs[4 : 4 + count]
    value_refs = refs[4 + count : 4 + 2 * count]
    rest = refs[4 + 2 * count :]
    members_ref, kinds_ref, bins_ref, places_ref, tables_ref = rest[:5]
    members_turned_ref, kinds_turned_ref = rest[5:7]
    grad_query_ref = rest[7]
    grad_pair_refs = rest[8 : 8 + count]
    grad_table_ref = rest[8 + count]
    query_wide, grad_wide, query_turned, grad_turned = rest[9 + count : 13 + count]
    band_bias, slopes_low, probs_low = rest[13 + count :]
    pair = pl.program_id(1) + first_pair
    rows, length, padded = layout.block_rows, layout.length, layout.padded
    factor = scale * LOG2E
    lane = lax.broadcasted_iota(jnp.int32, (1, LANES), 1)
    keys = jnp.concatenate([ref[...] for ref in key_refs], axis=0)
    values = jnp.concatenate([ref[...] for ref in value_refs], axis=0)
    members = members_ref[...]
    kinds = kinds_ref[...]
    tables = tables_ref[...]
    query = query_ref[...]
    grad = grad_ref[...]
    grad_full = grad.astype(jnp.float32)
    product = grad_full * out_ref[...]
    log_all = log_ref[...]
    tail = 2 * layout.groups
    ones = jnp.broadcast_to(jnp.where(lane < 3, 1.0, 0.0), (length, LANES)).astype(jnp.bfloat16)

    def three_parts(values):
        upper = values.astype(jnp.bfloat16).astype(jnp.float32)
        values = values - upper
        middle = values.astype(jnp.bfloat16).astype(jnp.float32)
        return upper, middle, values - middle

    def in_lanes(parts, first):
        return jnp.where(
            lane == first,
            parts[0],
            jnp.where(lane == first + 1, parts[1], jnp.where(lane == first + 2, parts[2], 0.0)),
        )

    @pl.when(pl.program_id(1) == 0)
    def _():
        band_bias[...] = jnp.zeros_like(band_bias)

    if padded > rows:
        for ref in (query_wide, grad_wide):
            for side in range(2):
                ref[side, rows:padded] = jnp.zeros((padded - rows, ref.shape[2]), jnp.bfloat16)
        for ref in (query_turned, grad_turned):
            ref[:, rows:padded] = jnp.zeros((LANES, padded - rows), jnp.bfloat16)
    query_turned[:, 0:rows] = query.T
    grad_turned[:, 0:rows] = grad.T
    for side in range(2):
        log_total = jnp.sum(
            jnp.where(lane == 2 * pair + side, log_all, 0.0), axis=1, keepdims=True
        )
        extra = group_columns(kinds, tables, side) + in_lanes(three_parts(log_total), tail)
        query_wide[side, 0:rows, 0:LANES] = query
        query_wide[side, 0:rows, LANES:] = extra.astype(jnp.bfloat16)
        delta = jnp.sum(half_of(product, lane, side), axis=1, keepdims=True)
        grad_wide[side, 0:rows, 0:LANES] = grad
        grad_wide[side, 0:rows, LANES:] = in_lanes(three_parts(-delta), 0).astype(jnp.bfloat16)

    key_columns = [
        jnp.concatenate([half_of(keys, lane, side), members], axis=1) for side in range(2)
    ]
    value_columns = [
        jnp.concatenate([half_of(values, lane, side), ones], axis=1) for side in range(2)
    ]
    inner_sums = [jnp.zeros((1, LANES), jnp.float32) for _ in range(2)]
    low_sums = [jnp.zeros((1, LANES), jnp.float32) for _ in range(2)]
    high_sums = [jnp.zeros((1, LANES), jnp.float32) for _ in range(2)]
    reach_tiles = list(range(layout.query_tiles)) + [-1]

    def put(which, start, stop, result):
        begin = 0
        for ref, size in zip(grad_pair_refs, layout.pieces):
            low, high = max(start, begin), min(stop, begin + size)
            if low < high:
                ref[which, low - begin : high - begin] = result[low - start : high - start]
            begin += size

    for start, stop in row_blocks(length, 384):
        size = stop - start
        for side in range(2):
            table_row = tables[8 * side : 8 * side + 1]
            near = []
            for index, tile in enumerate(reach_tiles):
                place = layout.tile_start(tile)
                if start <= place < stop:
                    near.append((index, tile, place, min(place + LANES, length)))
            for index, tile, place, final in near:
                for slot in range(3):
                    other = tile + slot - 1
                    if not 0 <= other < layout.query_tiles:
                        continue
                    bins = bins_ref[
                        index * LANES : index * LANES + final - place,
                        slot * LANES : (slot + 1) * LANES,
                    ]
                    band_bias[place:final, other * LANES : (other + 1) * LANES] = look_up(
                        table_row, bins
                    )
            scores = wide_dot(key_columns[side][start:stop], query_wide[side], NT)
            if near:
                scores = scores + band_bias[start:stop]
            probs = jnp.exp2(scores * factor).astype(jnp.bfloat16)
            probs_low[side, start:stop] = probs
            grad_probs = wide_dot(value_columns[side][start:stop], grad_wide[side], NT)
            slopes_low[side, start:stop] = (probs.astype(jnp.float32) * grad_probs).astype(
                jnp.bfloat16
            )
            for index, tile, place, final in near:
                for slot in range(3):
                    other = tile + slot - 1
                    if not 0 <= other < layout.query_tiles:
                        continue
                    bins = bins_ref[
                        index * LANES : index * LANES + final - place,
                        slot * LANES : (slot + 1) * LANES,
                    ]
                    cut = slopes_low[side, place:final, other * LANES : (other + 1) * LANES].astype(
                        jnp.float32
                    )
                    low_sums[side] += jnp.sum(
                        jnp.where(bins == 0, cut, 0.0), axis=0, keepdims=True
                    )
                    high_sums[side] += jnp.sum(
                        jnp.where(bins == 2 * (NEAR + 1), cut, 0.0), axis=0, keepdims=True
                    )
                for half in range(2):
                    base = 0 if tile < 0 else tile - 1 + half
                    for step in range(2):
                        other = base + step
                        if not 0 <= other < layout.query_tiles or (tile < 0 and step):
                            continue
                        begin, end = half * 64, half * 64 + 64
                        if tile >= 0 and other == tile - 1:
                            end = begin + 32
                        if tile >= 0 and other == tile + 1:
                            begin = end - 32
                        end = min(end, final - place)
                        if begin >= end:
                            continue
                        where = places_ref[index * LANES + begin : index * LANES + end]
                        spot = where & (LANES - 1)
                        cut = slopes_low[
                            side, place + begin : place + end, other * LANES : (other + 1) * LANES
                        ].astype(jnp.float32)
                        picked = jnp.take_along_axis(cut, spot, axis=1, mode="promise_in_bounds")
                        picked = jnp.where((where >> 7) == step, picked, 0.0)
                        inner_sums[side] += jnp.sum(picked, axis=0, keepdims=True)

    keys_turned = keys.T
    grad_keys, grad_values, grad_queries = [], [], []
    kinds_turned = kinds_turned_ref[...]
    for side in range(2):
        cut = slice(64 * side, 64 * side + 64)
        grad_values.append(wide_dot(grad_turned[cut], probs_low[side], NT))
        grad_keys.append(wide_dot(query_turned[cut], slopes_low[side], NT))
        left = jnp.concatenate([keys_turned[cut], members_turned_ref[...]], axis=0)
        both = wide_dot(left, slopes_low[side])
        grad_queries.append(both[:64])
        sums = both[64:]

        def total(kind):
            return jnp.sum(jnp.where(kinds_turned == kind, sums, 0.0))

        right = total(RIGHT) + jnp.sum(high_sums[side])
        left = total(LEFT) + jnp.sum(low_sums[side])
        apart = total(APART)
        grad_table_ref[side : side + 1] = jnp.where(
            lane == 0,
            left,
            jnp.where(
                lane == 2 * (NEAR + 1),
                right,
                jnp.where(lane == 2 * (NEAR + 1) + 1, apart, inner_sums[side]),
            ),
        )
    put(0, 0, length, (jnp.concatenate(grad_keys, axis=0) * scale).T.astype(jnp.bfloat16))
    put(1, 0, length, jnp.concatenate(grad_values, axis=0).T.astype(jnp.bfloat16))
    turned = jnp.concatenate(grad_queries, axis=0) * scale
    grad_query_ref[...] = turned.T[0:rows].astype(jnp.bfloat16)


def tile_columns(rows, offset=0):
    return pl.BlockSpec((None, rows, LANES), lambda crop, pair: (crop, 0, pair + offset))


def per_crop(rows, width):
    return pl.BlockSpec((None, rows, width), lambda crop, pair: (crop, 0, 0))


def kernel_params():
    return pltpu.CompilerParams(
        vmem_limit_bytes=VMEM_BYTES, dimension_semantics=("arbitrary", "arbitrary")
    )


def attention_forward(layout, scale, normed, weight, key_values, members, kinds, bins, tables):
    crops, rows, width = normed.shape
    pairs = tables.shape[0]
    specs = [per_crop(rows, width), pl.BlockSpec((width, LANES), lambda crop, pair: (0, pair))]
    operands = [normed, weight]
    for place in (1, 2):
        for piece in key_values:
            specs.append(tile_columns(piece[0].shape[1], piece[place]))
            operands.append(piece[0])
    specs += [
        per_crop(layout.length, LANES),
        per_crop(rows, LANES),
        per_crop(layout.padded, 3 * LANES),
        pl.BlockSpec((None, 16, LANES), lambda crop, pair: (pair, 0, 0)),
    ]
    flops = 2 * crops * pairs * 2 * rows * layout.length * 256 * 2
    return pl.pallas_call(
        functools.partial(forward_kernel, layout, scale),
        grid=(crops, pairs),
        in_specs=specs,
        out_specs=(tile_columns(rows), tile_columns(rows), per_crop(rows, LANES)),
        out_shape=(
            jax.ShapeDtypeStruct((crops, rows, pairs * LANES), jnp.bfloat16),
            jax.ShapeDtypeStruct((crops, rows, pairs * LANES), jnp.float32),
            jax.ShapeDtypeStruct((crops, rows, LANES), jnp.float32),
        ),
        scratch_shapes=[pltpu.VMEM((2, 256, layout.wide), jnp.float32)],
        compiler_params=kernel_params(),
        cost_estimate=pl.CostEstimate(
            flops=flops,
            bytes_accessed=12 * crops * rows * pairs * LANES,
            transcendentals=crops * pairs * 2 * rows * layout.length,
        ),
        name="attention_forward",
    )(*operands, members, kinds, bins, tables)


def attention_backward(
    layout,
    scale,
    first_pair,
    pairs,
    projected,
    grad_out,
    attended,
    logs,
    key_values,
    members,
    kinds,
    bins,
    places,
    members_turned,
    kinds_turned,
    tables,
):
    crops, rows, _ = projected.shape
    specs = [tile_columns(rows, first_pair)] * 3 + [per_crop(rows, LANES)]
    operands = [projected, grad_out, attended, logs]
    for place in (1, 2):
        for piece in key_values:
            specs.append(tile_columns(piece[0].shape[1], piece[place] + first_pair))
            operands.append(piece[0])
    specs += [
        per_crop(layout.length, LANES),
        per_crop(rows, LANES),
        per_crop(bins.shape[1], 3 * LANES),
        per_crop(places.shape[1], LANES),
        pl.BlockSpec((None, 16, LANES), lambda crop, pair: (pair + first_pair, 0, 0)),
        per_crop(64, layout.length),
        per_crop(64, layout.padded),
    ]
    out_specs = [tile_columns(rows)]
    out_shapes = [jax.ShapeDtypeStruct((crops, rows, pairs * LANES), jnp.bfloat16)]
    for piece in key_values:
        size = piece[0].shape[1]
        out_specs.append(
            pl.BlockSpec((None, 2, size, LANES), lambda crop, pair: (crop, 0, 0, pair))
        )
        out_shapes.append(jax.ShapeDtypeStruct((crops, 2, size, pairs * LANES), jnp.bfloat16))
    out_specs.append(pl.BlockSpec((None, None, 8, LANES), lambda crop, pair: (crop, pair, 0, 0)))
    out_shapes.append(jax.ShapeDtypeStruct((crops, pairs, 8, LANES), jnp.float32))
    padded = layout.padded
    return pl.pallas_call(
        functools.partial(backward_kernel, layout, scale, first_pair),
        grid=(crops, pairs),
        in_specs=specs,
        out_specs=tuple(out_specs),
        out_shape=tuple(out_shapes),
        scratch_shapes=[
            pltpu.VMEM((2, padded, 2 * LANES), jnp.bfloat16),
            pltpu.VMEM((2, padded, 2 * LANES), jnp.bfloat16),
            pltpu.VMEM((LANES, padded), jnp.bfloat16),
            pltpu.VMEM((LANES, padded), jnp.bfloat16),
            pltpu.VMEM((layout.length, padded), jnp.float32),
            pltpu.VMEM((2, layout.length, padded), jnp.bfloat16),
            pltpu.VMEM((2, layout.length, padded), jnp.bfloat16),
        ],
        compiler_params=kernel_params(),
        cost_estimate=pl.CostEstimate(
            flops=2 * crops * pairs * 2 * rows * layout.length * 256 * 5,
            bytes_accessed=20 * crops * rows * pairs * LANES,
            transcendentals=crops * pairs * 2 * rows * layout.length,
        ),
        name="attention_backward",
    )(*operands, members, kinds, bins, places, tables, members_turned, kinds_turned)


def sigmoid(values):
    return 0.5 * jnp.tanh(0.5 * values) + 0.5


def each_strip(rows, body, size=16):
    count = rows // size
    group = max(number for number in range(1, 9) if count % number == 0)

    @pl.loop(0, count // group)
    def _(index):
        for part in range(group):
            body(pl.ds(pl.multiple_of((index * group + part) * size, size), size))


def fold_rows(values):
    return jnp.sum(values.reshape(values.shape[0] // 8, 8, values.shape[1]), axis=0)


def feed_kernel(split, chunks, here_ref, *refs):
    (attended_ref, tokens_ref, upstream_ref, normed_a_ref, mod_ref, gate_weight_ref, output_ref) = refs[:7]
    gate_ref, up_ref, down_ref = refs[7:10]
    layer_ref, grad_middle_ref, grad_att_ref, grad_pre_ref, sums_ref = refs[10:15]
    grads = refs[15:-12]
    gated, grad_ff, normed, branch, middle, total, grad_normed, hidden, both, grad_branch = refs[-12:-2]
    gate_pre, turned = refs[-2:]
    step = pl.program_id(0)
    here = here_ref[0]
    rows, width = tokens_ref.shape
    size = gate_ref.shape[1]
    strip = 112 if rows % 112 == 0 else 64
    strips = rows // strip
    shift_f, scale_f = mod_ref[3:4], mod_ref[4:5]
    open_a, open_f = sigmoid(mod_ref[2:3]), sigmoid(mod_ref[5:6])

    def strip_of(index):
        return pl.ds(pl.multiple_of(index * strip, strip), strip)

    def norm_of(values):
        mean_value = jnp.mean(values, axis=1, keepdims=True)
        centred = values - mean_value
        spread = jnp.mean(centred * centred, axis=1, keepdims=True)
        root = lax.rsqrt(spread + 1e-06)
        return centred * root, root

    @pl.when(step == 0)
    def _():
        gate_pre[...] = wide_dot(normed_a_ref[...], gate_weight_ref[...])

        @pl.loop(0, strips)
        def _(index):
            cut = strip_of(index)
            gated[cut] = (attended_ref[cut] * sigmoid(gate_pre[cut])).astype(jnp.bfloat16)
            grad_ff[cut] = (upstream_ref[cut].astype(jnp.float32) * open_f).astype(jnp.bfloat16)

        branch[...] = wide_dot(gated[...], output_ref[...])

        @pl.loop(0, strips)
        def _(index):
            cut = strip_of(index)
            values = tokens_ref[cut].astype(jnp.float32) + open_a * branch[cut]
            middle[cut] = values
            normed[cut] = (norm_of(values)[0] * (1.0 + scale_f) + shift_f).astype(jnp.bfloat16)
            total[cut] = jnp.zeros((strip, width), jnp.float32)
            grad_normed[cut] = jnp.zeros((strip, width), jnp.float32)

        turned[...] = normed[...].T

    block = rows if rows <= 384 else rows // 2
    for start in range(0, rows, block):
        cut = slice(start, start + block)
        before = wide_dot(normed[cut], gate_ref[...])
        switch = sigmoid(before)
        silu_full = before * switch
        silu = silu_full.astype(jnp.bfloat16)
        slope = (switch + silu_full * (1.0 - switch)).astype(jnp.bfloat16)
        lifted = wide_dot(normed[cut], up_ref[...])
        hidden[cut] = (silu.astype(jnp.float32) * lifted).astype(jnp.bfloat16)
        sloped = (slope.astype(jnp.float32) * lifted).astype(jnp.bfloat16)
        grad_hidden = wide_dot(grad_ff[cut], down_ref[...], NT)
        both[cut, :size] = (grad_hidden * sloped.astype(jnp.float32)).astype(jnp.bfloat16)
        both[cut, size:] = (grad_hidden * silu.astype(jnp.float32)).astype(jnp.bfloat16)
        total[cut] += wide_dot(hidden[cut], down_ref[...])
        grad_normed[cut] += wide_dot(both[cut, :size], gate_ref[...], NT)
        grad_normed[cut] += wide_dot(both[cut, size:], up_ref[...], NT)

    def weights_back(gate_out, up_out):
        gate_out[...] = wide_dot(turned[...], both[:, :size]).astype(jnp.bfloat16)
        up_out[...] = wide_dot(turned[...], both[:, size:]).astype(jnp.bfloat16)

    if split:
        gate_send, gate_keep, up_send, up_keep, down_send, down_keep, small_send, small_keep = grads
        half = width // 2
        away = pl.ds(pl.multiple_of((1 - here) * half, LANES), half)
        home = pl.ds(pl.multiple_of(here * half, LANES), half)
        down_send[...] = wide_dot(hidden[...], grad_ff[:, away], TN).astype(jnp.bfloat16)
        down_keep[...] = wide_dot(hidden[...], grad_ff[:, home], TN).astype(jnp.bfloat16)

        @pl.when(step < chunks // 2)
        def _():
            weights_back(gate_send, up_send)

        @pl.when(step >= chunks // 2)
        def _():
            weights_back(gate_keep, up_keep)
    else:
        gate_all, up_all, down_all, small_all = grads
        weights_back(gate_all, up_all)
        down_all[...] = wide_dot(hidden[...], grad_ff[...], TN).astype(jnp.bfloat16)

    @pl.when(step == chunks - 1)
    def _():
        def finish(index, sums):
            gate_f_sum, shift_sum, scale_sum, gate_a_sum = sums
            cut = strip_of(index)
            values = middle[cut]
            fed = total[cut]
            upstream = upstream_ref[cut].astype(jnp.float32)
            layer_ref[cut] = (values + open_f * fed).astype(jnp.bfloat16)
            normal, root = norm_of(values)
            grad = grad_normed[cut]
            scaled = grad * (1.0 + scale_f)
            grad_middle = upstream + root * (
                scaled
                - jnp.mean(scaled, axis=1, keepdims=True)
                - normal * jnp.mean(scaled * normal, axis=1, keepdims=True)
            )
            grad_middle_ref[cut] = grad_middle
            grad_branch[cut] = (grad_middle * open_a).astype(jnp.bfloat16)
            return (
                gate_f_sum + fold_rows(upstream * fed),
                shift_sum + fold_rows(grad),
                scale_sum + fold_rows(grad * normal),
                gate_a_sum + fold_rows(grad_middle * branch[cut]),
            )

        zero = jnp.zeros((8, width), jnp.float32)
        sums = lax.fori_loop(0, strips, finish, (zero, zero, zero, zero))
        gate_f_sum, shift_sum, scale_sum, gate_a_sum = [
            jnp.sum(value, axis=0, keepdims=True) for value in sums
        ]
        none = jnp.zeros((1, width), jnp.float32)
        sums_ref[...] = jnp.concatenate(
            [
                none,
                none,
                gate_a_sum * open_a * (1.0 - open_a),
                shift_sum,
                scale_sum,
                gate_f_sum * open_f * (1.0 - open_f),
                none,
                none,
            ],
            axis=0,
        )
        total[...] = wide_dot(grad_branch[...], output_ref[...], NT)

        @pl.loop(0, strips)
        def _(index):
            cut = strip_of(index)
            grad_gated = total[cut]
            opened = sigmoid(gate_pre[cut])
            grad_att_ref[cut] = (grad_gated * opened).astype(jnp.bfloat16)
            grad_pre_ref[cut] = (
                grad_gated * attended_ref[cut] * (opened * (1.0 - opened))
            ).astype(jnp.bfloat16)

        if split:
            for side, ref in ((away, small_send), (home, small_keep)):
                ref[:, :half] = wide_dot(gated[...], grad_branch[:, side], TN).astype(jnp.bfloat16)
                ref[:, half:] = wide_dot(normed_a_ref[...], grad_pre_ref[:, side], TN).astype(
                    jnp.bfloat16
                )
        else:
            small_all[:, :width] = wide_dot(gated[...], grad_branch[...], TN).astype(jnp.bfloat16)
            small_all[:, width:] = wide_dot(normed_a_ref[...], grad_pre_ref[...], TN).astype(
                jnp.bfloat16
            )


def feed_layer(
    split, here, attended, tokens, upstream, normed_a, mod_rows, gate_weight, output_weight, feed_gate, feed_up, feed_down
):
    rows, width = tokens.shape
    inner = feed_gate.shape[1]
    size = 512
    chunks = inner // size
    half = chunks // 2

    def turn(step, here_ref):
        return (step + half * (1 - here_ref[0])) % chunks if split else step

    def fixed(shape):
        return pl.BlockSpec(shape, lambda step, here_ref: (0, 0), pipeline_mode=pl.Buffered(1))

    def columns(step, here_ref):
        return (0, turn(step, here_ref))

    def strips(step, here_ref):
        return (turn(step, here_ref), 0)

    whole = (rows, width)
    in_specs = [fixed(whole)] * 4 + [
        fixed((8, width)),
        fixed((width, width)),
        fixed((width, width)),
        pl.BlockSpec((width, size), columns),
        pl.BlockSpec((width, size), columns),
        pl.BlockSpec((size, width), strips),
    ]
    out_specs = [fixed(whole)] * 4 + [fixed((8, width))]
    bf16, f32 = jnp.bfloat16, jnp.float32
    out_shapes = [(whole, bf16), (whole, f32), (whole, bf16), (whole, bf16), ((8, width), f32)]
    if split:
        first = pl.BlockSpec((width, size), lambda step, here_ref: (0, jnp.minimum(step, half - 1)))
        second = pl.BlockSpec((width, size), lambda step, here_ref: (0, jnp.maximum(step - half, 0)))
        out_specs += [first, second, first, second]
        out_shapes += [((width, inner // 2), bf16)] * 4
        out_specs += [pl.BlockSpec((size, width // 2), strips)] * 2
        out_shapes += [((inner, width // 2), bf16)] * 2
        out_specs += [fixed((width, width))] * 2
        out_shapes += [((width, width), bf16)] * 2
    else:
        out_specs += [pl.BlockSpec((width, size), columns)] * 2
        out_shapes += [((width, inner), bf16)] * 2
        out_specs += [pl.BlockSpec((size, width), strips), fixed((width, 2 * width))]
        out_shapes += [((inner, width), bf16), ((width, 2 * width), bf16)]
    return pl.pallas_call(
        functools.partial(feed_kernel, split, chunks),
        grid_spec=pltpu.PrefetchScalarGridSpec(
            num_scalar_prefetch=1,
            grid=(chunks,),
            in_specs=in_specs,
            out_specs=tuple(out_specs),
            scratch_shapes=[
                pltpu.VMEM(whole, bf16),
                pltpu.VMEM(whole, bf16),
                pltpu.VMEM(whole, bf16),
                pltpu.VMEM(whole, f32),
                pltpu.VMEM(whole, f32),
                pltpu.VMEM(whole, f32),
                pltpu.VMEM(whole, f32),
                pltpu.VMEM((rows, size), bf16),
                pltpu.VMEM((rows, 2 * size), bf16),
                pltpu.VMEM(whole, bf16),
                pltpu.VMEM(whole, f32),
                pltpu.VMEM((width, rows), bf16),
            ],
        ),
        out_shape=tuple(jax.ShapeDtypeStruct(shape, kind) for shape, kind in out_shapes),
        compiler_params=pltpu.CompilerParams(vmem_limit_bytes=VMEM_BYTES),
        cost_estimate=pl.CostEstimate(
            flops=2 * rows * width * (9 * inner + 5 * width),
            bytes_accessed=12 * width * inner + 24 * rows * width,
            transcendentals=2 * rows * inner,
        ),
        name="feed_layer",
    )(
        jnp.reshape(here, (1,)).astype(jnp.int32),
        attended,
        tokens,
        upstream,
        normed_a,
        mod_rows,
        gate_weight,
        output_weight,
        feed_gate,
        feed_up,
        feed_down,
    )


MASKS = {"u": 8, "v": 4, "y": 2, "x": 1}


def exchange(values, mask):
    return lax.ppermute(values, "crop", [(i, i ^ mask) for i in range(16)])


def swap_res(values):
    return lax.ppermute(values, "res", [(0, 1), (1, 0)])


def tie(*values):
    return lax.optimization_barrier(values)


def add_low(former, latter, kind=jnp.bfloat16):
    return (former.astype(jnp.float32) + latter.astype(jnp.float32)).astype(kind)


def stage_kernel(plans, bits_ref, *refs):
    inputs = refs[: sum(plan["count"] for plan in plans)]
    outputs = list(refs[len(inputs) :])
    for plan in plans:
        mine, inputs = inputs[: plan["count"]], inputs[plan["count"] :]
        out_ref = None if plan["apart"] else outputs[0]
        if not plan["apart"] and plan["merge"] is None:
            outputs.pop(0)
        for column, width, own in plan["parts"]:
            result = outputs.pop(0) if plan["apart"] else out_ref
            target = 0 if plan["apart"] else column
            lead_sizes = () if plan["merge"] is not None else result.shape[:-2]
            for lead in itertools.product(*[range(size) for size in lead_sizes]):
                for first in range(0, plan["rows"], 16):
                    cut = (*lead, slice(first, first + 16))
                    across = slice(column, column + width)
                    total = None
                    for index in own:
                        value = mine[index][(*cut, slice(0, width))].astype(jnp.float32)
                        total = value if total is None else total + value
                    for index in plan["spans"]:
                        total = total + mine[index][(*cut, across)].astype(jnp.float32)
                    fold, local = first // plan["block"], first % plan["block"]
                    if plan["folds"]:
                        value = mine[plan["folds"][fold]][local : local + 16, across]
                        total = total + value.astype(jnp.float32)
                    if plan["merge"] is None:
                        result[(*cut, slice(target, target + width))] = total.astype(result.dtype)
                    else:
                        begin = plan["merge"] + fold * plan["wide"] + column
                        result[local : local + 16, begin : begin + width] = total.astype(result.dtype)


class Halving:
    def __init__(self, streams, orders):
        self.streams = streams
        self.orders = [list(order) for order in orders]
        self.past = [[] for _ in orders]
        self.came = [[] for _ in orders]

    def stage(self, last=False, merge=False, merged=None):
        index = lax.axis_index("crop")
        bits = scalars(*[(index // mask) % 2 for mask in MASKS.values()])
        self.masks, plans, specs, operands, out_specs, out_shapes = [], [], [], [], [], []
        left = 0 if last else len(self.orders[0]) - 1
        fewest = min(parts[0][0][0].shape[0] for parts in self.streams) // 16
        begin = 0
        steps = {3: 4, 2: 2}.get(left, 1)
        for stream, (parts, order, past) in enumerate(zip(self.streams, self.orders, self.past)):
            now = None if last else order.pop(0)
            rest = [axis for axis in MASKS if axis in order]

            def spec_of(axes, rows, width, block, now=now, rest=rest):
                def index_map(step, bits_ref):
                    places = []
                    for axis in axes:
                        bit = bits_ref[list(MASKS).index(axis)]
                        if axis == now:
                            places.append(1 - bit)
                        elif axis not in rest:
                            places.append(bit)
                        elif axis == rest[0] and steps > 1:
                            places.append(step // (steps // 2))
                        elif len(rest) > 1 and axis == rest[1] and steps > 2:
                            places.append(step % 2)
                        else:
                            places.append(0)
                    return (*places, 0, block)

                sizes = [
                    2
                    if axis in rest
                    and not (axis == rest[0] and steps > 1)
                    and not (len(rest) > 1 and axis == rest[1] and steps > 2)
                    else None
                    for axis in axes
                ]
                return pl.BlockSpec((*sizes, rows, width), index_map)

            column = 0
            rows = parts[0][0][0].shape[0] // 16
            wide = sum(width for _, _, width in parts)
            plan = {
                "parts": [],
                "spans": [],
                "folds": [],
                "count": 0,
                "apart": last,
                "rows": rows,
                "block": fewest,
                "wide": wide,
                "merge": begin if merge else None,
            }
            for arrays, block, width in parts:
                own = []
                for value in arrays:
                    operands.append(value.reshape(2, 2, 2, 2, rows, value.shape[1]))
                    specs.append(spec_of(list(MASKS), rows, width, block))
                    own.append(plan["count"])
                    plan["count"] += 1
                plan["parts"].append((column, width, own))
                column += width
            for axes, value in self.came[stream]:
                operands.append(value.reshape(*[2] * len(axes), rows, column))
                specs.append(spec_of(axes, rows, column, 0))
                plan["spans"].append(plan["count"])
                plan["count"] += 1
            if merged is not None:
                for fold in range(rows // fewest):
                    place = (begin + fold * wide) // wide
                    operands.append(merged)
                    specs.append(
                        pl.BlockSpec((fewest, wide), lambda step, bits_ref, place=place: (0, place))
                    )
                    plan["folds"].append(plan["count"])
                    plan["count"] += 1
            begin += wide * (rows // fewest)
            plans.append(plan)
            if last:
                for _, width, _ in plan["parts"]:
                    out_specs.append(pl.BlockSpec((rows, width), lambda step, bits_ref: (0, 0)))
                    out_shapes.append(jax.ShapeDtypeStruct((rows, width), jnp.float32))
            else:
                past.append(now)
                self.masks.append(MASKS[now])
                if not merge:
                    out_specs.append(spec_of(rest, rows, column, 0))
                    out_shapes.append(
                        jax.ShapeDtypeStruct((*[2] * len(rest), rows, column), jnp.bfloat16)
                    )
        if merge:
            out_specs.append(pl.BlockSpec((fewest, begin), lambda step, bits_ref: (0, 0)))
            out_shapes.append(jax.ShapeDtypeStruct((fewest, begin), jnp.bfloat16))
        self.axes = [[axis for axis in MASKS if axis in order] for order in self.orders]
        results = pl.pallas_call(
            functools.partial(stage_kernel, plans),
            grid_spec=pltpu.PrefetchScalarGridSpec(
                num_scalar_prefetch=1, grid=(steps,), in_specs=specs, out_specs=tuple(out_specs)
            ),
            out_shape=tuple(out_shapes),
            compiler_params=pltpu.CompilerParams(vmem_limit_bytes=VMEM_BYTES),
            cost_estimate=pl.CostEstimate(
                flops=sum(4 * math.prod(shape.shape) for shape in out_shapes),
                bytes_accessed=sum(8 * math.prod(shape.shape) for shape in out_shapes),
                transcendentals=0,
            ),
            name="halving_stage",
        )(bits, *operands)
        if merge or last:
            return list(results)
        return [value.reshape(-1, value.shape[-1]) for value in results]

    def send(self, values):
        return [exchange(value, mask) for value, mask in zip(values, self.masks)]

    def take(self, values):
        for came, axes, value in zip(self.came, self.axes, values):
            came.append((axes, value))


def share_columns(values, parts):
    if parts == 1:
        return values.astype(jnp.bfloat16)
    return lax.psum_scatter(values.astype(jnp.bfloat16), "res", scatter_dimension=1, tiled=True)


def scatter_crops(values):
    return lax.psum_scatter(values, "crop", scatter_dimension=0, tiled=True).astype(jnp.float32)


def gather_crops(values, crop_parts):
    if crop_parts != 16:
        return lax.all_gather(values, "crop", axis=0, tiled=True)
    index = lax.axis_index("crop")
    for mask in (1, 2, 4, 8):
        other = exchange(values, mask)
        low = (index // mask) % 2 == 0
        values = jnp.concatenate(
            [jnp.where(low, values, other), jnp.where(low, other, values)], axis=0
        )
    return values


def sum_res(values, parts):
    if parts == 1:
        return values
    if parts != 2:
        return lax.psum(values, "res")
    return values + swap_res(values)


PACK = 1152
SIDE = 384


def whole_vmem(count):
    return [pl.BlockSpec(memory_space=pltpu.VMEM)] * count


def scalars(*values):
    return jnp.stack([jnp.asarray(value, jnp.int32) for value in values])


def local_call(kernel, numbers, operands, shapes, name, flops=0):
    return pl.pallas_call(
        kernel,
        in_specs=[pl.BlockSpec(memory_space=pltpu.SMEM)] + whole_vmem(len(operands)),
        out_specs=tuple(whole_vmem(len(shapes))),
        out_shape=tuple(jax.ShapeDtypeStruct(shape, kind) for shape, kind in shapes),
        compiler_params=pltpu.CompilerParams(vmem_limit_bytes=VMEM_BYTES),
        cost_estimate=pl.CostEstimate(
            flops=flops,
            bytes_accessed=sum(value.size * value.dtype.itemsize for value in operands)
            + sum(4 * math.prod(shape) for shape, _ in shapes),
            transcendentals=0,
        ),
        name=name,
    )(numbers, *operands)


def projection_kernel(counts, here_ref, normed_ref, *refs):
    calls = len(counts)
    parts, (joined_ref, send_ref, keep_ref) = refs[: 3 * calls], refs[3 * calls :]
    width = joined_ref.shape[1] // 3
    column = 0
    for call, pairs in enumerate(counts):
        size = pairs * LANES
        query_ref, own_ref, came_ref = parts[3 * call : 3 * call + 3]
        joined_ref[:, column : column + size] = query_ref[...]
        for start in range(0, joined_ref.shape[0], 16):
            cut = slice(start, start + 16)
            for which in range(2):
                first = (1 + which) * width + column
                joined_ref[cut, first : first + size] = add_low(
                    own_ref[which, cut], came_ref[which, cut]
                )
        column += size
    half = send_ref.shape[1]
    for side, ref in ((1 - here_ref[0], send_ref), (here_ref[0], keep_ref)):
        columns = pl.ds(pl.multiple_of(side * half, LANES), half)
        ref[...] = wide_dot(normed_ref[...], joined_ref[:, columns], TN).astype(jnp.bfloat16)


def projection_gradient(here, normed_a, calls):
    rows, width = normed_a.shape
    counts = [call[0].shape[-1] // LANES for call in calls]
    return local_call(
        functools.partial(projection_kernel, counts),
        scalars(here),
        [normed_a] + [value for call in calls for value in call],
        [
            ((rows, 3 * width), jnp.bfloat16),
            ((width, 3 * width // 2), jnp.bfloat16),
            ((width, 3 * width // 2), jnp.bfloat16),
        ],
        "projection_gradient",
        6 * rows * width * width,
    )


def finish_kernel(counts, joined_ref, weight_ref, pre_ref, gate_ref, tokens_ref, middle_ref, mod_ref, *refs):
    feed_sums_ref, extra_ref = refs[:2]
    table_refs = refs[2 : 2 + len(counts)]
    out_ref, pack_ref, total, folded = refs[2 + len(counts) :]
    step = pl.program_id(0)
    rows, width = tokens_ref.shape
    part = wide_dot(joined_ref[...], weight_ref[...], NT)

    @pl.when(step == 0)
    def _():
        total[...] = part + wide_dot(pre_ref[...], gate_ref[...], NT)

    @pl.when(step > 0)
    def _():
        total[...] += part

    @pl.when(step == pl.num_programs(0) - 1)
    def _():
        scale = mod_ref[1:2]
        folded[...] = jnp.zeros_like(folded)

        def finish(cut):
            values = tokens_ref[cut].astype(jnp.float32)
            centred = values - jnp.mean(values, axis=1, keepdims=True)
            root = lax.rsqrt(jnp.mean(centred * centred, axis=1, keepdims=True) + 1e-06)
            normal = centred * root
            grad = total[cut]
            folded[0] += fold_rows(grad)
            folded[1] += fold_rows(grad * normal)
            scaled = grad * (1.0 + scale)
            out_ref[cut] = (
                middle_ref[cut]
                + root
                * (
                    scaled
                    - jnp.mean(scaled, axis=1, keepdims=True)
                    - normal * jnp.mean(scaled * normal, axis=1, keepdims=True)
                )
            ).astype(jnp.bfloat16)

        each_strip(rows, finish)
        shift_sum, scale_sum = folded[0], folded[1]
        heads = []
        for ref, pairs in zip(table_refs, counts):
            for pair in range(pairs):
                heads += [ref[pair, 0:1], ref[pair, 1:2]]

        def upper_of(values):
            return values.astype(jnp.bfloat16).astype(jnp.float32)

        rests = [head - upper_of(head) for head in heads]
        count = width // LANES
        left = [
            jnp.sum(shift_sum, axis=0, keepdims=True),
            jnp.sum(scale_sum, axis=0, keepdims=True),
            feed_sums_ref[2:6],
        ]
        left += [
            jnp.concatenate(rests[i : i + count], axis=1) for i in range(0, len(heads), count)
        ]
        right = [jnp.concatenate(heads[3 * i : 3 * i + 3], axis=1) for i in range(4)]
        line = extra_ref[5:6]
        right += [extra_ref[4:5], line, line - upper_of(line), extra_ref[7:8]]
        pack = jnp.concatenate(
            [jnp.concatenate(left, axis=0), jnp.concatenate(right, axis=0)], axis=1
        )
        pack_ref[...] = jnp.concatenate([pack, jnp.zeros_like(pack)], axis=0).astype(jnp.bfloat16)


def finish_layer(
    joined, weight, grad_pre, gate_weight, tokens, grad_middle, mod_rows, feed_sums, extra, grad_tables
):
    rows, width = tokens.shape
    counts = [table.shape[0] for table in grad_tables]

    def fixed(shape):
        return pl.BlockSpec(shape, lambda step: (0,) * len(shape), pipeline_mode=pl.Buffered(1))

    return pl.pallas_call(
        functools.partial(finish_kernel, counts),
        grid=(3,),
        in_specs=[
            pl.BlockSpec((rows, width), lambda step: (0, step)),
            pl.BlockSpec((width, width), lambda step: (0, step)),
            fixed((rows, width)),
            fixed((width, width)),
            fixed((rows, width)),
            fixed((rows, width)),
            fixed((8, width)),
            fixed((8, width)),
            fixed((8, SIDE)),
        ]
        + [fixed((count, 8, LANES)) for count in counts],
        out_specs=(fixed((rows, width)), fixed((16, PACK))),
        out_shape=(
            jax.ShapeDtypeStruct((rows, width), jnp.bfloat16),
            jax.ShapeDtypeStruct((16, PACK), jnp.bfloat16),
        ),
        scratch_shapes=[
            pltpu.VMEM((rows, width), jnp.float32),
            pltpu.VMEM((2, 8, width), jnp.float32),
        ],
        compiler_params=pltpu.CompilerParams(vmem_limit_bytes=VMEM_BYTES),
        cost_estimate=pl.CostEstimate(
            flops=8 * rows * width * width, bytes_accessed=24 * rows * width, transcendentals=0
        ),
        name="finish_layer",
    )(
        joined,
        weight,
        grad_pre,
        gate_weight,
        tokens,
        grad_middle,
        mod_rows,
        feed_sums,
        extra,
        *grad_tables,
    )


def fan_first_kernel(bits_ref, keep_ref, came_ref, mine_ref, *send_refs):
    chunk = keep_ref.shape[0] // 16
    for other, ref in enumerate((mine_ref, *send_refs)):
        for level in range(4):
            start = (level * 4 + (bits_ref[0] ^ other)) * chunk
            for first in range(0, chunk, 16):
                cut = pl.ds(pl.multiple_of(start + first, 16), 16)
                place = level * chunk + first
                ref[place : place + 16] = add_low(keep_ref[cut], came_ref[cut])


def fan_v_kernel(bits_ref, mine_ref, *refs):
    came_refs, (send_ref, out_ref) = refs[:3], refs[3:]
    chunk = mine_ref.shape[0] // 4
    for side, ref in ((1 - bits_ref[0], send_ref), (bits_ref[0], out_ref)):
        for far in range(2):
            for first in range(0, chunk, 16):
                cut = pl.ds(pl.multiple_of((2 * far + side) * chunk + first, 16), 16)
                total = mine_ref[cut].astype(jnp.float32)
                for came_ref in came_refs:
                    total = total + came_ref[cut].astype(jnp.float32)
                place = far * chunk + first
                ref[place : place + 16] = total.astype(jnp.bfloat16)


def fan_u_kernel(bits_ref, mine_ref, came_ref, send_ref, out_ref):
    chunk = mine_ref.shape[0] // 2
    for side, ref in ((1 - bits_ref[0], send_ref), (bits_ref[0], out_ref)):
        for first in range(0, chunk, 16):
            cut = pl.ds(pl.multiple_of(side * chunk + first, 16), 16)
            ref[first : first + 16] = add_low(mine_ref[cut], came_ref[cut])


def join_packs_kernel(bits_ref, *refs):
    packs = [ref[...].astype(jnp.float32)[0:8] for ref in refs[:4]]
    refs[4][...] = jnp.concatenate(packs, axis=0).astype(jnp.bfloat16)


def small_kernel(
    heads,
    here_ref,
    mine_ref,
    came_ref,
    modulation_ref,
    pair_norm_ref,
    relative_ref,
    gain_ref,
    pair_weight_ref,
    mod_grad_ref,
    time_ref,
    label_ref,
    relative_grad_ref,
    gain_grad_ref,
    pair_grad_ref,
    grad_condition,
    grad_mod,
    kept,
):
    step = pl.program_id(0)
    crops = mine_ref.shape[0] // 8
    width = mine_ref.shape[1] - SIDE
    conds = relative_ref.shape[1]
    parts = mod_grad_ref.shape[1] // width

    def parts_split(values):
        upper = values.astype(jnp.bfloat16)
        return upper, (values - upper.astype(jnp.float32)).astype(jnp.bfloat16)

    def dot_left(narrow, values, numbers):
        upper, rest = parts_split(values)
        return wide_dot(narrow, upper, numbers) + wide_dot(narrow, rest, numbers)

    def dot_right(values, narrow, numbers):
        upper, rest = parts_split(values)
        return wide_dot(upper, narrow, numbers) + wide_dot(rest, narrow, numbers)

    def both_twice(narrow):
        return jnp.concatenate([narrow, narrow], axis=0)

    def stacked(values):
        return jnp.concatenate(parts_split(values), axis=0)

    @pl.when(step == 0)
    def _():
        shape = (8 * crops, 8 * crops)
        picked = lax.broadcasted_iota(jnp.int32, shape, 0)
        source = lax.broadcasted_iota(jnp.int32, shape, 1)
        hit = ((source >> 3) == (picked & (crops - 1))) & ((source & 7) == (picked // crops))
        select = jnp.where(hit, 1.0, 0.0).astype(jnp.bfloat16)
        mine = wide_dot(select, mine_ref[...])
        grad_mod[...] = mine[: 6 * crops, :width] + wide_dot(select, came_ref[...])[: 6 * crops, :width]
        condition = (
            mine[5 * crops : 6 * crops, width : width + conds]
            + mine[6 * crops : 7 * crops, width : width + conds]
        )
        gate_value = sigmoid(condition)
        kept[0] = condition * gate_value
        kept[1] = gate_value * (1.0 + condition * (1.0 - gate_value))
        kept[2] = mine[4 * crops : 5 * crops, width : width + conds]
        kept[3] = jnp.broadcast_to(
            mine[5 * crops : 6 * crops, width + conds : width + conds + 1]
            + mine[6 * crops : 7 * crops, width + conds : width + conds + 1],
            (crops, conds),
        )
        grad_condition[...] = jnp.zeros_like(grad_condition)

    cond_act = both_twice(kept[0].astype(jnp.bfloat16))
    for turn in range(parts):
        columns = slice(turn * width, (turn + 1) * width)
        first = pl.multiple_of((step * parts + turn) * crops, crops)
        pair = stacked(grad_mod[pl.ds(first, crops)])
        mod_grad_ref[:, columns] = wide_dot(cond_act, pair, TN)
        more = wide_dot(pair, modulation_ref[:, columns], NT)
        grad_condition[...] += more[:crops] + more[crops:]

    @pl.when(step == 0)
    def _():
        shape = (8, 8 * crops)
        line = lax.broadcasted_iota(jnp.int32, shape, 0)
        local = lax.broadcasted_iota(jnp.int32, shape, 1) & 7
        every = jnp.where(local == line, 1.0, 0.0).astype(jnp.bfloat16)
        lines = wide_dot(every, mine_ref[...]) + wide_dot(every, came_ref[...])

        def of_head(head):
            upper = width + (head % 3) * LANES
            rest = (head % (width // LANES)) * LANES
            low = 6 + head // (width // LANES)
            return (
                lines[head // 3 : head // 3 + 1, upper : upper + LANES]
                + lines[low : low + 1, rest : rest + LANES]
            )

        table = jnp.concatenate(
            [of_head(head) for head in range(heads)]
            + [jnp.zeros((16 - heads, LANES), jnp.float32)],
            axis=0,
        )
        bins = relative_ref.shape[0]
        pair_grad_ref[...] = dot_right(table, pair_norm_ref[...], (((1,), (0,)), ((), ())))[:heads]
        grad_norm = dot_right(table, pair_weight_ref[...], (((0,), (1,)), ((), ())))[:bins]
        values = relative_ref[...].astype(jnp.float32)
        centred = values - jnp.mean(values, axis=1, keepdims=True)
        root = lax.rsqrt(jnp.mean(centred * centred, axis=1, keepdims=True) + 1e-06)
        normal = centred * root
        gain_grad_ref[...] = jnp.sum(grad_norm * normal, axis=0, keepdims=True)
        scaled = grad_norm * gain_ref[...].astype(jnp.float32)
        relative_grad_ref[...] = root * (
            scaled
            - jnp.mean(scaled, axis=1, keepdims=True)
            - normal * jnp.mean(scaled * normal, axis=1, keepdims=True)
        )

    @pl.when(step == pl.num_programs(0) - 1)
    def _():
        final = stacked(grad_condition[...] * kept[1])
        time_ref[...] = wide_dot(both_twice(kept[2].astype(jnp.bfloat16)), final, TN)
        label = lax.broadcasted_iota(jnp.int32, (crops, label_ref.shape[0]), 1)
        number = kept[3][:, 0:1].astype(jnp.int32)
        onehot = jnp.where(label == number, 1.0, 0.0).astype(jnp.bfloat16)
        label_ref[...] = wide_dot(both_twice(onehot), final, TN)


def small_gradients(heads, labels, mine, came, modulation_weight, pair_norm, relative, gain, pair_weight):
    conds, wide = modulation_weight.shape
    bins = relative.shape[0]
    rows = mine.shape[0]
    steps = 3

    def fixed(shape):
        return pl.BlockSpec(shape, lambda step: (0, 0))

    shapes = [(conds, wide), (conds, conds), (labels, conds), (bins, conds), (1, conds), (heads, conds)]
    return pl.pallas_call(
        functools.partial(small_kernel, heads),
        grid=(steps,),
        in_specs=[
            pl.BlockSpec(memory_space=pltpu.SMEM),
            fixed((rows, PACK)),
            fixed((rows, PACK)),
            pl.BlockSpec((conds, wide // steps), lambda step: (0, step)),
            fixed((LANES, conds)),
            fixed((bins, conds)),
            fixed((1, conds)),
            fixed((conds, 16)),
        ],
        out_specs=tuple(
            [pl.BlockSpec((conds, wide // steps), lambda step: (0, step))]
            + [fixed(s) for s in shapes[1:]]
        ),
        out_shape=tuple(jax.ShapeDtypeStruct(shape, jnp.float32) for shape in shapes),
        scratch_shapes=[
            pltpu.VMEM((rows // 8, conds), jnp.float32),
            pltpu.VMEM((6 * rows // 8, wide // 6), jnp.float32),
            pltpu.VMEM((4, rows // 8, conds), jnp.float32),
        ],
        compiler_params=pltpu.CompilerParams(vmem_limit_bytes=VMEM_BYTES),
        cost_estimate=pl.CostEstimate(
            flops=100000000, bytes_accessed=10000000, transcendentals=0
        ),
        name="small_gradients",
    )(
        scalars(0),
        mine,
        came,
        modulation_weight,
        pair_norm,
        relative,
        gain,
        pair_weight,
    )


def per_device(
    crop_parts,
    res_parts,
    tokens,
    cotangent,
    time_levels,
    cath_ids,
    residue_numbers,
    chain_mask,
    time_weight,
    label_table,
    modulation_weight,
    projection_weight,
    gate_weight,
    output_weight,
    relative_table,
    pair_gain,
    pair_weight,
    feed_gate,
    feed_up,
    feed_down,
):
    crop_count, row_count, model_width = tokens.shape
    crop_length = residue_numbers.shape[1]
    head_count = pair_weight.shape[1]
    head_width = model_width // head_count
    bin_count = relative_table.shape[0]
    label_count = label_table.shape[0]
    token_count = crop_count * row_count
    score_scale = head_width ** (-0.5)
    pairs = head_count // 2
    layout = Layout(row_count, crop_length)
    query_start = lax.axis_index("res") * row_count

    def conditioning(features, onehot):
        return jnp.dot(features, time_weight, preferred_element_type=jnp.float32) + jnp.dot(
            onehot, label_table, preferred_element_type=jnp.float32
        )

    features = time_features(time_levels, time_weight.shape[0]).astype(jnp.bfloat16)
    label_onehot = (cath_ids[:, None] == jnp.arange(label_count, dtype=jnp.int32)[None, :]).astype(
        jnp.bfloat16
    )
    condition = conditioning(features, label_onehot)
    cond_act = jax.nn.silu(condition).astype(jnp.bfloat16)
    modulation = jnp.dot(cond_act, modulation_weight, preferred_element_type=jnp.float32)
    modulation = modulation.reshape(crop_count, 6, 1, model_width)
    shift_a, scale_a = modulation[:, 0], modulation[:, 1]
    mod_rows = pad_to(modulation[:, :, 0], 1, 8, 0.0)

    rotated = lax.dynamic_slice_in_dim(
        jnp.concatenate([jnp.stack([residue_numbers, chain_mask])] * 2, 2), query_start, crop_length, 2
    )
    members, kinds, forward_bins, backward_bins, places, *turned, tables, pair_norm = attention_tables(
        layout,
        score_scale,
        rotated[0],
        rotated[1],
        query_start,
        relative_table,
        pair_gain,
        pair_weight,
    )

    token_values = tokens.astype(jnp.float32)
    normed_a = (
        modulate(token_values, shift_a, scale_a)
        .astype(jnp.bfloat16)
        .reshape(token_count, model_width)
    )
    def project(weight):
        rows = jnp.dot(normed_a, weight, preferred_element_type=jnp.float32)
        return rows.astype(jnp.bfloat16).reshape(crop_count, row_count, -1)

    key_values = project(projection_weight[:, model_width:])
    others = [
        lax.ppermute(
            key_values, "res", [((r + step) % res_parts, r) for r in range(res_parts)]
        )
        for step in range(1, res_parts)
    ]
    if len(layout.pieces) == 2:
        other = others[0] if len(others) == 1 else jnp.concatenate(others, axis=1)
        pieces = [(key_values, 0, pairs), (other, 0, pairs)]
    else:
        pieces = [(jnp.concatenate([key_values] + others, axis=1), 0, pairs)]

    def block_rows(values):
        return pad_to(values, 1, layout.block_rows, 0)

    queries, attended, logs = attention_forward(
        layout,
        score_scale,
        block_rows(normed_a.reshape(tokens.shape)),
        projection_weight,
        pieces,
        members,
        kinds,
        forward_bins,
        tables,
    )
    here = lax.axis_index("res")
    split = res_parts == 2 and crop_parts == 16
    per_crop_results = [
        feed_layer(
            split,
            here,
            attended[crop],
            block_rows(tokens)[crop],
            block_rows(cotangent)[crop],
            block_rows(normed_a.reshape(tokens.shape))[crop],
            mod_rows[crop],
            gate_weight,
            output_weight,
            feed_gate,
            feed_up,
            feed_down,
        )
        for crop in range(crop_count)
    ]
    layer_out, grad_middle, grad_attended, grad_gate_pre, feed_sums = (
        jnp.stack([result[place] for result in per_crop_results]) for place in range(5)
    )
    layer_out, grad_middle = layer_out[:, :row_count], grad_middle[:, :row_count]
    grad_gate_pre = grad_gate_pre[:, :row_count].reshape(token_count, model_width)
    weight_grads = [
        sum(result[place].astype(jnp.float32) for result in per_crop_results).astype(jnp.bfloat16)
        if crop_count > 1
        else per_crop_results[0][place]
        for place in range(5, len(per_crop_results[0]))
    ]

    def backward_of(first_pair, count, grad_now):
        return attention_backward(
            layout,
            score_scale,
            first_pair,
            count,
            queries,
            grad_now,
            attended,
            logs,
            pieces,
            members,
            kinds,
            backward_bins,
            places,
            *turned,
            tables,
        )

    if split:
        arrivals = [swap_res(weight_grads[place]) for place in (0, 2, 4, 6)]
        kept = [weight_grads[place] for place in (1, 3, 5, 7)]
        half = model_width // 2
        inner = feed_gate.shape[1] // 2
        calls = [list(backward_of(0, 1, grad_attended))]
        arrivals, calls[0] = tie(arrivals, calls[0])
        gate_w, up_w, down_w, small_w = zip(kept, arrivals)
        halving = Halving(
            [
                [(gate_w, 0, inner), (small_w, 0, half)],
                [(up_w, 0, inner), (small_w, 1, half)],
                [(down_w, 0, half)],
            ],
            ["xyvu", "yvxu", "vxyu"],
        )
        arrived = []
        for first_pair, count in ((1, 4), (5, 1)):
            arrived.append(swap_res(calls[-1][2][0]))
            sent = halving.stage()
            sent, grad_attended = tie(sent, grad_attended)
            came = halving.send(sent)
            calls.append(list(backward_of(first_pair, count, grad_attended)))
            came, calls[-1], arrived[-1] = tie(came, calls[-1], arrived[-1])
            halving.take(came)
        index = lax.axis_index("crop")
        bf16 = jnp.bfloat16
        share = model_width // 16
        away = swap_res(calls[2][2][0])
        sent = halving.stage()
        sent, calls[2][1] = tie(sent, calls[2][1])
        came = halving.send(sent)
        joined, proj_send, proj_keep = projection_gradient(
            here,
            normed_a,
            [
                (calls[0][0][0], calls[0][1][0], arrived[0]),
                (calls[1][0][0], calls[1][1][0], arrived[1]),
                (calls[2][0][0], calls[2][1][0], away),
            ],
        )
        came, proj_send, proj_keep = tie(came, proj_send, proj_keep)
        proj_came = swap_res(proj_send)
        halving.take(came)
        (sent,) = halving.stage(merge=True)
        sent, proj_came = tie(sent, proj_came)
        came = exchange(sent, MASKS["u"])
        mine, *fan = local_call(
            fan_first_kernel,
            scalars(index % 4),
            [proj_keep, proj_came],
            [((4 * share, PACK), bf16)] * 4,
            "fan_first",
        )
        fan, joined = tie(fan, joined)
        fan_came = [exchange(value, mask + 1) for mask, value in enumerate(fan)]
        extra = jnp.concatenate(
            [
                pad_to(features.astype(jnp.float32), 1, SIDE, 0.0),
                jnp.concatenate(
                    [condition, pad_to(cath_ids.astype(jnp.float32)[:, None], 1, LANES, 0.0)], axis=1
                ),
            ],
            axis=0,
        )
        tokens_grad, pack = finish_layer(
            joined,
            projection_weight,
            grad_gate_pre,
            gate_weight,
            tokens[0],
            grad_middle[0],
            mod_rows[0],
            feed_sums[0],
            jnp.pad(extra, ((4, 2), (0, 0))),
            [call[-1][0] for call in calls],
        )
        tokens_grad = tokens_grad[None]
        came, pack = tie(came, pack)
        packs = [pack] + [exchange(pack, mask + 1) for mask in range(3)]
        finals = halving.stage(last=True, merged=came)
        feed_gate_grad, output_weight_grad, feed_up_grad, gate_weight_grad, feed_down_grad = finals
        packs, finals = tie(packs, finals)
        (packs,) = local_call(join_packs_kernel, scalars(0), packs, [((32, PACK), bf16)], "join_packs")
        far_packs = exchange(packs, MASKS["v"])
        packs, fan_came, far_packs = tie(packs, fan_came, far_packs)
        sent, mine = local_call(
            fan_v_kernel,
            scalars((index // 4) % 2),
            [mine, *fan_came],
            [((2 * share, PACK), bf16), ((2 * share, PACK), bf16)],
            "fan_v",
        )
        packs = jnp.concatenate([packs, far_packs], axis=0)
        sent, packs = tie(sent, packs)
        came = exchange(sent, MASKS["v"])
        far_packs = exchange(packs, MASKS["u"])
        came, far_packs = tie(came, far_packs)
        packs = jnp.concatenate([packs, far_packs], axis=0)
        sent, mine = local_call(
            fan_u_kernel,
            scalars(index // 8),
            [mine, came],
            [((share, PACK), bf16), ((share, PACK), bf16)],
            "fan_u",
        )
        sent, packs = tie(sent, packs)
        came = exchange(sent, MASKS["u"])
        (
            modulation_weight_grad,
            time_weight_grad,
            label_table_grad,
            relative_table_grad,
            pair_gain_grad,
            pair_weight_grad,
        ) = small_gradients(
            head_count,
            label_count,
            packs,
            swap_res(packs),
            modulation_weight,
            pair_norm,
            relative_table,
            pair_gain.reshape(1, -1),
            pad_to(pair_weight, 1, 16, 0.0),
        )
        pair_weight_grad = pair_weight_grad.T
        came, pair_weight_grad = tie(came, pair_weight_grad)
        projection_weight_grad = add_low(mine, came, jnp.float32)
        pair_gain_grad = pair_gain_grad[0]
    else:
        results = backward_of(0, pairs, grad_attended)
        grad_table = results[-1]
        grad_pairs = results[1:-1]
        if len(grad_pairs) == 2:
            total, away = grad_pairs[0].astype(jnp.float32), grad_pairs[1]
        else:
            total = grad_pairs[0][:, :, :row_count].astype(jnp.float32)
            away = grad_pairs[0][:, :, row_count:]
        for step in range(1, res_parts):
            sent = away[:, :, (step - 1) * row_count : step * row_count]
            pairs_to = [(r, (r + step) % res_parts) for r in range(res_parts)]
            total = total + lax.ppermute(sent, "res", pairs_to).astype(jnp.float32)
        total = total.astype(jnp.bfloat16)
        grad_projected = jnp.concatenate(
            [results[0][:, :row_count], total[:, 0], total[:, 1]], axis=-1
        ).reshape(token_count, 3 * model_width)
        grad_normed_a = against_columns(grad_projected, projection_weight) + against_columns(
            grad_gate_pre, gate_weight
        )
        norm_back_a = jax.vjp(modulate, token_values, shift_a, scale_a)[1]
        grad_tokens, grad_shift_a, grad_scale_a = norm_back_a(
            grad_normed_a.reshape(crop_count, row_count, model_width)
        )
        tokens_grad = (grad_middle + grad_tokens).astype(jnp.bfloat16)
        feed_gate_grad, feed_up_grad, feed_down_grad = (
            scatter_crops(share_columns(value, res_parts)) for value in weight_grads[:3]
        )
        output_weight_grad, gate_weight_grad = (
            scatter_crops(share_columns(value, res_parts))
            for value in (weight_grads[3][:, :model_width], weight_grads[3][:, model_width:])
        )
        projection_weight_grad = scatter_crops(
            share_columns(across_rows(normed_a, grad_projected), res_parts)
        )
        grad_table = grad_table[:, :, :2].sum(0).reshape(head_count, LANES)

        grad_modulation = jnp.concatenate([grad_shift_a, grad_scale_a, feed_sums[:, 2:6]], axis=1)
        grad_modulation = grad_modulation.reshape(crop_count, 6 * model_width)
        table_row = grad_table.reshape(1, head_count * LANES)
        first_row = (jnp.arange(crop_count) == 0).astype(jnp.float32)[:, None]
        small_here = jnp.concatenate([grad_modulation, first_row * table_row], axis=1)
        levels_here = jnp.stack([time_levels, cath_ids.astype(jnp.float32)], axis=1)
        levels_here = pad_to(levels_here, 1, LANES, 0.0)
        small_all = gather_crops(
            jnp.concatenate([levels_here, sum_res(small_here, res_parts)], axis=1), crop_parts
        )
        levels_all, small_all = small_all[:, :2], small_all[:, LANES:]
        grad_modulation = small_all[:, : 6 * model_width]
        grad_table = jnp.sum(small_all[:, 6 * model_width :], axis=0).reshape(head_count, LANES)
        grad_table = grad_table[:, :bin_count]
        features_all = time_features(levels_all[:, 0], time_weight.shape[0]).astype(jnp.bfloat16)
        onehot_all = (
            levels_all[:, 1].astype(jnp.int32)[:, None]
            == jnp.arange(label_count, dtype=jnp.int32)[None, :]
        ).astype(jnp.bfloat16)
        condition = conditioning(features_all, onehot_all)
        cond_act = jax.nn.silu(condition).astype(jnp.bfloat16)
        modulation_weight_grad = split_left(cond_act, grad_modulation, 0, 0)
        grad_condition = split_left(modulation_weight, grad_modulation, 1, 1).T * silu_slope(condition)
        time_weight_grad = split_left(features_all, grad_condition, 0, 0)
        label_table_grad = split_left(onehot_all, grad_condition, 0, 0)
        relative_values = relative_table.astype(jnp.float32)
        gain_values = pair_gain.astype(jnp.float32)
        pair_norm = pair_norm[:bin_count]
        pair_weight_grad = split_left(pair_norm, grad_table, 0, 1)
        grad_pair_norm = split_right(grad_table, pair_weight, 0, 1)
        pair_back = jax.vjp(normalize_rows, relative_values, gain_values)[1]
        relative_table_grad, pair_gain_grad = pair_back(grad_pair_norm)
    return (
        layer_out,
        tokens_grad,
        time_weight_grad,
        label_table_grad,
        modulation_weight_grad,
        projection_weight_grad,
        gate_weight_grad,
        output_weight_grad,
        relative_table_grad,
        pair_gain_grad,
        pair_weight_grad,
        feed_gate_grad,
        feed_up_grad,
        feed_down_grad,
    )


def solution(mesh):
    return jax.shard_map(
        functools.partial(per_device, mesh.shape["crop"], mesh.shape["res"]),
        mesh=mesh,
        in_specs=(
            P("crop", "res", None),
            P("crop", "res", None),
            P("crop"),
            P("crop"),
            P("crop", None),
            P("crop", None),
            P(),
            P(),
            P(),
            P(),
            P(),
            P(),
            P(),
            P(),
            P(),
            P(),
            P(),
            P(),
        ),
        out_specs=(
            P("crop", "res", None),
            P("crop", "res", None),
            P(),
            P(),
            P(),
            P("crop", "res"),
            P("crop", "res"),
            P("crop", "res"),
            P(),
            P(),
            P(),
            P("crop", "res"),
            P("crop", "res"),
            P("crop", "res"),
        ),
        check_vma=False,
    )
```

```python
import functools
import itertools
import math

import jax
import jax.numpy as jnp
from jax import lax
from jax.experimental import pallas as pl
from jax.experimental.pallas import tpu as pltpu
from jax.sharding import PartitionSpec as P

LANES = 128
NEAR = 31
VMEM_BYTES = 56 * 1024 * 1024
LOG2E = 1.4426950408889634
NONE, RIGHT, LEFT, APART = 0, 1, 2, 3


def layer_norm(inputs):
    mean_value = jnp.mean(inputs, axis=-1, keepdims=True)
    centred = inputs - mean_value
    spread = jnp.mean(centred * centred, axis=-1, keepdims=True)
    return centred * lax.rsqrt(spread + 1e-06)


def modulate(inputs, shift_row, scale_row):
    return layer_norm(inputs) * (1.0 + scale_row) + shift_row


def normalize_rows(table_rows, gain_row):
    return layer_norm(table_rows) * gain_row


def time_features(time_levels, feature_width):
    half_width = feature_width // 2
    frequency = jnp.exp(-math.log(10000.0) * jnp.arange(half_width, dtype=jnp.float32) / half_width)
    angles = 1000.0 * time_levels[:, None] * frequency[None, :]
    return jnp.concatenate([jnp.sin(angles), jnp.cos(angles)], axis=-1)


def across_rows(former, latter):
    return lax.dot_general(
        former, latter, (((0,), (0,)), ((), ())), preferred_element_type=jnp.float32
    )


def against_columns(former, latter):
    return lax.dot_general(
        former, latter, (((1,), (1,)), ((), ())), preferred_element_type=jnp.float32
    )


def split_parts(values):
    upper = lax.reduce_precision(values, 8, 7)
    return (upper.astype(jnp.bfloat16), (values - upper).astype(jnp.bfloat16))


def split_left(narrow, values, former_dim, latter_dim):
    upper, rest = split_parts(values)
    numbers = (((former_dim,), (latter_dim,)), ((), ()))
    return lax.dot_general(
        narrow, upper, numbers, preferred_element_type=jnp.float32
    ) + lax.dot_general(narrow, rest, numbers, preferred_element_type=jnp.float32)


def split_right(values, narrow, former_dim, latter_dim):
    upper, rest = split_parts(values)
    numbers = (((former_dim,), (latter_dim,)), ((), ()))
    return lax.dot_general(
        upper, narrow, numbers, preferred_element_type=jnp.float32
    ) + lax.dot_general(rest, narrow, numbers, preferred_element_type=jnp.float32)


def sigmoid_slope(inputs):
    gate_value = jax.nn.sigmoid(inputs)
    return gate_value * (1.0 - gate_value)


def silu_slope(inputs):
    gate_value = jax.nn.sigmoid(inputs)
    return gate_value * (1.0 + inputs * (1.0 - gate_value))


class Layout:
    def __init__(self, rows, length):
        self.rows = rows
        self.length = length
        self.query_tiles = -(-rows // LANES)
        self.key_tiles = -(-length // LANES)
        self.padded = self.query_tiles * LANES
        self.wide = self.key_tiles * LANES
        self.last = self.key_tiles - 1
        self.groups = (self.query_tiles + 4) * 4
        assert 2 * self.groups + 3 <= LANES and self.groups <= 64
        assert rows - 1 + NEAR < self.padded and length - NEAR >= self.last * LANES
        assert rows % 8 == 0 and self.last > self.query_tiles
        self.block_rows = rows if rows % 16 == 0 else self.padded
        self.pieces = [rows, length - rows] if rows % 16 == 0 else [length]

    def tile_start(self, tile):
        return self.last * LANES if tile < 0 else tile * LANES


def pad_to(values, axis, size, fill):
    widths = [(0, 0)] * values.ndim
    widths[axis] = (0, size - values.shape[axis])
    return jnp.pad(values, widths, constant_values=fill)


def tables_kernel(
    layout, bin_count, heads, scale, start_ref, pairs_ref, relative_ref, gain_ref, weight_ref, *out_refs
):
    members_ref, kinds_ref, forward_ref, backward_ref, places_ref = out_refs[:5]
    members_turned, kinds_turned, tables_ref, norm_ref, codes = out_refs[5:]
    rows, length, queries, groups = layout.rows, layout.length, layout.query_tiles, layout.groups
    wrap = length - start_ref[0]
    reach = (bin_count - 2) // 2
    zero_bin = LANES - 1
    shape = (LANES, LANES)
    lane = lax.broadcasted_iota(jnp.int32, shape, 1)
    row = lax.broadcasted_iota(jnp.int32, shape, 0)
    last_start = layout.last * LANES

    values = relative_ref[...].astype(jnp.float32)
    centred = values - jnp.mean(values, axis=1, keepdims=True)
    root = lax.rsqrt(jnp.mean(centred * centred, axis=1, keepdims=True) + 1e-06)
    pair_norm = (centred * root * gain_ref[...].astype(jnp.float32)).astype(jnp.bfloat16)
    norm_ref[...] = pair_norm
    bias = lax.dot_general(
        weight_ref[...], pair_norm, (((0,), (1,)), ((), ())), preferred_element_type=jnp.float32
    )
    head_lane = lax.broadcasted_iota(jnp.int32, bias.shape, 1)
    final = jnp.sum(jnp.where(head_lane == bin_count - 1, bias, 0.0), axis=1, keepdims=True)
    table = jnp.where(head_lane < bin_count, (bias - final) * (1.0 / scale), 0.0)

    def columns(number):
        value = jnp.sum(jnp.where(head_lane == number, table, 0.0), axis=1, keepdims=True)
        upper = value.astype(jnp.bfloat16).astype(jnp.float32)
        return jnp.where(
            head_lane < groups, upper, jnp.where(head_lane < 2 * groups, value - upper, 0.0)
        )

    right_columns, left_columns = columns(bin_count - 2), columns(0)
    for head in range(heads):
        line = 8 * (head % 2)
        for place, rows_of in enumerate((table, right_columns, left_columns)):
            tables_ref[head // 2, line + place : line + place + 1] = rows_of[head : head + 1]

    tiles = pairs_ref.shape[1]
    marks = pairs_ref[1].astype(jnp.float32)
    place = lax.broadcasted_iota(jnp.int32, marks.shape, 0) * LANES + lax.broadcasted_iota(
        jnp.int32, marks.shape, 1
    )
    before = jnp.sum(jnp.where(place < wrap, marks, 0.0), keepdims=True)
    every = jnp.sum(marks, keepdims=True)
    triangle = jnp.where(row <= lane, 1.0, 0.0).astype(jnp.bfloat16)
    running = jnp.dot(marks.astype(jnp.bfloat16), triangle, preferred_element_type=jnp.float32)
    numbers, chains = [], []
    carry = jnp.zeros((1, 1), jnp.float32)
    for tile in range(layout.key_tiles):
        count = running[tile : tile + 1] + carry
        carry = carry + running[tile : tile + 1, LANES - 1 :]
        count = count + jnp.where(place[tile : tile + 1] < wrap, every - before, -before)
        chains.append(jnp.broadcast_to(count.astype(jnp.int32), shape))
        numbers.append(jnp.broadcast_to(pairs_ref[0, tile : tile + 1], shape))
    number_rows = [value.T for value in numbers]
    chain_rows = [value.T for value in chains]

    def bins_of(key_number, key_chain, query_number, query_chain):
        offset = jnp.clip(key_number - query_number, -reach, reach) + reach
        return jnp.where(key_chain == query_chain, offset, bin_count - 1)

    def touches(query, tile):
        begin = -LANES if tile < 0 else tile * LANES
        return (begin <= query + NEAR) & (query - NEAR <= begin + LANES - 1)

    for tile in range(layout.key_tiles):
        size = min(LANES, length - tile * LANES)
        key = tile * LANES + row
        if tile == layout.last:
            other = jnp.full(shape, queries + 3, jnp.int32)
        elif tile == queries - 1:
            other = jnp.full(shape, queries, jnp.int32)
        else:
            other = jnp.where(key < wrap, queries + 1, queries + 2)
        group = jnp.where(key < rows, tile, other)
        slot = group * 4 + chain_rows[tile] - 1
        hit = (lane == slot) | (lane == slot + groups)
        tail = (lane >= 2 * groups) & (lane < 2 * groups + 3)
        values = jnp.where(hit, 1.0, jnp.where(tail, -1.0, 0.0)).astype(jnp.bfloat16)
        members_ref[tile * LANES : tile * LANES + size] = values[:size]
        turned = jnp.where(hit & (lane < groups), 1.0, 0.0).T
        members_turned[:, tile * LANES : tile * LANES + size] = turned[:64, :size].astype(jnp.bfloat16)

    local = jnp.where(lane >= groups, lane - groups, lane)
    lane_group = local >> 2
    lane_chain = (local & 3) + 1
    lane_begin = jnp.where(
        lane_group < queries,
        lane_group * LANES,
        jnp.where(lane_group == queries, (queries - 1) * LANES, -LANES),
    )
    has_band = (lane_group <= queries) | (lane_group == queries + 3)
    other_right = jnp.where(
        lane_group == queries,
        rows,
        jnp.where(
            lane_group == queries + 3,
            last_start,
            jnp.where(lane_group == queries + 1, 0, 2 * length),
        ),
    )
    right_limit = jnp.where(lane_group > queries, jnp.where(lane_group == queries + 3, wrap, length), wrap)
    for tile in range(queries):
        size = min(LANES, layout.block_rows - tile * LANES)
        query = tile * LANES + row
        near = (lane_begin <= query + NEAR) & (query - NEAR <= lane_begin + LANES - 1) & has_band
        right = jnp.where(lane_group < queries, lane_group - tile, right_limit - other_right) > 0
        same = chain_rows[tile] == lane_chain
        kinds = jnp.where(same, jnp.where(near, NONE, jnp.where(right, RIGHT, LEFT)), APART)
        kinds = jnp.where((lane < 2 * groups) & (query < rows), kinds, NONE)
        kinds_ref[tile * LANES : tile * LANES + size] = kinds[:size]
        kinds_turned[:, tile * LANES : (tile + 1) * LANES] = jnp.where(lane < groups, kinds, NONE).T[:64]
        for step in range(3):
            near_tile = tile + step - 1
            index = layout.last if near_tile < 0 else near_tile
            if near_tile < queries:
                inside = touches(query, near_tile) & (query < rows)
                inside &= lane < length - index * LANES
                found = bins_of(
                    numbers[index], chains[index], number_rows[tile], chain_rows[tile]
                )
                found = jnp.where(inside, found, zero_bin)
            else:
                found = jnp.full(shape, zero_bin, jnp.int32)
            forward_ref[
                tile * LANES : (tile + 1) * LANES, step * LANES : (step + 1) * LANES
            ] = found

    codes[...] = jnp.full(codes.shape, -1, jnp.int32)
    for tile in range(queries):
        size = min(LANES, rows - tile * LANES)
        code = number_rows[tile] * 8 + chain_rows[tile]
        codes[(tile + 1) * LANES : (tile + 1) * LANES + size] = code[:size]

    for index, tile in enumerate(list(range(queries)) + [-1]):
        source = layout.last if tile < 0 else tile
        key_row = (row - (length - last_start)) if tile < 0 else tile * LANES + row
        present = row < length - source * LANES
        for step in range(3):
            near_tile = tile + step - 1
            if 0 <= near_tile < queries:
                near_query = near_tile * LANES + lane
                inside = touches(near_query, tile) & (near_query < rows) & present
                found = bins_of(
                    number_rows[source], chain_rows[source], numbers[near_tile], chains[near_tile]
                )
                found = jnp.where(inside, found, zero_bin)
            else:
                found = jnp.full(shape, zero_bin, jnp.int32)
            backward_ref[
                index * LANES : (index + 1) * LANES, step * LANES : (step + 1) * LANES
            ] = found
        target = (number_rows[source] + reach - lane) * 8 + chain_rows[source]
        target = jnp.where(present & (lane > 0) & (lane < 2 * reach), target, -9)
        offset = (LANES - (length - last_start)) if tile < 0 else (tile + 1) * LANES
        far = 4 * LANES
        shift = jnp.full(shape, far, jnp.int32)
        for distance in range(-NEAR, NEAR + 1):
            other = codes[offset - distance : offset - distance + LANES]
            shift = jnp.where(other == target, distance, shift)
        if tile < 0:
            base = jnp.zeros(shape, jnp.int32)
        else:
            base = jnp.where(row < LANES // 2, tile - 1, tile) * LANES
        places_ref[index * LANES : (index + 1) * LANES] = jnp.where(
            shift == far, far - 1, key_row - shift - base
        )


def attention_tables(layout, scale, numbers, marks, query_start, relative_table, pair_gain, pair_weight):
    crops = numbers.shape[0]
    bin_count, width = relative_table.shape
    heads = pair_weight.shape[1]
    pairs = jnp.stack([numbers, marks], axis=1)
    pairs = pad_to(pairs, 2, layout.wide, 0).reshape(crops, 2, layout.key_tiles, LANES)
    spots = (layout.query_tiles + 1) * LANES
    shapes = [
        ((layout.length, LANES), jnp.bfloat16),
        ((layout.block_rows, LANES), jnp.int32),
        ((layout.padded, 3 * LANES), jnp.int32),
        ((spots, 3 * LANES), jnp.int32),
        ((spots, LANES), jnp.int32),
        ((64, layout.length), jnp.bfloat16),
        ((64, layout.padded), jnp.int32),
    ]
    shared = [((heads // 2, 16, LANES), jnp.float32), ((LANES, width), jnp.bfloat16)]

    def whole(shape):
        return pl.BlockSpec(shape, lambda crop: (0,) * len(shape))

    return pl.pallas_call(
        functools.partial(tables_kernel, layout, bin_count, heads, scale),
        grid=(crops,),
        in_specs=[
            pl.BlockSpec(memory_space=pltpu.SMEM),
            pl.BlockSpec((None, 2, layout.key_tiles, LANES), lambda crop: (crop, 0, 0, 0)),
            whole((LANES, width)),
            whole((1, width)),
            whole((width, 16)),
        ],
        out_specs=tuple(
            [pl.BlockSpec((None, *shape), lambda crop: (crop, 0, 0)) for shape, _ in shapes]
            + [whole(shape) for shape, _ in shared]
        ),
        out_shape=tuple(
            [jax.ShapeDtypeStruct((crops, *shape), kind) for shape, kind in shapes]
            + [jax.ShapeDtypeStruct(shape, kind) for shape, kind in shared]
        ),
        scratch_shapes=[pltpu.VMEM((layout.padded + 2 * LANES, LANES), jnp.int32)],
        compiler_params=pltpu.CompilerParams(vmem_limit_bytes=VMEM_BYTES),
        cost_estimate=pl.CostEstimate(
            flops=40000000 * crops, bytes_accessed=4000000 * crops, transcendentals=0
        ),
        name="pair_tables",
    )(
        jnp.reshape(query_start, (1,)).astype(jnp.int32),
        pairs,
        pad_to(relative_table, 0, LANES, 0.0),
        pair_gain.reshape(1, -1),
        pad_to(pair_weight, 1, 16, 0.0),
    )


NT = (((1,), (1,)), ((), ()))
TN = (((0,), (0,)), ((), ()))


def wide_dot(former, latter, numbers=(((1,), (0,)), ((), ()))):
    return lax.dot_general(former, latter, numbers, preferred_element_type=jnp.float32)


def look_up(table_row, bins):
    table = jnp.broadcast_to(table_row, bins.shape)
    return jnp.take_along_axis(table, bins, axis=1, mode="promise_in_bounds")


def half_of(values, lane, side):
    return jnp.where((lane >= 64) == (side == 1), values, jnp.zeros_like(values))


def row_blocks(total, size):
    return [(start, min(start + size, total)) for start in range(0, total, size)]


def group_columns(kinds, tables, side):
    right = tables[8 * side + 1 : 8 * side + 2]
    left = tables[8 * side + 2 : 8 * side + 3]
    return jnp.where(kinds == RIGHT, right, jnp.where(kinds == LEFT, left, 0.0))


def forward_kernel(layout, scale, *refs):
    count = len(layout.pieces)
    normed_ref, weight_ref = refs[:2]
    key_refs = refs[2 : 2 + count]
    value_refs = refs[2 + count : 2 + 2 * count]
    members_ref, kinds_ref, bins_ref, tables_ref, query_ref, out_ref, log_ref = refs[2 + 2 * count :]
    pair = pl.program_id(1)
    rows, length = layout.block_rows, layout.length
    factor = scale * LOG2E
    lane = lax.broadcasted_iota(jnp.int32, (1, LANES), 1)
    query = wide_dot(normed_ref[...], weight_ref[...]).astype(jnp.bfloat16)
    query_ref[...] = query
    keys = jnp.concatenate([ref[...] for ref in key_refs], axis=0)
    values = jnp.concatenate([ref[...] for ref in value_refs], axis=0)
    members = members_ref[...]
    kinds = kinds_ref[...]
    tables = tables_ref[...]
    ones = jnp.ones((length, LANES), jnp.bfloat16)

    @pl.when(pair == 0)
    def _():
        log_ref[...] = jnp.zeros_like(log_ref)

    for side in range(2):
        key_columns = jnp.concatenate([half_of(keys, lane, side), members], axis=1)
        value_columns = jnp.concatenate([half_of(values, lane, side), ones], axis=1)
        extra = group_columns(kinds, tables, side).astype(jnp.bfloat16)
        query_columns = jnp.concatenate([query, extra], axis=1)
        table_row = tables[8 * side : 8 * side + 1]
        for start, stop in row_blocks(rows, 256):
            raw = wide_dot(query_columns[start:stop], key_columns, NT)
            strips = []
            for tile in range(start // LANES, -(-stop // LANES)):
                first, final = tile * LANES, min(tile * LANES + LANES, rows)
                strip = raw[first - start : final - start]
                segments, done = [], 0
                for slot in (1, 2, 0) if tile == 0 else (0, 1, 2):
                    other = tile + slot - 1
                    low, high = first, final
                    if slot == 0:
                        high = min(first + 32, final)
                    if slot == 2:
                        low = first + LANES - 32
                    if other >= layout.query_tiles or low >= high:
                        continue
                    place = layout.tile_start(other)
                    width = min(LANES, length - place)
                    bins = bins_ref[low:high, slot * LANES : (slot + 1) * LANES]
                    bias = look_up(table_row, bins)[:, :width]
                    piece = strip[:, place : place + width]
                    rows_of = [
                        piece[: low - first],
                        piece[low - first : high - first] + bias,
                        piece[high - first :],
                    ]
                    rows_of = [value for value in rows_of if value.shape[0]]
                    if done < place:
                        segments.append(strip[:, done:place])
                    segments.append(jnp.concatenate(rows_of, axis=0))
                    done = place + width
                if done < length:
                    segments.append(strip[:, done:])
                strips.append(jnp.concatenate(segments, axis=1))
            block = jnp.concatenate(strips, axis=0)
            top = jnp.max(block, axis=1, keepdims=True)
            weights = jnp.exp2((block - top) * factor).astype(jnp.bfloat16)
            sums = wide_dot(weights, value_columns)
            total = sums[:, LANES:]
            result = sums[:, :LANES] / total
            if side == 0:
                out_ref[start:stop] = result
            else:
                out_ref[start:stop] += result
            log_total = top + jnp.log(total) * (1.0 / scale)
            log_ref[start:stop] = jnp.where(
                lane == 2 * pair + side, log_total, log_ref[start:stop]
            )


def backward_kernel(layout, scale, first_pair, *refs):
    count = len(layout.pieces)
    query_ref, grad_ref, out_ref, log_ref = refs[:4]
    key_refs = refs[4 : 4 + count]
    value_refs = refs[4 + count : 4 + 2 * count]
    rest = refs[4 + 2 * count :]
    members_ref, kinds_ref, bins_ref, places_ref, tables_ref = rest[:5]
    members_turned_ref, kinds_turned_ref = rest[5:7]
    grad_query_ref = rest[7]
    grad_pair_refs = rest[8 : 8 + count]
    grad_table_ref = rest[8 + count]
    query_wide, grad_wide, query_turned, grad_turned = rest[9 + count :]
    pair = pl.program_id(1) + first_pair
    rows, length, padded = layout.block_rows, layout.length, layout.padded
    factor = scale * LOG2E
    lane = lax.broadcasted_iota(jnp.int32, (1, LANES), 1)
    keys = jnp.concatenate([ref[...] for ref in key_refs], axis=0)
    values = jnp.concatenate([ref[...] for ref in value_refs], axis=0)
    members = members_ref[...]
    kinds = kinds_ref[...]
    tables = tables_ref[...]
    query = query_ref[...]
    grad = grad_ref[...]
    grad_full = grad.astype(jnp.float32)
    product = grad_full * out_ref[...]
    log_all = log_ref[...]
    tail = 2 * layout.groups
    ones = jnp.broadcast_to(jnp.where(lane < 3, 1.0, 0.0), (length, LANES)).astype(jnp.bfloat16)

    def three_parts(values):
        upper = values.astype(jnp.bfloat16).astype(jnp.float32)
        values = values - upper
        middle = values.astype(jnp.bfloat16).astype(jnp.float32)
        return upper, middle, values - middle

    def in_lanes(parts, first):
        return jnp.where(
            lane == first,
            parts[0],
            jnp.where(lane == first + 1, parts[1], jnp.where(lane == first + 2, parts[2], 0.0)),
        )

    if padded > rows:
        for ref in (query_wide, grad_wide):
            for side in range(2):
                ref[side, rows:padded] = jnp.zeros((padded - rows, ref.shape[2]), jnp.bfloat16)
        for ref in (query_turned, grad_turned):
            ref[:, rows:padded] = jnp.zeros((LANES, padded - rows), jnp.bfloat16)
    query_turned[:, 0:rows] = query.T
    grad_turned[:, 0:rows] = grad.T
    for side in range(2):
        log_total = jnp.sum(
            jnp.where(lane == 2 * pair + side, log_all, 0.0), axis=1, keepdims=True
        )
        extra = group_columns(kinds, tables, side) + in_lanes(three_parts(log_total), tail)
        query_wide[side, 0:rows, 0:LANES] = query
        query_wide[side, 0:rows, LANES:] = extra.astype(jnp.bfloat16)
        delta = jnp.sum(half_of(product, lane, side), axis=1, keepdims=True)
        grad_wide[side, 0:rows, 0:LANES] = grad
        grad_wide[side, 0:rows, LANES:] = in_lanes(three_parts(-delta), 0).astype(jnp.bfloat16)

    key_columns = [
        jnp.concatenate([half_of(keys, lane, side), members], axis=1) for side in range(2)
    ]
    value_columns = [
        jnp.concatenate([half_of(values, lane, side), ones], axis=1) for side in range(2)
    ]
    inner_sums = [jnp.zeros((1, LANES), jnp.float32) for _ in range(2)]
    low_sums = [jnp.zeros((1, LANES), jnp.float32) for _ in range(2)]
    high_sums = [jnp.zeros((1, LANES), jnp.float32) for _ in range(2)]
    reach_tiles = list(range(layout.query_tiles)) + [-1]

    def put(which, start, stop, result):
        begin = 0
        for ref, size in zip(grad_pair_refs, layout.pieces):
            low, high = max(start, begin), min(stop, begin + size)
            if low < high:
                ref[which, low - begin : high - begin] = result[low - start : high - start]
            begin += size

    probs_parts, slope_parts = [[], []], [[], []]
    for start, stop in row_blocks(length, 384):
        near = {}
        for index, tile in enumerate(reach_tiles):
            place = layout.tile_start(tile)
            if start <= place < stop:
                near[place] = (index, tile, min(place + LANES, length))
        for side in range(2):
            table_row = tables[8 * side : 8 * side + 1]
            raw = wide_dot(key_columns[side][start:stop], query_wide[side], NT)
            strips = []
            for place in range(start, stop, LANES):
                strip = raw[place - start : min(place + LANES, stop) - start]
                if place in near:
                    index, tile, final = near[place]
                    columns = []
                    for other in range(layout.query_tiles):
                        piece = strip[:, other * LANES : (other + 1) * LANES]
                        slot = other - tile + 1
                        if 0 <= slot < 3:
                            bins = bins_ref[
                                index * LANES : index * LANES + final - place,
                                slot * LANES : (slot + 1) * LANES,
                            ]
                            piece = piece + look_up(table_row, bins)
                        columns.append(piece)
                    strip = jnp.concatenate(columns, axis=1)
                strips.append(strip)
            probs = jnp.exp2(jnp.concatenate(strips, axis=0) * factor)
            grad_probs = wide_dot(value_columns[side][start:stop], grad_wide[side], NT)
            slope = probs * grad_probs
            probs_parts[side].append(probs.astype(jnp.bfloat16))
            slope_parts[side].append(slope.astype(jnp.bfloat16))
            for place, (index, tile, final) in near.items():

                def cut_of(low, high, other, place=place, slope=slope):
                    return slope[
                        place - start + low : place - start + high,
                        other * LANES : (other + 1) * LANES,
                    ]

                for slot in range(3):
                    other = tile + slot - 1
                    if not 0 <= other < layout.query_tiles:
                        continue
                    bins = bins_ref[
                        index * LANES : index * LANES + final - place,
                        slot * LANES : (slot + 1) * LANES,
                    ]
                    cut = cut_of(0, final - place, other)
                    low_sums[side] += jnp.sum(jnp.where(bins == 0, cut, 0.0), axis=0, keepdims=True)
                    high_sums[side] += jnp.sum(
                        jnp.where(bins == 2 * (NEAR + 1), cut, 0.0), axis=0, keepdims=True
                    )
                for half in range(2):
                    base = 0 if tile < 0 else tile - 1 + half
                    for step in range(2):
                        other = base + step
                        if not 0 <= other < layout.query_tiles or (tile < 0 and step):
                            continue
                        begin, end = half * 64, half * 64 + 64
                        if tile >= 0 and other == tile - 1:
                            end = begin + 32
                        if tile >= 0 and other == tile + 1:
                            begin = end - 32
                        end = min(end, final - place)
                        if begin >= end:
                            continue
                        where = places_ref[index * LANES + begin : index * LANES + end]
                        picked = jnp.take_along_axis(
                            cut_of(begin, end, other),
                            where & (LANES - 1),
                            axis=1,
                            mode="promise_in_bounds",
                        )
                        picked = jnp.where((where >> 7) == step, picked, 0.0)
                        inner_sums[side] += jnp.sum(picked, axis=0, keepdims=True)

    probs_low = [jnp.concatenate(parts, axis=0) for parts in probs_parts]
    slopes_low = [jnp.concatenate(parts, axis=0) for parts in slope_parts]
    keys_turned = keys.T
    grad_keys, grad_values, grad_queries = [], [], []
    kinds_turned = kinds_turned_ref[...]
    for side in range(2):
        cut = slice(64 * side, 64 * side + 64)
        grad_values.append(wide_dot(grad_turned[cut], probs_low[side], NT))
        grad_keys.append(wide_dot(query_turned[cut], slopes_low[side], NT))
        left = jnp.concatenate([keys_turned[cut], members_turned_ref[...]], axis=0)
        both = wide_dot(left, slopes_low[side])
        grad_queries.append(both[:64])
        sums = both[64:]

        def total(kind):
            return jnp.sum(jnp.where(kinds_turned == kind, sums, 0.0))

        right = total(RIGHT) + jnp.sum(high_sums[side])
        left = total(LEFT) + jnp.sum(low_sums[side])
        apart = total(APART)
        grad_table_ref[side : side + 1] = jnp.where(
            lane == 0,
            left,
            jnp.where(
                lane == 2 * (NEAR + 1),
                right,
                jnp.where(lane == 2 * (NEAR + 1) + 1, apart, inner_sums[side]),
            ),
        )
    put(0, 0, length, (jnp.concatenate(grad_keys, axis=0) * scale).T.astype(jnp.bfloat16))
    put(1, 0, length, jnp.concatenate(grad_values, axis=0).T.astype(jnp.bfloat16))
    turned = jnp.concatenate(grad_queries, axis=0) * scale
    grad_query_ref[...] = turned.T[0:rows].astype(jnp.bfloat16)


def tile_columns(rows, offset=0):
    return pl.BlockSpec((None, rows, LANES), lambda crop, pair: (crop, 0, pair + offset))


def per_crop(rows, width):
    return pl.BlockSpec((None, rows, width), lambda crop, pair: (crop, 0, 0))


def kernel_params():
    return pltpu.CompilerParams(
        vmem_limit_bytes=VMEM_BYTES, dimension_semantics=("arbitrary", "arbitrary")
    )


def attention_forward(layout, scale, normed, weight, key_values, members, kinds, bins, tables):
    crops, rows, width = normed.shape
    pairs = tables.shape[0]
    specs = [per_crop(rows, width), pl.BlockSpec((width, LANES), lambda crop, pair: (0, pair))]
    operands = [normed, weight]
    for place in (1, 2):
        for piece in key_values:
            specs.append(tile_columns(piece[0].shape[1], piece[place]))
            operands.append(piece[0])
    specs += [
        per_crop(layout.length, LANES),
        per_crop(rows, LANES),
        per_crop(layout.padded, 3 * LANES),
        pl.BlockSpec((None, 16, LANES), lambda crop, pair: (pair, 0, 0)),
    ]
    flops = 2 * crops * pairs * 2 * rows * layout.length * 256 * 2
    return pl.pallas_call(
        functools.partial(forward_kernel, layout, scale),
        grid=(crops, pairs),
        in_specs=specs,
        out_specs=(tile_columns(rows), tile_columns(rows), per_crop(rows, LANES)),
        out_shape=(
            jax.ShapeDtypeStruct((crops, rows, pairs * LANES), jnp.bfloat16),
            jax.ShapeDtypeStruct((crops, rows, pairs * LANES), jnp.float32),
            jax.ShapeDtypeStruct((crops, rows, LANES), jnp.float32),
        ),
        compiler_params=kernel_params(),
        cost_estimate=pl.CostEstimate(
            flops=flops,
            bytes_accessed=12 * crops * rows * pairs * LANES,
            transcendentals=crops * pairs * 2 * rows * layout.length,
        ),
        name="attention_forward",
    )(*operands, members, kinds, bins, tables)


def attention_backward(
    layout,
    scale,
    first_pair,
    pairs,
    projected,
    grad_out,
    attended,
    logs,
    key_values,
    members,
    kinds,
    bins,
    places,
    members_turned,
    kinds_turned,
    tables,
):
    crops, rows, _ = projected.shape
    specs = [tile_columns(rows, first_pair)] * 3 + [per_crop(rows, LANES)]
    operands = [projected, grad_out, attended, logs]
    for place in (1, 2):
        for piece in key_values:
            specs.append(tile_columns(piece[0].shape[1], piece[place] + first_pair))
            operands.append(piece[0])
    specs += [
        per_crop(layout.length, LANES),
        per_crop(rows, LANES),
        per_crop(bins.shape[1], 3 * LANES),
        per_crop(places.shape[1], LANES),
        pl.BlockSpec((None, 16, LANES), lambda crop, pair: (pair + first_pair, 0, 0)),
        per_crop(64, layout.length),
        per_crop(64, layout.padded),
    ]
    out_specs = [tile_columns(rows)]
    out_shapes = [jax.ShapeDtypeStruct((crops, rows, pairs * LANES), jnp.bfloat16)]
    for piece in key_values:
        size = piece[0].shape[1]
        out_specs.append(
            pl.BlockSpec((None, 2, size, LANES), lambda crop, pair: (crop, 0, 0, pair))
        )
        out_shapes.append(jax.ShapeDtypeStruct((crops, 2, size, pairs * LANES), jnp.bfloat16))
    out_specs.append(pl.BlockSpec((None, None, 8, LANES), lambda crop, pair: (crop, pair, 0, 0)))
    out_shapes.append(jax.ShapeDtypeStruct((crops, pairs, 8, LANES), jnp.float32))
    padded = layout.padded
    return pl.pallas_call(
        functools.partial(backward_kernel, layout, scale, first_pair),
        grid=(crops, pairs),
        in_specs=specs,
        out_specs=tuple(out_specs),
        out_shape=tuple(out_shapes),
        scratch_shapes=[
            pltpu.VMEM((2, padded, 2 * LANES), jnp.bfloat16),
            pltpu.VMEM((2, padded, 2 * LANES), jnp.bfloat16),
            pltpu.VMEM((LANES, padded), jnp.bfloat16),
            pltpu.VMEM((LANES, padded), jnp.bfloat16),
        ],
        compiler_params=kernel_params(),
        cost_estimate=pl.CostEstimate(
            flops=2 * crops * pairs * 2 * rows * layout.length * 256 * 5,
            bytes_accessed=20 * crops * rows * pairs * LANES,
            transcendentals=crops * pairs * 2 * rows * layout.length,
        ),
        name="attention_backward",
    )(*operands, members, kinds, bins, places, tables, members_turned, kinds_turned)


def sigmoid(values):
    return 0.5 * jnp.tanh(0.5 * values) + 0.5


def each_strip(rows, body, size=16):
    count = rows // size
    group = max(number for number in range(1, 9) if count % number == 0)

    @pl.loop(0, count // group)
    def _(index):
        for part in range(group):
            body(pl.ds(pl.multiple_of((index * group + part) * size, size), size))


def fold_rows(values):
    return jnp.sum(values.reshape(values.shape[0] // 8, 8, values.shape[1]), axis=0)


def feed_kernel(split, chunks, here_ref, *refs):
    (attended_ref, tokens_ref, upstream_ref, normed_a_ref, mod_ref, gate_weight_ref, output_ref) = refs[:7]
    gate_ref, up_ref, down_ref = refs[7:10]
    layer_ref, grad_middle_ref, grad_att_ref, grad_pre_ref, sums_ref = refs[10:15]
    grads = refs[15:-10]
    gated, grad_ff, normed, branch, middle, total, grad_normed, grad_branch = refs[-10:-2]
    gate_pre, turned = refs[-2:]
    step = pl.program_id(0)
    here = here_ref[0]
    rows, width = tokens_ref.shape
    size = gate_ref.shape[1]
    strip = 112 if rows % 112 == 0 else 64
    strips = rows // strip
    shift_f, scale_f = mod_ref[3:4], mod_ref[4:5]
    open_a, open_f = sigmoid(mod_ref[2:3]), sigmoid(mod_ref[5:6])

    def strip_of(index):
        return pl.ds(pl.multiple_of(index * strip, strip), strip)

    def norm_of(values):
        mean_value = jnp.mean(values, axis=1, keepdims=True)
        centred = values - mean_value
        spread = jnp.mean(centred * centred, axis=1, keepdims=True)
        root = lax.rsqrt(spread + 1e-06)
        return centred * root, root

    @pl.when(step == 0)
    def _():
        gate_pre[...] = wide_dot(normed_a_ref[...], gate_weight_ref[...])

        @pl.loop(0, strips)
        def _(index):
            cut = strip_of(index)
            gated[cut] = (attended_ref[cut] * sigmoid(gate_pre[cut])).astype(jnp.bfloat16)
            grad_ff[cut] = (upstream_ref[cut].astype(jnp.float32) * open_f).astype(jnp.bfloat16)

        branch[...] = wide_dot(gated[...], output_ref[...])

        @pl.loop(0, strips)
        def _(index):
            cut = strip_of(index)
            values = tokens_ref[cut].astype(jnp.float32) + open_a * branch[cut]
            middle[cut] = values
            normed[cut] = (norm_of(values)[0] * (1.0 + scale_f) + shift_f).astype(jnp.bfloat16)
            total[cut] = jnp.zeros((strip, width), jnp.float32)
            grad_normed[cut] = jnp.zeros((strip, width), jnp.float32)

        turned[...] = normed[...].T

    block = rows if rows <= 384 else rows // 2
    parts, gate_parts, up_parts = [], [], []
    for start in range(0, rows, block):
        cut = slice(start, start + block)
        before = wide_dot(normed[cut], gate_ref[...])
        lifted = wide_dot(normed[cut], up_ref[...])
        grad_hidden = wide_dot(grad_ff[cut], down_ref[...], NT)
        switch = sigmoid(before)
        silu = before * switch
        part = (silu * lifted).astype(jnp.bfloat16)
        grad_up = (grad_hidden * silu).astype(jnp.bfloat16)
        grad_gate = (grad_hidden * lifted * (switch + silu * (1.0 - switch))).astype(jnp.bfloat16)
        parts.append(part)
        gate_parts.append(grad_gate)
        up_parts.append(grad_up)
        total[cut] += wide_dot(part, down_ref[...])
        grad_normed[cut] += wide_dot(grad_gate, gate_ref[...], NT) + wide_dot(
            grad_up, up_ref[...], NT
        )
    hidden = jnp.concatenate(parts, axis=0)
    both = jnp.concatenate(
        [jnp.concatenate(gate_parts, axis=0), jnp.concatenate(up_parts, axis=0)], axis=1
    )
    pair = wide_dot(turned[...], both).astype(jnp.bfloat16)
    if split:
        gate_send, gate_keep, up_send, up_keep, down_send, down_keep, small_send, small_keep = grads
        half = width // 2
        away = pl.ds(pl.multiple_of((1 - here) * half, LANES), half)
        home = pl.ds(pl.multiple_of(here * half, LANES), half)
        down_send[...] = wide_dot(hidden, grad_ff[:, away], TN).astype(jnp.bfloat16)
        down_keep[...] = wide_dot(hidden, grad_ff[:, home], TN).astype(jnp.bfloat16)

        @pl.when(step < chunks // 2)
        def _():
            gate_send[...] = pair[:, :size]
            up_send[...] = pair[:, size:]

        @pl.when(step >= chunks // 2)
        def _():
            gate_keep[...] = pair[:, :size]
            up_keep[...] = pair[:, size:]
    else:
        gate_all, up_all, down_all, small_all = grads
        gate_all[...] = pair[:, :size]
        up_all[...] = pair[:, size:]
        down_all[...] = wide_dot(hidden, grad_ff[...], TN).astype(jnp.bfloat16)

    @pl.when(step == chunks - 1)
    def _():
        def finish(index, sums):
            gate_f_sum, shift_sum, scale_sum, gate_a_sum = sums
            cut = strip_of(index)
            values = middle[cut]
            fed = total[cut]
            upstream = upstream_ref[cut].astype(jnp.float32)
            layer_ref[cut] = (values + open_f * fed).astype(jnp.bfloat16)
            normal, root = norm_of(values)
            grad = grad_normed[cut]
            scaled = grad * (1.0 + scale_f)
            grad_middle = upstream + root * (
                scaled
                - jnp.mean(scaled, axis=1, keepdims=True)
                - normal * jnp.mean(scaled * normal, axis=1, keepdims=True)
            )
            grad_middle_ref[cut] = grad_middle
            grad_branch[cut] = (grad_middle * open_a).astype(jnp.bfloat16)
            return (
                gate_f_sum + fold_rows(upstream * fed),
                shift_sum + fold_rows(grad),
                scale_sum + fold_rows(grad * normal),
                gate_a_sum + fold_rows(grad_middle * branch[cut]),
            )

        zero = jnp.zeros((8, width), jnp.float32)
        sums = lax.fori_loop(0, strips, finish, (zero, zero, zero, zero))
        gate_f_sum, shift_sum, scale_sum, gate_a_sum = [
            jnp.sum(value, axis=0, keepdims=True) for value in sums
        ]
        none = jnp.zeros((1, width), jnp.float32)
        sums_ref[...] = jnp.concatenate(
            [
                none,
                none,
                gate_a_sum * open_a * (1.0 - open_a),
                shift_sum,
                scale_sum,
                gate_f_sum * open_f * (1.0 - open_f),
                none,
                none,
            ],
            axis=0,
        )
        total[...] = wide_dot(grad_branch[...], output_ref[...], NT)

        @pl.loop(0, strips)
        def _(index):
            cut = strip_of(index)
            grad_gated = total[cut]
            opened = sigmoid(gate_pre[cut])
            grad_att_ref[cut] = (grad_gated * opened).astype(jnp.bfloat16)
            grad_pre_ref[cut] = (
                grad_gated * attended_ref[cut] * (opened * (1.0 - opened))
            ).astype(jnp.bfloat16)

        if split:
            for side, ref in ((away, small_send), (home, small_keep)):
                ref[:, :half] = wide_dot(gated[...], grad_branch[:, side], TN).astype(jnp.bfloat16)
                ref[:, half:] = wide_dot(normed_a_ref[...], grad_pre_ref[:, side], TN).astype(
                    jnp.bfloat16
                )
        else:
            small_all[:, :width] = wide_dot(gated[...], grad_branch[...], TN).astype(jnp.bfloat16)
            small_all[:, width:] = wide_dot(normed_a_ref[...], grad_pre_ref[...], TN).astype(
                jnp.bfloat16
            )


def feed_layer(
    split, here, attended, tokens, upstream, normed_a, mod_rows, gate_weight, output_weight, feed_gate, feed_up, feed_down
):
    rows, width = tokens.shape
    inner = feed_gate.shape[1]
    size = 512
    chunks = inner // size
    half = chunks // 2

    def turn(step, here_ref):
        return (step + half * (1 - here_ref[0])) % chunks if split else step

    def fixed(shape):
        return pl.BlockSpec(shape, lambda step, here_ref: (0, 0), pipeline_mode=pl.Buffered(1))

    def columns(step, here_ref):
        return (0, turn(step, here_ref))

    def strips(step, here_ref):
        return (turn(step, here_ref), 0)

    whole = (rows, width)
    in_specs = [fixed(whole)] * 4 + [
        fixed((8, width)),
        fixed((width, width)),
        fixed((width, width)),
        pl.BlockSpec((width, size), columns),
        pl.BlockSpec((width, size), columns),
        pl.BlockSpec((size, width), strips),
    ]
    out_specs = [fixed(whole)] * 4 + [fixed((8, width))]
    bf16, f32 = jnp.bfloat16, jnp.float32
    out_shapes = [(whole, bf16), (whole, f32), (whole, bf16), (whole, bf16), ((8, width), f32)]
    if split:
        first = pl.BlockSpec((width, size), lambda step, here_ref: (0, jnp.minimum(step, half - 1)))
        second = pl.BlockSpec((width, size), lambda step, here_ref: (0, jnp.maximum(step - half, 0)))
        out_specs += [first, second, first, second]
        out_shapes += [((width, inner // 2), bf16)] * 4
        out_specs += [pl.BlockSpec((size, width // 2), strips)] * 2
        out_shapes += [((inner, width // 2), bf16)] * 2
        out_specs += [fixed((width, width))] * 2
        out_shapes += [((width, width), bf16)] * 2
    else:
        out_specs += [pl.BlockSpec((width, size), columns)] * 2
        out_shapes += [((width, inner), bf16)] * 2
        out_specs += [pl.BlockSpec((size, width), strips), fixed((width, 2 * width))]
        out_shapes += [((inner, width), bf16), ((width, 2 * width), bf16)]
    return pl.pallas_call(
        functools.partial(feed_kernel, split, chunks),
        grid_spec=pltpu.PrefetchScalarGridSpec(
            num_scalar_prefetch=1,
            grid=(chunks,),
            in_specs=in_specs,
            out_specs=tuple(out_specs),
            scratch_shapes=[
                pltpu.VMEM(whole, bf16),
                pltpu.VMEM(whole, bf16),
                pltpu.VMEM(whole, bf16),
                pltpu.VMEM(whole, f32),
                pltpu.VMEM(whole, f32),
                pltpu.VMEM(whole, f32),
                pltpu.VMEM(whole, f32),
                pltpu.VMEM(whole, bf16),
                pltpu.VMEM(whole, f32),
                pltpu.VMEM((width, rows), bf16),
            ],
        ),
        out_shape=tuple(jax.ShapeDtypeStruct(shape, kind) for shape, kind in out_shapes),
        compiler_params=pltpu.CompilerParams(vmem_limit_bytes=VMEM_BYTES),
        cost_estimate=pl.CostEstimate(
            flops=2 * rows * width * (9 * inner + 5 * width),
            bytes_accessed=12 * width * inner + 24 * rows * width,
            transcendentals=2 * rows * inner,
        ),
        name="feed_layer",
    )(
        jnp.reshape(here, (1,)).astype(jnp.int32),
        attended,
        tokens,
        upstream,
        normed_a,
        mod_rows,
        gate_weight,
        output_weight,
        feed_gate,
        feed_up,
        feed_down,
    )


MASKS = {"u": 8, "v": 4, "y": 2, "x": 1}


def exchange(values, mask):
    return lax.ppermute(values, "crop", [(i, i ^ mask) for i in range(16)])


def swap_res(values):
    return lax.ppermute(values, "res", [(0, 1), (1, 0)])


def tie(*values):
    return lax.optimization_barrier(values)


def add_low(former, latter, kind=jnp.bfloat16):
    return (former.astype(jnp.float32) + latter.astype(jnp.float32)).astype(kind)


def stage_kernel(plans, bits_ref, *refs):
    inputs = refs[: sum(plan["count"] for plan in plans)]
    outputs = list(refs[len(inputs) :])
    for plan in plans:
        mine, inputs = inputs[: plan["count"]], inputs[plan["count"] :]
        out_ref = None if plan["apart"] else outputs[0]
        if not plan["apart"] and plan["merge"] is None:
            outputs.pop(0)
        for column, width, own in plan["parts"]:
            result = outputs.pop(0) if plan["apart"] else out_ref
            target = 0 if plan["apart"] else column
            lead_sizes = () if plan["merge"] is not None else result.shape[:-2]
            for lead in itertools.product(*[range(size) for size in lead_sizes]):
                for first in range(0, plan["rows"], 16):
                    cut = (*lead, slice(first, first + 16))
                    across = slice(column, column + width)
                    total = None
                    for index in own:
                        value = mine[index][(*cut, slice(0, width))].astype(jnp.float32)
                        total = value if total is None else total + value
                    for index in plan["spans"]:
                        total = total + mine[index][(*cut, across)].astype(jnp.float32)
                    fold, local = first // plan["block"], first % plan["block"]
                    if plan["folds"]:
                        value = mine[plan["folds"][fold]][local : local + 16, across]
                        total = total + value.astype(jnp.float32)
                    if plan["merge"] is None:
                        result[(*cut, slice(target, target + width))] = total.astype(result.dtype)
                    else:
                        begin = plan["merge"] + fold * plan["wide"] + column
                        result[local : local + 16, begin : begin + width] = total.astype(result.dtype)


class Halving:
    def __init__(self, streams, orders):
        self.streams = streams
        self.orders = [list(order) for order in orders]
        self.past = [[] for _ in orders]
        self.came = [[] for _ in orders]

    def stage(self, last=False, merge=False, merged=None):
        index = lax.axis_index("crop")
        bits = scalars(*[(index // mask) % 2 for mask in MASKS.values()])
        self.masks, plans, specs, operands, out_specs, out_shapes = [], [], [], [], [], []
        left = 0 if last else len(self.orders[0]) - 1
        fewest = min(parts[0][0][0].shape[0] for parts in self.streams) // 16
        begin = 0
        steps = {3: 4, 2: 2}.get(left, 1)
        for stream, (parts, order, past) in enumerate(zip(self.streams, self.orders, self.past)):
            now = None if last else order.pop(0)
            rest = [axis for axis in MASKS if axis in order]

            def spec_of(axes, rows, width, block, now=now, rest=rest):
                def index_map(step, bits_ref):
                    places = []
                    for axis in axes:
                        bit = bits_ref[list(MASKS).index(axis)]
                        if axis == now:
                            places.append(1 - bit)
                        elif axis not in rest:
                            places.append(bit)
                        elif axis == rest[0] and steps > 1:
                            places.append(step // (steps // 2))
                        elif len(rest) > 1 and axis == rest[1] and steps > 2:
                            places.append(step % 2)
                        else:
                            places.append(0)
                    return (*places, 0, block)

                sizes = [
                    2
                    if axis in rest
                    and not (axis == rest[0] and steps > 1)
                    and not (len(rest) > 1 and axis == rest[1] and steps > 2)
                    else None
                    for axis in axes
                ]
                return pl.BlockSpec((*sizes, rows, width), index_map)

            column = 0
            rows = parts[0][0][0].shape[0] // 16
            wide = sum(width for _, _, width in parts)
            plan = {
                "parts": [],
                "spans": [],
                "folds": [],
                "count": 0,
                "apart": last,
                "rows": rows,
                "block": fewest,
                "wide": wide,
                "merge": begin if merge else None,
            }
            for arrays, block, width in parts:
                own = []
                for value in arrays:
                    operands.append(value.reshape(2, 2, 2, 2, rows, value.shape[1]))
                    specs.append(spec_of(list(MASKS), rows, width, block))
                    own.append(plan["count"])
                    plan["count"] += 1
                plan["parts"].append((column, width, own))
                column += width
            for axes, value in self.came[stream]:
                operands.append(value.reshape(*[2] * len(axes), rows, column))
                specs.append(spec_of(axes, rows, column, 0))
                plan["spans"].append(plan["count"])
                plan["count"] += 1
            if merged is not None:
                for fold in range(rows // fewest):
                    place = (begin + fold * wide) // wide
                    operands.append(merged)
                    specs.append(
                        pl.BlockSpec((fewest, wide), lambda step, bits_ref, place=place: (0, place))
                    )
                    plan["folds"].append(plan["count"])
                    plan["count"] += 1
            begin += wide * (rows // fewest)
            plans.append(plan)
            if last:
                for _, width, _ in plan["parts"]:
                    out_specs.append(pl.BlockSpec((rows, width), lambda step, bits_ref: (0, 0)))
                    out_shapes.append(jax.ShapeDtypeStruct((rows, width), jnp.float32))
            else:
                past.append(now)
                self.masks.append(MASKS[now])
                if not merge:
                    out_specs.append(spec_of(rest, rows, column, 0))
                    out_shapes.append(
                        jax.ShapeDtypeStruct((*[2] * len(rest), rows, column), jnp.bfloat16)
                    )
        if merge:
            out_specs.append(pl.BlockSpec((fewest, begin), lambda step, bits_ref: (0, 0)))
            out_shapes.append(jax.ShapeDtypeStruct((fewest, begin), jnp.bfloat16))
        self.axes = [[axis for axis in MASKS if axis in order] for order in self.orders]
        results = pl.pallas_call(
            functools.partial(stage_kernel, plans),
            grid_spec=pltpu.PrefetchScalarGridSpec(
                num_scalar_prefetch=1, grid=(steps,), in_specs=specs, out_specs=tuple(out_specs)
            ),
            out_shape=tuple(out_shapes),
            compiler_params=pltpu.CompilerParams(vmem_limit_bytes=VMEM_BYTES),
            cost_estimate=pl.CostEstimate(
                flops=sum(4 * math.prod(shape.shape) for shape in out_shapes),
                bytes_accessed=sum(8 * math.prod(shape.shape) for shape in out_shapes),
                transcendentals=0,
            ),
            name="halving_stage",
        )(bits, *operands)
        if merge or last:
            return list(results)
        return [value.reshape(-1, value.shape[-1]) for value in results]

    def send(self, values):
        return [exchange(value, mask) for value, mask in zip(values, self.masks)]

    def take(self, values):
        for came, axes, value in zip(self.came, self.axes, values):
            came.append((axes, value))


def share_columns(values, parts):
    if parts == 1:
        return values.astype(jnp.bfloat16)
    return lax.psum_scatter(values.astype(jnp.bfloat16), "res", scatter_dimension=1, tiled=True)


def scatter_crops(values):
    return lax.psum_scatter(values, "crop", scatter_dimension=0, tiled=True).astype(jnp.float32)


def gather_crops(values, crop_parts):
    if crop_parts != 16:
        return lax.all_gather(values, "crop", axis=0, tiled=True)
    index = lax.axis_index("crop")
    for mask in (1, 2, 4, 8):
        other = exchange(values, mask)
        low = (index // mask) % 2 == 0
        values = jnp.concatenate(
            [jnp.where(low, values, other), jnp.where(low, other, values)], axis=0
        )
    return values


def sum_res(values, parts):
    if parts == 1:
        return values
    if parts != 2:
        return lax.psum(values, "res")
    return values + swap_res(values)


PACK = 1152
SIDE = 384


def whole_vmem(count):
    return [pl.BlockSpec(memory_space=pltpu.VMEM)] * count


def scalars(*values):
    return jnp.stack([jnp.asarray(value, jnp.int32) for value in values])


def local_call(kernel, numbers, operands, shapes, name, flops=0):
    return pl.pallas_call(
        kernel,
        in_specs=[pl.BlockSpec(memory_space=pltpu.SMEM)] + whole_vmem(len(operands)),
        out_specs=tuple(whole_vmem(len(shapes))),
        out_shape=tuple(jax.ShapeDtypeStruct(shape, kind) for shape, kind in shapes),
        compiler_params=pltpu.CompilerParams(vmem_limit_bytes=VMEM_BYTES),
        cost_estimate=pl.CostEstimate(
            flops=flops,
            bytes_accessed=sum(value.size * value.dtype.itemsize for value in operands)
            + sum(4 * math.prod(shape) for shape, _ in shapes),
            transcendentals=0,
        ),
        name=name,
    )(numbers, *operands)


def projection_kernel(counts, here_ref, normed_ref, *refs):
    calls = len(counts)
    parts, (joined_ref, send_ref, keep_ref) = refs[: 3 * calls], refs[3 * calls :]
    width = joined_ref.shape[1] // 3
    column = 0
    for call, pairs in enumerate(counts):
        size = pairs * LANES
        query_ref, own_ref, came_ref = parts[3 * call : 3 * call + 3]
        joined_ref[:, column : column + size] = query_ref[...]
        for start in range(0, joined_ref.shape[0], 16):
            cut = slice(start, start + 16)
            for which in range(2):
                first = (1 + which) * width + column
                joined_ref[cut, first : first + size] = add_low(
                    own_ref[which, cut], came_ref[which, cut]
                )
        column += size
    half = send_ref.shape[1]
    for side, ref in ((1 - here_ref[0], send_ref), (here_ref[0], keep_ref)):
        columns = pl.ds(pl.multiple_of(side * half, LANES), half)
        ref[...] = wide_dot(normed_ref[...], joined_ref[:, columns], TN).astype(jnp.bfloat16)


def projection_gradient(here, normed_a, calls):
    rows, width = normed_a.shape
    counts = [call[0].shape[-1] // LANES for call in calls]
    return local_call(
        functools.partial(projection_kernel, counts),
        scalars(here),
        [normed_a] + [value for call in calls for value in call],
        [
            ((rows, 3 * width), jnp.bfloat16),
            ((width, 3 * width // 2), jnp.bfloat16),
            ((width, 3 * width // 2), jnp.bfloat16),
        ],
        "projection_gradient",
        6 * rows * width * width,
    )


def finish_kernel(counts, joined_ref, weight_ref, pre_ref, gate_ref, tokens_ref, middle_ref, mod_ref, *refs):
    feed_sums_ref, extra_ref = refs[:2]
    table_refs = refs[2 : 2 + len(counts)]
    out_ref, pack_ref, total, folded = refs[2 + len(counts) :]
    step = pl.program_id(0)
    rows, width = tokens_ref.shape
    part = wide_dot(joined_ref[...], weight_ref[...], NT)

    @pl.when(step == 0)
    def _():
        total[...] = part + wide_dot(pre_ref[...], gate_ref[...], NT)

    @pl.when(step > 0)
    def _():
        total[...] += part

    @pl.when(step == pl.num_programs(0) - 1)
    def _():
        scale = mod_ref[1:2]
        folded[...] = jnp.zeros_like(folded)

        def finish(cut):
            values = tokens_ref[cut].astype(jnp.float32)
            centred = values - jnp.mean(values, axis=1, keepdims=True)
            root = lax.rsqrt(jnp.mean(centred * centred, axis=1, keepdims=True) + 1e-06)
            normal = centred * root
            grad = total[cut]
            folded[0] += fold_rows(grad)
            folded[1] += fold_rows(grad * normal)
            scaled = grad * (1.0 + scale)
            out_ref[cut] = (
                middle_ref[cut]
                + root
                * (
                    scaled
                    - jnp.mean(scaled, axis=1, keepdims=True)
                    - normal * jnp.mean(scaled * normal, axis=1, keepdims=True)
                )
            ).astype(jnp.bfloat16)

        each_strip(rows, finish)
        shift_sum, scale_sum = folded[0], folded[1]
        heads = []
        for ref, pairs in zip(table_refs, counts):
            for pair in range(pairs):
                heads += [ref[pair, 0:1], ref[pair, 1:2]]

        def upper_of(values):
            return values.astype(jnp.bfloat16).astype(jnp.float32)

        rests = [head - upper_of(head) for head in heads]
        count = width // LANES
        left = [
            jnp.sum(shift_sum, axis=0, keepdims=True),
            jnp.sum(scale_sum, axis=0, keepdims=True),
            feed_sums_ref[2:6],
        ]
        left += [
            jnp.concatenate(rests[i : i + count], axis=1) for i in range(0, len(heads), count)
        ]
        right = [jnp.concatenate(heads[3 * i : 3 * i + 3], axis=1) for i in range(4)]
        line = extra_ref[5:6]
        right += [extra_ref[4:5], line, line - upper_of(line), extra_ref[7:8]]
        pack = jnp.concatenate(
            [jnp.concatenate(left, axis=0), jnp.concatenate(right, axis=0)], axis=1
        )
        pack_ref[...] = jnp.concatenate([pack, jnp.zeros_like(pack)], axis=0).astype(jnp.bfloat16)


def finish_layer(
    joined, weight, grad_pre, gate_weight, tokens, grad_middle, mod_rows, feed_sums, extra, grad_tables
):
    rows, width = tokens.shape
    counts = [table.shape[0] for table in grad_tables]

    def fixed(shape):
        return pl.BlockSpec(shape, lambda step: (0,) * len(shape), pipeline_mode=pl.Buffered(1))

    return pl.pallas_call(
        functools.partial(finish_kernel, counts),
        grid=(3,),
        in_specs=[
            pl.BlockSpec((rows, width), lambda step: (0, step)),
            pl.BlockSpec((width, width), lambda step: (0, step)),
            fixed((rows, width)),
            fixed((width, width)),
            fixed((rows, width)),
            fixed((rows, width)),
            fixed((8, width)),
            fixed((8, width)),
            fixed((8, SIDE)),
        ]
        + [fixed((count, 8, LANES)) for count in counts],
        out_specs=(fixed((rows, width)), fixed((16, PACK))),
        out_shape=(
            jax.ShapeDtypeStruct((rows, width), jnp.bfloat16),
            jax.ShapeDtypeStruct((16, PACK), jnp.bfloat16),
        ),
        scratch_shapes=[
            pltpu.VMEM((rows, width), jnp.float32),
            pltpu.VMEM((2, 8, width), jnp.float32),
        ],
        compiler_params=pltpu.CompilerParams(vmem_limit_bytes=VMEM_BYTES),
        cost_estimate=pl.CostEstimate(
            flops=8 * rows * width * width, bytes_accessed=24 * rows * width, transcendentals=0
        ),
        name="finish_layer",
    )(
        joined,
        weight,
        grad_pre,
        gate_weight,
        tokens,
        grad_middle,
        mod_rows,
        feed_sums,
        extra,
        *grad_tables,
    )


def fan_first_kernel(bits_ref, keep_ref, came_ref, mine_ref, *send_refs):
    chunk = keep_ref.shape[0] // 16
    for other, ref in enumerate((mine_ref, *send_refs)):
        for level in range(4):
            start = (level * 4 + (bits_ref[0] ^ other)) * chunk
            for first in range(0, chunk, 16):
                cut = pl.ds(pl.multiple_of(start + first, 16), 16)
                place = level * chunk + first
                ref[place : place + 16] = add_low(keep_ref[cut], came_ref[cut])


def fan_v_kernel(bits_ref, mine_ref, *refs):
    came_refs, (send_ref, out_ref) = refs[:3], refs[3:]
    chunk = mine_ref.shape[0] // 4
    for side, ref in ((1 - bits_ref[0], send_ref), (bits_ref[0], out_ref)):
        for far in range(2):
            for first in range(0, chunk, 16):
                cut = pl.ds(pl.multiple_of((2 * far + side) * chunk + first, 16), 16)
                total = mine_ref[cut].astype(jnp.float32)
                for came_ref in came_refs:
                    total = total + came_ref[cut].astype(jnp.float32)
                place = far * chunk + first
                ref[place : place + 16] = total.astype(jnp.bfloat16)


def fan_u_kernel(bits_ref, mine_ref, came_ref, send_ref, out_ref):
    chunk = mine_ref.shape[0] // 2
    for side, ref in ((1 - bits_ref[0], send_ref), (bits_ref[0], out_ref)):
        for first in range(0, chunk, 16):
            cut = pl.ds(pl.multiple_of(side * chunk + first, 16), 16)
            ref[first : first + 16] = add_low(mine_ref[cut], came_ref[cut])


def join_packs_kernel(bits_ref, *refs):
    packs = [ref[...].astype(jnp.float32)[0:8] for ref in refs[:4]]
    refs[4][...] = jnp.concatenate(packs, axis=0).astype(jnp.bfloat16)


def small_kernel(
    heads,
    here_ref,
    mine_ref,
    came_ref,
    modulation_ref,
    pair_norm_ref,
    relative_ref,
    gain_ref,
    pair_weight_ref,
    mod_grad_ref,
    time_ref,
    label_ref,
    relative_grad_ref,
    gain_grad_ref,
    pair_grad_ref,
    grad_condition,
    grad_mod,
    kept,
):
    step = pl.program_id(0)
    crops = mine_ref.shape[0] // 8
    width = mine_ref.shape[1] - SIDE
    conds = relative_ref.shape[1]
    parts = mod_grad_ref.shape[1] // width

    def parts_split(values):
        upper = values.astype(jnp.bfloat16)
        return upper, (values - upper.astype(jnp.float32)).astype(jnp.bfloat16)

    def dot_left(narrow, values, numbers):
        upper, rest = parts_split(values)
        return wide_dot(narrow, upper, numbers) + wide_dot(narrow, rest, numbers)

    def dot_right(values, narrow, numbers):
        upper, rest = parts_split(values)
        return wide_dot(upper, narrow, numbers) + wide_dot(rest, narrow, numbers)

    def both_twice(narrow):
        return jnp.concatenate([narrow, narrow], axis=0)

    def stacked(values):
        return jnp.concatenate(parts_split(values), axis=0)

    @pl.when(step == 0)
    def _():
        shape = (8 * crops, 8 * crops)
        picked = lax.broadcasted_iota(jnp.int32, shape, 0)
        source = lax.broadcasted_iota(jnp.int32, shape, 1)
        hit = ((source >> 3) == (picked & (crops - 1))) & ((source & 7) == (picked // crops))
        select = jnp.where(hit, 1.0, 0.0).astype(jnp.bfloat16)
        mine = wide_dot(select, mine_ref[...])
        grad_mod[...] = mine[: 6 * crops, :width] + wide_dot(select, came_ref[...])[: 6 * crops, :width]
        condition = (
            mine[5 * crops : 6 * crops, width : width + conds]
            + mine[6 * crops : 7 * crops, width : width + conds]
        )
        gate_value = sigmoid(condition)
        kept[0] = condition * gate_value
        kept[1] = gate_value * (1.0 + condition * (1.0 - gate_value))
        kept[2] = mine[4 * crops : 5 * crops, width : width + conds]
        kept[3] = jnp.broadcast_to(
            mine[5 * crops : 6 * crops, width + conds : width + conds + 1]
            + mine[6 * crops : 7 * crops, width + conds : width + conds + 1],
            (crops, conds),
        )
        grad_condition[...] = jnp.zeros_like(grad_condition)

    cond_act = both_twice(kept[0].astype(jnp.bfloat16))
    for turn in range(parts):
        columns = slice(turn * width, (turn + 1) * width)
        first = pl.multiple_of((step * parts + turn) * crops, crops)
        pair = stacked(grad_mod[pl.ds(first, crops)])
        mod_grad_ref[:, columns] = wide_dot(cond_act, pair, TN)
        more = wide_dot(pair, modulation_ref[:, columns], NT)
        grad_condition[...] += more[:crops] + more[crops:]

    @pl.when(step == 0)
    def _():
        shape = (8, 8 * crops)
        line = lax.broadcasted_iota(jnp.int32, shape, 0)
        local = lax.broadcasted_iota(jnp.int32, shape, 1) & 7
        every = jnp.where(local == line, 1.0, 0.0).astype(jnp.bfloat16)
        lines = wide_dot(every, mine_ref[...]) + wide_dot(every, came_ref[...])

        def of_head(head):
            upper = width + (head % 3) * LANES
            rest = (head % (width // LANES)) * LANES
            low = 6 + head // (width // LANES)
            return (
                lines[head // 3 : head // 3 + 1, upper : upper + LANES]
                + lines[low : low + 1, rest : rest + LANES]
            )

        table = jnp.concatenate(
            [of_head(head) for head in range(heads)]
            + [jnp.zeros((16 - heads, LANES), jnp.float32)],
            axis=0,
        )
        bins = relative_ref.shape[0]
        pair_grad_ref[...] = dot_right(table, pair_norm_ref[...], (((1,), (0,)), ((), ())))[:heads]
        grad_norm = dot_right(table, pair_weight_ref[...], (((0,), (1,)), ((), ())))[:bins]
        values = relative_ref[...].astype(jnp.float32)
        centred = values - jnp.mean(values, axis=1, keepdims=True)
        root = lax.rsqrt(jnp.mean(centred * centred, axis=1, keepdims=True) + 1e-06)
        normal = centred * root
        gain_grad_ref[...] = jnp.sum(grad_norm * normal, axis=0, keepdims=True)
        scaled = grad_norm * gain_ref[...].astype(jnp.float32)
        relative_grad_ref[...] = root * (
            scaled
            - jnp.mean(scaled, axis=1, keepdims=True)
            - normal * jnp.mean(scaled * normal, axis=1, keepdims=True)
        )

    @pl.when(step == pl.num_programs(0) - 1)
    def _():
        final = stacked(grad_condition[...] * kept[1])
        time_ref[...] = wide_dot(both_twice(kept[2].astype(jnp.bfloat16)), final, TN)
        label = lax.broadcasted_iota(jnp.int32, (crops, label_ref.shape[0]), 1)
        number = kept[3][:, 0:1].astype(jnp.int32)
        onehot = jnp.where(label == number, 1.0, 0.0).astype(jnp.bfloat16)
        label_ref[...] = wide_dot(both_twice(onehot), final, TN)


def small_gradients(heads, labels, mine, came, modulation_weight, pair_norm, relative, gain, pair_weight):
    conds, wide = modulation_weight.shape
    bins = relative.shape[0]
    rows = mine.shape[0]
    steps = 3

    def fixed(shape):
        return pl.BlockSpec(shape, lambda step: (0, 0))

    shapes = [(conds, wide), (conds, conds), (labels, conds), (bins, conds), (1, conds), (heads, conds)]
    return pl.pallas_call(
        functools.partial(small_kernel, heads),
        grid=(steps,),
        in_specs=[
            pl.BlockSpec(memory_space=pltpu.SMEM),
            fixed((rows, PACK)),
            fixed((rows, PACK)),
            pl.BlockSpec((conds, wide // steps), lambda step: (0, step)),
            fixed((LANES, conds)),
            fixed((bins, conds)),
            fixed((1, conds)),
            fixed((conds, 16)),
        ],
        out_specs=tuple(
            [pl.BlockSpec((conds, wide // steps), lambda step: (0, step))]
            + [fixed(s) for s in shapes[1:]]
        ),
        out_shape=tuple(jax.ShapeDtypeStruct(shape, jnp.float32) for shape in shapes),
        scratch_shapes=[
            pltpu.VMEM((rows // 8, conds), jnp.float32),
            pltpu.VMEM((6 * rows // 8, wide // 6), jnp.float32),
            pltpu.VMEM((4, rows // 8, conds), jnp.float32),
        ],
        compiler_params=pltpu.CompilerParams(vmem_limit_bytes=VMEM_BYTES),
        cost_estimate=pl.CostEstimate(
            flops=100000000, bytes_accessed=10000000, transcendentals=0
        ),
        name="small_gradients",
    )(
        scalars(0),
        mine,
        came,
        modulation_weight,
        pair_norm,
        relative,
        gain,
        pair_weight,
    )


def per_device(
    crop_parts,
    res_parts,
    tokens,
    cotangent,
    time_levels,
    cath_ids,
    residue_numbers,
    chain_mask,
    time_weight,
    label_table,
    modulation_weight,
    projection_weight,
    gate_weight,
    output_weight,
    relative_table,
    pair_gain,
    pair_weight,
    feed_gate,
    feed_up,
    feed_down,
):
    crop_count, row_count, model_width = tokens.shape
    crop_length = residue_numbers.shape[1]
    head_count = pair_weight.shape[1]
    head_width = model_width // head_count
    bin_count = relative_table.shape[0]
    label_count = label_table.shape[0]
    token_count = crop_count * row_count
    score_scale = head_width ** (-0.5)
    pairs = head_count // 2
    layout = Layout(row_count, crop_length)
    query_start = lax.axis_index("res") * row_count

    def conditioning(features, onehot):
        return jnp.dot(features, time_weight, preferred_element_type=jnp.float32) + jnp.dot(
            onehot, label_table, preferred_element_type=jnp.float32
        )

    features = time_features(time_levels, time_weight.shape[0]).astype(jnp.bfloat16)
    label_onehot = (cath_ids[:, None] == jnp.arange(label_count, dtype=jnp.int32)[None, :]).astype(
        jnp.bfloat16
    )
    condition = conditioning(features, label_onehot)
    cond_act = jax.nn.silu(condition).astype(jnp.bfloat16)
    modulation = jnp.dot(cond_act, modulation_weight, preferred_element_type=jnp.float32)
    modulation = modulation.reshape(crop_count, 6, 1, model_width)
    shift_a, scale_a = modulation[:, 0], modulation[:, 1]
    mod_rows = pad_to(modulation[:, :, 0], 1, 8, 0.0)

    rotated = lax.dynamic_slice_in_dim(
        jnp.concatenate([jnp.stack([residue_numbers, chain_mask])] * 2, 2), query_start, crop_length, 2
    )
    members, kinds, forward_bins, backward_bins, places, *turned, tables, pair_norm = attention_tables(
        layout,
        score_scale,
        rotated[0],
        rotated[1],
        query_start,
        relative_table,
        pair_gain,
        pair_weight,
    )

    token_values = tokens.astype(jnp.float32)
    normed_a = (
        modulate(token_values, shift_a, scale_a)
        .astype(jnp.bfloat16)
        .reshape(token_count, model_width)
    )
    def project(weight):
        rows = jnp.dot(normed_a, weight, preferred_element_type=jnp.float32)
        return rows.astype(jnp.bfloat16).reshape(crop_count, row_count, -1)

    key_values = project(projection_weight[:, model_width:])
    others = [
        lax.ppermute(
            key_values, "res", [((r + step) % res_parts, r) for r in range(res_parts)]
        )
        for step in range(1, res_parts)
    ]
    if len(layout.pieces) == 2:
        other = others[0] if len(others) == 1 else jnp.concatenate(others, axis=1)
        pieces = [(key_values, 0, pairs), (other, 0, pairs)]
    else:
        pieces = [(jnp.concatenate([key_values] + others, axis=1), 0, pairs)]

    def block_rows(values):
        return pad_to(values, 1, layout.block_rows, 0)

    queries, attended, logs = attention_forward(
        layout,
        score_scale,
        block_rows(normed_a.reshape(tokens.shape)),
        projection_weight,
        pieces,
        members,
        kinds,
        forward_bins,
        tables,
    )
    here = lax.axis_index("res")
    split = res_parts == 2 and crop_parts == 16
    per_crop_results = [
        feed_layer(
            split,
            here,
            attended[crop],
            block_rows(tokens)[crop],
            block_rows(cotangent)[crop],
            block_rows(normed_a.reshape(tokens.shape))[crop],
            mod_rows[crop],
            gate_weight,
            output_weight,
            feed_gate,
            feed_up,
            feed_down,
        )
        for crop in range(crop_count)
    ]
    layer_out, grad_middle, grad_attended, grad_gate_pre, feed_sums = (
        jnp.stack([result[place] for result in per_crop_results]) for place in range(5)
    )
    layer_out, grad_middle = layer_out[:, :row_count], grad_middle[:, :row_count]
    grad_gate_pre = grad_gate_pre[:, :row_count].reshape(token_count, model_width)
    weight_grads = [
        sum(result[place].astype(jnp.float32) for result in per_crop_results).astype(jnp.bfloat16)
        if crop_count > 1
        else per_crop_results[0][place]
        for place in range(5, len(per_crop_results[0]))
    ]

    def backward_of(first_pair, count, grad_now):
        return attention_backward(
            layout,
            score_scale,
            first_pair,
            count,
            queries,
            grad_now,
            attended,
            logs,
            pieces,
            members,
            kinds,
            backward_bins,
            places,
            *turned,
            tables,
        )

    if split:
        arrivals = [swap_res(weight_grads[place]) for place in (0, 2, 4, 6)]
        kept = [weight_grads[place] for place in (1, 3, 5, 7)]
        half = model_width // 2
        inner = feed_gate.shape[1] // 2
        calls = [list(backward_of(0, 1, grad_attended))]
        arrivals, calls[0] = tie(arrivals, calls[0])
        gate_w, up_w, down_w, small_w = zip(kept, arrivals)
        halving = Halving(
            [
                [(gate_w, 0, inner), (small_w, 0, half)],
                [(up_w, 0, inner), (small_w, 1, half)],
                [(down_w, 0, half)],
            ],
            ["xyvu", "yvxu", "vxyu"],
        )
        arrived = []
        for first_pair, count in ((1, 4), (5, 1)):
            arrived.append(swap_res(calls[-1][2][0]))
            sent = halving.stage()
            sent, grad_attended = tie(sent, grad_attended)
            came = halving.send(sent)
            calls.append(list(backward_of(first_pair, count, grad_attended)))
            came, calls[-1], arrived[-1] = tie(came, calls[-1], arrived[-1])
            halving.take(came)
        index = lax.axis_index("crop")
        bf16 = jnp.bfloat16
        share = model_width // 16
        away = swap_res(calls[2][2][0])
        sent = halving.stage()
        sent, calls[2][1] = tie(sent, calls[2][1])
        came = halving.send(sent)
        joined, proj_send, proj_keep = projection_gradient(
            here,
            normed_a,
            [
                (calls[0][0][0], calls[0][1][0], arrived[0]),
                (calls[1][0][0], calls[1][1][0], arrived[1]),
                (calls[2][0][0], calls[2][1][0], away),
            ],
        )
        came, proj_send, proj_keep = tie(came, proj_send, proj_keep)
        proj_came = swap_res(proj_send)
        halving.take(came)
        (sent,) = halving.stage(merge=True)
        sent, proj_came = tie(sent, proj_came)
        came = exchange(sent, MASKS["u"])
        mine, *fan = local_call(
            fan_first_kernel,
            scalars(index % 4),
            [proj_keep, proj_came],
            [((4 * share, PACK), bf16)] * 4,
            "fan_first",
        )
        fan, joined = tie(fan, joined)
        fan_came = [exchange(value, mask + 1) for mask, value in enumerate(fan)]
        extra = jnp.concatenate(
            [
                pad_to(features.astype(jnp.float32), 1, SIDE, 0.0),
                jnp.concatenate(
                    [condition, pad_to(cath_ids.astype(jnp.float32)[:, None], 1, LANES, 0.0)], axis=1
                ),
            ],
            axis=0,
        )
        tokens_grad, pack = finish_layer(
            joined,
            projection_weight,
            grad_gate_pre,
            gate_weight,
            tokens[0],
            grad_middle[0],
            mod_rows[0],
            feed_sums[0],
            jnp.pad(extra, ((4, 2), (0, 0))),
            [call[-1][0] for call in calls],
        )
        tokens_grad = tokens_grad[None]
        came, pack = tie(came, pack)
        packs = [pack] + [exchange(pack, mask + 1) for mask in range(3)]
        finals = halving.stage(last=True, merged=came)
        feed_gate_grad, output_weight_grad, feed_up_grad, gate_weight_grad, feed_down_grad = finals
        packs, finals = tie(packs, finals)
        (packs,) = local_call(join_packs_kernel, scalars(0), packs, [((32, PACK), bf16)], "join_packs")
        far_packs = exchange(packs, MASKS["v"])
        packs, fan_came, far_packs = tie(packs, fan_came, far_packs)
        sent, mine = local_call(
            fan_v_kernel,
            scalars((index // 4) % 2),
            [mine, *fan_came],
            [((2 * share, PACK), bf16), ((2 * share, PACK), bf16)],
            "fan_v",
        )
        packs = jnp.concatenate([packs, far_packs], axis=0)
        sent, packs = tie(sent, packs)
        came = exchange(sent, MASKS["v"])
        far_packs = exchange(packs, MASKS["u"])
        came, far_packs = tie(came, far_packs)
        packs = jnp.concatenate([packs, far_packs], axis=0)
        sent, mine = local_call(
            fan_u_kernel,
            scalars(index // 8),
            [mine, came],
            [((share, PACK), bf16), ((share, PACK), bf16)],
            "fan_u",
        )
        sent, packs = tie(sent, packs)
        came = exchange(sent, MASKS["u"])
        (
            modulation_weight_grad,
            time_weight_grad,
            label_table_grad,
            relative_table_grad,
            pair_gain_grad,
            pair_weight_grad,
        ) = small_gradients(
            head_count,
            label_count,
            packs,
            swap_res(packs),
            modulation_weight,
            pair_norm,
            relative_table,
            pair_gain.reshape(1, -1),
            pad_to(pair_weight, 1, 16, 0.0),
        )
        pair_weight_grad = pair_weight_grad.T
        came, pair_weight_grad = tie(came, pair_weight_grad)
        projection_weight_grad = add_low(mine, came, jnp.float32)
        pair_gain_grad = pair_gain_grad[0]
    else:
        results = backward_of(0, pairs, grad_attended)
        grad_table = results[-1]
        grad_pairs = results[1:-1]
        if len(grad_pairs) == 2:
            total, away = grad_pairs[0].astype(jnp.float32), grad_pairs[1]
        else:
            total = grad_pairs[0][:, :, :row_count].astype(jnp.float32)
            away = grad_pairs[0][:, :, row_count:]
        for step in range(1, res_parts):
            sent = away[:, :, (step - 1) * row_count : step * row_count]
            pairs_to = [(r, (r + step) % res_parts) for r in range(res_parts)]
            total = total + lax.ppermute(sent, "res", pairs_to).astype(jnp.float32)
        total = total.astype(jnp.bfloat16)
        grad_projected = jnp.concatenate(
            [results[0][:, :row_count], total[:, 0], total[:, 1]], axis=-1
        ).reshape(token_count, 3 * model_width)
        grad_normed_a = against_columns(grad_projected, projection_weight) + against_columns(
            grad_gate_pre, gate_weight
        )
        norm_back_a = jax.vjp(modulate, token_values, shift_a, scale_a)[1]
        grad_tokens, grad_shift_a, grad_scale_a = norm_back_a(
            grad_normed_a.reshape(crop_count, row_count, model_width)
        )
        tokens_grad = (grad_middle + grad_tokens).astype(jnp.bfloat16)
        feed_gate_grad, feed_up_grad, feed_down_grad = (
            scatter_crops(share_columns(value, res_parts)) for value in weight_grads[:3]
        )
        output_weight_grad, gate_weight_grad = (
            scatter_crops(share_columns(value, res_parts))
            for value in (weight_grads[3][:, :model_width], weight_grads[3][:, model_width:])
        )
        projection_weight_grad = scatter_crops(
            share_columns(across_rows(normed_a, grad_projected), res_parts)
        )
        grad_table = grad_table[:, :, :2].sum(0).reshape(head_count, LANES)

        grad_modulation = jnp.concatenate([grad_shift_a, grad_scale_a, feed_sums[:, 2:6]], axis=1)
        grad_modulation = grad_modulation.reshape(crop_count, 6 * model_width)
        table_row = grad_table.reshape(1, head_count * LANES)
        first_row = (jnp.arange(crop_count) == 0).astype(jnp.float32)[:, None]
        small_here = jnp.concatenate([grad_modulation, first_row * table_row], axis=1)
        levels_here = jnp.stack([time_levels, cath_ids.astype(jnp.float32)], axis=1)
        levels_here = pad_to(levels_here, 1, LANES, 0.0)
        small_all = gather_crops(
            jnp.concatenate([levels_here, sum_res(small_here, res_parts)], axis=1), crop_parts
        )
        levels_all, small_all = small_all[:, :2], small_all[:, LANES:]
        grad_modulation = small_all[:, : 6 * model_width]
        grad_table = jnp.sum(small_all[:, 6 * model_width :], axis=0).reshape(head_count, LANES)
        grad_table = grad_table[:, :bin_count]
        features_all = time_features(levels_all[:, 0], time_weight.shape[0]).astype(jnp.bfloat16)
        onehot_all = (
            levels_all[:, 1].astype(jnp.int32)[:, None]
            == jnp.arange(label_count, dtype=jnp.int32)[None, :]
        ).astype(jnp.bfloat16)
        condition = conditioning(features_all, onehot_all)
        cond_act = jax.nn.silu(condition).astype(jnp.bfloat16)
        modulation_weight_grad = split_left(cond_act, grad_modulation, 0, 0)
        grad_condition = split_left(modulation_weight, grad_modulation, 1, 1).T * silu_slope(condition)
        time_weight_grad = split_left(features_all, grad_condition, 0, 0)
        label_table_grad = split_left(onehot_all, grad_condition, 0, 0)
        relative_values = relative_table.astype(jnp.float32)
        gain_values = pair_gain.astype(jnp.float32)
        pair_norm = pair_norm[:bin_count]
        pair_weight_grad = split_left(pair_norm, grad_table, 0, 1)
        grad_pair_norm = split_right(grad_table, pair_weight, 0, 1)
        pair_back = jax.vjp(normalize_rows, relative_values, gain_values)[1]
        relative_table_grad, pair_gain_grad = pair_back(grad_pair_norm)
    return (
        layer_out,
        tokens_grad,
        time_weight_grad,
        label_table_grad,
        modulation_weight_grad,
        projection_weight_grad,
        gate_weight_grad,
        output_weight_grad,
        relative_table_grad,
        pair_gain_grad,
        pair_weight_grad,
        feed_gate_grad,
        feed_up_grad,
        feed_down_grad,
    )


def solution(mesh):
    return jax.shard_map(
        functools.partial(per_device, mesh.shape["crop"], mesh.shape["res"]),
        mesh=mesh,
        in_specs=(
            P("crop", "res", None),
            P("crop", "res", None),
            P("crop"),
            P("crop"),
            P("crop", None),
            P("crop", None),
            P(),
            P(),
            P(),
            P(),
            P(),
            P(),
            P(),
            P(),
            P(),
            P(),
            P(),
            P(),
        ),
        out_specs=(
            P("crop", "res", None),
            P("crop", "res", None),
            P(),
            P(),
            P(),
            P("crop", "res"),
            P("crop", "res"),
            P("crop", "res"),
            P(),
            P(),
            P(),
            P("crop", "res"),
            P("crop", "res"),
            P("crop", "res"),
        ),
        check_vma=False,
    )
```

```python
import functools
import itertools
import math

import jax
import jax.numpy as jnp
from jax import lax
from jax.experimental import pallas as pl
from jax.experimental.pallas import tpu as pltpu
from jax.sharding import PartitionSpec as P

LANES = 128
NEAR = 31
VMEM_BYTES = 56 * 1024 * 1024
QUERY_BLOCK = 384
KEY_BLOCK = 768
LOG2E = 1.4426950408889634
NONE, RIGHT, LEFT, APART = 0, 1, 2, 3


def layer_norm(inputs):
    mean_value = jnp.mean(inputs, axis=-1, keepdims=True)
    centred = inputs - mean_value
    spread = jnp.mean(centred * centred, axis=-1, keepdims=True)
    return centred * lax.rsqrt(spread + 1e-06)


def modulate(inputs, shift_row, scale_row):
    return layer_norm(inputs) * (1.0 + scale_row) + shift_row


def normalize_rows(table_rows, gain_row):
    return layer_norm(table_rows) * gain_row


def time_features(time_levels, feature_width):
    half_width = feature_width // 2
    frequency = jnp.exp(-math.log(10000.0) * jnp.arange(half_width, dtype=jnp.float32) / half_width)
    angles = 1000.0 * time_levels[:, None] * frequency[None, :]
    return jnp.concatenate([jnp.sin(angles), jnp.cos(angles)], axis=-1)


def across_rows(former, latter):
    return lax.dot_general(
        former, latter, (((0,), (0,)), ((), ())), preferred_element_type=jnp.float32
    )


def against_columns(former, latter):
    return lax.dot_general(
        former, latter, (((1,), (1,)), ((), ())), preferred_element_type=jnp.float32
    )


def split_parts(values):
    upper = lax.reduce_precision(values, 8, 7)
    return (upper.astype(jnp.bfloat16), (values - upper).astype(jnp.bfloat16))


def split_left(narrow, values, former_dim, latter_dim):
    upper, rest = split_parts(values)
    numbers = (((former_dim,), (latter_dim,)), ((), ()))
    return lax.dot_general(
        narrow, upper, numbers, preferred_element_type=jnp.float32
    ) + lax.dot_general(narrow, rest, numbers, preferred_element_type=jnp.float32)


def split_right(values, narrow, former_dim, latter_dim):
    upper, rest = split_parts(values)
    numbers = (((former_dim,), (latter_dim,)), ((), ()))
    return lax.dot_general(
        upper, narrow, numbers, preferred_element_type=jnp.float32
    ) + lax.dot_general(rest, narrow, numbers, preferred_element_type=jnp.float32)


def sigmoid_slope(inputs):
    gate_value = jax.nn.sigmoid(inputs)
    return gate_value * (1.0 - gate_value)


def silu_slope(inputs):
    gate_value = jax.nn.sigmoid(inputs)
    return gate_value * (1.0 + inputs * (1.0 - gate_value))


class Layout:
    def __init__(self, rows, length):
        self.rows = rows
        self.length = length
        self.query_tiles = -(-rows // LANES)
        self.key_tiles = -(-length // LANES)
        self.padded = self.query_tiles * LANES
        self.wide = self.key_tiles * LANES
        self.last = self.key_tiles - 1
        self.groups = (self.query_tiles + 4) * 4
        assert 2 * self.groups + 3 <= LANES and self.groups <= 64
        assert rows - 1 + NEAR < self.padded and length - NEAR >= self.last * LANES
        assert rows % 8 == 0 and self.last > self.query_tiles
        self.block_rows = rows if rows % 16 == 0 else self.padded
        self.pieces = [rows, length - rows] if rows % 16 == 0 else [length]

    def tile_start(self, tile):
        return self.last * LANES if tile < 0 else tile * LANES


def pad_to(values, axis, size, fill):
    widths = [(0, 0)] * values.ndim
    widths[axis] = (0, size - values.shape[axis])
    return jnp.pad(values, widths, constant_values=fill)


def tables_kernel(
    layout, bin_count, heads, scale, start_ref, pairs_ref, relative_ref, gain_ref, weight_ref, *out_refs
):
    members_ref, kinds_ref, forward_ref, backward_ref, places_ref = out_refs[:5]
    members_turned, kinds_turned, tables_ref, norm_ref, codes = out_refs[5:]
    rows, length, queries, groups = layout.rows, layout.length, layout.query_tiles, layout.groups
    wrap = length - start_ref[0]
    reach = (bin_count - 2) // 2
    zero_bin = LANES - 1
    shape = (LANES, LANES)
    lane = lax.broadcasted_iota(jnp.int32, shape, 1)
    row = lax.broadcasted_iota(jnp.int32, shape, 0)
    last_start = layout.last * LANES

    values = relative_ref[...].astype(jnp.float32)
    centred = values - jnp.mean(values, axis=1, keepdims=True)
    root = lax.rsqrt(jnp.mean(centred * centred, axis=1, keepdims=True) + 1e-06)
    pair_norm = (centred * root * gain_ref[...].astype(jnp.float32)).astype(jnp.bfloat16)
    norm_ref[...] = pair_norm
    bias = lax.dot_general(
        weight_ref[...], pair_norm, (((0,), (1,)), ((), ())), preferred_element_type=jnp.float32
    )
    head_lane = lax.broadcasted_iota(jnp.int32, bias.shape, 1)
    final = jnp.sum(jnp.where(head_lane == bin_count - 1, bias, 0.0), axis=1, keepdims=True)
    table = jnp.where(head_lane < bin_count, (bias - final) * (1.0 / scale), 0.0)

    def columns(number):
        value = jnp.sum(jnp.where(head_lane == number, table, 0.0), axis=1, keepdims=True)
        upper = value.astype(jnp.bfloat16).astype(jnp.float32)
        return jnp.where(
            head_lane < groups, upper, jnp.where(head_lane < 2 * groups, value - upper, 0.0)
        )

    right_columns, left_columns = columns(bin_count - 2), columns(0)
    for head in range(heads):
        line = 8 * (head % 2)
        for place, rows_of in enumerate((table, right_columns, left_columns)):
            tables_ref[head // 2, line + place : line + place + 1] = rows_of[head : head + 1]

    tiles = pairs_ref.shape[1]
    marks = pairs_ref[1].astype(jnp.float32)
    place = lax.broadcasted_iota(jnp.int32, marks.shape, 0) * LANES + lax.broadcasted_iota(
        jnp.int32, marks.shape, 1
    )
    before = jnp.sum(jnp.where(place < wrap, marks, 0.0), keepdims=True)
    every = jnp.sum(marks, keepdims=True)
    triangle = jnp.where(row <= lane, 1.0, 0.0).astype(jnp.bfloat16)
    running = jnp.dot(marks.astype(jnp.bfloat16), triangle, preferred_element_type=jnp.float32)
    numbers, chains = [], []
    carry = jnp.zeros((1, 1), jnp.float32)
    for tile in range(layout.key_tiles):
        count = running[tile : tile + 1] + carry
        carry = carry + running[tile : tile + 1, LANES - 1 :]
        count = count + jnp.where(place[tile : tile + 1] < wrap, every - before, -before)
        chains.append(jnp.broadcast_to(count.astype(jnp.int32), shape))
        numbers.append(jnp.broadcast_to(pairs_ref[0, tile : tile + 1], shape))
    number_rows = [value.T for value in numbers]
    chain_rows = [value.T for value in chains]

    def bins_of(key_number, key_chain, query_number, query_chain):
        offset = jnp.clip(key_number - query_number, -reach, reach) + reach
        return jnp.where(key_chain == query_chain, offset, bin_count - 1)

    def touches(query, tile):
        begin = -LANES if tile < 0 else tile * LANES
        return (begin <= query + NEAR) & (query - NEAR <= begin + LANES - 1)

    for tile in range(layout.key_tiles):
        size = min(LANES, length - tile * LANES)
        key = tile * LANES + row
        if tile == layout.last:
            other = jnp.full(shape, queries + 3, jnp.int32)
        elif tile == queries - 1:
            other = jnp.full(shape, queries, jnp.int32)
        else:
            other = jnp.where(key < wrap, queries + 1, queries + 2)
        group = jnp.where(key < rows, tile, other)
        slot = group * 4 + chain_rows[tile] - 1
        hit = (lane == slot) | (lane == slot + groups)
        tail = (lane >= 2 * groups) & (lane < 2 * groups + 3)
        values = jnp.where(hit, 1.0, jnp.where(tail, -1.0, 0.0)).astype(jnp.bfloat16)
        members_ref[tile * LANES : tile * LANES + size] = values[:size]
        turned = jnp.where(hit & (lane < groups), 1.0, 0.0).T
        members_turned[:, tile * LANES : tile * LANES + size] = turned[:64, :size].astype(jnp.bfloat16)

    local = jnp.where(lane >= groups, lane - groups, lane)
    lane_group = local >> 2
    lane_chain = (local & 3) + 1
    lane_begin = jnp.where(
        lane_group < queries,
        lane_group * LANES,
        jnp.where(lane_group == queries, (queries - 1) * LANES, -LANES),
    )
    has_band = (lane_group <= queries) | (lane_group == queries + 3)
    other_right = jnp.where(
        lane_group == queries,
        rows,
        jnp.where(
            lane_group == queries + 3,
            last_start,
            jnp.where(lane_group == queries + 1, 0, 2 * length),
        ),
    )
    right_limit = jnp.where(lane_group > queries, jnp.where(lane_group == queries + 3, wrap, length), wrap)
    for tile in range(queries):
        size = min(LANES, layout.block_rows - tile * LANES)
        query = tile * LANES + row
        near = (lane_begin <= query + NEAR) & (query - NEAR <= lane_begin + LANES - 1) & has_band
        right = jnp.where(lane_group < queries, lane_group - tile, right_limit - other_right) > 0
        same = chain_rows[tile] == lane_chain
        kinds = jnp.where(same, jnp.where(near, NONE, jnp.where(right, RIGHT, LEFT)), APART)
        kinds = jnp.where((lane < 2 * groups) & (query < rows), kinds, NONE)
        kinds_ref[tile * LANES : tile * LANES + size] = kinds[:size]
        kinds_turned[:, tile * LANES : (tile + 1) * LANES] = jnp.where(lane < groups, kinds, NONE).T[:64]
        for step in range(3):
            near_tile = tile + step - 1
            index = layout.last if near_tile < 0 else near_tile
            if near_tile < queries:
                inside = touches(query, near_tile) & (query < rows)
                inside &= lane < length - index * LANES
                found = bins_of(
                    numbers[index], chains[index], number_rows[tile], chain_rows[tile]
                )
                found = jnp.where(inside, found, zero_bin)
            else:
                found = jnp.full(shape, zero_bin, jnp.int32)
            forward_ref[
                tile * LANES : (tile + 1) * LANES, step * LANES : (step + 1) * LANES
            ] = found

    codes[...] = jnp.full(codes.shape, -1, jnp.int32)
    for tile in range(queries):
        size = min(LANES, rows - tile * LANES)
        code = number_rows[tile] * 8 + chain_rows[tile]
        codes[(tile + 1) * LANES : (tile + 1) * LANES + size] = code[:size]

    for index, tile in enumerate(list(range(queries)) + [-1]):
        source = layout.last if tile < 0 else tile
        key_row = (row - (length - last_start)) if tile < 0 else tile * LANES + row
        present = row < length - source * LANES
        for step in range(3):
            near_tile = tile + step - 1
            if 0 <= near_tile < queries:
                near_query = near_tile * LANES + lane
                inside = touches(near_query, tile) & (near_query < rows) & present
                found = bins_of(
                    number_rows[source], chain_rows[source], numbers[near_tile], chains[near_tile]
                )
                found = jnp.where(inside, found, zero_bin)
            else:
                found = jnp.full(shape, zero_bin, jnp.int32)
            backward_ref[
                index * LANES : (index + 1) * LANES, step * LANES : (step + 1) * LANES
            ] = found
        target = (number_rows[source] + reach - lane) * 8 + chain_rows[source]
        target = jnp.where(present & (lane > 0) & (lane < 2 * reach), target, -9)
        offset = (LANES - (length - last_start)) if tile < 0 else (tile + 1) * LANES
        far = 4 * LANES
        shift = jnp.full(shape, far, jnp.int32)
        for distance in range(-NEAR, NEAR + 1):
            other = codes[offset - distance : offset - distance + LANES]
            shift = jnp.where(other == target, distance, shift)
        if tile < 0:
            base = jnp.zeros(shape, jnp.int32)
        else:
            base = jnp.where(row < LANES // 2, tile - 1, tile) * LANES
        places_ref[index * LANES : (index + 1) * LANES] = jnp.where(
            shift == far, far - 1, key_row - shift - base
        )


def attention_tables(layout, scale, numbers, marks, query_start, relative_table, pair_gain, pair_weight):
    crops = numbers.shape[0]
    bin_count, width = relative_table.shape
    heads = pair_weight.shape[1]
    pairs = jnp.stack([numbers, marks], axis=1)
    pairs = pad_to(pairs, 2, layout.wide, 0).reshape(crops, 2, layout.key_tiles, LANES)
    spots = (layout.query_tiles + 1) * LANES
    shapes = [
        ((layout.length, LANES), jnp.bfloat16),
        ((layout.block_rows, LANES), jnp.int32),
        ((layout.padded, 3 * LANES), jnp.int32),
        ((spots, 3 * LANES), jnp.int32),
        ((spots, LANES), jnp.int32),
        ((64, layout.length), jnp.bfloat16),
        ((64, layout.padded), jnp.int32),
    ]
    shared = [((heads // 2, 16, LANES), jnp.float32), ((LANES, width), jnp.bfloat16)]

    def whole(shape):
        return pl.BlockSpec(shape, lambda crop: (0,) * len(shape))

    return pl.pallas_call(
        functools.partial(tables_kernel, layout, bin_count, heads, scale),
        grid=(crops,),
        in_specs=[
            pl.BlockSpec(memory_space=pltpu.SMEM),
            pl.BlockSpec((None, 2, layout.key_tiles, LANES), lambda crop: (crop, 0, 0, 0)),
            whole((LANES, width)),
            whole((1, width)),
            whole((width, 16)),
        ],
        out_specs=tuple(
            [pl.BlockSpec((None, *shape), lambda crop: (crop, 0, 0)) for shape, _ in shapes]
            + [whole(shape) for shape, _ in shared]
        ),
        out_shape=tuple(
            [jax.ShapeDtypeStruct((crops, *shape), kind) for shape, kind in shapes]
            + [jax.ShapeDtypeStruct(shape, kind) for shape, kind in shared]
        ),
        scratch_shapes=[pltpu.VMEM((layout.padded + 2 * LANES, LANES), jnp.int32)],
        compiler_params=pltpu.CompilerParams(vmem_limit_bytes=VMEM_BYTES),
        cost_estimate=pl.CostEstimate(
            flops=40000000 * crops, bytes_accessed=4000000 * crops, transcendentals=0
        ),
        name="pair_tables",
    )(
        jnp.reshape(query_start, (1,)).astype(jnp.int32),
        pairs,
        pad_to(relative_table, 0, LANES, 0.0),
        pair_gain.reshape(1, -1),
        pad_to(pair_weight, 1, 16, 0.0),
    )


NT = (((1,), (1,)), ((), ()))
TN = (((0,), (0,)), ((), ()))


def wide_dot(former, latter, numbers=(((1,), (0,)), ((), ()))):
    return lax.dot_general(former, latter, numbers, preferred_element_type=jnp.float32)


def look_up(table_row, bins):
    table = jnp.broadcast_to(table_row, bins.shape)
    return jnp.take_along_axis(table, bins, axis=1, mode="promise_in_bounds")


def half_of(values, lane, side):
    return jnp.where((lane >= 64) == (side == 1), values, jnp.zeros_like(values))


def row_blocks(total, size):
    return [(start, min(start + size, total)) for start in range(0, total, size)]


def group_columns(kinds, tables, side):
    right = tables[8 * side + 1 : 8 * side + 2]
    left = tables[8 * side + 2 : 8 * side + 3]
    return jnp.where(kinds == RIGHT, right, jnp.where(kinds == LEFT, left, 0.0))


def forward_kernel(layout, scale, *refs):
    count = len(layout.pieces)
    normed_ref, weight_ref = refs[:2]
    key_refs = refs[2 : 2 + count]
    value_refs = refs[2 + count : 2 + 2 * count]
    members_ref, kinds_ref, bins_ref, tables_ref, query_ref, out_ref, log_ref = refs[
        2 + 2 * count : -1
    ]
    all_scores = refs[-1]
    pair = pl.program_id(1)
    rows, length = layout.block_rows, layout.length
    turn = 0
    factor = scale * LOG2E
    lane = lax.broadcasted_iota(jnp.int32, (1, LANES), 1)
    query = wide_dot(normed_ref[...], weight_ref[...]).astype(jnp.bfloat16)
    query_ref[...] = query
    keys = jnp.concatenate([ref[...] for ref in key_refs], axis=0)
    values = jnp.concatenate([ref[...] for ref in value_refs], axis=0)
    members = members_ref[...]
    kinds = kinds_ref[...]
    tables = tables_ref[...]
    ones = jnp.ones((length, LANES), jnp.bfloat16)

    @pl.when(pair == 0)
    def _():
        log_ref[...] = jnp.zeros_like(log_ref)

    for side in range(2):
        key_columns = jnp.concatenate([half_of(keys, lane, side), members], axis=1)
        value_columns = jnp.concatenate([half_of(values, lane, side), ones], axis=1)
        extra = group_columns(kinds, tables, side).astype(jnp.bfloat16)
        query_columns = jnp.concatenate([query, extra], axis=1)
        table_row = tables[8 * side : 8 * side + 1]
        for start, stop in row_blocks(rows, QUERY_BLOCK):
            size = stop - start
            scores = all_scores.at[turn % 2]
            turn += 1
            scores[0:size, 0:length] = wide_dot(query_columns[start:stop], key_columns, NT)
            for tile in range(start // LANES, -(-stop // LANES)):
                first, final = tile * LANES, min(tile * LANES + LANES, rows)
                for slot in range(3):
                    other = tile + slot - 1
                    if other >= layout.query_tiles:
                        continue
                    low, high = first, final
                    if slot == 0:
                        high = min(first + 32, final)
                    if slot == 2:
                        low = first + LANES - 32
                    if low >= high:
                        continue
                    place = layout.tile_start(other)
                    width = min(LANES, length - place)
                    bins = bins_ref[low:high, slot * LANES : (slot + 1) * LANES]
                    bias = look_up(table_row, bins)[:, :width]
                    scores[low - start : high - start, place : place + width] += bias
            block = scores[0:size, 0:length]
            top = jnp.max(block, axis=1, keepdims=True)
            weights = jnp.exp2((block - top) * factor).astype(jnp.bfloat16)
            sums = wide_dot(weights, value_columns)
            total = sums[:, LANES:]
            result = sums[:, :LANES] / total
            if side == 0:
                out_ref[start:stop] = result
            else:
                out_ref[start:stop] += result
            log_total = top + jnp.log(total) * (1.0 / scale)
            log_ref[start:stop] = jnp.where(
                lane == 2 * pair + side, log_total, log_ref[start:stop]
            )


def backward_kernel(layout, scale, first_pair, *refs):
    count = len(layout.pieces)
    query_ref, grad_ref, out_ref, log_ref = refs[:4]
    key_refs = refs[4 : 4 + count]
    value_refs = refs[4 + count : 4 + 2 * count]
    rest = refs[4 + 2 * count :]
    members_ref, kinds_ref, bins_ref, places_ref, tables_ref = rest[:5]
    members_turned_ref, kinds_turned_ref = rest[5:7]
    grad_query_ref = rest[7]
    grad_pair_refs = rest[8 : 8 + count]
    grad_table_ref = rest[8 + count]
    query_wide, grad_wide, query_turned, grad_turned = rest[9 + count : 13 + count]
    all_scores, slopes_low, probs_low = rest[13 + count :]
    pair = pl.program_id(1) + first_pair
    rows, length, padded = layout.block_rows, layout.length, layout.padded
    factor = scale * LOG2E
    lane = lax.broadcasted_iota(jnp.int32, (1, LANES), 1)
    keys = jnp.concatenate([ref[...] for ref in key_refs], axis=0)
    values = jnp.concatenate([ref[...] for ref in value_refs], axis=0)
    members = members_ref[...]
    kinds = kinds_ref[...]
    tables = tables_ref[...]
    query = query_ref[...]
    grad = grad_ref[...]
    grad_full = grad.astype(jnp.float32)
    product = grad_full * out_ref[...]
    log_all = log_ref[...]
    tail = 2 * layout.groups
    ones = jnp.broadcast_to(jnp.where(lane < 3, 1.0, 0.0), (length, LANES)).astype(jnp.bfloat16)

    def three_parts(values):
        upper = values.astype(jnp.bfloat16).astype(jnp.float32)
        values = values - upper
        middle = values.astype(jnp.bfloat16).astype(jnp.float32)
        return upper, middle, values - middle

    def in_lanes(parts, first):
        return jnp.where(
            lane == first,
            parts[0],
            jnp.where(lane == first + 1, parts[1], jnp.where(lane == first + 2, parts[2], 0.0)),
        )

    if padded > rows:
        for ref in (query_wide, grad_wide):
            for side in range(2):
                ref[side, rows:padded] = jnp.zeros((padded - rows, ref.shape[2]), jnp.bfloat16)
        for ref in (query_turned, grad_turned):
            ref[:, rows:padded] = jnp.zeros((LANES, padded - rows), jnp.bfloat16)
    query_turned[:, 0:rows] = query.T
    grad_turned[:, 0:rows] = grad.T
    for side in range(2):
        log_total = jnp.sum(
            jnp.where(lane == 2 * pair + side, log_all, 0.0), axis=1, keepdims=True
        )
        extra = group_columns(kinds, tables, side) + in_lanes(three_parts(log_total), tail)
        query_wide[side, 0:rows, 0:LANES] = query
        query_wide[side, 0:rows, LANES:] = extra.astype(jnp.bfloat16)
        delta = jnp.sum(half_of(product, lane, side), axis=1, keepdims=True)
        grad_wide[side, 0:rows, 0:LANES] = grad
        grad_wide[side, 0:rows, LANES:] = in_lanes(three_parts(-delta), 0).astype(jnp.bfloat16)

    key_columns = [
        jnp.concatenate([half_of(keys, lane, side), members], axis=1) for side in range(2)
    ]
    value_columns = [
        jnp.concatenate([half_of(values, lane, side), ones], axis=1) for side in range(2)
    ]
    inner_sums = [jnp.zeros((1, LANES), jnp.float32) for _ in range(2)]
    low_sums = [jnp.zeros((1, LANES), jnp.float32) for _ in range(2)]
    high_sums = [jnp.zeros((1, LANES), jnp.float32) for _ in range(2)]
    reach_tiles = list(range(layout.query_tiles)) + [-1]

    def put(which, start, stop, result):
        begin = 0
        for ref, size in zip(grad_pair_refs, layout.pieces):
            low, high = max(start, begin), min(stop, begin + size)
            if low < high:
                ref[which, low - begin : high - begin] = result[low - start : high - start]
            begin += size

    for start, stop in row_blocks(length, KEY_BLOCK):
        size = stop - start
        for side in range(2):
            table_row = tables[8 * side : 8 * side + 1]
            scores = all_scores.at[side]
            scores[0:size] = wide_dot(key_columns[side][start:stop], query_wide[side], NT)
            near = []
            for index, tile in enumerate(reach_tiles):
                place = layout.tile_start(tile)
                if start <= place < stop:
                    near.append((index, tile, place, min(place + LANES, length)))
            for index, tile, place, final in near:
                for slot in range(3):
                    other = tile + slot - 1
                    if not 0 <= other < layout.query_tiles:
                        continue
                    bins = bins_ref[
                        index * LANES : index * LANES + final - place,
                        slot * LANES : (slot + 1) * LANES,
                    ]
                    scores[
                        place - start : final - start, other * LANES : (other + 1) * LANES
                    ] += look_up(table_row, bins)
            probs = jnp.exp2(scores[0:size] * factor).astype(jnp.bfloat16)
            grad_probs = wide_dot(value_columns[side][start:stop], grad_wide[side], NT)
            probs_low[side, start:stop] = probs
            slopes_low[side, start:stop] = probs * grad_probs.astype(jnp.bfloat16)
            for index, tile, place, final in near:
                for slot in range(3):
                    other = tile + slot - 1
                    if not 0 <= other < layout.query_tiles:
                        continue
                    bins = bins_ref[
                        index * LANES : index * LANES + final - place,
                        slot * LANES : (slot + 1) * LANES,
                    ]
                    cut = slopes_low[side, place:final, other * LANES : (other + 1) * LANES].astype(
                        jnp.float32
                    )
                    low_sums[side] += jnp.sum(
                        jnp.where(bins == 0, cut, 0.0), axis=0, keepdims=True
                    )
                    high_sums[side] += jnp.sum(
                        jnp.where(bins == 2 * (NEAR + 1), cut, 0.0), axis=0, keepdims=True
                    )
                for half in range(2):
                    begin, end = half * 64, min(half * 64 + 64, final - place)
                    if begin >= end:
                        continue
                    base = 0 if tile < 0 else tile - 1 + half
                    where = places_ref[index * LANES + begin : index * LANES + end]
                    spot = where & (LANES - 1)
                    for step in range(2):
                        other = base + step
                        if not 0 <= other < layout.query_tiles or (tile < 0 and step):
                            continue
                        cut = slopes_low[
                            side, place + begin : place + end, other * LANES : (other + 1) * LANES
                        ].astype(jnp.float32)
                        picked = jnp.take_along_axis(cut, spot, axis=1, mode="promise_in_bounds")
                        picked = jnp.where((where >> 7) == step, picked, 0.0)
                        inner_sums[side] += jnp.sum(picked, axis=0, keepdims=True)

    keys_turned = keys.T
    grad_keys, grad_values, grad_queries = [], [], []
    kinds_turned = kinds_turned_ref[...]
    for side in range(2):
        cut = slice(64 * side, 64 * side + 64)
        grad_values.append(wide_dot(grad_turned[cut], probs_low[side], NT))
        grad_keys.append(wide_dot(query_turned[cut], slopes_low[side], NT))
        left = jnp.concatenate([keys_turned[cut], members_turned_ref[...]], axis=0)
        both = wide_dot(left, slopes_low[side])
        grad_queries.append(both[:64])
        sums = both[64:]

        def total(kind):
            return jnp.sum(jnp.where(kinds_turned == kind, sums, 0.0))

        right = total(RIGHT) + jnp.sum(high_sums[side])
        left = total(LEFT) + jnp.sum(low_sums[side])
        apart = total(APART)
        grad_table_ref[side : side + 1] = jnp.where(
            lane == 0,
            left,
            jnp.where(
                lane == 2 * (NEAR + 1),
                right,
                jnp.where(lane == 2 * (NEAR + 1) + 1, apart, inner_sums[side]),
            ),
        )
    put(0, 0, length, (jnp.concatenate(grad_keys, axis=0) * scale).T.astype(jnp.bfloat16))
    put(1, 0, length, jnp.concatenate(grad_values, axis=0).T.astype(jnp.bfloat16))
    turned = jnp.concatenate(grad_queries, axis=0) * scale
    grad_query_ref[...] = turned.T[0:rows].astype(jnp.bfloat16)


def tile_columns(rows, offset=0):
    return pl.BlockSpec((None, rows, LANES), lambda crop, pair: (crop, 0, pair + offset))


def per_crop(rows, width):
    return pl.BlockSpec((None, rows, width), lambda crop, pair: (crop, 0, 0))


def kernel_params():
    return pltpu.CompilerParams(
        vmem_limit_bytes=VMEM_BYTES, dimension_semantics=("arbitrary", "arbitrary")
    )


def attention_forward(layout, scale, normed, weight, key_values, members, kinds, bins, tables):
    crops, rows, width = normed.shape
    pairs = tables.shape[0]
    specs = [per_crop(rows, width), pl.BlockSpec((width, LANES), lambda crop, pair: (0, pair))]
    operands = [normed, weight]
    for place in (1, 2):
        for piece in key_values:
            specs.append(tile_columns(piece[0].shape[1], piece[place]))
            operands.append(piece[0])
    specs += [
        per_crop(layout.length, LANES),
        per_crop(rows, LANES),
        per_crop(layout.padded, 3 * LANES),
        pl.BlockSpec((None, 16, LANES), lambda crop, pair: (pair, 0, 0)),
    ]
    flops = 2 * crops * pairs * 2 * rows * layout.length * 256 * 2
    return pl.pallas_call(
        functools.partial(forward_kernel, layout, scale),
        grid=(crops, pairs),
        in_specs=specs,
        out_specs=(tile_columns(rows), tile_columns(rows), per_crop(rows, LANES)),
        out_shape=(
            jax.ShapeDtypeStruct((crops, rows, pairs * LANES), jnp.bfloat16),
            jax.ShapeDtypeStruct((crops, rows, pairs * LANES), jnp.float32),
            jax.ShapeDtypeStruct((crops, rows, LANES), jnp.float32),
        ),
        scratch_shapes=[pltpu.VMEM((2, QUERY_BLOCK, layout.wide), jnp.float32)],
        compiler_params=kernel_params(),
        cost_estimate=pl.CostEstimate(
            flops=flops,
            bytes_accessed=12 * crops * rows * pairs * LANES,
            transcendentals=crops * pairs * 2 * rows * layout.length,
        ),
        name="attention_forward",
    )(*operands, members, kinds, bins, tables)


def attention_backward(
    layout,
    scale,
    first_pair,
    pairs,
    projected,
    grad_out,
    attended,
    logs,
    key_values,
    members,
    kinds,
    bins,
    places,
    members_turned,
    kinds_turned,
    tables,
):
    crops, rows, _ = projected.shape
    specs = [tile_columns(rows, first_pair)] * 3 + [per_crop(rows, LANES)]
    operands = [projected, grad_out, attended, logs]
    for place in (1, 2):
        for piece in key_values:
            specs.append(tile_columns(piece[0].shape[1], piece[place] + first_pair))
            operands.append(piece[0])
    specs += [
        per_crop(layout.length, LANES),
        per_crop(rows, LANES),
        per_crop(bins.shape[1], 3 * LANES),
        per_crop(places.shape[1], LANES),
        pl.BlockSpec((None, 16, LANES), lambda crop, pair: (pair + first_pair, 0, 0)),
        per_crop(64, layout.length),
        per_crop(64, layout.padded),
    ]
    out_specs = [tile_columns(rows)]
    out_shapes = [jax.ShapeDtypeStruct((crops, rows, pairs * LANES), jnp.bfloat16)]
    for piece in key_values:
        size = piece[0].shape[1]
        out_specs.append(
            pl.BlockSpec((None, 2, size, LANES), lambda crop, pair: (crop, 0, 0, pair))
        )
        out_shapes.append(jax.ShapeDtypeStruct((crops, 2, size, pairs * LANES), jnp.bfloat16))
    out_specs.append(pl.BlockSpec((None, None, 8, LANES), lambda crop, pair: (crop, pair, 0, 0)))
    out_shapes.append(jax.ShapeDtypeStruct((crops, pairs, 8, LANES), jnp.float32))
    padded = layout.padded
    return pl.pallas_call(
        functools.partial(backward_kernel, layout, scale, first_pair),
        grid=(crops, pairs),
        in_specs=specs,
        out_specs=tuple(out_specs),
        out_shape=tuple(out_shapes),
        scratch_shapes=[
            pltpu.VMEM((2, padded, 2 * LANES), jnp.bfloat16),
            pltpu.VMEM((2, padded, 2 * LANES), jnp.bfloat16),
            pltpu.VMEM((LANES, padded), jnp.bfloat16),
            pltpu.VMEM((LANES, padded), jnp.bfloat16),
            pltpu.VMEM((2, KEY_BLOCK, padded), jnp.float32),
            pltpu.VMEM((2, layout.length, padded), jnp.bfloat16),
            pltpu.VMEM((2, layout.length, padded), jnp.bfloat16),
        ],
        compiler_params=kernel_params(),
        cost_estimate=pl.CostEstimate(
            flops=2 * crops * pairs * 2 * rows * layout.length * 256 * 5,
            bytes_accessed=20 * crops * rows * pairs * LANES,
            transcendentals=crops * pairs * 2 * rows * layout.length,
        ),
        name="attention_backward",
    )(*operands, members, kinds, bins, places, tables, members_turned, kinds_turned)


def sigmoid(values):
    return 0.5 * jnp.tanh(0.5 * values) + 0.5


def each_strip(rows, body, size=16):
    count = rows // size
    group = max(number for number in range(1, 9) if count % number == 0)

    @pl.loop(0, count // group)
    def _(index):
        for part in range(group):
            body(pl.ds(pl.multiple_of((index * group + part) * size, size), size))


def fold_rows(values):
    return jnp.sum(values.reshape(values.shape[0] // 8, 8, values.shape[1]), axis=0)


def feed_kernel(split, chunks, here_ref, *refs):
    (attended_ref, tokens_ref, upstream_ref, normed_a_ref, mod_ref, gate_weight_ref, output_ref) = refs[:7]
    gate_ref, up_ref, down_ref = refs[7:10]
    layer_ref, grad_middle_ref, grad_att_ref, grad_pre_ref, sums_ref = refs[10:15]
    grads = refs[15:-12]
    gated, grad_ff, normed, branch, middle, total, grad_normed, hidden, both, grad_branch = refs[-12:-2]
    gate_pre, turned = refs[-2:]
    step = pl.program_id(0)
    here = here_ref[0]
    rows, width = tokens_ref.shape
    size = gate_ref.shape[1]
    strip = 112 if rows % 112 == 0 else 64
    strips = rows // strip
    shift_f, scale_f = mod_ref[3:4], mod_ref[4:5]
    open_a, open_f = sigmoid(mod_ref[2:3]), sigmoid(mod_ref[5:6])

    def strip_of(index):
        return pl.ds(pl.multiple_of(index * strip, strip), strip)

    def norm_of(values):
        mean_value = jnp.mean(values, axis=1, keepdims=True)
        centred = values - mean_value
        spread = jnp.mean(centred * centred, axis=1, keepdims=True)
        root = lax.rsqrt(spread + 1e-06)
        return centred * root, root

    @pl.when(step == 0)
    def _():
        gate_pre[...] = wide_dot(normed_a_ref[...], gate_weight_ref[...])

        @pl.loop(0, strips)
        def _(index):
            cut = strip_of(index)
            gated[cut] = (attended_ref[cut] * sigmoid(gate_pre[cut])).astype(jnp.bfloat16)
            grad_ff[cut] = (upstream_ref[cut].astype(jnp.float32) * open_f).astype(jnp.bfloat16)

        branch[...] = wide_dot(gated[...], output_ref[...])

        @pl.loop(0, strips)
        def _(index):
            cut = strip_of(index)
            values = tokens_ref[cut].astype(jnp.float32) + open_a * branch[cut]
            middle[cut] = values
            normed[cut] = (norm_of(values)[0] * (1.0 + scale_f) + shift_f).astype(jnp.bfloat16)
            total[cut] = jnp.zeros((strip, width), jnp.float32)
            grad_normed[cut] = jnp.zeros((strip, width), jnp.float32)

        turned[...] = normed[...].T

    block = rows
    for start in range(0, rows, block):
        cut = slice(start, start + block)
        before = wide_dot(normed[cut], gate_ref[...])
        lifted = wide_dot(normed[cut], up_ref[...])
        grad_hidden = wide_dot(grad_ff[cut], down_ref[...], NT)
        switch = sigmoid(before)
        silu = before * switch
        part = (silu * lifted).astype(jnp.bfloat16)
        hidden[cut] = part
        grad_up = (grad_hidden * silu).astype(jnp.bfloat16)
        grad_gate = (grad_hidden * lifted * (switch + silu * (1.0 - switch))).astype(jnp.bfloat16)
        both[cut, :size] = grad_gate
        both[cut, size:] = grad_up
        total[cut] += wide_dot(part, down_ref[...])
        grad_normed[cut] += wide_dot(grad_gate, gate_ref[...], NT) + wide_dot(
            grad_up, up_ref[...], NT
        )

    pair = wide_dot(turned[...], both[...]).astype(jnp.bfloat16)
    if split:
        gate_send, gate_keep, up_send, up_keep, down_send, down_keep, small_send, small_keep = grads
        half = width // 2
        away = pl.ds(pl.multiple_of((1 - here) * half, LANES), half)
        home = pl.ds(pl.multiple_of(here * half, LANES), half)
        down_send[...] = wide_dot(hidden[...], grad_ff[:, away], TN).astype(jnp.bfloat16)
        down_keep[...] = wide_dot(hidden[...], grad_ff[:, home], TN).astype(jnp.bfloat16)

        @pl.when(step < chunks // 2)
        def _():
            gate_send[...] = pair[:, :size]
            up_send[...] = pair[:, size:]

        @pl.when(step >= chunks // 2)
        def _():
            gate_keep[...] = pair[:, :size]
            up_keep[...] = pair[:, size:]
    else:
        gate_all, up_all, down_all, small_all = grads
        gate_all[...] = pair[:, :size]
        up_all[...] = pair[:, size:]
        down_all[...] = wide_dot(hidden[...], grad_ff[...], TN).astype(jnp.bfloat16)

    @pl.when(step == chunks - 1)
    def _():
        def finish(index, sums):
            gate_f_sum, shift_sum, scale_sum, gate_a_sum = sums
            cut = strip_of(index)
            values = middle[cut]
            fed = total[cut]
            upstream = upstream_ref[cut].astype(jnp.float32)
            layer_ref[cut] = (values + open_f * fed).astype(jnp.bfloat16)
            normal, root = norm_of(values)
            grad = grad_normed[cut]
            scaled = grad * (1.0 + scale_f)
            grad_middle = upstream + root * (
                scaled
                - jnp.mean(scaled, axis=1, keepdims=True)
                - normal * jnp.mean(scaled * normal, axis=1, keepdims=True)
            )
            grad_middle_ref[cut] = grad_middle
            grad_branch[cut] = (grad_middle * open_a).astype(jnp.bfloat16)
            return (
                gate_f_sum + fold_rows(upstream * fed),
                shift_sum + fold_rows(grad),
                scale_sum + fold_rows(grad * normal),
                gate_a_sum + fold_rows(grad_middle * branch[cut]),
            )

        zero = jnp.zeros((8, width), jnp.float32)
        sums = lax.fori_loop(0, strips, finish, (zero, zero, zero, zero))
        gate_f_sum, shift_sum, scale_sum, gate_a_sum = [
            jnp.sum(value, axis=0, keepdims=True) for value in sums
        ]
        none = jnp.zeros((1, width), jnp.float32)
        sums_ref[...] = jnp.concatenate(
            [
                none,
                none,
                gate_a_sum * open_a * (1.0 - open_a),
                shift_sum,
                scale_sum,
                gate_f_sum * open_f * (1.0 - open_f),
                none,
                none,
            ],
            axis=0,
        )
        total[...] = wide_dot(grad_branch[...], output_ref[...], NT)

        @pl.loop(0, strips)
        def _(index):
            cut = strip_of(index)
            grad_gated = total[cut]
            opened = sigmoid(gate_pre[cut])
            grad_att_ref[cut] = (grad_gated * opened).astype(jnp.bfloat16)
            grad_pre_ref[cut] = (
                grad_gated * attended_ref[cut] * (opened * (1.0 - opened))
            ).astype(jnp.bfloat16)

        if split:
            for side, ref in ((away, small_send), (home, small_keep)):
                ref[:, :half] = wide_dot(gated[...], grad_branch[:, side], TN).astype(jnp.bfloat16)
                ref[:, half:] = wide_dot(normed_a_ref[...], grad_pre_ref[:, side], TN).astype(
                    jnp.bfloat16
                )
        else:
            small_all[:, :width] = wide_dot(gated[...], grad_branch[...], TN).astype(jnp.bfloat16)
            small_all[:, width:] = wide_dot(normed_a_ref[...], grad_pre_ref[...], TN).astype(
                jnp.bfloat16
            )


def feed_layer(
    split, here, attended, tokens, upstream, normed_a, mod_rows, gate_weight, output_weight, feed_gate, feed_up, feed_down
):
    rows, width = tokens.shape
    inner = feed_gate.shape[1]
    size = 512
    chunks = inner // size
    half = chunks // 2

    def turn(step, here_ref):
        return (step + half * (1 - here_ref[0])) % chunks if split else step

    def fixed(shape):
        return pl.BlockSpec(shape, lambda step, here_ref: (0, 0), pipeline_mode=pl.Buffered(1))

    def columns(step, here_ref):
        return (0, turn(step, here_ref))

    def strips(step, here_ref):
        return (turn(step, here_ref), 0)

    whole = (rows, width)
    in_specs = [fixed(whole)] * 4 + [
        fixed((8, width)),
        fixed((width, width)),
        fixed((width, width)),
        pl.BlockSpec((width, size), columns),
        pl.BlockSpec((width, size), columns),
        pl.BlockSpec((size, width), strips),
    ]
    out_specs = [fixed(whole)] * 4 + [fixed((8, width))]
    bf16, f32 = jnp.bfloat16, jnp.float32
    out_shapes = [(whole, bf16), (whole, f32), (whole, bf16), (whole, bf16), ((8, width), f32)]
    if split:
        first = pl.BlockSpec((width, size), lambda step, here_ref: (0, jnp.minimum(step, half - 1)))
        second = pl.BlockSpec((width, size), lambda step, here_ref: (0, jnp.maximum(step - half, 0)))
        out_specs += [first, second, first, second]
        out_shapes += [((width, inner // 2), bf16)] * 4
        out_specs += [pl.BlockSpec((size, width // 2), strips)] * 2
        out_shapes += [((inner, width // 2), bf16)] * 2
        out_specs += [fixed((width, width))] * 2
        out_shapes += [((width, width), bf16)] * 2
    else:
        out_specs += [pl.BlockSpec((width, size), columns)] * 2
        out_shapes += [((width, inner), bf16)] * 2
        out_specs += [pl.BlockSpec((size, width), strips), fixed((width, 2 * width))]
        out_shapes += [((inner, width), bf16), ((width, 2 * width), bf16)]
    return pl.pallas_call(
        functools.partial(feed_kernel, split, chunks),
        grid_spec=pltpu.PrefetchScalarGridSpec(
            num_scalar_prefetch=1,
            grid=(chunks,),
            in_specs=in_specs,
            out_specs=tuple(out_specs),
            scratch_shapes=[
                pltpu.VMEM(whole, bf16),
                pltpu.VMEM(whole, bf16),
                pltpu.VMEM(whole, bf16),
                pltpu.VMEM(whole, f32),
                pltpu.VMEM(whole, f32),
                pltpu.VMEM(whole, f32),
                pltpu.VMEM(whole, f32),
                pltpu.VMEM((rows, size), bf16),
                pltpu.VMEM((rows, 2 * size), bf16),
                pltpu.VMEM(whole, bf16),
                pltpu.VMEM(whole, f32),
                pltpu.VMEM((width, rows), bf16),
            ],
        ),
        out_shape=tuple(jax.ShapeDtypeStruct(shape, kind) for shape, kind in out_shapes),
        compiler_params=pltpu.CompilerParams(vmem_limit_bytes=VMEM_BYTES),
        cost_estimate=pl.CostEstimate(
            flops=2 * rows * width * (9 * inner + 5 * width),
            bytes_accessed=12 * width * inner + 24 * rows * width,
            transcendentals=2 * rows * inner,
        ),
        name="feed_layer",
    )(
        jnp.reshape(here, (1,)).astype(jnp.int32),
        attended,
        tokens,
        upstream,
        normed_a,
        mod_rows,
        gate_weight,
        output_weight,
        feed_gate,
        feed_up,
        feed_down,
    )


MASKS = {"u": 8, "v": 4, "y": 2, "x": 1}


def exchange(values, mask):
    return lax.ppermute(values, "crop", [(i, i ^ mask) for i in range(16)])


def swap_res(values):
    return lax.ppermute(values, "res", [(0, 1), (1, 0)])


def tie(*values):
    return lax.optimization_barrier(values)


def add_low(former, latter, kind=jnp.bfloat16):
    return (former.astype(jnp.float32) + latter.astype(jnp.float32)).astype(kind)


def stage_kernel(plans, bits_ref, *refs):
    inputs = refs[: sum(plan["count"] for plan in plans)]
    outputs = list(refs[len(inputs) :])
    for plan in plans:
        mine, inputs = inputs[: plan["count"]], inputs[plan["count"] :]
        out_ref = None if plan["apart"] else outputs[0]
        if not plan["apart"] and plan["merge"] is None:
            outputs.pop(0)
        for column, width, own in plan["parts"]:
            result = outputs.pop(0) if plan["apart"] else out_ref
            target = 0 if plan["apart"] else column
            lead_sizes = () if plan["merge"] is not None else result.shape[:-2]
            for lead in itertools.product(*[range(size) for size in lead_sizes]):
                for first in range(0, plan["rows"], 16):
                    cut = (*lead, slice(first, first + 16))
                    across = slice(column, column + width)
                    total = None
                    for index in own:
                        value = mine[index][(*cut, slice(0, width))].astype(jnp.float32)
                        total = value if total is None else total + value
                    for index in plan["spans"]:
                        total = total + mine[index][(*cut, across)].astype(jnp.float32)
                    fold, local = first // plan["block"], first % plan["block"]
                    if plan["folds"]:
                        value = mine[plan["folds"][fold]][local : local + 16, across]
                        total = total + value.astype(jnp.float32)
                    if plan["merge"] is None:
                        result[(*cut, slice(target, target + width))] = total.astype(result.dtype)
                    else:
                        begin = plan["merge"] + fold * plan["wide"] + column
                        result[local : local + 16, begin : begin + width] = total.astype(result.dtype)


class Halving:
    def __init__(self, streams, orders):
        self.streams = streams
        self.orders = [list(order) for order in orders]
        self.past = [[] for _ in orders]
        self.came = [[] for _ in orders]

    def stage(self, last=False, merge=False, merged=None):
        index = lax.axis_index("crop")
        bits = scalars(*[(index // mask) % 2 for mask in MASKS.values()])
        self.masks, plans, specs, operands, out_specs, out_shapes = [], [], [], [], [], []
        left = 0 if last else len(self.orders[0]) - 1
        fewest = min(parts[0][0][0].shape[0] for parts in self.streams) // 16
        begin = 0
        steps = {3: 4, 2: 2}.get(left, 1)
        for stream, (parts, order, past) in enumerate(zip(self.streams, self.orders, self.past)):
            now = None if last else order.pop(0)
            rest = [axis for axis in MASKS if axis in order]

            def spec_of(axes, rows, width, block, now=now, rest=rest):
                def index_map(step, bits_ref):
                    places = []
                    for axis in axes:
                        bit = bits_ref[list(MASKS).index(axis)]
                        if axis == now:
                            places.append(1 - bit)
                        elif axis not in rest:
                            places.append(bit)
                        elif axis == rest[0] and steps > 1:
                            places.append(step // (steps // 2))
                        elif len(rest) > 1 and axis == rest[1] and steps > 2:
                            places.append(step % 2)
                        else:
                            places.append(0)
                    return (*places, 0, block)

                sizes = [
                    2
                    if axis in rest
                    and not (axis == rest[0] and steps > 1)
                    and not (len(rest) > 1 and axis == rest[1] and steps > 2)
                    else None
                    for axis in axes
                ]
                return pl.BlockSpec((*sizes, rows, width), index_map)

            column = 0
            rows = parts[0][0][0].shape[0] // 16
            wide = sum(width for _, _, width in parts)
            plan = {
                "parts": [],
                "spans": [],
                "folds": [],
                "count": 0,
                "apart": last,
                "rows": rows,
                "block": fewest,
                "wide": wide,
                "merge": begin if merge else None,
            }
            for arrays, block, width in parts:
                own = []
                for value in arrays:
                    operands.append(value.reshape(2, 2, 2, 2, rows, value.shape[1]))
                    specs.append(spec_of(list(MASKS), rows, width, block))
                    own.append(plan["count"])
                    plan["count"] += 1
                plan["parts"].append((column, width, own))
                column += width
            for axes, value in self.came[stream]:
                operands.append(value.reshape(*[2] * len(axes), rows, column))
                specs.append(spec_of(axes, rows, column, 0))
                plan["spans"].append(plan["count"])
                plan["count"] += 1
            if merged is not None:
                for fold in range(rows // fewest):
                    place = (begin + fold * wide) // wide
                    operands.append(merged)
                    specs.append(
                        pl.BlockSpec((fewest, wide), lambda step, bits_ref, place=place: (0, place))
                    )
                    plan["folds"].append(plan["count"])
                    plan["count"] += 1
            begin += wide * (rows // fewest)
            plans.append(plan)
            if last:
                for _, width, _ in plan["parts"]:
                    out_specs.append(pl.BlockSpec((rows, width), lambda step, bits_ref: (0, 0)))
                    out_shapes.append(jax.ShapeDtypeStruct((rows, width), jnp.float32))
            else:
                past.append(now)
                self.masks.append(MASKS[now])
                if not merge:
                    out_specs.append(spec_of(rest, rows, column, 0))
                    out_shapes.append(
                        jax.ShapeDtypeStruct((*[2] * len(rest), rows, column), jnp.bfloat16)
                    )
        if merge:
            out_specs.append(pl.BlockSpec((fewest, begin), lambda step, bits_ref: (0, 0)))
            out_shapes.append(jax.ShapeDtypeStruct((fewest, begin), jnp.bfloat16))
        self.axes = [[axis for axis in MASKS if axis in order] for order in self.orders]
        results = pl.pallas_call(
            functools.partial(stage_kernel, plans),
            grid_spec=pltpu.PrefetchScalarGridSpec(
                num_scalar_prefetch=1, grid=(steps,), in_specs=specs, out_specs=tuple(out_specs)
            ),
            out_shape=tuple(out_shapes),
            compiler_params=pltpu.CompilerParams(vmem_limit_bytes=VMEM_BYTES),
            cost_estimate=pl.CostEstimate(
                flops=sum(4 * math.prod(shape.shape) for shape in out_shapes),
                bytes_accessed=sum(8 * math.prod(shape.shape) for shape in out_shapes),
                transcendentals=0,
            ),
            name="halving_stage",
        )(bits, *operands)
        if merge or last:
            return list(results)
        return [value.reshape(-1, value.shape[-1]) for value in results]

    def send(self, values):
        return [exchange(value, mask) for value, mask in zip(values, self.masks)]

    def take(self, values):
        for came, axes, value in zip(self.came, self.axes, values):
            came.append((axes, value))


def share_columns(values, parts):
    if parts == 1:
        return values.astype(jnp.bfloat16)
    return lax.psum_scatter(values.astype(jnp.bfloat16), "res", scatter_dimension=1, tiled=True)


def scatter_crops(values):
    return lax.psum_scatter(values, "crop", scatter_dimension=0, tiled=True).astype(jnp.float32)


def gather_crops(values, crop_parts):
    if crop_parts != 16:
        return lax.all_gather(values, "crop", axis=0, tiled=True)
    index = lax.axis_index("crop")
    for mask in (1, 2, 4, 8):
        other = exchange(values, mask)
        low = (index // mask) % 2 == 0
        values = jnp.concatenate(
            [jnp.where(low, values, other), jnp.where(low, other, values)], axis=0
        )
    return values


def sum_res(values, parts):
    if parts == 1:
        return values
    if parts != 2:
        return lax.psum(values, "res")
    return values + swap_res(values)


PACK = 1152
SIDE = 384


def whole_vmem(count):
    return [pl.BlockSpec(memory_space=pltpu.VMEM)] * count


def scalars(*values):
    return jnp.stack([jnp.asarray(value, jnp.int32) for value in values])


def local_call(kernel, numbers, operands, shapes, name, flops=0):
    return pl.pallas_call(
        kernel,
        in_specs=[pl.BlockSpec(memory_space=pltpu.SMEM)] + whole_vmem(len(operands)),
        out_specs=tuple(whole_vmem(len(shapes))),
        out_shape=tuple(jax.ShapeDtypeStruct(shape, kind) for shape, kind in shapes),
        compiler_params=pltpu.CompilerParams(vmem_limit_bytes=VMEM_BYTES),
        cost_estimate=pl.CostEstimate(
            flops=flops,
            bytes_accessed=sum(value.size * value.dtype.itemsize for value in operands)
            + sum(4 * math.prod(shape) for shape, _ in shapes),
            transcendentals=0,
        ),
        name=name,
    )(numbers, *operands)


def projection_kernel(counts, here_ref, normed_ref, *refs):
    calls = len(counts)
    parts, (joined_ref, send_ref, keep_ref) = refs[: 3 * calls], refs[3 * calls :]
    width = joined_ref.shape[1] // 3
    column = 0
    for call, pairs in enumerate(counts):
        size = pairs * LANES
        query_ref, own_ref, came_ref = parts[3 * call : 3 * call + 3]
        joined_ref[:, column : column + size] = query_ref[...]
        for start in range(0, joined_ref.shape[0], 16):
            cut = slice(start, start + 16)
            for which in range(2):
                first = (1 + which) * width + column
                joined_ref[cut, first : first + size] = add_low(
                    own_ref[which, cut], came_ref[which, cut]
                )
        column += size
    half = send_ref.shape[1]
    for side, ref in ((1 - here_ref[0], send_ref), (here_ref[0], keep_ref)):
        columns = pl.ds(pl.multiple_of(side * half, LANES), half)
        ref[...] = wide_dot(normed_ref[...], joined_ref[:, columns], TN).astype(jnp.bfloat16)


def projection_gradient(here, normed_a, calls):
    rows, width = normed_a.shape
    counts = [call[0].shape[-1] // LANES for call in calls]
    return local_call(
        functools.partial(projection_kernel, counts),
        scalars(here),
        [normed_a] + [value for call in calls for value in call],
        [
            ((rows, 3 * width), jnp.bfloat16),
            ((width, 3 * width // 2), jnp.bfloat16),
            ((width, 3 * width // 2), jnp.bfloat16),
        ],
        "projection_gradient",
        6 * rows * width * width,
    )


def finish_kernel(counts, joined_ref, weight_ref, pre_ref, gate_ref, tokens_ref, middle_ref, mod_ref, *refs):
    feed_sums_ref, extra_ref = refs[:2]
    table_refs = refs[2 : 2 + len(counts)]
    out_ref, pack_ref, total, folded = refs[2 + len(counts) :]
    step = pl.program_id(0)
    rows, width = tokens_ref.shape
    part = wide_dot(joined_ref[...], weight_ref[...], NT)

    @pl.when(step == 0)
    def _():
        total[...] = part + wide_dot(pre_ref[...], gate_ref[...], NT)

    @pl.when(step > 0)
    def _():
        total[...] += part

    @pl.when(step == pl.num_programs(0) - 1)
    def _():
        scale = mod_ref[1:2]
        folded[...] = jnp.zeros_like(folded)

        def finish(cut):
            values = tokens_ref[cut].astype(jnp.float32)
            centred = values - jnp.mean(values, axis=1, keepdims=True)
            root = lax.rsqrt(jnp.mean(centred * centred, axis=1, keepdims=True) + 1e-06)
            normal = centred * root
            grad = total[cut]
            folded[0] += fold_rows(grad)
            folded[1] += fold_rows(grad * normal)
            scaled = grad * (1.0 + scale)
            out_ref[cut] = (
                middle_ref[cut]
                + root
                * (
                    scaled
                    - jnp.mean(scaled, axis=1, keepdims=True)
                    - normal * jnp.mean(scaled * normal, axis=1, keepdims=True)
                )
            ).astype(jnp.bfloat16)

        each_strip(rows, finish)
        shift_sum, scale_sum = folded[0], folded[1]
        heads = []
        for ref, pairs in zip(table_refs, counts):
            for pair in range(pairs):
                heads += [ref[pair, 0:1], ref[pair, 1:2]]

        def upper_of(values):
            return values.astype(jnp.bfloat16).astype(jnp.float32)

        rests = [head - upper_of(head) for head in heads]
        count = width // LANES
        left = [
            jnp.sum(shift_sum, axis=0, keepdims=True),
            jnp.sum(scale_sum, axis=0, keepdims=True),
            feed_sums_ref[2:6],
        ]
        left += [
            jnp.concatenate(rests[i : i + count], axis=1) for i in range(0, len(heads), count)
        ]
        right = [jnp.concatenate(heads[3 * i : 3 * i + 3], axis=1) for i in range(4)]
        line = extra_ref[5:6]
        right += [extra_ref[4:5], line, line - upper_of(line), extra_ref[7:8]]
        pack = jnp.concatenate(
            [jnp.concatenate(left, axis=0), jnp.concatenate(right, axis=0)], axis=1
        )
        pack_ref[...] = jnp.concatenate([pack, jnp.zeros_like(pack)], axis=0).astype(jnp.bfloat16)


def finish_layer(
    joined, weight, grad_pre, gate_weight, tokens, grad_middle, mod_rows, feed_sums, extra, grad_tables
):
    rows, width = tokens.shape
    counts = [table.shape[0] for table in grad_tables]

    def fixed(shape):
        return pl.BlockSpec(shape, lambda step: (0,) * len(shape), pipeline_mode=pl.Buffered(1))

    return pl.pallas_call(
        functools.partial(finish_kernel, counts),
        grid=(3,),
        in_specs=[
            pl.BlockSpec((rows, width), lambda step: (0, step)),
            pl.BlockSpec((width, width), lambda step: (0, step)),
            fixed((rows, width)),
            fixed((width, width)),
            fixed((rows, width)),
            fixed((rows, width)),
            fixed((8, width)),
            fixed((8, width)),
            fixed((8, SIDE)),
        ]
        + [fixed((count, 8, LANES)) for count in counts],
        out_specs=(fixed((rows, width)), fixed((16, PACK))),
        out_shape=(
            jax.ShapeDtypeStruct((rows, width), jnp.bfloat16),
            jax.ShapeDtypeStruct((16, PACK), jnp.bfloat16),
        ),
        scratch_shapes=[
            pltpu.VMEM((rows, width), jnp.float32),
            pltpu.VMEM((2, 8, width), jnp.float32),
        ],
        compiler_params=pltpu.CompilerParams(vmem_limit_bytes=VMEM_BYTES),
        cost_estimate=pl.CostEstimate(
            flops=8 * rows * width * width, bytes_accessed=24 * rows * width, transcendentals=0
        ),
        name="finish_layer",
    )(
        joined,
        weight,
        grad_pre,
        gate_weight,
        tokens,
        grad_middle,
        mod_rows,
        feed_sums,
        extra,
        *grad_tables,
    )


def fan_first_kernel(bits_ref, keep_ref, came_ref, mine_ref, *send_refs):
    chunk = keep_ref.shape[0] // 16
    for other, ref in enumerate((mine_ref, *send_refs)):
        for level in range(4):
            start = (level * 4 + (bits_ref[0] ^ other)) * chunk
            for first in range(0, chunk, 16):
                cut = pl.ds(pl.multiple_of(start + first, 16), 16)
                place = level * chunk + first
                ref[place : place + 16] = add_low(keep_ref[cut], came_ref[cut])


def fan_v_kernel(bits_ref, mine_ref, *refs):
    came_refs, (send_ref, out_ref) = refs[:3], refs[3:]
    chunk = mine_ref.shape[0] // 4
    for side, ref in ((1 - bits_ref[0], send_ref), (bits_ref[0], out_ref)):
        for far in range(2):
            for first in range(0, chunk, 16):
                cut = pl.ds(pl.multiple_of((2 * far + side) * chunk + first, 16), 16)
                total = mine_ref[cut].astype(jnp.float32)
                for came_ref in came_refs:
                    total = total + came_ref[cut].astype(jnp.float32)
                place = far * chunk + first
                ref[place : place + 16] = total.astype(jnp.bfloat16)


def fan_u_kernel(bits_ref, mine_ref, came_ref, send_ref, out_ref):
    chunk = mine_ref.shape[0] // 2
    for side, ref in ((1 - bits_ref[0], send_ref), (bits_ref[0], out_ref)):
        for first in range(0, chunk, 16):
            cut = pl.ds(pl.multiple_of(side * chunk + first, 16), 16)
            ref[first : first + 16] = add_low(mine_ref[cut], came_ref[cut])


def join_packs_kernel(bits_ref, *refs):
    packs = [ref[...].astype(jnp.float32)[0:8] for ref in refs[:4]]
    refs[4][...] = jnp.concatenate(packs, axis=0).astype(jnp.bfloat16)


def small_kernel(
    heads,
    here_ref,
    mine_ref,
    came_ref,
    modulation_ref,
    pair_norm_ref,
    relative_ref,
    gain_ref,
    pair_weight_ref,
    mod_grad_ref,
    time_ref,
    label_ref,
    relative_grad_ref,
    gain_grad_ref,
    pair_grad_ref,
    grad_condition,
    grad_mod,
    kept,
):
    step = pl.program_id(0)
    crops = mine_ref.shape[0] // 8
    width = mine_ref.shape[1] - SIDE
    conds = relative_ref.shape[1]
    parts = mod_grad_ref.shape[1] // width

    def parts_split(values):
        upper = values.astype(jnp.bfloat16)
        return upper, (values - upper.astype(jnp.float32)).astype(jnp.bfloat16)

    def dot_left(narrow, values, numbers):
        upper, rest = parts_split(values)
        return wide_dot(narrow, upper, numbers) + wide_dot(narrow, rest, numbers)

    def dot_right(values, narrow, numbers):
        upper, rest = parts_split(values)
        return wide_dot(upper, narrow, numbers) + wide_dot(rest, narrow, numbers)

    def both_twice(narrow):
        return jnp.concatenate([narrow, narrow], axis=0)

    def stacked(values):
        return jnp.concatenate(parts_split(values), axis=0)

    @pl.when(step == 0)
    def _():
        shape = (8 * crops, 8 * crops)
        picked = lax.broadcasted_iota(jnp.int32, shape, 0)
        source = lax.broadcasted_iota(jnp.int32, shape, 1)
        hit = ((source >> 3) == (picked & (crops - 1))) & ((source & 7) == (picked // crops))
        select = jnp.where(hit, 1.0, 0.0).astype(jnp.bfloat16)
        mine = wide_dot(select, mine_ref[...])
        grad_mod[...] = mine[: 6 * crops, :width] + wide_dot(select, came_ref[...])[: 6 * crops, :width]
        condition = (
            mine[5 * crops : 6 * crops, width : width + conds]
            + mine[6 * crops : 7 * crops, width : width + conds]
        )
        gate_value = sigmoid(condition)
        kept[0] = condition * gate_value
        kept[1] = gate_value * (1.0 + condition * (1.0 - gate_value))
        kept[2] = mine[4 * crops : 5 * crops, width : width + conds]
        kept[3] = jnp.broadcast_to(
            mine[5 * crops : 6 * crops, width + conds : width + conds + 1]
            + mine[6 * crops : 7 * crops, width + conds : width + conds + 1],
            (crops, conds),
        )
        grad_condition[...] = jnp.zeros_like(grad_condition)

    cond_act = both_twice(kept[0].astype(jnp.bfloat16))
    for turn in range(parts):
        columns = slice(turn * width, (turn + 1) * width)
        first = pl.multiple_of((step * parts + turn) * crops, crops)
        pair = stacked(grad_mod[pl.ds(first, crops)])
        mod_grad_ref[:, columns] = wide_dot(cond_act, pair, TN)
        more = wide_dot(pair, modulation_ref[:, columns], NT)
        grad_condition[...] += more[:crops] + more[crops:]

    @pl.when(step == 0)
    def _():
        shape = (8, 8 * crops)
        line = lax.broadcasted_iota(jnp.int32, shape, 0)
        local = lax.broadcasted_iota(jnp.int32, shape, 1) & 7
        every = jnp.where(local == line, 1.0, 0.0).astype(jnp.bfloat16)
        lines = wide_dot(every, mine_ref[...]) + wide_dot(every, came_ref[...])

        def of_head(head):
            upper = width + (head % 3) * LANES
            rest = (head % (width // LANES)) * LANES
            low = 6 + head // (width // LANES)
            return (
                lines[head // 3 : head // 3 + 1, upper : upper + LANES]
                + lines[low : low + 1, rest : rest + LANES]
            )

        table = jnp.concatenate(
            [of_head(head) for head in range(heads)]
            + [jnp.zeros((16 - heads, LANES), jnp.float32)],
            axis=0,
        )
        bins = relative_ref.shape[0]
        pair_grad_ref[...] = dot_right(table, pair_norm_ref[...], (((1,), (0,)), ((), ())))[:heads]
        grad_norm = dot_right(table, pair_weight_ref[...], (((0,), (1,)), ((), ())))[:bins]
        values = relative_ref[...].astype(jnp.float32)
        centred = values - jnp.mean(values, axis=1, keepdims=True)
        root = lax.rsqrt(jnp.mean(centred * centred, axis=1, keepdims=True) + 1e-06)
        normal = centred * root
        gain_grad_ref[...] = jnp.sum(grad_norm * normal, axis=0, keepdims=True)
        scaled = grad_norm * gain_ref[...].astype(jnp.float32)
        relative_grad_ref[...] = root * (
            scaled
            - jnp.mean(scaled, axis=1, keepdims=True)
            - normal * jnp.mean(scaled * normal, axis=1, keepdims=True)
        )

    @pl.when(step == pl.num_programs(0) - 1)
    def _():
        final = stacked(grad_condition[...] * kept[1])
        time_ref[...] = wide_dot(both_twice(kept[2].astype(jnp.bfloat16)), final, TN)
        label = lax.broadcasted_iota(jnp.int32, (crops, label_ref.shape[0]), 1)
        number = kept[3][:, 0:1].astype(jnp.int32)
        onehot = jnp.where(label == number, 1.0, 0.0).astype(jnp.bfloat16)
        label_ref[...] = wide_dot(both_twice(onehot), final, TN)


def small_gradients(heads, labels, mine, came, modulation_weight, pair_norm, relative, gain, pair_weight):
    conds, wide = modulation_weight.shape
    bins = relative.shape[0]
    rows = mine.shape[0]
    steps = 3

    def fixed(shape):
        return pl.BlockSpec(shape, lambda step: (0, 0))

    shapes = [(conds, wide), (conds, conds), (labels, conds), (bins, conds), (1, conds), (heads, conds)]
    return pl.pallas_call(
        functools.partial(small_kernel, heads),
        grid=(steps,),
        in_specs=[
            pl.BlockSpec(memory_space=pltpu.SMEM),
            fixed((rows, PACK)),
            fixed((rows, PACK)),
            pl.BlockSpec((conds, wide // steps), lambda step: (0, step)),
            fixed((LANES, conds)),
            fixed((bins, conds)),
            fixed((1, conds)),
            fixed((conds, 16)),
        ],
        out_specs=tuple(
            [pl.BlockSpec((conds, wide // steps), lambda step: (0, step))]
            + [fixed(s) for s in shapes[1:]]
        ),
        out_shape=tuple(jax.ShapeDtypeStruct(shape, jnp.float32) for shape in shapes),
        scratch_shapes=[
            pltpu.VMEM((rows // 8, conds), jnp.float32),
            pltpu.VMEM((6 * rows // 8, wide // 6), jnp.float32),
            pltpu.VMEM((4, rows // 8, conds), jnp.float32),
        ],
        compiler_params=pltpu.CompilerParams(vmem_limit_bytes=VMEM_BYTES),
        cost_estimate=pl.CostEstimate(
            flops=100000000, bytes_accessed=10000000, transcendentals=0
        ),
        name="small_gradients",
    )(
        scalars(0),
        mine,
        came,
        modulation_weight,
        pair_norm,
        relative,
        gain,
        pair_weight,
    )


def per_device(
    crop_parts,
    res_parts,
    tokens,
    cotangent,
    time_levels,
    cath_ids,
    residue_numbers,
    chain_mask,
    time_weight,
    label_table,
    modulation_weight,
    projection_weight,
    gate_weight,
    output_weight,
    relative_table,
    pair_gain,
    pair_weight,
    feed_gate,
    feed_up,
    feed_down,
):
    crop_count, row_count, model_width = tokens.shape
    crop_length = residue_numbers.shape[1]
    head_count = pair_weight.shape[1]
    head_width = model_width // head_count
    bin_count = relative_table.shape[0]
    label_count = label_table.shape[0]
    token_count = crop_count * row_count
    score_scale = head_width ** (-0.5)
    pairs = head_count // 2
    layout = Layout(row_count, crop_length)
    query_start = lax.axis_index("res") * row_count

    def conditioning(features, onehot):
        return jnp.dot(features, time_weight, preferred_element_type=jnp.float32) + jnp.dot(
            onehot, label_table, preferred_element_type=jnp.float32
        )

    features = time_features(time_levels, time_weight.shape[0]).astype(jnp.bfloat16)
    label_onehot = (cath_ids[:, None] == jnp.arange(label_count, dtype=jnp.int32)[None, :]).astype(
        jnp.bfloat16
    )
    condition = conditioning(features, label_onehot)
    cond_act = jax.nn.silu(condition).astype(jnp.bfloat16)
    modulation = jnp.dot(cond_act, modulation_weight, preferred_element_type=jnp.float32)
    modulation = modulation.reshape(crop_count, 6, 1, model_width)
    shift_a, scale_a = modulation[:, 0], modulation[:, 1]
    mod_rows = pad_to(modulation[:, :, 0], 1, 8, 0.0)

    rotated = lax.dynamic_slice_in_dim(
        jnp.concatenate([jnp.stack([residue_numbers, chain_mask])] * 2, 2), query_start, crop_length, 2
    )
    members, kinds, forward_bins, backward_bins, places, *turned, tables, pair_norm = attention_tables(
        layout,
        score_scale,
        rotated[0],
        rotated[1],
        query_start,
        relative_table,
        pair_gain,
        pair_weight,
    )

    token_values = tokens.astype(jnp.float32)
    normed_a = (
        modulate(token_values, shift_a, scale_a)
        .astype(jnp.bfloat16)
        .reshape(token_count, model_width)
    )
    def project(weight):
        rows = jnp.dot(normed_a, weight, preferred_element_type=jnp.float32)
        return rows.astype(jnp.bfloat16).reshape(crop_count, row_count, -1)

    key_values = project(projection_weight[:, model_width:])
    others = [
        lax.ppermute(
            key_values, "res", [((r + step) % res_parts, r) for r in range(res_parts)]
        )
        for step in range(1, res_parts)
    ]
    if crop_count == 1 and others:
        line = jnp.concatenate(
            [condition, pad_to(cath_ids.astype(jnp.float32)[:, None], 1, LANES, 0.0)], axis=1
        )
        extra = jnp.concatenate([pad_to(features.astype(jnp.float32), 1, SIDE, 0.0), line], axis=0)
        others, extra = tie(others, jnp.pad(extra, ((4, 2), (0, 0))))
    if len(layout.pieces) == 2:
        other = others[0] if len(others) == 1 else jnp.concatenate(others, axis=1)
        pieces = [(key_values, 0, pairs), (other, 0, pairs)]
    else:
        pieces = [(jnp.concatenate([key_values] + others, axis=1), 0, pairs)]

    def block_rows(values):
        return pad_to(values, 1, layout.block_rows, 0)

    queries, attended, logs = attention_forward(
        layout,
        score_scale,
        block_rows(normed_a.reshape(tokens.shape)),
        projection_weight,
        pieces,
        members,
        kinds,
        forward_bins,
        tables,
    )
    here = lax.axis_index("res")
    split = res_parts == 2 and crop_parts == 16
    per_crop_results = [
        feed_layer(
            split,
            here,
            attended[crop],
            block_rows(tokens)[crop],
            block_rows(cotangent)[crop],
            block_rows(normed_a.reshape(tokens.shape))[crop],
            mod_rows[crop],
            gate_weight,
            output_weight,
            feed_gate,
            feed_up,
            feed_down,
        )
        for crop in range(crop_count)
    ]
    layer_out, grad_middle, grad_attended, grad_gate_pre, feed_sums = (
        jnp.stack([result[place] for result in per_crop_results]) for place in range(5)
    )
    layer_out, grad_middle = layer_out[:, :row_count], grad_middle[:, :row_count]
    grad_gate_pre = grad_gate_pre[:, :row_count].reshape(token_count, model_width)
    weight_grads = [
        sum(result[place].astype(jnp.float32) for result in per_crop_results).astype(jnp.bfloat16)
        if crop_count > 1
        else per_crop_results[0][place]
        for place in range(5, len(per_crop_results[0]))
    ]

    def backward_of(first_pair, count, grad_now):
        return attention_backward(
            layout,
            score_scale,
            first_pair,
            count,
            queries,
            grad_now,
            attended,
            logs,
            pieces,
            members,
            kinds,
            backward_bins,
            places,
            *turned,
            tables,
        )

    if split:
        arrivals = [swap_res(weight_grads[place]) for place in (0, 2, 4, 6)]
        kept = [weight_grads[place] for place in (1, 3, 5, 7)]
        half = model_width // 2
        inner = feed_gate.shape[1] // 2
        calls = [list(backward_of(0, 1, grad_attended))]
        arrivals, calls[0] = tie(arrivals, calls[0])
        gate_w, up_w, down_w, small_w = zip(kept, arrivals)
        halving = Halving(
            [
                [(gate_w, 0, inner), (small_w, 0, half)],
                [(up_w, 0, inner), (small_w, 1, half)],
                [(down_w, 0, half)],
            ],
            ["xyvu", "yvxu", "vxyu"],
        )
        arrived = []
        for first_pair, count in ((1, 4), (5, 1)):
            arrived.append(swap_res(calls[-1][2][0]))
            sent = halving.stage()
            sent, grad_attended = tie(sent, grad_attended)
            came = halving.send(sent)
            calls.append(list(backward_of(first_pair, count, grad_attended)))
            came, calls[-1], arrived[-1] = tie(came, calls[-1], arrived[-1])
            halving.take(came)
        index = lax.axis_index("crop")
        bf16 = jnp.bfloat16
        share = model_width // 16
        away = swap_res(calls[2][2][0])
        sent = halving.stage()
        sent, calls[2][1] = tie(sent, calls[2][1])
        came = halving.send(sent)
        joined, proj_send, proj_keep = projection_gradient(
            here,
            normed_a,
            [
                (calls[0][0][0], calls[0][1][0], arrived[0]),
                (calls[1][0][0], calls[1][1][0], arrived[1]),
                (calls[2][0][0], calls[2][1][0], away),
            ],
        )
        came, proj_send, proj_keep = tie(came, proj_send, proj_keep)
        proj_came = swap_res(proj_send)
        halving.take(came)
        (sent,) = halving.stage(merge=True)
        sent, proj_came = tie(sent, proj_came)
        came = exchange(sent, MASKS["u"])
        mine, *fan = local_call(
            fan_first_kernel,
            scalars(index % 4),
            [proj_keep, proj_came],
            [((4 * share, PACK), bf16)] * 4,
            "fan_first",
        )
        fan, joined = tie(fan, joined)
        fan_came = [exchange(value, mask + 1) for mask, value in enumerate(fan)]
        tokens_grad, pack = finish_layer(
            joined,
            projection_weight,
            grad_gate_pre,
            gate_weight,
            tokens[0],
            grad_middle[0],
            mod_rows[0],
            feed_sums[0],
            extra,
            [call[-1][0] for call in calls],
        )
        tokens_grad = tokens_grad[None]
        came, pack = tie(came, pack)
        packs = [pack] + [exchange(pack, mask + 1) for mask in range(3)]
        finals = halving.stage(last=True, merged=came)
        feed_gate_grad, output_weight_grad, feed_up_grad, gate_weight_grad, feed_down_grad = finals
        packs, finals = tie(packs, finals)
        (packs,) = local_call(join_packs_kernel, scalars(0), packs, [((32, PACK), bf16)], "join_packs")
        far_packs = exchange(packs, MASKS["v"])
        fan_came, packs = tie(fan_came, packs)
        sent, mine = local_call(
            fan_v_kernel,
            scalars((index // 4) % 2),
            [mine, *fan_came],
            [((2 * share, PACK), bf16), ((2 * share, PACK), bf16)],
            "fan_v",
        )
        far_packs, sent = tie(far_packs, sent)
        came = exchange(sent, MASKS["v"])
        packs = jnp.concatenate([packs, far_packs], axis=0)
        far_packs = exchange(packs, MASKS["u"])
        sent, mine = local_call(
            fan_u_kernel,
            scalars(index // 8),
            [mine, came],
            [((share, PACK), bf16), ((share, PACK), bf16)],
            "fan_u",
        )
        far_packs, sent = tie(far_packs, sent)
        came = exchange(sent, MASKS["u"])
        packs = jnp.concatenate([packs, far_packs], axis=0)
        (
            modulation_weight_grad,
            time_weight_grad,
            label_table_grad,
            relative_table_grad,
            pair_gain_grad,
            pair_weight_grad,
        ) = small_gradients(
            head_count,
            label_count,
            packs,
            swap_res(packs),
            modulation_weight,
            pair_norm,
            relative_table,
            pair_gain.reshape(1, -1),
            pad_to(pair_weight, 1, 16, 0.0),
        )
        pair_weight_grad = pair_weight_grad.T
        came, pair_weight_grad = tie(came, pair_weight_grad)
        projection_weight_grad = add_low(mine, came, jnp.float32)
        pair_gain_grad = pair_gain_grad[0]
    else:
        results = backward_of(0, pairs, grad_attended)
        grad_table = results[-1]
        grad_pairs = results[1:-1]
        if len(grad_pairs) == 2:
            total, away = grad_pairs[0].astype(jnp.float32), grad_pairs[1]
        else:
            total = grad_pairs[0][:, :, :row_count].astype(jnp.float32)
            away = grad_pairs[0][:, :, row_count:]
        for step in range(1, res_parts):
            sent = away[:, :, (step - 1) * row_count : step * row_count]
            pairs_to = [(r, (r + step) % res_parts) for r in range(res_parts)]
            total = total + lax.ppermute(sent, "res", pairs_to).astype(jnp.float32)
        total = total.astype(jnp.bfloat16)
        grad_projected = jnp.concatenate(
            [results[0][:, :row_count], total[:, 0], total[:, 1]], axis=-1
        ).reshape(token_count, 3 * model_width)
        grad_normed_a = against_columns(grad_projected, projection_weight) + against_columns(
            grad_gate_pre, gate_weight
        )
        norm_back_a = jax.vjp(modulate, token_values, shift_a, scale_a)[1]
        grad_tokens, grad_shift_a, grad_scale_a = norm_back_a(
            grad_normed_a.reshape(crop_count, row_count, model_width)
        )
        tokens_grad = (grad_middle + grad_tokens).astype(jnp.bfloat16)
        feed_gate_grad, feed_up_grad, feed_down_grad = (
            scatter_crops(share_columns(value, res_parts)) for value in weight_grads[:3]
        )
        output_weight_grad, gate_weight_grad = (
            scatter_crops(share_columns(value, res_parts))
            for value in (weight_grads[3][:, :model_width], weight_grads[3][:, model_width:])
        )
        projection_weight_grad = scatter_crops(
            share_columns(across_rows(normed_a, grad_projected), res_parts)
        )
        grad_table = grad_table[:, :, :2].sum(0).reshape(head_count, LANES)

        grad_modulation = jnp.concatenate([grad_shift_a, grad_scale_a, feed_sums[:, 2:6]], axis=1)
        grad_modulation = grad_modulation.reshape(crop_count, 6 * model_width)
        table_row = grad_table.reshape(1, head_count * LANES)
        first_row = (jnp.arange(crop_count) == 0).astype(jnp.float32)[:, None]
        small_here = jnp.concatenate([grad_modulation, first_row * table_row], axis=1)
        levels_here = jnp.stack([time_levels, cath_ids.astype(jnp.float32)], axis=1)
        levels_here = pad_to(levels_here, 1, LANES, 0.0)
        small_all = gather_crops(
            jnp.concatenate([levels_here, sum_res(small_here, res_parts)], axis=1), crop_parts
        )
        levels_all, small_all = small_all[:, :2], small_all[:, LANES:]
        grad_modulation = small_all[:, : 6 * model_width]
        grad_table = jnp.sum(small_all[:, 6 * model_width :], axis=0).reshape(head_count, LANES)
        grad_table = grad_table[:, :bin_count]
        features_all = time_features(levels_all[:, 0], time_weight.shape[0]).astype(jnp.bfloat16)
        onehot_all = (
            levels_all[:, 1].astype(jnp.int32)[:, None]
            == jnp.arange(label_count, dtype=jnp.int32)[None, :]
        ).astype(jnp.bfloat16)
        condition = conditioning(features_all, onehot_all)
        cond_act = jax.nn.silu(condition).astype(jnp.bfloat16)
        modulation_weight_grad = split_left(cond_act, grad_modulation, 0, 0)
        grad_condition = split_left(modulation_weight, grad_modulation, 1, 1).T * silu_slope(condition)
        time_weight_grad = split_left(features_all, grad_condition, 0, 0)
        label_table_grad = split_left(onehot_all, grad_condition, 0, 0)
        relative_values = relative_table.astype(jnp.float32)
        gain_values = pair_gain.astype(jnp.float32)
        pair_norm = pair_norm[:bin_count]
        pair_weight_grad = split_left(pair_norm, grad_table, 0, 1)
        grad_pair_norm = split_right(grad_table, pair_weight, 0, 1)
        pair_back = jax.vjp(normalize_rows, relative_values, gain_values)[1]
        relative_table_grad, pair_gain_grad = pair_back(grad_pair_norm)
    return (
        layer_out,
        tokens_grad,
        time_weight_grad,
        label_table_grad,
        modulation_weight_grad,
        projection_weight_grad,
        gate_weight_grad,
        output_weight_grad,
        relative_table_grad,
        pair_gain_grad,
        pair_weight_grad,
        feed_gate_grad,
        feed_up_grad,
        feed_down_grad,
    )


def solution(mesh):
    return jax.shard_map(
        functools.partial(per_device, mesh.shape["crop"], mesh.shape["res"]),
        mesh=mesh,
        in_specs=(
            P("crop", "res", None),
            P("crop", "res", None),
            P("crop"),
            P("crop"),
            P("crop", None),
            P("crop", None),
            P(),
            P(),
            P(),
            P(),
            P(),
            P(),
            P(),
            P(),
            P(),
            P(),
            P(),
            P(),
        ),
        out_specs=(
            P("crop", "res", None),
            P("crop", "res", None),
            P(),
            P(),
            P(),
            P("crop", "res"),
            P("crop", "res"),
            P("crop", "res"),
            P(),
            P(),
            P(),
            P("crop", "res"),
            P("crop", "res"),
            P("crop", "res"),
        ),
        check_vma=False,
    )
```

```python
import functools
import itertools
import math

import jax
import jax.numpy as jnp
from jax import lax
from jax.experimental import pallas as pl
from jax.experimental.pallas import tpu as pltpu
from jax.sharding import PartitionSpec as P

LANES = 128
NEAR = 31
VMEM_BYTES = 56 * 1024 * 1024
QUERY_BLOCK = 672
KEY_BLOCK = 768
LOG2E = 1.4426950408889634
NONE, RIGHT, LEFT, APART = 0, 1, 2, 3


def layer_norm(inputs):
    mean_value = jnp.mean(inputs, axis=-1, keepdims=True)
    centred = inputs - mean_value
    spread = jnp.mean(centred * centred, axis=-1, keepdims=True)
    return centred * lax.rsqrt(spread + 1e-06)


def modulate(inputs, shift_row, scale_row):
    return layer_norm(inputs) * (1.0 + scale_row) + shift_row


def normalize_rows(table_rows, gain_row):
    return layer_norm(table_rows) * gain_row


def time_features(time_levels, feature_width):
    half_width = feature_width // 2
    frequency = jnp.exp(-math.log(10000.0) * jnp.arange(half_width, dtype=jnp.float32) / half_width)
    angles = 1000.0 * time_levels[:, None] * frequency[None, :]
    return jnp.concatenate([jnp.sin(angles), jnp.cos(angles)], axis=-1)


def across_rows(former, latter):
    return lax.dot_general(
        former, latter, (((0,), (0,)), ((), ())), preferred_element_type=jnp.float32
    )


def against_columns(former, latter):
    return lax.dot_general(
        former, latter, (((1,), (1,)), ((), ())), preferred_element_type=jnp.float32
    )


def split_parts(values):
    upper = lax.reduce_precision(values, 8, 7)
    return (upper.astype(jnp.bfloat16), (values - upper).astype(jnp.bfloat16))


def split_left(narrow, values, former_dim, latter_dim):
    upper, rest = split_parts(values)
    numbers = (((former_dim,), (latter_dim,)), ((), ()))
    return lax.dot_general(
        narrow, upper, numbers, preferred_element_type=jnp.float32
    ) + lax.dot_general(narrow, rest, numbers, preferred_element_type=jnp.float32)


def split_right(values, narrow, former_dim, latter_dim):
    upper, rest = split_parts(values)
    numbers = (((former_dim,), (latter_dim,)), ((), ()))
    return lax.dot_general(
        upper, narrow, numbers, preferred_element_type=jnp.float32
    ) + lax.dot_general(rest, narrow, numbers, preferred_element_type=jnp.float32)


def sigmoid_slope(inputs):
    gate_value = jax.nn.sigmoid(inputs)
    return gate_value * (1.0 - gate_value)


def silu_slope(inputs):
    gate_value = jax.nn.sigmoid(inputs)
    return gate_value * (1.0 + inputs * (1.0 - gate_value))


class Layout:
    def __init__(self, rows, length):
        self.rows = rows
        self.length = length
        self.query_tiles = -(-rows // LANES)
        self.key_tiles = -(-length // LANES)
        self.padded = self.query_tiles * LANES
        self.wide = self.key_tiles * LANES
        self.last = self.key_tiles - 1
        self.groups = (self.query_tiles + 4) * 4
        assert 2 * self.groups + 3 <= LANES and self.groups <= 64
        assert rows - 1 + NEAR < self.padded and length - NEAR >= self.last * LANES
        assert rows % 8 == 0 and self.last > self.query_tiles
        self.block_rows = rows if rows % 16 == 0 else self.padded
        self.pieces = [rows, length - rows] if rows % 16 == 0 else [length]

    def tile_start(self, tile):
        return self.last * LANES if tile < 0 else tile * LANES


def pad_to(values, axis, size, fill):
    widths = [(0, 0)] * values.ndim
    widths[axis] = (0, size - values.shape[axis])
    return jnp.pad(values, widths, constant_values=fill)


def tables_kernel(
    layout, bin_count, heads, scale, start_ref, pairs_ref, relative_ref, gain_ref, weight_ref, *out_refs
):
    members_ref, kinds_ref, forward_ref, backward_ref, places_ref = out_refs[:5]
    members_turned, kinds_turned, tables_ref, norm_ref, codes = out_refs[5:]
    rows, length, queries, groups = layout.rows, layout.length, layout.query_tiles, layout.groups
    wrap = length - start_ref[0]
    reach = (bin_count - 2) // 2
    zero_bin = LANES - 1
    shape = (LANES, LANES)
    lane = lax.broadcasted_iota(jnp.int32, shape, 1)
    row = lax.broadcasted_iota(jnp.int32, shape, 0)
    last_start = layout.last * LANES

    values = relative_ref[...].astype(jnp.float32)
    centred = values - jnp.mean(values, axis=1, keepdims=True)
    root = lax.rsqrt(jnp.mean(centred * centred, axis=1, keepdims=True) + 1e-06)
    pair_norm = (centred * root * gain_ref[...].astype(jnp.float32)).astype(jnp.bfloat16)
    norm_ref[...] = pair_norm
    bias = lax.dot_general(
        weight_ref[...], pair_norm, (((0,), (1,)), ((), ())), preferred_element_type=jnp.float32
    )
    head_lane = lax.broadcasted_iota(jnp.int32, bias.shape, 1)
    final = jnp.sum(jnp.where(head_lane == bin_count - 1, bias, 0.0), axis=1, keepdims=True)
    table = jnp.where(head_lane < bin_count, (bias - final) * (1.0 / scale), 0.0)

    def columns(number):
        value = jnp.sum(jnp.where(head_lane == number, table, 0.0), axis=1, keepdims=True)
        upper = value.astype(jnp.bfloat16).astype(jnp.float32)
        return jnp.where(
            head_lane < groups, upper, jnp.where(head_lane < 2 * groups, value - upper, 0.0)
        )

    right_columns, left_columns = columns(bin_count - 2), columns(0)
    for head in range(heads):
        line = 8 * (head % 2)
        for place, rows_of in enumerate((table, right_columns, left_columns)):
            tables_ref[head // 2, line + place : line + place + 1] = rows_of[head : head + 1]

    tiles = pairs_ref.shape[1]
    marks = pairs_ref[1].astype(jnp.float32)
    place = lax.broadcasted_iota(jnp.int32, marks.shape, 0) * LANES + lax.broadcasted_iota(
        jnp.int32, marks.shape, 1
    )
    before = jnp.sum(jnp.where(place < wrap, marks, 0.0), keepdims=True)
    every = jnp.sum(marks, keepdims=True)
    triangle = jnp.where(row <= lane, 1.0, 0.0).astype(jnp.bfloat16)
    running = jnp.dot(marks.astype(jnp.bfloat16), triangle, preferred_element_type=jnp.float32)
    numbers, chains = [], []
    carry = jnp.zeros((1, 1), jnp.float32)
    for tile in range(layout.key_tiles):
        count = running[tile : tile + 1] + carry
        carry = carry + running[tile : tile + 1, LANES - 1 :]
        count = count + jnp.where(place[tile : tile + 1] < wrap, every - before, -before)
        chains.append(jnp.broadcast_to(count.astype(jnp.int32), shape))
        numbers.append(jnp.broadcast_to(pairs_ref[0, tile : tile + 1], shape))
    number_rows = [value.T for value in numbers]
    chain_rows = [value.T for value in chains]

    def bins_of(key_number, key_chain, query_number, query_chain):
        offset = jnp.clip(key_number - query_number, -reach, reach) + reach
        return jnp.where(key_chain == query_chain, offset, bin_count - 1)

    def touches(query, tile):
        begin = -LANES if tile < 0 else tile * LANES
        return (begin <= query + NEAR) & (query - NEAR <= begin + LANES - 1)

    for tile in range(layout.key_tiles):
        size = min(LANES, length - tile * LANES)
        key = tile * LANES + row
        if tile == layout.last:
            other = jnp.full(shape, queries + 3, jnp.int32)
        elif tile == queries - 1:
            other = jnp.full(shape, queries, jnp.int32)
        else:
            other = jnp.where(key < wrap, queries + 1, queries + 2)
        group = jnp.where(key < rows, tile, other)
        slot = group * 4 + chain_rows[tile] - 1
        hit = (lane == slot) | (lane == slot + groups)
        tail = (lane >= 2 * groups) & (lane < 2 * groups + 3)
        values = jnp.where(hit, 1.0, jnp.where(tail, -1.0, 0.0)).astype(jnp.bfloat16)
        members_ref[tile * LANES : tile * LANES + size] = values[:size]
        turned = jnp.where(hit & (lane < groups), 1.0, 0.0).T
        members_turned[:, tile * LANES : tile * LANES + size] = turned[:64, :size].astype(jnp.bfloat16)

    local = jnp.where(lane >= groups, lane - groups, lane)
    lane_group = local >> 2
    lane_chain = (local & 3) + 1
    lane_begin = jnp.where(
        lane_group < queries,
        lane_group * LANES,
        jnp.where(lane_group == queries, (queries - 1) * LANES, -LANES),
    )
    has_band = (lane_group <= queries) | (lane_group == queries + 3)
    other_right = jnp.where(
        lane_group == queries,
        rows,
        jnp.where(
            lane_group == queries + 3,
            last_start,
            jnp.where(lane_group == queries + 1, 0, 2 * length),
        ),
    )
    right_limit = jnp.where(lane_group > queries, jnp.where(lane_group == queries + 3, wrap, length), wrap)
    for tile in range(queries):
        size = min(LANES, layout.block_rows - tile * LANES)
        query = tile * LANES + row
        near = (lane_begin <= query + NEAR) & (query - NEAR <= lane_begin + LANES - 1) & has_band
        right = jnp.where(lane_group < queries, lane_group - tile, right_limit - other_right) > 0
        same = chain_rows[tile] == lane_chain
        kinds = jnp.where(same, jnp.where(near, NONE, jnp.where(right, RIGHT, LEFT)), APART)
        kinds = jnp.where((lane < 2 * groups) & (query < rows), kinds, NONE)
        kinds_ref[tile * LANES : tile * LANES + size] = kinds[:size]
        kinds_turned[:, tile * LANES : (tile + 1) * LANES] = jnp.where(lane < groups, kinds, NONE).T[:64]
        for step in range(3):
            near_tile = tile + step - 1
            index = layout.last if near_tile < 0 else near_tile
            if near_tile < queries:
                inside = touches(query, near_tile) & (query < rows)
                inside &= lane < length - index * LANES
                found = bins_of(
                    numbers[index], chains[index], number_rows[tile], chain_rows[tile]
                )
                found = jnp.where(inside, found, zero_bin)
            else:
                found = jnp.full(shape, zero_bin, jnp.int32)
            forward_ref[
                tile * LANES : (tile + 1) * LANES, step * LANES : (step + 1) * LANES
            ] = found

    codes[...] = jnp.full(codes.shape, -1, jnp.int32)
    for tile in range(queries):
        size = min(LANES, rows - tile * LANES)
        code = number_rows[tile] * 8 + chain_rows[tile]
        codes[(tile + 1) * LANES : (tile + 1) * LANES + size] = code[:size]

    for index, tile in enumerate(list(range(queries)) + [-1]):
        source = layout.last if tile < 0 else tile
        key_row = (row - (length - last_start)) if tile < 0 else tile * LANES + row
        present = row < length - source * LANES
        for step in range(3):
            near_tile = tile + step - 1
            if 0 <= near_tile < queries:
                near_query = near_tile * LANES + lane
                inside = touches(near_query, tile) & (near_query < rows) & present
                found = bins_of(
                    number_rows[source], chain_rows[source], numbers[near_tile], chains[near_tile]
                )
                found = jnp.where(inside, found, zero_bin)
            else:
                found = jnp.full(shape, zero_bin, jnp.int32)
            backward_ref[
                index * LANES : (index + 1) * LANES, step * LANES : (step + 1) * LANES
            ] = found
        target = (number_rows[source] + reach - lane) * 8 + chain_rows[source]
        target = jnp.where(present & (lane > 0) & (lane < 2 * reach), target, -9)
        offset = (LANES - (length - last_start)) if tile < 0 else (tile + 1) * LANES
        far = 4 * LANES
        shift = jnp.full(shape, far, jnp.int32)
        for distance in range(-NEAR, NEAR + 1):
            other = codes[offset - distance : offset - distance + LANES]
            shift = jnp.where(other == target, distance, shift)
        if tile < 0:
            base = jnp.zeros(shape, jnp.int32)
        else:
            base = jnp.where(row < LANES // 2, tile - 1, tile) * LANES
        places_ref[index * LANES : (index + 1) * LANES] = jnp.where(
            shift == far, far - 1, key_row - shift - base
        )


def attention_tables(layout, scale, numbers, marks, query_start, relative_table, pair_gain, pair_weight):
    crops = numbers.shape[0]
    bin_count, width = relative_table.shape
    heads = pair_weight.shape[1]
    pairs = jnp.stack([numbers, marks], axis=1)
    pairs = pad_to(pairs, 2, layout.wide, 0).reshape(crops, 2, layout.key_tiles, LANES)
    spots = (layout.query_tiles + 1) * LANES
    shapes = [
        ((layout.length, LANES), jnp.bfloat16),
        ((layout.block_rows, LANES), jnp.int32),
        ((layout.padded, 3 * LANES), jnp.int32),
        ((spots, 3 * LANES), jnp.int32),
        ((spots, LANES), jnp.int32),
        ((64, layout.length), jnp.bfloat16),
        ((64, layout.padded), jnp.int32),
    ]
    shared = [((heads // 2, 16, LANES), jnp.float32), ((LANES, width), jnp.bfloat16)]

    def whole(shape):
        return pl.BlockSpec(shape, lambda crop: (0,) * len(shape))

    return pl.pallas_call(
        functools.partial(tables_kernel, layout, bin_count, heads, scale),
        grid=(crops,),
        in_specs=[
            pl.BlockSpec(memory_space=pltpu.SMEM),
            pl.BlockSpec((None, 2, layout.key_tiles, LANES), lambda crop: (crop, 0, 0, 0)),
            whole((LANES, width)),
            whole((1, width)),
            whole((width, 16)),
        ],
        out_specs=tuple(
            [pl.BlockSpec((None, *shape), lambda crop: (crop, 0, 0)) for shape, _ in shapes]
            + [whole(shape) for shape, _ in shared]
        ),
        out_shape=tuple(
            [jax.ShapeDtypeStruct((crops, *shape), kind) for shape, kind in shapes]
            + [jax.ShapeDtypeStruct(shape, kind) for shape, kind in shared]
        ),
        scratch_shapes=[pltpu.VMEM((layout.padded + 2 * LANES, LANES), jnp.int32)],
        compiler_params=pltpu.CompilerParams(vmem_limit_bytes=VMEM_BYTES),
        cost_estimate=pl.CostEstimate(
            flops=40000000 * crops, bytes_accessed=4000000 * crops, transcendentals=0
        ),
        name="pair_tables",
    )(
        jnp.reshape(query_start, (1,)).astype(jnp.int32),
        pairs,
        pad_to(relative_table, 0, LANES, 0.0),
        pair_gain.reshape(1, -1),
        pad_to(pair_weight, 1, 16, 0.0),
    )


NT = (((1,), (1,)), ((), ()))
TN = (((0,), (0,)), ((), ()))


def wide_dot(former, latter, numbers=(((1,), (0,)), ((), ()))):
    return lax.dot_general(former, latter, numbers, preferred_element_type=jnp.float32)


def look_up(table_row, bins):
    table = jnp.broadcast_to(table_row, bins.shape)
    return jnp.take_along_axis(table, bins, axis=1, mode="promise_in_bounds")


def half_of(values, lane, side):
    return jnp.where((lane >= 64) == (side == 1), values, jnp.zeros_like(values))


def row_blocks(total, size):
    return [(start, min(start + size, total)) for start in range(0, total, size)]


def group_columns(kinds, tables, side):
    right = tables[8 * side + 1 : 8 * side + 2]
    left = tables[8 * side + 2 : 8 * side + 3]
    return jnp.where(kinds == RIGHT, right, jnp.where(kinds == LEFT, left, 0.0))


def forward_kernel(layout, scale, *refs):
    count = len(layout.pieces)
    normed_ref, weight_ref = refs[:2]
    key_refs = refs[2 : 2 + count]
    value_refs = refs[2 + count : 2 + 2 * count]
    members_ref, kinds_ref, bins_ref, tables_ref, query_ref, out_ref, log_ref = refs[
        2 + 2 * count : -1
    ]
    all_scores = refs[-1]
    pair = pl.program_id(1)
    rows, length = layout.block_rows, layout.length
    turn = 0
    factor = scale * LOG2E
    lane = lax.broadcasted_iota(jnp.int32, (1, LANES), 1)
    query = wide_dot(normed_ref[...], weight_ref[...]).astype(jnp.bfloat16)
    query_ref[...] = query
    keys = jnp.concatenate([ref[...] for ref in key_refs], axis=0)
    values = jnp.concatenate([ref[...] for ref in value_refs], axis=0)
    members = members_ref[...]
    kinds = kinds_ref[...]
    tables = tables_ref[...]
    ones = jnp.ones((length, LANES), jnp.bfloat16)

    @pl.when(pair == 0)
    def _():
        log_ref[...] = jnp.zeros_like(log_ref)

    for side in range(2):
        key_columns = jnp.concatenate([half_of(keys, lane, side), members], axis=1)
        value_columns = jnp.concatenate([half_of(values, lane, side), ones], axis=1)
        extra = group_columns(kinds, tables, side).astype(jnp.bfloat16)
        query_columns = jnp.concatenate([query, extra], axis=1)
        table_row = tables[8 * side : 8 * side + 1]
        for start, stop in row_blocks(rows, QUERY_BLOCK):
            size = stop - start
            scores = all_scores.at[turn % 2]
            turn += 1
            scores[0:size, 0:length] = wide_dot(query_columns[start:stop], key_columns, NT)
            for tile in range(start // LANES, -(-stop // LANES)):
                first, final = tile * LANES, min(tile * LANES + LANES, rows)
                for slot in range(3):
                    other = tile + slot - 1
                    if other >= layout.query_tiles:
                        continue
                    low, high = first, final
                    if slot == 0:
                        high = min(first + 32, final)
                    if slot == 2:
                        low = first + LANES - 32
                    if low >= high:
                        continue
                    place = layout.tile_start(other)
                    width = min(LANES, length - place)
                    bins = bins_ref[low:high, slot * LANES : (slot + 1) * LANES]
                    bias = look_up(table_row, bins)[:, :width]
                    scores[low - start : high - start, place : place + width] += bias
            block = scores[0:size, 0:length]
            top = jnp.max(block, axis=1, keepdims=True)
            weights = jnp.exp2((block - top) * factor).astype(jnp.bfloat16)
            sums = wide_dot(weights, value_columns)
            total = sums[:, LANES:]
            result = sums[:, :LANES] / total
            if side == 0:
                out_ref[start:stop] = result
            else:
                out_ref[start:stop] += result
            log_total = top + jnp.log(total) * (1.0 / scale)
            log_ref[start:stop] = jnp.where(
                lane == 2 * pair + side, log_total, log_ref[start:stop]
            )


def backward_kernel(layout, scale, first_pair, *refs):
    count = len(layout.pieces)
    query_ref, grad_ref, out_ref, log_ref = refs[:4]
    key_refs = refs[4 : 4 + count]
    value_refs = refs[4 + count : 4 + 2 * count]
    rest = refs[4 + 2 * count :]
    members_ref, kinds_ref, bins_ref, places_ref, tables_ref = rest[:5]
    members_turned_ref, kinds_turned_ref = rest[5:7]
    grad_query_ref = rest[7]
    grad_pair_refs = rest[8 : 8 + count]
    grad_table_ref = rest[8 + count]
    query_wide, grad_wide, query_turned, grad_turned = rest[9 + count : 13 + count]
    all_scores, slopes_low, probs_low = rest[13 + count :]
    pair = pl.program_id(1) + first_pair
    rows, length, padded = layout.block_rows, layout.length, layout.padded
    factor = scale * LOG2E
    lane = lax.broadcasted_iota(jnp.int32, (1, LANES), 1)
    keys = jnp.concatenate([ref[...] for ref in key_refs], axis=0)
    values = jnp.concatenate([ref[...] for ref in value_refs], axis=0)
    members = members_ref[...]
    kinds = kinds_ref[...]
    tables = tables_ref[...]
    query = query_ref[...]
    grad = grad_ref[...]
    grad_full = grad.astype(jnp.float32)
    product = grad_full * out_ref[...]
    log_all = log_ref[...]
    tail = 2 * layout.groups
    ones = jnp.broadcast_to(jnp.where(lane < 3, 1.0, 0.0), (length, LANES)).astype(jnp.bfloat16)

    def three_parts(values):
        upper = values.astype(jnp.bfloat16).astype(jnp.float32)
        values = values - upper
        middle = values.astype(jnp.bfloat16).astype(jnp.float32)
        return upper, middle, values - middle

    def in_lanes(parts, first):
        return jnp.where(
            lane == first,
            parts[0],
            jnp.where(lane == first + 1, parts[1], jnp.where(lane == first + 2, parts[2], 0.0)),
        )

    if padded > rows:
        for ref in (query_wide, grad_wide):
            for side in range(2):
                ref[side, rows:padded] = jnp.zeros((padded - rows, ref.shape[2]), jnp.bfloat16)
        for ref in (query_turned, grad_turned):
            ref[:, rows:padded] = jnp.zeros((LANES, padded - rows), jnp.bfloat16)
    query_turned[:, 0:rows] = query.T
    grad_turned[:, 0:rows] = grad.T
    for side in range(2):
        log_total = jnp.sum(
            jnp.where(lane == 2 * pair + side, log_all, 0.0), axis=1, keepdims=True
        )
        extra = group_columns(kinds, tables, side) + in_lanes(three_parts(log_total), tail)
        query_wide[side, 0:rows, 0:LANES] = query
        query_wide[side, 0:rows, LANES:] = extra.astype(jnp.bfloat16)
        delta = jnp.sum(half_of(product, lane, side), axis=1, keepdims=True)
        grad_wide[side, 0:rows, 0:LANES] = grad
        grad_wide[side, 0:rows, LANES:] = in_lanes(three_parts(-delta), 0).astype(jnp.bfloat16)

    key_columns = [
        jnp.concatenate([half_of(keys, lane, side), members], axis=1) for side in range(2)
    ]
    value_columns = [
        jnp.concatenate([half_of(values, lane, side), ones], axis=1) for side in range(2)
    ]
    inner_sums = [jnp.zeros((1, LANES), jnp.float32) for _ in range(2)]
    low_sums = [jnp.zeros((1, LANES), jnp.float32) for _ in range(2)]
    high_sums = [jnp.zeros((1, LANES), jnp.float32) for _ in range(2)]
    reach_tiles = list(range(layout.query_tiles)) + [-1]

    def put(which, start, stop, result):
        begin = 0
        for ref, size in zip(grad_pair_refs, layout.pieces):
            low, high = max(start, begin), min(stop, begin + size)
            if low < high:
                ref[which, low - begin : high - begin] = result[low - start : high - start]
            begin += size

    for start, stop in row_blocks(length, KEY_BLOCK):
        size = stop - start
        for side in range(2):
            table_row = tables[8 * side : 8 * side + 1]
            scores = all_scores.at[side]
            scores[0:size] = wide_dot(key_columns[side][start:stop], query_wide[side], NT)
            near = []
            for index, tile in enumerate(reach_tiles):
                place = layout.tile_start(tile)
                if start <= place < stop:
                    near.append((index, tile, place, min(place + LANES, length)))
            for index, tile, place, final in near:
                for slot in range(3):
                    other = tile + slot - 1
                    if not 0 <= other < layout.query_tiles:
                        continue
                    bins = bins_ref[
                        index * LANES : index * LANES + final - place,
                        slot * LANES : (slot + 1) * LANES,
                    ]
                    scores[
                        place - start : final - start, other * LANES : (other + 1) * LANES
                    ] += look_up(table_row, bins)
            probs = jnp.exp2(scores[0:size] * factor).astype(jnp.bfloat16)
            grad_probs = wide_dot(value_columns[side][start:stop], grad_wide[side], NT)
            probs_low[side, start:stop] = probs
            slopes_low[side, start:stop] = probs * grad_probs.astype(jnp.bfloat16)
            for index, tile, place, final in near:
                for slot in range(3):
                    other = tile + slot - 1
                    if not 0 <= other < layout.query_tiles:
                        continue
                    bins = bins_ref[
                        index * LANES : index * LANES + final - place,
                        slot * LANES : (slot + 1) * LANES,
                    ]
                    cut = slopes_low[side, place:final, other * LANES : (other + 1) * LANES].astype(
                        jnp.float32
                    )
                    low_sums[side] += jnp.sum(
                        jnp.where(bins == 0, cut, 0.0), axis=0, keepdims=True
                    )
                    high_sums[side] += jnp.sum(
                        jnp.where(bins == 2 * (NEAR + 1), cut, 0.0), axis=0, keepdims=True
                    )
                for half in range(2):
                    begin, end = half * 64, min(half * 64 + 64, final - place)
                    if begin >= end:
                        continue
                    base = 0 if tile < 0 else tile - 1 + half
                    where = places_ref[index * LANES + begin : index * LANES + end]
                    spot = where & (LANES - 1)
                    for step in range(2):
                        other = base + step
                        if not 0 <= other < layout.query_tiles or (tile < 0 and step):
                            continue
                        cut = slopes_low[
                            side, place + begin : place + end, other * LANES : (other + 1) * LANES
                        ].astype(jnp.float32)
                        picked = jnp.take_along_axis(cut, spot, axis=1, mode="promise_in_bounds")
                        picked = jnp.where((where >> 7) == step, picked, 0.0)
                        inner_sums[side] += jnp.sum(picked, axis=0, keepdims=True)

    keys_turned = keys.T
    grad_keys, grad_values, grad_queries = [], [], []
    kinds_turned = kinds_turned_ref[...]
    for side in range(2):
        cut = slice(64 * side, 64 * side + 64)
        grad_values.append(wide_dot(grad_turned[cut], probs_low[side], NT))
        grad_keys.append(wide_dot(query_turned[cut], slopes_low[side], NT))
        left = jnp.concatenate([keys_turned[cut], members_turned_ref[...]], axis=0)
        both = wide_dot(left, slopes_low[side])
        grad_queries.append(both[:64])
        sums = both[64:]

        def total(kind):
            return jnp.sum(jnp.where(kinds_turned == kind, sums, 0.0))

        right = total(RIGHT) + jnp.sum(high_sums[side])
        left = total(LEFT) + jnp.sum(low_sums[side])
        apart = total(APART)
        grad_table_ref[side : side + 1] = jnp.where(
            lane == 0,
            left,
            jnp.where(
                lane == 2 * (NEAR + 1),
                right,
                jnp.where(lane == 2 * (NEAR + 1) + 1, apart, inner_sums[side]),
            ),
        )
    put(0, 0, length, (jnp.concatenate(grad_keys, axis=0) * scale).T.astype(jnp.bfloat16))
    put(1, 0, length, jnp.concatenate(grad_values, axis=0).T.astype(jnp.bfloat16))
    turned = jnp.concatenate(grad_queries, axis=0) * scale
    grad_query_ref[...] = turned.T[0:rows].astype(jnp.bfloat16)


def tile_columns(rows, offset=0):
    return pl.BlockSpec((None, rows, LANES), lambda crop, pair: (crop, 0, pair + offset))


def per_crop(rows, width):
    return pl.BlockSpec((None, rows, width), lambda crop, pair: (crop, 0, 0))


def kernel_params():
    return pltpu.CompilerParams(
        vmem_limit_bytes=VMEM_BYTES, dimension_semantics=("arbitrary", "arbitrary")
    )


def attention_forward(layout, scale, normed, weight, key_values, members, kinds, bins, tables):
    crops, rows, width = normed.shape
    pairs = tables.shape[0]
    specs = [per_crop(rows, width), pl.BlockSpec((width, LANES), lambda crop, pair: (0, pair))]
    operands = [normed, weight]
    for place in (1, 2):
        for piece in key_values:
            specs.append(tile_columns(piece[0].shape[1], piece[place]))
            operands.append(piece[0])
    specs += [
        per_crop(layout.length, LANES),
        per_crop(rows, LANES),
        per_crop(layout.padded, 3 * LANES),
        pl.BlockSpec((None, 16, LANES), lambda crop, pair: (pair, 0, 0)),
    ]
    flops = 2 * crops * pairs * 2 * rows * layout.length * 256 * 2
    return pl.pallas_call(
        functools.partial(forward_kernel, layout, scale),
        grid=(crops, pairs),
        in_specs=specs,
        out_specs=(tile_columns(rows), tile_columns(rows), per_crop(rows, LANES)),
        out_shape=(
            jax.ShapeDtypeStruct((crops, rows, pairs * LANES), jnp.bfloat16),
            jax.ShapeDtypeStruct((crops, rows, pairs * LANES), jnp.float32),
            jax.ShapeDtypeStruct((crops, rows, LANES), jnp.float32),
        ),
        scratch_shapes=[pltpu.VMEM((2, QUERY_BLOCK, layout.wide), jnp.float32)],
        compiler_params=kernel_params(),
        cost_estimate=pl.CostEstimate(
            flops=flops,
            bytes_accessed=12 * crops * rows * pairs * LANES,
            transcendentals=crops * pairs * 2 * rows * layout.length,
        ),
        name="attention_forward",
    )(*operands, members, kinds, bins, tables)


def attention_backward(
    layout,
    scale,
    first_pair,
    pairs,
    projected,
    grad_out,
    attended,
    logs,
    key_values,
    members,
    kinds,
    bins,
    places,
    members_turned,
    kinds_turned,
    tables,
):
    crops, rows, _ = projected.shape
    specs = [tile_columns(rows, first_pair)] * 3 + [per_crop(rows, LANES)]
    operands = [projected, grad_out, attended, logs]
    for place in (1, 2):
        for piece in key_values:
            specs.append(tile_columns(piece[0].shape[1], piece[place] + first_pair))
            operands.append(piece[0])
    specs += [
        per_crop(layout.length, LANES),
        per_crop(rows, LANES),
        per_crop(bins.shape[1], 3 * LANES),
        per_crop(places.shape[1], LANES),
        pl.BlockSpec((None, 16, LANES), lambda crop, pair: (pair + first_pair, 0, 0)),
        per_crop(64, layout.length),
        per_crop(64, layout.padded),
    ]
    out_specs = [tile_columns(rows)]
    out_shapes = [jax.ShapeDtypeStruct((crops, rows, pairs * LANES), jnp.bfloat16)]
    for piece in key_values:
        size = piece[0].shape[1]
        out_specs.append(
            pl.BlockSpec((None, 2, size, LANES), lambda crop, pair: (crop, 0, 0, pair))
        )
        out_shapes.append(jax.ShapeDtypeStruct((crops, 2, size, pairs * LANES), jnp.bfloat16))
    out_specs.append(pl.BlockSpec((None, None, 8, LANES), lambda crop, pair: (crop, pair, 0, 0)))
    out_shapes.append(jax.ShapeDtypeStruct((crops, pairs, 8, LANES), jnp.float32))
    padded = layout.padded
    return pl.pallas_call(
        functools.partial(backward_kernel, layout, scale, first_pair),
        grid=(crops, pairs),
        in_specs=specs,
        out_specs=tuple(out_specs),
        out_shape=tuple(out_shapes),
        scratch_shapes=[
            pltpu.VMEM((2, padded, 2 * LANES), jnp.bfloat16),
            pltpu.VMEM((2, padded, 2 * LANES), jnp.bfloat16),
            pltpu.VMEM((LANES, padded), jnp.bfloat16),
            pltpu.VMEM((LANES, padded), jnp.bfloat16),
            pltpu.VMEM((2, KEY_BLOCK, padded), jnp.float32),
            pltpu.VMEM((2, layout.length, padded), jnp.bfloat16),
            pltpu.VMEM((2, layout.length, padded), jnp.bfloat16),
        ],
        compiler_params=kernel_params(),
        cost_estimate=pl.CostEstimate(
            flops=2 * crops * pairs * 2 * rows * layout.length * 256 * 5,
            bytes_accessed=20 * crops * rows * pairs * LANES,
            transcendentals=crops * pairs * 2 * rows * layout.length,
        ),
        name="attention_backward",
    )(*operands, members, kinds, bins, places, tables, members_turned, kinds_turned)


def sigmoid(values):
    return 0.5 * jnp.tanh(0.5 * values) + 0.5


def each_strip(rows, body, size=16):
    count = rows // size
    group = max(number for number in range(1, 9) if count % number == 0)

    @pl.loop(0, count // group)
    def _(index):
        for part in range(group):
            body(pl.ds(pl.multiple_of((index * group + part) * size, size), size))


def fold_rows(values):
    return jnp.sum(values.reshape(values.shape[0] // 8, 8, values.shape[1]), axis=0)


def feed_kernel(split, chunks, here_ref, *refs):
    (attended_ref, tokens_ref, upstream_ref, normed_a_ref, mod_ref, gate_weight_ref, output_ref) = refs[:7]
    gate_ref, up_ref, down_ref = refs[7:10]
    layer_ref, grad_middle_ref, grad_att_ref, grad_pre_ref, sums_ref = refs[10:15]
    grads = refs[15:-12]
    gated, grad_ff, normed, branch, middle, total, grad_normed, hidden, both, grad_branch = refs[-12:-2]
    gate_pre, turned = refs[-2:]
    step = pl.program_id(0)
    here = here_ref[0]
    rows, width = tokens_ref.shape
    size = gate_ref.shape[1]
    strip = 112 if rows % 112 == 0 else 64
    strips = rows // strip
    shift_f, scale_f = mod_ref[3:4], mod_ref[4:5]
    open_a, open_f = sigmoid(mod_ref[2:3]), sigmoid(mod_ref[5:6])

    def strip_of(index):
        return pl.ds(pl.multiple_of(index * strip, strip), strip)

    def norm_of(values):
        mean_value = jnp.mean(values, axis=1, keepdims=True)
        centred = values - mean_value
        spread = jnp.mean(centred * centred, axis=1, keepdims=True)
        root = lax.rsqrt(spread + 1e-06)
        return centred * root, root

    @pl.when(step == 0)
    def _():
        gate_pre[...] = wide_dot(normed_a_ref[...], gate_weight_ref[...])

        @pl.loop(0, strips)
        def _(index):
            cut = strip_of(index)
            gated[cut] = (attended_ref[cut] * sigmoid(gate_pre[cut])).astype(jnp.bfloat16)
            grad_ff[cut] = (upstream_ref[cut].astype(jnp.float32) * open_f).astype(jnp.bfloat16)

        branch[...] = wide_dot(gated[...], output_ref[...])

        @pl.loop(0, strips)
        def _(index):
            cut = strip_of(index)
            values = tokens_ref[cut].astype(jnp.float32) + open_a * branch[cut]
            middle[cut] = values
            normed[cut] = (norm_of(values)[0] * (1.0 + scale_f) + shift_f).astype(jnp.bfloat16)
            total[cut] = jnp.zeros((strip, width), jnp.float32)
            grad_normed[cut] = jnp.zeros((strip, width), jnp.float32)

        turned[...] = normed[...].T

    block = rows
    for start in range(0, rows, block):
        cut = slice(start, start + block)
        before = wide_dot(normed[cut], gate_ref[...])
        lifted = wide_dot(normed[cut], up_ref[...])
        grad_hidden = wide_dot(grad_ff[cut], down_ref[...], NT)
        switch = sigmoid(before)
        silu = before * switch
        part = (silu * lifted).astype(jnp.bfloat16)
        hidden[cut] = part
        grad_up = (grad_hidden * silu).astype(jnp.bfloat16)
        grad_gate = (grad_hidden * lifted * (switch + silu * (1.0 - switch))).astype(jnp.bfloat16)
        both[cut, :size] = grad_gate
        both[cut, size:] = grad_up
        total[cut] += wide_dot(part, down_ref[...])
        grad_normed[cut] += wide_dot(grad_gate, gate_ref[...], NT) + wide_dot(
            grad_up, up_ref[...], NT
        )

    pair = wide_dot(turned[...], both[...]).astype(jnp.bfloat16)
    if split:
        gate_send, gate_keep, up_send, up_keep, down_send, down_keep, small_send, small_keep = grads
        half = width // 2
        away = pl.ds(pl.multiple_of((1 - here) * half, LANES), half)
        home = pl.ds(pl.multiple_of(here * half, LANES), half)
        down_send[...] = wide_dot(hidden[...], grad_ff[:, away], TN).astype(jnp.bfloat16)
        down_keep[...] = wide_dot(hidden[...], grad_ff[:, home], TN).astype(jnp.bfloat16)

        @pl.when(step < chunks // 2)
        def _():
            gate_send[...] = pair[:, :size]
            up_send[...] = pair[:, size:]

        @pl.when(step >= chunks // 2)
        def _():
            gate_keep[...] = pair[:, :size]
            up_keep[...] = pair[:, size:]
    else:
        gate_all, up_all, down_all, small_all = grads
        gate_all[...] = pair[:, :size]
        up_all[...] = pair[:, size:]
        down_all[...] = wide_dot(hidden[...], grad_ff[...], TN).astype(jnp.bfloat16)

    @pl.when(step == chunks - 1)
    def _():
        def finish(index, sums):
            gate_f_sum, shift_sum, scale_sum, gate_a_sum = sums
            cut = strip_of(index)
            values = middle[cut]
            fed = total[cut]
            upstream = upstream_ref[cut].astype(jnp.float32)
            layer_ref[cut] = (values + open_f * fed).astype(jnp.bfloat16)
            normal, root = norm_of(values)
            grad = grad_normed[cut]
            scaled = grad * (1.0 + scale_f)
            grad_middle = upstream + root * (
                scaled
                - jnp.mean(scaled, axis=1, keepdims=True)
                - normal * jnp.mean(scaled * normal, axis=1, keepdims=True)
            )
            grad_middle_ref[cut] = grad_middle
            grad_branch[cut] = (grad_middle * open_a).astype(jnp.bfloat16)
            return (
                gate_f_sum + fold_rows(upstream * fed),
                shift_sum + fold_rows(grad),
                scale_sum + fold_rows(grad * normal),
                gate_a_sum + fold_rows(grad_middle * branch[cut]),
            )

        zero = jnp.zeros((8, width), jnp.float32)
        sums = lax.fori_loop(0, strips, finish, (zero, zero, zero, zero))
        gate_f_sum, shift_sum, scale_sum, gate_a_sum = [
            jnp.sum(value, axis=0, keepdims=True) for value in sums
        ]
        none = jnp.zeros((1, width), jnp.float32)
        sums_ref[...] = jnp.concatenate(
            [
                none,
                none,
                gate_a_sum * open_a * (1.0 - open_a),
                shift_sum,
                scale_sum,
                gate_f_sum * open_f * (1.0 - open_f),
                none,
                none,
            ],
            axis=0,
        )
        total[...] = wide_dot(grad_branch[...], output_ref[...], NT)

        @pl.loop(0, strips)
        def _(index):
            cut = strip_of(index)
            grad_gated = total[cut]
            opened = sigmoid(gate_pre[cut])
            grad_att_ref[cut] = (grad_gated * opened).astype(jnp.bfloat16)
            grad_pre_ref[cut] = (
                grad_gated * attended_ref[cut] * (opened * (1.0 - opened))
            ).astype(jnp.bfloat16)

        if split:
            for side, ref in ((away, small_send), (home, small_keep)):
                ref[:, :half] = wide_dot(gated[...], grad_branch[:, side], TN).astype(jnp.bfloat16)
                ref[:, half:] = wide_dot(normed_a_ref[...], grad_pre_ref[:, side], TN).astype(
                    jnp.bfloat16
                )
        else:
            small_all[:, :width] = wide_dot(gated[...], grad_branch[...], TN).astype(jnp.bfloat16)
            small_all[:, width:] = wide_dot(normed_a_ref[...], grad_pre_ref[...], TN).astype(
                jnp.bfloat16
            )


def feed_layer(
    split, here, attended, tokens, upstream, normed_a, mod_rows, gate_weight, output_weight, feed_gate, feed_up, feed_down
):
    rows, width = tokens.shape
    inner = feed_gate.shape[1]
    size = 512
    chunks = inner // size
    half = chunks // 2

    def turn(step, here_ref):
        return (step + half * (1 - here_ref[0])) % chunks if split else step

    def fixed(shape):
        return pl.BlockSpec(shape, lambda step, here_ref: (0, 0), pipeline_mode=pl.Buffered(1))

    def columns(step, here_ref):
        return (0, turn(step, here_ref))

    def strips(step, here_ref):
        return (turn(step, here_ref), 0)

    whole = (rows, width)
    in_specs = [fixed(whole)] * 4 + [
        fixed((8, width)),
        fixed((width, width)),
        fixed((width, width)),
        pl.BlockSpec((width, size), columns),
        pl.BlockSpec((width, size), columns),
        pl.BlockSpec((size, width), strips),
    ]
    out_specs = [fixed(whole)] * 4 + [fixed((8, width))]
    bf16, f32 = jnp.bfloat16, jnp.float32
    out_shapes = [(whole, bf16), (whole, f32), (whole, bf16), (whole, bf16), ((8, width), f32)]
    if split:
        first = pl.BlockSpec((width, size), lambda step, here_ref: (0, jnp.minimum(step, half - 1)))
        second = pl.BlockSpec((width, size), lambda step, here_ref: (0, jnp.maximum(step - half, 0)))
        out_specs += [first, second, first, second]
        out_shapes += [((width, inner // 2), bf16)] * 4
        out_specs += [pl.BlockSpec((size, width // 2), strips)] * 2
        out_shapes += [((inner, width // 2), bf16)] * 2
        out_specs += [fixed((width, width))] * 2
        out_shapes += [((width, width), bf16)] * 2
    else:
        out_specs += [pl.BlockSpec((width, size), columns)] * 2
        out_shapes += [((width, inner), bf16)] * 2
        out_specs += [pl.BlockSpec((size, width), strips), fixed((width, 2 * width))]
        out_shapes += [((inner, width), bf16), ((width, 2 * width), bf16)]
    return pl.pallas_call(
        functools.partial(feed_kernel, split, chunks),
        grid_spec=pltpu.PrefetchScalarGridSpec(
            num_scalar_prefetch=1,
            grid=(chunks,),
            in_specs=in_specs,
            out_specs=tuple(out_specs),
            scratch_shapes=[
                pltpu.VMEM(whole, bf16),
                pltpu.VMEM(whole, bf16),
                pltpu.VMEM(whole, bf16),
                pltpu.VMEM(whole, f32),
                pltpu.VMEM(whole, f32),
                pltpu.VMEM(whole, f32),
                pltpu.VMEM(whole, f32),
                pltpu.VMEM((rows, size), bf16),
                pltpu.VMEM((rows, 2 * size), bf16),
                pltpu.VMEM(whole, bf16),
                pltpu.VMEM(whole, f32),
                pltpu.VMEM((width, rows), bf16),
            ],
        ),
        out_shape=tuple(jax.ShapeDtypeStruct(shape, kind) for shape, kind in out_shapes),
        compiler_params=pltpu.CompilerParams(vmem_limit_bytes=VMEM_BYTES),
        cost_estimate=pl.CostEstimate(
            flops=2 * rows * width * (9 * inner + 5 * width),
            bytes_accessed=12 * width * inner + 24 * rows * width,
            transcendentals=2 * rows * inner,
        ),
        name="feed_layer",
    )(
        jnp.reshape(here, (1,)).astype(jnp.int32),
        attended,
        tokens,
        upstream,
        normed_a,
        mod_rows,
        gate_weight,
        output_weight,
        feed_gate,
        feed_up,
        feed_down,
    )


MASKS = {"u": 8, "v": 4, "y": 2, "x": 1}


def exchange(values, mask):
    return lax.ppermute(values, "crop", [(i, i ^ mask) for i in range(16)])


def swap_res(values):
    return lax.ppermute(values, "res", [(0, 1), (1, 0)])


def tie(*values):
    return lax.optimization_barrier(values)


def add_low(former, latter, kind=jnp.bfloat16):
    return (former.astype(jnp.float32) + latter.astype(jnp.float32)).astype(kind)


def stage_kernel(plans, bits_ref, *refs):
    inputs = refs[: sum(plan["count"] for plan in plans)]
    outputs = list(refs[len(inputs) :])
    for plan in plans:
        mine, inputs = inputs[: plan["count"]], inputs[plan["count"] :]
        out_ref = None if plan["apart"] else outputs[0]
        if not plan["apart"] and plan["merge"] is None:
            outputs.pop(0)
        for column, width, own in plan["parts"]:
            result = outputs.pop(0) if plan["apart"] else out_ref
            target = 0 if plan["apart"] else column
            lead_sizes = () if plan["merge"] is not None else result.shape[:-2]
            for lead in itertools.product(*[range(size) for size in lead_sizes]):
                for first in range(0, plan["rows"], 16):
                    cut = (*lead, slice(first, first + 16))
                    across = slice(column, column + width)
                    total = None
                    for index in own:
                        value = mine[index][(*cut, slice(0, width))].astype(jnp.float32)
                        total = value if total is None else total + value
                    for index in plan["spans"]:
                        total = total + mine[index][(*cut, across)].astype(jnp.float32)
                    fold, local = first // plan["block"], first % plan["block"]
                    if plan["folds"]:
                        value = mine[plan["folds"][fold]][local : local + 16, across]
                        total = total + value.astype(jnp.float32)
                    if plan["merge"] is None:
                        result[(*cut, slice(target, target + width))] = total.astype(result.dtype)
                    else:
                        begin = plan["merge"] + fold * plan["wide"] + column
                        result[local : local + 16, begin : begin + width] = total.astype(result.dtype)


class Halving:
    def __init__(self, streams, orders):
        self.streams = streams
        self.orders = [list(order) for order in orders]
        self.past = [[] for _ in orders]
        self.came = [[] for _ in orders]

    def stage(self, last=False, merge=False, merged=None):
        index = lax.axis_index("crop")
        bits = scalars(*[(index // mask) % 2 for mask in MASKS.values()])
        self.masks, plans, specs, operands, out_specs, out_shapes = [], [], [], [], [], []
        left = 0 if last else len(self.orders[0]) - 1
        fewest = min(parts[0][0][0].shape[0] for parts in self.streams) // 16
        begin = 0
        steps = {3: 4, 2: 2}.get(left, 1)
        for stream, (parts, order, past) in enumerate(zip(self.streams, self.orders, self.past)):
            now = None if last else order.pop(0)
            rest = [axis for axis in MASKS if axis in order]

            def spec_of(axes, rows, width, block, now=now, rest=rest):
                def index_map(step, bits_ref):
                    places = []
                    for axis in axes:
                        bit = bits_ref[list(MASKS).index(axis)]
                        if axis == now:
                            places.append(1 - bit)
                        elif axis not in rest:
                            places.append(bit)
                        elif axis == rest[0] and steps > 1:
                            places.append(step // (steps // 2))
                        elif len(rest) > 1 and axis == rest[1] and steps > 2:
                            places.append(step % 2)
                        else:
                            places.append(0)
                    return (*places, 0, block)

                sizes = [
                    2
                    if axis in rest
                    and not (axis == rest[0] and steps > 1)
                    and not (len(rest) > 1 and axis == rest[1] and steps > 2)
                    else None
                    for axis in axes
                ]
                return pl.BlockSpec((*sizes, rows, width), index_map)

            column = 0
            rows = parts[0][0][0].shape[0] // 16
            wide = sum(width for _, _, width in parts)
            plan = {
                "parts": [],
                "spans": [],
                "folds": [],
                "count": 0,
                "apart": last,
                "rows": rows,
                "block": fewest,
                "wide": wide,
                "merge": begin if merge else None,
            }
            for arrays, block, width in parts:
                own = []
                for value in arrays:
                    operands.append(value.reshape(2, 2, 2, 2, rows, value.shape[1]))
                    specs.append(spec_of(list(MASKS), rows, width, block))
                    own.append(plan["count"])
                    plan["count"] += 1
                plan["parts"].append((column, width, own))
                column += width
            for axes, value in self.came[stream]:
                operands.append(value.reshape(*[2] * len(axes), rows, column))
                specs.append(spec_of(axes, rows, column, 0))
                plan["spans"].append(plan["count"])
                plan["count"] += 1
            if merged is not None:
                for fold in range(rows // fewest):
                    place = (begin + fold * wide) // wide
                    operands.append(merged)
                    specs.append(
                        pl.BlockSpec((fewest, wide), lambda step, bits_ref, place=place: (0, place))
                    )
                    plan["folds"].append(plan["count"])
                    plan["count"] += 1
            begin += wide * (rows // fewest)
            plans.append(plan)
            if last:
                for _, width, _ in plan["parts"]:
                    out_specs.append(pl.BlockSpec((rows, width), lambda step, bits_ref: (0, 0)))
                    out_shapes.append(jax.ShapeDtypeStruct((rows, width), jnp.float32))
            else:
                past.append(now)
                self.masks.append(MASKS[now])
                if not merge:
                    out_specs.append(spec_of(rest, rows, column, 0))
                    out_shapes.append(
                        jax.ShapeDtypeStruct((*[2] * len(rest), rows, column), jnp.bfloat16)
                    )
        if merge:
            out_specs.append(pl.BlockSpec((fewest, begin), lambda step, bits_ref: (0, 0)))
            out_shapes.append(jax.ShapeDtypeStruct((fewest, begin), jnp.bfloat16))
        self.axes = [[axis for axis in MASKS if axis in order] for order in self.orders]
        results = pl.pallas_call(
            functools.partial(stage_kernel, plans),
            grid_spec=pltpu.PrefetchScalarGridSpec(
                num_scalar_prefetch=1, grid=(steps,), in_specs=specs, out_specs=tuple(out_specs)
            ),
            out_shape=tuple(out_shapes),
            compiler_params=pltpu.CompilerParams(vmem_limit_bytes=VMEM_BYTES),
            cost_estimate=pl.CostEstimate(
                flops=sum(4 * math.prod(shape.shape) for shape in out_shapes),
                bytes_accessed=sum(8 * math.prod(shape.shape) for shape in out_shapes),
                transcendentals=0,
            ),
            name="halving_stage",
        )(bits, *operands)
        if merge or last:
            return list(results)
        return [value.reshape(-1, value.shape[-1]) for value in results]

    def send(self, values):
        return [exchange(value, mask) for value, mask in zip(values, self.masks)]

    def take(self, values):
        for came, axes, value in zip(self.came, self.axes, values):
            came.append((axes, value))


def share_columns(values, parts):
    if parts == 1:
        return values.astype(jnp.bfloat16)
    return lax.psum_scatter(values.astype(jnp.bfloat16), "res", scatter_dimension=1, tiled=True)


def scatter_crops(values):
    return lax.psum_scatter(values, "crop", scatter_dimension=0, tiled=True).astype(jnp.float32)


def gather_crops(values, crop_parts):
    if crop_parts != 16:
        return lax.all_gather(values, "crop", axis=0, tiled=True)
    index = lax.axis_index("crop")
    for mask in (1, 2, 4, 8):
        other = exchange(values, mask)
        low = (index // mask) % 2 == 0
        values = jnp.concatenate(
            [jnp.where(low, values, other), jnp.where(low, other, values)], axis=0
        )
    return values


def sum_res(values, parts):
    if parts == 1:
        return values
    if parts != 2:
        return lax.psum(values, "res")
    return values + swap_res(values)


PACK = 1152
SIDE = 384


def whole_vmem(count):
    return [pl.BlockSpec(memory_space=pltpu.VMEM)] * count


def scalars(*values):
    return jnp.stack([jnp.asarray(value, jnp.int32) for value in values])


def local_call(kernel, numbers, operands, shapes, name, flops=0):
    return pl.pallas_call(
        kernel,
        in_specs=[pl.BlockSpec(memory_space=pltpu.SMEM)] + whole_vmem(len(operands)),
        out_specs=tuple(whole_vmem(len(shapes))),
        out_shape=tuple(jax.ShapeDtypeStruct(shape, kind) for shape, kind in shapes),
        compiler_params=pltpu.CompilerParams(vmem_limit_bytes=VMEM_BYTES),
        cost_estimate=pl.CostEstimate(
            flops=flops,
            bytes_accessed=sum(value.size * value.dtype.itemsize for value in operands)
            + sum(4 * math.prod(shape) for shape, _ in shapes),
            transcendentals=0,
        ),
        name=name,
    )(numbers, *operands)


def projection_kernel(counts, here_ref, normed_ref, *refs):
    calls = len(counts)
    parts, (joined_ref, send_ref, keep_ref) = refs[: 3 * calls], refs[3 * calls :]
    width = joined_ref.shape[1] // 3
    column = 0
    for call, pairs in enumerate(counts):
        size = pairs * LANES
        query_ref, own_ref, came_ref = parts[3 * call : 3 * call + 3]
        joined_ref[:, column : column + size] = query_ref[...]
        for start in range(0, joined_ref.shape[0], 16):
            cut = slice(start, start + 16)
            for which in range(2):
                first = (1 + which) * width + column
                joined_ref[cut, first : first + size] = add_low(
                    own_ref[which, cut], came_ref[which, cut]
                )
        column += size
    half = send_ref.shape[1]
    for side, ref in ((1 - here_ref[0], send_ref), (here_ref[0], keep_ref)):
        columns = pl.ds(pl.multiple_of(side * half, LANES), half)
        ref[...] = wide_dot(normed_ref[...], joined_ref[:, columns], TN).astype(jnp.bfloat16)


def projection_gradient(here, normed_a, calls):
    rows, width = normed_a.shape
    counts = [call[0].shape[-1] // LANES for call in calls]
    return local_call(
        functools.partial(projection_kernel, counts),
        scalars(here),
        [normed_a] + [value for call in calls for value in call],
        [
            ((rows, 3 * width), jnp.bfloat16),
            ((width, 3 * width // 2), jnp.bfloat16),
            ((width, 3 * width // 2), jnp.bfloat16),
        ],
        "projection_gradient",
        6 * rows * width * width,
    )


def finish_kernel(counts, joined_ref, weight_ref, pre_ref, gate_ref, tokens_ref, middle_ref, mod_ref, *refs):
    feed_sums_ref, extra_ref = refs[:2]
    table_refs = refs[2 : 2 + len(counts)]
    out_ref, pack_ref, total, folded = refs[2 + len(counts) :]
    step = pl.program_id(0)
    rows, width = tokens_ref.shape
    part = wide_dot(joined_ref[...], weight_ref[...], NT)

    @pl.when(step == 0)
    def _():
        total[...] = part + wide_dot(pre_ref[...], gate_ref[...], NT)

    @pl.when(step > 0)
    def _():
        total[...] += part

    @pl.when(step == pl.num_programs(0) - 1)
    def _():
        scale = mod_ref[1:2]
        folded[...] = jnp.zeros_like(folded)

        def finish(cut):
            values = tokens_ref[cut].astype(jnp.float32)
            centred = values - jnp.mean(values, axis=1, keepdims=True)
            root = lax.rsqrt(jnp.mean(centred * centred, axis=1, keepdims=True) + 1e-06)
            normal = centred * root
            grad = total[cut]
            folded[0] += fold_rows(grad)
            folded[1] += fold_rows(grad * normal)
            scaled = grad * (1.0 + scale)
            out_ref[cut] = (
                middle_ref[cut]
                + root
                * (
                    scaled
                    - jnp.mean(scaled, axis=1, keepdims=True)
                    - normal * jnp.mean(scaled * normal, axis=1, keepdims=True)
                )
            ).astype(jnp.bfloat16)

        each_strip(rows, finish)
        shift_sum, scale_sum = folded[0], folded[1]
        heads = []
        for ref, pairs in zip(table_refs, counts):
            for pair in range(pairs):
                heads += [ref[pair, 0:1], ref[pair, 1:2]]

        def upper_of(values):
            return values.astype(jnp.bfloat16).astype(jnp.float32)

        rests = [head - upper_of(head) for head in heads]
        count = width // LANES
        left = [
            jnp.sum(shift_sum, axis=0, keepdims=True),
            jnp.sum(scale_sum, axis=0, keepdims=True),
            feed_sums_ref[2:6],
        ]
        left += [
            jnp.concatenate(rests[i : i + count], axis=1) for i in range(0, len(heads), count)
        ]
        right = [jnp.concatenate(heads[3 * i : 3 * i + 3], axis=1) for i in range(4)]
        line = extra_ref[5:6]
        right += [extra_ref[4:5], line, line - upper_of(line), extra_ref[7:8]]
        pack = jnp.concatenate(
            [jnp.concatenate(left, axis=0), jnp.concatenate(right, axis=0)], axis=1
        )
        pack_ref[...] = jnp.concatenate([pack, jnp.zeros_like(pack)], axis=0).astype(jnp.bfloat16)


def finish_layer(
    joined, weight, grad_pre, gate_weight, tokens, grad_middle, mod_rows, feed_sums, extra, grad_tables
):
    rows, width = tokens.shape
    counts = [table.shape[0] for table in grad_tables]

    def fixed(shape):
        return pl.BlockSpec(shape, lambda step: (0,) * len(shape), pipeline_mode=pl.Buffered(1))

    return pl.pallas_call(
        functools.partial(finish_kernel, counts),
        grid=(3,),
        in_specs=[
            pl.BlockSpec((rows, width), lambda step: (0, step)),
            pl.BlockSpec((width, width), lambda step: (0, step)),
            fixed((rows, width)),
            fixed((width, width)),
            fixed((rows, width)),
            fixed((rows, width)),
            fixed((8, width)),
            fixed((8, width)),
            fixed((8, SIDE)),
        ]
        + [fixed((count, 8, LANES)) for count in counts],
        out_specs=(fixed((rows, width)), fixed((16, PACK))),
        out_shape=(
            jax.ShapeDtypeStruct((rows, width), jnp.bfloat16),
            jax.ShapeDtypeStruct((16, PACK), jnp.bfloat16),
        ),
        scratch_shapes=[
            pltpu.VMEM((rows, width), jnp.float32),
            pltpu.VMEM((2, 8, width), jnp.float32),
        ],
        compiler_params=pltpu.CompilerParams(vmem_limit_bytes=VMEM_BYTES),
        cost_estimate=pl.CostEstimate(
            flops=8 * rows * width * width, bytes_accessed=24 * rows * width, transcendentals=0
        ),
        name="finish_layer",
    )(
        joined,
        weight,
        grad_pre,
        gate_weight,
        tokens,
        grad_middle,
        mod_rows,
        feed_sums,
        extra,
        *grad_tables,
    )


def fan_first_kernel(bits_ref, keep_ref, came_ref, mine_ref, *send_refs):
    chunk = keep_ref.shape[0] // 16
    for other, ref in enumerate((mine_ref, *send_refs)):
        for level in range(4):
            start = (level * 4 + (bits_ref[0] ^ other)) * chunk
            for first in range(0, chunk, 16):
                cut = pl.ds(pl.multiple_of(start + first, 16), 16)
                place = level * chunk + first
                ref[place : place + 16] = add_low(keep_ref[cut], came_ref[cut])


def fan_v_kernel(bits_ref, mine_ref, *refs):
    came_refs, (send_ref, out_ref) = refs[:3], refs[3:]
    chunk = mine_ref.shape[0] // 4
    for side, ref in ((1 - bits_ref[0], send_ref), (bits_ref[0], out_ref)):
        for far in range(2):
            for first in range(0, chunk, 16):
                cut = pl.ds(pl.multiple_of((2 * far + side) * chunk + first, 16), 16)
                total = mine_ref[cut].astype(jnp.float32)
                for came_ref in came_refs:
                    total = total + came_ref[cut].astype(jnp.float32)
                place = far * chunk + first
                ref[place : place + 16] = total.astype(jnp.bfloat16)


def fan_u_kernel(bits_ref, mine_ref, came_ref, send_ref, out_ref):
    chunk = mine_ref.shape[0] // 2
    for side, ref in ((1 - bits_ref[0], send_ref), (bits_ref[0], out_ref)):
        for first in range(0, chunk, 16):
            cut = pl.ds(pl.multiple_of(side * chunk + first, 16), 16)
            ref[first : first + 16] = add_low(mine_ref[cut], came_ref[cut])


def join_packs_kernel(bits_ref, *refs):
    packs = [ref[...].astype(jnp.float32)[0:8] for ref in refs[:4]]
    refs[4][...] = jnp.concatenate(packs, axis=0).astype(jnp.bfloat16)


def small_kernel(
    heads,
    here_ref,
    mine_ref,
    came_ref,
    modulation_ref,
    pair_norm_ref,
    relative_ref,
    gain_ref,
    pair_weight_ref,
    mod_grad_ref,
    time_ref,
    label_ref,
    relative_grad_ref,
    gain_grad_ref,
    pair_grad_ref,
    grad_condition,
    grad_mod,
    kept,
):
    step = pl.program_id(0)
    crops = mine_ref.shape[0] // 8
    width = mine_ref.shape[1] - SIDE
    conds = relative_ref.shape[1]
    parts = mod_grad_ref.shape[1] // width

    def parts_split(values):
        upper = values.astype(jnp.bfloat16)
        return upper, (values - upper.astype(jnp.float32)).astype(jnp.bfloat16)

    def dot_left(narrow, values, numbers):
        upper, rest = parts_split(values)
        return wide_dot(narrow, upper, numbers) + wide_dot(narrow, rest, numbers)

    def dot_right(values, narrow, numbers):
        upper, rest = parts_split(values)
        return wide_dot(upper, narrow, numbers) + wide_dot(rest, narrow, numbers)

    def both_twice(narrow):
        return jnp.concatenate([narrow, narrow], axis=0)

    def stacked(values):
        return jnp.concatenate(parts_split(values), axis=0)

    @pl.when(step == 0)
    def _():
        shape = (8 * crops, 8 * crops)
        picked = lax.broadcasted_iota(jnp.int32, shape, 0)
        source = lax.broadcasted_iota(jnp.int32, shape, 1)
        hit = ((source >> 3) == (picked & (crops - 1))) & ((source & 7) == (picked // crops))
        select = jnp.where(hit, 1.0, 0.0).astype(jnp.bfloat16)
        mine = wide_dot(select, mine_ref[...])
        grad_mod[...] = mine[: 6 * crops, :width] + wide_dot(select, came_ref[...])[: 6 * crops, :width]
        condition = (
            mine[5 * crops : 6 * crops, width : width + conds]
            + mine[6 * crops : 7 * crops, width : width + conds]
        )
        gate_value = sigmoid(condition)
        kept[0] = condition * gate_value
        kept[1] = gate_value * (1.0 + condition * (1.0 - gate_value))
        kept[2] = mine[4 * crops : 5 * crops, width : width + conds]
        kept[3] = jnp.broadcast_to(
            mine[5 * crops : 6 * crops, width + conds : width + conds + 1]
            + mine[6 * crops : 7 * crops, width + conds : width + conds + 1],
            (crops, conds),
        )
        grad_condition[...] = jnp.zeros_like(grad_condition)

    cond_act = both_twice(kept[0].astype(jnp.bfloat16))
    for turn in range(parts):
        columns = slice(turn * width, (turn + 1) * width)
        first = pl.multiple_of((step * parts + turn) * crops, crops)
        pair = stacked(grad_mod[pl.ds(first, crops)])
        mod_grad_ref[:, columns] = wide_dot(cond_act, pair, TN)
        more = wide_dot(pair, modulation_ref[:, columns], NT)
        grad_condition[...] += more[:crops] + more[crops:]

    @pl.when(step == 0)
    def _():
        shape = (8, 8 * crops)
        line = lax.broadcasted_iota(jnp.int32, shape, 0)
        local = lax.broadcasted_iota(jnp.int32, shape, 1) & 7
        every = jnp.where(local == line, 1.0, 0.0).astype(jnp.bfloat16)
        lines = wide_dot(every, mine_ref[...]) + wide_dot(every, came_ref[...])

        def of_head(head):
            upper = width + (head % 3) * LANES
            rest = (head % (width // LANES)) * LANES
            low = 6 + head // (width // LANES)
            return (
                lines[head // 3 : head // 3 + 1, upper : upper + LANES]
                + lines[low : low + 1, rest : rest + LANES]
            )

        table = jnp.concatenate(
            [of_head(head) for head in range(heads)]
            + [jnp.zeros((16 - heads, LANES), jnp.float32)],
            axis=0,
        )
        bins = relative_ref.shape[0]
        pair_grad_ref[...] = dot_right(table, pair_norm_ref[...], (((1,), (0,)), ((), ())))[:heads]
        grad_norm = dot_right(table, pair_weight_ref[...], (((0,), (1,)), ((), ())))[:bins]
        values = relative_ref[...].astype(jnp.float32)
        centred = values - jnp.mean(values, axis=1, keepdims=True)
        root = lax.rsqrt(jnp.mean(centred * centred, axis=1, keepdims=True) + 1e-06)
        normal = centred * root
        gain_grad_ref[...] = jnp.sum(grad_norm * normal, axis=0, keepdims=True)
        scaled = grad_norm * gain_ref[...].astype(jnp.float32)
        relative_grad_ref[...] = root * (
            scaled
            - jnp.mean(scaled, axis=1, keepdims=True)
            - normal * jnp.mean(scaled * normal, axis=1, keepdims=True)
        )

    @pl.when(step == pl.num_programs(0) - 1)
    def _():
        final = stacked(grad_condition[...] * kept[1])
        time_ref[...] = wide_dot(both_twice(kept[2].astype(jnp.bfloat16)), final, TN)
        label = lax.broadcasted_iota(jnp.int32, (crops, label_ref.shape[0]), 1)
        number = kept[3][:, 0:1].astype(jnp.int32)
        onehot = jnp.where(label == number, 1.0, 0.0).astype(jnp.bfloat16)
        label_ref[...] = wide_dot(both_twice(onehot), final, TN)


def small_gradients(heads, labels, mine, came, modulation_weight, pair_norm, relative, gain, pair_weight):
    conds, wide = modulation_weight.shape
    bins = relative.shape[0]
    rows = mine.shape[0]
    steps = 3

    def fixed(shape):
        return pl.BlockSpec(shape, lambda step: (0, 0))

    shapes = [(conds, wide), (conds, conds), (labels, conds), (bins, conds), (1, conds), (heads, conds)]
    return pl.pallas_call(
        functools.partial(small_kernel, heads),
        grid=(steps,),
        in_specs=[
            pl.BlockSpec(memory_space=pltpu.SMEM),
            fixed((rows, PACK)),
            fixed((rows, PACK)),
            pl.BlockSpec((conds, wide // steps), lambda step: (0, step)),
            fixed((LANES, conds)),
            fixed((bins, conds)),
            fixed((1, conds)),
            fixed((conds, 16)),
        ],
        out_specs=tuple(
            [pl.BlockSpec((conds, wide // steps), lambda step: (0, step))]
            + [fixed(s) for s in shapes[1:]]
        ),
        out_shape=tuple(jax.ShapeDtypeStruct(shape, jnp.float32) for shape in shapes),
        scratch_shapes=[
            pltpu.VMEM((rows // 8, conds), jnp.float32),
            pltpu.VMEM((6 * rows // 8, wide // 6), jnp.float32),
            pltpu.VMEM((4, rows // 8, conds), jnp.float32),
        ],
        compiler_params=pltpu.CompilerParams(vmem_limit_bytes=VMEM_BYTES),
        cost_estimate=pl.CostEstimate(
            flops=100000000, bytes_accessed=10000000, transcendentals=0
        ),
        name="small_gradients",
    )(
        scalars(0),
        mine,
        came,
        modulation_weight,
        pair_norm,
        relative,
        gain,
        pair_weight,
    )


def per_device(
    crop_parts,
    res_parts,
    tokens,
    cotangent,
    time_levels,
    cath_ids,
    residue_numbers,
    chain_mask,
    time_weight,
    label_table,
    modulation_weight,
    projection_weight,
    gate_weight,
    output_weight,
    relative_table,
    pair_gain,
    pair_weight,
    feed_gate,
    feed_up,
    feed_down,
):
    crop_count, row_count, model_width = tokens.shape
    crop_length = residue_numbers.shape[1]
    head_count = pair_weight.shape[1]
    head_width = model_width // head_count
    bin_count = relative_table.shape[0]
    label_count = label_table.shape[0]
    token_count = crop_count * row_count
    score_scale = head_width ** (-0.5)
    pairs = head_count // 2
    layout = Layout(row_count, crop_length)
    query_start = lax.axis_index("res") * row_count

    def conditioning(features, onehot):
        return jnp.dot(features, time_weight, preferred_element_type=jnp.float32) + jnp.dot(
            onehot, label_table, preferred_element_type=jnp.float32
        )

    features = time_features(time_levels, time_weight.shape[0]).astype(jnp.bfloat16)
    label_onehot = (cath_ids[:, None] == jnp.arange(label_count, dtype=jnp.int32)[None, :]).astype(
        jnp.bfloat16
    )
    condition = conditioning(features, label_onehot)
    cond_act = jax.nn.silu(condition).astype(jnp.bfloat16)
    modulation = jnp.dot(cond_act, modulation_weight, preferred_element_type=jnp.float32)
    modulation = modulation.reshape(crop_count, 6, 1, model_width)
    shift_a, scale_a = modulation[:, 0], modulation[:, 1]
    mod_rows = pad_to(modulation[:, :, 0], 1, 8, 0.0)

    rotated = lax.dynamic_slice_in_dim(
        jnp.concatenate([jnp.stack([residue_numbers, chain_mask])] * 2, 2), query_start, crop_length, 2
    )
    members, kinds, forward_bins, backward_bins, places, *turned, tables, pair_norm = attention_tables(
        layout,
        score_scale,
        rotated[0],
        rotated[1],
        query_start,
        relative_table,
        pair_gain,
        pair_weight,
    )

    token_values = tokens.astype(jnp.float32)
    normed_a = (
        modulate(token_values, shift_a, scale_a)
        .astype(jnp.bfloat16)
        .reshape(token_count, model_width)
    )
    def project(weight):
        rows = jnp.dot(normed_a, weight, preferred_element_type=jnp.float32)
        return rows.astype(jnp.bfloat16).reshape(crop_count, row_count, -1)

    key_values = project(projection_weight[:, model_width:])
    others = [
        lax.ppermute(
            key_values, "res", [((r + step) % res_parts, r) for r in range(res_parts)]
        )
        for step in range(1, res_parts)
    ]
    if crop_count == 1 and others:
        line = jnp.concatenate(
            [condition, pad_to(cath_ids.astype(jnp.float32)[:, None], 1, LANES, 0.0)], axis=1
        )
        extra = jnp.concatenate([pad_to(features.astype(jnp.float32), 1, SIDE, 0.0), line], axis=0)
        others, extra = tie(others, jnp.pad(extra, ((4, 2), (0, 0))))
    if len(layout.pieces) == 2:
        other = others[0] if len(others) == 1 else jnp.concatenate(others, axis=1)
        pieces = [(key_values, 0, pairs), (other, 0, pairs)]
    else:
        pieces = [(jnp.concatenate([key_values] + others, axis=1), 0, pairs)]

    def block_rows(values):
        return pad_to(values, 1, layout.block_rows, 0)

    queries, attended, logs = attention_forward(
        layout,
        score_scale,
        block_rows(normed_a.reshape(tokens.shape)),
        projection_weight,
        pieces,
        members,
        kinds,
        forward_bins,
        tables,
    )
    here = lax.axis_index("res")
    split = res_parts == 2 and crop_parts == 16
    per_crop_results = [
        feed_layer(
            split,
            here,
            attended[crop],
            block_rows(tokens)[crop],
            block_rows(cotangent)[crop],
            block_rows(normed_a.reshape(tokens.shape))[crop],
            mod_rows[crop],
            gate_weight,
            output_weight,
            feed_gate,
            feed_up,
            feed_down,
        )
        for crop in range(crop_count)
    ]
    layer_out, grad_middle, grad_attended, grad_gate_pre, feed_sums = (
        jnp.stack([result[place] for result in per_crop_results]) for place in range(5)
    )
    layer_out, grad_middle = layer_out[:, :row_count], grad_middle[:, :row_count]
    grad_gate_pre = grad_gate_pre[:, :row_count].reshape(token_count, model_width)
    weight_grads = [
        sum(result[place].astype(jnp.float32) for result in per_crop_results).astype(jnp.bfloat16)
        if crop_count > 1
        else per_crop_results[0][place]
        for place in range(5, len(per_crop_results[0]))
    ]

    def backward_of(first_pair, count, grad_now):
        return attention_backward(
            layout,
            score_scale,
            first_pair,
            count,
            queries,
            grad_now,
            attended,
            logs,
            pieces,
            members,
            kinds,
            backward_bins,
            places,
            *turned,
            tables,
        )

    if split:
        arrivals = [swap_res(weight_grads[place]) for place in (0, 2, 4, 6)]
        kept = [weight_grads[place] for place in (1, 3, 5, 7)]
        half = model_width // 2
        inner = feed_gate.shape[1] // 2
        calls = [list(backward_of(0, 1, grad_attended))]
        arrivals, calls[0] = tie(arrivals, calls[0])
        gate_w, up_w, down_w, small_w = zip(kept, arrivals)
        halving = Halving(
            [
                [(gate_w, 0, inner), (small_w, 0, half)],
                [(up_w, 0, inner), (small_w, 1, half)],
                [(down_w, 0, half)],
            ],
            ["xyvu", "yvxu", "vxyu"],
        )
        arrived = []
        for first_pair, count in ((1, 4), (5, 1)):
            arrived.append(swap_res(calls[-1][2][0]))
            sent = halving.stage()
            sent, grad_attended = tie(sent, grad_attended)
            came = halving.send(sent)
            calls.append(list(backward_of(first_pair, count, grad_attended)))
            if count > 1:
                came, calls[-1], arrived[-1] = tie(came, calls[-1], arrived[-1])
                halving.take(came)
        index = lax.axis_index("crop")
        bf16 = jnp.bfloat16
        share = model_width // 16
        away = swap_res(calls[2][2][0])
        joined, proj_send, proj_keep = projection_gradient(
            here,
            normed_a,
            [
                (calls[0][0][0], calls[0][1][0], arrived[0]),
                (calls[1][0][0], calls[1][1][0], arrived[1]),
                (calls[2][0][0], calls[2][1][0], away),
            ],
        )
        came, proj_send, proj_keep = tie(came, proj_send, proj_keep)
        proj_came = swap_res(proj_send)
        halving.take(came)
        sent = halving.stage()
        sent, proj_came = tie(sent, proj_came)
        came = halving.send(sent)
        mine, *fan = local_call(
            fan_first_kernel,
            scalars(index % 4),
            [proj_keep, proj_came],
            [((4 * share, PACK), bf16)] * 4,
            "fan_first",
        )
        fan, came = tie(fan, came)
        fan_came = [exchange(value, mask + 1) for mask, value in enumerate(fan)]
        halving.take(came)
        (sent,) = halving.stage(merge=True)
        sent, joined = tie(sent, joined)
        last_came = exchange(sent, MASKS["u"])
        tokens_grad, pack = finish_layer(
            joined,
            projection_weight,
            grad_gate_pre,
            gate_weight,
            tokens[0],
            grad_middle[0],
            mod_rows[0],
            feed_sums[0],
            extra,
            [call[-1][0] for call in calls],
        )
        tokens_grad = tokens_grad[None]
        fan_came, pack = tie(fan_came, pack)
        packs = [pack] + [exchange(pack, 4 * (mask + 1)) for mask in range(3)]
        sent, mine = local_call(
            fan_v_kernel,
            scalars((index // 4) % 2),
            [mine, *fan_came],
            [((2 * share, PACK), bf16), ((2 * share, PACK), bf16)],
            "fan_v",
        )
        packs, sent = tie(packs, sent)
        came = exchange(sent, MASKS["v"])
        (packs,) = local_call(join_packs_kernel, scalars(0), packs, [((32, PACK), bf16)], "join_packs")
        far_packs = exchange(packs, MASKS["y"])
        packs = jnp.concatenate([packs, far_packs], axis=0)
        packs, last_came = tie(packs, last_came)
        far_packs = exchange(packs, MASKS["x"])
        finals = halving.stage(last=True, merged=last_came)
        feed_gate_grad, output_weight_grad, feed_up_grad, gate_weight_grad, feed_down_grad = finals
        far_packs, feed_down_grad = tie(far_packs, feed_down_grad)
        packs = jnp.concatenate([packs, far_packs], axis=0)
        came, packs = tie(came, packs)
        sent, mine = local_call(
            fan_u_kernel,
            scalars(index // 8),
            [mine, came],
            [((share, PACK), bf16), ((share, PACK), bf16)],
            "fan_u",
        )
        sent, packs = tie(sent, packs)
        came = exchange(sent, MASKS["u"])
        (
            modulation_weight_grad,
            time_weight_grad,
            label_table_grad,
            relative_table_grad,
            pair_gain_grad,
            pair_weight_grad,
        ) = small_gradients(
            head_count,
            label_count,
            packs,
            swap_res(packs),
            modulation_weight,
            pair_norm,
            relative_table,
            pair_gain.reshape(1, -1),
            pad_to(pair_weight, 1, 16, 0.0),
        )
        pair_weight_grad = pair_weight_grad.T
        came, pair_weight_grad = tie(came, pair_weight_grad)
        projection_weight_grad = add_low(mine, came, jnp.float32)
        pair_gain_grad = pair_gain_grad[0]
    else:
        results = backward_of(0, pairs, grad_attended)
        grad_table = results[-1]
        grad_pairs = results[1:-1]
        if len(grad_pairs) == 2:
            total, away = grad_pairs[0].astype(jnp.float32), grad_pairs[1]
        else:
            total = grad_pairs[0][:, :, :row_count].astype(jnp.float32)
            away = grad_pairs[0][:, :, row_count:]
        for step in range(1, res_parts):
            sent = away[:, :, (step - 1) * row_count : step * row_count]
            pairs_to = [(r, (r + step) % res_parts) for r in range(res_parts)]
            total = total + lax.ppermute(sent, "res", pairs_to).astype(jnp.float32)
        total = total.astype(jnp.bfloat16)
        grad_projected = jnp.concatenate(
            [results[0][:, :row_count], total[:, 0], total[:, 1]], axis=-1
        ).reshape(token_count, 3 * model_width)
        grad_normed_a = against_columns(grad_projected, projection_weight) + against_columns(
            grad_gate_pre, gate_weight
        )
        norm_back_a = jax.vjp(modulate, token_values, shift_a, scale_a)[1]
        grad_tokens, grad_shift_a, grad_scale_a = norm_back_a(
            grad_normed_a.reshape(crop_count, row_count, model_width)
        )
        tokens_grad = (grad_middle + grad_tokens).astype(jnp.bfloat16)
        feed_gate_grad, feed_up_grad, feed_down_grad = (
            scatter_crops(share_columns(value, res_parts)) for value in weight_grads[:3]
        )
        output_weight_grad, gate_weight_grad = (
            scatter_crops(share_columns(value, res_parts))
            for value in (weight_grads[3][:, :model_width], weight_grads[3][:, model_width:])
        )
        projection_weight_grad = scatter_crops(
            share_columns(across_rows(normed_a, grad_projected), res_parts)
        )
        grad_table = grad_table[:, :, :2].sum(0).reshape(head_count, LANES)

        grad_modulation = jnp.concatenate([grad_shift_a, grad_scale_a, feed_sums[:, 2:6]], axis=1)
        grad_modulation = grad_modulation.reshape(crop_count, 6 * model_width)
        table_row = grad_table.reshape(1, head_count * LANES)
        first_row = (jnp.arange(crop_count) == 0).astype(jnp.float32)[:, None]
        small_here = jnp.concatenate([grad_modulation, first_row * table_row], axis=1)
        levels_here = jnp.stack([time_levels, cath_ids.astype(jnp.float32)], axis=1)
        levels_here = pad_to(levels_here, 1, LANES, 0.0)
        small_all = gather_crops(
            jnp.concatenate([levels_here, sum_res(small_here, res_parts)], axis=1), crop_parts
        )
        levels_all, small_all = small_all[:, :2], small_all[:, LANES:]
        grad_modulation = small_all[:, : 6 * model_width]
        grad_table = jnp.sum(small_all[:, 6 * model_width :], axis=0).reshape(head_count, LANES)
        grad_table = grad_table[:, :bin_count]
        features_all = time_features(levels_all[:, 0], time_weight.shape[0]).astype(jnp.bfloat16)
        onehot_all = (
            levels_all[:, 1].astype(jnp.int32)[:, None]
            == jnp.arange(label_count, dtype=jnp.int32)[None, :]
        ).astype(jnp.bfloat16)
        condition = conditioning(features_all, onehot_all)
        cond_act = jax.nn.silu(condition).astype(jnp.bfloat16)
        modulation_weight_grad = split_left(cond_act, grad_modulation, 0, 0)
        grad_condition = split_left(modulation_weight, grad_modulation, 1, 1).T * silu_slope(condition)
        time_weight_grad = split_left(features_all, grad_condition, 0, 0)
        label_table_grad = split_left(onehot_all, grad_condition, 0, 0)
        relative_values = relative_table.astype(jnp.float32)
        gain_values = pair_gain.astype(jnp.float32)
        pair_norm = pair_norm[:bin_count]
        pair_weight_grad = split_left(pair_norm, grad_table, 0, 1)
        grad_pair_norm = split_right(grad_table, pair_weight, 0, 1)
        pair_back = jax.vjp(normalize_rows, relative_values, gain_values)[1]
        relative_table_grad, pair_gain_grad = pair_back(grad_pair_norm)
    return (
        layer_out,
        tokens_grad,
        time_weight_grad,
        label_table_grad,
        modulation_weight_grad,
        projection_weight_grad,
        gate_weight_grad,
        output_weight_grad,
        relative_table_grad,
        pair_gain_grad,
        pair_weight_grad,
        feed_gate_grad,
        feed_up_grad,
        feed_down_grad,
    )


def solution(mesh):
    return jax.shard_map(
        functools.partial(per_device, mesh.shape["crop"], mesh.shape["res"]),
        mesh=mesh,
        in_specs=(
            P("crop", "res", None),
            P("crop", "res", None),
            P("crop"),
            P("crop"),
            P("crop", None),
            P("crop", None),
            P(),
            P(),
            P(),
            P(),
            P(),
            P(),
            P(),
            P(),
            P(),
            P(),
            P(),
            P(),
        ),
        out_specs=(
            P("crop", "res", None),
            P("crop", "res", None),
            P(),
            P(),
            P(),
            P("crop", "res"),
            P("crop", "res"),
            P("crop", "res"),
            P(),
            P(),
            P(),
            P("crop", "res"),
            P("crop", "res"),
            P("crop", "res"),
        ),
        check_vma=False,
    )
```

```python
import functools
import itertools
import math

import jax
import jax.numpy as jnp
from jax import lax
from jax.experimental import pallas as pl
from jax.experimental.pallas import tpu as pltpu
from jax.sharding import PartitionSpec as P

LANES = 128
NEAR = 31
VMEM_BYTES = 56 * 1024 * 1024
QUERY_BLOCK = 384
KEY_BLOCK = 768
LOG2E = 1.4426950408889634
NONE, RIGHT, LEFT, APART = 0, 1, 2, 3


def layer_norm(inputs):
    mean_value = jnp.mean(inputs, axis=-1, keepdims=True)
    centred = inputs - mean_value
    spread = jnp.mean(centred * centred, axis=-1, keepdims=True)
    return centred * lax.rsqrt(spread + 1e-06)


def modulate(inputs, shift_row, scale_row):
    return layer_norm(inputs) * (1.0 + scale_row) + shift_row


def normalize_rows(table_rows, gain_row):
    return layer_norm(table_rows) * gain_row


def time_features(time_levels, feature_width):
    half_width = feature_width // 2
    frequency = jnp.exp(-math.log(10000.0) * jnp.arange(half_width, dtype=jnp.float32) / half_width)
    angles = 1000.0 * time_levels[:, None] * frequency[None, :]
    return jnp.concatenate([jnp.sin(angles), jnp.cos(angles)], axis=-1)


def across_rows(former, latter):
    return lax.dot_general(
        former, latter, (((0,), (0,)), ((), ())), preferred_element_type=jnp.float32
    )


def against_columns(former, latter):
    return lax.dot_general(
        former, latter, (((1,), (1,)), ((), ())), preferred_element_type=jnp.float32
    )


def split_parts(values):
    upper = lax.reduce_precision(values, 8, 7)
    return (upper.astype(jnp.bfloat16), (values - upper).astype(jnp.bfloat16))


def split_left(narrow, values, former_dim, latter_dim):
    upper, rest = split_parts(values)
    numbers = (((former_dim,), (latter_dim,)), ((), ()))
    return lax.dot_general(
        narrow, upper, numbers, preferred_element_type=jnp.float32
    ) + lax.dot_general(narrow, rest, numbers, preferred_element_type=jnp.float32)


def split_right(values, narrow, former_dim, latter_dim):
    upper, rest = split_parts(values)
    numbers = (((former_dim,), (latter_dim,)), ((), ()))
    return lax.dot_general(
        upper, narrow, numbers, preferred_element_type=jnp.float32
    ) + lax.dot_general(rest, narrow, numbers, preferred_element_type=jnp.float32)


def sigmoid_slope(inputs):
    gate_value = jax.nn.sigmoid(inputs)
    return gate_value * (1.0 - gate_value)


def silu_slope(inputs):
    gate_value = jax.nn.sigmoid(inputs)
    return gate_value * (1.0 + inputs * (1.0 - gate_value))


class Layout:
    def __init__(self, rows, length):
        self.rows = rows
        self.length = length
        self.query_tiles = -(-rows // LANES)
        self.key_tiles = -(-length // LANES)
        self.padded = self.query_tiles * LANES
        self.wide = self.key_tiles * LANES
        self.last = self.key_tiles - 1
        self.groups = (self.query_tiles + 4) * 4
        assert 2 * self.groups + 3 <= LANES and self.groups <= 64
        assert rows - 1 + NEAR < self.padded and length - NEAR >= self.last * LANES
        assert rows % 8 == 0 and self.last > self.query_tiles
        self.block_rows = rows if rows % 16 == 0 else self.padded
        self.pieces = [rows, length - rows] if rows % 16 == 0 else [length]

    def tile_start(self, tile):
        return self.last * LANES if tile < 0 else tile * LANES


def pad_to(values, axis, size, fill):
    widths = [(0, 0)] * values.ndim
    widths[axis] = (0, size - values.shape[axis])
    return jnp.pad(values, widths, constant_values=fill)


def tables_kernel(
    layout, bin_count, heads, scale, start_ref, pairs_ref, relative_ref, gain_ref, weight_ref, *out_refs
):
    members_ref, kinds_ref, forward_ref, backward_ref, places_ref = out_refs[:5]
    members_turned, kinds_turned, tables_ref, norm_ref, codes = out_refs[5:]
    rows, length, queries, groups = layout.rows, layout.length, layout.query_tiles, layout.groups
    wrap = length - start_ref[0]
    reach = (bin_count - 2) // 2
    zero_bin = LANES - 1
    shape = (LANES, LANES)
    lane = lax.broadcasted_iota(jnp.int32, shape, 1)
    row = lax.broadcasted_iota(jnp.int32, shape, 0)
    last_start = layout.last * LANES

    values = relative_ref[...].astype(jnp.float32)
    centred = values - jnp.mean(values, axis=1, keepdims=True)
    root = lax.rsqrt(jnp.mean(centred * centred, axis=1, keepdims=True) + 1e-06)
    pair_norm = (centred * root * gain_ref[...].astype(jnp.float32)).astype(jnp.bfloat16)
    norm_ref[...] = pair_norm
    bias = lax.dot_general(
        weight_ref[...], pair_norm, (((0,), (1,)), ((), ())), preferred_element_type=jnp.float32
    )
    head_lane = lax.broadcasted_iota(jnp.int32, bias.shape, 1)
    final = jnp.sum(jnp.where(head_lane == bin_count - 1, bias, 0.0), axis=1, keepdims=True)
    table = jnp.where(head_lane < bin_count, (bias - final) * (1.0 / scale), 0.0)

    def columns(number):
        value = jnp.sum(jnp.where(head_lane == number, table, 0.0), axis=1, keepdims=True)
        upper = value.astype(jnp.bfloat16).astype(jnp.float32)
        return jnp.where(
            head_lane < groups, upper, jnp.where(head_lane < 2 * groups, value - upper, 0.0)
        )

    right_columns, left_columns = columns(bin_count - 2), columns(0)
    for head in range(heads):
        line = 8 * (head % 2)
        for place, rows_of in enumerate((table, right_columns, left_columns)):
            tables_ref[head // 2, line + place : line + place + 1] = rows_of[head : head + 1]

    tiles = pairs_ref.shape[1]
    marks = pairs_ref[1].astype(jnp.float32)
    place = lax.broadcasted_iota(jnp.int32, marks.shape, 0) * LANES + lax.broadcasted_iota(
        jnp.int32, marks.shape, 1
    )
    before = jnp.sum(jnp.where(place < wrap, marks, 0.0), keepdims=True)
    every = jnp.sum(marks, keepdims=True)
    triangle = jnp.where(row <= lane, 1.0, 0.0).astype(jnp.bfloat16)
    running = jnp.dot(marks.astype(jnp.bfloat16), triangle, preferred_element_type=jnp.float32)
    numbers, chains = [], []
    carry = jnp.zeros((1, 1), jnp.float32)
    for tile in range(layout.key_tiles):
        count = running[tile : tile + 1] + carry
        carry = carry + running[tile : tile + 1, LANES - 1 :]
        count = count + jnp.where(place[tile : tile + 1] < wrap, every - before, -before)
        chains.append(jnp.broadcast_to(count.astype(jnp.int32), shape))
        numbers.append(jnp.broadcast_to(pairs_ref[0, tile : tile + 1], shape))
    number_rows = [value.T for value in numbers]
    chain_rows = [value.T for value in chains]

    def bins_of(key_number, key_chain, query_number, query_chain):
        offset = jnp.clip(key_number - query_number, -reach, reach) + reach
        return jnp.where(key_chain == query_chain, offset, bin_count - 1)

    def touches(query, tile):
        begin = -LANES if tile < 0 else tile * LANES
        return (begin <= query + NEAR) & (query - NEAR <= begin + LANES - 1)

    for tile in range(layout.key_tiles):
        size = min(LANES, length - tile * LANES)
        key = tile * LANES + row
        if tile == layout.last:
            other = jnp.full(shape, queries + 3, jnp.int32)
        elif tile == queries - 1:
            other = jnp.full(shape, queries, jnp.int32)
        else:
            other = jnp.where(key < wrap, queries + 1, queries + 2)
        group = jnp.where(key < rows, tile, other)
        slot = group * 4 + chain_rows[tile] - 1
        hit = (lane == slot) | (lane == slot + groups)
        tail = (lane >= 2 * groups) & (lane < 2 * groups + 3)
        values = jnp.where(hit, 1.0, jnp.where(tail, -1.0, 0.0)).astype(jnp.bfloat16)
        members_ref[tile * LANES : tile * LANES + size] = values[:size]
        turned = jnp.where(hit & (lane < groups), 1.0, 0.0).T
        members_turned[:, tile * LANES : tile * LANES + size] = turned[:64, :size].astype(jnp.bfloat16)

    local = jnp.where(lane >= groups, lane - groups, lane)
    lane_group = local >> 2
    lane_chain = (local & 3) + 1
    lane_begin = jnp.where(
        lane_group < queries,
        lane_group * LANES,
        jnp.where(lane_group == queries, (queries - 1) * LANES, -LANES),
    )
    has_band = (lane_group <= queries) | (lane_group == queries + 3)
    other_right = jnp.where(
        lane_group == queries,
        rows,
        jnp.where(
            lane_group == queries + 3,
            last_start,
            jnp.where(lane_group == queries + 1, 0, 2 * length),
        ),
    )
    right_limit = jnp.where(lane_group > queries, jnp.where(lane_group == queries + 3, wrap, length), wrap)
    for tile in range(queries):
        size = min(LANES, layout.block_rows - tile * LANES)
        query = tile * LANES + row
        near = (lane_begin <= query + NEAR) & (query - NEAR <= lane_begin + LANES - 1) & has_band
        right = jnp.where(lane_group < queries, lane_group - tile, right_limit - other_right) > 0
        same = chain_rows[tile] == lane_chain
        kinds = jnp.where(same, jnp.where(near, NONE, jnp.where(right, RIGHT, LEFT)), APART)
        kinds = jnp.where((lane < 2 * groups) & (query < rows), kinds, NONE)
        kinds_ref[tile * LANES : tile * LANES + size] = kinds[:size]
        kinds_turned[:, tile * LANES : (tile + 1) * LANES] = jnp.where(lane < groups, kinds, NONE).T[:64]
        for step in range(3):
            near_tile = tile + step - 1
            index = layout.last if near_tile < 0 else near_tile
            if near_tile < queries:
                inside = touches(query, near_tile) & (query < rows)
                inside &= lane < length - index * LANES
                found = bins_of(
                    numbers[index], chains[index], number_rows[tile], chain_rows[tile]
                )
                found = jnp.where(inside, found, zero_bin)
            else:
                found = jnp.full(shape, zero_bin, jnp.int32)
            forward_ref[
                tile * LANES : (tile + 1) * LANES, step * LANES : (step + 1) * LANES
            ] = found

    codes[...] = jnp.full(codes.shape, -1, jnp.int32)
    for tile in range(queries):
        size = min(LANES, rows - tile * LANES)
        code = number_rows[tile] * 8 + chain_rows[tile]
        codes[(tile + 1) * LANES : (tile + 1) * LANES + size] = code[:size]

    for index, tile in enumerate(list(range(queries)) + [-1]):
        source = layout.last if tile < 0 else tile
        key_row = (row - (length - last_start)) if tile < 0 else tile * LANES + row
        present = row < length - source * LANES
        for step in range(3):
            near_tile = tile + step - 1
            if 0 <= near_tile < queries:
                near_query = near_tile * LANES + lane
                inside = touches(near_query, tile) & (near_query < rows) & present
                found = bins_of(
                    number_rows[source], chain_rows[source], numbers[near_tile], chains[near_tile]
                )
                found = jnp.where(inside, found, zero_bin)
            else:
                found = jnp.full(shape, zero_bin, jnp.int32)
            backward_ref[
                index * LANES : (index + 1) * LANES, step * LANES : (step + 1) * LANES
            ] = found
        target = (number_rows[source] + reach - lane) * 8 + chain_rows[source]
        target = jnp.where(present & (lane > 0) & (lane < 2 * reach), target, -9)
        offset = (LANES - (length - last_start)) if tile < 0 else (tile + 1) * LANES
        far = 4 * LANES
        shift = jnp.full(shape, far, jnp.int32)
        for distance in range(-NEAR, NEAR + 1):
            other = codes[offset - distance : offset - distance + LANES]
            shift = jnp.where(other == target, distance, shift)
        if tile < 0:
            base = jnp.zeros(shape, jnp.int32)
        else:
            base = jnp.where(row < LANES // 2, tile - 1, tile) * LANES
        places_ref[index * LANES : (index + 1) * LANES] = jnp.where(
            shift == far, far - 1, key_row - shift - base
        )


def attention_tables(layout, scale, numbers, marks, query_start, relative_table, pair_gain, pair_weight):
    crops = numbers.shape[0]
    bin_count, width = relative_table.shape
    heads = pair_weight.shape[1]
    pairs = jnp.stack([numbers, marks], axis=1)
    pairs = pad_to(pairs, 2, layout.wide, 0).reshape(crops, 2, layout.key_tiles, LANES)
    spots = (layout.query_tiles + 1) * LANES
    shapes = [
        ((layout.length, LANES), jnp.bfloat16),
        ((layout.block_rows, LANES), jnp.int32),
        ((layout.padded, 3 * LANES), jnp.int32),
        ((spots, 3 * LANES), jnp.int32),
        ((spots, LANES), jnp.int32),
        ((64, layout.length), jnp.bfloat16),
        ((64, layout.padded), jnp.int32),
    ]
    shared = [((heads // 2, 16, LANES), jnp.float32), ((LANES, width), jnp.bfloat16)]

    def whole(shape):
        return pl.BlockSpec(shape, lambda crop: (0,) * len(shape))

    return pl.pallas_call(
        functools.partial(tables_kernel, layout, bin_count, heads, scale),
        grid=(crops,),
        in_specs=[
            pl.BlockSpec(memory_space=pltpu.SMEM),
            pl.BlockSpec((None, 2, layout.key_tiles, LANES), lambda crop: (crop, 0, 0, 0)),
            whole((LANES, width)),
            whole((1, width)),
            whole((width, 16)),
        ],
        out_specs=tuple(
            [pl.BlockSpec((None, *shape), lambda crop: (crop, 0, 0)) for shape, _ in shapes]
            + [whole(shape) for shape, _ in shared]
        ),
        out_shape=tuple(
            [jax.ShapeDtypeStruct((crops, *shape), kind) for shape, kind in shapes]
            + [jax.ShapeDtypeStruct(shape, kind) for shape, kind in shared]
        ),
        scratch_shapes=[pltpu.VMEM((layout.padded + 2 * LANES, LANES), jnp.int32)],
        compiler_params=pltpu.CompilerParams(vmem_limit_bytes=VMEM_BYTES),
        cost_estimate=pl.CostEstimate(
            flops=40000000 * crops, bytes_accessed=4000000 * crops, transcendentals=0
        ),
        name="pair_tables",
    )(
        jnp.reshape(query_start, (1,)).astype(jnp.int32),
        pairs,
        pad_to(relative_table, 0, LANES, 0.0),
        pair_gain.reshape(1, -1),
        pad_to(pair_weight, 1, 16, 0.0),
    )


NT = (((1,), (1,)), ((), ()))
TN = (((0,), (0,)), ((), ()))


def wide_dot(former, latter, numbers=(((1,), (0,)), ((), ()))):
    return lax.dot_general(former, latter, numbers, preferred_element_type=jnp.float32)


def look_up(table_row, bins):
    table = jnp.broadcast_to(table_row, bins.shape)
    return jnp.take_along_axis(table, bins, axis=1, mode="promise_in_bounds")


def half_of(values, lane, side):
    return jnp.where((lane >= 64) == (side == 1), values, jnp.zeros_like(values))


def row_blocks(total, size):
    return [(start, min(start + size, total)) for start in range(0, total, size)]


def group_columns(kinds, tables, side):
    right = tables[8 * side + 1 : 8 * side + 2]
    left = tables[8 * side + 2 : 8 * side + 3]
    return jnp.where(kinds == RIGHT, right, jnp.where(kinds == LEFT, left, 0.0))


def forward_kernel(layout, scale, *refs):
    count = len(layout.pieces)
    normed_ref, weight_ref = refs[:2]
    key_refs = refs[2 : 2 + count]
    value_refs = refs[2 + count : 2 + 2 * count]
    members_ref, kinds_ref, bins_ref, tables_ref, query_ref, out_ref, log_ref = refs[
        2 + 2 * count : -1
    ]
    all_scores = refs[-1]
    pair = pl.program_id(1)
    rows, length = layout.block_rows, layout.length
    turn = 0
    factor = scale * LOG2E
    lane = lax.broadcasted_iota(jnp.int32, (1, LANES), 1)
    query = wide_dot(normed_ref[...], weight_ref[...]).astype(jnp.bfloat16)
    query_ref[...] = query
    keys = jnp.concatenate([ref[...] for ref in key_refs], axis=0)
    values = jnp.concatenate([ref[...] for ref in value_refs], axis=0)
    members = members_ref[...]
    kinds = kinds_ref[...]
    tables = tables_ref[...]
    ones = jnp.ones((length, LANES), jnp.bfloat16)

    @pl.when(pair == 0)
    def _():
        log_ref[...] = jnp.zeros_like(log_ref)

    for side in range(2):
        key_columns = jnp.concatenate([half_of(keys, lane, side), members], axis=1)
        value_columns = jnp.concatenate([half_of(values, lane, side), ones], axis=1)
        extra = group_columns(kinds, tables, side).astype(jnp.bfloat16)
        query_columns = jnp.concatenate([query, extra], axis=1)
        table_row = tables[8 * side : 8 * side + 1]
        for start, stop in row_blocks(rows, QUERY_BLOCK):
            size = stop - start
            scores = all_scores.at[turn % 2]
            turn += 1
            scores[0:size, 0:length] = wide_dot(query_columns[start:stop], key_columns, NT)
            for tile in range(start // LANES, -(-stop // LANES)):
                first, final = tile * LANES, min(tile * LANES + LANES, rows)
                for slot in range(3):
                    other = tile + slot - 1
                    if other >= layout.query_tiles:
                        continue
                    low, high = first, final
                    if slot == 0:
                        high = min(first + 32, final)
                    if slot == 2:
                        low = first + LANES - 32
                    if low >= high:
                        continue
                    place = layout.tile_start(other)
                    width = min(LANES, length - place)
                    bins = bins_ref[low:high, slot * LANES : (slot + 1) * LANES]
                    bias = look_up(table_row, bins)[:, :width]
                    scores[low - start : high - start, place : place + width] += bias
            block = scores[0:size, 0:length]
            top = jnp.max(block, axis=1, keepdims=True)
            weights = jnp.exp2((block - top) * factor).astype(jnp.bfloat16)
            sums = wide_dot(weights, value_columns)
            total = sums[:, LANES:]
            result = sums[:, :LANES] / total
            if side == 0:
                out_ref[start:stop] = result
            else:
                out_ref[start:stop] += result
            log_total = top + jnp.log(total) * (1.0 / scale)
            log_ref[start:stop] = jnp.where(
                lane == 2 * pair + side, log_total, log_ref[start:stop]
            )


def backward_kernel(layout, scale, first_pair, *refs):
    count = len(layout.pieces)
    query_ref, grad_ref, out_ref, log_ref = refs[:4]
    key_refs = refs[4 : 4 + count]
    value_refs = refs[4 + count : 4 + 2 * count]
    rest = refs[4 + 2 * count :]
    members_ref, kinds_ref, bins_ref, places_ref, tables_ref = rest[:5]
    members_turned_ref, kinds_turned_ref = rest[5:7]
    grad_query_ref = rest[7]
    grad_pair_refs = rest[8 : 8 + count]
    grad_table_ref = rest[8 + count]
    query_wide, grad_wide, query_turned, grad_turned = rest[9 + count : 13 + count]
    all_scores, slopes_low, probs_low = rest[13 + count :]
    pair = pl.program_id(1) + first_pair
    rows, length, padded = layout.block_rows, layout.length, layout.padded
    factor = scale * LOG2E
    lane = lax.broadcasted_iota(jnp.int32, (1, LANES), 1)
    keys = jnp.concatenate([ref[...] for ref in key_refs], axis=0)
    values = jnp.concatenate([ref[...] for ref in value_refs], axis=0)
    members = members_ref[...]
    kinds = kinds_ref[...]
    tables = tables_ref[...]
    query = query_ref[...]
    grad = grad_ref[...]
    grad_full = grad.astype(jnp.float32)
    product = grad_full * out_ref[...]
    log_all = log_ref[...]
    tail = 2 * layout.groups
    ones = jnp.broadcast_to(jnp.where(lane < 3, 1.0, 0.0), (length, LANES)).astype(jnp.bfloat16)

    def three_parts(values):
        upper = values.astype(jnp.bfloat16).astype(jnp.float32)
        values = values - upper
        middle = values.astype(jnp.bfloat16).astype(jnp.float32)
        return upper, middle, values - middle

    def in_lanes(parts, first):
        return jnp.where(
            lane == first,
            parts[0],
            jnp.where(lane == first + 1, parts[1], jnp.where(lane == first + 2, parts[2], 0.0)),
        )

    if padded > rows:
        for ref in (query_wide, grad_wide):
            for side in range(2):
                ref[side, rows:padded] = jnp.zeros((padded - rows, ref.shape[2]), jnp.bfloat16)
        for ref in (query_turned, grad_turned):
            ref[:, rows:padded] = jnp.zeros((LANES, padded - rows), jnp.bfloat16)
    query_turned[:, 0:rows] = query.T
    grad_turned[:, 0:rows] = grad.T
    for side in range(2):
        log_total = jnp.sum(
            jnp.where(lane == 2 * pair + side, log_all, 0.0), axis=1, keepdims=True
        )
        extra = group_columns(kinds, tables, side) + in_lanes(three_parts(log_total), tail)
        query_wide[side, 0:rows, 0:LANES] = query
        query_wide[side, 0:rows, LANES:] = extra.astype(jnp.bfloat16)
        delta = jnp.sum(half_of(product, lane, side), axis=1, keepdims=True)
        grad_wide[side, 0:rows, 0:LANES] = grad
        grad_wide[side, 0:rows, LANES:] = in_lanes(three_parts(-delta), 0).astype(jnp.bfloat16)

    key_columns = [
        jnp.concatenate([half_of(keys, lane, side), members], axis=1) for side in range(2)
    ]
    value_columns = [
        jnp.concatenate([half_of(values, lane, side), ones], axis=1) for side in range(2)
    ]
    inner_sums = [jnp.zeros((1, LANES), jnp.float32) for _ in range(2)]
    low_sums = [jnp.zeros((1, LANES), jnp.float32) for _ in range(2)]
    high_sums = [jnp.zeros((1, LANES), jnp.float32) for _ in range(2)]
    reach_tiles = list(range(layout.query_tiles)) + [-1]

    def put(which, start, stop, result):
        begin = 0
        for ref, size in zip(grad_pair_refs, layout.pieces):
            low, high = max(start, begin), min(stop, begin + size)
            if low < high:
                ref[which, low - begin : high - begin] = result[low - start : high - start]
            begin += size

    for start, stop in row_blocks(length, KEY_BLOCK):
        size = stop - start
        for side in range(2):
            table_row = tables[8 * side : 8 * side + 1]
            scores = all_scores.at[side]
            scores[0:size] = wide_dot(key_columns[side][start:stop], query_wide[side], NT)
            near = []
            for index, tile in enumerate(reach_tiles):
                place = layout.tile_start(tile)
                if start <= place < stop:
                    near.append((index, tile, place, min(place + LANES, length)))
            for index, tile, place, final in near:
                for slot in range(3):
                    other = tile + slot - 1
                    if not 0 <= other < layout.query_tiles:
                        continue
                    bins = bins_ref[
                        index * LANES : index * LANES + final - place,
                        slot * LANES : (slot + 1) * LANES,
                    ]
                    scores[
                        place - start : final - start, other * LANES : (other + 1) * LANES
                    ] += look_up(table_row, bins)
            probs = jnp.exp2(scores[0:size] * factor).astype(jnp.bfloat16)
            grad_probs = wide_dot(value_columns[side][start:stop], grad_wide[side], NT)
            probs_low[side, start:stop] = probs
            slopes_low[side, start:stop] = probs * grad_probs.astype(jnp.bfloat16)
            for index, tile, place, final in near:
                for slot in range(3):
                    other = tile + slot - 1
                    if not 0 <= other < layout.query_tiles:
                        continue
                    bins = bins_ref[
                        index * LANES : index * LANES + final - place,
                        slot * LANES : (slot + 1) * LANES,
                    ]
                    cut = slopes_low[side, place:final, other * LANES : (other + 1) * LANES].astype(
                        jnp.float32
                    )
                    low_sums[side] += jnp.sum(
                        jnp.where(bins == 0, cut, 0.0), axis=0, keepdims=True
                    )
                    high_sums[side] += jnp.sum(
                        jnp.where(bins == 2 * (NEAR + 1), cut, 0.0), axis=0, keepdims=True
                    )
                for half in range(2):
                    begin, end = half * 64, min(half * 64 + 64, final - place)
                    if begin >= end:
                        continue
                    base = 0 if tile < 0 else tile - 1 + half
                    where = places_ref[index * LANES + begin : index * LANES + end]
                    spot = where & (LANES - 1)
                    for step in range(2):
                        other = base + step
                        if not 0 <= other < layout.query_tiles or (tile < 0 and step):
                            continue
                        cut = slopes_low[
                            side, place + begin : place + end, other * LANES : (other + 1) * LANES
                        ].astype(jnp.float32)
                        picked = jnp.take_along_axis(cut, spot, axis=1, mode="promise_in_bounds")
                        picked = jnp.where((where >> 7) == step, picked, 0.0)
                        inner_sums[side] += jnp.sum(picked, axis=0, keepdims=True)

    keys_turned = keys.T
    grad_keys, grad_values, grad_queries = [], [], []
    kinds_turned = kinds_turned_ref[...]
    for side in range(2):
        cut = slice(64 * side, 64 * side + 64)
        grad_values.append(wide_dot(grad_turned[cut], probs_low[side], NT))
        grad_keys.append(wide_dot(query_turned[cut], slopes_low[side], NT))
        left = jnp.concatenate([keys_turned[cut], members_turned_ref[...]], axis=0)
        both = wide_dot(left, slopes_low[side])
        grad_queries.append(both[:64])
        sums = both[64:]

        def total(kind):
            return jnp.sum(jnp.where(kinds_turned == kind, sums, 0.0))

        right = total(RIGHT) + jnp.sum(high_sums[side])
        left = total(LEFT) + jnp.sum(low_sums[side])
        apart = total(APART)
        grad_table_ref[side : side + 1] = jnp.where(
            lane == 0,
            left,
            jnp.where(
                lane == 2 * (NEAR + 1),
                right,
                jnp.where(lane == 2 * (NEAR + 1) + 1, apart, inner_sums[side]),
            ),
        )
    put(0, 0, length, (jnp.concatenate(grad_keys, axis=0) * scale).T.astype(jnp.bfloat16))
    put(1, 0, length, jnp.concatenate(grad_values, axis=0).T.astype(jnp.bfloat16))
    turned = jnp.concatenate(grad_queries, axis=0) * scale
    grad_query_ref[...] = turned.T[0:rows].astype(jnp.bfloat16)


def tile_columns(rows, offset=0):
    return pl.BlockSpec((None, rows, LANES), lambda crop, pair: (crop, 0, pair + offset))


def per_crop(rows, width):
    return pl.BlockSpec((None, rows, width), lambda crop, pair: (crop, 0, 0))


def kernel_params():
    return pltpu.CompilerParams(
        vmem_limit_bytes=VMEM_BYTES, dimension_semantics=("arbitrary", "arbitrary")
    )


def attention_forward(layout, scale, normed, weight, key_values, members, kinds, bins, tables):
    crops, rows, width = normed.shape
    pairs = tables.shape[0]
    specs = [per_crop(rows, width), pl.BlockSpec((width, LANES), lambda crop, pair: (0, pair))]
    operands = [normed, weight]
    for place in (1, 2):
        for piece in key_values:
            specs.append(tile_columns(piece[0].shape[1], piece[place]))
            operands.append(piece[0])
    specs += [
        per_crop(layout.length, LANES),
        per_crop(rows, LANES),
        per_crop(layout.padded, 3 * LANES),
        pl.BlockSpec((None, 16, LANES), lambda crop, pair: (pair, 0, 0)),
    ]
    flops = 2 * crops * pairs * 2 * rows * layout.length * 256 * 2
    return pl.pallas_call(
        functools.partial(forward_kernel, layout, scale),
        grid=(crops, pairs),
        in_specs=specs,
        out_specs=(tile_columns(rows), tile_columns(rows), per_crop(rows, LANES)),
        out_shape=(
            jax.ShapeDtypeStruct((crops, rows, pairs * LANES), jnp.bfloat16),
            jax.ShapeDtypeStruct((crops, rows, pairs * LANES), jnp.float32),
            jax.ShapeDtypeStruct((crops, rows, LANES), jnp.float32),
        ),
        scratch_shapes=[pltpu.VMEM((2, QUERY_BLOCK, layout.wide), jnp.float32)],
        compiler_params=kernel_params(),
        cost_estimate=pl.CostEstimate(
            flops=flops,
            bytes_accessed=12 * crops * rows * pairs * LANES,
            transcendentals=crops * pairs * 2 * rows * layout.length,
        ),
        name="attention_forward",
    )(*operands, members, kinds, bins, tables)


def attention_backward(
    layout,
    scale,
    first_pair,
    pairs,
    projected,
    grad_out,
    attended,
    logs,
    key_values,
    members,
    kinds,
    bins,
    places,
    members_turned,
    kinds_turned,
    tables,
):
    crops, rows, _ = projected.shape
    specs = [tile_columns(rows, first_pair)] * 3 + [per_crop(rows, LANES)]
    operands = [projected, grad_out, attended, logs]
    for place in (1, 2):
        for piece in key_values:
            specs.append(tile_columns(piece[0].shape[1], piece[place] + first_pair))
            operands.append(piece[0])
    specs += [
        per_crop(layout.length, LANES),
        per_crop(rows, LANES),
        per_crop(bins.shape[1], 3 * LANES),
        per_crop(places.shape[1], LANES),
        pl.BlockSpec((None, 16, LANES), lambda crop, pair: (pair + first_pair, 0, 0)),
        per_crop(64, layout.length),
        per_crop(64, layout.padded),
    ]
    out_specs = [tile_columns(rows)]
    out_shapes = [jax.ShapeDtypeStruct((crops, rows, pairs * LANES), jnp.bfloat16)]
    for piece in key_values:
        size = piece[0].shape[1]
        out_specs.append(
            pl.BlockSpec((None, 2, size, LANES), lambda crop, pair: (crop, 0, 0, pair))
        )
        out_shapes.append(jax.ShapeDtypeStruct((crops, 2, size, pairs * LANES), jnp.bfloat16))
    out_specs.append(pl.BlockSpec((None, None, 8, LANES), lambda crop, pair: (crop, pair, 0, 0)))
    out_shapes.append(jax.ShapeDtypeStruct((crops, pairs, 8, LANES), jnp.float32))
    padded = layout.padded
    return pl.pallas_call(
        functools.partial(backward_kernel, layout, scale, first_pair),
        grid=(crops, pairs),
        in_specs=specs,
        out_specs=tuple(out_specs),
        out_shape=tuple(out_shapes),
        scratch_shapes=[
            pltpu.VMEM((2, padded, 2 * LANES), jnp.bfloat16),
            pltpu.VMEM((2, padded, 2 * LANES), jnp.bfloat16),
            pltpu.VMEM((LANES, padded), jnp.bfloat16),
            pltpu.VMEM((LANES, padded), jnp.bfloat16),
            pltpu.VMEM((2, KEY_BLOCK, padded), jnp.float32),
            pltpu.VMEM((2, layout.length, padded), jnp.bfloat16),
            pltpu.VMEM((2, layout.length, padded), jnp.bfloat16),
        ],
        compiler_params=kernel_params(),
        cost_estimate=pl.CostEstimate(
            flops=2 * crops * pairs * 2 * rows * layout.length * 256 * 5,
            bytes_accessed=20 * crops * rows * pairs * LANES,
            transcendentals=crops * pairs * 2 * rows * layout.length,
        ),
        name="attention_backward",
    )(*operands, members, kinds, bins, places, tables, members_turned, kinds_turned)


def sigmoid(values):
    return 0.5 * jnp.tanh(0.5 * values) + 0.5


def each_strip(rows, body, size=16):
    count = rows // size
    group = max(number for number in range(1, 9) if count % number == 0)

    @pl.loop(0, count // group)
    def _(index):
        for part in range(group):
            body(pl.ds(pl.multiple_of((index * group + part) * size, size), size))


def fold_rows(values):
    return jnp.sum(values.reshape(values.shape[0] // 8, 8, values.shape[1]), axis=0)


def feed_kernel(split, chunks, here_ref, *refs):
    (attended_ref, tokens_ref, upstream_ref, normed_a_ref, mod_ref, gate_weight_ref, output_ref) = refs[:7]
    gate_ref, up_ref, down_ref = refs[7:10]
    layer_ref, grad_middle_ref, grad_att_ref, grad_pre_ref, sums_ref = refs[10:15]
    grads = refs[15:-12]
    gated, grad_ff, normed, branch, middle, total, grad_normed, hidden, both, grad_branch = refs[-12:-2]
    gate_pre, turned = refs[-2:]
    step = pl.program_id(0)
    here = here_ref[0]
    rows, width = tokens_ref.shape
    size = gate_ref.shape[1]
    strip = 112 if rows % 112 == 0 else 64
    strips = rows // strip
    shift_f, scale_f = mod_ref[3:4], mod_ref[4:5]
    open_a, open_f = sigmoid(mod_ref[2:3]), sigmoid(mod_ref[5:6])

    def strip_of(index):
        return pl.ds(pl.multiple_of(index * strip, strip), strip)

    def norm_of(values):
        mean_value = jnp.mean(values, axis=1, keepdims=True)
        centred = values - mean_value
        spread = jnp.mean(centred * centred, axis=1, keepdims=True)
        root = lax.rsqrt(spread + 1e-06)
        return centred * root, root

    @pl.when(step == 0)
    def _():
        gate_pre[...] = wide_dot(normed_a_ref[...], gate_weight_ref[...])

        @pl.loop(0, strips)
        def _(index):
            cut = strip_of(index)
            gated[cut] = (attended_ref[cut] * sigmoid(gate_pre[cut])).astype(jnp.bfloat16)
            grad_ff[cut] = (upstream_ref[cut].astype(jnp.float32) * open_f).astype(jnp.bfloat16)

        branch[...] = wide_dot(gated[...], output_ref[...])

        @pl.loop(0, strips)
        def _(index):
            cut = strip_of(index)
            values = tokens_ref[cut].astype(jnp.float32) + open_a * branch[cut]
            middle[cut] = values
            normed[cut] = (norm_of(values)[0] * (1.0 + scale_f) + shift_f).astype(jnp.bfloat16)
            total[cut] = jnp.zeros((strip, width), jnp.float32)
            grad_normed[cut] = jnp.zeros((strip, width), jnp.float32)

        turned[...] = normed[...].T

    block = rows
    for start in range(0, rows, block):
        cut = slice(start, start + block)
        before = wide_dot(normed[cut], gate_ref[...])
        lifted = wide_dot(normed[cut], up_ref[...])
        grad_hidden = wide_dot(grad_ff[cut], down_ref[...], NT)
        switch = sigmoid(before)
        silu = before * switch
        part = (silu * lifted).astype(jnp.bfloat16)
        hidden[cut] = part
        grad_up = (grad_hidden * silu).astype(jnp.bfloat16)
        grad_gate = (grad_hidden * lifted * (switch + silu * (1.0 - switch))).astype(jnp.bfloat16)
        both[cut, :size] = grad_gate
        both[cut, size:] = grad_up
        total[cut] += wide_dot(part, down_ref[...])
        grad_normed[cut] += wide_dot(grad_gate, gate_ref[...], NT) + wide_dot(
            grad_up, up_ref[...], NT
        )

    pair = wide_dot(turned[...], both[...]).astype(jnp.bfloat16)
    if split:
        gate_send, gate_keep, up_send, up_keep, down_send, down_keep, small_send, small_keep = grads
        half = width // 2
        away = pl.ds(pl.multiple_of((1 - here) * half, LANES), half)
        home = pl.ds(pl.multiple_of(here * half, LANES), half)
        down_send[...] = wide_dot(hidden[...], grad_ff[:, away], TN).astype(jnp.bfloat16)
        down_keep[...] = wide_dot(hidden[...], grad_ff[:, home], TN).astype(jnp.bfloat16)

        @pl.when(step < chunks // 2)
        def _():
            gate_send[...] = pair[:, :size]
            up_send[...] = pair[:, size:]

        @pl.when(step >= chunks // 2)
        def _():
            gate_keep[...] = pair[:, :size]
            up_keep[...] = pair[:, size:]
    else:
        gate_all, up_all, down_all, small_all = grads
        gate_all[...] = pair[:, :size]
        up_all[...] = pair[:, size:]
        down_all[...] = wide_dot(hidden[...], grad_ff[...], TN).astype(jnp.bfloat16)

    @pl.when(step == chunks - 1)
    def _():
        def finish(index, sums):
            gate_f_sum, shift_sum, scale_sum, gate_a_sum = sums
            cut = strip_of(index)
            values = middle[cut]
            fed = total[cut]
            upstream = upstream_ref[cut].astype(jnp.float32)
            layer_ref[cut] = (values + open_f * fed).astype(jnp.bfloat16)
            normal, root = norm_of(values)
            grad = grad_normed[cut]
            scaled = grad * (1.0 + scale_f)
            grad_middle = upstream + root * (
                scaled
                - jnp.mean(scaled, axis=1, keepdims=True)
                - normal * jnp.mean(scaled * normal, axis=1, keepdims=True)
            )
            grad_middle_ref[cut] = grad_middle
            grad_branch[cut] = (grad_middle * open_a).astype(jnp.bfloat16)
            return (
                gate_f_sum + fold_rows(upstream * fed),
                shift_sum + fold_rows(grad),
                scale_sum + fold_rows(grad * normal),
                gate_a_sum + fold_rows(grad_middle * branch[cut]),
            )

        zero = jnp.zeros((8, width), jnp.float32)
        sums = lax.fori_loop(0, strips, finish, (zero, zero, zero, zero))
        gate_f_sum, shift_sum, scale_sum, gate_a_sum = [
            jnp.sum(value, axis=0, keepdims=True) for value in sums
        ]
        none = jnp.zeros((1, width), jnp.float32)
        sums_ref[...] = jnp.concatenate(
            [
                none,
                none,
                gate_a_sum * open_a * (1.0 - open_a),
                shift_sum,
                scale_sum,
                gate_f_sum * open_f * (1.0 - open_f),
                none,
                none,
            ],
            axis=0,
        )
        total[...] = wide_dot(grad_branch[...], output_ref[...], NT)

        @pl.loop(0, strips)
        def _(index):
            cut = strip_of(index)
            grad_gated = total[cut]
            opened = sigmoid(gate_pre[cut])
            grad_att_ref[cut] = (grad_gated * opened).astype(jnp.bfloat16)
            grad_pre_ref[cut] = (
                grad_gated * attended_ref[cut] * (opened * (1.0 - opened))
            ).astype(jnp.bfloat16)

        if split:
            for side, ref in ((away, small_send), (home, small_keep)):
                ref[:, :half] = wide_dot(gated[...], grad_branch[:, side], TN).astype(jnp.bfloat16)
                ref[:, half:] = wide_dot(normed_a_ref[...], grad_pre_ref[:, side], TN).astype(
                    jnp.bfloat16
                )
        else:
            small_all[:, :width] = wide_dot(gated[...], grad_branch[...], TN).astype(jnp.bfloat16)
            small_all[:, width:] = wide_dot(normed_a_ref[...], grad_pre_ref[...], TN).astype(
                jnp.bfloat16
            )


def feed_layer(
    split, here, attended, tokens, upstream, normed_a, mod_rows, gate_weight, output_weight, feed_gate, feed_up, feed_down
):
    rows, width = tokens.shape
    inner = feed_gate.shape[1]
    size = 512
    chunks = inner // size
    half = chunks // 2

    def turn(step, here_ref):
        return (step + half * (1 - here_ref[0])) % chunks if split else step

    def fixed(shape):
        return pl.BlockSpec(shape, lambda step, here_ref: (0, 0), pipeline_mode=pl.Buffered(1))

    def columns(step, here_ref):
        return (0, turn(step, here_ref))

    def strips(step, here_ref):
        return (turn(step, here_ref), 0)

    whole = (rows, width)
    in_specs = [fixed(whole)] * 4 + [
        fixed((8, width)),
        fixed((width, width)),
        fixed((width, width)),
        pl.BlockSpec((width, size), columns),
        pl.BlockSpec((width, size), columns),
        pl.BlockSpec((size, width), strips),
    ]
    out_specs = [fixed(whole)] * 4 + [fixed((8, width))]
    bf16, f32 = jnp.bfloat16, jnp.float32
    out_shapes = [(whole, bf16), (whole, f32), (whole, bf16), (whole, bf16), ((8, width), f32)]
    if split:
        first = pl.BlockSpec((width, size), lambda step, here_ref: (0, jnp.minimum(step, half - 1)))
        second = pl.BlockSpec((width, size), lambda step, here_ref: (0, jnp.maximum(step - half, 0)))
        out_specs += [first, second, first, second]
        out_shapes += [((width, inner // 2), bf16)] * 4
        out_specs += [pl.BlockSpec((size, width // 2), strips)] * 2
        out_shapes += [((inner, width // 2), bf16)] * 2
        out_specs += [fixed((width, width))] * 2
        out_shapes += [((width, width), bf16)] * 2
    else:
        out_specs += [pl.BlockSpec((width, size), columns)] * 2
        out_shapes += [((width, inner), bf16)] * 2
        out_specs += [pl.BlockSpec((size, width), strips), fixed((width, 2 * width))]
        out_shapes += [((inner, width), bf16), ((width, 2 * width), bf16)]
    return pl.pallas_call(
        functools.partial(feed_kernel, split, chunks),
        grid_spec=pltpu.PrefetchScalarGridSpec(
            num_scalar_prefetch=1,
            grid=(chunks,),
            in_specs=in_specs,
            out_specs=tuple(out_specs),
            scratch_shapes=[
                pltpu.VMEM(whole, bf16),
                pltpu.VMEM(whole, bf16),
                pltpu.VMEM(whole, bf16),
                pltpu.VMEM(whole, f32),
                pltpu.VMEM(whole, f32),
                pltpu.VMEM(whole, f32),
                pltpu.VMEM(whole, f32),
                pltpu.VMEM((rows, size), bf16),
                pltpu.VMEM((rows, 2 * size), bf16),
                pltpu.VMEM(whole, bf16),
                pltpu.VMEM(whole, f32),
                pltpu.VMEM((width, rows), bf16),
            ],
        ),
        out_shape=tuple(jax.ShapeDtypeStruct(shape, kind) for shape, kind in out_shapes),
        compiler_params=pltpu.CompilerParams(vmem_limit_bytes=VMEM_BYTES),
        cost_estimate=pl.CostEstimate(
            flops=2 * rows * width * (9 * inner + 5 * width),
            bytes_accessed=12 * width * inner + 24 * rows * width,
            transcendentals=2 * rows * inner,
        ),
        name="feed_layer",
    )(
        jnp.reshape(here, (1,)).astype(jnp.int32),
        attended,
        tokens,
        upstream,
        normed_a,
        mod_rows,
        gate_weight,
        output_weight,
        feed_gate,
        feed_up,
        feed_down,
    )


MASKS = {"u": 8, "v": 4, "y": 2, "x": 1}


def exchange(values, mask):
    return lax.ppermute(values, "crop", [(i, i ^ mask) for i in range(16)])


def swap_res(values):
    return lax.ppermute(values, "res", [(0, 1), (1, 0)])


def tie(*values):
    return lax.optimization_barrier(values)


def add_low(former, latter, kind=jnp.bfloat16):
    return (former.astype(jnp.float32) + latter.astype(jnp.float32)).astype(kind)


def stage_kernel(plans, bits_ref, *refs):
    inputs = refs[: sum(plan["count"] for plan in plans)]
    outputs = list(refs[len(inputs) :])
    for plan in plans:
        mine, inputs = inputs[: plan["count"]], inputs[plan["count"] :]
        out_ref = None if plan["apart"] else outputs[0]
        if not plan["apart"] and plan["merge"] is None:
            outputs.pop(0)
        for column, width, own in plan["parts"]:
            result = outputs.pop(0) if plan["apart"] else out_ref
            target = 0 if plan["apart"] else column
            lead_sizes = () if plan["merge"] is not None else result.shape[:-2]
            for lead in itertools.product(*[range(size) for size in lead_sizes]):
                for first in range(0, plan["rows"], 16):
                    cut = (*lead, slice(first, first + 16))
                    across = slice(column, column + width)
                    total = None
                    for index in own:
                        value = mine[index][(*cut, slice(0, width))].astype(jnp.float32)
                        total = value if total is None else total + value
                    for index in plan["spans"]:
                        total = total + mine[index][(*cut, across)].astype(jnp.float32)
                    fold, local = first // plan["block"], first % plan["block"]
                    if plan["folds"]:
                        value = mine[plan["folds"][fold]][local : local + 16, across]
                        total = total + value.astype(jnp.float32)
                    if plan["merge"] is None:
                        result[(*cut, slice(target, target + width))] = total.astype(result.dtype)
                    else:
                        begin = plan["merge"] + fold * plan["wide"] + column
                        result[local : local + 16, begin : begin + width] = total.astype(result.dtype)


class Halving:
    def __init__(self, streams, orders):
        self.streams = streams
        self.orders = [list(order) for order in orders]
        self.past = [[] for _ in orders]
        self.came = [[] for _ in orders]

    def stage(self, last=False, merge=False, merged=None):
        index = lax.axis_index("crop")
        bits = scalars(*[(index // mask) % 2 for mask in MASKS.values()])
        self.masks, plans, specs, operands, out_specs, out_shapes = [], [], [], [], [], []
        left = 0 if last else len(self.orders[0]) - 1
        fewest = min(parts[0][0][0].shape[0] for parts in self.streams) // 16
        begin = 0
        steps = {3: 4, 2: 2}.get(left, 1)
        for stream, (parts, order, past) in enumerate(zip(self.streams, self.orders, self.past)):
            now = None if last else order.pop(0)
            rest = [axis for axis in MASKS if axis in order]

            def spec_of(axes, rows, width, block, now=now, rest=rest):
                def index_map(step, bits_ref):
                    places = []
                    for axis in axes:
                        bit = bits_ref[list(MASKS).index(axis)]
                        if axis == now:
                            places.append(1 - bit)
                        elif axis not in rest:
                            places.append(bit)
                        elif axis == rest[0] and steps > 1:
                            places.append(step // (steps // 2))
                        elif len(rest) > 1 and axis == rest[1] and steps > 2:
                            places.append(step % 2)
                        else:
                            places.append(0)
                    return (*places, 0, block)

                sizes = [
                    2
                    if axis in rest
                    and not (axis == rest[0] and steps > 1)
                    and not (len(rest) > 1 and axis == rest[1] and steps > 2)
                    else None
                    for axis in axes
                ]
                return pl.BlockSpec((*sizes, rows, width), index_map)

            column = 0
            rows = parts[0][0][0].shape[0] // 16
            wide = sum(width for _, _, width in parts)
            plan = {
                "parts": [],
                "spans": [],
                "folds": [],
                "count": 0,
                "apart": last,
                "rows": rows,
                "block": fewest,
                "wide": wide,
                "merge": begin if merge else None,
            }
            for arrays, block, width in parts:
                own = []
                for value in arrays:
                    operands.append(value.reshape(2, 2, 2, 2, rows, value.shape[1]))
                    specs.append(spec_of(list(MASKS), rows, width, block))
                    own.append(plan["count"])
                    plan["count"] += 1
                plan["parts"].append((column, width, own))
                column += width
            for axes, value in self.came[stream]:
                operands.append(value.reshape(*[2] * len(axes), rows, column))
                specs.append(spec_of(axes, rows, column, 0))
                plan["spans"].append(plan["count"])
                plan["count"] += 1
            if merged is not None:
                for fold in range(rows // fewest):
                    place = (begin + fold * wide) // wide
                    operands.append(merged)
                    specs.append(
                        pl.BlockSpec((fewest, wide), lambda step, bits_ref, place=place: (0, place))
                    )
                    plan["folds"].append(plan["count"])
                    plan["count"] += 1
            begin += wide * (rows // fewest)
            plans.append(plan)
            if last:
                for _, width, _ in plan["parts"]:
                    out_specs.append(pl.BlockSpec((rows, width), lambda step, bits_ref: (0, 0)))
                    out_shapes.append(jax.ShapeDtypeStruct((rows, width), jnp.float32))
            else:
                past.append(now)
                self.masks.append(MASKS[now])
                if not merge:
                    out_specs.append(spec_of(rest, rows, column, 0))
                    out_shapes.append(
                        jax.ShapeDtypeStruct((*[2] * len(rest), rows, column), jnp.bfloat16)
                    )
        if merge:
            out_specs.append(pl.BlockSpec((fewest, begin), lambda step, bits_ref: (0, 0)))
            out_shapes.append(jax.ShapeDtypeStruct((fewest, begin), jnp.bfloat16))
        self.axes = [[axis for axis in MASKS if axis in order] for order in self.orders]
        results = pl.pallas_call(
            functools.partial(stage_kernel, plans),
            grid_spec=pltpu.PrefetchScalarGridSpec(
                num_scalar_prefetch=1, grid=(steps,), in_specs=specs, out_specs=tuple(out_specs)
            ),
            out_shape=tuple(out_shapes),
            compiler_params=pltpu.CompilerParams(vmem_limit_bytes=VMEM_BYTES),
            cost_estimate=pl.CostEstimate(
                flops=sum(4 * math.prod(shape.shape) for shape in out_shapes),
                bytes_accessed=sum(8 * math.prod(shape.shape) for shape in out_shapes),
                transcendentals=0,
            ),
            name="halving_stage",
        )(bits, *operands)
        if merge or last:
            return list(results)
        return [value.reshape(-1, value.shape[-1]) for value in results]

    def send(self, values):
        return [exchange(value, mask) for value, mask in zip(values, self.masks)]

    def take(self, values):
        for came, axes, value in zip(self.came, self.axes, values):
            came.append((axes, value))


def share_columns(values, parts):
    if parts == 1:
        return values.astype(jnp.bfloat16)
    return lax.psum_scatter(values.astype(jnp.bfloat16), "res", scatter_dimension=1, tiled=True)


def scatter_crops(values):
    return lax.psum_scatter(values, "crop", scatter_dimension=0, tiled=True).astype(jnp.float32)


def gather_crops(values, crop_parts):
    if crop_parts != 16:
        return lax.all_gather(values, "crop", axis=0, tiled=True)
    index = lax.axis_index("crop")
    for mask in (1, 2, 4, 8):
        other = exchange(values, mask)
        low = (index // mask) % 2 == 0
        values = jnp.concatenate(
            [jnp.where(low, values, other), jnp.where(low, other, values)], axis=0
        )
    return values


def sum_res(values, parts):
    if parts == 1:
        return values
    if parts != 2:
        return lax.psum(values, "res")
    return values + swap_res(values)


PACK = 1152
SIDE = 384


def whole_vmem(count):
    return [pl.BlockSpec(memory_space=pltpu.VMEM)] * count


def scalars(*values):
    return jnp.stack([jnp.asarray(value, jnp.int32) for value in values])


def local_call(kernel, numbers, operands, shapes, name, flops=0):
    return pl.pallas_call(
        kernel,
        in_specs=[pl.BlockSpec(memory_space=pltpu.SMEM)] + whole_vmem(len(operands)),
        out_specs=tuple(whole_vmem(len(shapes))),
        out_shape=tuple(jax.ShapeDtypeStruct(shape, kind) for shape, kind in shapes),
        compiler_params=pltpu.CompilerParams(vmem_limit_bytes=VMEM_BYTES),
        cost_estimate=pl.CostEstimate(
            flops=flops,
            bytes_accessed=sum(value.size * value.dtype.itemsize for value in operands)
            + sum(4 * math.prod(shape) for shape, _ in shapes),
            transcendentals=0,
        ),
        name=name,
    )(numbers, *operands)


def projection_kernel(counts, here_ref, normed_ref, *refs):
    calls = len(counts)
    parts, (joined_ref, send_ref, keep_ref) = refs[: 3 * calls], refs[3 * calls :]
    width = joined_ref.shape[1] // 3
    column = 0
    for call, pairs in enumerate(counts):
        size = pairs * LANES
        query_ref, own_ref, came_ref = parts[3 * call : 3 * call + 3]
        joined_ref[:, column : column + size] = query_ref[...]
        for start in range(0, joined_ref.shape[0], 16):
            cut = slice(start, start + 16)
            for which in range(2):
                first = (1 + which) * width + column
                joined_ref[cut, first : first + size] = add_low(
                    own_ref[which, cut], came_ref[which, cut]
                )
        column += size
    half = send_ref.shape[1]
    for side, ref in ((1 - here_ref[0], send_ref), (here_ref[0], keep_ref)):
        columns = pl.ds(pl.multiple_of(side * half, LANES), half)
        ref[...] = wide_dot(normed_ref[...], joined_ref[:, columns], TN).astype(jnp.bfloat16)


def projection_gradient(here, normed_a, calls):
    rows, width = normed_a.shape
    counts = [call[0].shape[-1] // LANES for call in calls]
    return local_call(
        functools.partial(projection_kernel, counts),
        scalars(here),
        [normed_a] + [value for call in calls for value in call],
        [
            ((rows, 3 * width), jnp.bfloat16),
            ((width, 3 * width // 2), jnp.bfloat16),
            ((width, 3 * width // 2), jnp.bfloat16),
        ],
        "projection_gradient",
        6 * rows * width * width,
    )


def finish_kernel(counts, joined_ref, weight_ref, pre_ref, gate_ref, tokens_ref, middle_ref, mod_ref, *refs):
    feed_sums_ref, extra_ref = refs[:2]
    table_refs = refs[2 : 2 + len(counts)]
    out_ref, pack_ref, total, folded = refs[2 + len(counts) :]
    step = pl.program_id(0)
    rows, width = tokens_ref.shape
    part = wide_dot(joined_ref[...], weight_ref[...], NT)

    @pl.when(step == 0)
    def _():
        total[...] = part + wide_dot(pre_ref[...], gate_ref[...], NT)

    @pl.when(step > 0)
    def _():
        total[...] += part

    @pl.when(step == pl.num_programs(0) - 1)
    def _():
        scale = mod_ref[1:2]
        folded[...] = jnp.zeros_like(folded)

        def finish(cut):
            values = tokens_ref[cut].astype(jnp.float32)
            centred = values - jnp.mean(values, axis=1, keepdims=True)
            root = lax.rsqrt(jnp.mean(centred * centred, axis=1, keepdims=True) + 1e-06)
            normal = centred * root
            grad = total[cut]
            folded[0] += fold_rows(grad)
            folded[1] += fold_rows(grad * normal)
            scaled = grad * (1.0 + scale)
            out_ref[cut] = (
                middle_ref[cut]
                + root
                * (
                    scaled
                    - jnp.mean(scaled, axis=1, keepdims=True)
                    - normal * jnp.mean(scaled * normal, axis=1, keepdims=True)
                )
            ).astype(jnp.bfloat16)

        each_strip(rows, finish)
        shift_sum, scale_sum = folded[0], folded[1]
        heads = []
        for ref, pairs in zip(table_refs, counts):
            for pair in range(pairs):
                heads += [ref[pair, 0:1], ref[pair, 1:2]]

        def upper_of(values):
            return values.astype(jnp.bfloat16).astype(jnp.float32)

        rests = [head - upper_of(head) for head in heads]
        count = width // LANES
        left = [
            jnp.sum(shift_sum, axis=0, keepdims=True),
            jnp.sum(scale_sum, axis=0, keepdims=True),
            feed_sums_ref[2:6],
        ]
        left += [
            jnp.concatenate(rests[i : i + count], axis=1) for i in range(0, len(heads), count)
        ]
        right = [jnp.concatenate(heads[3 * i : 3 * i + 3], axis=1) for i in range(4)]
        line = extra_ref[5:6]
        right += [extra_ref[4:5], line, line - upper_of(line), extra_ref[7:8]]
        pack = jnp.concatenate(
            [jnp.concatenate(left, axis=0), jnp.concatenate(right, axis=0)], axis=1
        )
        pack_ref[...] = jnp.concatenate([pack, jnp.zeros_like(pack)], axis=0).astype(jnp.bfloat16)


def finish_layer(
    joined, weight, grad_pre, gate_weight, tokens, grad_middle, mod_rows, feed_sums, extra, grad_tables
):
    rows, width = tokens.shape
    counts = [table.shape[0] for table in grad_tables]

    def fixed(shape):
        return pl.BlockSpec(shape, lambda step: (0,) * len(shape), pipeline_mode=pl.Buffered(1))

    return pl.pallas_call(
        functools.partial(finish_kernel, counts),
        grid=(3,),
        in_specs=[
            pl.BlockSpec((rows, width), lambda step: (0, step)),
            pl.BlockSpec((width, width), lambda step: (0, step)),
            fixed((rows, width)),
            fixed((width, width)),
            fixed((rows, width)),
            fixed((rows, width)),
            fixed((8, width)),
            fixed((8, width)),
            fixed((8, SIDE)),
        ]
        + [fixed((count, 8, LANES)) for count in counts],
        out_specs=(fixed((rows, width)), fixed((16, PACK))),
        out_shape=(
            jax.ShapeDtypeStruct((rows, width), jnp.bfloat16),
            jax.ShapeDtypeStruct((16, PACK), jnp.bfloat16),
        ),
        scratch_shapes=[
            pltpu.VMEM((rows, width), jnp.float32),
            pltpu.VMEM((2, 8, width), jnp.float32),
        ],
        compiler_params=pltpu.CompilerParams(vmem_limit_bytes=VMEM_BYTES),
        cost_estimate=pl.CostEstimate(
            flops=8 * rows * width * width, bytes_accessed=24 * rows * width, transcendentals=0
        ),
        name="finish_layer",
    )(
        joined,
        weight,
        grad_pre,
        gate_weight,
        tokens,
        grad_middle,
        mod_rows,
        feed_sums,
        extra,
        *grad_tables,
    )


def fan_first_kernel(bits_ref, keep_ref, came_ref, mine_ref, *send_refs):
    chunk = keep_ref.shape[0] // 16
    for other, ref in enumerate((mine_ref, *send_refs)):
        for level in range(4):
            start = (level * 4 + (bits_ref[0] ^ other)) * chunk
            for first in range(0, chunk, 16):
                cut = pl.ds(pl.multiple_of(start + first, 16), 16)
                place = level * chunk + first
                ref[place : place + 16] = add_low(keep_ref[cut], came_ref[cut])


def fan_v_kernel(bits_ref, mine_ref, *refs):
    came_refs, (send_ref, out_ref) = refs[:3], refs[3:]
    chunk = mine_ref.shape[0] // 4
    for side, ref in ((1 - bits_ref[0], send_ref), (bits_ref[0], out_ref)):
        for far in range(2):
            for first in range(0, chunk, 16):
                cut = pl.ds(pl.multiple_of((2 * far + side) * chunk + first, 16), 16)
                total = mine_ref[cut].astype(jnp.float32)
                for came_ref in came_refs:
                    total = total + came_ref[cut].astype(jnp.float32)
                place = far * chunk + first
                ref[place : place + 16] = total.astype(jnp.bfloat16)


def fan_u_kernel(bits_ref, mine_ref, came_ref, send_ref, out_ref):
    chunk = mine_ref.shape[0] // 2
    for side, ref in ((1 - bits_ref[0], send_ref), (bits_ref[0], out_ref)):
        for first in range(0, chunk, 16):
            cut = pl.ds(pl.multiple_of(side * chunk + first, 16), 16)
            ref[first : first + 16] = add_low(mine_ref[cut], came_ref[cut])


def join_packs_kernel(bits_ref, *refs):
    packs = [ref[...].astype(jnp.float32)[0:8] for ref in refs[:4]]
    refs[4][...] = jnp.concatenate(packs, axis=0).astype(jnp.bfloat16)


def small_kernel(
    heads,
    here_ref,
    mine_ref,
    came_ref,
    modulation_ref,
    pair_norm_ref,
    relative_ref,
    gain_ref,
    pair_weight_ref,
    mod_grad_ref,
    time_ref,
    label_ref,
    relative_grad_ref,
    gain_grad_ref,
    pair_grad_ref,
    grad_condition,
    grad_mod,
    kept,
):
    step = pl.program_id(0)
    crops = mine_ref.shape[0] // 8
    width = mine_ref.shape[1] - SIDE
    conds = relative_ref.shape[1]
    parts = mod_grad_ref.shape[1] // width

    def parts_split(values):
        upper = values.astype(jnp.bfloat16)
        return upper, (values - upper.astype(jnp.float32)).astype(jnp.bfloat16)

    def dot_left(narrow, values, numbers):
        upper, rest = parts_split(values)
        return wide_dot(narrow, upper, numbers) + wide_dot(narrow, rest, numbers)

    def dot_right(values, narrow, numbers):
        upper, rest = parts_split(values)
        return wide_dot(upper, narrow, numbers) + wide_dot(rest, narrow, numbers)

    def both_twice(narrow):
        return jnp.concatenate([narrow, narrow], axis=0)

    def stacked(values):
        return jnp.concatenate(parts_split(values), axis=0)

    @pl.when(step == 0)
    def _():
        shape = (8 * crops, 8 * crops)
        picked = lax.broadcasted_iota(jnp.int32, shape, 0)
        source = lax.broadcasted_iota(jnp.int32, shape, 1)
        hit = ((source >> 3) == (picked & (crops - 1))) & ((source & 7) == (picked // crops))
        select = jnp.where(hit, 1.0, 0.0).astype(jnp.bfloat16)
        mine = wide_dot(select, mine_ref[...])
        grad_mod[...] = mine[: 6 * crops, :width] + wide_dot(select, came_ref[...])[: 6 * crops, :width]
        condition = (
            mine[5 * crops : 6 * crops, width : width + conds]
            + mine[6 * crops : 7 * crops, width : width + conds]
        )
        gate_value = sigmoid(condition)
        kept[0] = condition * gate_value
        kept[1] = gate_value * (1.0 + condition * (1.0 - gate_value))
        kept[2] = mine[4 * crops : 5 * crops, width : width + conds]
        kept[3] = jnp.broadcast_to(
            mine[5 * crops : 6 * crops, width + conds : width + conds + 1]
            + mine[6 * crops : 7 * crops, width + conds : width + conds + 1],
            (crops, conds),
        )
        grad_condition[...] = jnp.zeros_like(grad_condition)

    cond_act = both_twice(kept[0].astype(jnp.bfloat16))
    for turn in range(parts):
        columns = slice(turn * width, (turn + 1) * width)
        first = pl.multiple_of((step * parts + turn) * crops, crops)
        pair = stacked(grad_mod[pl.ds(first, crops)])
        mod_grad_ref[:, columns] = wide_dot(cond_act, pair, TN)
        more = wide_dot(pair, modulation_ref[:, columns], NT)
        grad_condition[...] += more[:crops] + more[crops:]

    @pl.when(step == 0)
    def _():
        shape = (8, 8 * crops)
        line = lax.broadcasted_iota(jnp.int32, shape, 0)
        local = lax.broadcasted_iota(jnp.int32, shape, 1) & 7
        every = jnp.where(local == line, 1.0, 0.0).astype(jnp.bfloat16)
        lines = wide_dot(every, mine_ref[...]) + wide_dot(every, came_ref[...])

        def of_head(head):
            upper = width + (head % 3) * LANES
            rest = (head % (width // LANES)) * LANES
            low = 6 + head // (width // LANES)
            return (
                lines[head // 3 : head // 3 + 1, upper : upper + LANES]
                + lines[low : low + 1, rest : rest + LANES]
            )

        table = jnp.concatenate(
            [of_head(head) for head in range(heads)]
            + [jnp.zeros((16 - heads, LANES), jnp.float32)],
            axis=0,
        )
        bins = relative_ref.shape[0]
        pair_grad_ref[...] = dot_right(table, pair_norm_ref[...], (((1,), (0,)), ((), ())))[:heads]
        grad_norm = dot_right(table, pair_weight_ref[...], (((0,), (1,)), ((), ())))[:bins]
        values = relative_ref[...].astype(jnp.float32)
        centred = values - jnp.mean(values, axis=1, keepdims=True)
        root = lax.rsqrt(jnp.mean(centred * centred, axis=1, keepdims=True) + 1e-06)
        normal = centred * root
        gain_grad_ref[...] = jnp.sum(grad_norm * normal, axis=0, keepdims=True)
        scaled = grad_norm * gain_ref[...].astype(jnp.float32)
        relative_grad_ref[...] = root * (
            scaled
            - jnp.mean(scaled, axis=1, keepdims=True)
            - normal * jnp.mean(scaled * normal, axis=1, keepdims=True)
        )

    @pl.when(step == pl.num_programs(0) - 1)
    def _():
        final = stacked(grad_condition[...] * kept[1])
        time_ref[...] = wide_dot(both_twice(kept[2].astype(jnp.bfloat16)), final, TN)
        label = lax.broadcasted_iota(jnp.int32, (crops, label_ref.shape[0]), 1)
        number = kept[3][:, 0:1].astype(jnp.int32)
        onehot = jnp.where(label == number, 1.0, 0.0).astype(jnp.bfloat16)
        label_ref[...] = wide_dot(both_twice(onehot), final, TN)


def small_gradients(heads, labels, mine, came, modulation_weight, pair_norm, relative, gain, pair_weight):
    conds, wide = modulation_weight.shape
    bins = relative.shape[0]
    rows = mine.shape[0]
    steps = 3

    def fixed(shape):
        return pl.BlockSpec(shape, lambda step: (0, 0))

    shapes = [(conds, wide), (conds, conds), (labels, conds), (bins, conds), (1, conds), (heads, conds)]
    return pl.pallas_call(
        functools.partial(small_kernel, heads),
        grid=(steps,),
        in_specs=[
            pl.BlockSpec(memory_space=pltpu.SMEM),
            fixed((rows, PACK)),
            fixed((rows, PACK)),
            pl.BlockSpec((conds, wide // steps), lambda step: (0, step)),
            fixed((LANES, conds)),
            fixed((bins, conds)),
            fixed((1, conds)),
            fixed((conds, 16)),
        ],
        out_specs=tuple(
            [pl.BlockSpec((conds, wide // steps), lambda step: (0, step))]
            + [fixed(s) for s in shapes[1:]]
        ),
        out_shape=tuple(jax.ShapeDtypeStruct(shape, jnp.float32) for shape in shapes),
        scratch_shapes=[
            pltpu.VMEM((rows // 8, conds), jnp.float32),
            pltpu.VMEM((6 * rows // 8, wide // 6), jnp.float32),
            pltpu.VMEM((4, rows // 8, conds), jnp.float32),
        ],
        compiler_params=pltpu.CompilerParams(vmem_limit_bytes=VMEM_BYTES),
        cost_estimate=pl.CostEstimate(
            flops=100000000, bytes_accessed=10000000, transcendentals=0
        ),
        name="small_gradients",
    )(
        scalars(0),
        mine,
        came,
        modulation_weight,
        pair_norm,
        relative,
        gain,
        pair_weight,
    )


def per_device(
    crop_parts,
    res_parts,
    tokens,
    cotangent,
    time_levels,
    cath_ids,
    residue_numbers,
    chain_mask,
    time_weight,
    label_table,
    modulation_weight,
    projection_weight,
    gate_weight,
    output_weight,
    relative_table,
    pair_gain,
    pair_weight,
    feed_gate,
    feed_up,
    feed_down,
):
    crop_count, row_count, model_width = tokens.shape
    crop_length = residue_numbers.shape[1]
    head_count = pair_weight.shape[1]
    head_width = model_width // head_count
    bin_count = relative_table.shape[0]
    label_count = label_table.shape[0]
    token_count = crop_count * row_count
    score_scale = head_width ** (-0.5)
    pairs = head_count // 2
    layout = Layout(row_count, crop_length)
    query_start = lax.axis_index("res") * row_count

    def conditioning(features, onehot):
        return jnp.dot(features, time_weight, preferred_element_type=jnp.float32) + jnp.dot(
            onehot, label_table, preferred_element_type=jnp.float32
        )

    features = time_features(time_levels, time_weight.shape[0]).astype(jnp.bfloat16)
    label_onehot = (cath_ids[:, None] == jnp.arange(label_count, dtype=jnp.int32)[None, :]).astype(
        jnp.bfloat16
    )
    condition = conditioning(features, label_onehot)
    cond_act = jax.nn.silu(condition).astype(jnp.bfloat16)
    modulation = jnp.dot(cond_act, modulation_weight, preferred_element_type=jnp.float32)
    modulation = modulation.reshape(crop_count, 6, 1, model_width)
    shift_a, scale_a = modulation[:, 0], modulation[:, 1]
    mod_rows = pad_to(modulation[:, :, 0], 1, 8, 0.0)

    rotated = lax.dynamic_slice_in_dim(
        jnp.concatenate([jnp.stack([residue_numbers, chain_mask])] * 2, 2), query_start, crop_length, 2
    )
    members, kinds, forward_bins, backward_bins, places, *turned, tables, pair_norm = attention_tables(
        layout,
        score_scale,
        rotated[0],
        rotated[1],
        query_start,
        relative_table,
        pair_gain,
        pair_weight,
    )

    token_values = tokens.astype(jnp.float32)
    normed_a = (
        modulate(token_values, shift_a, scale_a)
        .astype(jnp.bfloat16)
        .reshape(token_count, model_width)
    )
    (normed_a,) = tie(normed_a)

    def project(weight):
        rows = jnp.dot(normed_a, weight, preferred_element_type=jnp.float32)
        return rows.astype(jnp.bfloat16).reshape(crop_count, row_count, -1)

    key_values = project(projection_weight[:, model_width:])
    others = [
        lax.ppermute(
            key_values, "res", [((r + step) % res_parts, r) for r in range(res_parts)]
        )
        for step in range(1, res_parts)
    ]
    if crop_count == 1 and others:
        line = jnp.concatenate(
            [condition, pad_to(cath_ids.astype(jnp.float32)[:, None], 1, LANES, 0.0)], axis=1
        )
        extra = jnp.concatenate([pad_to(features.astype(jnp.float32), 1, SIDE, 0.0), line], axis=0)
        others, extra = tie(others, jnp.pad(extra, ((4, 2), (0, 0))))
    if len(layout.pieces) == 2:
        other = others[0] if len(others) == 1 else jnp.concatenate(others, axis=1)
        pieces = [(key_values, 0, pairs), (other, 0, pairs)]
    else:
        pieces = [(jnp.concatenate([key_values] + others, axis=1), 0, pairs)]

    def block_rows(values):
        return pad_to(values, 1, layout.block_rows, 0)

    queries, attended, logs = attention_forward(
        layout,
        score_scale,
        block_rows(normed_a.reshape(tokens.shape)),
        projection_weight,
        pieces,
        members,
        kinds,
        forward_bins,
        tables,
    )
    here = lax.axis_index("res")
    split = res_parts == 2 and crop_parts == 16
    per_crop_results = [
        feed_layer(
            split,
            here,
            attended[crop],
            block_rows(tokens)[crop],
            block_rows(cotangent)[crop],
            block_rows(normed_a.reshape(tokens.shape))[crop],
            mod_rows[crop],
            gate_weight,
            output_weight,
            feed_gate,
            feed_up,
            feed_down,
        )
        for crop in range(crop_count)
    ]
    layer_out, grad_middle, grad_attended, grad_gate_pre, feed_sums = (
        jnp.stack([result[place] for result in per_crop_results]) for place in range(5)
    )
    layer_out, grad_middle = layer_out[:, :row_count], grad_middle[:, :row_count]
    grad_gate_pre = grad_gate_pre[:, :row_count].reshape(token_count, model_width)
    weight_grads = [
        sum(result[place].astype(jnp.float32) for result in per_crop_results).astype(jnp.bfloat16)
        if crop_count > 1
        else per_crop_results[0][place]
        for place in range(5, len(per_crop_results[0]))
    ]

    def backward_of(first_pair, count, grad_now):
        return attention_backward(
            layout,
            score_scale,
            first_pair,
            count,
            queries,
            grad_now,
            attended,
            logs,
            pieces,
            members,
            kinds,
            backward_bins,
            places,
            *turned,
            tables,
        )

    if split:
        arrivals = [swap_res(weight_grads[place]) for place in (0, 2, 4, 6)]
        kept = [weight_grads[place] for place in (1, 3, 5, 7)]
        half = model_width // 2
        inner = feed_gate.shape[1] // 2
        calls = [list(backward_of(0, 1, grad_attended))]
        arrivals, calls[0] = tie(arrivals, calls[0])
        gate_w, up_w, down_w, small_w = zip(kept, arrivals)
        halving = Halving(
            [
                [(gate_w, 0, inner), (small_w, 0, half)],
                [(up_w, 0, inner), (small_w, 1, half)],
                [(down_w, 0, half)],
            ],
            ["xyvu", "yvxu", "vxyu"],
        )
        arrived = []
        for first_pair, count in ((1, 4), (5, 1)):
            arrived.append(swap_res(calls[-1][2][0]))
            sent = halving.stage()
            sent, grad_attended = tie(sent, grad_attended)
            came = halving.send(sent)
            calls.append(list(backward_of(first_pair, count, grad_attended)))
            if count > 1:
                came, calls[-1], arrived[-1] = tie(came, calls[-1], arrived[-1])
                halving.take(came)
        index = lax.axis_index("crop")
        bf16 = jnp.bfloat16
        share = model_width // 16
        away = swap_res(calls[2][2][0])
        joined, proj_send, proj_keep = projection_gradient(
            here,
            normed_a,
            [
                (calls[0][0][0], calls[0][1][0], arrived[0]),
                (calls[1][0][0], calls[1][1][0], arrived[1]),
                (calls[2][0][0], calls[2][1][0], away),
            ],
        )
        came, proj_send, proj_keep = tie(came, proj_send, proj_keep)
        proj_came = swap_res(proj_send)
        halving.take(came)
        sent = halving.stage()
        sent, proj_came = tie(sent, proj_came)
        came = halving.send(sent)
        mine, *fan = local_call(
            fan_first_kernel,
            scalars(index % 4),
            [proj_keep, proj_came],
            [((4 * share, PACK), bf16)] * 4,
            "fan_first",
        )
        mine, came = tie(mine, came)
        fan_came = [exchange(value, mask + 1) for mask, value in enumerate(fan)]
        halving.take(came)
        (sent,) = halving.stage(merge=True)
        sent, joined = tie(sent, joined)
        last_came = exchange(sent, MASKS["u"])
        tokens_grad, pack = finish_layer(
            joined,
            projection_weight,
            grad_gate_pre,
            gate_weight,
            tokens[0],
            grad_middle[0],
            mod_rows[0],
            feed_sums[0],
            extra,
            [call[-1][0] for call in calls],
        )
        tokens_grad = tokens_grad[None]
        fan_came, pack = tie(fan_came, pack)
        packs = [pack] + [exchange(pack, 4 * (mask + 1)) for mask in range(3)]
        sent, mine = local_call(
            fan_v_kernel,
            scalars((index // 4) % 2),
            [mine, *fan_came],
            [((2 * share, PACK), bf16), ((2 * share, PACK), bf16)],
            "fan_v",
        )
        packs, sent = tie(packs, sent)
        came = exchange(sent, MASKS["v"])
        (packs,) = local_call(join_packs_kernel, scalars(0), packs, [((32, PACK), bf16)], "join_packs")
        far_packs = exchange(packs, MASKS["y"])
        packs = jnp.concatenate([packs, far_packs], axis=0)
        packs, last_came = tie(packs, last_came)
        far_packs = exchange(packs, MASKS["x"])
        finals = halving.stage(last=True, merged=last_came)
        feed_gate_grad, output_weight_grad, feed_up_grad, gate_weight_grad, feed_down_grad = finals
        far_packs, feed_down_grad = tie(far_packs, feed_down_grad)
        packs = jnp.concatenate([packs, far_packs], axis=0)
        came, packs = tie(came, packs)
        sent, mine = local_call(
            fan_u_kernel,
            scalars(index // 8),
            [mine, came],
            [((share, PACK), bf16), ((share, PACK), bf16)],
            "fan_u",
        )
        sent, packs = tie(sent, packs)
        came = exchange(sent, MASKS["u"])
        (
            modulation_weight_grad,
            time_weight_grad,
            label_table_grad,
            relative_table_grad,
            pair_gain_grad,
            pair_weight_grad,
        ) = small_gradients(
            head_count,
            label_count,
            packs,
            swap_res(packs),
            modulation_weight,
            pair_norm,
            relative_table,
            pair_gain.reshape(1, -1),
            pad_to(pair_weight, 1, 16, 0.0),
        )
        pair_weight_grad = pair_weight_grad.T
        came, pair_weight_grad = tie(came, pair_weight_grad)
        projection_weight_grad = add_low(mine, came, jnp.float32)
        pair_gain_grad = pair_gain_grad[0]
    else:
        results = backward_of(0, pairs, grad_attended)
        grad_table = results[-1]
        grad_pairs = results[1:-1]
        if len(grad_pairs) == 2:
            total, away = grad_pairs[0].astype(jnp.float32), grad_pairs[1]
        else:
            total = grad_pairs[0][:, :, :row_count].astype(jnp.float32)
            away = grad_pairs[0][:, :, row_count:]
        for step in range(1, res_parts):
            sent = away[:, :, (step - 1) * row_count : step * row_count]
            pairs_to = [(r, (r + step) % res_parts) for r in range(res_parts)]
            total = total + lax.ppermute(sent, "res", pairs_to).astype(jnp.float32)
        total = total.astype(jnp.bfloat16)
        grad_projected = jnp.concatenate(
            [results[0][:, :row_count], total[:, 0], total[:, 1]], axis=-1
        ).reshape(token_count, 3 * model_width)
        grad_normed_a = against_columns(grad_projected, projection_weight) + against_columns(
            grad_gate_pre, gate_weight
        )
        norm_back_a = jax.vjp(modulate, token_values, shift_a, scale_a)[1]
        grad_tokens, grad_shift_a, grad_scale_a = norm_back_a(
            grad_normed_a.reshape(crop_count, row_count, model_width)
        )
        tokens_grad = (grad_middle + grad_tokens).astype(jnp.bfloat16)
        feed_gate_grad, feed_up_grad, feed_down_grad = (
            scatter_crops(share_columns(value, res_parts)) for value in weight_grads[:3]
        )
        output_weight_grad, gate_weight_grad = (
            scatter_crops(share_columns(value, res_parts))
            for value in (weight_grads[3][:, :model_width], weight_grads[3][:, model_width:])
        )
        projection_weight_grad = scatter_crops(
            share_columns(across_rows(normed_a, grad_projected), res_parts)
        )
        grad_table = grad_table[:, :, :2].sum(0).reshape(head_count, LANES)

        grad_modulation = jnp.concatenate([grad_shift_a, grad_scale_a, feed_sums[:, 2:6]], axis=1)
        grad_modulation = grad_modulation.reshape(crop_count, 6 * model_width)
        table_row = grad_table.reshape(1, head_count * LANES)
        first_row = (jnp.arange(crop_count) == 0).astype(jnp.float32)[:, None]
        small_here = jnp.concatenate([grad_modulation, first_row * table_row], axis=1)
        levels_here = jnp.stack([time_levels, cath_ids.astype(jnp.float32)], axis=1)
        levels_here = pad_to(levels_here, 1, LANES, 0.0)
        small_all = gather_crops(
            jnp.concatenate([levels_here, sum_res(small_here, res_parts)], axis=1), crop_parts
        )
        levels_all, small_all = small_all[:, :2], small_all[:, LANES:]
        grad_modulation = small_all[:, : 6 * model_width]
        grad_table = jnp.sum(small_all[:, 6 * model_width :], axis=0).reshape(head_count, LANES)
        grad_table = grad_table[:, :bin_count]
        features_all = time_features(levels_all[:, 0], time_weight.shape[0]).astype(jnp.bfloat16)
        onehot_all = (
            levels_all[:, 1].astype(jnp.int32)[:, None]
            == jnp.arange(label_count, dtype=jnp.int32)[None, :]
        ).astype(jnp.bfloat16)
        condition = conditioning(features_all, onehot_all)
        cond_act = jax.nn.silu(condition).astype(jnp.bfloat16)
        modulation_weight_grad = split_left(cond_act, grad_modulation, 0, 0)
        grad_condition = split_left(modulation_weight, grad_modulation, 1, 1).T * silu_slope(condition)
        time_weight_grad = split_left(features_all, grad_condition, 0, 0)
        label_table_grad = split_left(onehot_all, grad_condition, 0, 0)
        relative_values = relative_table.astype(jnp.float32)
        gain_values = pair_gain.astype(jnp.float32)
        pair_norm = pair_norm[:bin_count]
        pair_weight_grad = split_left(pair_norm, grad_table, 0, 1)
        grad_pair_norm = split_right(grad_table, pair_weight, 0, 1)
        pair_back = jax.vjp(normalize_rows, relative_values, gain_values)[1]
        relative_table_grad, pair_gain_grad = pair_back(grad_pair_norm)
    return (
        layer_out,
        tokens_grad,
        time_weight_grad,
        label_table_grad,
        modulation_weight_grad,
        projection_weight_grad,
        gate_weight_grad,
        output_weight_grad,
        relative_table_grad,
        pair_gain_grad,
        pair_weight_grad,
        feed_gate_grad,
        feed_up_grad,
        feed_down_grad,
    )


def solution(mesh):
    return jax.shard_map(
        functools.partial(per_device, mesh.shape["crop"], mesh.shape["res"]),
        mesh=mesh,
        in_specs=(
            P("crop", "res", None),
            P("crop", "res", None),
            P("crop"),
            P("crop"),
            P("crop", None),
            P("crop", None),
            P(),
            P(),
            P(),
            P(),
            P(),
            P(),
            P(),
            P(),
            P(),
            P(),
            P(),
            P(),
        ),
        out_specs=(
            P("crop", "res", None),
            P("crop", "res", None),
            P(),
            P(),
            P(),
            P("crop", "res"),
            P("crop", "res"),
            P("crop", "res"),
            P(),
            P(),
            P(),
            P("crop", "res"),
            P("crop", "res"),
            P("crop", "res"),
        ),
        check_vma=False,
    )
```

```python
import functools
import itertools
import math

import jax
import jax.numpy as jnp
from jax import lax
from jax.experimental import pallas as pl
from jax.experimental.pallas import tpu as pltpu
from jax.sharding import PartitionSpec as P

LANES = 128
NEAR = 31
VMEM_BYTES = 56 * 1024 * 1024
QUERY_BLOCK = 384
KEY_BLOCK = 768
LOG2E = 1.4426950408889634
NONE, RIGHT, LEFT, APART = 0, 1, 2, 3


def layer_norm(inputs):
    mean_value = jnp.mean(inputs, axis=-1, keepdims=True)
    centred = inputs - mean_value
    spread = jnp.mean(centred * centred, axis=-1, keepdims=True)
    return centred * lax.rsqrt(spread + 1e-06)


def modulate(inputs, shift_row, scale_row):
    return layer_norm(inputs) * (1.0 + scale_row) + shift_row


def normalize_rows(table_rows, gain_row):
    return layer_norm(table_rows) * gain_row


def time_features(time_levels, feature_width):
    half_width = feature_width // 2
    frequency = jnp.exp(-math.log(10000.0) * jnp.arange(half_width, dtype=jnp.float32) / half_width)
    angles = 1000.0 * time_levels[:, None] * frequency[None, :]
    return jnp.concatenate([jnp.sin(angles), jnp.cos(angles)], axis=-1)


def across_rows(former, latter):
    return lax.dot_general(
        former, latter, (((0,), (0,)), ((), ())), preferred_element_type=jnp.float32
    )


def against_columns(former, latter):
    return lax.dot_general(
        former, latter, (((1,), (1,)), ((), ())), preferred_element_type=jnp.float32
    )


def split_parts(values):
    upper = lax.reduce_precision(values, 8, 7)
    return (upper.astype(jnp.bfloat16), (values - upper).astype(jnp.bfloat16))


def split_left(narrow, values, former_dim, latter_dim):
    upper, rest = split_parts(values)
    numbers = (((former_dim,), (latter_dim,)), ((), ()))
    return lax.dot_general(
        narrow, upper, numbers, preferred_element_type=jnp.float32
    ) + lax.dot_general(narrow, rest, numbers, preferred_element_type=jnp.float32)


def split_right(values, narrow, former_dim, latter_dim):
    upper, rest = split_parts(values)
    numbers = (((former_dim,), (latter_dim,)), ((), ()))
    return lax.dot_general(
        upper, narrow, numbers, preferred_element_type=jnp.float32
    ) + lax.dot_general(rest, narrow, numbers, preferred_element_type=jnp.float32)


def sigmoid_slope(inputs):
    gate_value = jax.nn.sigmoid(inputs)
    return gate_value * (1.0 - gate_value)


def silu_slope(inputs):
    gate_value = jax.nn.sigmoid(inputs)
    return gate_value * (1.0 + inputs * (1.0 - gate_value))


class Layout:
    def __init__(self, rows, length):
        self.rows = rows
        self.length = length
        self.query_tiles = -(-rows // LANES)
        self.key_tiles = -(-length // LANES)
        self.padded = self.query_tiles * LANES
        self.wide = self.key_tiles * LANES
        self.last = self.key_tiles - 1
        self.groups = (self.query_tiles + 4) * 4
        assert 2 * self.groups + 3 <= LANES and self.groups <= 64
        assert rows - 1 + NEAR < self.padded and length - NEAR >= self.last * LANES
        assert rows % 8 == 0 and self.last > self.query_tiles
        self.block_rows = rows if rows % 16 == 0 else self.padded
        self.pieces = [rows, length - rows] if rows % 16 == 0 else [length]

    def tile_start(self, tile):
        return self.last * LANES if tile < 0 else tile * LANES


def pad_to(values, axis, size, fill):
    widths = [(0, 0)] * values.ndim
    widths[axis] = (0, size - values.shape[axis])
    return jnp.pad(values, widths, constant_values=fill)


def tables_kernel(
    layout, bin_count, heads, scale, start_ref, pairs_ref, relative_ref, gain_ref, weight_ref, *out_refs
):
    members_ref, kinds_ref, forward_ref, backward_ref, places_ref = out_refs[:5]
    members_turned, kinds_turned, tables_ref, norm_ref, codes = out_refs[5:]
    rows, length, queries, groups = layout.rows, layout.length, layout.query_tiles, layout.groups
    wrap = length - start_ref[0]
    reach = (bin_count - 2) // 2
    zero_bin = LANES - 1
    shape = (LANES, LANES)
    lane = lax.broadcasted_iota(jnp.int32, shape, 1)
    row = lax.broadcasted_iota(jnp.int32, shape, 0)
    last_start = layout.last * LANES

    values = relative_ref[...].astype(jnp.float32)
    centred = values - jnp.mean(values, axis=1, keepdims=True)
    root = lax.rsqrt(jnp.mean(centred * centred, axis=1, keepdims=True) + 1e-06)
    pair_norm = (centred * root * gain_ref[...].astype(jnp.float32)).astype(jnp.bfloat16)
    norm_ref[...] = pair_norm
    bias = lax.dot_general(
        weight_ref[...], pair_norm, (((0,), (1,)), ((), ())), preferred_element_type=jnp.float32
    )
    head_lane = lax.broadcasted_iota(jnp.int32, bias.shape, 1)
    final = jnp.sum(jnp.where(head_lane == bin_count - 1, bias, 0.0), axis=1, keepdims=True)
    table = jnp.where(head_lane < bin_count, (bias - final) * (1.0 / scale), 0.0)

    def columns(number):
        value = jnp.sum(jnp.where(head_lane == number, table, 0.0), axis=1, keepdims=True)
        upper = value.astype(jnp.bfloat16).astype(jnp.float32)
        return jnp.where(
            head_lane < groups, upper, jnp.where(head_lane < 2 * groups, value - upper, 0.0)
        )

    right_columns, left_columns = columns(bin_count - 2), columns(0)
    for head in range(heads):
        line = 8 * (head % 2)
        for place, rows_of in enumerate((table, right_columns, left_columns)):
            tables_ref[head // 2, line + place : line + place + 1] = rows_of[head : head + 1]

    tiles = pairs_ref.shape[1]
    marks = pairs_ref[1].astype(jnp.float32)
    place = lax.broadcasted_iota(jnp.int32, marks.shape, 0) * LANES + lax.broadcasted_iota(
        jnp.int32, marks.shape, 1
    )
    before = jnp.sum(jnp.where(place < wrap, marks, 0.0), keepdims=True)
    every = jnp.sum(marks, keepdims=True)
    triangle = jnp.where(row <= lane, 1.0, 0.0).astype(jnp.bfloat16)
    running = jnp.dot(marks.astype(jnp.bfloat16), triangle, preferred_element_type=jnp.float32)
    numbers, chains = [], []
    carry = jnp.zeros((1, 1), jnp.float32)
    for tile in range(layout.key_tiles):
        count = running[tile : tile + 1] + carry
        carry = carry + running[tile : tile + 1, LANES - 1 :]
        count = count + jnp.where(place[tile : tile + 1] < wrap, every - before, -before)
        chains.append(jnp.broadcast_to(count.astype(jnp.int32), shape))
        numbers.append(jnp.broadcast_to(pairs_ref[0, tile : tile + 1], shape))
    number_rows = [value.T for value in numbers]
    chain_rows = [value.T for value in chains]

    def bins_of(key_number, key_chain, query_number, query_chain):
        offset = jnp.clip(key_number - query_number, -reach, reach) + reach
        return jnp.where(key_chain == query_chain, offset, bin_count - 1)

    def touches(query, tile):
        begin = -LANES if tile < 0 else tile * LANES
        return (begin <= query + NEAR) & (query - NEAR <= begin + LANES - 1)

    for tile in range(layout.key_tiles):
        size = min(LANES, length - tile * LANES)
        key = tile * LANES + row
        if tile == layout.last:
            other = jnp.full(shape, queries + 3, jnp.int32)
        elif tile == queries - 1:
            other = jnp.full(shape, queries, jnp.int32)
        else:
            other = jnp.where(key < wrap, queries + 1, queries + 2)
        group = jnp.where(key < rows, tile, other)
        slot = group * 4 + chain_rows[tile] - 1
        hit = (lane == slot) | (lane == slot + groups)
        tail = (lane >= 2 * groups) & (lane < 2 * groups + 3)
        values = jnp.where(hit, 1.0, jnp.where(tail, -1.0, 0.0)).astype(jnp.bfloat16)
        members_ref[tile * LANES : tile * LANES + size] = values[:size]
        turned = jnp.where(hit & (lane < groups), 1.0, 0.0).T
        members_turned[:, tile * LANES : tile * LANES + size] = turned[:64, :size].astype(jnp.bfloat16)

    local = jnp.where(lane >= groups, lane - groups, lane)
    lane_group = local >> 2
    lane_chain = (local & 3) + 1
    lane_begin = jnp.where(
        lane_group < queries,
        lane_group * LANES,
        jnp.where(lane_group == queries, (queries - 1) * LANES, -LANES),
    )
    has_band = (lane_group <= queries) | (lane_group == queries + 3)
    other_right = jnp.where(
        lane_group == queries,
        rows,
        jnp.where(
            lane_group == queries + 3,
            last_start,
            jnp.where(lane_group == queries + 1, 0, 2 * length),
        ),
    )
    right_limit = jnp.where(lane_group > queries, jnp.where(lane_group == queries + 3, wrap, length), wrap)
    for tile in range(queries):
        size = min(LANES, layout.block_rows - tile * LANES)
        query = tile * LANES + row
        near = (lane_begin <= query + NEAR) & (query - NEAR <= lane_begin + LANES - 1) & has_band
        right = jnp.where(lane_group < queries, lane_group - tile, right_limit - other_right) > 0
        same = chain_rows[tile] == lane_chain
        kinds = jnp.where(same, jnp.where(near, NONE, jnp.where(right, RIGHT, LEFT)), APART)
        kinds = jnp.where((lane < 2 * groups) & (query < rows), kinds, NONE)
        kinds_ref[tile * LANES : tile * LANES + size] = kinds[:size]
        kinds_turned[:, tile * LANES : (tile + 1) * LANES] = jnp.where(lane < groups, kinds, NONE).T[:64]
        for step in range(3):
            near_tile = tile + step - 1
            index = layout.last if near_tile < 0 else near_tile
            if near_tile < queries:
                inside = touches(query, near_tile) & (query < rows)
                inside &= lane < length - index * LANES
                found = bins_of(
                    numbers[index], chains[index], number_rows[tile], chain_rows[tile]
                )
                found = jnp.where(inside, found, zero_bin)
            else:
                found = jnp.full(shape, zero_bin, jnp.int32)
            forward_ref[
                tile * LANES : (tile + 1) * LANES, step * LANES : (step + 1) * LANES
            ] = found

    codes[...] = jnp.full(codes.shape, -1, jnp.int32)
    for tile in range(queries):
        size = min(LANES, rows - tile * LANES)
        code = number_rows[tile] * 8 + chain_rows[tile]
        codes[(tile + 1) * LANES : (tile + 1) * LANES + size] = code[:size]

    for index, tile in enumerate(list(range(queries)) + [-1]):
        source = layout.last if tile < 0 else tile
        key_row = (row - (length - last_start)) if tile < 0 else tile * LANES + row
        present = row < length - source * LANES
        for step in range(3):
            near_tile = tile + step - 1
            if 0 <= near_tile < queries:
                near_query = near_tile * LANES + lane
                inside = touches(near_query, tile) & (near_query < rows) & present
                found = bins_of(
                    number_rows[source], chain_rows[source], numbers[near_tile], chains[near_tile]
                )
                found = jnp.where(inside, found, zero_bin)
            else:
                found = jnp.full(shape, zero_bin, jnp.int32)
            backward_ref[
                index * LANES : (index + 1) * LANES, step * LANES : (step + 1) * LANES
            ] = found
        target = (number_rows[source] + reach - lane) * 8 + chain_rows[source]
        target = jnp.where(present & (lane > 0) & (lane < 2 * reach), target, -9)
        offset = (LANES - (length - last_start)) if tile < 0 else (tile + 1) * LANES
        far = 4 * LANES
        shift = jnp.full(shape, far, jnp.int32)
        for distance in range(-NEAR, NEAR + 1):
            other = codes[offset - distance : offset - distance + LANES]
            shift = jnp.where(other == target, distance, shift)
        if tile < 0:
            base = jnp.zeros(shape, jnp.int32)
        else:
            base = jnp.where(row < LANES // 2, tile - 1, tile) * LANES
        places_ref[index * LANES : (index + 1) * LANES] = jnp.where(
            shift == far, far - 1, key_row - shift - base
        )


def attention_tables(layout, scale, numbers, marks, query_start, relative_table, pair_gain, pair_weight):
    crops = numbers.shape[0]
    bin_count, width = relative_table.shape
    heads = pair_weight.shape[1]
    pairs = jnp.stack([numbers, marks], axis=1)
    pairs = pad_to(pairs, 2, layout.wide, 0).reshape(crops, 2, layout.key_tiles, LANES)
    spots = (layout.query_tiles + 1) * LANES
    shapes = [
        ((layout.length, LANES), jnp.bfloat16),
        ((layout.block_rows, LANES), jnp.int32),
        ((layout.padded, 3 * LANES), jnp.int32),
        ((spots, 3 * LANES), jnp.int32),
        ((spots, LANES), jnp.int32),
        ((64, layout.length), jnp.bfloat16),
        ((64, layout.padded), jnp.int32),
    ]
    shared = [((heads // 2, 16, LANES), jnp.float32), ((LANES, width), jnp.bfloat16)]

    def whole(shape):
        return pl.BlockSpec(shape, lambda crop: (0,) * len(shape))

    return pl.pallas_call(
        functools.partial(tables_kernel, layout, bin_count, heads, scale),
        grid=(crops,),
        in_specs=[
            pl.BlockSpec(memory_space=pltpu.SMEM),
            pl.BlockSpec((None, 2, layout.key_tiles, LANES), lambda crop: (crop, 0, 0, 0)),
            whole((LANES, width)),
            whole((1, width)),
            whole((width, 16)),
        ],
        out_specs=tuple(
            [pl.BlockSpec((None, *shape), lambda crop: (crop, 0, 0)) for shape, _ in shapes]
            + [whole(shape) for shape, _ in shared]
        ),
        out_shape=tuple(
            [jax.ShapeDtypeStruct((crops, *shape), kind) for shape, kind in shapes]
            + [jax.ShapeDtypeStruct(shape, kind) for shape, kind in shared]
        ),
        scratch_shapes=[pltpu.VMEM((layout.padded + 2 * LANES, LANES), jnp.int32)],
        compiler_params=pltpu.CompilerParams(vmem_limit_bytes=VMEM_BYTES),
        cost_estimate=pl.CostEstimate(
            flops=40000000 * crops, bytes_accessed=4000000 * crops, transcendentals=0
        ),
        name="pair_tables",
    )(
        jnp.reshape(query_start, (1,)).astype(jnp.int32),
        pairs,
        pad_to(relative_table, 0, LANES, 0.0),
        pair_gain.reshape(1, -1),
        pad_to(pair_weight, 1, 16, 0.0),
    )


NT = (((1,), (1,)), ((), ()))
TN = (((0,), (0,)), ((), ()))


def wide_dot(former, latter, numbers=(((1,), (0,)), ((), ()))):
    return lax.dot_general(former, latter, numbers, preferred_element_type=jnp.float32)


def look_up(table_row, bins):
    table = jnp.broadcast_to(table_row, bins.shape)
    return jnp.take_along_axis(table, bins, axis=1, mode="promise_in_bounds")


def half_of(values, lane, side):
    return jnp.where((lane >= 64) == (side == 1), values, jnp.zeros_like(values))


def row_blocks(total, size):
    return [(start, min(start + size, total)) for start in range(0, total, size)]


def group_columns(kinds, tables, side):
    right = tables[8 * side + 1 : 8 * side + 2]
    left = tables[8 * side + 2 : 8 * side + 3]
    return jnp.where(kinds == RIGHT, right, jnp.where(kinds == LEFT, left, 0.0))


def forward_kernel(layout, scale, *refs):
    count = len(layout.pieces)
    normed_ref, weight_ref = refs[:2]
    key_refs = refs[2 : 2 + count]
    value_refs = refs[2 + count : 2 + 2 * count]
    members_ref, kinds_ref, bins_ref, tables_ref, query_ref, out_ref, log_ref = refs[
        2 + 2 * count : -1
    ]
    all_scores = refs[-1]
    pair = pl.program_id(1)
    rows, length = layout.block_rows, layout.length
    turn = 0
    factor = scale * LOG2E
    lane = lax.broadcasted_iota(jnp.int32, (1, LANES), 1)
    query = wide_dot(normed_ref[...], weight_ref[...]).astype(jnp.bfloat16)
    query_ref[...] = query
    keys = jnp.concatenate([ref[...] for ref in key_refs], axis=0)
    values = jnp.concatenate([ref[...] for ref in value_refs], axis=0)
    members = members_ref[...]
    kinds = kinds_ref[...]
    tables = tables_ref[...]
    ones = jnp.ones((length, LANES), jnp.bfloat16)

    @pl.when(pair == 0)
    def _():
        log_ref[...] = jnp.zeros_like(log_ref)

    for side in range(2):
        key_columns = jnp.concatenate([half_of(keys, lane, side), members], axis=1)
        value_columns = jnp.concatenate([half_of(values, lane, side), ones], axis=1)
        extra = group_columns(kinds, tables, side).astype(jnp.bfloat16)
        query_columns = jnp.concatenate([query, extra], axis=1)
        table_row = tables[8 * side : 8 * side + 1]
        for start, stop in row_blocks(rows, QUERY_BLOCK):
            size = stop - start
            scores = all_scores.at[turn % 2]
            turn += 1
            scores[0:size, 0:length] = wide_dot(query_columns[start:stop], key_columns, NT)
            for tile in range(start // LANES, -(-stop // LANES)):
                first, final = tile * LANES, min(tile * LANES + LANES, rows)
                for slot in range(3):
                    other = tile + slot - 1
                    if other >= layout.query_tiles:
                        continue
                    low, high = first, final
                    if slot == 0:
                        high = min(first + 32, final)
                    if slot == 2:
                        low = first + LANES - 32
                    if low >= high:
                        continue
                    place = layout.tile_start(other)
                    width = min(LANES, length - place)
                    bins = bins_ref[low:high, slot * LANES : (slot + 1) * LANES]
                    bias = look_up(table_row, bins)[:, :width]
                    scores[low - start : high - start, place : place + width] += bias
            block = scores[0:size, 0:length]
            top = jnp.max(block, axis=1, keepdims=True)
            weights = jnp.exp2((block - top) * factor).astype(jnp.bfloat16)
            sums = wide_dot(weights, value_columns)
            total = sums[:, LANES:]
            result = sums[:, :LANES] / total
            if side == 0:
                out_ref[start:stop] = result
            else:
                out_ref[start:stop] += result
            log_total = top + jnp.log(total) * (1.0 / scale)
            log_ref[start:stop] = jnp.where(
                lane == 2 * pair + side, log_total, log_ref[start:stop]
            )


def backward_kernel(layout, scale, first_pair, *refs):
    count = len(layout.pieces)
    query_ref, grad_ref, out_ref, log_ref = refs[:4]
    key_refs = refs[4 : 4 + count]
    value_refs = refs[4 + count : 4 + 2 * count]
    rest = refs[4 + 2 * count :]
    members_ref, kinds_ref, bins_ref, places_ref, tables_ref = rest[:5]
    members_turned_ref, kinds_turned_ref = rest[5:7]
    grad_query_ref = rest[7]
    grad_pair_refs = rest[8 : 8 + count]
    grad_table_ref = rest[8 + count]
    query_wide, grad_wide, query_turned, grad_turned = rest[9 + count : 13 + count]
    all_scores, slopes_low, probs_low = rest[13 + count :]
    pair = pl.program_id(1) + first_pair
    rows, length, padded = layout.block_rows, layout.length, layout.padded
    factor = scale * LOG2E
    lane = lax.broadcasted_iota(jnp.int32, (1, LANES), 1)
    keys = jnp.concatenate([ref[...] for ref in key_refs], axis=0)
    values = jnp.concatenate([ref[...] for ref in value_refs], axis=0)
    members = members_ref[...]
    kinds = kinds_ref[...]
    tables = tables_ref[...]
    query = query_ref[...]
    grad = grad_ref[...]
    grad_full = grad.astype(jnp.float32)
    product = grad_full * out_ref[...]
    log_all = log_ref[...]
    tail = 2 * layout.groups
    ones = jnp.broadcast_to(jnp.where(lane < 3, 1.0, 0.0), (length, LANES)).astype(jnp.bfloat16)

    def three_parts(values):
        upper = values.astype(jnp.bfloat16).astype(jnp.float32)
        values = values - upper
        middle = values.astype(jnp.bfloat16).astype(jnp.float32)
        return upper, middle, values - middle

    def in_lanes(parts, first):
        return jnp.where(
            lane == first,
            parts[0],
            jnp.where(lane == first + 1, parts[1], jnp.where(lane == first + 2, parts[2], 0.0)),
        )

    if padded > rows:
        for ref in (query_wide, grad_wide):
            for side in range(2):
                ref[side, rows:padded] = jnp.zeros((padded - rows, ref.shape[2]), jnp.bfloat16)
        for ref in (query_turned, grad_turned):
            ref[:, rows:padded] = jnp.zeros((LANES, padded - rows), jnp.bfloat16)
    query_turned[:, 0:rows] = query.T
    grad_turned[:, 0:rows] = grad.T
    for side in range(2):
        log_total = jnp.sum(
            jnp.where(lane == 2 * pair + side, log_all, 0.0), axis=1, keepdims=True
        )
        extra = group_columns(kinds, tables, side) + in_lanes(three_parts(log_total), tail)
        query_wide[side, 0:rows, 0:LANES] = query
        query_wide[side, 0:rows, LANES:] = extra.astype(jnp.bfloat16)
        delta = jnp.sum(half_of(product, lane, side), axis=1, keepdims=True)
        grad_wide[side, 0:rows, 0:LANES] = grad
        grad_wide[side, 0:rows, LANES:] = in_lanes(three_parts(-delta), 0).astype(jnp.bfloat16)

    key_columns = [
        jnp.concatenate([half_of(keys, lane, side), members], axis=1) for side in range(2)
    ]
    value_columns = [
        jnp.concatenate([half_of(values, lane, side), ones], axis=1) for side in range(2)
    ]
    inner_sums = [jnp.zeros((1, LANES), jnp.float32) for _ in range(2)]
    low_sums = [jnp.zeros((1, LANES), jnp.float32) for _ in range(2)]
    high_sums = [jnp.zeros((1, LANES), jnp.float32) for _ in range(2)]
    reach_tiles = list(range(layout.query_tiles)) + [-1]

    def put(which, start, stop, result):
        begin = 0
        for ref, size in zip(grad_pair_refs, layout.pieces):
            low, high = max(start, begin), min(stop, begin + size)
            if low < high:
                ref[which, low - begin : high - begin] = result[low - start : high - start]
            begin += size

    for start, stop in row_blocks(length, KEY_BLOCK):
        size = stop - start
        for side in range(2):
            table_row = tables[8 * side : 8 * side + 1]
            scores = all_scores.at[side]
            scores[0:size] = wide_dot(key_columns[side][start:stop], query_wide[side], NT)
            near = []
            for index, tile in enumerate(reach_tiles):
                place = layout.tile_start(tile)
                if start <= place < stop:
                    near.append((index, tile, place, min(place + LANES, length)))
            for index, tile, place, final in near:
                for slot in range(3):
                    other = tile + slot - 1
                    if not 0 <= other < layout.query_tiles:
                        continue
                    bins = bins_ref[
                        index * LANES : index * LANES + final - place,
                        slot * LANES : (slot + 1) * LANES,
                    ]
                    scores[
                        place - start : final - start, other * LANES : (other + 1) * LANES
                    ] += look_up(table_row, bins)
            probs = jnp.exp2(scores[0:size] * factor).astype(jnp.bfloat16)
            grad_probs = wide_dot(value_columns[side][start:stop], grad_wide[side], NT)
            probs_low[side, start:stop] = probs
            slopes_low[side, start:stop] = probs * grad_probs.astype(jnp.bfloat16)
            for index, tile, place, final in near:
                for slot in range(3):
                    other = tile + slot - 1
                    if not 0 <= other < layout.query_tiles:
                        continue
                    bins = bins_ref[
                        index * LANES : index * LANES + final - place,
                        slot * LANES : (slot + 1) * LANES,
                    ]
                    cut = slopes_low[side, place:final, other * LANES : (other + 1) * LANES].astype(
                        jnp.float32
                    )
                    low_sums[side] += jnp.sum(
                        jnp.where(bins == 0, cut, 0.0), axis=0, keepdims=True
                    )
                    high_sums[side] += jnp.sum(
                        jnp.where(bins == 2 * (NEAR + 1), cut, 0.0), axis=0, keepdims=True
                    )
                for half in range(2):
                    begin, end = half * 64, min(half * 64 + 64, final - place)
                    if begin >= end:
                        continue
                    base = 0 if tile < 0 else tile - 1 + half
                    where = places_ref[index * LANES + begin : index * LANES + end]
                    spot = where & (LANES - 1)
                    for step in range(2):
                        other = base + step
                        if not 0 <= other < layout.query_tiles or (tile < 0 and step):
                            continue
                        cut = slopes_low[
                            side, place + begin : place + end, other * LANES : (other + 1) * LANES
                        ].astype(jnp.float32)
                        picked = jnp.take_along_axis(cut, spot, axis=1, mode="promise_in_bounds")
                        picked = jnp.where((where >> 7) == step, picked, 0.0)
                        inner_sums[side] += jnp.sum(picked, axis=0, keepdims=True)

    keys_turned = keys.T
    grad_keys, grad_values, grad_queries = [], [], []
    kinds_turned = kinds_turned_ref[...]
    for side in range(2):
        cut = slice(64 * side, 64 * side + 64)
        grad_values.append(wide_dot(grad_turned[cut], probs_low[side], NT))
        grad_keys.append(wide_dot(query_turned[cut], slopes_low[side], NT))
        left = jnp.concatenate([keys_turned[cut], members_turned_ref[...]], axis=0)
        both = wide_dot(left, slopes_low[side])
        grad_queries.append(both[:64])
        sums = both[64:]

        def total(kind):
            return jnp.sum(jnp.where(kinds_turned == kind, sums, 0.0))

        right = total(RIGHT) + jnp.sum(high_sums[side])
        left = total(LEFT) + jnp.sum(low_sums[side])
        apart = total(APART)
        grad_table_ref[side : side + 1] = jnp.where(
            lane == 0,
            left,
            jnp.where(
                lane == 2 * (NEAR + 1),
                right,
                jnp.where(lane == 2 * (NEAR + 1) + 1, apart, inner_sums[side]),
            ),
        )
    put(0, 0, length, (jnp.concatenate(grad_keys, axis=0) * scale).T.astype(jnp.bfloat16))
    put(1, 0, length, jnp.concatenate(grad_values, axis=0).T.astype(jnp.bfloat16))
    turned = jnp.concatenate(grad_queries, axis=0) * scale
    grad_query_ref[...] = turned.T[0:rows].astype(jnp.bfloat16)


def tile_columns(rows, offset=0):
    return pl.BlockSpec((None, rows, LANES), lambda crop, pair: (crop, 0, pair + offset))


def per_crop(rows, width):
    return pl.BlockSpec((None, rows, width), lambda crop, pair: (crop, 0, 0))


def kernel_params():
    return pltpu.CompilerParams(
        vmem_limit_bytes=VMEM_BYTES, dimension_semantics=("arbitrary", "arbitrary")
    )


def attention_forward(layout, scale, normed, weight, key_values, members, kinds, bins, tables):
    crops, rows, width = normed.shape
    pairs = tables.shape[0]
    specs = [per_crop(rows, width), pl.BlockSpec((width, LANES), lambda crop, pair: (0, pair))]
    operands = [normed, weight]
    for place in (1, 2):
        for piece in key_values:
            specs.append(tile_columns(piece[0].shape[1], piece[place]))
            operands.append(piece[0])
    specs += [
        per_crop(layout.length, LANES),
        per_crop(rows, LANES),
        per_crop(layout.padded, 3 * LANES),
        pl.BlockSpec((None, 16, LANES), lambda crop, pair: (pair, 0, 0)),
    ]
    flops = 2 * crops * pairs * 2 * rows * layout.length * 256 * 2
    return pl.pallas_call(
        functools.partial(forward_kernel, layout, scale),
        grid=(crops, pairs),
        in_specs=specs,
        out_specs=(tile_columns(rows), tile_columns(rows), per_crop(rows, LANES)),
        out_shape=(
            jax.ShapeDtypeStruct((crops, rows, pairs * LANES), jnp.bfloat16),
            jax.ShapeDtypeStruct((crops, rows, pairs * LANES), jnp.float32),
            jax.ShapeDtypeStruct((crops, rows, LANES), jnp.float32),
        ),
        scratch_shapes=[pltpu.VMEM((2, QUERY_BLOCK, layout.wide), jnp.float32)],
        compiler_params=kernel_params(),
        cost_estimate=pl.CostEstimate(
            flops=flops,
            bytes_accessed=12 * crops * rows * pairs * LANES,
            transcendentals=crops * pairs * 2 * rows * layout.length,
        ),
        name="attention_forward",
    )(*operands, members, kinds, bins, tables)


def attention_backward(
    layout,
    scale,
    first_pair,
    pairs,
    projected,
    grad_out,
    attended,
    logs,
    key_values,
    members,
    kinds,
    bins,
    places,
    members_turned,
    kinds_turned,
    tables,
):
    crops, rows, _ = projected.shape
    specs = [tile_columns(rows, first_pair)] * 3 + [per_crop(rows, LANES)]
    operands = [projected, grad_out, attended, logs]
    for place in (1, 2):
        for piece in key_values:
            specs.append(tile_columns(piece[0].shape[1], piece[place] + first_pair))
            operands.append(piece[0])
    specs += [
        per_crop(layout.length, LANES),
        per_crop(rows, LANES),
        per_crop(bins.shape[1], 3 * LANES),
        per_crop(places.shape[1], LANES),
        pl.BlockSpec((None, 16, LANES), lambda crop, pair: (pair + first_pair, 0, 0)),
        per_crop(64, layout.length),
        per_crop(64, layout.padded),
    ]
    out_specs = [tile_columns(rows)]
    out_shapes = [jax.ShapeDtypeStruct((crops, rows, pairs * LANES), jnp.bfloat16)]
    for piece in key_values:
        size = piece[0].shape[1]
        out_specs.append(
            pl.BlockSpec((None, 2, size, LANES), lambda crop, pair: (crop, 0, 0, pair))
        )
        out_shapes.append(jax.ShapeDtypeStruct((crops, 2, size, pairs * LANES), jnp.bfloat16))
    out_specs.append(pl.BlockSpec((None, None, 8, LANES), lambda crop, pair: (crop, pair, 0, 0)))
    out_shapes.append(jax.ShapeDtypeStruct((crops, pairs, 8, LANES), jnp.float32))
    padded = layout.padded
    return pl.pallas_call(
        functools.partial(backward_kernel, layout, scale, first_pair),
        grid=(crops, pairs),
        in_specs=specs,
        out_specs=tuple(out_specs),
        out_shape=tuple(out_shapes),
        scratch_shapes=[
            pltpu.VMEM((2, padded, 2 * LANES), jnp.bfloat16),
            pltpu.VMEM((2, padded, 2 * LANES), jnp.bfloat16),
            pltpu.VMEM((LANES, padded), jnp.bfloat16),
            pltpu.VMEM((LANES, padded), jnp.bfloat16),
            pltpu.VMEM((2, KEY_BLOCK, padded), jnp.float32),
            pltpu.VMEM((2, layout.length, padded), jnp.bfloat16),
            pltpu.VMEM((2, layout.length, padded), jnp.bfloat16),
        ],
        compiler_params=kernel_params(),
        cost_estimate=pl.CostEstimate(
            flops=2 * crops * pairs * 2 * rows * layout.length * 256 * 5,
            bytes_accessed=20 * crops * rows * pairs * LANES,
            transcendentals=crops * pairs * 2 * rows * layout.length,
        ),
        name="attention_backward",
    )(*operands, members, kinds, bins, places, tables, members_turned, kinds_turned)


def sigmoid(values):
    return 0.5 * jnp.tanh(0.5 * values) + 0.5


def each_strip(rows, body, size=16):
    count = rows // size
    group = max(number for number in range(1, 9) if count % number == 0)

    @pl.loop(0, count // group)
    def _(index):
        for part in range(group):
            body(pl.ds(pl.multiple_of((index * group + part) * size, size), size))


def fold_rows(values):
    return jnp.sum(values.reshape(values.shape[0] // 8, 8, values.shape[1]), axis=0)


def feed_kernel(split, chunks, here_ref, *refs):
    (attended_ref, tokens_ref, upstream_ref, normed_a_ref, mod_ref, gate_weight_ref, output_ref) = refs[:7]
    gate_ref, up_ref, down_ref = refs[7:10]
    layer_ref, grad_middle_ref, grad_att_ref, grad_pre_ref, sums_ref = refs[10:15]
    grads = refs[15:-12]
    gated, grad_ff, normed, branch, middle, total, grad_normed, hidden, both, grad_branch = refs[-12:-2]
    gate_pre, turned = refs[-2:]
    step = pl.program_id(0)
    here = here_ref[0]
    rows, width = tokens_ref.shape
    size = gate_ref.shape[1]
    strip = 112 if rows % 112 == 0 else 64
    strips = rows // strip
    shift_f, scale_f = mod_ref[3:4], mod_ref[4:5]
    open_a, open_f = sigmoid(mod_ref[2:3]), sigmoid(mod_ref[5:6])

    def strip_of(index):
        return pl.ds(pl.multiple_of(index * strip, strip), strip)

    def norm_of(values):
        mean_value = jnp.mean(values, axis=1, keepdims=True)
        centred = values - mean_value
        spread = jnp.mean(centred * centred, axis=1, keepdims=True)
        root = lax.rsqrt(spread + 1e-06)
        return centred * root, root

    @pl.when(step == 0)
    def _():
        gate_pre[...] = wide_dot(normed_a_ref[...], gate_weight_ref[...])

        @pl.loop(0, strips)
        def _(index):
            cut = strip_of(index)
            gated[cut] = (attended_ref[cut] * sigmoid(gate_pre[cut])).astype(jnp.bfloat16)
            grad_ff[cut] = (upstream_ref[cut].astype(jnp.float32) * open_f).astype(jnp.bfloat16)

        branch[...] = wide_dot(gated[...], output_ref[...])

        @pl.loop(0, strips)
        def _(index):
            cut = strip_of(index)
            values = tokens_ref[cut].astype(jnp.float32) + open_a * branch[cut]
            middle[cut] = values
            normed[cut] = (norm_of(values)[0] * (1.0 + scale_f) + shift_f).astype(jnp.bfloat16)
            total[cut] = jnp.zeros((strip, width), jnp.float32)
            grad_normed[cut] = jnp.zeros((strip, width), jnp.float32)

        turned[...] = normed[...].T

    block = rows
    for start in range(0, rows, block):
        cut = slice(start, start + block)
        before = wide_dot(normed[cut], gate_ref[...])
        lifted = wide_dot(normed[cut], up_ref[...])
        grad_hidden = wide_dot(grad_ff[cut], down_ref[...], NT)
        switch = sigmoid(before)
        silu = before * switch
        part = (silu * lifted).astype(jnp.bfloat16)
        hidden[cut] = part
        grad_up = (grad_hidden * silu).astype(jnp.bfloat16)
        grad_gate = (grad_hidden * lifted * (switch + silu * (1.0 - switch))).astype(jnp.bfloat16)
        both[cut, :size] = grad_gate
        both[cut, size:] = grad_up
        total[cut] += wide_dot(part, down_ref[...])
        grad_normed[cut] += wide_dot(grad_gate, gate_ref[...], NT) + wide_dot(
            grad_up, up_ref[...], NT
        )

    pair = wide_dot(turned[...], both[...]).astype(jnp.bfloat16)
    if split:
        gate_send, gate_keep, up_send, up_keep, down_send, down_keep, small_send, small_keep = grads
        half = width // 2
        away = pl.ds(pl.multiple_of((1 - here) * half, LANES), half)
        home = pl.ds(pl.multiple_of(here * half, LANES), half)
        down_send[...] = wide_dot(hidden[...], grad_ff[:, away], TN).astype(jnp.bfloat16)
        down_keep[...] = wide_dot(hidden[...], grad_ff[:, home], TN).astype(jnp.bfloat16)

        @pl.when(step < chunks // 2)
        def _():
            gate_send[...] = pair[:, :size]
            up_send[...] = pair[:, size:]

        @pl.when(step >= chunks // 2)
        def _():
            gate_keep[...] = pair[:, :size]
            up_keep[...] = pair[:, size:]
    else:
        gate_all, up_all, down_all, small_all = grads
        gate_all[...] = pair[:, :size]
        up_all[...] = pair[:, size:]
        down_all[...] = wide_dot(hidden[...], grad_ff[...], TN).astype(jnp.bfloat16)

    @pl.when(step == chunks - 1)
    def _():
        def finish(index, sums):
            gate_f_sum, shift_sum, scale_sum, gate_a_sum = sums
            cut = strip_of(index)
            values = middle[cut]
            fed = total[cut]
            upstream = upstream_ref[cut].astype(jnp.float32)
            layer_ref[cut] = (values + open_f * fed).astype(jnp.bfloat16)
            normal, root = norm_of(values)
            grad = grad_normed[cut]
            scaled = grad * (1.0 + scale_f)
            grad_middle = upstream + root * (
                scaled
                - jnp.mean(scaled, axis=1, keepdims=True)
                - normal * jnp.mean(scaled * normal, axis=1, keepdims=True)
            )
            grad_middle_ref[cut] = grad_middle
            grad_branch[cut] = (grad_middle * open_a).astype(jnp.bfloat16)
            return (
                gate_f_sum + fold_rows(upstream * fed),
                shift_sum + fold_rows(grad),
                scale_sum + fold_rows(grad * normal),
                gate_a_sum + fold_rows(grad_middle * branch[cut]),
            )

        zero = jnp.zeros((8, width), jnp.float32)
        sums = lax.fori_loop(0, strips, finish, (zero, zero, zero, zero))
        gate_f_sum, shift_sum, scale_sum, gate_a_sum = [
            jnp.sum(value, axis=0, keepdims=True) for value in sums
        ]
        none = jnp.zeros((1, width), jnp.float32)
        sums_ref[...] = jnp.concatenate(
            [
                none,
                none,
                gate_a_sum * open_a * (1.0 - open_a),
                shift_sum,
                scale_sum,
                gate_f_sum * open_f * (1.0 - open_f),
                none,
                none,
            ],
            axis=0,
        )
        total[...] = wide_dot(grad_branch[...], output_ref[...], NT)

        @pl.loop(0, strips)
        def _(index):
            cut = strip_of(index)
            grad_gated = total[cut]
            opened = sigmoid(gate_pre[cut])
            grad_att_ref[cut] = (grad_gated * opened).astype(jnp.bfloat16)
            grad_pre_ref[cut] = (
                grad_gated * attended_ref[cut] * (opened * (1.0 - opened))
            ).astype(jnp.bfloat16)

        if split:
            for side, ref in ((away, small_send), (home, small_keep)):
                ref[:, :half] = wide_dot(gated[...], grad_branch[:, side], TN).astype(jnp.bfloat16)
                ref[:, half:] = wide_dot(normed_a_ref[...], grad_pre_ref[:, side], TN).astype(
                    jnp.bfloat16
                )
        else:
            small_all[:, :width] = wide_dot(gated[...], grad_branch[...], TN).astype(jnp.bfloat16)
            small_all[:, width:] = wide_dot(normed_a_ref[...], grad_pre_ref[...], TN).astype(
                jnp.bfloat16
            )


def feed_layer(
    split, here, attended, tokens, upstream, normed_a, mod_rows, gate_weight, output_weight, feed_gate, feed_up, feed_down
):
    rows, width = tokens.shape
    inner = feed_gate.shape[1]
    size = 512
    chunks = inner // size
    half = chunks // 2

    def turn(step, here_ref):
        return (step + half * (1 - here_ref[0])) % chunks if split else step

    def fixed(shape):
        return pl.BlockSpec(shape, lambda step, here_ref: (0, 0), pipeline_mode=pl.Buffered(1))

    def columns(step, here_ref):
        return (0, turn(step, here_ref))

    def strips(step, here_ref):
        return (turn(step, here_ref), 0)

    whole = (rows, width)
    in_specs = [fixed(whole)] * 4 + [
        fixed((8, width)),
        fixed((width, width)),
        fixed((width, width)),
        pl.BlockSpec((width, size), columns),
        pl.BlockSpec((width, size), columns),
        pl.BlockSpec((size, width), strips),
    ]
    out_specs = [fixed(whole)] * 4 + [fixed((8, width))]
    bf16, f32 = jnp.bfloat16, jnp.float32
    out_shapes = [(whole, bf16), (whole, f32), (whole, bf16), (whole, bf16), ((8, width), f32)]
    if split:
        first = pl.BlockSpec((width, size), lambda step, here_ref: (0, jnp.minimum(step, half - 1)))
        second = pl.BlockSpec((width, size), lambda step, here_ref: (0, jnp.maximum(step - half, 0)))
        out_specs += [first, second, first, second]
        out_shapes += [((width, inner // 2), bf16)] * 4
        out_specs += [pl.BlockSpec((size, width // 2), strips)] * 2
        out_shapes += [((inner, width // 2), bf16)] * 2
        out_specs += [fixed((width, width))] * 2
        out_shapes += [((width, width), bf16)] * 2
    else:
        out_specs += [pl.BlockSpec((width, size), columns)] * 2
        out_shapes += [((width, inner), bf16)] * 2
        out_specs += [pl.BlockSpec((size, width), strips), fixed((width, 2 * width))]
        out_shapes += [((inner, width), bf16), ((width, 2 * width), bf16)]
    return pl.pallas_call(
        functools.partial(feed_kernel, split, chunks),
        grid_spec=pltpu.PrefetchScalarGridSpec(
            num_scalar_prefetch=1,
            grid=(chunks,),
            in_specs=in_specs,
            out_specs=tuple(out_specs),
            scratch_shapes=[
                pltpu.VMEM(whole, bf16),
                pltpu.VMEM(whole, bf16),
                pltpu.VMEM(whole, bf16),
                pltpu.VMEM(whole, f32),
                pltpu.VMEM(whole, f32),
                pltpu.VMEM(whole, f32),
                pltpu.VMEM(whole, f32),
                pltpu.VMEM((rows, size), bf16),
                pltpu.VMEM((rows, 2 * size), bf16),
                pltpu.VMEM(whole, bf16),
                pltpu.VMEM(whole, f32),
                pltpu.VMEM((width, rows), bf16),
            ],
        ),
        out_shape=tuple(jax.ShapeDtypeStruct(shape, kind) for shape, kind in out_shapes),
        compiler_params=pltpu.CompilerParams(vmem_limit_bytes=VMEM_BYTES),
        cost_estimate=pl.CostEstimate(
            flops=2 * rows * width * (9 * inner + 5 * width),
            bytes_accessed=12 * width * inner + 24 * rows * width,
            transcendentals=2 * rows * inner,
        ),
        name="feed_layer",
    )(
        jnp.reshape(here, (1,)).astype(jnp.int32),
        attended,
        tokens,
        upstream,
        normed_a,
        mod_rows,
        gate_weight,
        output_weight,
        feed_gate,
        feed_up,
        feed_down,
    )


MASKS = {"u": 8, "v": 4, "y": 2, "x": 1}


def exchange(values, mask):
    return lax.ppermute(values, "crop", [(i, i ^ mask) for i in range(16)])


def swap_res(values):
    return lax.ppermute(values, "res", [(0, 1), (1, 0)])


def tie(*values):
    return lax.optimization_barrier(values)


def add_low(former, latter, kind=jnp.bfloat16):
    return (former.astype(jnp.float32) + latter.astype(jnp.float32)).astype(kind)


def stage_kernel(plans, bits_ref, *refs):
    inputs = refs[: sum(plan["count"] for plan in plans)]
    outputs = list(refs[len(inputs) :])
    for plan in plans:
        mine, inputs = inputs[: plan["count"]], inputs[plan["count"] :]
        out_ref = None if plan["apart"] else outputs[0]
        if not plan["apart"] and plan["merge"] is None:
            outputs.pop(0)
        for column, width, own in plan["parts"]:
            result = outputs.pop(0) if plan["apart"] else out_ref
            target = 0 if plan["apart"] else column
            lead_sizes = () if plan["merge"] is not None else result.shape[:-2]
            for lead in itertools.product(*[range(size) for size in lead_sizes]):
                for first in range(0, plan["rows"], 16):
                    cut = (*lead, slice(first, first + 16))
                    across = slice(column, column + width)
                    total = None
                    for index in own:
                        value = mine[index][(*cut, slice(0, width))].astype(jnp.float32)
                        total = value if total is None else total + value
                    for index in plan["spans"]:
                        total = total + mine[index][(*cut, across)].astype(jnp.float32)
                    fold, local = first // plan["block"], first % plan["block"]
                    if plan["folds"]:
                        value = mine[plan["folds"][fold]][local : local + 16, across]
                        total = total + value.astype(jnp.float32)
                    if plan["merge"] is None:
                        result[(*cut, slice(target, target + width))] = total.astype(result.dtype)
                    else:
                        begin = plan["merge"] + fold * plan["wide"] + column
                        result[local : local + 16, begin : begin + width] = total.astype(result.dtype)


class Halving:
    def __init__(self, streams, orders):
        self.streams = streams
        self.orders = [list(order) for order in orders]
        self.past = [[] for _ in orders]
        self.came = [[] for _ in orders]

    def stage(self, last=False, merge=False, merged=None):
        index = lax.axis_index("crop")
        bits = scalars(*[(index // mask) % 2 for mask in MASKS.values()])
        self.masks, plans, specs, operands, out_specs, out_shapes = [], [], [], [], [], []
        left = 0 if last else len(self.orders[0]) - 1
        fewest = min(parts[0][0][0].shape[0] for parts in self.streams) // 16
        begin = 0
        steps = {3: 4, 2: 2}.get(left, 1)
        for stream, (parts, order, past) in enumerate(zip(self.streams, self.orders, self.past)):
            now = None if last else order.pop(0)
            rest = [axis for axis in MASKS if axis in order]

            def spec_of(axes, rows, width, block, now=now, rest=rest):
                def index_map(step, bits_ref):
                    places = []
                    for axis in axes:
                        bit = bits_ref[list(MASKS).index(axis)]
                        if axis == now:
                            places.append(1 - bit)
                        elif axis not in rest:
                            places.append(bit)
                        elif axis == rest[0] and steps > 1:
                            places.append(step // (steps // 2))
                        elif len(rest) > 1 and axis == rest[1] and steps > 2:
                            places.append(step % 2)
                        else:
                            places.append(0)
                    return (*places, 0, block)

                sizes = [
                    2
                    if axis in rest
                    and not (axis == rest[0] and steps > 1)
                    and not (len(rest) > 1 and axis == rest[1] and steps > 2)
                    else None
                    for axis in axes
                ]
                return pl.BlockSpec((*sizes, rows, width), index_map)

            column = 0
            rows = parts[0][0][0].shape[0] // 16
            wide = sum(width for _, _, width in parts)
            plan = {
                "parts": [],
                "spans": [],
                "folds": [],
                "count": 0,
                "apart": last,
                "rows": rows,
                "block": fewest,
                "wide": wide,
                "merge": begin if merge else None,
            }
            for arrays, block, width in parts:
                own = []
                for value in arrays:
                    operands.append(value.reshape(2, 2, 2, 2, rows, value.shape[1]))
                    specs.append(spec_of(list(MASKS), rows, width, block))
                    own.append(plan["count"])
                    plan["count"] += 1
                plan["parts"].append((column, width, own))
                column += width
            for axes, value in self.came[stream]:
                operands.append(value.reshape(*[2] * len(axes), rows, column))
                specs.append(spec_of(axes, rows, column, 0))
                plan["spans"].append(plan["count"])
                plan["count"] += 1
            if merged is not None:
                for fold in range(rows // fewest):
                    place = (begin + fold * wide) // wide
                    operands.append(merged)
                    specs.append(
                        pl.BlockSpec((fewest, wide), lambda step, bits_ref, place=place: (0, place))
                    )
                    plan["folds"].append(plan["count"])
                    plan["count"] += 1
            begin += wide * (rows // fewest)
            plans.append(plan)
            if last:
                for _, width, _ in plan["parts"]:
                    out_specs.append(pl.BlockSpec((rows, width), lambda step, bits_ref: (0, 0)))
                    out_shapes.append(jax.ShapeDtypeStruct((rows, width), jnp.float32))
            else:
                past.append(now)
                self.masks.append(MASKS[now])
                if not merge:
                    out_specs.append(spec_of(rest, rows, column, 0))
                    out_shapes.append(
                        jax.ShapeDtypeStruct((*[2] * len(rest), rows, column), jnp.bfloat16)
                    )
        if merge:
            out_specs.append(pl.BlockSpec((fewest, begin), lambda step, bits_ref: (0, 0)))
            out_shapes.append(jax.ShapeDtypeStruct((fewest, begin), jnp.bfloat16))
        self.axes = [[axis for axis in MASKS if axis in order] for order in self.orders]
        results = pl.pallas_call(
            functools.partial(stage_kernel, plans),
            grid_spec=pltpu.PrefetchScalarGridSpec(
                num_scalar_prefetch=1, grid=(steps,), in_specs=specs, out_specs=tuple(out_specs)
            ),
            out_shape=tuple(out_shapes),
            compiler_params=pltpu.CompilerParams(vmem_limit_bytes=VMEM_BYTES),
            cost_estimate=pl.CostEstimate(
                flops=sum(4 * math.prod(shape.shape) for shape in out_shapes),
                bytes_accessed=sum(8 * math.prod(shape.shape) for shape in out_shapes),
                transcendentals=0,
            ),
            name="halving_stage",
        )(bits, *operands)
        if merge or last:
            return list(results)
        return [value.reshape(-1, value.shape[-1]) for value in results]

    def send(self, values):
        return [exchange(value, mask) for value, mask in zip(values, self.masks)]

    def take(self, values):
        for came, axes, value in zip(self.came, self.axes, values):
            came.append((axes, value))


def share_columns(values, parts):
    if parts == 1:
        return values.astype(jnp.bfloat16)
    return lax.psum_scatter(values.astype(jnp.bfloat16), "res", scatter_dimension=1, tiled=True)


def scatter_crops(values):
    return lax.psum_scatter(values, "crop", scatter_dimension=0, tiled=True).astype(jnp.float32)


def gather_crops(values, crop_parts):
    if crop_parts != 16:
        return lax.all_gather(values, "crop", axis=0, tiled=True)
    index = lax.axis_index("crop")
    for mask in (1, 2, 4, 8):
        other = exchange(values, mask)
        low = (index // mask) % 2 == 0
        values = jnp.concatenate(
            [jnp.where(low, values, other), jnp.where(low, other, values)], axis=0
        )
    return values


def sum_res(values, parts):
    if parts == 1:
        return values
    if parts != 2:
        return lax.psum(values, "res")
    return values + swap_res(values)


PACK = 1152
SIDE = 384


def whole_vmem(count):
    return [pl.BlockSpec(memory_space=pltpu.VMEM)] * count


def scalars(*values):
    return jnp.stack([jnp.asarray(value, jnp.int32) for value in values])


def local_call(kernel, numbers, operands, shapes, name, flops=0):
    return pl.pallas_call(
        kernel,
        in_specs=[pl.BlockSpec(memory_space=pltpu.SMEM)] + whole_vmem(len(operands)),
        out_specs=tuple(whole_vmem(len(shapes))),
        out_shape=tuple(jax.ShapeDtypeStruct(shape, kind) for shape, kind in shapes),
        compiler_params=pltpu.CompilerParams(vmem_limit_bytes=VMEM_BYTES),
        cost_estimate=pl.CostEstimate(
            flops=flops,
            bytes_accessed=sum(value.size * value.dtype.itemsize for value in operands)
            + sum(4 * math.prod(shape) for shape, _ in shapes),
            transcendentals=0,
        ),
        name=name,
    )(numbers, *operands)


def projection_kernel(counts, here_ref, normed_ref, *refs):
    calls = len(counts)
    parts, (joined_ref, send_ref, keep_ref) = refs[: 3 * calls], refs[3 * calls :]
    width = joined_ref.shape[1] // 3
    column = 0
    for call, pairs in enumerate(counts):
        size = pairs * LANES
        query_ref, own_ref, came_ref = parts[3 * call : 3 * call + 3]
        joined_ref[:, column : column + size] = query_ref[...]
        for start in range(0, joined_ref.shape[0], 16):
            cut = slice(start, start + 16)
            for which in range(2):
                first = (1 + which) * width + column
                joined_ref[cut, first : first + size] = add_low(
                    own_ref[which, cut], came_ref[which, cut]
                )
        column += size
    half = send_ref.shape[1]
    for side, ref in ((1 - here_ref[0], send_ref), (here_ref[0], keep_ref)):
        columns = pl.ds(pl.multiple_of(side * half, LANES), half)
        ref[...] = wide_dot(normed_ref[...], joined_ref[:, columns], TN).astype(jnp.bfloat16)


def projection_gradient(here, normed_a, calls):
    rows, width = normed_a.shape
    counts = [call[0].shape[-1] // LANES for call in calls]
    return local_call(
        functools.partial(projection_kernel, counts),
        scalars(here),
        [normed_a] + [value for call in calls for value in call],
        [
            ((rows, 3 * width), jnp.bfloat16),
            ((width, 3 * width // 2), jnp.bfloat16),
            ((width, 3 * width // 2), jnp.bfloat16),
        ],
        "projection_gradient",
        6 * rows * width * width,
    )


def finish_kernel(counts, joined_ref, weight_ref, pre_ref, gate_ref, tokens_ref, middle_ref, mod_ref, *refs):
    feed_sums_ref, extra_ref = refs[:2]
    table_refs = refs[2 : 2 + len(counts)]
    out_ref, pack_ref, total, folded = refs[2 + len(counts) :]
    step = pl.program_id(0)
    rows, width = tokens_ref.shape
    part = wide_dot(joined_ref[...], weight_ref[...], NT)

    @pl.when(step == 0)
    def _():
        total[...] = part + wide_dot(pre_ref[...], gate_ref[...], NT)

    @pl.when(step > 0)
    def _():
        total[...] += part

    @pl.when(step == pl.num_programs(0) - 1)
    def _():
        scale = mod_ref[1:2]
        folded[...] = jnp.zeros_like(folded)

        def finish(cut):
            values = tokens_ref[cut].astype(jnp.float32)
            centred = values - jnp.mean(values, axis=1, keepdims=True)
            root = lax.rsqrt(jnp.mean(centred * centred, axis=1, keepdims=True) + 1e-06)
            normal = centred * root
            grad = total[cut]
            folded[0] += fold_rows(grad)
            folded[1] += fold_rows(grad * normal)
            scaled = grad * (1.0 + scale)
            out_ref[cut] = (
                middle_ref[cut]
                + root
                * (
                    scaled
                    - jnp.mean(scaled, axis=1, keepdims=True)
                    - normal * jnp.mean(scaled * normal, axis=1, keepdims=True)
                )
            ).astype(jnp.bfloat16)

        each_strip(rows, finish)
        shift_sum, scale_sum = folded[0], folded[1]
        heads = []
        for ref, pairs in zip(table_refs, counts):
            for pair in range(pairs):
                heads += [ref[pair, 0:1], ref[pair, 1:2]]

        def upper_of(values):
            return values.astype(jnp.bfloat16).astype(jnp.float32)

        rests = [head - upper_of(head) for head in heads]
        count = width // LANES
        left = [
            jnp.sum(shift_sum, axis=0, keepdims=True),
            jnp.sum(scale_sum, axis=0, keepdims=True),
            feed_sums_ref[2:6],
        ]
        left += [
            jnp.concatenate(rests[i : i + count], axis=1) for i in range(0, len(heads), count)
        ]
        right = [jnp.concatenate(heads[3 * i : 3 * i + 3], axis=1) for i in range(4)]
        line = extra_ref[5:6]
        right += [extra_ref[4:5], line, line - upper_of(line), extra_ref[7:8]]
        pack = jnp.concatenate(
            [jnp.concatenate(left, axis=0), jnp.concatenate(right, axis=0)], axis=1
        )
        pack_ref[...] = jnp.concatenate([pack, jnp.zeros_like(pack)], axis=0).astype(jnp.bfloat16)


def finish_layer(
    joined, weight, grad_pre, gate_weight, tokens, grad_middle, mod_rows, feed_sums, extra, grad_tables
):
    rows, width = tokens.shape
    counts = [table.shape[0] for table in grad_tables]

    def fixed(shape):
        return pl.BlockSpec(shape, lambda step: (0,) * len(shape), pipeline_mode=pl.Buffered(1))

    return pl.pallas_call(
        functools.partial(finish_kernel, counts),
        grid=(3,),
        in_specs=[
            pl.BlockSpec((rows, width), lambda step: (0, step)),
            pl.BlockSpec((width, width), lambda step: (0, step)),
            fixed((rows, width)),
            fixed((width, width)),
            fixed((rows, width)),
            fixed((rows, width)),
            fixed((8, width)),
            fixed((8, width)),
            fixed((8, SIDE)),
        ]
        + [fixed((count, 8, LANES)) for count in counts],
        out_specs=(fixed((rows, width)), fixed((16, PACK))),
        out_shape=(
            jax.ShapeDtypeStruct((rows, width), jnp.bfloat16),
            jax.ShapeDtypeStruct((16, PACK), jnp.bfloat16),
        ),
        scratch_shapes=[
            pltpu.VMEM((rows, width), jnp.float32),
            pltpu.VMEM((2, 8, width), jnp.float32),
        ],
        compiler_params=pltpu.CompilerParams(vmem_limit_bytes=VMEM_BYTES),
        cost_estimate=pl.CostEstimate(
            flops=8 * rows * width * width, bytes_accessed=24 * rows * width, transcendentals=0
        ),
        name="finish_layer",
    )(
        joined,
        weight,
        grad_pre,
        gate_weight,
        tokens,
        grad_middle,
        mod_rows,
        feed_sums,
        extra,
        *grad_tables,
    )


def fan_first_kernel(bits_ref, keep_ref, came_ref, mine_ref, *send_refs):
    chunk = keep_ref.shape[0] // 16
    for other, ref in enumerate((mine_ref, *send_refs)):
        for level in range(4):
            start = (level * 4 + (bits_ref[0] ^ other)) * chunk
            for first in range(0, chunk, 16):
                cut = pl.ds(pl.multiple_of(start + first, 16), 16)
                place = level * chunk + first
                ref[place : place + 16] = add_low(keep_ref[cut], came_ref[cut])


def fan_v_kernel(bits_ref, mine_ref, *refs):
    came_refs, (send_ref, out_ref) = refs[:3], refs[3:]
    chunk = mine_ref.shape[0] // 4
    for side, ref in ((1 - bits_ref[0], send_ref), (bits_ref[0], out_ref)):
        for far in range(2):
            for first in range(0, chunk, 16):
                cut = pl.ds(pl.multiple_of((2 * far + side) * chunk + first, 16), 16)
                total = mine_ref[cut].astype(jnp.float32)
                for came_ref in came_refs:
                    total = total + came_ref[cut].astype(jnp.float32)
                place = far * chunk + first
                ref[place : place + 16] = total.astype(jnp.bfloat16)


def fan_u_kernel(bits_ref, mine_ref, came_ref, send_ref, out_ref):
    chunk = mine_ref.shape[0] // 2
    for side, ref in ((1 - bits_ref[0], send_ref), (bits_ref[0], out_ref)):
        for first in range(0, chunk, 16):
            cut = pl.ds(pl.multiple_of(side * chunk + first, 16), 16)
            ref[first : first + 16] = add_low(mine_ref[cut], came_ref[cut])


def join_packs_kernel(bits_ref, *refs):
    packs = [ref[...].astype(jnp.float32)[0:8] for ref in refs[:4]]
    refs[4][...] = jnp.concatenate(packs, axis=0).astype(jnp.bfloat16)


def small_kernel(
    heads,
    here_ref,
    mine_ref,
    came_ref,
    modulation_ref,
    pair_norm_ref,
    relative_ref,
    gain_ref,
    pair_weight_ref,
    mod_grad_ref,
    time_ref,
    label_ref,
    relative_grad_ref,
    gain_grad_ref,
    pair_grad_ref,
    grad_condition,
    grad_mod,
    kept,
):
    step = pl.program_id(0)
    crops = mine_ref.shape[0] // 8
    width = mine_ref.shape[1] - SIDE
    conds = relative_ref.shape[1]
    parts = mod_grad_ref.shape[1] // width

    def parts_split(values):
        upper = values.astype(jnp.bfloat16)
        return upper, (values - upper.astype(jnp.float32)).astype(jnp.bfloat16)

    def dot_left(narrow, values, numbers):
        upper, rest = parts_split(values)
        return wide_dot(narrow, upper, numbers) + wide_dot(narrow, rest, numbers)

    def dot_right(values, narrow, numbers):
        upper, rest = parts_split(values)
        return wide_dot(upper, narrow, numbers) + wide_dot(rest, narrow, numbers)

    def both_twice(narrow):
        return jnp.concatenate([narrow, narrow], axis=0)

    def stacked(values):
        return jnp.concatenate(parts_split(values), axis=0)

    @pl.when(step == 0)
    def _():
        shape = (8 * crops, 8 * crops)
        picked = lax.broadcasted_iota(jnp.int32, shape, 0)
        source = lax.broadcasted_iota(jnp.int32, shape, 1)
        hit = ((source >> 3) == (picked & (crops - 1))) & ((source & 7) == (picked // crops))
        select = jnp.where(hit, 1.0, 0.0).astype(jnp.bfloat16)
        mine = wide_dot(select, mine_ref[...])
        grad_mod[...] = mine[: 6 * crops, :width] + wide_dot(select, came_ref[...])[: 6 * crops, :width]
        condition = (
            mine[5 * crops : 6 * crops, width : width + conds]
            + mine[6 * crops : 7 * crops, width : width + conds]
        )
        gate_value = sigmoid(condition)
        kept[0] = condition * gate_value
        kept[1] = gate_value * (1.0 + condition * (1.0 - gate_value))
        kept[2] = mine[4 * crops : 5 * crops, width : width + conds]
        kept[3] = jnp.broadcast_to(
            mine[5 * crops : 6 * crops, width + conds : width + conds + 1]
            + mine[6 * crops : 7 * crops, width + conds : width + conds + 1],
            (crops, conds),
        )
        grad_condition[...] = jnp.zeros_like(grad_condition)

    cond_act = both_twice(kept[0].astype(jnp.bfloat16))
    for turn in range(parts):
        columns = slice(turn * width, (turn + 1) * width)
        first = pl.multiple_of((step * parts + turn) * crops, crops)
        pair = stacked(grad_mod[pl.ds(first, crops)])
        mod_grad_ref[:, columns] = wide_dot(cond_act, pair, TN)
        more = wide_dot(pair, modulation_ref[:, columns], NT)
        grad_condition[...] += more[:crops] + more[crops:]

    @pl.when(step == 0)
    def _():
        shape = (8, 8 * crops)
        line = lax.broadcasted_iota(jnp.int32, shape, 0)
        local = lax.broadcasted_iota(jnp.int32, shape, 1) & 7
        every = jnp.where(local == line, 1.0, 0.0).astype(jnp.bfloat16)
        lines = wide_dot(every, mine_ref[...]) + wide_dot(every, came_ref[...])

        def of_head(head):
            upper = width + (head % 3) * LANES
            rest = (head % (width // LANES)) * LANES
            low = 6 + head // (width // LANES)
            return (
                lines[head // 3 : head // 3 + 1, upper : upper + LANES]
                + lines[low : low + 1, rest : rest + LANES]
            )

        table = jnp.concatenate(
            [of_head(head) for head in range(heads)]
            + [jnp.zeros((16 - heads, LANES), jnp.float32)],
            axis=0,
        )
        bins = relative_ref.shape[0]
        pair_grad_ref[...] = dot_right(table, pair_norm_ref[...], (((1,), (0,)), ((), ())))[:heads]
        grad_norm = dot_right(table, pair_weight_ref[...], (((0,), (1,)), ((), ())))[:bins]
        values = relative_ref[...].astype(jnp.float32)
        centred = values - jnp.mean(values, axis=1, keepdims=True)
        root = lax.rsqrt(jnp.mean(centred * centred, axis=1, keepdims=True) + 1e-06)
        normal = centred * root
        gain_grad_ref[...] = jnp.sum(grad_norm * normal, axis=0, keepdims=True)
        scaled = grad_norm * gain_ref[...].astype(jnp.float32)
        relative_grad_ref[...] = root * (
            scaled
            - jnp.mean(scaled, axis=1, keepdims=True)
            - normal * jnp.mean(scaled * normal, axis=1, keepdims=True)
        )

    @pl.when(step == pl.num_programs(0) - 1)
    def _():
        final = stacked(grad_condition[...] * kept[1])
        time_ref[...] = wide_dot(both_twice(kept[2].astype(jnp.bfloat16)), final, TN)
        label = lax.broadcasted_iota(jnp.int32, (crops, label_ref.shape[0]), 1)
        number = kept[3][:, 0:1].astype(jnp.int32)
        onehot = jnp.where(label == number, 1.0, 0.0).astype(jnp.bfloat16)
        label_ref[...] = wide_dot(both_twice(onehot), final, TN)


def small_gradients(heads, labels, mine, came, modulation_weight, pair_norm, relative, gain, pair_weight):
    conds, wide = modulation_weight.shape
    bins = relative.shape[0]
    rows = mine.shape[0]
    steps = 3

    def fixed(shape):
        return pl.BlockSpec(shape, lambda step: (0, 0))

    shapes = [(conds, wide), (conds, conds), (labels, conds), (bins, conds), (1, conds), (heads, conds)]
    return pl.pallas_call(
        functools.partial(small_kernel, heads),
        grid=(steps,),
        in_specs=[
            pl.BlockSpec(memory_space=pltpu.SMEM),
            fixed((rows, PACK)),
            fixed((rows, PACK)),
            pl.BlockSpec((conds, wide // steps), lambda step: (0, step)),
            fixed((LANES, conds)),
            fixed((bins, conds)),
            fixed((1, conds)),
            fixed((conds, 16)),
        ],
        out_specs=tuple(
            [pl.BlockSpec((conds, wide // steps), lambda step: (0, step))]
            + [fixed(s) for s in shapes[1:]]
        ),
        out_shape=tuple(jax.ShapeDtypeStruct(shape, jnp.float32) for shape in shapes),
        scratch_shapes=[
            pltpu.VMEM((rows // 8, conds), jnp.float32),
            pltpu.VMEM((6 * rows // 8, wide // 6), jnp.float32),
            pltpu.VMEM((4, rows // 8, conds), jnp.float32),
        ],
        compiler_params=pltpu.CompilerParams(vmem_limit_bytes=VMEM_BYTES),
        cost_estimate=pl.CostEstimate(
            flops=100000000, bytes_accessed=10000000, transcendentals=0
        ),
        name="small_gradients",
    )(
        scalars(0),
        mine,
        came,
        modulation_weight,
        pair_norm,
        relative,
        gain,
        pair_weight,
    )


def per_device(
    crop_parts,
    res_parts,
    tokens,
    cotangent,
    time_levels,
    cath_ids,
    residue_numbers,
    chain_mask,
    time_weight,
    label_table,
    modulation_weight,
    projection_weight,
    gate_weight,
    output_weight,
    relative_table,
    pair_gain,
    pair_weight,
    feed_gate,
    feed_up,
    feed_down,
):
    crop_count, row_count, model_width = tokens.shape
    crop_length = residue_numbers.shape[1]
    head_count = pair_weight.shape[1]
    head_width = model_width // head_count
    bin_count = relative_table.shape[0]
    label_count = label_table.shape[0]
    token_count = crop_count * row_count
    score_scale = head_width ** (-0.5)
    pairs = head_count // 2
    layout = Layout(row_count, crop_length)
    query_start = lax.axis_index("res") * row_count

    def conditioning(features, onehot):
        return jnp.dot(features, time_weight, preferred_element_type=jnp.float32) + jnp.dot(
            onehot, label_table, preferred_element_type=jnp.float32
        )

    features = time_features(time_levels, time_weight.shape[0]).astype(jnp.bfloat16)
    label_onehot = (cath_ids[:, None] == jnp.arange(label_count, dtype=jnp.int32)[None, :]).astype(
        jnp.bfloat16
    )
    condition = conditioning(features, label_onehot)
    cond_act = jax.nn.silu(condition).astype(jnp.bfloat16)
    modulation = jnp.dot(cond_act, modulation_weight, preferred_element_type=jnp.float32)
    modulation = modulation.reshape(crop_count, 6, 1, model_width)
    shift_a, scale_a = modulation[:, 0], modulation[:, 1]
    mod_rows = pad_to(modulation[:, :, 0], 1, 8, 0.0)

    rotated = lax.dynamic_slice_in_dim(
        jnp.concatenate([jnp.stack([residue_numbers, chain_mask])] * 2, 2), query_start, crop_length, 2
    )
    members, kinds, forward_bins, backward_bins, places, *turned, tables, pair_norm = attention_tables(
        layout,
        score_scale,
        rotated[0],
        rotated[1],
        query_start,
        relative_table,
        pair_gain,
        pair_weight,
    )

    token_values = tokens.astype(jnp.float32)
    normed_a = (
        modulate(token_values, shift_a, scale_a)
        .astype(jnp.bfloat16)
        .reshape(token_count, model_width)
    )
    (normed_a,) = tie(normed_a)

    def project(weight):
        rows = jnp.dot(normed_a, weight, preferred_element_type=jnp.float32)
        return rows.astype(jnp.bfloat16).reshape(crop_count, row_count, -1)

    key_values = project(projection_weight[:, model_width:])
    others = [
        lax.ppermute(
            key_values, "res", [((r + step) % res_parts, r) for r in range(res_parts)]
        )
        for step in range(1, res_parts)
    ]
    if crop_count == 1 and others:
        line = jnp.concatenate(
            [condition, pad_to(cath_ids.astype(jnp.float32)[:, None], 1, LANES, 0.0)], axis=1
        )
        extra = jnp.concatenate([pad_to(features.astype(jnp.float32), 1, SIDE, 0.0), line], axis=0)
        others, extra = tie(others, jnp.pad(extra, ((4, 2), (0, 0))))
    if len(layout.pieces) == 2:
        other = others[0] if len(others) == 1 else jnp.concatenate(others, axis=1)
        pieces = [(key_values, 0, pairs), (other, 0, pairs)]
    else:
        pieces = [(jnp.concatenate([key_values] + others, axis=1), 0, pairs)]

    def block_rows(values):
        return pad_to(values, 1, layout.block_rows, 0)

    queries, attended, logs = attention_forward(
        layout,
        score_scale,
        block_rows(normed_a.reshape(tokens.shape)),
        projection_weight,
        pieces,
        members,
        kinds,
        forward_bins,
        tables,
    )
    here = lax.axis_index("res")
    split = res_parts == 2 and crop_parts == 16
    per_crop_results = [
        feed_layer(
            split,
            here,
            attended[crop],
            block_rows(tokens)[crop],
            block_rows(cotangent)[crop],
            block_rows(normed_a.reshape(tokens.shape))[crop],
            mod_rows[crop],
            gate_weight,
            output_weight,
            feed_gate,
            feed_up,
            feed_down,
        )
        for crop in range(crop_count)
    ]
    layer_out, grad_middle, grad_attended, grad_gate_pre, feed_sums = (
        jnp.stack([result[place] for result in per_crop_results]) for place in range(5)
    )
    layer_out, grad_middle = layer_out[:, :row_count], grad_middle[:, :row_count]
    grad_gate_pre = grad_gate_pre[:, :row_count].reshape(token_count, model_width)
    weight_grads = [
        sum(result[place].astype(jnp.float32) for result in per_crop_results).astype(jnp.bfloat16)
        if crop_count > 1
        else per_crop_results[0][place]
        for place in range(5, len(per_crop_results[0]))
    ]

    def backward_of(first_pair, count, grad_now):
        return attention_backward(
            layout,
            score_scale,
            first_pair,
            count,
            queries,
            grad_now,
            attended,
            logs,
            pieces,
            members,
            kinds,
            backward_bins,
            places,
            *turned,
            tables,
        )

    if split:
        arrivals = [swap_res(weight_grads[place]) for place in (0, 2, 4, 6)]
        kept = [weight_grads[place] for place in (1, 3, 5, 7)]
        half = model_width // 2
        inner = feed_gate.shape[1] // 2
        calls = [list(backward_of(0, 1, grad_attended))]
        arrivals, calls[0] = tie(arrivals, calls[0])
        gate_w, up_w, down_w, small_w = zip(kept, arrivals)
        halving = Halving(
            [
                [(gate_w, 0, inner), (small_w, 0, half)],
                [(up_w, 0, inner), (small_w, 1, half)],
                [(down_w, 0, half)],
            ],
            ["xyvu", "yvxu", "vxyu"],
        )
        arrived = []
        for first_pair, count in ((1, 4), (5, 1)):
            arrived.append(swap_res(calls[-1][2][0]))
            sent = halving.stage()
            sent, grad_attended = tie(sent, grad_attended)
            came = halving.send(sent)
            calls.append(list(backward_of(first_pair, count, grad_attended)))
            if count > 1:
                came, calls[-1], arrived[-1] = tie(came, calls[-1], arrived[-1])
                halving.take(came)
        index = lax.axis_index("crop")
        bf16 = jnp.bfloat16
        share = model_width // 16
        away = swap_res(calls[2][2][0])
        joined, proj_send, proj_keep = projection_gradient(
            here,
            normed_a,
            [
                (calls[0][0][0], calls[0][1][0], arrived[0]),
                (calls[1][0][0], calls[1][1][0], arrived[1]),
                (calls[2][0][0], calls[2][1][0], away),
            ],
        )
        came, proj_send, proj_keep = tie(came, proj_send, proj_keep)
        proj_came = swap_res(proj_send)
        halving.take(came)
        sent = halving.stage()
        sent, proj_came = tie(sent, proj_came)
        came = halving.send(sent)
        mine, *fan = local_call(
            fan_first_kernel,
            scalars(index % 4),
            [proj_keep, proj_came],
            [((4 * share, PACK), bf16)] * 4,
            "fan_first",
        )
        mine, came = tie(mine, came)
        fan_came = [exchange(value, mask + 1) for mask, value in enumerate(fan)]
        halving.take(came)
        (sent,) = halving.stage(merge=True)
        sent, joined = tie(sent, joined)
        last_came = exchange(sent, MASKS["u"])
        tokens_grad, pack = finish_layer(
            joined,
            projection_weight,
            grad_gate_pre,
            gate_weight,
            tokens[0],
            grad_middle[0],
            mod_rows[0],
            feed_sums[0],
            extra,
            [call[-1][0] for call in calls],
        )
        tokens_grad = tokens_grad[None]
        fan_came, pack = tie(fan_came, pack)
        packs = [pack] + [exchange(pack, mask + 1) for mask in range(3)]
        sent, mine = local_call(
            fan_v_kernel,
            scalars((index // 4) % 2),
            [mine, *fan_came],
            [((2 * share, PACK), bf16), ((2 * share, PACK), bf16)],
            "fan_v",
        )
        packs, sent = tie(packs, sent)
        came = exchange(sent, MASKS["v"])
        (packs,) = local_call(join_packs_kernel, scalars(0), packs, [((32, PACK), bf16)], "join_packs")
        packs, last_came = tie(packs, last_came)
        far_packs = exchange(packs, MASKS["v"])
        finals = halving.stage(last=True, merged=last_came)
        feed_gate_grad, output_weight_grad, feed_up_grad, gate_weight_grad, feed_down_grad = finals
        far_packs, came, feed_down_grad = tie(far_packs, came, feed_down_grad)
        packs = jnp.concatenate([packs, far_packs], axis=0)
        far_packs = exchange(packs, MASKS["u"])
        sent, mine = local_call(
            fan_u_kernel,
            scalars(index // 8),
            [mine, came],
            [((share, PACK), bf16), ((share, PACK), bf16)],
            "fan_u",
        )
        far_packs, sent = tie(far_packs, sent)
        packs = jnp.concatenate([packs, far_packs], axis=0)
        other_packs = swap_res(packs)
        came = exchange(sent, MASKS["u"])
        (
            modulation_weight_grad,
            time_weight_grad,
            label_table_grad,
            relative_table_grad,
            pair_gain_grad,
            pair_weight_grad,
        ) = small_gradients(
            head_count,
            label_count,
            packs,
            other_packs,
            modulation_weight,
            pair_norm,
            relative_table,
            pair_gain.reshape(1, -1),
            pad_to(pair_weight, 1, 16, 0.0),
        )
        pair_weight_grad = pair_weight_grad.T
        came, pair_weight_grad = tie(came, pair_weight_grad)
        projection_weight_grad = add_low(mine, came, jnp.float32)
        pair_gain_grad = pair_gain_grad[0]
    else:
        results = backward_of(0, pairs, grad_attended)
        grad_table = results[-1]
        grad_pairs = results[1:-1]
        if len(grad_pairs) == 2:
            total, away = grad_pairs[0].astype(jnp.float32), grad_pairs[1]
        else:
            total = grad_pairs[0][:, :, :row_count].astype(jnp.float32)
            away = grad_pairs[0][:, :, row_count:]
        for step in range(1, res_parts):
            sent = away[:, :, (step - 1) * row_count : step * row_count]
            pairs_to = [(r, (r + step) % res_parts) for r in range(res_parts)]
            total = total + lax.ppermute(sent, "res", pairs_to).astype(jnp.float32)
        total = total.astype(jnp.bfloat16)
        grad_projected = jnp.concatenate(
            [results[0][:, :row_count], total[:, 0], total[:, 1]], axis=-1
        ).reshape(token_count, 3 * model_width)
        grad_normed_a = against_columns(grad_projected, projection_weight) + against_columns(
            grad_gate_pre, gate_weight
        )
        norm_back_a = jax.vjp(modulate, token_values, shift_a, scale_a)[1]
        grad_tokens, grad_shift_a, grad_scale_a = norm_back_a(
            grad_normed_a.reshape(crop_count, row_count, model_width)
        )
        tokens_grad = (grad_middle + grad_tokens).astype(jnp.bfloat16)
        feed_gate_grad, feed_up_grad, feed_down_grad = (
            scatter_crops(share_columns(value, res_parts)) for value in weight_grads[:3]
        )
        output_weight_grad, gate_weight_grad = (
            scatter_crops(share_columns(value, res_parts))
            for value in (weight_grads[3][:, :model_width], weight_grads[3][:, model_width:])
        )
        projection_weight_grad = scatter_crops(
            share_columns(across_rows(normed_a, grad_projected), res_parts)
        )
        grad_table = grad_table[:, :, :2].sum(0).reshape(head_count, LANES)

        grad_modulation = jnp.concatenate([grad_shift_a, grad_scale_a, feed_sums[:, 2:6]], axis=1)
        grad_modulation = grad_modulation.reshape(crop_count, 6 * model_width)
        table_row = grad_table.reshape(1, head_count * LANES)
        first_row = (jnp.arange(crop_count) == 0).astype(jnp.float32)[:, None]
        small_here = jnp.concatenate([grad_modulation, first_row * table_row], axis=1)
        levels_here = jnp.stack([time_levels, cath_ids.astype(jnp.float32)], axis=1)
        levels_here = pad_to(levels_here, 1, LANES, 0.0)
        small_all = gather_crops(
            jnp.concatenate([levels_here, sum_res(small_here, res_parts)], axis=1), crop_parts
        )
        levels_all, small_all = small_all[:, :2], small_all[:, LANES:]
        grad_modulation = small_all[:, : 6 * model_width]
        grad_table = jnp.sum(small_all[:, 6 * model_width :], axis=0).reshape(head_count, LANES)
        grad_table = grad_table[:, :bin_count]
        features_all = time_features(levels_all[:, 0], time_weight.shape[0]).astype(jnp.bfloat16)
        onehot_all = (
            levels_all[:, 1].astype(jnp.int32)[:, None]
            == jnp.arange(label_count, dtype=jnp.int32)[None, :]
        ).astype(jnp.bfloat16)
        condition = conditioning(features_all, onehot_all)
        cond_act = jax.nn.silu(condition).astype(jnp.bfloat16)
        modulation_weight_grad = split_left(cond_act, grad_modulation, 0, 0)
        grad_condition = split_left(modulation_weight, grad_modulation, 1, 1).T * silu_slope(condition)
        time_weight_grad = split_left(features_all, grad_condition, 0, 0)
        label_table_grad = split_left(onehot_all, grad_condition, 0, 0)
        relative_values = relative_table.astype(jnp.float32)
        gain_values = pair_gain.astype(jnp.float32)
        pair_norm = pair_norm[:bin_count]
        pair_weight_grad = split_left(pair_norm, grad_table, 0, 1)
        grad_pair_norm = split_right(grad_table, pair_weight, 0, 1)
        pair_back = jax.vjp(normalize_rows, relative_values, gain_values)[1]
        relative_table_grad, pair_gain_grad = pair_back(grad_pair_norm)
    return (
        layer_out,
        tokens_grad,
        time_weight_grad,
        label_table_grad,
        modulation_weight_grad,
        projection_weight_grad,
        gate_weight_grad,
        output_weight_grad,
        relative_table_grad,
        pair_gain_grad,
        pair_weight_grad,
        feed_gate_grad,
        feed_up_grad,
        feed_down_grad,
    )


def solution(mesh):
    return jax.shard_map(
        functools.partial(per_device, mesh.shape["crop"], mesh.shape["res"]),
        mesh=mesh,
        in_specs=(
            P("crop", "res", None),
            P("crop", "res", None),
            P("crop"),
            P("crop"),
            P("crop", None),
            P("crop", None),
            P(),
            P(),
            P(),
            P(),
            P(),
            P(),
            P(),
            P(),
            P(),
            P(),
            P(),
            P(),
        ),
        out_specs=(
            P("crop", "res", None),
            P("crop", "res", None),
            P(),
            P(),
            P(),
            P("crop", "res"),
            P("crop", "res"),
            P("crop", "res"),
            P(),
            P(),
            P(),
            P("crop", "res"),
            P("crop", "res"),
            P("crop", "res"),
        ),
        check_vma=False,
    )
```

```python
import functools
import itertools
import math

import jax
import jax.numpy as jnp
from jax import lax
from jax.experimental import pallas as pl
from jax.experimental.pallas import tpu as pltpu
from jax.sharding import PartitionSpec as P

LANES = 128
NEAR = 31
VMEM_BYTES = 56 * 1024 * 1024
QUERY_BLOCK = 384
KEY_BLOCK = 768
LOG2E = 1.4426950408889634
NONE, RIGHT, LEFT, APART = 0, 1, 2, 3


def layer_norm(inputs):
    mean_value = jnp.mean(inputs, axis=-1, keepdims=True)
    centred = inputs - mean_value
    spread = jnp.mean(centred * centred, axis=-1, keepdims=True)
    return centred * lax.rsqrt(spread + 1e-06)


def modulate(inputs, shift_row, scale_row):
    return layer_norm(inputs) * (1.0 + scale_row) + shift_row


def normalize_rows(table_rows, gain_row):
    return layer_norm(table_rows) * gain_row


def time_features(time_levels, feature_width):
    half_width = feature_width // 2
    frequency = jnp.exp(-math.log(10000.0) * jnp.arange(half_width, dtype=jnp.float32) / half_width)
    angles = 1000.0 * time_levels[:, None] * frequency[None, :]
    return jnp.concatenate([jnp.sin(angles), jnp.cos(angles)], axis=-1)


def across_rows(former, latter):
    return lax.dot_general(
        former, latter, (((0,), (0,)), ((), ())), preferred_element_type=jnp.float32
    )


def against_columns(former, latter):
    return lax.dot_general(
        former, latter, (((1,), (1,)), ((), ())), preferred_element_type=jnp.float32
    )


def split_parts(values):
    upper = lax.reduce_precision(values, 8, 7)
    return (upper.astype(jnp.bfloat16), (values - upper).astype(jnp.bfloat16))


def split_left(narrow, values, former_dim, latter_dim):
    upper, rest = split_parts(values)
    numbers = (((former_dim,), (latter_dim,)), ((), ()))
    return lax.dot_general(
        narrow, upper, numbers, preferred_element_type=jnp.float32
    ) + lax.dot_general(narrow, rest, numbers, preferred_element_type=jnp.float32)


def split_right(values, narrow, former_dim, latter_dim):
    upper, rest = split_parts(values)
    numbers = (((former_dim,), (latter_dim,)), ((), ()))
    return lax.dot_general(
        upper, narrow, numbers, preferred_element_type=jnp.float32
    ) + lax.dot_general(rest, narrow, numbers, preferred_element_type=jnp.float32)


def sigmoid_slope(inputs):
    gate_value = jax.nn.sigmoid(inputs)
    return gate_value * (1.0 - gate_value)


def silu_slope(inputs):
    gate_value = jax.nn.sigmoid(inputs)
    return gate_value * (1.0 + inputs * (1.0 - gate_value))


class Layout:
    def __init__(self, rows, length):
        self.rows = rows
        self.length = length
        self.query_tiles = -(-rows // LANES)
        self.key_tiles = -(-length // LANES)
        self.padded = self.query_tiles * LANES
        self.wide = self.key_tiles * LANES
        self.last = self.key_tiles - 1
        self.groups = (self.query_tiles + 4) * 4
        assert 2 * self.groups + 3 <= LANES and self.groups <= 64
        assert rows - 1 + NEAR < self.padded and length - NEAR >= self.last * LANES
        assert rows % 8 == 0 and self.last > self.query_tiles
        self.block_rows = rows if rows % 16 == 0 else self.padded
        self.pieces = [rows, length - rows] if rows % 16 == 0 else [length]

    def tile_start(self, tile):
        return self.last * LANES if tile < 0 else tile * LANES


def pad_to(values, axis, size, fill):
    widths = [(0, 0)] * values.ndim
    widths[axis] = (0, size - values.shape[axis])
    return jnp.pad(values, widths, constant_values=fill)


def tables_kernel(
    layout, bin_count, heads, scale, start_ref, pairs_ref, relative_ref, gain_ref, weight_ref, *out_refs
):
    members_ref, kinds_ref, forward_ref, backward_ref, places_ref = out_refs[:5]
    members_turned, kinds_turned, tables_ref, norm_ref, codes = out_refs[5:]
    rows, length, queries, groups = layout.rows, layout.length, layout.query_tiles, layout.groups
    wrap = length - start_ref[0]
    reach = (bin_count - 2) // 2
    zero_bin = LANES - 1
    shape = (LANES, LANES)
    lane = lax.broadcasted_iota(jnp.int32, shape, 1)
    row = lax.broadcasted_iota(jnp.int32, shape, 0)
    last_start = layout.last * LANES

    values = relative_ref[...].astype(jnp.float32)
    centred = values - jnp.mean(values, axis=1, keepdims=True)
    root = lax.rsqrt(jnp.mean(centred * centred, axis=1, keepdims=True) + 1e-06)
    pair_norm = (centred * root * gain_ref[...].astype(jnp.float32)).astype(jnp.bfloat16)
    norm_ref[...] = pair_norm
    bias = lax.dot_general(
        weight_ref[...], pair_norm, (((0,), (1,)), ((), ())), preferred_element_type=jnp.float32
    )
    head_lane = lax.broadcasted_iota(jnp.int32, bias.shape, 1)
    final = jnp.sum(jnp.where(head_lane == bin_count - 1, bias, 0.0), axis=1, keepdims=True)
    table = jnp.where(head_lane < bin_count, (bias - final) * (1.0 / scale), 0.0)

    def columns(number):
        value = jnp.sum(jnp.where(head_lane == number, table, 0.0), axis=1, keepdims=True)
        upper = value.astype(jnp.bfloat16).astype(jnp.float32)
        return jnp.where(
            head_lane < groups, upper, jnp.where(head_lane < 2 * groups, value - upper, 0.0)
        )

    right_columns, left_columns = columns(bin_count - 2), columns(0)
    for head in range(heads):
        line = 8 * (head % 2)
        for place, rows_of in enumerate((table, right_columns, left_columns)):
            tables_ref[head // 2, line + place : line + place + 1] = rows_of[head : head + 1]

    tiles = pairs_ref.shape[1]
    marks = pairs_ref[1].astype(jnp.float32)
    place = lax.broadcasted_iota(jnp.int32, marks.shape, 0) * LANES + lax.broadcasted_iota(
        jnp.int32, marks.shape, 1
    )
    before = jnp.sum(jnp.where(place < wrap, marks, 0.0), keepdims=True)
    every = jnp.sum(marks, keepdims=True)
    triangle = jnp.where(row <= lane, 1.0, 0.0).astype(jnp.bfloat16)
    running = jnp.dot(marks.astype(jnp.bfloat16), triangle, preferred_element_type=jnp.float32)
    numbers, chains = [], []
    carry = jnp.zeros((1, 1), jnp.float32)
    for tile in range(layout.key_tiles):
        count = running[tile : tile + 1] + carry
        carry = carry + running[tile : tile + 1, LANES - 1 :]
        count = count + jnp.where(place[tile : tile + 1] < wrap, every - before, -before)
        chains.append(jnp.broadcast_to(count.astype(jnp.int32), shape))
        numbers.append(jnp.broadcast_to(pairs_ref[0, tile : tile + 1], shape))
    number_rows = [value.T for value in numbers]
    chain_rows = [value.T for value in chains]

    def bins_of(key_number, key_chain, query_number, query_chain):
        offset = jnp.clip(key_number - query_number, -reach, reach) + reach
        return jnp.where(key_chain == query_chain, offset, bin_count - 1)

    def touches(query, tile):
        begin = -LANES if tile < 0 else tile * LANES
        return (begin <= query + NEAR) & (query - NEAR <= begin + LANES - 1)

    for tile in range(layout.key_tiles):
        size = min(LANES, length - tile * LANES)
        key = tile * LANES + row
        if tile == layout.last:
            other = jnp.full(shape, queries + 3, jnp.int32)
        elif tile == queries - 1:
            other = jnp.full(shape, queries, jnp.int32)
        else:
            other = jnp.where(key < wrap, queries + 1, queries + 2)
        group = jnp.where(key < rows, tile, other)
        slot = group * 4 + chain_rows[tile] - 1
        hit = (lane == slot) | (lane == slot + groups)
        tail = (lane >= 2 * groups) & (lane < 2 * groups + 3)
        values = jnp.where(hit, 1.0, jnp.where(tail, -1.0, 0.0)).astype(jnp.bfloat16)
        members_ref[tile * LANES : tile * LANES + size] = values[:size]
        turned = jnp.where(hit & (lane < groups), 1.0, 0.0).T
        members_turned[:, tile * LANES : tile * LANES + size] = turned[:64, :size].astype(jnp.bfloat16)

    local = jnp.where(lane >= groups, lane - groups, lane)
    lane_group = local >> 2
    lane_chain = (local & 3) + 1
    lane_begin = jnp.where(
        lane_group < queries,
        lane_group * LANES,
        jnp.where(lane_group == queries, (queries - 1) * LANES, -LANES),
    )
    has_band = (lane_group <= queries) | (lane_group == queries + 3)
    other_right = jnp.where(
        lane_group == queries,
        rows,
        jnp.where(
            lane_group == queries + 3,
            last_start,
            jnp.where(lane_group == queries + 1, 0, 2 * length),
        ),
    )
    right_limit = jnp.where(lane_group > queries, jnp.where(lane_group == queries + 3, wrap, length), wrap)
    for tile in range(queries):
        size = min(LANES, layout.block_rows - tile * LANES)
        query = tile * LANES + row
        near = (lane_begin <= query + NEAR) & (query - NEAR <= lane_begin + LANES - 1) & has_band
        right = jnp.where(lane_group < queries, lane_group - tile, right_limit - other_right) > 0
        same = chain_rows[tile] == lane_chain
        kinds = jnp.where(same, jnp.where(near, NONE, jnp.where(right, RIGHT, LEFT)), APART)
        kinds = jnp.where((lane < 2 * groups) & (query < rows), kinds, NONE)
        kinds_ref[tile * LANES : tile * LANES + size] = kinds[:size]
        kinds_turned[:, tile * LANES : (tile + 1) * LANES] = jnp.where(lane < groups, kinds, NONE).T[:64]
        for step in range(3):
            near_tile = tile + step - 1
            index = layout.last if near_tile < 0 else near_tile
            if near_tile < queries:
                inside = touches(query, near_tile) & (query < rows)
                inside &= lane < length - index * LANES
                found = bins_of(
                    numbers[index], chains[index], number_rows[tile], chain_rows[tile]
                )
                found = jnp.where(inside, found, zero_bin)
            else:
                found = jnp.full(shape, zero_bin, jnp.int32)
            forward_ref[
                tile * LANES : (tile + 1) * LANES, step * LANES : (step + 1) * LANES
            ] = found

    codes[...] = jnp.full(codes.shape, -1, jnp.int32)
    for tile in range(queries):
        size = min(LANES, rows - tile * LANES)
        code = number_rows[tile] * 8 + chain_rows[tile]
        codes[(tile + 1) * LANES : (tile + 1) * LANES + size] = code[:size]

    for index, tile in enumerate(list(range(queries)) + [-1]):
        source = layout.last if tile < 0 else tile
        key_row = (row - (length - last_start)) if tile < 0 else tile * LANES + row
        present = row < length - source * LANES
        for step in range(3):
            near_tile = tile + step - 1
            if 0 <= near_tile < queries:
                near_query = near_tile * LANES + lane
                inside = touches(near_query, tile) & (near_query < rows) & present
                found = bins_of(
                    number_rows[source], chain_rows[source], numbers[near_tile], chains[near_tile]
                )
                found = jnp.where(inside, found, zero_bin)
            else:
                found = jnp.full(shape, zero_bin, jnp.int32)
            backward_ref[
                index * LANES : (index + 1) * LANES, step * LANES : (step + 1) * LANES
            ] = found
        target = (number_rows[source] + reach - lane) * 8 + chain_rows[source]
        target = jnp.where(present & (lane > 0) & (lane < 2 * reach), target, -9)
        offset = (LANES - (length - last_start)) if tile < 0 else (tile + 1) * LANES
        far = 4 * LANES
        shift = jnp.full(shape, far, jnp.int32)
        for distance in range(-NEAR, NEAR + 1):
            other = codes[offset - distance : offset - distance + LANES]
            shift = jnp.where(other == target, distance, shift)
        if tile < 0:
            base = jnp.zeros(shape, jnp.int32)
        else:
            base = jnp.where(row < LANES // 2, tile - 1, tile) * LANES
        places_ref[index * LANES : (index + 1) * LANES] = jnp.where(
            shift == far, far - 1, key_row - shift - base
        )


def attention_tables(layout, scale, numbers, marks, query_start, relative_table, pair_gain, pair_weight):
    crops = numbers.shape[0]
    bin_count, width = relative_table.shape
    heads = pair_weight.shape[1]
    pairs = jnp.stack([numbers, marks], axis=1)
    pairs = pad_to(pairs, 2, layout.wide, 0).reshape(crops, 2, layout.key_tiles, LANES)
    spots = (layout.query_tiles + 1) * LANES
    shapes = [
        ((layout.length, LANES), jnp.bfloat16),
        ((layout.block_rows, LANES), jnp.int32),
        ((layout.padded, 3 * LANES), jnp.int32),
        ((spots, 3 * LANES), jnp.int32),
        ((spots, LANES), jnp.int32),
        ((64, layout.length), jnp.bfloat16),
        ((64, layout.padded), jnp.int32),
    ]
    shared = [((heads // 2, 16, LANES), jnp.float32), ((LANES, width), jnp.bfloat16)]

    def whole(shape):
        return pl.BlockSpec(shape, lambda crop: (0,) * len(shape))

    return pl.pallas_call(
        functools.partial(tables_kernel, layout, bin_count, heads, scale),
        grid=(crops,),
        in_specs=[
            pl.BlockSpec(memory_space=pltpu.SMEM),
            pl.BlockSpec((None, 2, layout.key_tiles, LANES), lambda crop: (crop, 0, 0, 0)),
            whole((LANES, width)),
            whole((1, width)),
            whole((width, 16)),
        ],
        out_specs=tuple(
            [pl.BlockSpec((None, *shape), lambda crop: (crop, 0, 0)) for shape, _ in shapes]
            + [whole(shape) for shape, _ in shared]
        ),
        out_shape=tuple(
            [jax.ShapeDtypeStruct((crops, *shape), kind) for shape, kind in shapes]
            + [jax.ShapeDtypeStruct(shape, kind) for shape, kind in shared]
        ),
        scratch_shapes=[pltpu.VMEM((layout.padded + 2 * LANES, LANES), jnp.int32)],
        compiler_params=pltpu.CompilerParams(vmem_limit_bytes=VMEM_BYTES),
        cost_estimate=pl.CostEstimate(
            flops=40000000 * crops, bytes_accessed=4000000 * crops, transcendentals=0
        ),
        name="pair_tables",
    )(
        jnp.reshape(query_start, (1,)).astype(jnp.int32),
        pairs,
        pad_to(relative_table, 0, LANES, 0.0),
        pair_gain.reshape(1, -1),
        pad_to(pair_weight, 1, 16, 0.0),
    )


NT = (((1,), (1,)), ((), ()))
TN = (((0,), (0,)), ((), ()))


def wide_dot(former, latter, numbers=(((1,), (0,)), ((), ()))):
    return lax.dot_general(former, latter, numbers, preferred_element_type=jnp.float32)


def look_up(table_row, bins):
    table = jnp.broadcast_to(table_row, bins.shape)
    return jnp.take_along_axis(table, bins, axis=1, mode="promise_in_bounds")


def half_of(values, lane, side):
    return jnp.where((lane >= 64) == (side == 1), values, jnp.zeros_like(values))


def row_blocks(total, size):
    return [(start, min(start + size, total)) for start in range(0, total, size)]


def group_columns(kinds, tables, side):
    right = tables[8 * side + 1 : 8 * side + 2]
    left = tables[8 * side + 2 : 8 * side + 3]
    return jnp.where(kinds == RIGHT, right, jnp.where(kinds == LEFT, left, 0.0))


def forward_kernel(layout, scale, *refs):
    count = len(layout.pieces)
    normed_ref, weight_ref = refs[:2]
    key_refs = refs[2 : 2 + count]
    value_refs = refs[2 + count : 2 + 2 * count]
    members_ref, kinds_ref, bins_ref, tables_ref, query_ref, out_ref, log_ref = refs[
        2 + 2 * count : -1
    ]
    all_scores = refs[-1]
    pair = pl.program_id(1)
    rows, length = layout.block_rows, layout.length
    turn = 0
    factor = scale * LOG2E
    lane = lax.broadcasted_iota(jnp.int32, (1, LANES), 1)
    query = wide_dot(normed_ref[...], weight_ref[...]).astype(jnp.bfloat16)
    query_ref[...] = query
    keys = jnp.concatenate([ref[...] for ref in key_refs], axis=0)
    values = jnp.concatenate([ref[...] for ref in value_refs], axis=0)
    members = members_ref[...]
    kinds = kinds_ref[...]
    tables = tables_ref[...]
    ones = jnp.ones((length, LANES), jnp.bfloat16)

    @pl.when(pair == 0)
    def _():
        log_ref[...] = jnp.zeros_like(log_ref)

    for side in range(2):
        key_columns = jnp.concatenate([half_of(keys, lane, side), members], axis=1)
        value_columns = jnp.concatenate([half_of(values, lane, side), ones], axis=1)
        extra = group_columns(kinds, tables, side).astype(jnp.bfloat16)
        query_columns = jnp.concatenate([query, extra], axis=1)
        table_row = tables[8 * side : 8 * side + 1]
        for start, stop in row_blocks(rows, QUERY_BLOCK):
            size = stop - start
            scores = all_scores.at[turn % 2]
            turn += 1
            scores[0:size, 0:length] = wide_dot(query_columns[start:stop], key_columns, NT)
            for tile in range(start // LANES, -(-stop // LANES)):
                first, final = tile * LANES, min(tile * LANES + LANES, rows)
                for slot in range(3):
                    other = tile + slot - 1
                    if other >= layout.query_tiles:
                        continue
                    low, high = first, final
                    if slot == 0:
                        high = min(first + 32, final)
                    if slot == 2:
                        low = first + LANES - 32
                    if low >= high:
                        continue
                    place = layout.tile_start(other)
                    width = min(LANES, length - place)
                    bins = bins_ref[low:high, slot * LANES : (slot + 1) * LANES]
                    bias = look_up(table_row, bins)[:, :width]
                    scores[low - start : high - start, place : place + width] += bias
            block = scores[0:size, 0:length]
            top = jnp.max(block, axis=1, keepdims=True)
            weights = jnp.exp2((block - top) * factor).astype(jnp.bfloat16)
            sums = wide_dot(weights, value_columns)
            total = sums[:, LANES:]
            result = sums[:, :LANES] / total
            if side == 0:
                out_ref[start:stop] = result
            else:
                out_ref[start:stop] += result
            log_total = top + jnp.log(total) * (1.0 / scale)
            log_ref[start:stop] = jnp.where(
                lane == 2 * pair + side, log_total, log_ref[start:stop]
            )


def backward_kernel(layout, scale, first_pair, *refs):
    count = len(layout.pieces)
    query_ref, grad_ref, out_ref, log_ref = refs[:4]
    key_refs = refs[4 : 4 + count]
    value_refs = refs[4 + count : 4 + 2 * count]
    rest = refs[4 + 2 * count :]
    members_ref, kinds_ref, bins_ref, places_ref, tables_ref = rest[:5]
    members_turned_ref, kinds_turned_ref = rest[5:7]
    grad_query_ref = rest[7]
    grad_pair_refs = rest[8 : 8 + count]
    grad_table_ref = rest[8 + count]
    query_wide, grad_wide, query_turned, grad_turned = rest[9 + count : 13 + count]
    all_scores, slopes_low, probs_low = rest[13 + count :]
    pair = pl.program_id(1) + first_pair
    rows, length, padded = layout.block_rows, layout.length, layout.padded
    factor = scale * LOG2E
    lane = lax.broadcasted_iota(jnp.int32, (1, LANES), 1)
    keys = jnp.concatenate([ref[...] for ref in key_refs], axis=0)
    values = jnp.concatenate([ref[...] for ref in value_refs], axis=0)
    members = members_ref[...]
    kinds = kinds_ref[...]
    tables = tables_ref[...]
    query = query_ref[...]
    grad = grad_ref[...]
    grad_full = grad.astype(jnp.float32)
    product = grad_full * out_ref[...]
    log_all = log_ref[...]
    tail = 2 * layout.groups
    ones = jnp.broadcast_to(jnp.where(lane < 3, 1.0, 0.0), (length, LANES)).astype(jnp.bfloat16)

    def three_parts(values):
        upper = values.astype(jnp.bfloat16).astype(jnp.float32)
        values = values - upper
        middle = values.astype(jnp.bfloat16).astype(jnp.float32)
        return upper, middle, values - middle

    def in_lanes(parts, first):
        return jnp.where(
            lane == first,
            parts[0],
            jnp.where(lane == first + 1, parts[1], jnp.where(lane == first + 2, parts[2], 0.0)),
        )

    if padded > rows:
        for ref in (query_wide, grad_wide):
            for side in range(2):
                ref[side, rows:padded] = jnp.zeros((padded - rows, ref.shape[2]), jnp.bfloat16)
        for ref in (query_turned, grad_turned):
            ref[:, rows:padded] = jnp.zeros((LANES, padded - rows), jnp.bfloat16)
    query_turned[:, 0:rows] = query.T
    grad_turned[:, 0:rows] = grad.T
    for side in range(2):
        log_total = jnp.sum(
            jnp.where(lane == 2 * pair + side, log_all, 0.0), axis=1, keepdims=True
        )
        extra = group_columns(kinds, tables, side) + in_lanes(three_parts(log_total), tail)
        query_wide[side, 0:rows, 0:LANES] = query
        query_wide[side, 0:rows, LANES:] = extra.astype(jnp.bfloat16)
        delta = jnp.sum(half_of(product, lane, side), axis=1, keepdims=True)
        grad_wide[side, 0:rows, 0:LANES] = grad
        grad_wide[side, 0:rows, LANES:] = in_lanes(three_parts(-delta), 0).astype(jnp.bfloat16)

    key_columns = [
        jnp.concatenate([half_of(keys, lane, side), members], axis=1) for side in range(2)
    ]
    value_columns = [
        jnp.concatenate([half_of(values, lane, side), ones], axis=1) for side in range(2)
    ]
    inner_sums = [jnp.zeros((1, LANES), jnp.float32) for _ in range(2)]
    low_sums = [jnp.zeros((1, LANES), jnp.float32) for _ in range(2)]
    high_sums = [jnp.zeros((1, LANES), jnp.float32) for _ in range(2)]
    reach_tiles = list(range(layout.query_tiles)) + [-1]

    def put(which, start, stop, result):
        begin = 0
        for ref, size in zip(grad_pair_refs, layout.pieces):
            low, high = max(start, begin), min(stop, begin + size)
            if low < high:
                ref[which, low - begin : high - begin] = result[low - start : high - start]
            begin += size

    for start, stop in row_blocks(length, KEY_BLOCK):
        size = stop - start
        for side in range(2):
            table_row = tables[8 * side : 8 * side + 1]
            scores = all_scores.at[side]
            scores[0:size] = wide_dot(key_columns[side][start:stop], query_wide[side], NT)
            near = []
            for index, tile in enumerate(reach_tiles):
                place = layout.tile_start(tile)
                if start <= place < stop:
                    near.append((index, tile, place, min(place + LANES, length)))
            for index, tile, place, final in near:
                for slot in range(3):
                    other = tile + slot - 1
                    if not 0 <= other < layout.query_tiles:
                        continue
                    bins = bins_ref[
                        index * LANES : index * LANES + final - place,
                        slot * LANES : (slot + 1) * LANES,
                    ]
                    scores[
                        place - start : final - start, other * LANES : (other + 1) * LANES
                    ] += look_up(table_row, bins)
            probs = jnp.exp2(scores[0:size] * factor).astype(jnp.bfloat16)
            grad_probs = wide_dot(value_columns[side][start:stop], grad_wide[side], NT)
            probs_low[side, start:stop] = probs
            slopes_low[side, start:stop] = probs * grad_probs.astype(jnp.bfloat16)
            for index, tile, place, final in near:
                for slot in range(3):
                    other = tile + slot - 1
                    if not 0 <= other < layout.query_tiles:
                        continue
                    bins = bins_ref[
                        index * LANES : index * LANES + final - place,
                        slot * LANES : (slot + 1) * LANES,
                    ]
                    cut = slopes_low[side, place:final, other * LANES : (other + 1) * LANES].astype(
                        jnp.float32
                    )
                    low_sums[side] += jnp.sum(
                        jnp.where(bins == 0, cut, 0.0), axis=0, keepdims=True
                    )
                    high_sums[side] += jnp.sum(
                        jnp.where(bins == 2 * (NEAR + 1), cut, 0.0), axis=0, keepdims=True
                    )
                for half in range(2):
                    begin, end = half * 64, min(half * 64 + 64, final - place)
                    if begin >= end:
                        continue
                    base = 0 if tile < 0 else tile - 1 + half
                    where = places_ref[index * LANES + begin : index * LANES + end]
                    spot = where & (LANES - 1)
                    for step in range(2):
                        other = base + step
                        if not 0 <= other < layout.query_tiles or (tile < 0 and step):
                            continue
                        cut = slopes_low[
                            side, place + begin : place + end, other * LANES : (other + 1) * LANES
                        ].astype(jnp.float32)
                        picked = jnp.take_along_axis(cut, spot, axis=1, mode="promise_in_bounds")
                        picked = jnp.where((where >> 7) == step, picked, 0.0)
                        inner_sums[side] += jnp.sum(picked, axis=0, keepdims=True)

    keys_turned = keys.T
    grad_keys, grad_values, grad_queries = [], [], []
    kinds_turned = kinds_turned_ref[...]
    for side in range(2):
        cut = slice(64 * side, 64 * side + 64)
        grad_values.append(wide_dot(grad_turned[cut], probs_low[side], NT))
        grad_keys.append(wide_dot(query_turned[cut], slopes_low[side], NT))
        left = jnp.concatenate([keys_turned[cut], members_turned_ref[...]], axis=0)
        both = wide_dot(left, slopes_low[side])
        grad_queries.append(both[:64])
        sums = both[64:]

        def total(kind):
            return jnp.sum(jnp.where(kinds_turned == kind, sums, 0.0))

        right = total(RIGHT) + jnp.sum(high_sums[side])
        left = total(LEFT) + jnp.sum(low_sums[side])
        apart = total(APART)
        grad_table_ref[side : side + 1] = jnp.where(
            lane == 0,
            left,
            jnp.where(
                lane == 2 * (NEAR + 1),
                right,
                jnp.where(lane == 2 * (NEAR + 1) + 1, apart, inner_sums[side]),
            ),
        )
    put(0, 0, length, (jnp.concatenate(grad_keys, axis=0) * scale).T.astype(jnp.bfloat16))
    put(1, 0, length, jnp.concatenate(grad_values, axis=0).T.astype(jnp.bfloat16))
    turned = jnp.concatenate(grad_queries, axis=0) * scale
    grad_query_ref[...] = turned.T[0:rows].astype(jnp.bfloat16)


def tile_columns(rows, offset=0):
    return pl.BlockSpec((None, rows, LANES), lambda crop, pair: (crop, 0, pair + offset))


def per_crop(rows, width):
    return pl.BlockSpec((None, rows, width), lambda crop, pair: (crop, 0, 0))


def kernel_params():
    return pltpu.CompilerParams(
        vmem_limit_bytes=VMEM_BYTES, dimension_semantics=("arbitrary", "arbitrary")
    )


def attention_forward(layout, scale, normed, weight, key_values, members, kinds, bins, tables):
    crops, rows, width = normed.shape
    pairs = tables.shape[0]
    specs = [per_crop(rows, width), pl.BlockSpec((width, LANES), lambda crop, pair: (0, pair))]
    operands = [normed, weight]
    for place in (1, 2):
        for piece in key_values:
            specs.append(tile_columns(piece[0].shape[1], piece[place]))
            operands.append(piece[0])
    specs += [
        per_crop(layout.length, LANES),
        per_crop(rows, LANES),
        per_crop(layout.padded, 3 * LANES),
        pl.BlockSpec((None, 16, LANES), lambda crop, pair: (pair, 0, 0)),
    ]
    flops = 2 * crops * pairs * 2 * rows * layout.length * 256 * 2
    return pl.pallas_call(
        functools.partial(forward_kernel, layout, scale),
        grid=(crops, pairs),
        in_specs=specs,
        out_specs=(tile_columns(rows), tile_columns(rows), per_crop(rows, LANES)),
        out_shape=(
            jax.ShapeDtypeStruct((crops, rows, pairs * LANES), jnp.bfloat16),
            jax.ShapeDtypeStruct((crops, rows, pairs * LANES), jnp.float32),
            jax.ShapeDtypeStruct((crops, rows, LANES), jnp.float32),
        ),
        scratch_shapes=[pltpu.VMEM((2, QUERY_BLOCK, layout.wide), jnp.float32)],
        compiler_params=kernel_params(),
        cost_estimate=pl.CostEstimate(
            flops=flops,
            bytes_accessed=12 * crops * rows * pairs * LANES,
            transcendentals=crops * pairs * 2 * rows * layout.length,
        ),
        name="attention_forward",
    )(*operands, members, kinds, bins, tables)


def attention_backward(
    layout,
    scale,
    first_pair,
    pairs,
    projected,
    grad_out,
    attended,
    logs,
    key_values,
    members,
    kinds,
    bins,
    places,
    members_turned,
    kinds_turned,
    tables,
):
    crops, rows, _ = projected.shape
    specs = [tile_columns(rows, first_pair)] * 3 + [per_crop(rows, LANES)]
    operands = [projected, grad_out, attended, logs]
    for place in (1, 2):
        for piece in key_values:
            specs.append(tile_columns(piece[0].shape[1], piece[place] + first_pair))
            operands.append(piece[0])
    specs += [
        per_crop(layout.length, LANES),
        per_crop(rows, LANES),
        per_crop(bins.shape[1], 3 * LANES),
        per_crop(places.shape[1], LANES),
        pl.BlockSpec((None, 16, LANES), lambda crop, pair: (pair + first_pair, 0, 0)),
        per_crop(64, layout.length),
        per_crop(64, layout.padded),
    ]
    out_specs = [tile_columns(rows)]
    out_shapes = [jax.ShapeDtypeStruct((crops, rows, pairs * LANES), jnp.bfloat16)]
    for piece in key_values:
        size = piece[0].shape[1]
        out_specs.append(
            pl.BlockSpec((None, 2, size, LANES), lambda crop, pair: (crop, 0, 0, pair))
        )
        out_shapes.append(jax.ShapeDtypeStruct((crops, 2, size, pairs * LANES), jnp.bfloat16))
    out_specs.append(pl.BlockSpec((None, None, 8, LANES), lambda crop, pair: (crop, pair, 0, 0)))
    out_shapes.append(jax.ShapeDtypeStruct((crops, pairs, 8, LANES), jnp.float32))
    padded = layout.padded
    return pl.pallas_call(
        functools.partial(backward_kernel, layout, scale, first_pair),
        grid=(crops, pairs),
        in_specs=specs,
        out_specs=tuple(out_specs),
        out_shape=tuple(out_shapes),
        scratch_shapes=[
            pltpu.VMEM((2, padded, 2 * LANES), jnp.bfloat16),
            pltpu.VMEM((2, padded, 2 * LANES), jnp.bfloat16),
            pltpu.VMEM((LANES, padded), jnp.bfloat16),
            pltpu.VMEM((LANES, padded), jnp.bfloat16),
            pltpu.VMEM((2, KEY_BLOCK, padded), jnp.float32),
            pltpu.VMEM((2, layout.length, padded), jnp.bfloat16),
            pltpu.VMEM((2, layout.length, padded), jnp.bfloat16),
        ],
        compiler_params=kernel_params(),
        cost_estimate=pl.CostEstimate(
            flops=2 * crops * pairs * 2 * rows * layout.length * 256 * 5,
            bytes_accessed=20 * crops * rows * pairs * LANES,
            transcendentals=crops * pairs * 2 * rows * layout.length,
        ),
        name="attention_backward",
    )(*operands, members, kinds, bins, places, tables, members_turned, kinds_turned)


def sigmoid(values):
    return 0.5 * jnp.tanh(0.5 * values) + 0.5


def each_strip(rows, body, size=16):
    count = rows // size
    group = max(number for number in range(1, 9) if count % number == 0)

    @pl.loop(0, count // group)
    def _(index):
        for part in range(group):
            body(pl.ds(pl.multiple_of((index * group + part) * size, size), size))


def fold_rows(values):
    return jnp.sum(values.reshape(values.shape[0] // 8, 8, values.shape[1]), axis=0)


def feed_kernel(split, chunks, here_ref, *refs):
    (attended_ref, tokens_ref, upstream_ref, normed_a_ref, mod_ref, gate_weight_ref, output_ref) = refs[:7]
    gate_ref, up_ref, down_ref = refs[7:10]
    layer_ref, grad_middle_ref, grad_att_ref, grad_pre_ref, sums_ref = refs[10:15]
    grads = refs[15:-12]
    gated, grad_ff, normed, branch, middle, total, grad_normed, hidden, both, grad_branch = refs[-12:-2]
    gate_pre, turned = refs[-2:]
    step = pl.program_id(0)
    here = here_ref[0]
    rows, width = tokens_ref.shape
    size = gate_ref.shape[1]
    strip = 112 if rows % 112 == 0 else 64
    strips = rows // strip
    shift_f, scale_f = mod_ref[3:4], mod_ref[4:5]
    open_a, open_f = sigmoid(mod_ref[2:3]), sigmoid(mod_ref[5:6])

    def strip_of(index):
        return pl.ds(pl.multiple_of(index * strip, strip), strip)

    def norm_of(values):
        mean_value = jnp.mean(values, axis=1, keepdims=True)
        centred = values - mean_value
        spread = jnp.mean(centred * centred, axis=1, keepdims=True)
        root = lax.rsqrt(spread + 1e-06)
        return centred * root, root

    @pl.when(step == 0)
    def _():
        gate_pre[...] = wide_dot(normed_a_ref[...], gate_weight_ref[...])

        @pl.loop(0, strips)
        def _(index):
            cut = strip_of(index)
            gated[cut] = (attended_ref[cut] * sigmoid(gate_pre[cut])).astype(jnp.bfloat16)
            grad_ff[cut] = (upstream_ref[cut].astype(jnp.float32) * open_f).astype(jnp.bfloat16)

        branch[...] = wide_dot(gated[...], output_ref[...])

        @pl.loop(0, strips)
        def _(index):
            cut = strip_of(index)
            values = tokens_ref[cut].astype(jnp.float32) + open_a * branch[cut]
            middle[cut] = values
            normed[cut] = (norm_of(values)[0] * (1.0 + scale_f) + shift_f).astype(jnp.bfloat16)
            total[cut] = jnp.zeros((strip, width), jnp.float32)
            grad_normed[cut] = jnp.zeros((strip, width), jnp.float32)

        turned[...] = normed[...].T

    block = rows
    for start in range(0, rows, block):
        cut = slice(start, start + block)
        before = wide_dot(normed[cut], gate_ref[...])
        lifted = wide_dot(normed[cut], up_ref[...])
        grad_hidden = wide_dot(grad_ff[cut], down_ref[...], NT)
        switch = sigmoid(before)
        silu = before * switch
        part = (silu * lifted).astype(jnp.bfloat16)
        hidden[cut] = part
        grad_up = (grad_hidden * silu).astype(jnp.bfloat16)
        grad_gate = (grad_hidden * lifted * (switch + silu * (1.0 - switch))).astype(jnp.bfloat16)
        both[cut, :size] = grad_gate
        both[cut, size:] = grad_up
        total[cut] += wide_dot(part, down_ref[...])
        grad_normed[cut] += wide_dot(grad_gate, gate_ref[...], NT) + wide_dot(
            grad_up, up_ref[...], NT
        )

    pair = wide_dot(turned[...], both[...]).astype(jnp.bfloat16)
    if split:
        gate_send, gate_keep, up_send, up_keep, down_send, down_keep, small_send, small_keep = grads
        half = width // 2
        away = pl.ds(pl.multiple_of((1 - here) * half, LANES), half)
        home = pl.ds(pl.multiple_of(here * half, LANES), half)
        down_send[...] = wide_dot(hidden[...], grad_ff[:, away], TN).astype(jnp.bfloat16)
        down_keep[...] = wide_dot(hidden[...], grad_ff[:, home], TN).astype(jnp.bfloat16)

        @pl.when(step < chunks // 2)
        def _():
            gate_send[...] = pair[:, :size]
            up_send[...] = pair[:, size:]

        @pl.when(step >= chunks // 2)
        def _():
            gate_keep[...] = pair[:, :size]
            up_keep[...] = pair[:, size:]
    else:
        gate_all, up_all, down_all, small_all = grads
        gate_all[...] = pair[:, :size]
        up_all[...] = pair[:, size:]
        down_all[...] = wide_dot(hidden[...], grad_ff[...], TN).astype(jnp.bfloat16)

    @pl.when(step == chunks - 1)
    def _():
        def finish(index, sums):
            gate_f_sum, shift_sum, scale_sum, gate_a_sum = sums
            cut = strip_of(index)
            values = middle[cut]
            fed = total[cut]
            upstream = upstream_ref[cut].astype(jnp.float32)
            layer_ref[cut] = (values + open_f * fed).astype(jnp.bfloat16)
            normal, root = norm_of(values)
            grad = grad_normed[cut]
            scaled = grad * (1.0 + scale_f)
            grad_middle = upstream + root * (
                scaled
                - jnp.mean(scaled, axis=1, keepdims=True)
                - normal * jnp.mean(scaled * normal, axis=1, keepdims=True)
            )
            grad_middle_ref[cut] = grad_middle
            grad_branch[cut] = (grad_middle * open_a).astype(jnp.bfloat16)
            return (
                gate_f_sum + fold_rows(upstream * fed),
                shift_sum + fold_rows(grad),
                scale_sum + fold_rows(grad * normal),
                gate_a_sum + fold_rows(grad_middle * branch[cut]),
            )

        zero = jnp.zeros((8, width), jnp.float32)
        sums = lax.fori_loop(0, strips, finish, (zero, zero, zero, zero))
        gate_f_sum, shift_sum, scale_sum, gate_a_sum = [
            jnp.sum(value, axis=0, keepdims=True) for value in sums
        ]
        none = jnp.zeros((1, width), jnp.float32)
        sums_ref[...] = jnp.concatenate(
            [
                none,
                none,
                gate_a_sum * open_a * (1.0 - open_a),
                shift_sum,
                scale_sum,
                gate_f_sum * open_f * (1.0 - open_f),
                none,
                none,
            ],
            axis=0,
        )
        total[...] = wide_dot(grad_branch[...], output_ref[...], NT)

        @pl.loop(0, strips)
        def _(index):
            cut = strip_of(index)
            grad_gated = total[cut]
            opened = sigmoid(gate_pre[cut])
            grad_att_ref[cut] = (grad_gated * opened).astype(jnp.bfloat16)
            grad_pre_ref[cut] = (
                grad_gated * attended_ref[cut] * (opened * (1.0 - opened))
            ).astype(jnp.bfloat16)

        if split:
            for side, ref in ((away, small_send), (home, small_keep)):
                ref[:, :half] = wide_dot(gated[...], grad_branch[:, side], TN).astype(jnp.bfloat16)
                ref[:, half:] = wide_dot(normed_a_ref[...], grad_pre_ref[:, side], TN).astype(
                    jnp.bfloat16
                )
        else:
            small_all[:, :width] = wide_dot(gated[...], grad_branch[...], TN).astype(jnp.bfloat16)
            small_all[:, width:] = wide_dot(normed_a_ref[...], grad_pre_ref[...], TN).astype(
                jnp.bfloat16
            )


def feed_layer(
    split, here, attended, tokens, upstream, normed_a, mod_rows, gate_weight, output_weight, feed_gate, feed_up, feed_down
):
    rows, width = tokens.shape
    inner = feed_gate.shape[1]
    size = 512
    chunks = inner // size
    half = chunks // 2

    def turn(step, here_ref):
        return (step + half * (1 - here_ref[0])) % chunks if split else step

    def fixed(shape):
        return pl.BlockSpec(shape, lambda step, here_ref: (0, 0), pipeline_mode=pl.Buffered(1))

    def columns(step, here_ref):
        return (0, turn(step, here_ref))

    def strips(step, here_ref):
        return (turn(step, here_ref), 0)

    whole = (rows, width)
    in_specs = [fixed(whole)] * 4 + [
        fixed((8, width)),
        fixed((width, width)),
        fixed((width, width)),
        pl.BlockSpec((width, size), columns),
        pl.BlockSpec((width, size), columns),
        pl.BlockSpec((size, width), strips),
    ]
    out_specs = [fixed(whole)] * 4 + [fixed((8, width))]
    bf16, f32 = jnp.bfloat16, jnp.float32
    out_shapes = [(whole, bf16), (whole, f32), (whole, bf16), (whole, bf16), ((8, width), f32)]
    if split:
        first = pl.BlockSpec((width, size), lambda step, here_ref: (0, jnp.minimum(step, half - 1)))
        second = pl.BlockSpec((width, size), lambda step, here_ref: (0, jnp.maximum(step - half, 0)))
        out_specs += [first, second, first, second]
        out_shapes += [((width, inner // 2), bf16)] * 4
        out_specs += [pl.BlockSpec((size, width // 2), strips)] * 2
        out_shapes += [((inner, width // 2), bf16)] * 2
        out_specs += [fixed((width, width))] * 2
        out_shapes += [((width, width), bf16)] * 2
    else:
        out_specs += [pl.BlockSpec((width, size), columns)] * 2
        out_shapes += [((width, inner), bf16)] * 2
        out_specs += [pl.BlockSpec((size, width), strips), fixed((width, 2 * width))]
        out_shapes += [((inner, width), bf16), ((width, 2 * width), bf16)]
    return pl.pallas_call(
        functools.partial(feed_kernel, split, chunks),
        grid_spec=pltpu.PrefetchScalarGridSpec(
            num_scalar_prefetch=1,
            grid=(chunks,),
            in_specs=in_specs,
            out_specs=tuple(out_specs),
            scratch_shapes=[
                pltpu.VMEM(whole, bf16),
                pltpu.VMEM(whole, bf16),
                pltpu.VMEM(whole, bf16),
                pltpu.VMEM(whole, f32),
                pltpu.VMEM(whole, f32),
                pltpu.VMEM(whole, f32),
                pltpu.VMEM(whole, f32),
                pltpu.VMEM((rows, size), bf16),
                pltpu.VMEM((rows, 2 * size), bf16),
                pltpu.VMEM(whole, bf16),
                pltpu.VMEM(whole, f32),
                pltpu.VMEM((width, rows), bf16),
            ],
        ),
        out_shape=tuple(jax.ShapeDtypeStruct(shape, kind) for shape, kind in out_shapes),
        compiler_params=pltpu.CompilerParams(vmem_limit_bytes=VMEM_BYTES),
        cost_estimate=pl.CostEstimate(
            flops=2 * rows * width * (9 * inner + 5 * width),
            bytes_accessed=12 * width * inner + 24 * rows * width,
            transcendentals=2 * rows * inner,
        ),
        name="feed_layer",
    )(
        jnp.reshape(here, (1,)).astype(jnp.int32),
        attended,
        tokens,
        upstream,
        normed_a,
        mod_rows,
        gate_weight,
        output_weight,
        feed_gate,
        feed_up,
        feed_down,
    )


MASKS = {"u": 8, "v": 4, "y": 2, "x": 1}


def exchange(values, mask):
    return lax.ppermute(values, "crop", [(i, i ^ mask) for i in range(16)])


def swap_res(values):
    return lax.ppermute(values, "res", [(0, 1), (1, 0)])


def tie(*values):
    return lax.optimization_barrier(values)


def add_low(former, latter, kind=jnp.bfloat16):
    return (former.astype(jnp.float32) + latter.astype(jnp.float32)).astype(kind)


def stage_kernel(plans, bits_ref, *refs):
    inputs = refs[: sum(plan["count"] for plan in plans)]
    outputs = list(refs[len(inputs) :])
    for plan in plans:
        mine, inputs = inputs[: plan["count"]], inputs[plan["count"] :]
        out_ref = None if plan["apart"] else outputs[0]
        if not plan["apart"] and plan["merge"] is None:
            outputs.pop(0)
        for column, width, own in plan["parts"]:
            result = outputs.pop(0) if plan["apart"] else out_ref
            target = 0 if plan["apart"] else column
            lead_sizes = () if plan["merge"] is not None else result.shape[:-2]
            for lead in itertools.product(*[range(size) for size in lead_sizes]):
                for first in range(0, plan["rows"], 16):
                    cut = (*lead, slice(first, first + 16))
                    across = slice(column, column + width)
                    total = None
                    for index in own:
                        value = mine[index][(*cut, slice(0, width))].astype(jnp.float32)
                        total = value if total is None else total + value
                    for index in plan["spans"]:
                        total = total + mine[index][(*cut, across)].astype(jnp.float32)
                    fold, local = first // plan["block"], first % plan["block"]
                    if plan["folds"]:
                        value = mine[plan["folds"][fold]][local : local + 16, across]
                        total = total + value.astype(jnp.float32)
                    if plan["merge"] is None:
                        result[(*cut, slice(target, target + width))] = total.astype(result.dtype)
                    else:
                        begin = plan["merge"] + fold * plan["wide"] + column
                        result[local : local + 16, begin : begin + width] = total.astype(result.dtype)


class Halving:
    def __init__(self, streams, orders):
        self.streams = streams
        self.orders = [list(order) for order in orders]
        self.past = [[] for _ in orders]
        self.came = [[] for _ in orders]

    def stage(self, last=False, merge=False, merged=None):
        index = lax.axis_index("crop")
        bits = scalars(*[(index // mask) % 2 for mask in MASKS.values()])
        self.masks, plans, specs, operands, out_specs, out_shapes = [], [], [], [], [], []
        left = 0 if last else len(self.orders[0]) - 1
        fewest = min(parts[0][0][0].shape[0] for parts in self.streams) // 16
        begin = 0
        steps = {3: 4, 2: 2}.get(left, 1)
        for stream, (parts, order, past) in enumerate(zip(self.streams, self.orders, self.past)):
            now = None if last else order.pop(0)
            rest = [axis for axis in MASKS if axis in order]

            def spec_of(axes, rows, width, block, now=now, rest=rest):
                def index_map(step, bits_ref):
                    places = []
                    for axis in axes:
                        bit = bits_ref[list(MASKS).index(axis)]
                        if axis == now:
                            places.append(1 - bit)
                        elif axis not in rest:
                            places.append(bit)
                        elif axis == rest[0] and steps > 1:
                            places.append(step // (steps // 2))
                        elif len(rest) > 1 and axis == rest[1] and steps > 2:
                            places.append(step % 2)
                        else:
                            places.append(0)
                    return (*places, 0, block)

                sizes = [
                    2
                    if axis in rest
                    and not (axis == rest[0] and steps > 1)
                    and not (len(rest) > 1 and axis == rest[1] and steps > 2)
                    else None
                    for axis in axes
                ]
                return pl.BlockSpec((*sizes, rows, width), index_map)

            column = 0
            rows = parts[0][0][0].shape[0] // 16
            wide = sum(width for _, _, width in parts)
            plan = {
                "parts": [],
                "spans": [],
                "folds": [],
                "count": 0,
                "apart": last,
                "rows": rows,
                "block": fewest,
                "wide": wide,
                "merge": begin if merge else None,
            }
            for arrays, block, width in parts:
                own = []
                for value in arrays:
                    operands.append(value.reshape(2, 2, 2, 2, rows, value.shape[1]))
                    specs.append(spec_of(list(MASKS), rows, width, block))
                    own.append(plan["count"])
                    plan["count"] += 1
                plan["parts"].append((column, width, own))
                column += width
            for axes, value in self.came[stream]:
                operands.append(value.reshape(*[2] * len(axes), rows, column))
                specs.append(spec_of(axes, rows, column, 0))
                plan["spans"].append(plan["count"])
                plan["count"] += 1
            if merged is not None:
                for fold in range(rows // fewest):
                    place = (begin + fold * wide) // wide
                    operands.append(merged)
                    specs.append(
                        pl.BlockSpec((fewest, wide), lambda step, bits_ref, place=place: (0, place))
                    )
                    plan["folds"].append(plan["count"])
                    plan["count"] += 1
            begin += wide * (rows // fewest)
            plans.append(plan)
            if last:
                for _, width, _ in plan["parts"]:
                    out_specs.append(pl.BlockSpec((rows, width), lambda step, bits_ref: (0, 0)))
                    out_shapes.append(jax.ShapeDtypeStruct((rows, width), jnp.float32))
            else:
                past.append(now)
                self.masks.append(MASKS[now])
                if not merge:
                    out_specs.append(spec_of(rest, rows, column, 0))
                    out_shapes.append(
                        jax.ShapeDtypeStruct((*[2] * len(rest), rows, column), jnp.bfloat16)
                    )
        if merge:
            out_specs.append(pl.BlockSpec((fewest, begin), lambda step, bits_ref: (0, 0)))
            out_shapes.append(jax.ShapeDtypeStruct((fewest, begin), jnp.bfloat16))
        self.axes = [[axis for axis in MASKS if axis in order] for order in self.orders]
        results = pl.pallas_call(
            functools.partial(stage_kernel, plans),
            grid_spec=pltpu.PrefetchScalarGridSpec(
                num_scalar_prefetch=1, grid=(steps,), in_specs=specs, out_specs=tuple(out_specs)
            ),
            out_shape=tuple(out_shapes),
            compiler_params=pltpu.CompilerParams(vmem_limit_bytes=VMEM_BYTES),
            cost_estimate=pl.CostEstimate(
                flops=sum(4 * math.prod(shape.shape) for shape in out_shapes),
                bytes_accessed=sum(8 * math.prod(shape.shape) for shape in out_shapes),
                transcendentals=0,
            ),
            name="halving_stage",
        )(bits, *operands)
        if merge or last:
            return list(results)
        return [value.reshape(-1, value.shape[-1]) for value in results]

    def send(self, values):
        return [exchange(value, mask) for value, mask in zip(values, self.masks)]

    def take(self, values):
        for came, axes, value in zip(self.came, self.axes, values):
            came.append((axes, value))


def share_columns(values, parts):
    if parts == 1:
        return values.astype(jnp.bfloat16)
    return lax.psum_scatter(values.astype(jnp.bfloat16), "res", scatter_dimension=1, tiled=True)


def scatter_crops(values):
    return lax.psum_scatter(values, "crop", scatter_dimension=0, tiled=True).astype(jnp.float32)


def gather_crops(values, crop_parts):
    if crop_parts != 16:
        return lax.all_gather(values, "crop", axis=0, tiled=True)
    index = lax.axis_index("crop")
    for mask in (1, 2, 4, 8):
        other = exchange(values, mask)
        low = (index // mask) % 2 == 0
        values = jnp.concatenate(
            [jnp.where(low, values, other), jnp.where(low, other, values)], axis=0
        )
    return values


def sum_res(values, parts):
    if parts == 1:
        return values
    if parts != 2:
        return lax.psum(values, "res")
    return values + swap_res(values)


PACK = 1152
SIDE = 384


def whole_vmem(count):
    return [pl.BlockSpec(memory_space=pltpu.VMEM)] * count


def scalars(*values):
    return jnp.stack([jnp.asarray(value, jnp.int32) for value in values])


def local_call(kernel, numbers, operands, shapes, name, flops=0):
    return pl.pallas_call(
        kernel,
        in_specs=[pl.BlockSpec(memory_space=pltpu.SMEM)] + whole_vmem(len(operands)),
        out_specs=tuple(whole_vmem(len(shapes))),
        out_shape=tuple(jax.ShapeDtypeStruct(shape, kind) for shape, kind in shapes),
        compiler_params=pltpu.CompilerParams(vmem_limit_bytes=VMEM_BYTES),
        cost_estimate=pl.CostEstimate(
            flops=flops,
            bytes_accessed=sum(value.size * value.dtype.itemsize for value in operands)
            + sum(4 * math.prod(shape) for shape, _ in shapes),
            transcendentals=0,
        ),
        name=name,
    )(numbers, *operands)


def projection_kernel(counts, here_ref, normed_ref, *refs):
    calls = len(counts)
    parts, (joined_ref, send_ref, keep_ref) = refs[: 3 * calls], refs[3 * calls :]
    width = joined_ref.shape[1] // 3
    column = 0
    for call, pairs in enumerate(counts):
        size = pairs * LANES
        query_ref, own_ref, came_ref = parts[3 * call : 3 * call + 3]
        joined_ref[:, column : column + size] = query_ref[...]
        for start in range(0, joined_ref.shape[0], 16):
            cut = slice(start, start + 16)
            for which in range(2):
                first = (1 + which) * width + column
                joined_ref[cut, first : first + size] = add_low(
                    own_ref[which, cut], came_ref[which, cut]
                )
        column += size
    half = send_ref.shape[1]
    for side, ref in ((1 - here_ref[0], send_ref), (here_ref[0], keep_ref)):
        columns = pl.ds(pl.multiple_of(side * half, LANES), half)
        ref[...] = wide_dot(normed_ref[...], joined_ref[:, columns], TN).astype(jnp.bfloat16)


def projection_gradient(here, normed_a, calls):
    rows, width = normed_a.shape
    counts = [call[0].shape[-1] // LANES for call in calls]
    return local_call(
        functools.partial(projection_kernel, counts),
        scalars(here),
        [normed_a] + [value for call in calls for value in call],
        [
            ((rows, 3 * width), jnp.bfloat16),
            ((width, 3 * width // 2), jnp.bfloat16),
            ((width, 3 * width // 2), jnp.bfloat16),
        ],
        "projection_gradient",
        6 * rows * width * width,
    )


def finish_kernel(counts, joined_ref, weight_ref, pre_ref, gate_ref, tokens_ref, middle_ref, mod_ref, *refs):
    feed_sums_ref, extra_ref = refs[:2]
    table_refs = refs[2 : 2 + len(counts)]
    out_ref, pack_ref, total, folded = refs[2 + len(counts) :]
    step = pl.program_id(0)
    rows, width = tokens_ref.shape
    part = wide_dot(joined_ref[...], weight_ref[...], NT)

    @pl.when(step == 0)
    def _():
        total[...] = part + wide_dot(pre_ref[...], gate_ref[...], NT)

    @pl.when(step > 0)
    def _():
        total[...] += part

    @pl.when(step == pl.num_programs(0) - 1)
    def _():
        scale = mod_ref[1:2]
        folded[...] = jnp.zeros_like(folded)

        def finish(cut):
            values = tokens_ref[cut].astype(jnp.float32)
            centred = values - jnp.mean(values, axis=1, keepdims=True)
            root = lax.rsqrt(jnp.mean(centred * centred, axis=1, keepdims=True) + 1e-06)
            normal = centred * root
            grad = total[cut]
            folded[0] += fold_rows(grad)
            folded[1] += fold_rows(grad * normal)
            scaled = grad * (1.0 + scale)
            out_ref[cut] = (
                middle_ref[cut]
                + root
                * (
                    scaled
                    - jnp.mean(scaled, axis=1, keepdims=True)
                    - normal * jnp.mean(scaled * normal, axis=1, keepdims=True)
                )
            ).astype(jnp.bfloat16)

        each_strip(rows, finish)
        shift_sum, scale_sum = folded[0], folded[1]
        heads = []
        for ref, pairs in zip(table_refs, counts):
            for pair in range(pairs):
                heads += [ref[pair, 0:1], ref[pair, 1:2]]

        def upper_of(values):
            return values.astype(jnp.bfloat16).astype(jnp.float32)

        rests = [head - upper_of(head) for head in heads]
        count = width // LANES
        left = [
            jnp.sum(shift_sum, axis=0, keepdims=True),
            jnp.sum(scale_sum, axis=0, keepdims=True),
            feed_sums_ref[2:6],
        ]
        left += [
            jnp.concatenate(rests[i : i + count], axis=1) for i in range(0, len(heads), count)
        ]
        right = [jnp.concatenate(heads[3 * i : 3 * i + 3], axis=1) for i in range(4)]
        line = extra_ref[5:6]
        right += [extra_ref[4:5], line, line - upper_of(line), extra_ref[7:8]]
        pack = jnp.concatenate(
            [jnp.concatenate(left, axis=0), jnp.concatenate(right, axis=0)], axis=1
        )
        pack_ref[...] = jnp.concatenate([pack, jnp.zeros_like(pack)], axis=0).astype(jnp.bfloat16)


def finish_layer(
    joined, weight, grad_pre, gate_weight, tokens, grad_middle, mod_rows, feed_sums, extra, grad_tables
):
    rows, width = tokens.shape
    counts = [table.shape[0] for table in grad_tables]

    def fixed(shape):
        return pl.BlockSpec(shape, lambda step: (0,) * len(shape), pipeline_mode=pl.Buffered(1))

    return pl.pallas_call(
        functools.partial(finish_kernel, counts),
        grid=(3,),
        in_specs=[
            pl.BlockSpec((rows, width), lambda step: (0, step)),
            pl.BlockSpec((width, width), lambda step: (0, step)),
            fixed((rows, width)),
            fixed((width, width)),
            fixed((rows, width)),
            fixed((rows, width)),
            fixed((8, width)),
            fixed((8, width)),
            fixed((8, SIDE)),
        ]
        + [fixed((count, 8, LANES)) for count in counts],
        out_specs=(fixed((rows, width)), fixed((16, PACK))),
        out_shape=(
            jax.ShapeDtypeStruct((rows, width), jnp.bfloat16),
            jax.ShapeDtypeStruct((16, PACK), jnp.bfloat16),
        ),
        scratch_shapes=[
            pltpu.VMEM((rows, width), jnp.float32),
            pltpu.VMEM((2, 8, width), jnp.float32),
        ],
        compiler_params=pltpu.CompilerParams(vmem_limit_bytes=VMEM_BYTES),
        cost_estimate=pl.CostEstimate(
            flops=8 * rows * width * width, bytes_accessed=24 * rows * width, transcendentals=0
        ),
        name="finish_layer",
    )(
        joined,
        weight,
        grad_pre,
        gate_weight,
        tokens,
        grad_middle,
        mod_rows,
        feed_sums,
        extra,
        *grad_tables,
    )


def fan_first_kernel(bits_ref, keep_ref, came_ref, mine_ref, *send_refs):
    chunk = keep_ref.shape[0] // 16
    for other, ref in enumerate((mine_ref, *send_refs)):
        for level in range(4):
            start = (level * 4 + (bits_ref[0] ^ other)) * chunk
            for first in range(0, chunk, 16):
                cut = pl.ds(pl.multiple_of(start + first, 16), 16)
                place = level * chunk + first
                ref[place : place + 16] = add_low(keep_ref[cut], came_ref[cut])


def fan_v_kernel(bits_ref, mine_ref, *refs):
    came_refs, (send_ref, out_ref) = refs[:3], refs[3:]
    chunk = mine_ref.shape[0] // 4
    for side, ref in ((1 - bits_ref[0], send_ref), (bits_ref[0], out_ref)):
        for far in range(2):
            for first in range(0, chunk, 16):
                cut = pl.ds(pl.multiple_of((2 * far + side) * chunk + first, 16), 16)
                total = mine_ref[cut].astype(jnp.float32)
                for came_ref in came_refs:
                    total = total + came_ref[cut].astype(jnp.float32)
                place = far * chunk + first
                ref[place : place + 16] = total.astype(jnp.bfloat16)


def fan_u_kernel(bits_ref, mine_ref, came_ref, send_ref, out_ref):
    chunk = mine_ref.shape[0] // 2
    for side, ref in ((1 - bits_ref[0], send_ref), (bits_ref[0], out_ref)):
        for first in range(0, chunk, 16):
            cut = pl.ds(pl.multiple_of(side * chunk + first, 16), 16)
            ref[first : first + 16] = add_low(mine_ref[cut], came_ref[cut])


def join_packs_kernel(bits_ref, *refs):
    packs = [ref[...].astype(jnp.float32)[0:8] for ref in refs[:4]]
    refs[4][...] = jnp.concatenate(packs, axis=0).astype(jnp.bfloat16)


def small_kernel(
    heads,
    here_ref,
    mine_ref,
    came_ref,
    modulation_ref,
    pair_norm_ref,
    relative_ref,
    gain_ref,
    pair_weight_ref,
    mod_grad_ref,
    time_ref,
    label_ref,
    relative_grad_ref,
    gain_grad_ref,
    pair_grad_ref,
    grad_condition,
    grad_mod,
    kept,
):
    step = pl.program_id(0)
    crops = mine_ref.shape[0] // 8
    width = mine_ref.shape[1] - SIDE
    conds = relative_ref.shape[1]
    parts = mod_grad_ref.shape[1] // width

    def parts_split(values):
        upper = values.astype(jnp.bfloat16)
        return upper, (values - upper.astype(jnp.float32)).astype(jnp.bfloat16)

    def dot_left(narrow, values, numbers):
        upper, rest = parts_split(values)
        return wide_dot(narrow, upper, numbers) + wide_dot(narrow, rest, numbers)

    def dot_right(values, narrow, numbers):
        upper, rest = parts_split(values)
        return wide_dot(upper, narrow, numbers) + wide_dot(rest, narrow, numbers)

    def both_twice(narrow):
        return jnp.concatenate([narrow, narrow], axis=0)

    def stacked(values):
        return jnp.concatenate(parts_split(values), axis=0)

    @pl.when(step == 0)
    def _():
        shape = (8 * crops, 8 * crops)
        picked = lax.broadcasted_iota(jnp.int32, shape, 0)
        source = lax.broadcasted_iota(jnp.int32, shape, 1)
        hit = ((source >> 3) == (picked & (crops - 1))) & ((source & 7) == (picked // crops))
        select = jnp.where(hit, 1.0, 0.0).astype(jnp.bfloat16)
        mine = wide_dot(select, mine_ref[...])
        grad_mod[...] = mine[: 6 * crops, :width] + wide_dot(select, came_ref[...])[: 6 * crops, :width]
        condition = (
            mine[5 * crops : 6 * crops, width : width + conds]
            + mine[6 * crops : 7 * crops, width : width + conds]
        )
        gate_value = sigmoid(condition)
        kept[0] = condition * gate_value
        kept[1] = gate_value * (1.0 + condition * (1.0 - gate_value))
        kept[2] = mine[4 * crops : 5 * crops, width : width + conds]
        kept[3] = jnp.broadcast_to(
            mine[5 * crops : 6 * crops, width + conds : width + conds + 1]
            + mine[6 * crops : 7 * crops, width + conds : width + conds + 1],
            (crops, conds),
        )
        grad_condition[...] = jnp.zeros_like(grad_condition)

    cond_act = both_twice(kept[0].astype(jnp.bfloat16))
    for turn in range(parts):
        columns = slice(turn * width, (turn + 1) * width)
        first = pl.multiple_of((step * parts + turn) * crops, crops)
        pair = stacked(grad_mod[pl.ds(first, crops)])
        mod_grad_ref[:, columns] = wide_dot(cond_act, pair, TN)
        more = wide_dot(pair, modulation_ref[:, columns], NT)
        grad_condition[...] += more[:crops] + more[crops:]

    @pl.when(step == 0)
    def _():
        shape = (8, 8 * crops)
        line = lax.broadcasted_iota(jnp.int32, shape, 0)
        local = lax.broadcasted_iota(jnp.int32, shape, 1) & 7
        every = jnp.where(local == line, 1.0, 0.0).astype(jnp.bfloat16)
        lines = wide_dot(every, mine_ref[...]) + wide_dot(every, came_ref[...])

        def of_head(head):
            upper = width + (head % 3) * LANES
            rest = (head % (width // LANES)) * LANES
            low = 6 + head // (width // LANES)
            return (
                lines[head // 3 : head // 3 + 1, upper : upper + LANES]
                + lines[low : low + 1, rest : rest + LANES]
            )

        table = jnp.concatenate(
            [of_head(head) for head in range(heads)]
            + [jnp.zeros((16 - heads, LANES), jnp.float32)],
            axis=0,
        )
        bins = relative_ref.shape[0]
        pair_grad_ref[...] = dot_right(table, pair_norm_ref[...], (((1,), (0,)), ((), ())))[:heads]
        grad_norm = dot_right(table, pair_weight_ref[...], (((0,), (1,)), ((), ())))[:bins]
        values = relative_ref[...].astype(jnp.float32)
        centred = values - jnp.mean(values, axis=1, keepdims=True)
        root = lax.rsqrt(jnp.mean(centred * centred, axis=1, keepdims=True) + 1e-06)
        normal = centred * root
        gain_grad_ref[...] = jnp.sum(grad_norm * normal, axis=0, keepdims=True)
        scaled = grad_norm * gain_ref[...].astype(jnp.float32)
        relative_grad_ref[...] = root * (
            scaled
            - jnp.mean(scaled, axis=1, keepdims=True)
            - normal * jnp.mean(scaled * normal, axis=1, keepdims=True)
        )

    @pl.when(step == pl.num_programs(0) - 1)
    def _():
        final = stacked(grad_condition[...] * kept[1])
        time_ref[...] = wide_dot(both_twice(kept[2].astype(jnp.bfloat16)), final, TN)
        label = lax.broadcasted_iota(jnp.int32, (crops, label_ref.shape[0]), 1)
        number = kept[3][:, 0:1].astype(jnp.int32)
        onehot = jnp.where(label == number, 1.0, 0.0).astype(jnp.bfloat16)
        label_ref[...] = wide_dot(both_twice(onehot), final, TN)


def small_gradients(heads, labels, mine, came, modulation_weight, pair_norm, relative, gain, pair_weight):
    conds, wide = modulation_weight.shape
    bins = relative.shape[0]
    rows = mine.shape[0]
    steps = 3

    def fixed(shape):
        return pl.BlockSpec(shape, lambda step: (0, 0))

    shapes = [(conds, wide), (conds, conds), (labels, conds), (bins, conds), (1, conds), (heads, conds)]
    return pl.pallas_call(
        functools.partial(small_kernel, heads),
        grid=(steps,),
        in_specs=[
            pl.BlockSpec(memory_space=pltpu.SMEM),
            fixed((rows, PACK)),
            fixed((rows, PACK)),
            pl.BlockSpec((conds, wide // steps), lambda step: (0, step)),
            fixed((LANES, conds)),
            fixed((bins, conds)),
            fixed((1, conds)),
            fixed((conds, 16)),
        ],
        out_specs=tuple(
            [pl.BlockSpec((conds, wide // steps), lambda step: (0, step))]
            + [fixed(s) for s in shapes[1:]]
        ),
        out_shape=tuple(jax.ShapeDtypeStruct(shape, jnp.float32) for shape in shapes),
        scratch_shapes=[
            pltpu.VMEM((rows // 8, conds), jnp.float32),
            pltpu.VMEM((6 * rows // 8, wide // 6), jnp.float32),
            pltpu.VMEM((4, rows // 8, conds), jnp.float32),
        ],
        compiler_params=pltpu.CompilerParams(vmem_limit_bytes=VMEM_BYTES),
        cost_estimate=pl.CostEstimate(
            flops=100000000, bytes_accessed=10000000, transcendentals=0
        ),
        name="small_gradients",
    )(
        scalars(0),
        mine,
        came,
        modulation_weight,
        pair_norm,
        relative,
        gain,
        pair_weight,
    )


def per_device(
    crop_parts,
    res_parts,
    tokens,
    cotangent,
    time_levels,
    cath_ids,
    residue_numbers,
    chain_mask,
    time_weight,
    label_table,
    modulation_weight,
    projection_weight,
    gate_weight,
    output_weight,
    relative_table,
    pair_gain,
    pair_weight,
    feed_gate,
    feed_up,
    feed_down,
):
    crop_count, row_count, model_width = tokens.shape
    crop_length = residue_numbers.shape[1]
    head_count = pair_weight.shape[1]
    head_width = model_width // head_count
    bin_count = relative_table.shape[0]
    label_count = label_table.shape[0]
    token_count = crop_count * row_count
    score_scale = head_width ** (-0.5)
    pairs = head_count // 2
    layout = Layout(row_count, crop_length)
    query_start = lax.axis_index("res") * row_count

    def conditioning(features, onehot):
        return jnp.dot(features, time_weight, preferred_element_type=jnp.float32) + jnp.dot(
            onehot, label_table, preferred_element_type=jnp.float32
        )

    features = time_features(time_levels, time_weight.shape[0]).astype(jnp.bfloat16)
    label_onehot = (cath_ids[:, None] == jnp.arange(label_count, dtype=jnp.int32)[None, :]).astype(
        jnp.bfloat16
    )
    condition = conditioning(features, label_onehot)
    cond_act = jax.nn.silu(condition).astype(jnp.bfloat16)
    modulation = jnp.dot(cond_act, modulation_weight, preferred_element_type=jnp.float32)
    modulation = modulation.reshape(crop_count, 6, 1, model_width)
    shift_a, scale_a = modulation[:, 0], modulation[:, 1]
    mod_rows = pad_to(modulation[:, :, 0], 1, 8, 0.0)

    rotated = lax.dynamic_slice_in_dim(
        jnp.concatenate([jnp.stack([residue_numbers, chain_mask])] * 2, 2), query_start, crop_length, 2
    )
    members, kinds, forward_bins, backward_bins, places, *turned, tables, pair_norm = attention_tables(
        layout,
        score_scale,
        rotated[0],
        rotated[1],
        query_start,
        relative_table,
        pair_gain,
        pair_weight,
    )

    token_values = tokens.astype(jnp.float32)
    normed_a = (
        modulate(token_values, shift_a, scale_a)
        .astype(jnp.bfloat16)
        .reshape(token_count, model_width)
    )
    (normed_a,) = tie(normed_a)

    def project(weight):
        rows = jnp.dot(normed_a, weight, preferred_element_type=jnp.float32)
        return rows.astype(jnp.bfloat16).reshape(crop_count, row_count, -1)

    key_values = project(projection_weight[:, model_width:])
    others = [
        lax.ppermute(
            key_values, "res", [((r + step) % res_parts, r) for r in range(res_parts)]
        )
        for step in range(1, res_parts)
    ]
    if crop_count == 1 and others:
        line = jnp.concatenate(
            [condition, pad_to(cath_ids.astype(jnp.float32)[:, None], 1, LANES, 0.0)], axis=1
        )
        extra = jnp.concatenate([pad_to(features.astype(jnp.float32), 1, SIDE, 0.0), line], axis=0)
        others, extra = tie(others, jnp.pad(extra, ((4, 2), (0, 0))))
    if len(layout.pieces) == 2:
        other = others[0] if len(others) == 1 else jnp.concatenate(others, axis=1)
        pieces = [(key_values, 0, pairs), (other, 0, pairs)]
    else:
        pieces = [(jnp.concatenate([key_values] + others, axis=1), 0, pairs)]

    def block_rows(values):
        return pad_to(values, 1, layout.block_rows, 0)

    queries, attended, logs = attention_forward(
        layout,
        score_scale,
        block_rows(normed_a.reshape(tokens.shape)),
        projection_weight,
        pieces,
        members,
        kinds,
        forward_bins,
        tables,
    )
    here = lax.axis_index("res")
    split = res_parts == 2 and crop_parts == 16
    per_crop_results = [
        feed_layer(
            split,
            here,
            attended[crop],
            block_rows(tokens)[crop],
            block_rows(cotangent)[crop],
            block_rows(normed_a.reshape(tokens.shape))[crop],
            mod_rows[crop],
            gate_weight,
            output_weight,
            feed_gate,
            feed_up,
            feed_down,
        )
        for crop in range(crop_count)
    ]
    layer_out, grad_middle, grad_attended, grad_gate_pre, feed_sums = (
        jnp.stack([result[place] for result in per_crop_results]) for place in range(5)
    )
    layer_out, grad_middle = layer_out[:, :row_count], grad_middle[:, :row_count]
    grad_gate_pre = grad_gate_pre[:, :row_count].reshape(token_count, model_width)
    weight_grads = [
        sum(result[place].astype(jnp.float32) for result in per_crop_results).astype(jnp.bfloat16)
        if crop_count > 1
        else per_crop_results[0][place]
        for place in range(5, len(per_crop_results[0]))
    ]

    def backward_of(first_pair, count, grad_now):
        return attention_backward(
            layout,
            score_scale,
            first_pair,
            count,
            queries,
            grad_now,
            attended,
            logs,
            pieces,
            members,
            kinds,
            backward_bins,
            places,
            *turned,
            tables,
        )

    if split:
        arrivals = [swap_res(weight_grads[place]) for place in (0, 2, 4, 6)]
        kept = [weight_grads[place] for place in (1, 3, 5, 7)]
        half = model_width // 2
        inner = feed_gate.shape[1] // 2
        calls = [list(backward_of(0, 1, grad_attended))]
        arrivals, calls[0] = tie(arrivals, calls[0])
        gate_w, up_w, down_w, small_w = zip(kept, arrivals)
        halving = Halving(
            [
                [(gate_w, 0, inner), (small_w, 0, half)],
                [(up_w, 0, inner), (small_w, 1, half)],
                [(down_w, 0, half)],
            ],
            ["xyvu", "yvxu", "vxyu"],
        )
        arrived = []
        for first_pair, count in ((1, 4), (5, 1)):
            arrived.append(swap_res(calls[-1][2][0]))
            sent = halving.stage()
            sent, grad_attended = tie(sent, grad_attended)
            came = halving.send(sent)
            calls.append(list(backward_of(first_pair, count, grad_attended)))
            if count > 1:
                came, calls[-1], arrived[-1] = tie(came, calls[-1], arrived[-1])
                halving.take(came)
        index = lax.axis_index("crop")
        bf16 = jnp.bfloat16
        share = model_width // 16
        away = swap_res(calls[2][2][0])
        joined, proj_send, proj_keep = projection_gradient(
            here,
            normed_a,
            [
                (calls[0][0][0], calls[0][1][0], arrived[0]),
                (calls[1][0][0], calls[1][1][0], arrived[1]),
                (calls[2][0][0], calls[2][1][0], away),
            ],
        )
        came, proj_send, proj_keep = tie(came, proj_send, proj_keep)
        proj_came = swap_res(proj_send)
        halving.take(came)
        sent = halving.stage()
        sent, proj_came = tie(sent, proj_came)
        came = halving.send(sent)
        mine, *fan = local_call(
            fan_first_kernel,
            scalars(index % 4),
            [proj_keep, proj_came],
            [((4 * share, PACK), bf16)] * 4,
            "fan_first",
        )
        mine, came = tie(mine, came)
        fan_came = [exchange(value, mask + 1) for mask, value in enumerate(fan)]
        halving.take(came)
        (sent,) = halving.stage(merge=True)
        sent, joined = tie(sent, joined)
        last_came = exchange(sent, MASKS["u"])
        tokens_grad, pack = finish_layer(
            joined,
            projection_weight,
            grad_gate_pre,
            gate_weight,
            tokens[0],
            grad_middle[0],
            mod_rows[0],
            feed_sums[0],
            extra,
            [call[-1][0] for call in calls],
        )
        tokens_grad = tokens_grad[None]
        fan_came, pack = tie(fan_came, pack)
        packs = [pack] + [exchange(pack, mask + 1) for mask in range(3)]
        sent, mine = local_call(
            fan_v_kernel,
            scalars((index // 4) % 2),
            [mine, *fan_came],
            [((2 * share, PACK), bf16), ((2 * share, PACK), bf16)],
            "fan_v",
        )
        packs, sent = tie(packs, sent)
        came = exchange(sent, MASKS["v"])
        (packs,) = local_call(join_packs_kernel, scalars(0), packs, [((32, PACK), bf16)], "join_packs")
        far_packs = exchange(packs, MASKS["v"])
        far_packs, came = tie(far_packs, came)
        packs = jnp.concatenate([packs, far_packs], axis=0)
        packs, last_came = tie(packs, last_came)
        far_packs = exchange(packs, MASKS["u"])
        finals = halving.stage(last=True, merged=last_came)
        feed_gate_grad, output_weight_grad, feed_up_grad, gate_weight_grad, feed_down_grad = finals
        far_packs, feed_down_grad = tie(far_packs, feed_down_grad)
        sent, mine = local_call(
            fan_u_kernel,
            scalars(index // 8),
            [mine, came],
            [((share, PACK), bf16), ((share, PACK), bf16)],
            "fan_u",
        )
        far_packs, sent = tie(far_packs, sent)
        packs = jnp.concatenate([packs, far_packs], axis=0)
        other_packs = swap_res(packs)
        came = exchange(sent, MASKS["u"])
        (
            modulation_weight_grad,
            time_weight_grad,
            label_table_grad,
            relative_table_grad,
            pair_gain_grad,
            pair_weight_grad,
        ) = small_gradients(
            head_count,
            label_count,
            packs,
            other_packs,
            modulation_weight,
            pair_norm,
            relative_table,
            pair_gain.reshape(1, -1),
            pad_to(pair_weight, 1, 16, 0.0),
        )
        pair_weight_grad = pair_weight_grad.T
        came, pair_weight_grad = tie(came, pair_weight_grad)
        projection_weight_grad = add_low(mine, came, jnp.float32)
        pair_gain_grad = pair_gain_grad[0]
    else:
        results = backward_of(0, pairs, grad_attended)
        grad_table = results[-1]
        grad_pairs = results[1:-1]
        if len(grad_pairs) == 2:
            total, away = grad_pairs[0].astype(jnp.float32), grad_pairs[1]
        else:
            total = grad_pairs[0][:, :, :row_count].astype(jnp.float32)
            away = grad_pairs[0][:, :, row_count:]
        for step in range(1, res_parts):
            sent = away[:, :, (step - 1) * row_count : step * row_count]
            pairs_to = [(r, (r + step) % res_parts) for r in range(res_parts)]
            total = total + lax.ppermute(sent, "res", pairs_to).astype(jnp.float32)
        total = total.astype(jnp.bfloat16)
        grad_projected = jnp.concatenate(
            [results[0][:, :row_count], total[:, 0], total[:, 1]], axis=-1
        ).reshape(token_count, 3 * model_width)
        grad_normed_a = against_columns(grad_projected, projection_weight) + against_columns(
            grad_gate_pre, gate_weight
        )
        norm_back_a = jax.vjp(modulate, token_values, shift_a, scale_a)[1]
        grad_tokens, grad_shift_a, grad_scale_a = norm_back_a(
            grad_normed_a.reshape(crop_count, row_count, model_width)
        )
        tokens_grad = (grad_middle + grad_tokens).astype(jnp.bfloat16)
        feed_gate_grad, feed_up_grad, feed_down_grad = (
            scatter_crops(share_columns(value, res_parts)) for value in weight_grads[:3]
        )
        output_weight_grad, gate_weight_grad = (
            scatter_crops(share_columns(value, res_parts))
            for value in (weight_grads[3][:, :model_width], weight_grads[3][:, model_width:])
        )
        projection_weight_grad = scatter_crops(
            share_columns(across_rows(normed_a, grad_projected), res_parts)
        )
        grad_table = grad_table[:, :, :2].sum(0).reshape(head_count, LANES)

        grad_modulation = jnp.concatenate([grad_shift_a, grad_scale_a, feed_sums[:, 2:6]], axis=1)
        grad_modulation = grad_modulation.reshape(crop_count, 6 * model_width)
        table_row = grad_table.reshape(1, head_count * LANES)
        first_row = (jnp.arange(crop_count) == 0).astype(jnp.float32)[:, None]
        small_here = jnp.concatenate([grad_modulation, first_row * table_row], axis=1)
        levels_here = jnp.stack([time_levels, cath_ids.astype(jnp.float32)], axis=1)
        levels_here = pad_to(levels_here, 1, LANES, 0.0)
        small_all = gather_crops(
            jnp.concatenate([levels_here, sum_res(small_here, res_parts)], axis=1), crop_parts
        )
        levels_all, small_all = small_all[:, :2], small_all[:, LANES:]
        grad_modulation = small_all[:, : 6 * model_width]
        grad_table = jnp.sum(small_all[:, 6 * model_width :], axis=0).reshape(head_count, LANES)
        grad_table = grad_table[:, :bin_count]
        features_all = time_features(levels_all[:, 0], time_weight.shape[0]).astype(jnp.bfloat16)
        onehot_all = (
            levels_all[:, 1].astype(jnp.int32)[:, None]
            == jnp.arange(label_count, dtype=jnp.int32)[None, :]
        ).astype(jnp.bfloat16)
        condition = conditioning(features_all, onehot_all)
        cond_act = jax.nn.silu(condition).astype(jnp.bfloat16)
        modulation_weight_grad = split_left(cond_act, grad_modulation, 0, 0)
        grad_condition = split_left(modulation_weight, grad_modulation, 1, 1).T * silu_slope(condition)
        time_weight_grad = split_left(features_all, grad_condition, 0, 0)
        label_table_grad = split_left(onehot_all, grad_condition, 0, 0)
        relative_values = relative_table.astype(jnp.float32)
        gain_values = pair_gain.astype(jnp.float32)
        pair_norm = pair_norm[:bin_count]
        pair_weight_grad = split_left(pair_norm, grad_table, 0, 1)
        grad_pair_norm = split_right(grad_table, pair_weight, 0, 1)
        pair_back = jax.vjp(normalize_rows, relative_values, gain_values)[1]
        relative_table_grad, pair_gain_grad = pair_back(grad_pair_norm)
    return (
        layer_out,
        tokens_grad,
        time_weight_grad,
        label_table_grad,
        modulation_weight_grad,
        projection_weight_grad,
        gate_weight_grad,
        output_weight_grad,
        relative_table_grad,
        pair_gain_grad,
        pair_weight_grad,
        feed_gate_grad,
        feed_up_grad,
        feed_down_grad,
    )


def solution(mesh):
    return jax.shard_map(
        functools.partial(per_device, mesh.shape["crop"], mesh.shape["res"]),
        mesh=mesh,
        in_specs=(
            P("crop", "res", None),
            P("crop", "res", None),
            P("crop"),
            P("crop"),
            P("crop", None),
            P("crop", None),
            P(),
            P(),
            P(),
            P(),
            P(),
            P(),
            P(),
            P(),
            P(),
            P(),
            P(),
            P(),
        ),
        out_specs=(
            P("crop", "res", None),
            P("crop", "res", None),
            P(),
            P(),
            P(),
            P("crop", "res"),
            P("crop", "res"),
            P("crop", "res"),
            P(),
            P(),
            P(),
            P("crop", "res"),
            P("crop", "res"),
            P("crop", "res"),
        ),
        check_vma=False,
    )
```
